32 devices in a mesh: fsdp: 4 (over x, core), ctx: 2 (over y), tp: 4 (over z).
Axes of the slice: x: 2, y: 2, z: 4, core: 2. Of those that a mesh axis runs over, the one named last changes fastest.
Arguments:
- tokens: bfloat16 [8192, 2048], P(('fsdp', 'ctx'), 'tp'), may hold values from -6 to 6
- segments: int32 [8192], replicated, may hold values from 0 to 11, as said below
- query_weight: bfloat16 [2048, 2048], P(('fsdp', 'ctx'), 'tp'), may hold values from -0.125 to 0.125
- key_weight: bfloat16 [2048, 2048], P(('fsdp', 'ctx'), 'tp'), may hold values from -0.125 to 0.125
- value_weight: bfloat16 [2048, 2048], P(('fsdp', 'ctx'), 'tp'), may hold values from -0.125 to 0.125
- output_weight: bfloat16 [2048, 2048], P(('fsdp', 'ctx'), 'tp'), may hold values from -3 to 3
- expand_weight: bfloat16 [2048, 8192], P(('fsdp', 'ctx'), 'tp'), may hold values from -0.125 to 0.125
- shrink_weight: bfloat16 [2048, 8192], P(('fsdp', 'ctx'), 'tp'), may hold values from -0.0625 to 0.0625
- query_bias: bfloat16 [2048], P('tp'), may hold values from -3 to 3
- value_bias: bfloat16 [2048], P('tp'), may hold values from -0.1796875 to 0.1796875
- hidden_bias: bfloat16 [8192], P('tp'), may hold values from -3 to 3
- norm_gains: bfloat16 [2, 2048], P(None, 'tp'), may hold values from 0.25 to 1.75
- row_biases: bfloat16 [4, 2048], P(None, 'tp'), may hold values from -1.796875 to 1.796875
- out_grad: bfloat16 [8192, 2048], P(('fsdp', 'ctx'), 'tp'), may hold values from -6 to 6
Outputs:
- mixed: bfloat16 [8192, 2048], P(('fsdp', 'ctx'), 'tp')
- input_grad: bfloat16 [8192, 2048], P(('fsdp', 'ctx'), 'tp')
- query_weight_grad: float32 [2048, 2048], P(('fsdp', 'ctx'), 'tp')
- key_weight_grad: float32 [2048, 2048], P(('fsdp', 'ctx'), 'tp')
- value_weight_grad: float32 [2048, 2048], P(('fsdp', 'ctx'), 'tp')
- output_weight_grad: float32 [2048, 2048], P(('fsdp', 'ctx'), 'tp')
- expand_weight_grad: float32 [2048, 8192], P(('fsdp', 'ctx'), 'tp')
- shrink_weight_grad: float32 [2048, 8192], P(('fsdp', 'ctx'), 'tp')
- query_bias_grad: float32 [2048], P('tp')
- value_bias_grad: float32 [2048], P('tp')
- hidden_bias_grad: float32 [8192], P('tp')
- norm_gains_grad: float32 [2, 2048], P(None, 'tp')
- row_biases_grad: float32 [4, 2048], P(None, 'tp')
The draws below stay inside these ranges and needn't reach their ends.
Inputs may be any that keep to these rules, and one draw needn't show every extreme that they name: `segments`: the tokens form 4 runs of 2048 tokens; run s holds three documents with ids 3 s, 3 s + 1 and 3 s + 2 in this order, the middle one starting within the run's first 1024 tokens and ending within its last 1024.
All inputs are finite; a program needn't handle non-finite values.
Results may differ from the reference program's by a relative error of at most 0.015.
Values may be sent and summed in bfloat16 or wider, within the bound.
A program may use at most 320 MiB of HBM per device.

```python
import math
import jax
import jax.numpy as jnp
from jax import lax

D = 2048
HEADS = 16
HD = 128
FF = 8192
BLK = 1024
WIN = 1024
QB = 512
SEQ = 2048
TOKENS = 8192
N_FSDP = 4


def draw_segments(key, part):
    key = jax.random.fold_in(key, 7)
    head_key, tail_key = jax.random.split(key)
    head_length = jax.random.randint(head_key, (N_FSDP, 1), 1, BLK)
    tail_length = jax.random.randint(tail_key, (N_FSDP, 1), 1, BLK)
    places = jnp.arange(SEQ, dtype=jnp.int32)[None, :]
    first_ids = 3 * jnp.arange(N_FSDP, dtype=jnp.int32)[:, None]
    labels = first_ids + (places >= head_length).astype(jnp.int32) + (places >= SEQ - tail_length).astype(jnp.int32)
    return labels.reshape(-1).astype(jnp.int32)


def steps_of(own_key, extent, cuts, low, largest):
    factor_of = 1.0
    for position, shards_of in cuts:
        draws = jax.random.uniform(jax.random.fold_in(jax.random.fold_in(own_key, 6), position), (shards_of,), jnp.float32, low / len(cuts), largest / len(cuts))
        factor_of = factor_of * jnp.repeat(jnp.exp(draws), extent[position] // shards_of).reshape((-1,) + (1,) * (len(extent) - 1 - position))
    return factor_of


def centred(own_key, extent, deviation, reach, cuts=(), kind=jnp.bfloat16):
    level = steps_of(own_key, extent, cuts, -0.22, 0.18) if cuts else 1.0
    result = jax.random.normal(own_key, extent, jnp.float32) * deviation * level
    return jnp.minimum(jnp.maximum(result, -reach), reach).astype(kind)


def setup_inputs(seed: int = 0) -> dict:
    seeds = jax.random.split(jax.random.key(seed), 15)
    tokens = centred(seeds[0], (TOKENS, D), 1.0, 6.0, ((0, 8), (1, 4)))
    segments = draw_segments(jax.random.fold_in(seeds[14], 71), 0)
    query_weight = centred(seeds[2], (D, D), D ** -0.5, 0.125, ((0, 8), (1, 4)))
    key_weight = centred(seeds[3], (D, D), D ** -0.5, 0.125, ((0, 8), (1, 4)))
    value_weight = centred(seeds[4], (D, D), D ** -0.5, 0.125, ((0, 8), (1, 4)))
    output_weight = centred(seeds[5], (D, D), (max(D // 512, 1)) ** -0.5, 3.0, ((0, 8), (1, 4)))
    expand_weight = centred(seeds[6], (D, FF), D ** -0.5, 0.125, ((0, 8), (1, 4)))
    shrink_weight = centred(seeds[7], (D, FF), FF ** -0.5, 0.0625, ((0, 8), (1, 4)))
    query_bias = centred(seeds[8], (D,), 0.5, 3.0, ((0, 4),))
    value_bias = centred(seeds[9], (D,), 0.03, 0.1796875, ((0, 4),))
    hidden_bias = centred(seeds[10], (FF,), 0.5, 3.0, ((0, 4),))
    norm_gains = jnp.clip(1.0 + 0.15 * jax.random.normal(seeds[11], (2, D), jnp.float32), 0.25, 1.75).astype(jnp.bfloat16)
    row_biases = centred(seeds[12], (4, D), 0.3, 1.796875, ((1, 4),))
    out_grad = centred(seeds[13], (TOKENS, D), 1.0, 6.0, ((0, 8), (1, 4)))
    return {"tokens": tokens, "segments": segments, "query_weight": query_weight, "key_weight": key_weight, "value_weight": value_weight, "output_weight": output_weight, "expand_weight": expand_weight, "shrink_weight": shrink_weight, "query_bias": query_bias, "value_bias": value_bias, "hidden_bias": hidden_bias, "norm_gains": norm_gains, "row_biases": row_biases, "out_grad": out_grad}


epsilon = 1e-06
masked_value = -1000000000.0

@jax.custom_vjp
def low(v):
    return lax.optimization_barrier(v.astype(jnp.bfloat16)).astype(jnp.float32)

@jax.custom_vjp
def low_back(v):
    return v

def low_keep(v):
    return (low(v), None)

def low_pass(kept, grad):
    return (grad,)

def back_keep(v):
    return (v, None)

def back_low(kept, grad):
    return (low(grad),)
low.defvjp(low_keep, low_pass)
low_back.defvjp(back_keep, back_low)

def matmul(left, right):
    return jnp.dot(left, right, precision=lax.Precision.HIGHEST)

def layer_norm(rows, gain, shift):
    row_mean = lax.optimization_barrier(jnp.mean(rows, axis=-1, keepdims=True))
    row_var = lax.optimization_barrier(jnp.mean(rows * rows, axis=-1, keepdims=True)) - row_mean * row_mean
    return (rows - row_mean) * lax.rsqrt(row_var + epsilon) * gain + shift

def attend_stream(queries, keys_all, values_all, stream_ids):
    length = queries.shape[0]
    span = QB + 2 * WIN
    query_heads = queries.reshape(length, HEADS, HD)
    key_pad = jnp.pad(keys_all.reshape(length, HEADS, HD), ((WIN, WIN), (0, 0), (0, 0)))
    value_pad = jnp.pad(values_all.reshape(length, HEADS, HD), ((WIN, WIN), (0, 0), (0, 0)))
    id_pad = jnp.pad(stream_ids, (WIN, WIN), constant_values=-1)
    distance = jnp.arange(span, dtype=jnp.int32)[None, :] - WIN - jnp.arange(QB, dtype=jnp.int32)[:, None]
    in_reach = jnp.abs(distance) <= WIN
    score_scale = 1.0 / math.sqrt(HD)

    def one_block(offset):
        query_rows = lax.dynamic_slice_in_dim(query_heads, offset, QB, 0)
        key_rows = lax.dynamic_slice_in_dim(key_pad, offset, span, 0)
        value_rows = lax.dynamic_slice_in_dim(value_pad, offset, span, 0)
        own_ids = lax.dynamic_slice_in_dim(stream_ids, offset, QB, 0)
        key_ids = lax.dynamic_slice_in_dim(id_pad, offset, span, 0)
        visible = in_reach & (own_ids[:, None] == key_ids[None, :])
        scores = low_back(jnp.einsum('qhd,khd->hqk', query_rows, key_rows, precision=lax.Precision.HIGHEST) * score_scale)
        scores = jnp.where(visible[None], scores, masked_value)
        highest = lax.optimization_barrier(jnp.max(scores, axis=-1, keepdims=True))
        powers = jnp.exp(scores - highest)
        attn_probs = low(powers / lax.optimization_barrier(jnp.sum(powers, axis=-1, keepdims=True)))
        return jnp.einsum('hqk,khd->qhd', attn_probs, value_rows, precision=lax.Precision.HIGHEST)
    offsets = jnp.arange(length // QB, dtype=jnp.int32) * QB
    attended = lax.map(jax.checkpoint(one_block), offsets)
    return attended.reshape(length, HEADS * HD)

def layer_stream(params, stream, stream_ids):
    query_weight, key_weight, value_weight, output_weight, expand_weight, shrink_weight, query_bias, value_bias, hidden_bias, norm_gains, row_biases = params
    queries = low_back(low(matmul(stream, query_weight) + query_bias))
    keys_all = low_back(low(matmul(stream, key_weight)))
    values_all = low_back(low(matmul(stream, value_weight) + value_bias))
    attended = low_back(low(attend_stream(queries, keys_all, values_all, stream_ids)))
    branch = low_back(matmul(attended, output_weight.T) + row_biases[0])
    first_norm = layer_norm(stream + branch, norm_gains[0], row_biases[1])
    hidden = low_back(matmul(low(first_norm), expand_weight) + hidden_bias)
    activated = low(jax.nn.gelu(hidden, approximate=True))
    ffn_out = low_back(matmul(activated, shrink_weight.T) + row_biases[2])
    return layer_norm(first_norm + ffn_out, norm_gains[1], row_biases[3])

def reference(tokens, segments, query_weight, key_weight, value_weight, output_weight, expand_weight, shrink_weight, query_bias, value_bias, hidden_bias, norm_gains, row_biases, out_grad):
    params = tuple((item.astype(jnp.float32) for item in (query_weight, key_weight, value_weight, output_weight, expand_weight, shrink_weight, query_bias, value_bias, hidden_bias, norm_gains, row_biases)))
    streams = tokens.astype(jnp.float32).reshape(N_FSDP, SEQ, D)
    stream_ids = segments.astype(jnp.int32).reshape(N_FSDP, SEQ)

    def forward(params, streams):

        def advance(carry, item):
            return (carry, jax.checkpoint(layer_stream)(params, item[0], item[1]))
        carry_out, results = lax.scan(advance, jnp.zeros((), jnp.float32), (streams, stream_ids))
        return results
    results, pullback = jax.vjp(forward, params, streams)
    gradients, stream_grads = pullback(out_grad.astype(jnp.float32).reshape(N_FSDP, SEQ, D))
    return (results.reshape(TOKENS, D).astype(jnp.bfloat16), stream_grads.reshape(TOKENS, D).astype(jnp.bfloat16), gradients[0], gradients[1], gradients[2], gradients[3], gradients[4], gradients[5], gradients[6], gradients[7], gradients[8], gradients[9], gradients[10])
```

```python
import functools
import math

import jax
import jax.numpy as jnp
from jax import lax
from jax.experimental import pallas as pl
from jax.experimental.pallas import tpu as pltpu
from jax.sharding import PartitionSpec as P

HD = 128
WIN = 1024
QB = 512
KB = 512

epsilon = 1e-06
hidden_floor = -1e30
score_scale = 1.0 / math.sqrt(HD)
log2_e = 1.0 / math.log(2.0)


def dot_plain(left, right):
    return jnp.dot(left, right, preferred_element_type=jnp.float32)


def dot_rows(left, right):
    return lax.dot_general(
        left, right, (((0,), (0,)), ((), ())), preferred_element_type=jnp.float32
    )


def dot_cols(left, right):
    return lax.dot_general(
        left, right, (((1,), (1,)), ((), ())), preferred_element_type=jnp.float32
    )


def attend_kernel(first, last, q_ref, k_ref, v_ref, low_ref, high_ref, out_ref, lse_ref, vt):
    block = pl.program_id(1)
    rows = q_ref.shape[0]

    @pl.when(block == 0)
    def _():
        vt[...] = v_ref[...].T

    queries = q_ref[...]
    low, high = low_ref[...], high_ref[...]
    places = lax.broadcasted_iota(jnp.int32, (KB, rows), 0)

    def step(number, carry):
        top, total, mixed = carry
        start = pl.multiple_of(number * KB, KB)
        scores = dot_cols(k_ref[pl.ds(start, KB), :], queries) * (score_scale * log2_e)
        keep = (places >= low - start) & (places <= high - start)
        scores = jnp.where(keep, scores, hidden_floor)
        new_top = jnp.maximum(top, jnp.max(scores, axis=0, keepdims=True))
        shrink = jnp.exp2(top - new_top)
        powers = jnp.exp2(scores - new_top)
        total = total * shrink + jnp.sum(powers, axis=0, keepdims=True)
        mixed = mixed * shrink + dot_plain(vt[:, pl.ds(start, KB)], powers.astype(jnp.bfloat16))
        return new_top, total, mixed

    top, total, mixed = lax.fori_loop(
        first[block],
        last[block],
        step,
        (
            jnp.full((1, rows), hidden_floor, jnp.float32),
            jnp.zeros((1, rows), jnp.float32),
            jnp.zeros((HD, rows), jnp.float32),
        ),
    )
    out_ref[...] = (mixed / total).T.astype(out_ref.dtype)
    lse_ref[...] = (top + jnp.log2(total))[None]


def attend(queries, keys, values, low, high, first, last):
    rows, width = queries.shape
    span = keys.shape[0]
    heads = width // HD
    return pl.pallas_call(
        attend_kernel,
        out_shape=(
            jax.ShapeDtypeStruct((rows, width), jnp.bfloat16),
            jax.ShapeDtypeStruct((heads, 1, rows), jnp.float32),
        ),
        grid_spec=pltpu.PrefetchScalarGridSpec(
            num_scalar_prefetch=2,
            grid=(heads, rows // QB),
            in_specs=[
                pl.BlockSpec((QB, HD), lambda h, i, *_: (i, h)),
                pl.BlockSpec((span, HD), lambda h, i, *_: (0, h)),
                pl.BlockSpec((span, HD), lambda h, i, *_: (0, h)),
                pl.BlockSpec((1, QB), lambda h, i, *_: (0, i)),
                pl.BlockSpec((1, QB), lambda h, i, *_: (0, i)),
            ],
            out_specs=[
                pl.BlockSpec((QB, HD), lambda h, i, *_: (i, h)),
                pl.BlockSpec((1, 1, QB), lambda h, i, *_: (h, 0, i)),
            ],
            scratch_shapes=[pltpu.VMEM((HD, span), jnp.bfloat16)],
        ),
        compiler_params=pltpu.CompilerParams(vmem_limit_bytes=32 << 20),
        cost_estimate=pl.CostEstimate(
            flops=3 * rows * span * width,
            bytes_accessed=2 * (2 * rows + 2 * span) * width,
            transcendentals=rows * span * heads,
        ),
        name="attend",
    )(first, last, queries, keys, values, low, high)


def attend_back_kernel(
    first, last, q_ref, k_ref, v_ref, o_ref, g_ref, lse_ref, low_ref, high_ref,
    dq_ref, dk_ref, dv_ref, kt, dk_sum, dv_sum,
):
    block = pl.program_id(1)
    rows = q_ref.shape[0]

    @pl.when(block == 0)
    def _():
        kt[...] = k_ref[...].T
        dk_sum[...] = jnp.zeros_like(dk_sum)
        dv_sum[...] = jnp.zeros_like(dv_sum)

    queries = q_ref[...]
    upstream = g_ref[...]
    lse = lse_ref[0]
    low, high = low_ref[...], high_ref[...]
    places = lax.broadcasted_iota(jnp.int32, (KB, rows), 0)
    product = upstream.astype(jnp.float32) * o_ref[...].astype(jnp.float32)
    delta = jnp.sum(product.T, axis=0, keepdims=True)

    def step(number, dq):
        start = pl.multiple_of(number * KB, KB)
        window = pl.ds(start, KB)
        scores = dot_cols(k_ref[window, :], queries) * (score_scale * log2_e)
        keep = (places >= low - start) & (places <= high - start)
        probs = jnp.exp2(jnp.where(keep, scores - lse, hidden_floor))
        prob_grad = dot_cols(v_ref[window, :], upstream)
        score_grad = (probs * (prob_grad - delta)).astype(jnp.bfloat16)
        dv_sum[window, :] += dot_plain(probs.astype(jnp.bfloat16), upstream)
        dk_sum[window, :] += dot_plain(score_grad, queries)
        return dq + dot_plain(kt[:, window], score_grad)

    dq = lax.fori_loop(
        first[block], last[block], step, jnp.zeros((HD, rows), jnp.float32)
    )
    dq_ref[...] = (dq * score_scale).T.astype(dq_ref.dtype)

    @pl.when(block == pl.num_programs(1) - 1)
    def _():
        dk_ref[...] = (dk_sum[...] * score_scale).astype(dk_ref.dtype)
        dv_ref[...] = dv_sum[...].astype(dv_ref.dtype)


def attend_back(queries, keys, values, out, upstream, lse, low, high, first, last, kind):
    rows, width = queries.shape
    span = keys.shape[0]
    heads = width // HD
    row_spec = pl.BlockSpec((QB, HD), lambda h, i, *_: (i, h))
    key_spec = pl.BlockSpec((span, HD), lambda h, i, *_: (0, h))
    mark_spec = pl.BlockSpec((1, QB), lambda h, i, *_: (0, i))
    return pl.pallas_call(
        attend_back_kernel,
        out_shape=(
            jax.ShapeDtypeStruct((rows, width), jnp.bfloat16),
            jax.ShapeDtypeStruct((span, width), kind),
            jax.ShapeDtypeStruct((span, width), kind),
        ),
        grid_spec=pltpu.PrefetchScalarGridSpec(
            num_scalar_prefetch=2,
            grid=(heads, rows // QB),
            in_specs=[
                row_spec, key_spec, key_spec, row_spec, row_spec,
                pl.BlockSpec((1, 1, QB), lambda h, i, *_: (h, 0, i)),
                mark_spec, mark_spec,
            ],
            out_specs=[row_spec, key_spec, key_spec],
            scratch_shapes=[
                pltpu.VMEM((HD, span), jnp.bfloat16),
                pltpu.VMEM((span, HD), jnp.float32),
                pltpu.VMEM((span, HD), jnp.float32),
            ],
        ),
        compiler_params=pltpu.CompilerParams(vmem_limit_bytes=32 << 20),
        cost_estimate=pl.CostEstimate(
            flops=8 * rows * span * width,
            bytes_accessed=2 * (4 * rows + 4 * span) * width,
            transcendentals=rows * span * heads,
        ),
        name="attend_back",
    )(first, last, queries, keys, values, out, upstream, lse, low, high)


def key_bounds(query_ids, key_ids, offset):
    rows, span = query_ids.shape[0], key_ids.shape[0]
    start = jnp.sum(key_ids[:, None] < query_ids[None, :], axis=0, dtype=jnp.int32)
    stop = jnp.sum(key_ids[:, None] <= query_ids[None, :], axis=0, dtype=jnp.int32)
    places = jnp.arange(rows, dtype=jnp.int32) + offset
    low = jnp.maximum(start, places - WIN)
    high = jnp.minimum(stop - 1, places + WIN)
    first = jnp.min(low.reshape(-1, QB), axis=1) // KB
    last = jnp.max(high.reshape(-1, QB), axis=1) // KB + 1
    return low[None], high[None], first, last


def padded(block, width):
    count = lax.axis_size("ctx")
    forward = [(i, i + 1) for i in range(count - 1)]
    backward = [(target, source) for source, target in forward]
    below = lax.ppermute(block[block.shape[0] - width :], "ctx", forward)
    above = lax.ppermute(block[:width], "ctx", backward)
    return jnp.concatenate([below, block, above], axis=0)


def swap_halves(own, other):
    got = lax.ppermute(other, "ctx", [(0, 1), (1, 0)])
    here = lax.axis_index("ctx") == 0
    return jnp.where(here, own, got), jnp.where(here, got, own)


def heads_in(block):
    half = block.shape[1] // 2
    here = lax.axis_index("ctx") == 0
    left, right = block[:, :half], block[:, half:]
    pair = swap_halves(jnp.where(here, left, right), jnp.where(here, right, left))
    return jnp.concatenate(pair, axis=0)


def heads_out(block):
    half = block.shape[0] // 2
    here = lax.axis_index("ctx") == 0
    top, bottom = block[:half], block[half:]
    pair = swap_halves(jnp.where(here, top, bottom), jnp.where(here, bottom, top))
    return jnp.concatenate(pair, axis=1)


def norm_parts(rows):
    mean = jnp.mean(rows, axis=-1, keepdims=True)
    square = jnp.mean(rows * rows, axis=-1, keepdims=True)
    inverse = lax.rsqrt(square - mean * mean + epsilon)
    return (rows - mean) * inverse, inverse


def norm_back(upstream, normed, inverse, gain):
    scaled = upstream * gain
    first_mean = jnp.mean(scaled, axis=-1, keepdims=True)
    second_mean = jnp.mean(scaled * normed, axis=-1, keepdims=True)
    return inverse * (scaled - first_mean - normed * second_mean)


def gelu_tanh(values):
    return jax.nn.gelu(values, approximate=True)


def gather_rows(rows):
    return lax.all_gather(rows, "tp", axis=0, tiled=True)


def scatter_rows(partial_rows):
    low = partial_rows.astype(jnp.bfloat16)
    return lax.psum_scatter(low, "tp", scatter_dimension=0, tiled=True).astype(jnp.float32)


def spread(block):
    return lax.all_to_all(block, "tp", split_axis=0, concat_axis=1, tiled=True)


def unspread(block):
    return lax.all_to_all(block, "tp", split_axis=1, concat_axis=0, tiled=True)


def body(
    tokens,
    segments,
    query_weight,
    key_weight,
    value_weight,
    output_weight,
    expand_weight,
    shrink_weight,
    query_bias,
    value_bias,
    hidden_bias,
    norm_gains,
    row_biases,
    out_grad,
):
    rows = tokens.shape[0]
    head_cols = query_weight.shape[1]
    plane = ("fsdp", "ctx")
    ctx_size = lax.axis_size("ctx")
    own_rows = rows // lax.axis_size("tp")
    by_heads = ctx_size == 2 and (head_cols // HD) % 2 == 0

    def weight_rows(weight):
        return lax.all_gather(weight, plane, axis=0, tiled=True)

    wide_qkv = weight_rows(jnp.concatenate([query_weight, key_weight, value_weight], axis=1))
    wide_tokens = lax.all_gather(tokens, "tp", axis=1, tiled=True)
    full_output = weight_rows(output_weight)
    full_expand = weight_rows(expand_weight)
    full_shrink = weight_rows(shrink_weight)
    gains = lax.all_gather(norm_gains, "tp", axis=1, tiled=True).astype(jnp.float32)
    biases = lax.all_gather(row_biases, "tp", axis=1, tiled=True).astype(jnp.float32)
    upstream = spread(out_grad).astype(jnp.float32)

    qkv_bias = jnp.concatenate([query_bias, jnp.zeros_like(query_bias), value_bias])
    qkv = (dot_plain(wide_tokens, wide_qkv) + qkv_bias.astype(jnp.float32)).astype(jnp.bfloat16)
    queries, keys, values = (
        qkv[:, i * head_cols : (i + 1) * head_cols] for i in range(3)
    )
    block_index = lax.axis_index("fsdp") * ctx_size + lax.axis_index("ctx")
    if by_heads:
        queries, keys, values = heads_in(queries), heads_in(keys), heads_in(values)
        stream_ids = lax.dynamic_slice_in_dim(
            segments, lax.axis_index("fsdp") * ctx_size * rows, ctx_size * rows, 0
        )
        bounds = key_bounds(stream_ids, stream_ids, 0)
    else:
        keys, values = padded(keys, WIN), padded(values, WIN)
        ids = jnp.concatenate(
            [
                jnp.full((WIN,), -1, jnp.int32),
                segments,
                jnp.full((WIN,), jnp.iinfo(jnp.int32).max, jnp.int32),
            ]
        )
        key_ids = lax.dynamic_slice_in_dim(ids, block_index * rows, rows + 2 * WIN, 0)
        bounds = key_bounds(key_ids[WIN : WIN + rows], key_ids, WIN)
    attended_heads, lse = attend(queries, keys, values, *bounds)
    attended = heads_out(attended_heads) if by_heads else attended_heads

    own_start = lax.axis_index("tp") * own_rows
    own_tokens = lax.dynamic_slice_in_dim(wide_tokens, own_start, own_rows, 0)
    branch = scatter_rows(dot_cols(attended, full_output)) + biases[0]
    normed_one, inverse_one = norm_parts(own_tokens.astype(jnp.float32) + branch)
    first_norm = normed_one * gains[0] + biases[1]
    norm_low = gather_rows(first_norm.astype(jnp.bfloat16))
    hidden = dot_plain(norm_low, full_expand) + hidden_bias.astype(jnp.float32)
    activated = gelu_tanh(hidden).astype(jnp.bfloat16)
    second_sum = first_norm + scatter_rows(dot_cols(activated, full_shrink)) + biases[2]
    normed_two, inverse_two = norm_parts(second_sum)
    mixed = unspread((normed_two * gains[1] + biases[3]).astype(jnp.bfloat16))

    grad_second = norm_back(upstream, normed_two, inverse_two, gains[1])
    gain_two_grad = jnp.sum(upstream * normed_two, axis=0)
    shift_two_grad = jnp.sum(upstream, axis=0)
    ffn_own = grad_second.astype(jnp.bfloat16)
    ffn_bias_grad = jnp.sum(ffn_own.astype(jnp.float32), axis=0)
    ffn_low = gather_rows(ffn_own)

    def owner_sum(grad):
        return lax.psum_scatter(
            grad.astype(jnp.bfloat16), plane, scatter_dimension=0, tiled=True
        ).astype(jnp.float32)

    shrink_grad = owner_sum(dot_rows(ffn_low, activated))
    _, gelu_pull = jax.vjp(gelu_tanh, hidden)
    hidden_low = gelu_pull(dot_plain(ffn_low, full_shrink))[0].astype(jnp.bfloat16)
    hidden_bias_grad = jnp.sum(hidden_low.astype(jnp.float32), axis=0)
    grad_first = grad_second + scatter_rows(dot_cols(hidden_low, full_expand))
    expand_grad = owner_sum(dot_rows(norm_low, hidden_low))
    gain_one_grad = jnp.sum(grad_first * normed_one, axis=0)
    shift_one_grad = jnp.sum(grad_first, axis=0)
    grad_inner = norm_back(grad_first, normed_one, inverse_one, gains[0])
    branch_own = grad_inner.astype(jnp.bfloat16)
    branch_bias_grad = jnp.sum(branch_own.astype(jnp.float32), axis=0)
    branch_low = gather_rows(branch_own)
    output_grad = owner_sum(dot_rows(branch_low, attended))
    attended_grad = dot_plain(branch_low, full_output).astype(jnp.bfloat16)

    if by_heads:
        grads = attend_back(
            queries, keys, values, attended_heads, heads_in(attended_grad), lse, *bounds,
            jnp.bfloat16,
        )
        query_low, key_low, value_low = (heads_out(grad) for grad in grads)
    else:
        query_low, key_ext, value_ext = attend_back(
            queries, keys, values, attended_heads, attended_grad, lse, *bounds, jnp.float32
        )

        def fold(ext):
            edges = jnp.concatenate([ext[:WIN], ext[WIN + rows :]], axis=0)
            around = padded(edges, WIN)
            own = ext[WIN : WIN + rows]
            own = own.at[:WIN].add(around[:WIN]).at[rows - WIN :].add(around[3 * WIN :])
            return own.astype(jnp.bfloat16)

        key_low, value_low = fold(key_ext), fold(value_ext)
    qkv_low = jnp.concatenate([query_low, key_low, value_low], axis=1)
    qkv_grad = owner_sum(dot_rows(wide_tokens, qkv_low))
    input_partial = dot_cols(qkv_low, wide_qkv)
    own_part = lax.dynamic_slice_in_dim(input_partial, own_start, own_rows, 0) + grad_inner
    input_partial = lax.dynamic_update_slice_in_dim(input_partial, own_part, own_start, 0)
    input_grad = lax.psum_scatter(
        input_partial.astype(jnp.bfloat16), "tp", scatter_dimension=1, tiled=True
    )
    row_vectors = jnp.stack(
        [
            gain_one_grad, gain_two_grad,
            branch_bias_grad, shift_one_grad, ffn_bias_grad, shift_two_grad,
        ]
    )
    own_vectors = lax.psum_scatter(row_vectors, "tp", scatter_dimension=1, tiled=True)
    qkv_sums = jnp.sum(qkv_low.astype(jnp.float32), axis=0)
    own_vectors, qkv_sums, hidden_bias_grad = lax.psum(
        (own_vectors, qkv_sums, hidden_bias_grad), plane
    )
    return (
        mixed,
        input_grad,
        qkv_grad[:, :head_cols],
        qkv_grad[:, head_cols : 2 * head_cols],
        qkv_grad[:, 2 * head_cols :],
        output_grad,
        expand_grad,
        shrink_grad,
        qkv_sums[:head_cols],
        qkv_sums[2 * head_cols :],
        hidden_bias_grad,
        own_vectors[:2],
        own_vectors[2:],
    )


def solution(mesh):
    rows, whole, cols = P(("fsdp", "ctx"), "tp"), P(), P("tp")
    wide = P(None, "tp")
    return jax.shard_map(
        body,
        mesh=mesh,
        in_specs=(rows, whole) + (rows,) * 6 + (cols,) * 3 + (wide,) * 2 + (rows,),
        out_specs=(rows,) * 8 + (cols,) * 3 + (wide,) * 2,
        check_vma=False,
    )
```

```python
import functools
import math

import jax
import jax.numpy as jnp
from jax import lax
from jax.experimental import pallas as pl
from jax.experimental.pallas import tpu as pltpu
from jax.sharding import PartitionSpec as P

HD = 128
WIN = 1024
QB = 512
KB = 512

epsilon = 1e-06
hidden_floor = -1e30
score_scale = 1.0 / math.sqrt(HD)
log2_e = 1.0 / math.log(2.0)


def dot_plain(left, right):
    return jnp.dot(left, right, preferred_element_type=jnp.float32)


def dot_rows(left, right):
    return lax.dot_general(
        left, right, (((0,), (0,)), ((), ())), preferred_element_type=jnp.float32
    )


def dot_cols(left, right):
    return lax.dot_general(
        left, right, (((1,), (1,)), ((), ())), preferred_element_type=jnp.float32
    )


def attend_kernel(first, last, q_ref, k_ref, v_ref, low_ref, high_ref, out_ref, lse_ref, vt):
    block = pl.program_id(1)
    rows = q_ref.shape[0]

    @pl.when(block == 0)
    def _():
        vt[...] = v_ref[...].T

    queries = q_ref[...]
    low, high = low_ref[...], high_ref[...]
    places = lax.broadcasted_iota(jnp.int32, (KB, rows), 0)

    def step(number, carry):
        top, total, mixed = carry
        start = pl.multiple_of(number * KB, KB)
        scores = dot_cols(k_ref[pl.ds(start, KB), :], queries) * (score_scale * log2_e)
        keep = (places >= low - start) & (places <= high - start)
        scores = jnp.where(keep, scores, hidden_floor)
        new_top = jnp.maximum(top, jnp.max(scores, axis=0, keepdims=True))
        shrink = jnp.exp2(top - new_top)
        powers = jnp.exp2(scores - new_top)
        total = total * shrink + jnp.sum(powers, axis=0, keepdims=True)
        mixed = mixed * shrink + dot_plain(vt[:, pl.ds(start, KB)], powers.astype(jnp.bfloat16))
        return new_top, total, mixed

    top, total, mixed = lax.fori_loop(
        first[block],
        last[block],
        step,
        (
            jnp.full((1, rows), hidden_floor, jnp.float32),
            jnp.zeros((1, rows), jnp.float32),
            jnp.zeros((HD, rows), jnp.float32),
        ),
    )
    out_ref[...] = (mixed / total).T.astype(out_ref.dtype)
    lse_ref[...] = (top + jnp.log2(total))[None]


def attend(queries, keys, values, low, high, first, last):
    rows, width = queries.shape
    span = keys.shape[0]
    heads = width // HD
    return pl.pallas_call(
        attend_kernel,
        out_shape=(
            jax.ShapeDtypeStruct((rows, width), jnp.bfloat16),
            jax.ShapeDtypeStruct((heads, 1, rows), jnp.float32),
        ),
        grid_spec=pltpu.PrefetchScalarGridSpec(
            num_scalar_prefetch=2,
            grid=(heads, rows // QB),
            in_specs=[
                pl.BlockSpec((QB, HD), lambda h, i, *_: (i, h)),
                pl.BlockSpec((span, HD), lambda h, i, *_: (0, h)),
                pl.BlockSpec((span, HD), lambda h, i, *_: (0, h)),
                pl.BlockSpec((1, QB), lambda h, i, *_: (0, i)),
                pl.BlockSpec((1, QB), lambda h, i, *_: (0, i)),
            ],
            out_specs=[
                pl.BlockSpec((QB, HD), lambda h, i, *_: (i, h)),
                pl.BlockSpec((1, 1, QB), lambda h, i, *_: (h, 0, i)),
            ],
            scratch_shapes=[pltpu.VMEM((HD, span), jnp.bfloat16)],
        ),
        compiler_params=pltpu.CompilerParams(vmem_limit_bytes=32 << 20),
        cost_estimate=pl.CostEstimate(
            flops=3 * rows * span * width,
            bytes_accessed=2 * (2 * rows + 2 * span) * width,
            transcendentals=rows * span * heads,
        ),
        name="attend",
    )(first, last, queries, keys, values, low, high)


def attend_back_kernel(
    first, last, q_ref, k_ref, v_ref, o_ref, g_ref, lse_ref, low_ref, high_ref,
    dq_ref, dk_ref, dv_ref, kt, dk_sum, dv_sum,
):
    block = pl.program_id(1)
    rows = q_ref.shape[0]

    @pl.when(block == 0)
    def _():
        kt[...] = k_ref[...].T
        dk_sum[...] = jnp.zeros_like(dk_sum)
        dv_sum[...] = jnp.zeros_like(dv_sum)

    queries = q_ref[...]
    upstream = g_ref[...]
    lse = lse_ref[0]
    low, high = low_ref[...], high_ref[...]
    places = lax.broadcasted_iota(jnp.int32, (KB, rows), 0)
    product = upstream.astype(jnp.float32) * o_ref[...].astype(jnp.float32)
    delta = jnp.sum(product.T, axis=0, keepdims=True)

    def step(number, dq):
        start = pl.multiple_of(number * KB, KB)
        window = pl.ds(start, KB)
        scores = dot_cols(k_ref[window, :], queries) * (score_scale * log2_e)
        keep = (places >= low - start) & (places <= high - start)
        probs = jnp.exp2(jnp.where(keep, scores - lse, hidden_floor))
        prob_grad = dot_cols(v_ref[window, :], upstream)
        score_grad = (probs * (prob_grad - delta)).astype(jnp.bfloat16)
        dv_sum[window, :] += dot_plain(probs.astype(jnp.bfloat16), upstream)
        dk_sum[window, :] += dot_plain(score_grad, queries)
        return dq + dot_plain(kt[:, window], score_grad)

    dq = lax.fori_loop(
        first[block], last[block], step, jnp.zeros((HD, rows), jnp.float32)
    )
    dq_ref[...] = (dq * score_scale).T.astype(dq_ref.dtype)

    @pl.when(block == pl.num_programs(1) - 1)
    def _():
        dk_ref[...] = (dk_sum[...] * score_scale).astype(dk_ref.dtype)
        dv_ref[...] = dv_sum[...].astype(dv_ref.dtype)


def attend_back(queries, keys, values, out, upstream, lse, low, high, first, last, kind):
    rows, width = queries.shape
    span = keys.shape[0]
    heads = width // HD
    row_spec = pl.BlockSpec((QB, HD), lambda h, i, *_: (i, h))
    key_spec = pl.BlockSpec((span, HD), lambda h, i, *_: (0, h))
    mark_spec = pl.BlockSpec((1, QB), lambda h, i, *_: (0, i))
    return pl.pallas_call(
        attend_back_kernel,
        out_shape=(
            jax.ShapeDtypeStruct((rows, width), jnp.bfloat16),
            jax.ShapeDtypeStruct((span, width), kind),
            jax.ShapeDtypeStruct((span, width), kind),
        ),
        grid_spec=pltpu.PrefetchScalarGridSpec(
            num_scalar_prefetch=2,
            grid=(heads, rows // QB),
            in_specs=[
                row_spec, key_spec, key_spec, row_spec, row_spec,
                pl.BlockSpec((1, 1, QB), lambda h, i, *_: (h, 0, i)),
                mark_spec, mark_spec,
            ],
            out_specs=[row_spec, key_spec, key_spec],
            scratch_shapes=[
                pltpu.VMEM((HD, span), jnp.bfloat16),
                pltpu.VMEM((span, HD), jnp.float32),
                pltpu.VMEM((span, HD), jnp.float32),
            ],
        ),
        compiler_params=pltpu.CompilerParams(vmem_limit_bytes=32 << 20),
        cost_estimate=pl.CostEstimate(
            flops=8 * rows * span * width,
            bytes_accessed=2 * (4 * rows + 4 * span) * width,
            transcendentals=rows * span * heads,
        ),
        name="attend_back",
    )(first, last, queries, keys, values, out, upstream, lse, low, high)


def key_bounds(query_ids, key_ids, offset):
    rows, span = query_ids.shape[0], key_ids.shape[0]
    start = jnp.sum(key_ids[:, None] < query_ids[None, :], axis=0, dtype=jnp.int32)
    stop = jnp.sum(key_ids[:, None] <= query_ids[None, :], axis=0, dtype=jnp.int32)
    places = jnp.arange(rows, dtype=jnp.int32) + offset
    low = jnp.maximum(start, places - WIN)
    high = jnp.minimum(stop - 1, places + WIN)
    first = jnp.min(low.reshape(-1, QB), axis=1) // KB
    last = jnp.max(high.reshape(-1, QB), axis=1) // KB + 1
    return low[None], high[None], first, last


def padded(block, width):
    count = lax.axis_size("ctx")
    forward = [(i, i + 1) for i in range(count - 1)]
    backward = [(target, source) for source, target in forward]
    below = lax.ppermute(block[block.shape[0] - width :], "ctx", forward)
    above = lax.ppermute(block[:width], "ctx", backward)
    return jnp.concatenate([below, block, above], axis=0)


def swap_halves(own, other):
    got = lax.ppermute(other, "ctx", [(0, 1), (1, 0)])
    here = lax.axis_index("ctx") == 0
    return jnp.where(here, own, got), jnp.where(here, got, own)


def heads_in(block):
    half = block.shape[1] // 2
    here = lax.axis_index("ctx") == 0
    left, right = block[:, :half], block[:, half:]
    pair = swap_halves(jnp.where(here, left, right), jnp.where(here, right, left))
    return jnp.concatenate(pair, axis=0)


def heads_out(block):
    half = block.shape[0] // 2
    here = lax.axis_index("ctx") == 0
    top, bottom = block[:half], block[half:]
    pair = swap_halves(jnp.where(here, top, bottom), jnp.where(here, bottom, top))
    return jnp.concatenate(pair, axis=1)


def norm_parts(rows):
    mean = jnp.mean(rows, axis=-1, keepdims=True)
    square = jnp.mean(rows * rows, axis=-1, keepdims=True)
    inverse = lax.rsqrt(square - mean * mean + epsilon)
    return (rows - mean) * inverse, inverse


def norm_back(upstream, normed, inverse, gain):
    scaled = upstream * gain
    first_mean = jnp.mean(scaled, axis=-1, keepdims=True)
    second_mean = jnp.mean(scaled * normed, axis=-1, keepdims=True)
    return inverse * (scaled - first_mean - normed * second_mean)


def gelu_tanh(values):
    return jax.nn.gelu(values, approximate=True)


MESH = pl.DeviceIdType.MESH
PIECES = 4
TILE = 512


def greet(me, count):
    barrier = pltpu.get_barrier_semaphore()

    @pl.when(me > 0)
    def _():
        pl.semaphore_signal(barrier, inc=1, device_id={"tp": me - 1}, device_id_type=MESH)

    @pl.when(me < count - 1)
    def _():
        pl.semaphore_signal(barrier, inc=1, device_id={"tp": me + 1}, device_id_type=MESH)

    @pl.when((me == 0) | (me == count - 1))
    def _():
        pl.semaphore_wait(barrier, 1)

    @pl.when((me > 0) & (me < count - 1))
    def _():
        pl.semaphore_wait(barrier, 2)


def at_distance(me, count, distance, action):
    for index in (me - distance, me + distance):

        @pl.when((index >= 0) & (index < count))
        def _(index=index):
            action(index)


class Line:
    def __init__(self, me, count, sum_slots, sum_sent, sum_got, spread_view, spread_sent, spread_got):
        self.me, self.count = me, count
        self.sum_slots, self.sum_sent, self.sum_got = sum_slots, sum_sent, sum_got
        self.spread_view, self.spread_sent, self.spread_got = spread_view, spread_sent, spread_got

    def sum_copy(self, piece, owner):
        onward = jnp.where(owner > self.me, self.me + 1, self.me - 1)
        place = jnp.where((owner < self.me) & (owner == self.me - 1), self.count, owner)
        return pltpu.make_async_remote_copy(
            src_ref=self.sum_slots.at[piece, owner],
            dst_ref=self.sum_slots.at[piece, place],
            send_sem=self.sum_sent.at[piece, owner],
            recv_sem=self.sum_got.at[piece, place],
            device_id={"tp": onward},
            device_id_type=MESH,
        )

    def sum_arrival(self, piece, place):
        pltpu.make_async_copy(
            self.sum_slots.at[piece, place],
            self.sum_slots.at[piece, place],
            self.sum_got.at[piece, place],
        ).wait()

    def sum_start(self, piece, term):
        me, count = self.me, self.count

        @pl.when((me == 0) | (me == count - 1))
        def _():
            for k in range(count - 1):
                owner = jnp.where(me == 0, count - 1 - k, k)
                self.sum_slots[piece, owner] = term(owner).astype(jnp.bfloat16)
                self.sum_copy(piece, owner).start()

    def sum_onward(self, piece, term):
        me, count = self.me, self.count

        @pl.when((me > 0) & (me < count - 1))
        def _():
            for distance in range(count - 2, 0, -1):

                def pass_on(owner):
                    self.sum_arrival(piece, owner)
                    total = self.sum_slots[piece, owner].astype(jnp.float32) + term(owner)
                    self.sum_slots[piece, owner] = total.astype(jnp.bfloat16)
                    self.sum_copy(piece, owner).start()

                at_distance(me, count, distance, pass_on)

    def sum_end(self, piece, total):
        me, count = self.me, self.count

        @pl.when(me > 0)
        def _():
            self.sum_arrival(piece, me)
            total[...] += self.sum_slots[piece, me].astype(jnp.float32)

        @pl.when(me < count - 1)
        def _():
            self.sum_arrival(piece, count)
            total[...] += self.sum_slots[piece, count].astype(jnp.float32)

    def sum_finish(self, pieces):
        @pl.loop(0, pieces)
        def _(piece):
            for distance in range(1, self.count):
                at_distance(
                    self.me, self.count, distance,
                    lambda owner: self.sum_copy(piece, owner).wait_send(),
                )

    def spread_copy(self, piece, owner, to, sent, source=None):
        return pltpu.make_async_remote_copy(
            src_ref=self.spread_view(piece, owner) if source is None else source,
            dst_ref=self.spread_view(piece, owner),
            send_sem=self.spread_sent.at[piece, sent],
            recv_sem=self.spread_got.at[piece, owner],
            device_id={"tp": to},
            device_id_type=MESH,
        )

    def own_copies(self, piece, action, source=None):
        me, count = self.me, self.count

        @pl.when(me > 0)
        def _():
            action(self.spread_copy(piece, me, me - 1, count, source))

        @pl.when(me < count - 1)
        def _():
            action(self.spread_copy(piece, me, me + 1, me, source))

    def spread_start(self, piece, source=None):
        self.own_copies(piece, lambda copy: copy.start(), source)

    def onward_copy(self, piece, owner, action):
        me, count = self.me, self.count

        @pl.when((owner < me) & (me < count - 1))
        def _():
            action(self.spread_copy(piece, owner, me + 1, owner))

        @pl.when((owner > me) & (me > 0))
        def _():
            action(self.spread_copy(piece, owner, me - 1, owner))

    def spread_onward(self, piece, distance):
        def pass_on(owner):
            view = self.spread_view(piece, owner)
            pltpu.make_async_copy(view, view, self.spread_got.at[piece, owner]).wait()
            self.onward_copy(piece, owner, lambda copy: copy.start())

        at_distance(self.me, self.count, distance, pass_on)

    def spread_finish(self, pieces, source=None):
        @pl.loop(0, pieces)
        def _(piece):
            self.own_copies(
                piece, lambda copy: copy.wait_send(), None if source is None else source(piece)
            )
            for distance in range(1, self.count):
                at_distance(
                    self.me, self.count, distance,
                    lambda owner: self.onward_copy(piece, owner, lambda copy: copy.wait_send()),
                )


def line_semaphores(count, pieces):
    return [
        pltpu.SemaphoreType.DMA((pieces, count)),
        pltpu.SemaphoreType.DMA((pieces, count + 1)),
    ], [
        pltpu.SemaphoreType.DMA((pieces, count + 1)),
        pltpu.SemaphoreType.DMA((pieces, count)),
    ]


def gather_kernel(count, x_ref, out_ref, sent, got):
    me = lax.axis_index("tp")
    height = x_ref.shape[0] // PIECES
    width = x_ref.shape[1]

    def view(piece, owner):
        return out_ref.at[
            pl.ds(pl.multiple_of(piece * height, height), height),
            pl.ds(pl.multiple_of(owner * width, width), width),
        ]

    def source(piece):
        return x_ref.at[pl.ds(pl.multiple_of(piece * height, height), height)]

    line = Line(me, count, None, None, None, view, sent, got)
    greet(me, count)

    @pl.loop(0, PIECES)
    def _(piece):
        line.spread_start(piece, source(piece))

    out_ref[:, pl.ds(pl.multiple_of(me * width, width), width)] = x_ref[...]
    for distance in range(1, count):

        @pl.loop(0, PIECES)
        def _(piece, distance=distance):
            line.spread_onward(piece, distance)

    line.spread_finish(PIECES, source)


def gather_features(x, collective_id):
    count = lax.axis_size("tp")
    rows, width = x.shape
    return pl.pallas_call(
        functools.partial(gather_kernel, count),
        out_shape=jax.ShapeDtypeStruct((rows, count * width), x.dtype),
        in_specs=[pl.BlockSpec(memory_space=pltpu.VMEM)],
        out_specs=pl.BlockSpec(memory_space=pltpu.VMEM),
        scratch_shapes=line_semaphores(count, PIECES)[1],
        compiler_params=pltpu.CompilerParams(
            collective_id=collective_id, has_side_effects=True, vmem_limit_bytes=16 << 20
        ),
        cost_estimate=pl.CostEstimate(
            flops=0, bytes_accessed=64 * rows * count * width, transcendentals=0
        ),
        name="gather_features",
    )(x)


def relay_kernel(count, row_step, use_step, sizes, *refs):
    row_in, use_in, row_out, use_out, shared = sizes
    refs = list(refs)

    def take(number):
        taken = refs[:number]
        del refs[:number]
        return taken

    x_ref, sum_weight = take(2)
    use_weight = sum_weight if shared else take(1)[0]
    row_inputs, use_inputs = take(row_in), take(use_in)
    (gathered,) = take(1)
    row_outputs, use_outputs = take(row_out), take(use_out)
    terms, total, slots, sum_sent, sum_got, spread_sent, spread_got = refs
    me = lax.axis_index("tp")
    height = x_ref.shape[0] // PIECES
    own = height // count
    width = sum_weight.shape[0]

    def view(piece, owner):
        return gathered.at[pl.ds(pl.multiple_of(piece * height + owner * own, own), own)]

    line = Line(me, count, slots, sum_sent, sum_got, view, spread_sent, spread_got)
    greet(me, count)

    def piece_rows(piece):
        return pl.ds(pl.multiple_of(piece * height, height), height)

    @pl.loop(0, PIECES + 2)
    def _(step):
        odd = lax.rem(step, 2)

        def term(owner):
            return terms[odd, pl.ds(pl.multiple_of(owner * own, own), own), :]

        @pl.when(step < PIECES)
        def _():
            x = x_ref[piece_rows(step), :]

            @pl.loop(0, width // TILE)
            def _(tile):
                part = pl.ds(pl.multiple_of(tile * TILE, TILE), TILE)
                terms[odd, :, part] = dot_cols(x, sum_weight[part, :])

            line.sum_start(step, term)

        @pl.when((step >= 1) & (step <= PIECES))
        def _():
            piece = step - 1
            total[...] = terms[1 - odd, pl.ds(pl.multiple_of(me * own, own), own), :]
            line.sum_end(piece, total)
            view(piece, me)[...] = row_step(piece, total, row_inputs, row_outputs)
            line.spread_start(piece)

        @pl.when(step >= 2)
        def _():
            for distance in range(2, count):
                line.spread_onward(step - 2, distance)

        @pl.when(step < PIECES)
        def _():
            line.sum_onward(step, term)

        @pl.when((step >= 1) & (step <= PIECES))
        def _():
            line.spread_onward(step - 1, 1)

        @pl.when(step >= 2)
        def _():
            rows = piece_rows(step - 2)
            use_step(rows, gathered[rows, :], use_weight, use_inputs, use_outputs)

    line.sum_finish(PIECES)
    line.spread_finish(PIECES)


def relay(
    x, sum_weight, use_weight, row_inputs, row_step, row_shapes, use_inputs, use_step, use_shapes,
    collective_id, name,
):
    count = lax.axis_size("tp")
    rows = x.shape[0]
    width = sum_weight.shape[0]
    height = rows // PIECES
    own = height // count
    shared = use_weight is None
    operands = [x, sum_weight, *([] if shared else [use_weight]), *row_inputs, *use_inputs]
    shapes = [jax.ShapeDtypeStruct((rows, width), jnp.bfloat16), *row_shapes, *use_shapes]
    sums, spreads = line_semaphores(count, PIECES)
    sizes = (len(row_inputs), len(use_inputs), len(row_shapes), len(use_shapes), shared)
    return pl.pallas_call(
        functools.partial(relay_kernel, count, row_step, use_step, sizes),
        out_shape=shapes,
        in_specs=[pl.BlockSpec(memory_space=pltpu.VMEM)] * len(operands),
        out_specs=[pl.BlockSpec(memory_space=pltpu.VMEM)] * len(shapes),
        scratch_shapes=[
            pltpu.VMEM((2, height, width), jnp.float32),
            pltpu.VMEM((own, width), jnp.float32),
            pltpu.VMEM((PIECES, count + 1, own, width), jnp.bfloat16),
            *sums,
            *spreads,
        ],
        compiler_params=pltpu.CompilerParams(
            collective_id=collective_id, has_side_effects=True, vmem_limit_bytes=60 << 20
        ),
        cost_estimate=pl.CostEstimate(
            flops=100_000_000_000, bytes_accessed=64 * rows * width, transcendentals=0
        ),
        name=name,
    )(*operands)


def own_rows_of(piece, like):
    own = like.shape[0] // PIECES
    return pl.ds(pl.multiple_of(piece * own, own), own)


def first_norm_step(piece, total, inputs, outputs):
    tokens, gains, biases = inputs
    first_norm, normed_one, inverse_one = outputs
    part = own_rows_of(piece, tokens)
    summed = tokens[part, :].astype(jnp.float32) + (total[...] + biases[0:1, :])
    normed, inverse = norm_parts(summed)
    result = normed * gains[0:1, :] + biases[1:2, :]
    first_norm[part, :] = result
    normed_one[part, :] = normed
    inverse_one[part, :] = jnp.broadcast_to(inverse, (inverse.shape[0], 128))
    return result.astype(jnp.bfloat16)


def expand_step(rows, chunk, weight, inputs, outputs):
    (bias,) = inputs
    hidden, activated = outputs

    @pl.loop(0, hidden.shape[1] // TILE)
    def _(tile):
        part = pl.ds(pl.multiple_of(tile * TILE, TILE), TILE)
        values = dot_plain(chunk, weight[:, part]) + bias[:, part]
        hidden[rows, part] = values
        activated[rows, part] = gelu_tanh(values).astype(jnp.bfloat16)


def add_sums(piece, sums, *values):
    @pl.when(piece == 0)
    def _():
        sums[...] = jnp.zeros_like(sums)

    for i, value in enumerate(values):
        sums[i : i + 1, :] += jnp.sum(value, axis=0, keepdims=True)


def second_norm_step(piece, total, inputs, outputs):
    first_norm, out_grad, gains, biases = inputs
    mixed, grad_second, sums = outputs
    part = own_rows_of(piece, first_norm)
    normed, inverse = norm_parts(first_norm[part, :] + total[...] + biases[2:3, :])
    mixed[part, :] = (normed * gains[1:2, :] + biases[3:4, :]).astype(jnp.bfloat16)
    upstream = out_grad[part, :].astype(jnp.float32)
    grad = norm_back(upstream, normed, inverse, gains[1:2, :])
    grad_second[part, :] = grad
    low = grad.astype(jnp.bfloat16)
    add_sums(piece, sums, upstream * normed, upstream, low.astype(jnp.float32))
    return low


def gelu_slope(values):
    scale = math.sqrt(2.0 / math.pi)
    square = values * values
    bend = jnp.tanh(scale * values * (1.0 + 0.044715 * square))
    inner = scale * (1.0 + 3 * 0.044715 * square)
    return 0.5 * (1.0 + bend) + 0.5 * values * (1.0 - bend * bend) * inner


def shrink_step(rows, chunk, weight, inputs, outputs):
    (hidden,) = inputs
    hidden_low, sums = outputs

    @pl.when(rows.start == 0)
    def _():
        sums[...] = jnp.zeros_like(sums)

    @pl.loop(0, hidden.shape[1] // TILE)
    def _(tile):
        part = pl.ds(pl.multiple_of(tile * TILE, TILE), TILE)
        grad = dot_plain(chunk, weight[:, part]) * gelu_slope(hidden[rows, part])
        low = grad.astype(jnp.bfloat16)
        hidden_low[rows, part] = low
        sums[0:1, part] += jnp.sum(low.astype(jnp.float32), axis=0, keepdims=True)


def first_back_step(piece, total, inputs, outputs):
    grad_second, normed_one, inverse_one, gains = inputs
    grad_inner, sums = outputs
    part = own_rows_of(piece, grad_second)
    normed = normed_one[part, :]
    grad_first = grad_second[part, :] + total[...]
    grad = norm_back(grad_first, normed, inverse_one[part, 0:1], gains[0:1, :])
    grad_inner[part, :] = grad
    low = grad.astype(jnp.bfloat16)
    add_sums(piece, sums, grad_first * normed, grad_first, low.astype(jnp.float32))
    return low


def attended_step(rows, chunk, weight, inputs, outputs):
    (attended_grad,) = outputs
    attended_grad[rows, :] = dot_plain(chunk, weight[...]).astype(jnp.bfloat16)


def input_kernel(
    count, x_ref, weight, inner_ref, out_ref, term_ref, total, slots, sum_sent, sum_got
):
    me = lax.axis_index("tp")
    height = x_ref.shape[0] // PIECES
    own = height // count
    width = out_ref.shape[1]
    line = Line(me, count, slots, sum_sent, sum_got, None, None, None)
    greet(me, count)

    def terms(piece):
        def term(owner):
            features = pl.ds(pl.multiple_of(owner * width, width), width)
            term_ref[...] = dot_cols(
                x_ref[pl.ds(pl.multiple_of(piece * height, height), height), :],
                weight[features, :],
            )
            inner = inner_ref[pl.ds(pl.multiple_of(piece * own, own), own), features]
            term_ref[pl.ds(pl.multiple_of(me * own, own), own), :] += inner
            return term_ref[...]

        return term

    @pl.loop(0, PIECES + 1)
    def _(step):
        @pl.when(step < PIECES)
        def _():
            line.sum_start(step, terms(step))
            line.sum_onward(step, terms(step))

        @pl.when(step >= 1)
        def _():
            piece = step - 1
            total[...] = terms(piece)(me)
            line.sum_end(piece, total)
            rows = pl.ds(pl.multiple_of(piece * height, height), height)
            out_ref[rows, :] = total[...].astype(out_ref.dtype)

    line.sum_finish(PIECES)


def input_sum(x, weight, inner, collective_id):
    count = lax.axis_size("tp")
    rows = x.shape[0]
    width = weight.shape[0] // count
    height = rows // PIECES
    return pl.pallas_call(
        functools.partial(input_kernel, count),
        out_shape=jax.ShapeDtypeStruct((rows, width), jnp.bfloat16),
        in_specs=[pl.BlockSpec(memory_space=pltpu.VMEM)] * 3,
        out_specs=pl.BlockSpec(memory_space=pltpu.VMEM),
        scratch_shapes=[
            pltpu.VMEM((height, width), jnp.float32),
            pltpu.VMEM((height, width), jnp.float32),
            pltpu.VMEM((PIECES, count + 1, height, width), jnp.bfloat16),
            *line_semaphores(count, PIECES)[0],
        ],
        compiler_params=pltpu.CompilerParams(
            collective_id=collective_id, has_side_effects=True, vmem_limit_bytes=40 << 20
        ),
        cost_estimate=pl.CostEstimate(
            flops=60_000_000_000, bytes_accessed=64 * rows * width, transcendentals=0
        ),
        name="input_sum",
    )(x, weight, inner)


def to_own_rows(wide):
    count = lax.axis_size("tp")
    parts = wide.reshape(PIECES, count, -1, wide.shape[1])
    return lax.dynamic_index_in_dim(parts, lax.axis_index("tp"), 1, keepdims=False).reshape(
        -1, wide.shape[1]
    )


def spread_own(block):
    count = lax.axis_size("tp")
    rows, width = block.shape
    parts = block.reshape(PIECES, count, -1, width)
    got = lax.all_to_all(parts, "tp", split_axis=1, concat_axis=1, tiled=True)
    return got.transpose(0, 2, 1, 3).reshape(rows // count, count * width)


def unspread_own(block):
    count = lax.axis_size("tp")
    rows, width = block.shape
    parts = block.reshape(PIECES, -1, count, width // count).transpose(0, 2, 1, 3)
    got = lax.all_to_all(parts, "tp", split_axis=1, concat_axis=1, tiled=True)
    return got.reshape(rows * count, width // count)


def body(
    tokens,
    segments,
    query_weight,
    key_weight,
    value_weight,
    output_weight,
    expand_weight,
    shrink_weight,
    query_bias,
    value_bias,
    hidden_bias,
    norm_gains,
    row_biases,
    out_grad,
):
    rows = tokens.shape[0]
    head_cols = query_weight.shape[1]
    plane = ("fsdp", "ctx")
    ctx_size = lax.axis_size("ctx")
    by_heads = ctx_size == 2 and (head_cols // HD) % 2 == 0

    def weight_rows(weight):
        return lax.all_gather(weight, plane, axis=0, tiled=True)

    wide_qkv = weight_rows(jnp.concatenate([query_weight, key_weight, value_weight], axis=1))
    wide_tokens = gather_features(tokens, 0)
    full_output = weight_rows(output_weight)
    full_expand = weight_rows(expand_weight)
    full_shrink = weight_rows(shrink_weight)
    gains = lax.all_gather(norm_gains, "tp", axis=1, tiled=True).astype(jnp.float32)
    biases = lax.all_gather(row_biases, "tp", axis=1, tiled=True).astype(jnp.float32)
    upstream = spread_own(out_grad)

    qkv_bias = jnp.concatenate([query_bias, jnp.zeros_like(query_bias), value_bias])
    qkv = (dot_plain(wide_tokens, wide_qkv) + qkv_bias.astype(jnp.float32)).astype(jnp.bfloat16)
    queries, keys, values = (
        qkv[:, i * head_cols : (i + 1) * head_cols] for i in range(3)
    )
    block_index = lax.axis_index("fsdp") * ctx_size + lax.axis_index("ctx")
    if by_heads:
        queries, keys, values = heads_in(queries), heads_in(keys), heads_in(values)
        stream_ids = lax.dynamic_slice_in_dim(
            segments, lax.axis_index("fsdp") * ctx_size * rows, ctx_size * rows, 0
        )
        bounds = key_bounds(stream_ids, stream_ids, 0)
    else:
        keys, values = padded(keys, WIN), padded(values, WIN)
        ids = jnp.concatenate(
            [
                jnp.full((WIN,), -1, jnp.int32),
                segments,
                jnp.full((WIN,), jnp.iinfo(jnp.int32).max, jnp.int32),
            ]
        )
        key_ids = lax.dynamic_slice_in_dim(ids, block_index * rows, rows + 2 * WIN, 0)
        bounds = key_bounds(key_ids[WIN : WIN + rows], key_ids, WIN)
    attended_heads, lse = attend(queries, keys, values, *bounds)
    attended = heads_out(attended_heads) if by_heads else attended_heads

    own_tokens = to_own_rows(wide_tokens)
    own_rows, features = own_tokens.shape
    hidden_cols = expand_weight.shape[1]

    def shape(extent, kind=jnp.float32):
        return jax.ShapeDtypeStruct(extent, kind)

    own_shape = shape((own_rows, features))
    norm_low, first_norm, normed_one, inverse_one, hidden, activated = relay(
        attended, full_output, full_expand,
        [own_tokens, gains, biases], first_norm_step,
        [own_shape, own_shape, shape((own_rows, 128))],
        [hidden_bias.astype(jnp.float32)[None]], expand_step,
        [shape((rows, hidden_cols)), shape((rows, hidden_cols), jnp.bfloat16)],
        1, "first_norm",
    )
    ffn_low, mixed_own, grad_second, second_sums, hidden_low, hidden_sums = relay(
        activated, full_shrink, None,
        [first_norm, upstream, gains, biases], second_norm_step,
        [shape((own_rows, features), jnp.bfloat16), own_shape, shape((8, features))],
        [hidden], shrink_step,
        [shape((rows, hidden_cols), jnp.bfloat16), shape((8, hidden_cols))],
        2, "second_norm",
    )
    mixed = unspread_own(mixed_own)

    def owner_sum(grad):
        return lax.psum_scatter(
            grad.astype(jnp.bfloat16), plane, scatter_dimension=0, tiled=True
        ).astype(jnp.float32)

    shrink_grad = owner_sum(dot_rows(ffn_low, activated))
    branch_low, grad_inner, first_sums, attended_grad = relay(
        hidden_low, full_expand, full_output,
        [grad_second, normed_one, inverse_one, gains], first_back_step,
        [own_shape, shape((8, features))],
        [], attended_step,
        [shape((rows, head_cols), jnp.bfloat16)],
        3, "first_back",
    )
    expand_grad = owner_sum(dot_rows(norm_low, hidden_low))
    output_grad = owner_sum(dot_rows(branch_low, attended))

    if by_heads:
        grads = attend_back(
            queries, keys, values, attended_heads, heads_in(attended_grad), lse, *bounds,
            jnp.bfloat16,
        )
        query_low, key_low, value_low = (heads_out(grad) for grad in grads)
    else:
        query_low, key_ext, value_ext = attend_back(
            queries, keys, values, attended_heads, attended_grad, lse, *bounds, jnp.float32
        )

        def fold(ext):
            edges = jnp.concatenate([ext[:WIN], ext[WIN + rows :]], axis=0)
            around = padded(edges, WIN)
            own = ext[WIN : WIN + rows]
            own = own.at[:WIN].add(around[:WIN]).at[rows - WIN :].add(around[3 * WIN :])
            return own.astype(jnp.bfloat16)

        key_low, value_low = fold(key_ext), fold(value_ext)
    qkv_low = jnp.concatenate([query_low, key_low, value_low], axis=1)
    qkv_grad = owner_sum(dot_rows(wide_tokens, qkv_low))
    input_grad = input_sum(qkv_low, wide_qkv, grad_inner, 4)
    gain_one_grad, shift_one_grad, branch_bias_grad = first_sums[:3]
    gain_two_grad, shift_two_grad, ffn_bias_grad = second_sums[:3]
    row_vectors = jnp.stack(
        [
            gain_one_grad, gain_two_grad,
            branch_bias_grad, shift_one_grad, ffn_bias_grad, shift_two_grad,
        ]
    )
    own_vectors = lax.psum_scatter(row_vectors, "tp", scatter_dimension=1, tiled=True)
    qkv_sums = jnp.sum(qkv_low.astype(jnp.float32), axis=0)
    own_vectors, qkv_sums, hidden_bias_grad = lax.psum(
        (own_vectors, qkv_sums, hidden_sums[0]), plane
    )
    return (
        mixed,
        input_grad,
        qkv_grad[:, :head_cols],
        qkv_grad[:, head_cols : 2 * head_cols],
        qkv_grad[:, 2 * head_cols :],
        output_grad,
        expand_grad,
        shrink_grad,
        qkv_sums[:head_cols],
        qkv_sums[2 * head_cols :],
        hidden_bias_grad,
        own_vectors[:2],
        own_vectors[2:],
    )


def solution(mesh):
    rows, whole, cols = P(("fsdp", "ctx"), "tp"), P(), P("tp")
    wide = P(None, "tp")
    return jax.shard_map(
        body,
        mesh=mesh,
        in_specs=(rows, whole) + (rows,) * 6 + (cols,) * 3 + (wide,) * 2 + (rows,),
        out_specs=(rows,) * 8 + (cols,) * 3 + (wide,) * 2,
        check_vma=False,
    )
```

```python
import functools
import math

import jax
import jax.numpy as jnp
from jax import lax
from jax.experimental import pallas as pl
from jax.experimental.pallas import tpu as pltpu
from jax.sharding import PartitionSpec as P

HD = 128
WIN = 1024
QB = 512
KB = 512

epsilon = 1e-06
hidden_floor = -1e30
score_scale = 1.0 / math.sqrt(HD)
log2_e = 1.0 / math.log(2.0)


def dot_plain(left, right):
    return jnp.dot(left, right, preferred_element_type=jnp.float32)


def dot_rows(left, right):
    return lax.dot_general(
        left, right, (((0,), (0,)), ((), ())), preferred_element_type=jnp.float32
    )


def dot_cols(left, right):
    return lax.dot_general(
        left, right, (((1,), (1,)), ((), ())), preferred_element_type=jnp.float32
    )


def attend_kernel(first, last, q_ref, k_ref, v_ref, low_ref, high_ref, out_ref, lse_ref, vt):
    block = pl.program_id(1)
    rows = q_ref.shape[0]

    @pl.when(block == 0)
    def _():
        vt[...] = v_ref[...].T

    queries = q_ref[...]
    low, high = low_ref[...], high_ref[...]
    places = lax.broadcasted_iota(jnp.int32, (KB, rows), 0)

    def step(number, carry):
        top, total, mixed = carry
        start = pl.multiple_of(number * KB, KB)
        scores = dot_cols(k_ref[pl.ds(start, KB), :], queries) * (score_scale * log2_e)
        keep = (places >= low - start) & (places <= high - start)
        scores = jnp.where(keep, scores, hidden_floor)
        new_top = jnp.maximum(top, jnp.max(scores, axis=0, keepdims=True))
        shrink = jnp.exp2(top - new_top)
        powers = jnp.exp2(scores - new_top)
        total = total * shrink + jnp.sum(powers, axis=0, keepdims=True)
        mixed = mixed * shrink + dot_plain(vt[:, pl.ds(start, KB)], powers.astype(jnp.bfloat16))
        return new_top, total, mixed

    top, total, mixed = lax.fori_loop(
        first[block],
        last[block],
        step,
        (
            jnp.full((1, rows), hidden_floor, jnp.float32),
            jnp.zeros((1, rows), jnp.float32),
            jnp.zeros((HD, rows), jnp.float32),
        ),
    )
    out_ref[...] = (mixed / total).T.astype(out_ref.dtype)
    lse_ref[...] = (top + jnp.log2(total))[None]


def attend(queries, keys, values, low, high, first, last):
    rows, width = queries.shape
    span = keys.shape[0]
    heads = width // HD
    return pl.pallas_call(
        attend_kernel,
        out_shape=(
            jax.ShapeDtypeStruct((rows, width), jnp.bfloat16),
            jax.ShapeDtypeStruct((heads, 1, rows), jnp.float32),
        ),
        grid_spec=pltpu.PrefetchScalarGridSpec(
            num_scalar_prefetch=2,
            grid=(heads, rows // QB),
            in_specs=[
                pl.BlockSpec((QB, HD), lambda h, i, *_: (i, h)),
                pl.BlockSpec((span, HD), lambda h, i, *_: (0, h)),
                pl.BlockSpec((span, HD), lambda h, i, *_: (0, h)),
                pl.BlockSpec((1, QB), lambda h, i, *_: (0, i)),
                pl.BlockSpec((1, QB), lambda h, i, *_: (0, i)),
            ],
            out_specs=[
                pl.BlockSpec((QB, HD), lambda h, i, *_: (i, h)),
                pl.BlockSpec((1, 1, QB), lambda h, i, *_: (h, 0, i)),
            ],
            scratch_shapes=[pltpu.VMEM((HD, span), jnp.bfloat16)],
        ),
        compiler_params=pltpu.CompilerParams(vmem_limit_bytes=32 << 20),
        cost_estimate=pl.CostEstimate(
            flops=3 * rows * span * width,
            bytes_accessed=2 * (2 * rows + 2 * span) * width,
            transcendentals=rows * span * heads,
        ),
        name="attend",
    )(first, last, queries, keys, values, low, high)


def attend_back_kernel(
    first, last, q_ref, k_ref, v_ref, o_ref, g_ref, lse_ref, low_ref, high_ref,
    dq_ref, dk_ref, dv_ref, kt, dk_sum, dv_sum,
):
    block = pl.program_id(1)
    rows = q_ref.shape[0]

    @pl.when(block == 0)
    def _():
        kt[...] = k_ref[...].T
        dk_sum[...] = jnp.zeros_like(dk_sum)
        dv_sum[...] = jnp.zeros_like(dv_sum)

    queries = q_ref[...]
    upstream = g_ref[...]
    lse = lse_ref[0]
    low, high = low_ref[...], high_ref[...]
    places = lax.broadcasted_iota(jnp.int32, (KB, rows), 0)
    product = upstream.astype(jnp.float32) * o_ref[...].astype(jnp.float32)
    delta = jnp.sum(product.T, axis=0, keepdims=True)

    def step(number, dq):
        start = pl.multiple_of(number * KB, KB)
        window = pl.ds(start, KB)
        scores = dot_cols(k_ref[window, :], queries) * (score_scale * log2_e)
        keep = (places >= low - start) & (places <= high - start)
        probs = jnp.exp2(jnp.where(keep, scores - lse, hidden_floor))
        prob_grad = dot_cols(v_ref[window, :], upstream)
        score_grad = (probs * (prob_grad - delta)).astype(jnp.bfloat16)
        dv_sum[window, :] += dot_plain(probs.astype(jnp.bfloat16), upstream)
        dk_sum[window, :] += dot_plain(score_grad, queries)
        return dq + dot_plain(kt[:, window], score_grad)

    dq = lax.fori_loop(
        first[block], last[block], step, jnp.zeros((HD, rows), jnp.float32)
    )
    dq_ref[...] = (dq * score_scale).T.astype(dq_ref.dtype)

    @pl.when(block == pl.num_programs(1) - 1)
    def _():
        dk_ref[...] = (dk_sum[...] * score_scale).astype(dk_ref.dtype)
        dv_ref[...] = dv_sum[...].astype(dv_ref.dtype)


def attend_back(queries, keys, values, out, upstream, lse, low, high, first, last, kind):
    rows, width = queries.shape
    span = keys.shape[0]
    heads = width // HD
    row_spec = pl.BlockSpec((QB, HD), lambda h, i, *_: (i, h))
    key_spec = pl.BlockSpec((span, HD), lambda h, i, *_: (0, h))
    mark_spec = pl.BlockSpec((1, QB), lambda h, i, *_: (0, i))
    return pl.pallas_call(
        attend_back_kernel,
        out_shape=(
            jax.ShapeDtypeStruct((rows, width), jnp.bfloat16),
            jax.ShapeDtypeStruct((span, width), kind),
            jax.ShapeDtypeStruct((span, width), kind),
        ),
        grid_spec=pltpu.PrefetchScalarGridSpec(
            num_scalar_prefetch=2,
            grid=(heads, rows // QB),
            in_specs=[
                row_spec, key_spec, key_spec, row_spec, row_spec,
                pl.BlockSpec((1, 1, QB), lambda h, i, *_: (h, 0, i)),
                mark_spec, mark_spec,
            ],
            out_specs=[row_spec, key_spec, key_spec],
            scratch_shapes=[
                pltpu.VMEM((HD, span), jnp.bfloat16),
                pltpu.VMEM((span, HD), jnp.float32),
                pltpu.VMEM((span, HD), jnp.float32),
            ],
        ),
        compiler_params=pltpu.CompilerParams(vmem_limit_bytes=32 << 20),
        cost_estimate=pl.CostEstimate(
            flops=8 * rows * span * width,
            bytes_accessed=2 * (4 * rows + 4 * span) * width,
            transcendentals=rows * span * heads,
        ),
        name="attend_back",
    )(first, last, queries, keys, values, out, upstream, lse, low, high)


def key_bounds(query_ids, key_ids, offset):
    rows, span = query_ids.shape[0], key_ids.shape[0]
    start = jnp.sum(key_ids[:, None] < query_ids[None, :], axis=0, dtype=jnp.int32)
    stop = jnp.sum(key_ids[:, None] <= query_ids[None, :], axis=0, dtype=jnp.int32)
    places = jnp.arange(rows, dtype=jnp.int32) + offset
    low = jnp.maximum(start, places - WIN)
    high = jnp.minimum(stop - 1, places + WIN)
    first = jnp.min(low.reshape(-1, QB), axis=1) // KB
    last = jnp.max(high.reshape(-1, QB), axis=1) // KB + 1
    return low[None], high[None], first, last


def padded(block, width):
    count = lax.axis_size("ctx")
    forward = [(i, i + 1) for i in range(count - 1)]
    backward = [(target, source) for source, target in forward]
    below = lax.ppermute(block[block.shape[0] - width :], "ctx", forward)
    above = lax.ppermute(block[:width], "ctx", backward)
    return jnp.concatenate([below, block, above], axis=0)


def swap_halves(own, other):
    got = lax.ppermute(other, "ctx", [(0, 1), (1, 0)])
    here = lax.axis_index("ctx") == 0
    return jnp.where(here, own, got), jnp.where(here, got, own)


def heads_in(block):
    half = block.shape[1] // 2
    here = lax.axis_index("ctx") == 0
    left, right = block[:, :half], block[:, half:]
    pair = swap_halves(jnp.where(here, left, right), jnp.where(here, right, left))
    return jnp.concatenate(pair, axis=0)


def heads_out(block):
    half = block.shape[0] // 2
    here = lax.axis_index("ctx") == 0
    top, bottom = block[:half], block[half:]
    pair = swap_halves(jnp.where(here, top, bottom), jnp.where(here, bottom, top))
    return jnp.concatenate(pair, axis=1)


def norm_parts(rows):
    mean = jnp.mean(rows, axis=-1, keepdims=True)
    square = jnp.mean(rows * rows, axis=-1, keepdims=True)
    inverse = lax.rsqrt(square - mean * mean + epsilon)
    return (rows - mean) * inverse, inverse


def norm_back(upstream, normed, inverse, gain):
    scaled = upstream * gain
    first_mean = jnp.mean(scaled, axis=-1, keepdims=True)
    second_mean = jnp.mean(scaled * normed, axis=-1, keepdims=True)
    return inverse * (scaled - first_mean - normed * second_mean)


def gelu_tanh(values):
    return jax.nn.gelu(values, approximate=True)


MESH = pl.DeviceIdType.MESH
PIECES = 4
TILE = 512


def greet(me, count):
    barrier = pltpu.get_barrier_semaphore()

    @pl.when(me > 0)
    def _():
        pl.semaphore_signal(barrier, inc=1, device_id={"tp": me - 1}, device_id_type=MESH)

    @pl.when(me < count - 1)
    def _():
        pl.semaphore_signal(barrier, inc=1, device_id={"tp": me + 1}, device_id_type=MESH)

    @pl.when((me == 0) | (me == count - 1))
    def _():
        pl.semaphore_wait(barrier, 1)

    @pl.when((me > 0) & (me < count - 1))
    def _():
        pl.semaphore_wait(barrier, 2)


def peers_along_tp(me, count):
    return [{"tp": lax.rem(me + i, count)} for i in range(1, count)]


def greet_peers(peers):
    barrier = pltpu.get_barrier_semaphore()
    for peer in peers:
        pl.semaphore_signal(barrier, inc=1, device_id=peer, device_id_type=MESH)
    pl.semaphore_wait(barrier, len(peers))


class Exchange:
    def __init__(self, peers, sent, got, source, place):
        self.peers, self.sent, self.got = peers, sent, got
        self.source, self.place = source, place

    def copies(self):
        for i, peer in enumerate(self.peers):
            yield pltpu.make_async_remote_copy(
                src_ref=self.source(i + 1),
                dst_ref=self.place(i),
                send_sem=self.sent.at[i],
                recv_sem=self.got.at[i],
                device_id=peer,
                device_id_type=MESH,
            )

    def start(self):
        for copy in self.copies():
            copy.start()

    def wait_arrivals(self):
        for copy in self.copies():
            copy.wait_recv()

    def wait_sent(self):
        for copy in self.copies():
            copy.wait_send()


def at_distance(me, count, distance, action):
    for index in (me - distance, me + distance):

        @pl.when((index >= 0) & (index < count))
        def _(index=index):
            action(index)


class Line:
    def __init__(self, me, count, sum_slots, sum_sent, sum_got, spread_view, spread_sent, spread_got):
        self.me, self.count = me, count
        self.sum_slots, self.sum_sent, self.sum_got = sum_slots, sum_sent, sum_got
        self.spread_view, self.spread_sent, self.spread_got = spread_view, spread_sent, spread_got

    def sum_copy(self, piece, owner):
        onward = jnp.where(owner > self.me, self.me + 1, self.me - 1)
        place = jnp.where((owner < self.me) & (owner == self.me - 1), self.count, owner)
        return pltpu.make_async_remote_copy(
            src_ref=self.sum_slots.at[piece, owner],
            dst_ref=self.sum_slots.at[piece, place],
            send_sem=self.sum_sent.at[piece, owner],
            recv_sem=self.sum_got.at[piece, place],
            device_id={"tp": onward},
            device_id_type=MESH,
        )

    def sum_arrival(self, piece, place):
        pltpu.make_async_copy(
            self.sum_slots.at[piece, place],
            self.sum_slots.at[piece, place],
            self.sum_got.at[piece, place],
        ).wait()

    def sum_start(self, piece, term):
        me, count = self.me, self.count

        @pl.when((me == 0) | (me == count - 1))
        def _():
            for k in range(count - 1):
                owner = jnp.where(me == 0, count - 1 - k, k)
                self.sum_slots[piece, owner] = term(owner).astype(jnp.bfloat16)
                self.sum_copy(piece, owner).start()

    def sum_onward(self, piece, term):
        me, count = self.me, self.count

        @pl.when((me > 0) & (me < count - 1))
        def _():
            for distance in range(count - 2, 0, -1):

                def pass_on(owner):
                    self.sum_arrival(piece, owner)
                    total = self.sum_slots[piece, owner].astype(jnp.float32) + term(owner)
                    self.sum_slots[piece, owner] = total.astype(jnp.bfloat16)
                    self.sum_copy(piece, owner).start()

                at_distance(me, count, distance, pass_on)

    def sum_end(self, piece, total):
        me, count = self.me, self.count

        @pl.when(me > 0)
        def _():
            self.sum_arrival(piece, me)
            total[...] += self.sum_slots[piece, me].astype(jnp.float32)

        @pl.when(me < count - 1)
        def _():
            self.sum_arrival(piece, count)
            total[...] += self.sum_slots[piece, count].astype(jnp.float32)

    def sum_finish(self, pieces):
        @pl.loop(0, pieces)
        def _(piece):
            for distance in range(1, self.count):
                at_distance(
                    self.me, self.count, distance,
                    lambda owner: self.sum_copy(piece, owner).wait_send(),
                )

    def spread_copy(self, piece, owner, to, sent, source=None):
        return pltpu.make_async_remote_copy(
            src_ref=self.spread_view(piece, owner) if source is None else source,
            dst_ref=self.spread_view(piece, owner),
            send_sem=self.spread_sent.at[piece, sent],
            recv_sem=self.spread_got.at[piece, owner],
            device_id={"tp": to},
            device_id_type=MESH,
        )

    def own_copies(self, piece, action, source=None):
        me, count = self.me, self.count

        @pl.when(me > 0)
        def _():
            action(self.spread_copy(piece, me, me - 1, count, source))

        @pl.when(me < count - 1)
        def _():
            action(self.spread_copy(piece, me, me + 1, me, source))

    def spread_start(self, piece, source=None):
        self.own_copies(piece, lambda copy: copy.start(), source)

    def onward_copy(self, piece, owner, action):
        me, count = self.me, self.count

        @pl.when((owner < me) & (me < count - 1))
        def _():
            action(self.spread_copy(piece, owner, me + 1, owner))

        @pl.when((owner > me) & (me > 0))
        def _():
            action(self.spread_copy(piece, owner, me - 1, owner))

    def spread_onward(self, piece, distance):
        def pass_on(owner):
            view = self.spread_view(piece, owner)
            pltpu.make_async_copy(view, view, self.spread_got.at[piece, owner]).wait()
            self.onward_copy(piece, owner, lambda copy: copy.start())

        at_distance(self.me, self.count, distance, pass_on)

    def spread_finish(self, pieces, source=None):
        @pl.loop(0, pieces)
        def _(piece):
            self.own_copies(
                piece, lambda copy: copy.wait_send(), None if source is None else source(piece)
            )
            for distance in range(1, self.count):
                at_distance(
                    self.me, self.count, distance,
                    lambda owner: self.onward_copy(piece, owner, lambda copy: copy.wait_send()),
                )


def line_semaphores(count, pieces):
    return [
        pltpu.SemaphoreType.DMA((pieces, count)),
        pltpu.SemaphoreType.DMA((pieces, count + 1)),
    ], [
        pltpu.SemaphoreType.DMA((pieces, count + 1)),
        pltpu.SemaphoreType.DMA((pieces, count)),
    ]


def gather_kernel(
    count, x_ref, marks_ref, out_ref, marks_out, slots, sent, got, marks_sent, marks_got
):
    me = lax.axis_index("tp")
    height = x_ref.shape[0] // PIECES
    width = x_ref.shape[1]

    def view(piece, owner):
        return out_ref.at[
            pl.ds(pl.multiple_of(piece * height, height), height),
            pl.ds(pl.multiple_of(owner * width, width), width),
        ]

    def source(piece):
        return x_ref.at[pl.ds(pl.multiple_of(piece * height, height), height)]

    line = Line(me, count, None, None, None, view, sent, got)
    peers = peers_along_tp(me, count)
    greet_peers(peers)

    @pl.loop(0, PIECES)
    def _(piece):
        line.spread_start(piece, source(piece))

    marks = Exchange(
        peers, marks_sent, marks_got, lambda _: marks_ref, lambda i: slots.at[i]
    )
    marks.start()
    own = pl.ds(pl.multiple_of(me * width, width), width)
    out_ref[:, own] = x_ref[...]
    marks_out[:, own] = marks_ref[...]
    for distance in range(1, count):

        @pl.loop(0, PIECES)
        def _(piece, distance=distance):
            line.spread_onward(piece, distance)

    marks.wait_arrivals()
    for i in range(1, count):
        owner = lax.rem(me - i + count, count)
        marks_out[:, pl.ds(pl.multiple_of(owner * width, width), width)] = slots[i - 1]
    marks.wait_sent()
    line.spread_finish(PIECES, source)


def gather_features(x, marks, collective_id):
    count = lax.axis_size("tp")
    rows, width = x.shape
    return pl.pallas_call(
        functools.partial(gather_kernel, count),
        out_shape=[
            jax.ShapeDtypeStruct((rows, count * width), x.dtype),
            jax.ShapeDtypeStruct((marks.shape[0], count * width), marks.dtype),
        ],
        in_specs=[pl.BlockSpec(memory_space=pltpu.VMEM)] * 2,
        out_specs=[pl.BlockSpec(memory_space=pltpu.VMEM)] * 2,
        scratch_shapes=[
            pltpu.VMEM((count - 1, *marks.shape), marks.dtype),
            *line_semaphores(count, PIECES)[1],
            pltpu.SemaphoreType.DMA((count - 1,)),
            pltpu.SemaphoreType.DMA((count - 1,)),
        ],
        compiler_params=pltpu.CompilerParams(
            collective_id=collective_id, has_side_effects=True, vmem_limit_bytes=16 << 20
        ),
        cost_estimate=pl.CostEstimate(
            flops=0, bytes_accessed=64 * rows * count * width, transcendentals=0
        ),
        name="gather_features",
    )(x, marks)


def relay_kernel(count, row_step, use_step, sizes, *refs):
    row_in, use_in, row_out, use_out, shared = sizes
    refs = list(refs)

    def take(number):
        taken = refs[:number]
        del refs[:number]
        return taken

    x_ref, sum_weight = take(2)
    use_weight = sum_weight if shared else take(1)[0]
    row_inputs, use_inputs = take(row_in), take(use_in)
    (gathered,) = take(1)
    row_outputs, use_outputs = take(row_out), take(use_out)
    terms, total, slots, sum_sent, sum_got, spread_sent, spread_got = refs
    me = lax.axis_index("tp")
    height = x_ref.shape[0] // PIECES
    own = height // count
    width = sum_weight.shape[0]

    def view(piece, owner):
        return gathered.at[pl.ds(pl.multiple_of(piece * height + owner * own, own), own)]

    line = Line(me, count, slots, sum_sent, sum_got, view, spread_sent, spread_got)
    greet(me, count)

    def piece_rows(piece):
        return pl.ds(pl.multiple_of(piece * height, height), height)

    @pl.loop(0, PIECES + 2)
    def _(step):
        odd = lax.rem(step, 2)

        def term(owner):
            return terms[odd, pl.ds(pl.multiple_of(owner * own, own), own), :]

        @pl.when(step < PIECES)
        def _():
            x = x_ref[piece_rows(step), :]

            @pl.loop(0, width // TILE)
            def _(tile):
                part = pl.ds(pl.multiple_of(tile * TILE, TILE), TILE)
                terms[odd, :, part] = dot_cols(x, sum_weight[part, :])

            line.sum_start(step, term)

        @pl.when((step >= 1) & (step <= PIECES))
        def _():
            piece = step - 1
            total[...] = terms[1 - odd, pl.ds(pl.multiple_of(me * own, own), own), :]
            line.sum_end(piece, total)
            view(piece, me)[...] = row_step(piece, total, row_inputs, row_outputs)
            line.spread_start(piece)

        @pl.when(step >= 2)
        def _():
            for distance in range(2, count):
                line.spread_onward(step - 2, distance)

        @pl.when(step < PIECES)
        def _():
            line.sum_onward(step, term)

        @pl.when((step >= 1) & (step <= PIECES))
        def _():
            line.spread_onward(step - 1, 1)

        @pl.when(step >= 2)
        def _():
            rows = piece_rows(step - 2)
            use_step(rows, gathered[rows, :], use_weight, use_inputs, use_outputs)

    line.sum_finish(PIECES)
    line.spread_finish(PIECES)


def relay(
    x, sum_weight, use_weight, row_inputs, row_step, row_shapes, use_inputs, use_step, use_shapes,
    collective_id, name,
):
    count = lax.axis_size("tp")
    rows = x.shape[0]
    width = sum_weight.shape[0]
    height = rows // PIECES
    own = height // count
    shared = use_weight is None
    operands = [x, sum_weight, *([] if shared else [use_weight]), *row_inputs, *use_inputs]
    shapes = [jax.ShapeDtypeStruct((rows, width), jnp.bfloat16), *row_shapes, *use_shapes]
    sums, spreads = line_semaphores(count, PIECES)
    sizes = (len(row_inputs), len(use_inputs), len(row_shapes), len(use_shapes), shared)
    return pl.pallas_call(
        functools.partial(relay_kernel, count, row_step, use_step, sizes),
        out_shape=shapes,
        in_specs=[pl.BlockSpec(memory_space=pltpu.VMEM)] * len(operands),
        out_specs=[pl.BlockSpec(memory_space=pltpu.VMEM)] * len(shapes),
        scratch_shapes=[
            pltpu.VMEM((2, height, width), jnp.float32),
            pltpu.VMEM((own, width), jnp.float32),
            pltpu.VMEM((PIECES, count + 1, own, width), jnp.bfloat16),
            *sums,
            *spreads,
        ],
        compiler_params=pltpu.CompilerParams(
            collective_id=collective_id, has_side_effects=True, vmem_limit_bytes=60 << 20
        ),
        cost_estimate=pl.CostEstimate(
            flops=100_000_000_000, bytes_accessed=64 * rows * width, transcendentals=0
        ),
        name=name,
    )(*operands)


def own_rows_of(piece, like):
    own = like.shape[0] // PIECES
    return pl.ds(pl.multiple_of(piece * own, own), own)


def first_norm_step(piece, total, inputs, outputs):
    tokens, gains, biases = inputs
    first_norm, normed_one, inverse_one = outputs
    part = own_rows_of(piece, tokens)
    summed = tokens[part, :].astype(jnp.float32) + (total[...] + biases[0:1, :])
    normed, inverse = norm_parts(summed)
    result = normed * gains[0:1, :] + biases[1:2, :]
    first_norm[part, :] = result
    normed_one[part, :] = normed
    inverse_one[part, :] = jnp.broadcast_to(inverse, (inverse.shape[0], 128))
    return result.astype(jnp.bfloat16)


def expand_step(rows, chunk, weight, inputs, outputs):
    (bias,) = inputs
    hidden, activated = outputs

    @pl.loop(0, hidden.shape[1] // TILE)
    def _(tile):
        part = pl.ds(pl.multiple_of(tile * TILE, TILE), TILE)
        values = dot_plain(chunk, weight[:, part]) + bias[:, part]
        hidden[rows, part] = values
        activated[rows, part] = gelu_tanh(values).astype(jnp.bfloat16)


def add_sums(piece, sums, *values):
    @pl.when(piece == 0)
    def _():
        sums[...] = jnp.zeros_like(sums)

    for i, value in enumerate(values):
        sums[i : i + 1, :] += jnp.sum(value, axis=0, keepdims=True)


def second_norm_step(piece, total, inputs, outputs):
    first_norm, out_grad, gains, biases = inputs
    mixed, grad_second, sums = outputs
    part = own_rows_of(piece, first_norm)
    normed, inverse = norm_parts(first_norm[part, :] + total[...] + biases[2:3, :])
    mixed[part, :] = (normed * gains[1:2, :] + biases[3:4, :]).astype(jnp.bfloat16)
    upstream = out_grad[part, :].astype(jnp.float32)
    grad = norm_back(upstream, normed, inverse, gains[1:2, :])
    grad_second[part, :] = grad
    low = grad.astype(jnp.bfloat16)
    add_sums(piece, sums, upstream * normed, upstream, low.astype(jnp.float32))
    return low


def gelu_slope(values):
    scale = math.sqrt(2.0 / math.pi)
    square = values * values
    bend = jnp.tanh(scale * values * (1.0 + 0.044715 * square))
    inner = scale * (1.0 + 3 * 0.044715 * square)
    return 0.5 * (1.0 + bend) + 0.5 * values * (1.0 - bend * bend) * inner


def shrink_step(rows, chunk, weight, inputs, outputs):
    (hidden,) = inputs
    hidden_low, sums = outputs

    @pl.when(rows.start == 0)
    def _():
        sums[...] = jnp.zeros_like(sums)

    @pl.loop(0, hidden.shape[1] // TILE)
    def _(tile):
        part = pl.ds(pl.multiple_of(tile * TILE, TILE), TILE)
        grad = dot_plain(chunk, weight[:, part]) * gelu_slope(hidden[rows, part])
        low = grad.astype(jnp.bfloat16)
        hidden_low[rows, part] = low
        sums[0:1, part] += jnp.sum(low.astype(jnp.float32), axis=0, keepdims=True)


def first_back_step(piece, total, inputs, outputs):
    grad_second, normed_one, inverse_one, gains = inputs
    grad_inner, sums = outputs
    part = own_rows_of(piece, grad_second)
    normed = normed_one[part, :]
    grad_first = grad_second[part, :] + total[...]
    grad = norm_back(grad_first, normed, inverse_one[part, 0:1], gains[0:1, :])
    grad_inner[part, :] = grad
    low = grad.astype(jnp.bfloat16)
    add_sums(piece, sums, grad_first * normed, grad_first, low.astype(jnp.float32))
    return low


def attended_step(rows, chunk, weight, inputs, outputs):
    (attended_grad,) = outputs
    attended_grad[rows, :] = dot_plain(chunk, weight[...]).astype(jnp.bfloat16)


def peers_in_plane(sizes):
    fsdp, ctx = lax.axis_index("fsdp"), lax.axis_index("ctx")
    return [
        {"fsdp": lax.rem(fsdp + i, sizes[0]), "ctx": lax.rem(ctx + j, sizes[1])}
        for i in range(sizes[0])
        for j in range(sizes[1])
        if i or j
    ]


def input_kernel(
    sizes, x_ref, weight, inner_ref, rows_ref, hidden_ref, out_ref, vectors_ref,
    term_ref, total, slots, own_vectors, tp_slots, plane_slots,
    sum_sent, sum_got, tp_sent, tp_got, plane_sent, plane_got,
):
    count = sizes[2]
    me = lax.axis_index("tp")
    height = x_ref.shape[0] // PIECES
    own = height // count
    width = out_ref.shape[1]
    line = Line(me, count, slots, sum_sent, sum_got, None, None, None)
    tp_peers, plane_peers = peers_along_tp(me, count), peers_in_plane(sizes)
    greet_peers(tp_peers + plane_peers)

    def own_part(index):
        return rows_ref.at[:, pl.ds(pl.multiple_of(index * width, width), width)]

    over_tp = Exchange(
        tp_peers, tp_sent, tp_got,
        lambda i: own_part(lax.rem(me + i, count)), lambda i: tp_slots.at[i],
    )
    over_plane = Exchange(
        plane_peers, plane_sent, plane_got, lambda _: own_vectors, lambda i: plane_slots.at[i]
    )
    over_tp.start()

    def terms(piece):
        def term(owner):
            features = pl.ds(pl.multiple_of(owner * width, width), width)
            term_ref[...] = dot_cols(
                x_ref[pl.ds(pl.multiple_of(piece * height, height), height), :],
                weight[features, :],
            )
            inner = inner_ref[pl.ds(pl.multiple_of(piece * own, own), own), features]
            term_ref[pl.ds(pl.multiple_of(me * own, own), own), :] += inner
            return term_ref[...]

        return term

    def pack():
        over_tp.wait_arrivals()
        own_vectors[0:8, :] = own_part(me)[...]
        for i in range(count - 1):
            own_vectors[0:8, :] += tp_slots[i]
        own_vectors[8:, :] = jnp.zeros_like(own_vectors[8:, :])
        hidden_rows = hidden_ref.shape[1] // width
        for i in range(hidden_rows):
            own_vectors[8 + i : 9 + i, :] = hidden_ref[0:1, i * width : (i + 1) * width]
        for i in range(x_ref.shape[1] // width):
            part = x_ref[:, i * width : (i + 1) * width].astype(jnp.float32)
            place = 8 + hidden_rows + i
            own_vectors[place : place + 1, :] = jnp.sum(part, axis=0, keepdims=True)
        over_plane.start()

    @pl.loop(0, PIECES + 1)
    def _(step):
        @pl.when(step < PIECES)
        def _():
            line.sum_start(step, terms(step))
            line.sum_onward(step, terms(step))

        pl.when(step == 1)(pack)

        @pl.when(step >= 1)
        def _():
            piece = step - 1
            total[...] = terms(piece)(me)
            line.sum_end(piece, total)
            rows = pl.ds(pl.multiple_of(piece * height, height), height)
            out_ref[rows, :] = total[...].astype(out_ref.dtype)

    over_plane.wait_arrivals()
    vectors_ref[...] = own_vectors[...]
    for i in range(len(plane_peers)):
        vectors_ref[...] += plane_slots[i]
    over_tp.wait_sent()
    over_plane.wait_sent()
    line.sum_finish(PIECES)


def input_sum(x, weight, inner, row_sums, hidden_sums, collective_id):
    sizes = tuple(lax.axis_size(axis) for axis in ("fsdp", "ctx", "tp"))
    count = sizes[2]
    others = sizes[0] * sizes[1] - 1
    rows = x.shape[0]
    width = weight.shape[0] // count
    height = rows // PIECES
    packed = 8 + -(-(hidden_sums.shape[1] + x.shape[1]) // (8 * width)) * 8
    return pl.pallas_call(
        functools.partial(input_kernel, sizes),
        out_shape=[
            jax.ShapeDtypeStruct((rows, width), jnp.bfloat16),
            jax.ShapeDtypeStruct((packed, width), jnp.float32),
        ],
        in_specs=[pl.BlockSpec(memory_space=pltpu.VMEM)] * 5,
        out_specs=[pl.BlockSpec(memory_space=pltpu.VMEM)] * 2,
        scratch_shapes=[
            pltpu.VMEM((height, width), jnp.float32),
            pltpu.VMEM((height, width), jnp.float32),
            pltpu.VMEM((PIECES, count + 1, height, width), jnp.bfloat16),
            pltpu.VMEM((packed, width), jnp.float32),
            pltpu.VMEM((count - 1, 8, width), jnp.float32),
            pltpu.VMEM((others, packed, width), jnp.float32),
            *line_semaphores(count, PIECES)[0],
            pltpu.SemaphoreType.DMA((count - 1,)),
            pltpu.SemaphoreType.DMA((count - 1,)),
            pltpu.SemaphoreType.DMA((others,)),
            pltpu.SemaphoreType.DMA((others,)),
        ],
        compiler_params=pltpu.CompilerParams(
            collective_id=collective_id, has_side_effects=True, vmem_limit_bytes=40 << 20
        ),
        cost_estimate=pl.CostEstimate(
            flops=60_000_000_000, bytes_accessed=64 * rows * width, transcendentals=0
        ),
        name="input_sum",
    )(x, weight, inner, row_sums, hidden_sums)


def to_own_rows(wide):
    count = lax.axis_size("tp")
    parts = wide.reshape(PIECES, count, -1, wide.shape[1])
    return lax.dynamic_index_in_dim(parts, lax.axis_index("tp"), 1, keepdims=False).reshape(
        -1, wide.shape[1]
    )


def spread_own(block):
    count = lax.axis_size("tp")
    rows, width = block.shape
    parts = block.reshape(PIECES, count, -1, width)
    got = lax.all_to_all(parts, "tp", split_axis=1, concat_axis=1, tiled=True)
    return got.transpose(0, 2, 1, 3).reshape(rows // count, count * width)


def unspread_own(block):
    count = lax.axis_size("tp")
    rows, width = block.shape
    parts = block.reshape(PIECES, -1, count, width // count).transpose(0, 2, 1, 3)
    got = lax.all_to_all(parts, "tp", split_axis=1, concat_axis=1, tiled=True)
    return got.reshape(rows * count, width // count)


def body(
    tokens,
    segments,
    query_weight,
    key_weight,
    value_weight,
    output_weight,
    expand_weight,
    shrink_weight,
    query_bias,
    value_bias,
    hidden_bias,
    norm_gains,
    row_biases,
    out_grad,
):
    rows = tokens.shape[0]
    head_cols = query_weight.shape[1]
    plane = ("fsdp", "ctx")
    ctx_size = lax.axis_size("ctx")
    by_heads = ctx_size == 2 and (head_cols // HD) % 2 == 0

    def weight_rows(weight):
        return lax.all_gather(weight, plane, axis=0, tiled=True)

    wide_qkv = weight_rows(jnp.concatenate([query_weight, key_weight, value_weight], axis=1))
    marks = jnp.concatenate(
        [norm_gains, row_biases, jnp.zeros((10, norm_gains.shape[1]), norm_gains.dtype)]
    )
    wide_tokens, wide_marks = gather_features(tokens, marks, 0)
    gains = wide_marks[:2].astype(jnp.float32)
    biases = wide_marks[2:6].astype(jnp.float32)
    full_output = weight_rows(output_weight)
    full_expand = weight_rows(expand_weight)
    full_shrink = weight_rows(shrink_weight)
    upstream = spread_own(out_grad)

    qkv_bias = jnp.concatenate([query_bias, jnp.zeros_like(query_bias), value_bias])
    qkv = (dot_plain(wide_tokens, wide_qkv) + qkv_bias.astype(jnp.float32)).astype(jnp.bfloat16)
    queries, keys, values = (
        qkv[:, i * head_cols : (i + 1) * head_cols] for i in range(3)
    )
    block_index = lax.axis_index("fsdp") * ctx_size + lax.axis_index("ctx")
    if by_heads:
        queries, keys, values = heads_in(queries), heads_in(keys), heads_in(values)
        stream_ids = lax.dynamic_slice_in_dim(
            segments, lax.axis_index("fsdp") * ctx_size * rows, ctx_size * rows, 0
        )
        bounds = key_bounds(stream_ids, stream_ids, 0)
    else:
        keys, values = padded(keys, WIN), padded(values, WIN)
        ids = jnp.concatenate(
            [
                jnp.full((WIN,), -1, jnp.int32),
                segments,
                jnp.full((WIN,), jnp.iinfo(jnp.int32).max, jnp.int32),
            ]
        )
        key_ids = lax.dynamic_slice_in_dim(ids, block_index * rows, rows + 2 * WIN, 0)
        bounds = key_bounds(key_ids[WIN : WIN + rows], key_ids, WIN)
    attended_heads, lse = attend(queries, keys, values, *bounds)
    attended = heads_out(attended_heads) if by_heads else attended_heads

    own_tokens = to_own_rows(wide_tokens)
    own_rows, features = own_tokens.shape
    hidden_cols = expand_weight.shape[1]

    def shape(extent, kind=jnp.float32):
        return jax.ShapeDtypeStruct(extent, kind)

    own_shape = shape((own_rows, features))
    norm_low, first_norm, normed_one, inverse_one, hidden, activated = relay(
        attended, full_output, full_expand,
        [own_tokens, gains, biases], first_norm_step,
        [own_shape, own_shape, shape((own_rows, 128))],
        [hidden_bias.astype(jnp.float32)[None]], expand_step,
        [shape((rows, hidden_cols)), shape((rows, hidden_cols), jnp.bfloat16)],
        1, "first_norm",
    )
    ffn_low, mixed_own, grad_second, second_sums, hidden_low, hidden_sums = relay(
        activated, full_shrink, None,
        [first_norm, upstream, gains, biases], second_norm_step,
        [shape((own_rows, features), jnp.bfloat16), own_shape, shape((8, features))],
        [hidden], shrink_step,
        [shape((rows, hidden_cols), jnp.bfloat16), shape((8, hidden_cols))],
        2, "second_norm",
    )
    mixed = unspread_own(mixed_own)

    def owner_sum(grad):
        return lax.psum_scatter(
            grad, plane, scatter_dimension=0, tiled=True
        ).astype(jnp.float32)

    hidden_low, shrink_part = lax.optimization_barrier(
        (hidden_low, dot_rows(ffn_low, activated).astype(jnp.bfloat16))
    )
    shrink_grad = owner_sum(shrink_part)
    branch_low, grad_inner, first_sums, attended_grad = relay(
        hidden_low, full_expand, full_output,
        [grad_second, normed_one, inverse_one, gains], first_back_step,
        [own_shape, shape((8, features))],
        [], attended_step,
        [shape((rows, head_cols), jnp.bfloat16)],
        3, "first_back",
    )
    attended_grad, expand_part, output_part = lax.optimization_barrier(
        (
            attended_grad,
            dot_rows(norm_low, hidden_low).astype(jnp.bfloat16),
            dot_rows(branch_low, attended).astype(jnp.bfloat16),
        )
    )
    expand_grad = owner_sum(expand_part)
    output_grad = owner_sum(output_part)

    if by_heads:
        grads = attend_back(
            queries, keys, values, attended_heads, heads_in(attended_grad), lse, *bounds,
            jnp.bfloat16,
        )
        query_low, key_low, value_low = (heads_out(grad) for grad in grads)
    else:
        query_low, key_ext, value_ext = attend_back(
            queries, keys, values, attended_heads, attended_grad, lse, *bounds, jnp.float32
        )

        def fold(ext):
            edges = jnp.concatenate([ext[:WIN], ext[WIN + rows :]], axis=0)
            around = padded(edges, WIN)
            own = ext[WIN : WIN + rows]
            own = own.at[:WIN].add(around[:WIN]).at[rows - WIN :].add(around[3 * WIN :])
            return own.astype(jnp.bfloat16)

        key_low, value_low = fold(key_ext), fold(value_ext)
    qkv_low = jnp.concatenate([query_low, key_low, value_low], axis=1)
    qkv_low, qkv_part = lax.optimization_barrier(
        (qkv_low, dot_rows(wide_tokens, qkv_low).astype(jnp.bfloat16))
    )
    qkv_grad = owner_sum(qkv_part)
    row_sums = jnp.concatenate(
        [
            first_sums[0:1], second_sums[0:1],
            first_sums[2:3], first_sums[1:2], second_sums[2:3], second_sums[1:2],
            jnp.zeros_like(first_sums[:2]),
        ]
    )
    input_grad, vectors = input_sum(qkv_low, wide_qkv, grad_inner, row_sums, hidden_sums[:1], 4)
    hidden_rows = hidden_cols // head_cols
    query_place = 8 + hidden_rows
    return (
        mixed,
        input_grad,
        qkv_grad[:, :head_cols],
        qkv_grad[:, head_cols : 2 * head_cols],
        qkv_grad[:, 2 * head_cols :],
        output_grad,
        expand_grad,
        shrink_grad,
        vectors[query_place],
        vectors[query_place + 2],
        vectors[8:query_place].reshape(-1),
        vectors[:2],
        vectors[2:6],
    )


def solution(mesh):
    rows, whole, cols = P(("fsdp", "ctx"), "tp"), P(), P("tp")
    wide = P(None, "tp")
    return jax.shard_map(
        body,
        mesh=mesh,
        in_specs=(rows, whole) + (rows,) * 6 + (cols,) * 3 + (wide,) * 2 + (rows,),
        out_specs=(rows,) * 8 + (cols,) * 3 + (wide,) * 2,
        check_vma=False,
    )
```

```python
import functools
import math

import jax
import jax.numpy as jnp
from jax import lax
from jax.experimental import pallas as pl
from jax.experimental.pallas import tpu as pltpu
from jax.sharding import PartitionSpec as P

HD = 128
WIN = 1024
QB = 512
KB = 512

epsilon = 1e-06
hidden_floor = -1e30
score_scale = 1.0 / math.sqrt(HD)
log2_e = 1.0 / math.log(2.0)


def dot_plain(left, right):
    return jnp.dot(left, right, preferred_element_type=jnp.float32)


def dot_rows(left, right):
    return lax.dot_general(
        left, right, (((0,), (0,)), ((), ())), preferred_element_type=jnp.float32
    )


def dot_cols(left, right):
    return lax.dot_general(
        left, right, (((1,), (1,)), ((), ())), preferred_element_type=jnp.float32
    )


def attend_kernel(first, last, q_ref, k_ref, v_ref, low_ref, high_ref, out_ref, lse_ref, vt):
    block = pl.program_id(1)
    rows = q_ref.shape[0]

    @pl.when(block == 0)
    def _():
        vt[...] = v_ref[...].T

    queries = q_ref[...]
    low, high = low_ref[...], high_ref[...]
    places = lax.broadcasted_iota(jnp.int32, (KB, rows), 0)

    def step(number, carry):
        top, total, mixed = carry
        start = pl.multiple_of(number * KB, KB)
        scores = dot_cols(k_ref[pl.ds(start, KB), :], queries) * (score_scale * log2_e)
        keep = (places >= low - start) & (places <= high - start)
        scores = jnp.where(keep, scores, hidden_floor)
        new_top = jnp.maximum(top, jnp.max(scores, axis=0, keepdims=True))
        shrink = jnp.exp2(top - new_top)
        powers = jnp.exp2(scores - new_top)
        total = total * shrink + jnp.sum(powers, axis=0, keepdims=True)
        mixed = mixed * shrink + dot_plain(vt[:, pl.ds(start, KB)], powers.astype(jnp.bfloat16))
        return new_top, total, mixed

    top, total, mixed = lax.fori_loop(
        first[block],
        last[block],
        step,
        (
            jnp.full((1, rows), hidden_floor, jnp.float32),
            jnp.zeros((1, rows), jnp.float32),
            jnp.zeros((HD, rows), jnp.float32),
        ),
    )
    out_ref[...] = (mixed / total).T.astype(out_ref.dtype)
    lse_ref[...] = (top + jnp.log2(total))[None]


def attend(queries, keys, values, low, high, first, last):
    rows, width = queries.shape
    span = keys.shape[0]
    heads = width // HD
    return pl.pallas_call(
        attend_kernel,
        out_shape=(
            jax.ShapeDtypeStruct((rows, width), jnp.bfloat16),
            jax.ShapeDtypeStruct((heads, 1, rows), jnp.float32),
        ),
        grid_spec=pltpu.PrefetchScalarGridSpec(
            num_scalar_prefetch=2,
            grid=(heads, rows // QB),
            in_specs=[
                pl.BlockSpec((QB, HD), lambda h, i, *_: (i, h)),
                pl.BlockSpec((span, HD), lambda h, i, *_: (0, h)),
                pl.BlockSpec((span, HD), lambda h, i, *_: (0, h)),
                pl.BlockSpec((1, QB), lambda h, i, *_: (0, i)),
                pl.BlockSpec((1, QB), lambda h, i, *_: (0, i)),
            ],
            out_specs=[
                pl.BlockSpec((QB, HD), lambda h, i, *_: (i, h)),
                pl.BlockSpec((1, 1, QB), lambda h, i, *_: (h, 0, i)),
            ],
            scratch_shapes=[pltpu.VMEM((HD, span), jnp.bfloat16)],
        ),
        compiler_params=pltpu.CompilerParams(vmem_limit_bytes=32 << 20),
        cost_estimate=pl.CostEstimate(
            flops=3 * rows * span * width,
            bytes_accessed=2 * (2 * rows + 2 * span) * width,
            transcendentals=rows * span * heads,
        ),
        name="attend",
    )(first, last, queries, keys, values, low, high)


def attend_back_kernel(
    first, last, q_ref, k_ref, v_ref, o_ref, g_ref, lse_ref, low_ref, high_ref,
    dq_ref, dk_ref, dv_ref, kt, dk_sum, dv_sum,
):
    block = pl.program_id(1)
    rows = q_ref.shape[0]

    @pl.when(block == 0)
    def _():
        kt[...] = k_ref[...].T
        dk_sum[...] = jnp.zeros_like(dk_sum)
        dv_sum[...] = jnp.zeros_like(dv_sum)

    queries = q_ref[...]
    upstream = g_ref[...]
    lse = lse_ref[0]
    low, high = low_ref[...], high_ref[...]
    places = lax.broadcasted_iota(jnp.int32, (KB, rows), 0)
    product = upstream.astype(jnp.float32) * o_ref[...].astype(jnp.float32)
    delta = jnp.sum(product.T, axis=0, keepdims=True)

    def step(number, dq):
        start = pl.multiple_of(number * KB, KB)
        window = pl.ds(start, KB)
        scores = dot_cols(k_ref[window, :], queries) * (score_scale * log2_e)
        keep = (places >= low - start) & (places <= high - start)
        probs = jnp.exp2(jnp.where(keep, scores - lse, hidden_floor))
        prob_grad = dot_cols(v_ref[window, :], upstream)
        score_grad = (probs * (prob_grad - delta)).astype(jnp.bfloat16)
        dv_sum[window, :] += dot_plain(probs.astype(jnp.bfloat16), upstream)
        dk_sum[window, :] += dot_plain(score_grad, queries)
        return dq + dot_plain(kt[:, window], score_grad)

    dq = lax.fori_loop(
        first[block], last[block], step, jnp.zeros((HD, rows), jnp.float32)
    )
    dq_ref[...] = (dq * score_scale).T.astype(dq_ref.dtype)

    @pl.when(block == pl.num_programs(1) - 1)
    def _():
        dk_ref[...] = (dk_sum[...] * score_scale).astype(dk_ref.dtype)
        dv_ref[...] = dv_sum[...].astype(dv_ref.dtype)


def attend_back(queries, keys, values, out, upstream, lse, low, high, first, last, kind):
    rows, width = queries.shape
    span = keys.shape[0]
    heads = width // HD
    row_spec = pl.BlockSpec((QB, HD), lambda h, i, *_: (i, h))
    key_spec = pl.BlockSpec((span, HD), lambda h, i, *_: (0, h))
    mark_spec = pl.BlockSpec((1, QB), lambda h, i, *_: (0, i))
    return pl.pallas_call(
        attend_back_kernel,
        out_shape=(
            jax.ShapeDtypeStruct((rows, width), jnp.bfloat16),
            jax.ShapeDtypeStruct((span, width), kind),
            jax.ShapeDtypeStruct((span, width), kind),
        ),
        grid_spec=pltpu.PrefetchScalarGridSpec(
            num_scalar_prefetch=2,
            grid=(heads, rows // QB),
            in_specs=[
                row_spec, key_spec, key_spec, row_spec, row_spec,
                pl.BlockSpec((1, 1, QB), lambda h, i, *_: (h, 0, i)),
                mark_spec, mark_spec,
            ],
            out_specs=[row_spec, key_spec, key_spec],
            scratch_shapes=[
                pltpu.VMEM((HD, span), jnp.bfloat16),
                pltpu.VMEM((span, HD), jnp.float32),
                pltpu.VMEM((span, HD), jnp.float32),
            ],
        ),
        compiler_params=pltpu.CompilerParams(vmem_limit_bytes=32 << 20),
        cost_estimate=pl.CostEstimate(
            flops=8 * rows * span * width,
            bytes_accessed=2 * (4 * rows + 4 * span) * width,
            transcendentals=rows * span * heads,
        ),
        name="attend_back",
    )(first, last, queries, keys, values, out, upstream, lse, low, high)


def key_bounds(query_ids, key_ids, offset):
    rows, span = query_ids.shape[0], key_ids.shape[0]
    start = jnp.sum(key_ids[:, None] < query_ids[None, :], axis=0, dtype=jnp.int32)
    stop = jnp.sum(key_ids[:, None] <= query_ids[None, :], axis=0, dtype=jnp.int32)
    places = jnp.arange(rows, dtype=jnp.int32) + offset
    low = jnp.maximum(start, places - WIN)
    high = jnp.minimum(stop - 1, places + WIN)
    first = jnp.min(low.reshape(-1, QB), axis=1) // KB
    last = jnp.max(high.reshape(-1, QB), axis=1) // KB + 1
    return low[None], high[None], first, last


def padded(block, width):
    count = lax.axis_size("ctx")
    forward = [(i, i + 1) for i in range(count - 1)]
    backward = [(target, source) for source, target in forward]
    below = lax.ppermute(block[block.shape[0] - width :], "ctx", forward)
    above = lax.ppermute(block[:width], "ctx", backward)
    return jnp.concatenate([below, block, above], axis=0)


def swap_halves(own, other):
    got = lax.ppermute(other, "ctx", [(0, 1), (1, 0)])
    here = lax.axis_index("ctx") == 0
    return jnp.where(here, own, got), jnp.where(here, got, own)


def heads_in(block):
    half = block.shape[1] // 2
    here = lax.axis_index("ctx") == 0
    left, right = block[:, :half], block[:, half:]
    pair = swap_halves(jnp.where(here, left, right), jnp.where(here, right, left))
    return jnp.concatenate(pair, axis=0)


def heads_out(block):
    half = block.shape[0] // 2
    here = lax.axis_index("ctx") == 0
    top, bottom = block[:half], block[half:]
    pair = swap_halves(jnp.where(here, top, bottom), jnp.where(here, bottom, top))
    return jnp.concatenate(pair, axis=1)


def norm_parts(rows):
    mean = jnp.mean(rows, axis=-1, keepdims=True)
    square = jnp.mean(rows * rows, axis=-1, keepdims=True)
    inverse = lax.rsqrt(square - mean * mean + epsilon)
    return (rows - mean) * inverse, inverse


def norm_back(upstream, normed, inverse, gain):
    scaled = upstream * gain
    first_mean = jnp.mean(scaled, axis=-1, keepdims=True)
    second_mean = jnp.mean(scaled * normed, axis=-1, keepdims=True)
    return inverse * (scaled - first_mean - normed * second_mean)


def gelu_tanh(values):
    return jax.nn.gelu(values, approximate=True)


MESH = pl.DeviceIdType.MESH
PIECES = 4
TILE = 512


def greet(me, count):
    barrier = pltpu.get_barrier_semaphore()

    @pl.when(me > 0)
    def _():
        pl.semaphore_signal(barrier, inc=1, device_id={"tp": me - 1}, device_id_type=MESH)

    @pl.when(me < count - 1)
    def _():
        pl.semaphore_signal(barrier, inc=1, device_id={"tp": me + 1}, device_id_type=MESH)

    @pl.when((me == 0) | (me == count - 1))
    def _():
        pl.semaphore_wait(barrier, 1)

    @pl.when((me > 0) & (me < count - 1))
    def _():
        pl.semaphore_wait(barrier, 2)


def peers_along_tp(me, count):
    return [{"tp": lax.rem(me + i, count)} for i in range(1, count)]


def greet_peers(peers):
    barrier = pltpu.get_barrier_semaphore()
    for peer in peers:
        pl.semaphore_signal(barrier, inc=1, device_id=peer, device_id_type=MESH)
    pl.semaphore_wait(barrier, len(peers))


class Exchange:
    def __init__(self, peers, sent, got, source, place):
        self.peers, self.sent, self.got = peers, sent, got
        self.source, self.place = source, place

    def copies(self):
        for i, peer in enumerate(self.peers):
            yield pltpu.make_async_remote_copy(
                src_ref=self.source(i + 1),
                dst_ref=self.place(i),
                send_sem=self.sent.at[i],
                recv_sem=self.got.at[i],
                device_id=peer,
                device_id_type=MESH,
            )

    def start(self):
        for copy in self.copies():
            copy.start()

    def wait_arrivals(self):
        for copy in self.copies():
            copy.wait_recv()

    def wait_sent(self):
        for copy in self.copies():
            copy.wait_send()


def at_distance(me, count, distance, action):
    for index in (me - distance, me + distance):

        @pl.when((index >= 0) & (index < count))
        def _(index=index):
            action(index)


class Line:
    def __init__(self, me, count, sum_slots, sum_sent, sum_got, spread_view, spread_sent, spread_got):
        self.me, self.count = me, count
        self.sum_slots, self.sum_sent, self.sum_got = sum_slots, sum_sent, sum_got
        self.spread_view, self.spread_sent, self.spread_got = spread_view, spread_sent, spread_got

    def sum_copy(self, piece, owner):
        onward = jnp.where(owner > self.me, self.me + 1, self.me - 1)
        place = jnp.where((owner < self.me) & (owner == self.me - 1), self.count, owner)
        return pltpu.make_async_remote_copy(
            src_ref=self.sum_slots.at[piece, owner],
            dst_ref=self.sum_slots.at[piece, place],
            send_sem=self.sum_sent.at[piece, owner],
            recv_sem=self.sum_got.at[piece, place],
            device_id={"tp": onward},
            device_id_type=MESH,
        )

    def sum_arrival(self, piece, place):
        pltpu.make_async_copy(
            self.sum_slots.at[piece, place],
            self.sum_slots.at[piece, place],
            self.sum_got.at[piece, place],
        ).wait()

    def sum_start(self, piece, term):
        me, count = self.me, self.count

        @pl.when((me == 0) | (me == count - 1))
        def _():
            for k in range(count - 1):
                owner = jnp.where(me == 0, count - 1 - k, k)
                self.sum_slots[piece, owner] = term(owner).astype(jnp.bfloat16)
                self.sum_copy(piece, owner).start()

    def sum_onward(self, piece, term):
        me, count = self.me, self.count

        @pl.when((me > 0) & (me < count - 1))
        def _():
            for distance in range(count - 2, 0, -1):

                def pass_on(owner):
                    self.sum_arrival(piece, owner)
                    total = self.sum_slots[piece, owner].astype(jnp.float32) + term(owner)
                    self.sum_slots[piece, owner] = total.astype(jnp.bfloat16)
                    self.sum_copy(piece, owner).start()

                at_distance(me, count, distance, pass_on)

    def sum_end(self, piece, total):
        me, count = self.me, self.count

        @pl.when(me > 0)
        def _():
            self.sum_arrival(piece, me)
            total[...] += self.sum_slots[piece, me].astype(jnp.float32)

        @pl.when(me < count - 1)
        def _():
            self.sum_arrival(piece, count)
            total[...] += self.sum_slots[piece, count].astype(jnp.float32)

    def sum_finish(self, pieces):
        @pl.loop(0, pieces)
        def _(piece):
            for distance in range(1, self.count):
                at_distance(
                    self.me, self.count, distance,
                    lambda owner: self.sum_copy(piece, owner).wait_send(),
                )

    def spread_copy(self, piece, owner, to, sent, source=None):
        return pltpu.make_async_remote_copy(
            src_ref=self.spread_view(piece, owner) if source is None else source,
            dst_ref=self.spread_view(piece, owner),
            send_sem=self.spread_sent.at[piece, sent],
            recv_sem=self.spread_got.at[piece, owner],
            device_id={"tp": to},
            device_id_type=MESH,
        )

    def own_copies(self, piece, action, source=None):
        me, count = self.me, self.count

        @pl.when(me > 0)
        def _():
            action(self.spread_copy(piece, me, me - 1, count, source))

        @pl.when(me < count - 1)
        def _():
            action(self.spread_copy(piece, me, me + 1, me, source))

    def spread_start(self, piece, source=None):
        self.own_copies(piece, lambda copy: copy.start(), source)

    def onward_copy(self, piece, owner, action):
        me, count = self.me, self.count

        @pl.when((owner < me) & (me < count - 1))
        def _():
            action(self.spread_copy(piece, owner, me + 1, owner))

        @pl.when((owner > me) & (me > 0))
        def _():
            action(self.spread_copy(piece, owner, me - 1, owner))

    def spread_onward(self, piece, distance):
        def pass_on(owner):
            view = self.spread_view(piece, owner)
            pltpu.make_async_copy(view, view, self.spread_got.at[piece, owner]).wait()
            self.onward_copy(piece, owner, lambda copy: copy.start())

        at_distance(self.me, self.count, distance, pass_on)

    def spread_finish(self, pieces, source=None):
        @pl.loop(0, pieces)
        def _(piece):
            self.own_copies(
                piece, lambda copy: copy.wait_send(), None if source is None else source(piece)
            )
            for distance in range(1, self.count):
                at_distance(
                    self.me, self.count, distance,
                    lambda owner: self.onward_copy(piece, owner, lambda copy: copy.wait_send()),
                )


def line_semaphores(count, pieces):
    return [
        pltpu.SemaphoreType.DMA((pieces, count)),
        pltpu.SemaphoreType.DMA((pieces, count + 1)),
    ], [
        pltpu.SemaphoreType.DMA((pieces, count + 1)),
        pltpu.SemaphoreType.DMA((pieces, count)),
    ]


def gather_kernel(
    count, x_ref, marks_ref, out_ref, marks_out, slots, sent, got, marks_sent, marks_got
):
    me = lax.axis_index("tp")
    height = x_ref.shape[0] // PIECES
    width = x_ref.shape[1]

    def view(piece, owner):
        return out_ref.at[
            pl.ds(pl.multiple_of(piece * height, height), height),
            pl.ds(pl.multiple_of(owner * width, width), width),
        ]

    def source(piece):
        return x_ref.at[pl.ds(pl.multiple_of(piece * height, height), height)]

    line = Line(me, count, None, None, None, view, sent, got)
    peers = peers_along_tp(me, count)
    greet_peers(peers)

    @pl.loop(0, PIECES)
    def _(piece):
        line.spread_start(piece, source(piece))

    marks = Exchange(
        peers, marks_sent, marks_got, lambda _: marks_ref, lambda i: slots.at[i]
    )
    marks.start()
    own = pl.ds(pl.multiple_of(me * width, width), width)
    out_ref[:, own] = x_ref[...]
    marks_out[:, own] = marks_ref[...]
    for distance in range(1, count):

        @pl.loop(0, PIECES)
        def _(piece, distance=distance):
            line.spread_onward(piece, distance)

    marks.wait_arrivals()
    for i in range(1, count):
        owner = lax.rem(me - i + count, count)
        marks_out[:, pl.ds(pl.multiple_of(owner * width, width), width)] = slots[i - 1]
    marks.wait_sent()
    line.spread_finish(PIECES, source)


def gather_features(x, marks, collective_id):
    count = lax.axis_size("tp")
    rows, width = x.shape
    return pl.pallas_call(
        functools.partial(gather_kernel, count),
        out_shape=[
            jax.ShapeDtypeStruct((rows, count * width), x.dtype),
            jax.ShapeDtypeStruct((marks.shape[0], count * width), marks.dtype),
        ],
        in_specs=[pl.BlockSpec(memory_space=pltpu.VMEM)] * 2,
        out_specs=[pl.BlockSpec(memory_space=pltpu.VMEM)] * 2,
        scratch_shapes=[
            pltpu.VMEM((count - 1, *marks.shape), marks.dtype),
            *line_semaphores(count, PIECES)[1],
            pltpu.SemaphoreType.DMA((count - 1,)),
            pltpu.SemaphoreType.DMA((count - 1,)),
        ],
        compiler_params=pltpu.CompilerParams(
            collective_id=collective_id, has_side_effects=True, vmem_limit_bytes=16 << 20
        ),
        cost_estimate=pl.CostEstimate(
            flops=0, bytes_accessed=64 * rows * count * width, transcendentals=0
        ),
        name="gather_features",
    )(x, marks)


def relay_kernel(count, row_step, use_step, sizes, *refs):
    row_in, use_in, row_out, use_out, shared = sizes
    refs = list(refs)

    def take(number):
        taken = refs[:number]
        del refs[:number]
        return taken

    x_ref, sum_weight = take(2)
    use_weight = sum_weight if shared else take(1)[0]
    row_inputs, use_inputs = take(row_in), take(use_in)
    (gathered,) = take(1)
    row_outputs, use_outputs = take(row_out), take(use_out)
    terms, total, slots, sum_sent, sum_got, spread_sent, spread_got = refs
    me = lax.axis_index("tp")
    height = x_ref.shape[0] // PIECES
    own = height // count
    width = sum_weight.shape[0]

    def view(piece, owner):
        return gathered.at[pl.ds(pl.multiple_of(piece * height + owner * own, own), own)]

    line = Line(me, count, slots, sum_sent, sum_got, view, spread_sent, spread_got)
    greet(me, count)

    def piece_rows(piece):
        return pl.ds(pl.multiple_of(piece * height, height), height)

    @pl.loop(0, PIECES + 2)
    def _(step):
        odd = lax.rem(step, 2)

        def term(owner):
            return terms[odd, pl.ds(pl.multiple_of(owner * own, own), own), :]

        @pl.when(step < PIECES)
        def _():
            x = x_ref[piece_rows(step), :]

            @pl.loop(0, width // TILE)
            def _(tile):
                part = pl.ds(pl.multiple_of(tile * TILE, TILE), TILE)
                terms[odd, :, part] = dot_cols(x, sum_weight[part, :])

            line.sum_start(step, term)

        @pl.when((step >= 1) & (step <= PIECES))
        def _():
            piece = step - 1
            total[...] = terms[1 - odd, pl.ds(pl.multiple_of(me * own, own), own), :]
            line.sum_end(piece, total)
            view(piece, me)[...] = row_step(piece, total, row_inputs, row_outputs)
            line.spread_start(piece)

        @pl.when(step >= 2)
        def _():
            for distance in range(2, count):
                line.spread_onward(step - 2, distance)

        @pl.when(step < PIECES)
        def _():
            line.sum_onward(step, term)

        @pl.when((step >= 1) & (step <= PIECES))
        def _():
            line.spread_onward(step - 1, 1)

        @pl.when(step >= 2)
        def _():
            rows = piece_rows(step - 2)
            use_step(rows, gathered[rows, :], use_weight, use_inputs, use_outputs)

    line.sum_finish(PIECES)
    line.spread_finish(PIECES)


def relay(
    x, sum_weight, use_weight, row_inputs, row_step, row_shapes, use_inputs, use_step, use_shapes,
    collective_id, name,
):
    count = lax.axis_size("tp")
    rows = x.shape[0]
    width = sum_weight.shape[0]
    height = rows // PIECES
    own = height // count
    shared = use_weight is None
    operands = [x, sum_weight, *([] if shared else [use_weight]), *row_inputs, *use_inputs]
    shapes = [jax.ShapeDtypeStruct((rows, width), jnp.bfloat16), *row_shapes, *use_shapes]
    sums, spreads = line_semaphores(count, PIECES)
    sizes = (len(row_inputs), len(use_inputs), len(row_shapes), len(use_shapes), shared)
    return pl.pallas_call(
        functools.partial(relay_kernel, count, row_step, use_step, sizes),
        out_shape=shapes,
        in_specs=[pl.BlockSpec(memory_space=pltpu.VMEM)] * len(operands),
        out_specs=[pl.BlockSpec(memory_space=pltpu.VMEM)] * len(shapes),
        scratch_shapes=[
            pltpu.VMEM((2, height, width), jnp.float32),
            pltpu.VMEM((own, width), jnp.float32),
            pltpu.VMEM((PIECES, count + 1, own, width), jnp.bfloat16),
            *sums,
            *spreads,
        ],
        compiler_params=pltpu.CompilerParams(
            collective_id=collective_id, has_side_effects=True, vmem_limit_bytes=60 << 20
        ),
        cost_estimate=pl.CostEstimate(
            flops=100_000_000_000, bytes_accessed=64 * rows * width, transcendentals=0
        ),
        name=name,
    )(*operands)


def own_rows_of(piece, like):
    own = like.shape[0] // PIECES
    return pl.ds(pl.multiple_of(piece * own, own), own)


def first_norm_step(piece, total, inputs, outputs):
    tokens, gains, biases = inputs
    first_norm, normed_one, inverse_one = outputs
    part = own_rows_of(piece, tokens)
    summed = tokens[part, :].astype(jnp.float32) + (total[...] + biases[0:1, :])
    normed, inverse = norm_parts(summed)
    result = normed * gains[0:1, :] + biases[1:2, :]
    first_norm[part, :] = result
    normed_one[part, :] = normed
    inverse_one[part, :] = jnp.broadcast_to(inverse, (inverse.shape[0], 128))
    return result.astype(jnp.bfloat16)


def expand_step(rows, chunk, weight, inputs, outputs):
    (bias,) = inputs
    hidden, activated = outputs

    @pl.loop(0, hidden.shape[1] // TILE)
    def _(tile):
        part = pl.ds(pl.multiple_of(tile * TILE, TILE), TILE)
        values = dot_plain(chunk, weight[:, part]) + bias[:, part]
        hidden[rows, part] = values
        activated[rows, part] = gelu_tanh(values).astype(jnp.bfloat16)


def add_sums(piece, sums, *values):
    @pl.when(piece == 0)
    def _():
        sums[...] = jnp.zeros_like(sums)

    for i, value in enumerate(values):
        sums[i : i + 1, :] += jnp.sum(value, axis=0, keepdims=True)


def second_norm_step(piece, total, inputs, outputs):
    first_norm, out_grad, gains, biases = inputs
    mixed, grad_second, sums = outputs
    part = own_rows_of(piece, first_norm)
    normed, inverse = norm_parts(first_norm[part, :] + total[...] + biases[2:3, :])
    mixed[part, :] = (normed * gains[1:2, :] + biases[3:4, :]).astype(jnp.bfloat16)
    upstream = out_grad[part, :].astype(jnp.float32)
    grad = norm_back(upstream, normed, inverse, gains[1:2, :])
    grad_second[part, :] = grad
    low = grad.astype(jnp.bfloat16)
    add_sums(piece, sums, upstream * normed, upstream, low.astype(jnp.float32))
    return low


def gelu_slope(values):
    scale = math.sqrt(2.0 / math.pi)
    square = values * values
    bend = jnp.tanh(scale * values * (1.0 + 0.044715 * square))
    inner = scale * (1.0 + 3 * 0.044715 * square)
    return 0.5 * (1.0 + bend) + 0.5 * values * (1.0 - bend * bend) * inner


def shrink_step(rows, chunk, weight, inputs, outputs):
    (hidden,) = inputs
    hidden_low, sums = outputs

    @pl.when(rows.start == 0)
    def _():
        sums[...] = jnp.zeros_like(sums)

    @pl.loop(0, hidden.shape[1] // TILE)
    def _(tile):
        part = pl.ds(pl.multiple_of(tile * TILE, TILE), TILE)
        grad = dot_plain(chunk, weight[:, part]) * gelu_slope(hidden[rows, part])
        low = grad.astype(jnp.bfloat16)
        hidden_low[rows, part] = low
        sums[0:1, part] += jnp.sum(low.astype(jnp.float32), axis=0, keepdims=True)


def first_back_step(piece, total, inputs, outputs):
    grad_second, normed_one, inverse_one, gains = inputs
    grad_inner, sums = outputs
    part = own_rows_of(piece, grad_second)
    normed = normed_one[part, :]
    grad_first = grad_second[part, :] + total[...]
    grad = norm_back(grad_first, normed, inverse_one[part, 0:1], gains[0:1, :])
    grad_inner[part, :] = grad
    low = grad.astype(jnp.bfloat16)
    add_sums(piece, sums, grad_first * normed, grad_first, low.astype(jnp.float32))
    return low


def attended_step(rows, chunk, weight, inputs, outputs):
    (attended_grad,) = outputs
    attended_grad[rows, :] = dot_plain(chunk, weight[...]).astype(jnp.bfloat16)


def peers_in_plane(sizes):
    fsdp, ctx = lax.axis_index("fsdp"), lax.axis_index("ctx")
    return [
        {"fsdp": lax.rem(fsdp + i, sizes[0]), "ctx": lax.rem(ctx + j, sizes[1])}
        for i in range(sizes[0])
        for j in range(sizes[1])
        if i or j
    ]


def input_kernel(
    sizes, x_ref, weight, inner_ref, rows_ref, hidden_ref, out_ref, vectors_ref,
    term_ref, total, slots, own_vectors, tp_slots, plane_slots,
    sum_sent, sum_got, tp_sent, tp_got, plane_sent, plane_got,
):
    count = sizes[2]
    me = lax.axis_index("tp")
    height = x_ref.shape[0] // PIECES
    own = height // count
    width = out_ref.shape[1]
    line = Line(me, count, slots, sum_sent, sum_got, None, None, None)
    tp_peers, plane_peers = peers_along_tp(me, count), peers_in_plane(sizes)
    greet_peers(tp_peers + plane_peers)

    def own_part(index):
        return rows_ref.at[:, pl.ds(pl.multiple_of(index * width, width), width)]

    over_tp = Exchange(
        tp_peers, tp_sent, tp_got,
        lambda i: own_part(lax.rem(me + i, count)), lambda i: tp_slots.at[i],
    )
    over_plane = Exchange(
        plane_peers, plane_sent, plane_got, lambda _: own_vectors, lambda i: plane_slots.at[i]
    )
    over_tp.start()

    def terms(piece):
        def term(owner):
            features = pl.ds(pl.multiple_of(owner * width, width), width)
            term_ref[...] = dot_cols(
                x_ref[pl.ds(pl.multiple_of(piece * height, height), height), :],
                weight[features, :],
            )
            inner = inner_ref[pl.ds(pl.multiple_of(piece * own, own), own), features]
            term_ref[pl.ds(pl.multiple_of(me * own, own), own), :] += inner
            return term_ref[...]

        return term

    def pack():
        over_tp.wait_arrivals()
        own_vectors[0:8, :] = own_part(me)[...]
        for i in range(count - 1):
            own_vectors[0:8, :] += tp_slots[i]
        own_vectors[8:, :] = jnp.zeros_like(own_vectors[8:, :])
        hidden_rows = hidden_ref.shape[1] // width
        for i in range(hidden_rows):
            own_vectors[8 + i : 9 + i, :] = hidden_ref[0:1, i * width : (i + 1) * width]
        for i in range(x_ref.shape[1] // width):
            part = x_ref[:, i * width : (i + 1) * width].astype(jnp.float32)
            place = 8 + hidden_rows + i
            own_vectors[place : place + 1, :] = jnp.sum(part, axis=0, keepdims=True)
        over_plane.start()

    @pl.loop(0, PIECES + 1)
    def _(step):
        @pl.when(step < PIECES)
        def _():
            line.sum_start(step, terms(step))
            line.sum_onward(step, terms(step))

        pl.when(step == 1)(pack)

        @pl.when(step >= 1)
        def _():
            piece = step - 1
            total[...] = terms(piece)(me)
            line.sum_end(piece, total)
            rows = pl.ds(pl.multiple_of(piece * height, height), height)
            out_ref[rows, :] = total[...].astype(out_ref.dtype)

    over_plane.wait_arrivals()
    vectors_ref[...] = own_vectors[...]
    for i in range(len(plane_peers)):
        vectors_ref[...] += plane_slots[i]
    over_tp.wait_sent()
    over_plane.wait_sent()
    line.sum_finish(PIECES)


def input_sum(x, weight, inner, row_sums, hidden_sums, collective_id):
    sizes = tuple(lax.axis_size(axis) for axis in ("fsdp", "ctx", "tp"))
    count = sizes[2]
    others = sizes[0] * sizes[1] - 1
    rows = x.shape[0]
    width = weight.shape[0] // count
    height = rows // PIECES
    packed = 8 + -(-(hidden_sums.shape[1] + x.shape[1]) // (8 * width)) * 8
    return pl.pallas_call(
        functools.partial(input_kernel, sizes),
        out_shape=[
            jax.ShapeDtypeStruct((rows, width), jnp.bfloat16),
            jax.ShapeDtypeStruct((packed, width), jnp.float32),
        ],
        in_specs=[pl.BlockSpec(memory_space=pltpu.VMEM)] * 5,
        out_specs=[pl.BlockSpec(memory_space=pltpu.VMEM)] * 2,
        scratch_shapes=[
            pltpu.VMEM((height, width), jnp.float32),
            pltpu.VMEM((height, width), jnp.float32),
            pltpu.VMEM((PIECES, count + 1, height, width), jnp.bfloat16),
            pltpu.VMEM((packed, width), jnp.float32),
            pltpu.VMEM((count - 1, 8, width), jnp.float32),
            pltpu.VMEM((others, packed, width), jnp.float32),
            *line_semaphores(count, PIECES)[0],
            pltpu.SemaphoreType.DMA((count - 1,)),
            pltpu.SemaphoreType.DMA((count - 1,)),
            pltpu.SemaphoreType.DMA((others,)),
            pltpu.SemaphoreType.DMA((others,)),
        ],
        compiler_params=pltpu.CompilerParams(
            collective_id=collective_id, has_side_effects=True, vmem_limit_bytes=40 << 20
        ),
        cost_estimate=pl.CostEstimate(
            flops=60_000_000_000, bytes_accessed=64 * rows * width, transcendentals=0
        ),
        name="input_sum",
    )(x, weight, inner, row_sums, hidden_sums)


def to_own_rows(wide):
    count = lax.axis_size("tp")
    parts = wide.reshape(PIECES, count, -1, wide.shape[1])
    return lax.dynamic_index_in_dim(parts, lax.axis_index("tp"), 1, keepdims=False).reshape(
        -1, wide.shape[1]
    )


def spread_own(block):
    count = lax.axis_size("tp")
    rows, width = block.shape
    parts = block.reshape(PIECES, count, -1, width)
    got = lax.all_to_all(parts, "tp", split_axis=1, concat_axis=1, tiled=True)
    return got.transpose(0, 2, 1, 3).reshape(rows // count, count * width)


def unspread_own(block):
    count = lax.axis_size("tp")
    rows, width = block.shape
    parts = block.reshape(PIECES, -1, count, width // count).transpose(0, 2, 1, 3)
    got = lax.all_to_all(parts, "tp", split_axis=1, concat_axis=1, tiled=True)
    return got.reshape(rows * count, width // count)


def body(
    tokens,
    segments,
    query_weight,
    key_weight,
    value_weight,
    output_weight,
    expand_weight,
    shrink_weight,
    query_bias,
    value_bias,
    hidden_bias,
    norm_gains,
    row_biases,
    out_grad,
):
    rows = tokens.shape[0]
    head_cols = query_weight.shape[1]
    plane = ("fsdp", "ctx")
    ctx_size = lax.axis_size("ctx")
    by_heads = ctx_size == 2 and (head_cols // HD) % 2 == 0

    def weight_rows(weight):
        return lax.all_gather(weight, plane, axis=0, tiled=True)

    wide_qkv = weight_rows(jnp.concatenate([query_weight, key_weight, value_weight], axis=1))
    marks = jnp.concatenate(
        [norm_gains, row_biases, jnp.zeros((10, norm_gains.shape[1]), norm_gains.dtype)]
    )
    wide_tokens, wide_marks = gather_features(tokens, marks, 0)
    gains = wide_marks[:2].astype(jnp.float32)
    biases = wide_marks[2:6].astype(jnp.float32)
    full_output = weight_rows(output_weight)
    full_expand = weight_rows(expand_weight)
    full_shrink = weight_rows(shrink_weight)
    upstream = spread_own(out_grad)

    qkv_bias = jnp.concatenate([query_bias, jnp.zeros_like(query_bias), value_bias])
    qkv = (dot_plain(wide_tokens, wide_qkv) + qkv_bias.astype(jnp.float32)).astype(jnp.bfloat16)
    queries, keys, values = (
        qkv[:, i * head_cols : (i + 1) * head_cols] for i in range(3)
    )
    block_index = lax.axis_index("fsdp") * ctx_size + lax.axis_index("ctx")
    if by_heads:
        queries, keys, values = heads_in(queries), heads_in(keys), heads_in(values)
        stream_ids = lax.dynamic_slice_in_dim(
            segments, lax.axis_index("fsdp") * ctx_size * rows, ctx_size * rows, 0
        )
        bounds = key_bounds(stream_ids, stream_ids, 0)
    else:
        keys, values = padded(keys, WIN), padded(values, WIN)
        ids = jnp.concatenate(
            [
                jnp.full((WIN,), -1, jnp.int32),
                segments,
                jnp.full((WIN,), jnp.iinfo(jnp.int32).max, jnp.int32),
            ]
        )
        key_ids = lax.dynamic_slice_in_dim(ids, block_index * rows, rows + 2 * WIN, 0)
        bounds = key_bounds(key_ids[WIN : WIN + rows], key_ids, WIN)
    attended_heads, lse = attend(queries, keys, values, *bounds)
    attended = heads_out(attended_heads) if by_heads else attended_heads

    own_tokens = to_own_rows(wide_tokens)
    own_rows, features = own_tokens.shape
    hidden_cols = expand_weight.shape[1]

    def shape(extent, kind=jnp.float32):
        return jax.ShapeDtypeStruct(extent, kind)

    own_shape = shape((own_rows, features))
    norm_low, first_norm, normed_one, inverse_one, hidden, activated = relay(
        attended, full_output, full_expand,
        [own_tokens, gains, biases], first_norm_step,
        [own_shape, own_shape, shape((own_rows, 128))],
        [hidden_bias.astype(jnp.float32)[None]], expand_step,
        [shape((rows, hidden_cols)), shape((rows, hidden_cols), jnp.bfloat16)],
        1, "first_norm",
    )
    ffn_low, mixed_own, grad_second, second_sums, hidden_low, hidden_sums = relay(
        activated, full_shrink, None,
        [first_norm, upstream, gains, biases], second_norm_step,
        [shape((own_rows, features), jnp.bfloat16), own_shape, shape((8, features))],
        [hidden], shrink_step,
        [shape((rows, hidden_cols), jnp.bfloat16), shape((8, hidden_cols))],
        2, "second_norm",
    )
    mixed = unspread_own(mixed_own)

    def owner_sum(grad):
        return lax.psum_scatter(
            grad, plane, scatter_dimension=0, tiled=True
        )

    hidden_low, shrink_part = lax.optimization_barrier(
        (hidden_low, dot_rows(ffn_low, activated).astype(jnp.bfloat16))
    )
    shrink_grad = owner_sum(shrink_part)
    branch_low, grad_inner, first_sums, attended_grad = relay(
        hidden_low, full_expand, full_output,
        [grad_second, normed_one, inverse_one, gains], first_back_step,
        [own_shape, shape((8, features))],
        [], attended_step,
        [shape((rows, head_cols), jnp.bfloat16)],
        3, "first_back",
    )
    attended_grad, shrink_grad, expand_part, output_part = lax.optimization_barrier(
        (
            attended_grad,
            shrink_grad,
            dot_rows(norm_low, hidden_low).astype(jnp.bfloat16),
            dot_rows(branch_low, attended).astype(jnp.bfloat16),
        )
    )
    expand_grad = owner_sum(expand_part)
    output_grad = owner_sum(output_part)

    if by_heads:
        grads = attend_back(
            queries, keys, values, attended_heads, heads_in(attended_grad), lse, *bounds,
            jnp.bfloat16,
        )
        query_low, key_low, value_low = (heads_out(grad) for grad in grads)
    else:
        query_low, key_ext, value_ext = attend_back(
            queries, keys, values, attended_heads, attended_grad, lse, *bounds, jnp.float32
        )

        def fold(ext):
            edges = jnp.concatenate([ext[:WIN], ext[WIN + rows :]], axis=0)
            around = padded(edges, WIN)
            own = ext[WIN : WIN + rows]
            own = own.at[:WIN].add(around[:WIN]).at[rows - WIN :].add(around[3 * WIN :])
            return own.astype(jnp.bfloat16)

        key_low, value_low = fold(key_ext), fold(value_ext)
    qkv_low = jnp.concatenate([query_low, key_low, value_low], axis=1)
    qkv_low, expand_grad, qkv_part = lax.optimization_barrier(
        (qkv_low, expand_grad, dot_rows(wide_tokens, qkv_low).astype(jnp.bfloat16))
    )
    qkv_grad = owner_sum(qkv_part)
    row_sums = jnp.concatenate(
        [
            first_sums[0:1], second_sums[0:1],
            first_sums[2:3], first_sums[1:2], second_sums[2:3], second_sums[1:2],
            jnp.zeros_like(first_sums[:2]),
        ]
    )
    input_grad, vectors = input_sum(qkv_low, wide_qkv, grad_inner, row_sums, hidden_sums[:1], 4)
    hidden_rows = hidden_cols // head_cols
    query_place = 8 + hidden_rows
    return (
        mixed,
        input_grad,
        qkv_grad[:, :head_cols].astype(jnp.float32),
        qkv_grad[:, head_cols : 2 * head_cols].astype(jnp.float32),
        qkv_grad[:, 2 * head_cols :].astype(jnp.float32),
        output_grad.astype(jnp.float32),
        expand_grad.astype(jnp.float32),
        shrink_grad.astype(jnp.float32),
        vectors[query_place],
        vectors[query_place + 2],
        vectors[8:query_place].reshape(-1),
        vectors[:2],
        vectors[2:6],
    )


def solution(mesh):
    rows, whole, cols = P(("fsdp", "ctx"), "tp"), P(), P("tp")
    wide = P(None, "tp")
    return jax.shard_map(
        body,
        mesh=mesh,
        in_specs=(rows, whole) + (rows,) * 6 + (cols,) * 3 + (wide,) * 2 + (rows,),
        out_specs=(rows,) * 8 + (cols,) * 3 + (wide,) * 2,
        check_vma=False,
    )
```

```python
import functools
import math

import jax
import jax.numpy as jnp
from jax import lax
from jax.experimental import pallas as pl
from jax.experimental.pallas import tpu as pltpu
from jax.sharding import PartitionSpec as P

HD = 128
WIN = 1024
QB = 512
KB = 512

epsilon = 1e-06
hidden_floor = -1e30
score_scale = 1.0 / math.sqrt(HD)
log2_e = 1.0 / math.log(2.0)


def dot_plain(left, right):
    return jnp.dot(left, right, preferred_element_type=jnp.float32)


def dot_rows(left, right):
    return lax.dot_general(
        left, right, (((0,), (0,)), ((), ())), preferred_element_type=jnp.float32
    )


def dot_cols(left, right):
    return lax.dot_general(
        left, right, (((1,), (1,)), ((), ())), preferred_element_type=jnp.float32
    )


def attend_kernel(first, last, q_ref, k_ref, v_ref, low_ref, high_ref, out_ref, lse_ref, vt):
    block = pl.program_id(1)
    rows = q_ref.shape[0]

    @pl.when(block == 0)
    def _():
        vt[...] = v_ref[...].T

    queries = q_ref[...]
    low, high = low_ref[...], high_ref[...]
    places = lax.broadcasted_iota(jnp.int32, (KB, rows), 0)

    def step(number, carry):
        top, total, mixed = carry
        start = pl.multiple_of(number * KB, KB)
        scores = dot_cols(k_ref[pl.ds(start, KB), :], queries) * (score_scale * log2_e)
        keep = (places >= low - start) & (places <= high - start)
        scores = jnp.where(keep, scores, hidden_floor)
        new_top = jnp.maximum(top, jnp.max(scores, axis=0, keepdims=True))
        shrink = jnp.exp2(top - new_top)
        powers = jnp.exp2(scores - new_top)
        total = total * shrink + jnp.sum(powers, axis=0, keepdims=True)
        mixed = mixed * shrink + dot_plain(vt[:, pl.ds(start, KB)], powers.astype(jnp.bfloat16))
        return new_top, total, mixed

    top, total, mixed = lax.fori_loop(
        first[block],
        last[block],
        step,
        (
            jnp.full((1, rows), hidden_floor, jnp.float32),
            jnp.zeros((1, rows), jnp.float32),
            jnp.zeros((HD, rows), jnp.float32),
        ),
    )
    out_ref[...] = (mixed / total).T.astype(out_ref.dtype)
    lse_ref[...] = (top + jnp.log2(total))[None]


def attend(queries, keys, values, heads, low, high, first, last, places=(0, 0, 0)):
    rows, span = queries.shape[0], keys.shape[0]
    width = heads * HD
    q_at, k_at, v_at = places
    return pl.pallas_call(
        attend_kernel,
        out_shape=(
            jax.ShapeDtypeStruct((rows, width), jnp.bfloat16),
            jax.ShapeDtypeStruct((heads, 1, rows), jnp.float32),
        ),
        grid_spec=pltpu.PrefetchScalarGridSpec(
            num_scalar_prefetch=2,
            grid=(heads, rows // QB),
            in_specs=[
                pl.BlockSpec((QB, HD), lambda h, i, *_: (i, h + q_at)),
                pl.BlockSpec((span, HD), lambda h, i, *_: (0, h + k_at)),
                pl.BlockSpec((span, HD), lambda h, i, *_: (0, h + v_at)),
                pl.BlockSpec((1, QB), lambda h, i, *_: (0, i)),
                pl.BlockSpec((1, QB), lambda h, i, *_: (0, i)),
            ],
            out_specs=[
                pl.BlockSpec((QB, HD), lambda h, i, *_: (i, h)),
                pl.BlockSpec((1, 1, QB), lambda h, i, *_: (h, 0, i)),
            ],
            scratch_shapes=[pltpu.VMEM((HD, span), jnp.bfloat16)],
        ),
        compiler_params=pltpu.CompilerParams(vmem_limit_bytes=32 << 20),
        cost_estimate=pl.CostEstimate(
            flops=3 * rows * span * width,
            bytes_accessed=2 * (2 * rows + 2 * span) * width,
            transcendentals=rows * span * heads,
        ),
        name="attend",
    )(first, last, queries, keys, values, low, high)


def attend_back_kernel(
    first, last, q_ref, k_ref, v_ref, o_ref, g_ref, lse_ref, low_ref, high_ref,
    dq_ref, dk_ref, dv_ref, kt, dk_sum, dv_sum,
):
    block = pl.program_id(1)
    rows = q_ref.shape[0]

    @pl.when(block == 0)
    def _():
        kt[...] = k_ref[...].T
        dk_sum[...] = jnp.zeros_like(dk_sum)
        dv_sum[...] = jnp.zeros_like(dv_sum)

    queries = q_ref[...]
    upstream = g_ref[...]
    lse = lse_ref[0]
    low, high = low_ref[...], high_ref[...]
    places = lax.broadcasted_iota(jnp.int32, (KB, rows), 0)
    product = upstream.astype(jnp.float32) * o_ref[...].astype(jnp.float32)
    delta = jnp.sum(product.T, axis=0, keepdims=True)

    def step(number, dq):
        start = pl.multiple_of(number * KB, KB)
        window = pl.ds(start, KB)
        scores = dot_cols(k_ref[window, :], queries) * (score_scale * log2_e)
        keep = (places >= low - start) & (places <= high - start)
        probs = jnp.exp2(jnp.where(keep, scores - lse, hidden_floor))
        prob_grad = dot_cols(v_ref[window, :], upstream)
        score_grad = (probs * (prob_grad - delta)).astype(jnp.bfloat16)
        dv_sum[window, :] += dot_plain(probs.astype(jnp.bfloat16), upstream)
        dk_sum[window, :] += dot_plain(score_grad, queries)
        return dq + dot_plain(kt[:, window], score_grad)

    dq = lax.fori_loop(
        first[block], last[block], step, jnp.zeros((HD, rows), jnp.float32)
    )
    dq_ref[...] = (dq * score_scale).T.astype(dq_ref.dtype)

    @pl.when(block == pl.num_programs(1) - 1)
    def _():
        dk_ref[...] = (dk_sum[...] * score_scale).astype(dk_ref.dtype)
        dv_ref[...] = dv_sum[...].astype(dv_ref.dtype)


def attend_back(
    queries, keys, values, out, upstream, lse, low, high, first, last, kind, places=(0, 0, 0)
):
    rows, width = out.shape
    span = keys.shape[0]
    heads = width // HD
    q_at, k_at, v_at = places
    row_spec = pl.BlockSpec((QB, HD), lambda h, i, *_: (i, h))
    key_spec = pl.BlockSpec((span, HD), lambda h, i, *_: (0, h))
    mark_spec = pl.BlockSpec((1, QB), lambda h, i, *_: (0, i))
    return pl.pallas_call(
        attend_back_kernel,
        out_shape=(
            jax.ShapeDtypeStruct((rows, width), jnp.bfloat16),
            jax.ShapeDtypeStruct((span, width), kind),
            jax.ShapeDtypeStruct((span, width), kind),
        ),
        grid_spec=pltpu.PrefetchScalarGridSpec(
            num_scalar_prefetch=2,
            grid=(heads, rows // QB),
            in_specs=[
                pl.BlockSpec((QB, HD), lambda h, i, *_: (i, h + q_at)),
                pl.BlockSpec((span, HD), lambda h, i, *_: (0, h + k_at)),
                pl.BlockSpec((span, HD), lambda h, i, *_: (0, h + v_at)),
                row_spec, row_spec,
                pl.BlockSpec((1, 1, QB), lambda h, i, *_: (h, 0, i)),
                mark_spec, mark_spec,
            ],
            out_specs=[row_spec, key_spec, key_spec],
            scratch_shapes=[
                pltpu.VMEM((HD, span), jnp.bfloat16),
                pltpu.VMEM((span, HD), jnp.float32),
                pltpu.VMEM((span, HD), jnp.float32),
            ],
        ),
        compiler_params=pltpu.CompilerParams(vmem_limit_bytes=32 << 20),
        cost_estimate=pl.CostEstimate(
            flops=8 * rows * span * width,
            bytes_accessed=2 * (4 * rows + 4 * span) * width,
            transcendentals=rows * span * heads,
        ),
        name="attend_back",
    )(first, last, queries, keys, values, out, upstream, lse, low, high)


def key_bounds(query_ids, key_ids, offset):
    rows, span = query_ids.shape[0], key_ids.shape[0]
    start = jnp.sum(key_ids[:, None] < query_ids[None, :], axis=0, dtype=jnp.int32)
    stop = jnp.sum(key_ids[:, None] <= query_ids[None, :], axis=0, dtype=jnp.int32)
    places = jnp.arange(rows, dtype=jnp.int32) + offset
    low = jnp.maximum(start, places - WIN)
    high = jnp.minimum(stop - 1, places + WIN)
    first = jnp.min(low.reshape(-1, QB), axis=1) // KB
    last = jnp.max(high.reshape(-1, QB), axis=1) // KB + 1
    return low[None], high[None], first, last


def padded(block, width):
    count = lax.axis_size("ctx")
    forward = [(i, i + 1) for i in range(count - 1)]
    backward = [(target, source) for source, target in forward]
    below = lax.ppermute(block[block.shape[0] - width :], "ctx", forward)
    above = lax.ppermute(block[:width], "ctx", backward)
    return jnp.concatenate([below, block, above], axis=0)


def norm_parts(rows):
    mean = jnp.mean(rows, axis=-1, keepdims=True)
    square = jnp.mean(rows * rows, axis=-1, keepdims=True)
    inverse = lax.rsqrt(square - mean * mean + epsilon)
    return (rows - mean) * inverse, inverse


def norm_back(upstream, normed, inverse, gain):
    scaled = upstream * gain
    first_mean = jnp.mean(scaled, axis=-1, keepdims=True)
    second_mean = jnp.mean(scaled * normed, axis=-1, keepdims=True)
    return inverse * (scaled - first_mean - normed * second_mean)


def gelu_tanh(values):
    return jax.nn.gelu(values, approximate=True)


MESH = pl.DeviceIdType.MESH
PIECES = 4
TILE = 512


def greet(me, count, others=()):
    barrier = pltpu.get_barrier_semaphore()

    @pl.when(me > 0)
    def _():
        pl.semaphore_signal(barrier, inc=1, device_id={"tp": me - 1}, device_id_type=MESH)

    @pl.when(me < count - 1)
    def _():
        pl.semaphore_signal(barrier, inc=1, device_id={"tp": me + 1}, device_id_type=MESH)

    for other in others:
        pl.semaphore_signal(barrier, inc=1, device_id=other, device_id_type=MESH)

    @pl.when((me == 0) | (me == count - 1))
    def _():
        pl.semaphore_wait(barrier, 1 + len(others))

    @pl.when((me > 0) & (me < count - 1))
    def _():
        pl.semaphore_wait(barrier, 2 + len(others))


def peers_along_tp(me, count):
    return [{"tp": lax.rem(me + i, count)} for i in range(1, count)]


def greet_peers(peers):
    barrier = pltpu.get_barrier_semaphore()
    for peer in peers:
        pl.semaphore_signal(barrier, inc=1, device_id=peer, device_id_type=MESH)
    pl.semaphore_wait(barrier, len(peers))


class Exchange:
    def __init__(self, peers, sent, got, source, place):
        self.peers, self.sent, self.got = peers, sent, got
        self.source, self.place = source, place

    def copies(self):
        for i, peer in enumerate(self.peers):
            yield pltpu.make_async_remote_copy(
                src_ref=self.source(i + 1),
                dst_ref=self.place(i),
                send_sem=self.sent.at[i],
                recv_sem=self.got.at[i],
                device_id=peer,
                device_id_type=MESH,
            )

    def start(self):
        for copy in self.copies():
            copy.start()

    def wait_arrivals(self):
        for copy in self.copies():
            copy.wait_recv()

    def wait_sent(self):
        for copy in self.copies():
            copy.wait_send()


def at_distance(me, count, distance, action):
    for index in (me - distance, me + distance):

        @pl.when((index >= 0) & (index < count))
        def _(index=index):
            action(index)


class Line:
    def __init__(self, me, count, sum_slots, sum_sent, sum_got, spread_view, spread_sent, spread_got):
        self.me, self.count = me, count
        self.sum_slots, self.sum_sent, self.sum_got = sum_slots, sum_sent, sum_got
        self.spread_view, self.spread_sent, self.spread_got = spread_view, spread_sent, spread_got

    def sum_copy(self, piece, owner):
        onward = jnp.where(owner > self.me, self.me + 1, self.me - 1)
        place = jnp.where((owner < self.me) & (owner == self.me - 1), self.count, owner)
        return pltpu.make_async_remote_copy(
            src_ref=self.sum_slots.at[piece, owner],
            dst_ref=self.sum_slots.at[piece, place],
            send_sem=self.sum_sent.at[piece, owner],
            recv_sem=self.sum_got.at[piece, place],
            device_id={"tp": onward},
            device_id_type=MESH,
        )

    def sum_arrival(self, piece, place):
        pltpu.make_async_copy(
            self.sum_slots.at[piece, place],
            self.sum_slots.at[piece, place],
            self.sum_got.at[piece, place],
        ).wait()

    def sum_start(self, piece, term):
        me, count = self.me, self.count

        @pl.when((me == 0) | (me == count - 1))
        def _():
            for k in range(count - 1):
                owner = jnp.where(me == 0, count - 1 - k, k)
                self.sum_slots[piece, owner] = term(owner).astype(jnp.bfloat16)
                self.sum_copy(piece, owner).start()

    def sum_onward(self, piece, term):
        me, count = self.me, self.count

        @pl.when((me > 0) & (me < count - 1))
        def _():
            for distance in range(count - 2, 0, -1):

                def pass_on(owner):
                    self.sum_arrival(piece, owner)
                    total = self.sum_slots[piece, owner].astype(jnp.float32) + term(owner)
                    self.sum_slots[piece, owner] = total.astype(jnp.bfloat16)
                    self.sum_copy(piece, owner).start()

                at_distance(me, count, distance, pass_on)

    def sum_end(self, piece, total):
        me, count = self.me, self.count

        @pl.when(me > 0)
        def _():
            self.sum_arrival(piece, me)
            total[...] += self.sum_slots[piece, me].astype(jnp.float32)

        @pl.when(me < count - 1)
        def _():
            self.sum_arrival(piece, count)
            total[...] += self.sum_slots[piece, count].astype(jnp.float32)

    def sum_finish(self, pieces):
        @pl.loop(0, pieces)
        def _(piece):
            for distance in range(1, self.count):
                at_distance(
                    self.me, self.count, distance,
                    lambda owner: self.sum_copy(piece, owner).wait_send(),
                )

    def spread_copy(self, piece, owner, to, sent, source=None):
        return pltpu.make_async_remote_copy(
            src_ref=self.spread_view(piece, owner) if source is None else source,
            dst_ref=self.spread_view(piece, owner),
            send_sem=self.spread_sent.at[piece, sent],
            recv_sem=self.spread_got.at[piece, owner],
            device_id={"tp": to},
            device_id_type=MESH,
        )

    def own_copies(self, piece, action, source=None):
        me, count = self.me, self.count

        @pl.when(me > 0)
        def _():
            action(self.spread_copy(piece, me, me - 1, count, source))

        @pl.when(me < count - 1)
        def _():
            action(self.spread_copy(piece, me, me + 1, me, source))

    def spread_start(self, piece, source=None):
        self.own_copies(piece, lambda copy: copy.start(), source)

    def onward_copy(self, piece, owner, action):
        me, count = self.me, self.count

        @pl.when((owner < me) & (me < count - 1))
        def _():
            action(self.spread_copy(piece, owner, me + 1, owner))

        @pl.when((owner > me) & (me > 0))
        def _():
            action(self.spread_copy(piece, owner, me - 1, owner))

    def spread_onward(self, piece, distance):
        def pass_on(owner):
            view = self.spread_view(piece, owner)
            pltpu.make_async_copy(view, view, self.spread_got.at[piece, owner]).wait()
            self.onward_copy(piece, owner, lambda copy: copy.start())

        at_distance(self.me, self.count, distance, pass_on)

    def spread_finish(self, pieces, source=None):
        @pl.loop(0, pieces)
        def _(piece):
            self.own_copies(
                piece, lambda copy: copy.wait_send(), None if source is None else source(piece)
            )
            for distance in range(1, self.count):
                at_distance(
                    self.me, self.count, distance,
                    lambda owner: self.onward_copy(piece, owner, lambda copy: copy.wait_send()),
                )


def line_semaphores(count, pieces):
    return [
        pltpu.SemaphoreType.DMA((pieces, count)),
        pltpu.SemaphoreType.DMA((pieces, count + 1)),
    ], [
        pltpu.SemaphoreType.DMA((pieces, count + 1)),
        pltpu.SemaphoreType.DMA((pieces, count)),
    ]


def gather_kernel(
    count, x_ref, marks_ref, out_ref, marks_out, slots, sent, got, marks_sent, marks_got
):
    me = lax.axis_index("tp")
    height = x_ref.shape[0] // PIECES
    width = x_ref.shape[1]

    def view(piece, owner):
        return out_ref.at[
            pl.ds(pl.multiple_of(piece * height, height), height),
            pl.ds(pl.multiple_of(owner * width, width), width),
        ]

    def source(piece):
        return x_ref.at[pl.ds(pl.multiple_of(piece * height, height), height)]

    line = Line(me, count, None, None, None, view, sent, got)
    peers = peers_along_tp(me, count)
    greet_peers(peers)

    @pl.loop(0, PIECES)
    def _(piece):
        line.spread_start(piece, source(piece))

    marks = Exchange(
        peers, marks_sent, marks_got, lambda _: marks_ref, lambda i: slots.at[i]
    )
    marks.start()
    own = pl.ds(pl.multiple_of(me * width, width), width)
    out_ref[:, own] = x_ref[...]
    marks_out[:, own] = marks_ref[...]
    for distance in range(1, count):

        @pl.loop(0, PIECES)
        def _(piece, distance=distance):
            line.spread_onward(piece, distance)

    marks.wait_arrivals()
    for i in range(1, count):
        owner = lax.rem(me - i + count, count)
        marks_out[:, pl.ds(pl.multiple_of(owner * width, width), width)] = slots[i - 1]
    marks.wait_sent()
    line.spread_finish(PIECES, source)


def gather_features(x, marks, collective_id):
    count = lax.axis_size("tp")
    rows, width = x.shape
    return pl.pallas_call(
        functools.partial(gather_kernel, count),
        out_shape=[
            jax.ShapeDtypeStruct((rows, count * width), x.dtype),
            jax.ShapeDtypeStruct((marks.shape[0], count * width), marks.dtype),
        ],
        in_specs=[pl.BlockSpec(memory_space=pltpu.VMEM)] * 2,
        out_specs=[pl.BlockSpec(memory_space=pltpu.VMEM)] * 2,
        scratch_shapes=[
            pltpu.VMEM((count - 1, *marks.shape), marks.dtype),
            *line_semaphores(count, PIECES)[1],
            pltpu.SemaphoreType.DMA((count - 1,)),
            pltpu.SemaphoreType.DMA((count - 1,)),
        ],
        compiler_params=pltpu.CompilerParams(
            collective_id=collective_id, has_side_effects=True, vmem_limit_bytes=16 << 20
        ),
        cost_estimate=pl.CostEstimate(
            flops=0, bytes_accessed=64 * rows * count * width, transcendentals=0
        ),
        name="gather_features",
    )(x, marks)


class Swap:
    def __init__(self, sent, got, source, place):
        self.sent, self.got, self.source, self.place = sent, got, source, place

    def copy(self, piece):
        return pltpu.make_async_remote_copy(
            src_ref=self.source(piece),
            dst_ref=self.place(piece),
            send_sem=self.sent.at[piece],
            recv_sem=self.got.at[piece],
            device_id={"ctx": 1 - lax.axis_index("ctx")},
            device_id_type=MESH,
        )

    def start(self, piece):
        self.copy(piece).start()

    def wait_arrival(self, piece):
        self.copy(piece).wait_recv()

    def wait_sent(self, piece):
        self.copy(piece).wait_send()


class PlaneGather:
    def __init__(self, whole, sent, got):
        self.whole, self.sent, self.got = whole, sent, got
        fsdp, self.ctx = lax.axis_index("fsdp"), lax.axis_index("ctx")
        self.fsdp = fsdp
        self.twin = fsdp + 1 - 2 * lax.rem(fsdp, 2)
        self.along_x = lax.rem(fsdp + 2, 4)
        self.twin_x = lax.rem(self.twin + 2, 4)
        self.core_peer = {"fsdp": self.twin}
        self.x_peer = {"fsdp": self.along_x}
        self.y_peer = {"ctx": 1 - self.ctx}

    def peers(self):
        return [self.core_peer, self.x_peer, self.y_peer]

    def shard(self, fsdp, ctx, half=None):
        height = self.whole.shape[0] // 8
        start = (fsdp * 2 + ctx) * height
        if half is not None:
            height //= 2
            start += half * height
        return self.whole.at[pl.ds(pl.multiple_of(start, height), height)]

    def copy(self, number, view, peer):
        return pltpu.make_async_remote_copy(
            src_ref=view,
            dst_ref=view,
            send_sem=self.sent.at[number],
            recv_sem=self.got.at[number],
            device_id=peer,
            device_id_type=MESH,
        )

    def copies(self):
        own = self.shard(self.fsdp, self.ctx)
        from_x = self.shard(self.along_x, self.ctx)
        from_y = self.shard(self.fsdp, 1 - self.ctx)
        return [
            (own, self.core_peer),
            (own, self.x_peer),
            (own, self.y_peer),
            (from_x, self.core_peer),
            (self.shard(self.along_x, self.ctx, 0), self.y_peer),
            (from_y, self.core_peer),
            (self.shard(self.fsdp, 1 - self.ctx, 1), self.x_peer),
            (self.shard(self.along_x, 1 - self.ctx, 0), self.core_peer),
            (self.shard(self.along_x, 1 - self.ctx, 1), self.core_peer),
        ]

    def arrivals(self):
        return [
            self.shard(self.twin, self.ctx),
            self.shard(self.along_x, self.ctx),
            self.shard(self.fsdp, 1 - self.ctx),
            self.shard(self.twin_x, self.ctx),
            self.shard(self.along_x, 1 - self.ctx, 0),
            self.shard(self.twin, 1 - self.ctx),
            self.shard(self.along_x, 1 - self.ctx, 1),
            self.shard(self.twin_x, 1 - self.ctx, 0),
            self.shard(self.twin_x, 1 - self.ctx, 1),
        ]

    def start(self, *numbers):
        copies = self.copies()
        for number in numbers:
            self.copy(number, *copies[number]).start()

    def wait(self, *numbers):
        arrivals = self.arrivals()
        for number in numbers:
            view = arrivals[number]
            pltpu.make_async_copy(view, view, self.got.at[number]).wait()

    def first(self):
        self.start(1, 2, 0)

    def second(self):
        self.wait(1)
        self.start(4, 3)
        self.wait(2)
        self.start(6, 5)

    def third(self):
        self.wait(4)
        self.start(7)
        self.wait(6)
        self.start(8)

    def last(self):
        self.wait(0, 3, 5, 7, 8)

    def wait_sent(self):
        for number, (view, peer) in enumerate(self.copies()):
            self.copy(number, view, peer).wait_send()


def enter_kernel(
    count, x_ref, marks_ref, query_ref, key_ref, value_ref, bias,
    wide, marks_out, weight, heads,
    mark_slots, stage, sent, got, marks_sent, marks_got,
    weight_sent, weight_got, swap_sent, swap_got,
):
    me, ctx = lax.axis_index("tp"), lax.axis_index("ctx")
    rows, width = x_ref.shape
    height = rows // PIECES
    half = query_ref.shape[1] // 2
    part = 3 * half

    def piece_rows(piece, start=0):
        return pl.ds(pl.multiple_of(start + piece * height, height), height)

    def view(piece, owner):
        return wide.at[piece_rows(piece), pl.ds(pl.multiple_of(owner * width, width), width)]

    gather = PlaneGather(weight, weight_sent, weight_got)
    own_shard = gather.shard(gather.fsdp, ctx)
    for side in range(2):
        for i, ref in enumerate((query_ref, key_ref, value_ref)):
            start = side * part + i * half
            own_shard[:, start : start + half] = ref[:, side * half : (side + 1) * half]
    line = Line(me, count, None, None, None, view, sent, got)
    tp_peers = peers_along_tp(me, count)
    greet_peers(tp_peers + gather.peers())

    def source(piece):
        return x_ref.at[piece_rows(piece)]

    @pl.loop(0, PIECES)
    def _(piece):
        line.spread_start(piece, source(piece))

    gather.first()
    marks = Exchange(
        tp_peers, marks_sent, marks_got, lambda _: marks_ref, lambda i: mark_slots.at[i]
    )
    marks.start()
    own = pl.ds(pl.multiple_of(me * width, width), width)
    wide[:, own] = x_ref[...]
    marks_out[:, own] = marks_ref[...]
    swap = Swap(
        swap_sent, swap_got,
        lambda piece: stage.at[piece_rows(piece)],
        lambda piece: heads.at[piece_rows(piece, ctx * rows)],
    )

    def products(piece, side, place):
        x = wide[piece_rows(piece), :]

        @pl.loop(0, 3)
        def _(tile):
            start = pl.multiple_of(side * part + tile * half, half)
            columns = pl.ds(start, half)
            values = dot_plain(x, weight[:, columns]) + bias[:, columns]
            place[:, pl.ds(pl.multiple_of(tile * half, half), half)] = values.astype(jnp.bfloat16)

    for distance in range(1, count):
        if distance == count - 1:
            gather.last()

        @pl.loop(0, PIECES)
        def _(piece, distance=distance):
            line.spread_onward(piece, distance)
            if distance == count - 1:
                products(piece, 1 - ctx, stage.at[piece_rows(piece)])
                swap.start(piece)
                products(piece, ctx, heads.at[piece_rows(piece, ctx * rows)])

        if distance == 1:
            gather.second()
        if distance == count - 2:
            gather.third()

    marks.wait_arrivals()
    for i in range(1, count):
        owner = lax.rem(me - i + count, count)
        marks_out[:, pl.ds(pl.multiple_of(owner * width, width), width)] = mark_slots[i - 1]

    @pl.loop(0, PIECES)
    def _(piece):
        swap.wait_arrival(piece)
        swap.wait_sent(piece)

    marks.wait_sent()
    gather.wait_sent()
    line.spread_finish(PIECES, source)


def enter(tokens, marks, query_weight, key_weight, value_weight, bias, collective_id):
    count = lax.axis_size("tp")
    rows, width = tokens.shape
    head_cols = query_weight.shape[1]
    plane = 8
    part = 3 * head_cols // 2
    return pl.pallas_call(
        functools.partial(enter_kernel, count),
        out_shape=[
            jax.ShapeDtypeStruct((rows, count * width), tokens.dtype),
            jax.ShapeDtypeStruct((marks.shape[0], count * width), marks.dtype),
            jax.ShapeDtypeStruct((plane * query_weight.shape[0], 2 * part), query_weight.dtype),
            jax.ShapeDtypeStruct((2 * rows, part), jnp.bfloat16),
        ],
        in_specs=[pl.BlockSpec(memory_space=pltpu.VMEM)] * 6,
        out_specs=[pl.BlockSpec(memory_space=pltpu.VMEM)] * 4,
        scratch_shapes=[
            pltpu.VMEM((count - 1, *marks.shape), marks.dtype),
            pltpu.VMEM((rows, part), jnp.bfloat16),
            *line_semaphores(count, PIECES)[1],
            pltpu.SemaphoreType.DMA((count - 1,)),
            pltpu.SemaphoreType.DMA((count - 1,)),
            pltpu.SemaphoreType.DMA((9,)),
            pltpu.SemaphoreType.DMA((9,)),
            pltpu.SemaphoreType.DMA((PIECES,)),
            pltpu.SemaphoreType.DMA((PIECES,)),
        ],
        compiler_params=pltpu.CompilerParams(
            collective_id=collective_id, has_side_effects=True, vmem_limit_bytes=40 << 20
        ),
        cost_estimate=pl.CostEstimate(
            flops=80_000_000_000, bytes_accessed=64 * rows * count * width, transcendentals=0
        ),
        name="enter",
    )(tokens, marks, query_weight, key_weight, value_weight, bias)


def relay_kernel(count, row_step, use_step, sizes, *refs):
    row_in, use_in, row_out, use_out, shared, swap_in, swap_out = sizes
    refs = list(refs)

    def take(number):
        taken = refs[:number]
        del refs[:number]
        return taken

    x_ref, sum_weight = take(2)
    use_weight = sum_weight if shared else take(1)[0]
    row_inputs, use_inputs = take(row_in), take(use_in)
    (gathered,) = take(1)
    row_outputs, use_outputs = take(row_out), take(use_out)
    swapped = take(1)[0] if swap_in or swap_out else None
    terms, total, slots, sum_sent, sum_got, spread_sent, spread_got = take(7)
    me, ctx = lax.axis_index("tp"), lax.axis_index("ctx")
    rows = gathered.shape[0]
    height = rows // PIECES
    own = height // count
    width = sum_weight.shape[0]

    def piece_rows(piece, start=0):
        return pl.ds(pl.multiple_of(start + piece * height, height), height)

    def view(piece, owner):
        return gathered.at[pl.ds(pl.multiple_of(piece * height + owner * own, own), own)]

    line = Line(me, count, slots, sum_sent, sum_got, view, spread_sent, spread_got)
    greet(me, count, [{"ctx": 1 - ctx}] if swap_in or swap_out else [])
    swap = None
    if swap_in:
        half = x_ref.shape[1]
        own_half = pl.ds(pl.multiple_of(ctx * half, half), half)
        swap = Swap(
            *refs,
            lambda piece: x_ref.at[piece_rows(piece, (1 - ctx) * rows)],
            lambda piece: swapped.at[piece_rows(piece), own_half],
        )

        @pl.loop(0, PIECES)
        def _(piece):
            swap.start(piece)
            swapped[piece_rows(piece), own_half] = x_ref[piece_rows(piece, ctx * rows), :]

    if swap_out:
        stage, swap_sent, swap_got = refs
        half = swapped.shape[1]
        swap = Swap(
            swap_sent, swap_got,
            lambda piece: stage.at[piece_rows(piece)],
            lambda piece: swapped.at[piece_rows(piece, ctx * rows)],
        )

    @pl.loop(0, PIECES + 2)
    def _(step):
        odd = lax.rem(step, 2)

        def term(owner):
            return terms[odd, pl.ds(pl.multiple_of(owner * own, own), own), :]

        @pl.when(step < PIECES)
        def _():
            if swap_in:
                swap.wait_arrival(step)
            x = (swapped if swap_in else x_ref)[piece_rows(step), :]

            @pl.loop(0, width // TILE)
            def _(tile):
                part = pl.ds(pl.multiple_of(tile * TILE, TILE), TILE)
                terms[odd, :, part] = dot_cols(x, sum_weight[part, :])

            line.sum_start(step, term)

        @pl.when((step >= 1) & (step <= PIECES))
        def _():
            piece = step - 1
            total[...] = terms[1 - odd, pl.ds(pl.multiple_of(me * own, own), own), :]
            line.sum_end(piece, total)
            view(piece, me)[...] = row_step(piece, total, row_inputs, row_outputs)
            line.spread_start(piece)

        @pl.when(step >= 2)
        def _():
            for distance in range(2, count):
                line.spread_onward(step - 2, distance)

        @pl.when(step < PIECES)
        def _():
            line.sum_onward(step, term)

        @pl.when((step >= 1) & (step <= PIECES))
        def _():
            line.spread_onward(step - 1, 1)

        @pl.when(step >= 2)
        def _():
            piece = step - 2
            part = piece_rows(piece)
            result = use_step(part, gathered[part, :], use_weight, use_inputs, use_outputs)
            if swap_out:
                here = ctx == 0
                left, right = result[:, :half], result[:, half:]
                stage[part, :] = jnp.where(here, right, left)
                swap.start(piece)
                swapped[piece_rows(piece, ctx * rows), :] = jnp.where(here, left, right)

    if swap is not None:

        @pl.loop(0, PIECES)
        def _(piece):
            if swap_out:
                swap.wait_arrival(piece)
            swap.wait_sent(piece)

    line.sum_finish(PIECES)
    line.spread_finish(PIECES)


def relay(
    x, sum_weight, use_weight, row_inputs, row_step, row_shapes, use_inputs, use_step, use_shapes,
    collective_id, name, rows, swap_in=None, swap_out=None,
):
    count = lax.axis_size("tp")
    width = sum_weight.shape[0]
    height = rows // PIECES
    own = height // count
    shared = use_weight is None
    operands = [x, sum_weight, *([] if shared else [use_weight]), *row_inputs, *use_inputs]
    shapes = [jax.ShapeDtypeStruct((rows, width), jnp.bfloat16), *row_shapes, *use_shapes]
    shapes += [shape for shape in (swap_in, swap_out) if shape is not None]
    sums, spreads = line_semaphores(count, PIECES)
    swaps = []
    if swap_out is not None:
        swaps.append(pltpu.VMEM((rows, swap_out.shape[1]), swap_out.dtype))
    if swap_in is not None or swap_out is not None:
        swaps += [pltpu.SemaphoreType.DMA((PIECES,))] * 2
    sizes = (
        len(row_inputs), len(use_inputs), len(row_shapes), len(use_shapes), shared,
        swap_in is not None, swap_out is not None,
    )
    return pl.pallas_call(
        functools.partial(relay_kernel, count, row_step, use_step, sizes),
        out_shape=shapes,
        in_specs=[pl.BlockSpec(memory_space=pltpu.VMEM)] * len(operands),
        out_specs=[pl.BlockSpec(memory_space=pltpu.VMEM)] * len(shapes),
        scratch_shapes=[
            pltpu.VMEM((2, height, width), jnp.float32),
            pltpu.VMEM((own, width), jnp.float32),
            pltpu.VMEM((PIECES, count + 1, own, width), jnp.bfloat16),
            *sums,
            *spreads,
            *swaps,
        ],
        compiler_params=pltpu.CompilerParams(
            collective_id=collective_id, has_side_effects=True, vmem_limit_bytes=60 << 20
        ),
        cost_estimate=pl.CostEstimate(
            flops=100_000_000_000, bytes_accessed=64 * rows * width, transcendentals=0
        ),
        name=name,
    )(*operands)


def own_rows_of(piece, like):
    own = like.shape[0] // PIECES
    return pl.ds(pl.multiple_of(piece * own, own), own)


def first_norm_step(piece, total, inputs, outputs):
    tokens, gains, biases = inputs
    first_norm, normed_one, inverse_one = outputs
    part = own_rows_of(piece, tokens)
    summed = tokens[part, :].astype(jnp.float32) + (total[...] + biases[0:1, :])
    normed, inverse = norm_parts(summed)
    result = normed * gains[0:1, :] + biases[1:2, :]
    first_norm[part, :] = result
    normed_one[part, :] = normed
    inverse_one[part, :] = jnp.broadcast_to(inverse, (inverse.shape[0], 128))
    return result.astype(jnp.bfloat16)


def expand_step(rows, chunk, weight, inputs, outputs):
    (bias,) = inputs
    hidden, activated = outputs

    @pl.loop(0, hidden.shape[1] // TILE)
    def _(tile):
        part = pl.ds(pl.multiple_of(tile * TILE, TILE), TILE)
        values = dot_plain(chunk, weight[:, part]) + bias[:, part]
        hidden[rows, part] = values
        activated[rows, part] = gelu_tanh(values).astype(jnp.bfloat16)


def add_sums(piece, sums, *values):
    @pl.when(piece == 0)
    def _():
        sums[...] = jnp.zeros_like(sums)

    for i, value in enumerate(values):
        sums[i : i + 1, :] += jnp.sum(value, axis=0, keepdims=True)


def second_norm_step(piece, total, inputs, outputs):
    first_norm, out_grad, gains, biases = inputs
    mixed, grad_second, sums = outputs
    part = own_rows_of(piece, first_norm)
    normed, inverse = norm_parts(first_norm[part, :] + total[...] + biases[2:3, :])
    mixed[part, :] = (normed * gains[1:2, :] + biases[3:4, :]).astype(jnp.bfloat16)
    upstream = out_grad[part, :].astype(jnp.float32)
    grad = norm_back(upstream, normed, inverse, gains[1:2, :])
    grad_second[part, :] = grad
    low = grad.astype(jnp.bfloat16)
    add_sums(piece, sums, upstream * normed, upstream, low.astype(jnp.float32))
    return low


def gelu_slope(values):
    scale = math.sqrt(2.0 / math.pi)
    square = values * values
    bend = jnp.tanh(scale * values * (1.0 + 0.044715 * square))
    inner = scale * (1.0 + 3 * 0.044715 * square)
    return 0.5 * (1.0 + bend) + 0.5 * values * (1.0 - bend * bend) * inner


def shrink_step(rows, chunk, weight, inputs, outputs):
    (hidden,) = inputs
    hidden_low, sums = outputs

    @pl.when(rows.start == 0)
    def _():
        sums[...] = jnp.zeros_like(sums)

    @pl.loop(0, hidden.shape[1] // TILE)
    def _(tile):
        part = pl.ds(pl.multiple_of(tile * TILE, TILE), TILE)
        grad = dot_plain(chunk, weight[:, part]) * gelu_slope(hidden[rows, part])
        low = grad.astype(jnp.bfloat16)
        hidden_low[rows, part] = low
        sums[0:1, part] += jnp.sum(low.astype(jnp.float32), axis=0, keepdims=True)


def first_back_step(piece, total, inputs, outputs):
    grad_second, normed_one, inverse_one, gains = inputs
    grad_inner, sums = outputs
    part = own_rows_of(piece, grad_second)
    normed = normed_one[part, :]
    grad_first = grad_second[part, :] + total[...]
    grad = norm_back(grad_first, normed, inverse_one[part, 0:1], gains[0:1, :])
    grad_inner[part, :] = grad
    low = grad.astype(jnp.bfloat16)
    add_sums(piece, sums, grad_first * normed, grad_first, low.astype(jnp.float32))
    return low


def attended_step(rows, chunk, weight, inputs, outputs):
    result = dot_plain(chunk, weight[...]).astype(jnp.bfloat16)
    if outputs:
        outputs[0][rows, :] = result
    return result


def peers_in_plane(sizes):
    fsdp, ctx = lax.axis_index("fsdp"), lax.axis_index("ctx")
    return [
        {"fsdp": lax.rem(fsdp + i, sizes[0]), "ctx": lax.rem(ctx + j, sizes[1])}
        for i in range(sizes[0])
        for j in range(sizes[1])
        if i or j
    ]


def input_kernel(
    sizes, x_ref, weight, inner_ref, rows_ref, hidden_ref, out_ref, vectors_ref,
    term_ref, total, slots, own_vectors, tp_slots, plane_slots,
    sum_sent, sum_got, tp_sent, tp_got, plane_sent, plane_got,
):
    count = sizes[2]
    me = lax.axis_index("tp")
    height = x_ref.shape[0] // PIECES
    own = height // count
    width = out_ref.shape[1]
    line = Line(me, count, slots, sum_sent, sum_got, None, None, None)
    tp_peers, plane_peers = peers_along_tp(me, count), peers_in_plane(sizes)
    greet_peers(tp_peers + plane_peers)

    def own_part(index):
        return rows_ref.at[:, pl.ds(pl.multiple_of(index * width, width), width)]

    over_tp = Exchange(
        tp_peers, tp_sent, tp_got,
        lambda i: own_part(lax.rem(me + i, count)), lambda i: tp_slots.at[i],
    )
    over_plane = Exchange(
        plane_peers, plane_sent, plane_got, lambda _: own_vectors, lambda i: plane_slots.at[i]
    )
    over_tp.start()

    def terms(piece):
        def term(owner):
            features = pl.ds(pl.multiple_of(owner * width, width), width)
            term_ref[...] = dot_cols(
                x_ref[pl.ds(pl.multiple_of(piece * height, height), height), :],
                weight[features, :],
            )
            inner = inner_ref[pl.ds(pl.multiple_of(piece * own, own), own), features]
            term_ref[pl.ds(pl.multiple_of(me * own, own), own), :] += inner
            return term_ref[...]

        return term

    def pack():
        over_tp.wait_arrivals()
        own_vectors[0:8, :] = own_part(me)[...]
        for i in range(count - 1):
            own_vectors[0:8, :] += tp_slots[i]
        own_vectors[8:, :] = jnp.zeros_like(own_vectors[8:, :])
        hidden_rows = hidden_ref.shape[1] // width
        for i in range(hidden_rows):
            own_vectors[8 + i : 9 + i, :] = hidden_ref[0:1, i * width : (i + 1) * width]
        for i in range(x_ref.shape[1] // width):
            part = x_ref[:, i * width : (i + 1) * width].astype(jnp.float32)
            place = 8 + hidden_rows + i
            own_vectors[place : place + 1, :] = jnp.sum(part, axis=0, keepdims=True)
        over_plane.start()

    @pl.loop(0, PIECES + 1)
    def _(step):
        @pl.when(step < PIECES)
        def _():
            line.sum_start(step, terms(step))
            line.sum_onward(step, terms(step))

        pl.when(step == 1)(pack)

        @pl.when(step >= 1)
        def _():
            piece = step - 1
            total[...] = terms(piece)(me)
            line.sum_end(piece, total)
            rows = pl.ds(pl.multiple_of(piece * height, height), height)
            out_ref[rows, :] = total[...].astype(out_ref.dtype)

    over_plane.wait_arrivals()
    vectors_ref[...] = own_vectors[...]
    for i in range(len(plane_peers)):
        vectors_ref[...] += plane_slots[i]
    over_tp.wait_sent()
    over_plane.wait_sent()
    line.sum_finish(PIECES)


def input_sum(x, weight, inner, row_sums, hidden_sums, collective_id):
    sizes = tuple(lax.axis_size(axis) for axis in ("fsdp", "ctx", "tp"))
    count = sizes[2]
    others = sizes[0] * sizes[1] - 1
    rows = x.shape[0]
    width = weight.shape[0] // count
    height = rows // PIECES
    packed = 8 + -(-(hidden_sums.shape[1] + x.shape[1]) // (8 * width)) * 8
    return pl.pallas_call(
        functools.partial(input_kernel, sizes),
        out_shape=[
            jax.ShapeDtypeStruct((rows, width), jnp.bfloat16),
            jax.ShapeDtypeStruct((packed, width), jnp.float32),
        ],
        in_specs=[pl.BlockSpec(memory_space=pltpu.VMEM)] * 5,
        out_specs=[pl.BlockSpec(memory_space=pltpu.VMEM)] * 2,
        scratch_shapes=[
            pltpu.VMEM((height, width), jnp.float32),
            pltpu.VMEM((height, width), jnp.float32),
            pltpu.VMEM((PIECES, count + 1, height, width), jnp.bfloat16),
            pltpu.VMEM((packed, width), jnp.float32),
            pltpu.VMEM((count - 1, 8, width), jnp.float32),
            pltpu.VMEM((others, packed, width), jnp.float32),
            *line_semaphores(count, PIECES)[0],
            pltpu.SemaphoreType.DMA((count - 1,)),
            pltpu.SemaphoreType.DMA((count - 1,)),
            pltpu.SemaphoreType.DMA((others,)),
            pltpu.SemaphoreType.DMA((others,)),
        ],
        compiler_params=pltpu.CompilerParams(
            collective_id=collective_id, has_side_effects=True, vmem_limit_bytes=40 << 20
        ),
        cost_estimate=pl.CostEstimate(
            flops=60_000_000_000, bytes_accessed=64 * rows * width, transcendentals=0
        ),
        name="input_sum",
    )(x, weight, inner, row_sums, hidden_sums)


def to_own_rows(wide):
    count = lax.axis_size("tp")
    parts = wide.reshape(PIECES, count, -1, wide.shape[1])
    return lax.dynamic_index_in_dim(parts, lax.axis_index("tp"), 1, keepdims=False).reshape(
        -1, wide.shape[1]
    )


def spread_own(block):
    count = lax.axis_size("tp")
    rows, width = block.shape
    parts = block.reshape(PIECES, count, -1, width)
    got = lax.all_to_all(parts, "tp", split_axis=1, concat_axis=1, tiled=True)
    return got.transpose(0, 2, 1, 3).reshape(rows // count, count * width)


def unspread_own(block):
    count = lax.axis_size("tp")
    rows, width = block.shape
    parts = block.reshape(PIECES, -1, count, width // count).transpose(0, 2, 1, 3)
    got = lax.all_to_all(parts, "tp", split_axis=1, concat_axis=1, tiled=True)
    return got.reshape(rows * count, width // count)


def body(
    tokens,
    segments,
    query_weight,
    key_weight,
    value_weight,
    output_weight,
    expand_weight,
    shrink_weight,
    query_bias,
    value_bias,
    hidden_bias,
    norm_gains,
    row_biases,
    out_grad,
):
    rows = tokens.shape[0]
    head_cols = query_weight.shape[1]
    heads = head_cols // HD
    plane = ("fsdp", "ctx")
    plane_sizes = tuple(lax.axis_size(axis) for axis in plane)
    by_heads = plane_sizes == (4, 2) and heads % 2 == 0

    def weight_rows(weight):
        return lax.all_gather(weight, plane, axis=0, tiled=True)

    marks = jnp.concatenate(
        [norm_gains, row_biases, jnp.zeros((10, norm_gains.shape[1]), norm_gains.dtype)]
    )
    block_index = lax.axis_index("fsdp") * plane_sizes[1] + lax.axis_index("ctx")
    qkv_bias = jnp.stack([query_bias, jnp.zeros_like(query_bias), value_bias])
    qkv_bias = qkv_bias.astype(jnp.float32)
    if by_heads:
        half_bias = qkv_bias.reshape(3, 2, -1).transpose(1, 0, 2).reshape(1, -1)
        wide_tokens, wide_marks, wide_qkv, qkv_heads = enter(
            tokens, marks, query_weight, key_weight, value_weight, half_bias, 0
        )
        queries = keys = values = qkv_heads
        own_heads = heads // 2
        stream_rows = plane_sizes[1] * rows
        stream_ids = lax.dynamic_slice_in_dim(
            segments, lax.axis_index("fsdp") * stream_rows, stream_rows, 0
        )
        bounds = key_bounds(stream_ids, stream_ids, 0)
    else:
        wide_qkv = weight_rows(jnp.concatenate([query_weight, key_weight, value_weight], axis=1))
        wide_tokens, wide_marks = gather_features(tokens, marks, 0)
        qkv = dot_plain(wide_tokens, wide_qkv) + qkv_bias.reshape(1, -1)
        queries, keys, values = jnp.split(qkv.astype(jnp.bfloat16), 3, axis=1)
        own_heads = heads
        keys, values = padded(keys, WIN), padded(values, WIN)
        ids = jnp.concatenate(
            [
                jnp.full((WIN,), -1, jnp.int32),
                segments,
                jnp.full((WIN,), jnp.iinfo(jnp.int32).max, jnp.int32),
            ]
        )
        key_ids = lax.dynamic_slice_in_dim(ids, block_index * rows, rows + 2 * WIN, 0)
        bounds = key_bounds(key_ids[WIN : WIN + rows], key_ids, WIN)
    places = (0, own_heads, 2 * own_heads) if by_heads else (0, 0, 0)
    gains = wide_marks[:2].astype(jnp.float32)
    biases = wide_marks[2:6].astype(jnp.float32)
    full_output = weight_rows(output_weight)
    full_expand = weight_rows(expand_weight)
    full_shrink = weight_rows(shrink_weight)
    attended_heads, lse = attend(queries, keys, values, own_heads, *bounds, places)
    attended_heads, out_grad = lax.optimization_barrier((attended_heads, out_grad))
    upstream = spread_own(out_grad)

    own_tokens = to_own_rows(wide_tokens)
    own_rows, features = own_tokens.shape
    hidden_cols = expand_weight.shape[1]

    def shape(extent, kind=jnp.float32):
        return jax.ShapeDtypeStruct(extent, kind)

    own_shape = shape((own_rows, features))
    norm_low, first_norm, normed_one, inverse_one, hidden, activated, *swapped = relay(
        attended_heads, full_output, full_expand,
        [own_tokens, gains, biases], first_norm_step,
        [own_shape, own_shape, shape((own_rows, 128))],
        [hidden_bias.astype(jnp.float32)[None]], expand_step,
        [shape((rows, hidden_cols)), shape((rows, hidden_cols), jnp.bfloat16)],
        1, "first_norm", rows,
        swap_in=shape((rows, head_cols), jnp.bfloat16) if by_heads else None,
    )
    attended = swapped[0] if by_heads else attended_heads
    ffn_low, mixed_own, grad_second, second_sums, hidden_low, hidden_sums = relay(
        activated, full_shrink, None,
        [first_norm, upstream, gains, biases], second_norm_step,
        [shape((own_rows, features), jnp.bfloat16), own_shape, shape((8, features))],
        [hidden], shrink_step,
        [shape((rows, hidden_cols), jnp.bfloat16), shape((8, hidden_cols))],
        2, "second_norm", rows,
    )
    mixed = unspread_own(mixed_own)

    def owner_sum(grad):
        return lax.psum_scatter(
            grad, plane, scatter_dimension=0, tiled=True
        )

    hidden_low, shrink_part = lax.optimization_barrier(
        (hidden_low, dot_rows(ffn_low, activated).astype(jnp.bfloat16))
    )
    shrink_grad = owner_sum(shrink_part)
    branch_low, grad_inner, first_sums, attended_grad = relay(
        hidden_low, full_expand, full_output,
        [grad_second, normed_one, inverse_one, gains], first_back_step,
        [own_shape, shape((8, features))],
        [], attended_step,
        [] if by_heads else [shape((rows, head_cols), jnp.bfloat16)],
        3, "first_back", rows,
        swap_out=shape((2 * rows, head_cols // 2), jnp.bfloat16) if by_heads else None,
    )
    attended_grad, shrink_grad, expand_part, output_part = lax.optimization_barrier(
        (
            attended_grad,
            shrink_grad,
            dot_rows(norm_low, hidden_low).astype(jnp.bfloat16),
            dot_rows(branch_low, attended).astype(jnp.bfloat16),
        )
    )
    expand_grad = owner_sum(expand_part)
    output_grad = owner_sum(output_part)

    if by_heads:
        grads = attend_back(
            queries, keys, values, attended_heads, attended_grad, lse, *bounds,
            jnp.bfloat16, places,
        )
        halves = jnp.concatenate(grads, axis=1).reshape(2, rows, -1)
        first = lax.axis_index("ctx") == 0
        mine, other = (jnp.where(first, halves[i], halves[1 - i]) for i in range(2))
        other = lax.ppermute(other, "ctx", [(0, 1), (1, 0)])
        qkv_low = jnp.concatenate(
            [jnp.where(first, mine, other), jnp.where(first, other, mine)], axis=1
        )
    else:
        query_low, key_ext, value_ext = attend_back(
            queries, keys, values, attended_heads, attended_grad, lse, *bounds, jnp.float32
        )

        def fold(ext):
            edges = jnp.concatenate([ext[:WIN], ext[WIN + rows :]], axis=0)
            around = padded(edges, WIN)
            own = ext[WIN : WIN + rows]
            own = own.at[:WIN].add(around[:WIN]).at[rows - WIN :].add(around[3 * WIN :])
            return own.astype(jnp.bfloat16)

        qkv_low = jnp.concatenate([query_low, fold(key_ext), fold(value_ext)], axis=1)
    qkv_low, expand_grad, qkv_part = lax.optimization_barrier(
        (qkv_low, expand_grad, dot_rows(wide_tokens, qkv_low).astype(jnp.bfloat16))
    )
    qkv_grad = owner_sum(qkv_part)
    row_sums = jnp.concatenate(
        [
            first_sums[0:1], second_sums[0:1],
            first_sums[2:3], first_sums[1:2], second_sums[2:3], second_sums[1:2],
            jnp.zeros_like(first_sums[:2]),
        ]
    )
    input_grad, vectors = input_sum(qkv_low, wide_qkv, grad_inner, row_sums, hidden_sums[:1], 4)
    hidden_rows = hidden_cols // head_cols
    sides = 2 if by_heads else 1

    def by_kind(columns):
        parts = columns.reshape(-1, sides, 3, head_cols // sides)
        return [parts[:, :, i].reshape(-1, head_cols) for i in range(3)]

    query_grad, key_grad, value_grad = by_kind(qkv_grad.astype(jnp.float32))
    query_sum, _, value_sum = by_kind(
        vectors[8 + hidden_rows : 8 + hidden_rows + 3].reshape(1, -1)
    )
    return (
        mixed,
        input_grad,
        query_grad,
        key_grad,
        value_grad,
        output_grad.astype(jnp.float32),
        expand_grad.astype(jnp.float32),
        shrink_grad.astype(jnp.float32),
        query_sum[0],
        value_sum[0],
        vectors[8 : 8 + hidden_rows].reshape(-1),
        vectors[:2],
        vectors[2:6],
    )


def solution(mesh):
    rows, whole, cols = P(("fsdp", "ctx"), "tp"), P(), P("tp")
    wide = P(None, "tp")
    return jax.shard_map(
        body,
        mesh=mesh,
        in_specs=(rows, whole) + (rows,) * 6 + (cols,) * 3 + (wide,) * 2 + (rows,),
        out_specs=(rows,) * 8 + (cols,) * 3 + (wide,) * 2,
        check_vma=False,
    )
```

```python
import functools
import math

import jax
import jax.numpy as jnp
from jax import lax
from jax.experimental import pallas as pl
from jax.experimental.pallas import tpu as pltpu
from jax.sharding import PartitionSpec as P

HD = 128
WIN = 1024
QB = 512
KB = 512

epsilon = 1e-06
hidden_floor = -1e30
score_scale = 1.0 / math.sqrt(HD)
log2_e = 1.0 / math.log(2.0)


def dot_plain(left, right):
    return jnp.dot(left, right, preferred_element_type=jnp.float32)


def dot_rows(left, right):
    return lax.dot_general(
        left, right, (((0,), (0,)), ((), ())), preferred_element_type=jnp.float32
    )


def dot_cols(left, right):
    return lax.dot_general(
        left, right, (((1,), (1,)), ((), ())), preferred_element_type=jnp.float32
    )


def attend_kernel(first, last, q_ref, k_ref, v_ref, low_ref, high_ref, out_ref, lse_ref, vt):
    block = pl.program_id(1)
    rows = q_ref.shape[0]

    @pl.when(block == 0)
    def _():
        vt[...] = v_ref[...].T

    queries = q_ref[...]
    low, high = low_ref[...], high_ref[...]
    places = lax.broadcasted_iota(jnp.int32, (KB, rows), 0)

    def step(number, carry):
        top, total, mixed = carry
        start = pl.multiple_of(number * KB, KB)
        scores = dot_cols(k_ref[pl.ds(start, KB), :], queries) * (score_scale * log2_e)
        keep = (places >= low - start) & (places <= high - start)
        scores = jnp.where(keep, scores, hidden_floor)
        new_top = jnp.maximum(top, jnp.max(scores, axis=0, keepdims=True))
        shrink = jnp.exp2(top - new_top)
        powers = jnp.exp2(scores - new_top)
        total = total * shrink + jnp.sum(powers, axis=0, keepdims=True)
        mixed = mixed * shrink + dot_plain(vt[:, pl.ds(start, KB)], powers.astype(jnp.bfloat16))
        return new_top, total, mixed

    top, total, mixed = lax.fori_loop(
        first[block],
        last[block],
        step,
        (
            jnp.full((1, rows), hidden_floor, jnp.float32),
            jnp.zeros((1, rows), jnp.float32),
            jnp.zeros((HD, rows), jnp.float32),
        ),
    )
    out_ref[...] = (mixed / total).T.astype(out_ref.dtype)
    lse_ref[...] = (top + jnp.log2(total))[None]


def attend(queries, keys, values, heads, low, high, first, last, places=(0, 0, 0)):
    rows, span = queries.shape[0], keys.shape[0]
    width = heads * HD
    q_at, k_at, v_at = places
    return pl.pallas_call(
        attend_kernel,
        out_shape=(
            jax.ShapeDtypeStruct((rows, width), jnp.bfloat16),
            jax.ShapeDtypeStruct((heads, 1, rows), jnp.float32),
        ),
        grid_spec=pltpu.PrefetchScalarGridSpec(
            num_scalar_prefetch=2,
            grid=(heads, rows // QB),
            in_specs=[
                pl.BlockSpec((QB, HD), lambda h, i, *_: (i, h + q_at)),
                pl.BlockSpec((span, HD), lambda h, i, *_: (0, h + k_at)),
                pl.BlockSpec((span, HD), lambda h, i, *_: (0, h + v_at)),
                pl.BlockSpec((1, QB), lambda h, i, *_: (0, i)),
                pl.BlockSpec((1, QB), lambda h, i, *_: (0, i)),
            ],
            out_specs=[
                pl.BlockSpec((QB, HD), lambda h, i, *_: (i, h)),
                pl.BlockSpec((1, 1, QB), lambda h, i, *_: (h, 0, i)),
            ],
            scratch_shapes=[pltpu.VMEM((HD, span), jnp.bfloat16)],
        ),
        compiler_params=pltpu.CompilerParams(vmem_limit_bytes=32 << 20),
        cost_estimate=pl.CostEstimate(
            flops=3 * rows * span * width,
            bytes_accessed=2 * (2 * rows + 2 * span) * width,
            transcendentals=rows * span * heads,
        ),
        name="attend",
    )(first, last, queries, keys, values, low, high)


def attend_back_kernel(
    first, last, q_ref, k_ref, v_ref, o_ref, g_ref, lse_ref, low_ref, high_ref,
    *outputs,
):
    *results, kt, dk_sum, dv_sum = outputs
    head, block = pl.program_id(0), pl.program_id(1)
    rows = q_ref.shape[0]

    @pl.when(block == 0)
    def _():
        kt[...] = k_ref[...].T
        dk_sum[...] = jnp.zeros_like(dk_sum)
        dv_sum[...] = jnp.zeros_like(dv_sum)

    queries = q_ref[...]
    upstream = g_ref[...]
    lse = lse_ref[0]
    low, high = low_ref[...], high_ref[...]
    places = lax.broadcasted_iota(jnp.int32, (KB, rows), 0)
    product = upstream.astype(jnp.float32) * o_ref[...].astype(jnp.float32)
    delta = jnp.sum(product.T, axis=0, keepdims=True)

    def step(number, dq):
        start = pl.multiple_of(number * KB, KB)
        window = pl.ds(start, KB)
        scores = dot_cols(k_ref[window, :], queries) * (score_scale * log2_e)
        keep = (places >= low - start) & (places <= high - start)
        probs = jnp.exp2(jnp.where(keep, scores - lse, hidden_floor))
        prob_grad = dot_cols(v_ref[window, :], upstream)
        score_grad = (probs * (prob_grad - delta)).astype(jnp.bfloat16)
        dv_sum[window, :] += dot_plain(probs.astype(jnp.bfloat16), upstream)
        dk_sum[window, :] += dot_plain(score_grad, queries)
        return dq + dot_plain(kt[:, window], score_grad)

    dq = lax.fori_loop(
        first[block], last[block], step, jnp.zeros((HD, rows), jnp.float32)
    )
    dq = (dq * score_scale).T
    if len(results) == 1:
        width = results[0].shape[1] // 3

        def place(part):
            start = pl.multiple_of(part * width + head * HD, HD)
            return results[0].at[:, pl.ds(start, HD)]

        query_place = place(0).at[pl.ds(pl.multiple_of(block * rows, rows), rows)]
        key_place, value_place = place(1), place(2)
    else:
        query_place, key_place, value_place = results
    query_place[...] = dq.astype(query_place.dtype)

    @pl.when(block == pl.num_programs(1) - 1)
    def _():
        key_place[...] = (dk_sum[...] * score_scale).astype(key_place.dtype)
        value_place[...] = dv_sum[...].astype(value_place.dtype)


def attend_back(
    queries, keys, values, out, upstream, lse, low, high, first, last, places=(0, 0, 0), merged=False
):
    rows, width = out.shape
    span = keys.shape[0]
    heads = width // HD
    q_at, k_at, v_at = places
    row_spec = pl.BlockSpec((QB, HD), lambda h, i, *_: (i, h))
    key_spec = pl.BlockSpec((span, HD), lambda h, i, *_: (0, h))
    mark_spec = pl.BlockSpec((1, QB), lambda h, i, *_: (0, i))
    return pl.pallas_call(
        attend_back_kernel,
        out_shape=[jax.ShapeDtypeStruct((rows, 3 * width), jnp.bfloat16)]
        if merged
        else [
            jax.ShapeDtypeStruct((rows, width), jnp.bfloat16),
            jax.ShapeDtypeStruct((span, width), jnp.float32),
            jax.ShapeDtypeStruct((span, width), jnp.float32),
        ],
        grid_spec=pltpu.PrefetchScalarGridSpec(
            num_scalar_prefetch=2,
            grid=(heads, rows // QB),
            in_specs=[
                pl.BlockSpec((QB, HD), lambda h, i, *_: (i, h + q_at)),
                pl.BlockSpec((span, HD), lambda h, i, *_: (0, h + k_at)),
                pl.BlockSpec((span, HD), lambda h, i, *_: (0, h + v_at)),
                row_spec, row_spec,
                pl.BlockSpec((1, 1, QB), lambda h, i, *_: (h, 0, i)),
                mark_spec, mark_spec,
            ],
            out_specs=[pl.BlockSpec((rows, 3 * width), lambda h, i, *_: (0, 0))]
            if merged
            else [row_spec, key_spec, key_spec],
            scratch_shapes=[
                pltpu.VMEM((HD, span), jnp.bfloat16),
                pltpu.VMEM((span, HD), jnp.float32),
                pltpu.VMEM((span, HD), jnp.float32),
            ],
        ),
        compiler_params=pltpu.CompilerParams(vmem_limit_bytes=32 << 20),
        cost_estimate=pl.CostEstimate(
            flops=8 * rows * span * width,
            bytes_accessed=2 * (4 * rows + 4 * span) * width,
            transcendentals=rows * span * heads,
        ),
        name="attend_back",
    )(first, last, queries, keys, values, out, upstream, lse, low, high)


def key_bounds(query_ids, key_ids, offset):
    rows, span = query_ids.shape[0], key_ids.shape[0]
    start = jnp.sum(key_ids[:, None] < query_ids[None, :], axis=0, dtype=jnp.int32)
    stop = jnp.sum(key_ids[:, None] <= query_ids[None, :], axis=0, dtype=jnp.int32)
    places = jnp.arange(rows, dtype=jnp.int32) + offset
    low = jnp.maximum(start, places - WIN)
    high = jnp.minimum(stop - 1, places + WIN)
    first = jnp.min(low.reshape(-1, QB), axis=1) // KB
    last = jnp.max(high.reshape(-1, QB), axis=1) // KB + 1
    return low[None], high[None], first, last


def padded(block, width):
    count = lax.axis_size("ctx")
    forward = [(i, i + 1) for i in range(count - 1)]
    backward = [(target, source) for source, target in forward]
    below = lax.ppermute(block[block.shape[0] - width :], "ctx", forward)
    above = lax.ppermute(block[:width], "ctx", backward)
    return jnp.concatenate([below, block, above], axis=0)


def norm_parts(rows):
    mean = jnp.mean(rows, axis=-1, keepdims=True)
    square = jnp.mean(rows * rows, axis=-1, keepdims=True)
    inverse = lax.rsqrt(square - mean * mean + epsilon)
    return (rows - mean) * inverse, inverse


def norm_back(upstream, normed, inverse, gain):
    scaled = upstream * gain
    first_mean = jnp.mean(scaled, axis=-1, keepdims=True)
    second_mean = jnp.mean(scaled * normed, axis=-1, keepdims=True)
    return inverse * (scaled - first_mean - normed * second_mean)


def gelu_tanh(values):
    return jax.nn.gelu(values, approximate=True)


MESH = pl.DeviceIdType.MESH
PIECES = 4
TILE = 512


def greet(me, count, others=()):
    barrier = pltpu.get_barrier_semaphore()

    @pl.when(me > 0)
    def _():
        pl.semaphore_signal(barrier, inc=1, device_id={"tp": me - 1}, device_id_type=MESH)

    @pl.when(me < count - 1)
    def _():
        pl.semaphore_signal(barrier, inc=1, device_id={"tp": me + 1}, device_id_type=MESH)

    for other in others:
        pl.semaphore_signal(barrier, inc=1, device_id=other, device_id_type=MESH)

    @pl.when((me == 0) | (me == count - 1))
    def _():
        pl.semaphore_wait(barrier, 1 + len(others))

    @pl.when((me > 0) & (me < count - 1))
    def _():
        pl.semaphore_wait(barrier, 2 + len(others))


def peers_along_tp(me, count):
    return [{"tp": lax.rem(me + i, count)} for i in range(1, count)]


def greet_peers(peers):
    barrier = pltpu.get_barrier_semaphore()
    for peer in peers:
        pl.semaphore_signal(barrier, inc=1, device_id=peer, device_id_type=MESH)
    pl.semaphore_wait(barrier, len(peers))


class Exchange:
    def __init__(self, peers, sent, got, source, place):
        self.peers, self.sent, self.got = peers, sent, got
        self.source, self.place = source, place

    def copies(self):
        for i, peer in enumerate(self.peers):
            yield pltpu.make_async_remote_copy(
                src_ref=self.source(i + 1),
                dst_ref=self.place(i),
                send_sem=self.sent.at[i],
                recv_sem=self.got.at[i],
                device_id=peer,
                device_id_type=MESH,
            )

    def start(self):
        for copy in self.copies():
            copy.start()

    def wait_arrivals(self):
        for copy in self.copies():
            copy.wait_recv()

    def wait_sent(self):
        for copy in self.copies():
            copy.wait_send()


def at_distance(me, count, distance, action):
    for index in (me - distance, me + distance):

        @pl.when((index >= 0) & (index < count))
        def _(index=index):
            action(index)


class Line:
    def __init__(self, me, count, sum_slots, sum_sent, sum_got, spread_view, spread_sent, spread_got):
        self.me, self.count = me, count
        self.sum_slots, self.sum_sent, self.sum_got = sum_slots, sum_sent, sum_got
        self.spread_view, self.spread_sent, self.spread_got = spread_view, spread_sent, spread_got

    def sum_copy(self, piece, owner):
        onward = jnp.where(owner > self.me, self.me + 1, self.me - 1)
        place = jnp.where((owner < self.me) & (owner == self.me - 1), self.count, owner)
        return pltpu.make_async_remote_copy(
            src_ref=self.sum_slots.at[piece, owner],
            dst_ref=self.sum_slots.at[piece, place],
            send_sem=self.sum_sent.at[piece, owner],
            recv_sem=self.sum_got.at[piece, place],
            device_id={"tp": onward},
            device_id_type=MESH,
        )

    def sum_arrival(self, piece, place):
        pltpu.make_async_copy(
            self.sum_slots.at[piece, place],
            self.sum_slots.at[piece, place],
            self.sum_got.at[piece, place],
        ).wait()

    def sum_start(self, piece, term):
        me, count = self.me, self.count

        @pl.when((me == 0) | (me == count - 1))
        def _():
            for k in range(count - 1):
                owner = jnp.where(me == 0, count - 1 - k, k)
                self.sum_slots[piece, owner] = term(owner).astype(jnp.bfloat16)
                self.sum_copy(piece, owner).start()

    def sum_onward(self, piece, term):
        me, count = self.me, self.count

        @pl.when((me > 0) & (me < count - 1))
        def _():
            for distance in range(count - 2, 0, -1):

                def pass_on(owner):
                    self.sum_arrival(piece, owner)
                    total = self.sum_slots[piece, owner].astype(jnp.float32) + term(owner)
                    self.sum_slots[piece, owner] = total.astype(jnp.bfloat16)
                    self.sum_copy(piece, owner).start()

                at_distance(me, count, distance, pass_on)

    def sum_end(self, piece, total):
        me, count = self.me, self.count

        @pl.when(me > 0)
        def _():
            self.sum_arrival(piece, me)
            total[...] += self.sum_slots[piece, me].astype(jnp.float32)

        @pl.when(me < count - 1)
        def _():
            self.sum_arrival(piece, count)
            total[...] += self.sum_slots[piece, count].astype(jnp.float32)

    def sum_finish(self, pieces):
        @pl.loop(0, pieces)
        def _(piece):
            for distance in range(1, self.count):
                at_distance(
                    self.me, self.count, distance,
                    lambda owner: self.sum_copy(piece, owner).wait_send(),
                )

    def spread_copy(self, piece, owner, to, sent, source=None):
        return pltpu.make_async_remote_copy(
            src_ref=self.spread_view(piece, owner) if source is None else source,
            dst_ref=self.spread_view(piece, owner),
            send_sem=self.spread_sent.at[piece, sent],
            recv_sem=self.spread_got.at[piece, owner],
            device_id={"tp": to},
            device_id_type=MESH,
        )

    def own_copies(self, piece, action, source=None):
        me, count = self.me, self.count

        @pl.when(me > 0)
        def _():
            action(self.spread_copy(piece, me, me - 1, count, source))

        @pl.when(me < count - 1)
        def _():
            action(self.spread_copy(piece, me, me + 1, me, source))

    def spread_start(self, piece, source=None):
        self.own_copies(piece, lambda copy: copy.start(), source)

    def onward_copy(self, piece, owner, action):
        me, count = self.me, self.count

        @pl.when((owner < me) & (me < count - 1))
        def _():
            action(self.spread_copy(piece, owner, me + 1, owner))

        @pl.when((owner > me) & (me > 0))
        def _():
            action(self.spread_copy(piece, owner, me - 1, owner))

    def spread_onward(self, piece, distance):
        def pass_on(owner):
            view = self.spread_view(piece, owner)
            pltpu.make_async_copy(view, view, self.spread_got.at[piece, owner]).wait()
            self.onward_copy(piece, owner, lambda copy: copy.start())

        at_distance(self.me, self.count, distance, pass_on)

    def spread_finish(self, pieces, source=None):
        @pl.loop(0, pieces)
        def _(piece):
            self.own_copies(
                piece, lambda copy: copy.wait_send(), None if source is None else source(piece)
            )
            for distance in range(1, self.count):
                at_distance(
                    self.me, self.count, distance,
                    lambda owner: self.onward_copy(piece, owner, lambda copy: copy.wait_send()),
                )


def line_semaphores(count, pieces):
    return [
        pltpu.SemaphoreType.DMA((pieces, count)),
        pltpu.SemaphoreType.DMA((pieces, count + 1)),
    ], [
        pltpu.SemaphoreType.DMA((pieces, count + 1)),
        pltpu.SemaphoreType.DMA((pieces, count)),
    ]


def gather_kernel(
    count, x_ref, marks_ref, out_ref, marks_out, slots, sent, got, marks_sent, marks_got
):
    me = lax.axis_index("tp")
    height = x_ref.shape[0] // PIECES
    width = x_ref.shape[1]

    def view(piece, owner):
        return out_ref.at[
            pl.ds(pl.multiple_of(piece * height, height), height),
            pl.ds(pl.multiple_of(owner * width, width), width),
        ]

    def source(piece):
        return x_ref.at[pl.ds(pl.multiple_of(piece * height, height), height)]

    line = Line(me, count, None, None, None, view, sent, got)
    peers = peers_along_tp(me, count)
    greet_peers(peers)

    @pl.loop(0, PIECES)
    def _(piece):
        line.spread_start(piece, source(piece))

    marks = Exchange(
        peers, marks_sent, marks_got, lambda _: marks_ref, lambda i: slots.at[i]
    )
    marks.start()
    own = pl.ds(pl.multiple_of(me * width, width), width)
    out_ref[:, own] = x_ref[...]
    marks_out[:, own] = marks_ref[...]
    for distance in range(1, count):

        @pl.loop(0, PIECES)
        def _(piece, distance=distance):
            line.spread_onward(piece, distance)

    marks.wait_arrivals()
    for i in range(1, count):
        owner = lax.rem(me - i + count, count)
        marks_out[:, pl.ds(pl.multiple_of(owner * width, width), width)] = slots[i - 1]
    marks.wait_sent()
    line.spread_finish(PIECES, source)


def gather_features(x, marks, collective_id):
    count = lax.axis_size("tp")
    rows, width = x.shape
    return pl.pallas_call(
        functools.partial(gather_kernel, count),
        out_shape=[
            jax.ShapeDtypeStruct((rows, count * width), x.dtype),
            jax.ShapeDtypeStruct((marks.shape[0], count * width), marks.dtype),
        ],
        in_specs=[pl.BlockSpec(memory_space=pltpu.VMEM)] * 2,
        out_specs=[pl.BlockSpec(memory_space=pltpu.VMEM)] * 2,
        scratch_shapes=[
            pltpu.VMEM((count - 1, *marks.shape), marks.dtype),
            *line_semaphores(count, PIECES)[1],
            pltpu.SemaphoreType.DMA((count - 1,)),
            pltpu.SemaphoreType.DMA((count - 1,)),
        ],
        compiler_params=pltpu.CompilerParams(
            collective_id=collective_id, has_side_effects=True, vmem_limit_bytes=16 << 20
        ),
        cost_estimate=pl.CostEstimate(
            flops=0, bytes_accessed=64 * rows * count * width, transcendentals=0
        ),
        name="gather_features",
    )(x, marks)


class Swap:
    def __init__(self, sent, got, source, place):
        self.sent, self.got, self.source, self.place = sent, got, source, place

    def copy(self, piece):
        return pltpu.make_async_remote_copy(
            src_ref=self.source(piece),
            dst_ref=self.place(piece),
            send_sem=self.sent.at[piece],
            recv_sem=self.got.at[piece],
            device_id={"ctx": 1 - lax.axis_index("ctx")},
            device_id_type=MESH,
        )

    def start(self, piece):
        self.copy(piece).start()

    def wait_arrival(self, piece):
        self.copy(piece).wait_recv()

    def wait_sent(self, piece):
        self.copy(piece).wait_send()


class PlaneGather:
    def __init__(self, whole, sent, got):
        self.whole, self.sent, self.got = whole, sent, got
        fsdp, self.ctx = lax.axis_index("fsdp"), lax.axis_index("ctx")
        self.fsdp = fsdp
        self.twin = fsdp + 1 - 2 * lax.rem(fsdp, 2)
        self.along_x = lax.rem(fsdp + 2, 4)
        self.twin_x = lax.rem(self.twin + 2, 4)
        self.core_peer = {"fsdp": self.twin}
        self.x_peer = {"fsdp": self.along_x}
        self.y_peer = {"ctx": 1 - self.ctx}

    def peers(self):
        return [self.core_peer, self.x_peer, self.y_peer]

    def shard(self, fsdp, ctx, half=None):
        height = self.whole.shape[0] // 8
        start = (fsdp * 2 + ctx) * height
        if half is not None:
            height //= 2
            start += half * height
        return self.whole.at[pl.ds(pl.multiple_of(start, height), height)]

    def copy(self, number, view, peer):
        return pltpu.make_async_remote_copy(
            src_ref=view,
            dst_ref=view,
            send_sem=self.sent.at[number],
            recv_sem=self.got.at[number],
            device_id=peer,
            device_id_type=MESH,
        )

    def copies(self):
        own = self.shard(self.fsdp, self.ctx)
        from_x = self.shard(self.along_x, self.ctx)
        from_y = self.shard(self.fsdp, 1 - self.ctx)
        return [
            (own, self.core_peer),
            (own, self.x_peer),
            (own, self.y_peer),
            (from_x, self.core_peer),
            (self.shard(self.along_x, self.ctx, 0), self.y_peer),
            (from_y, self.core_peer),
            (self.shard(self.fsdp, 1 - self.ctx, 1), self.x_peer),
            (self.shard(self.along_x, 1 - self.ctx, 0), self.core_peer),
            (self.shard(self.along_x, 1 - self.ctx, 1), self.core_peer),
        ]

    def arrivals(self):
        return [
            self.shard(self.twin, self.ctx),
            self.shard(self.along_x, self.ctx),
            self.shard(self.fsdp, 1 - self.ctx),
            self.shard(self.twin_x, self.ctx),
            self.shard(self.along_x, 1 - self.ctx, 0),
            self.shard(self.twin, 1 - self.ctx),
            self.shard(self.along_x, 1 - self.ctx, 1),
            self.shard(self.twin_x, 1 - self.ctx, 0),
            self.shard(self.twin_x, 1 - self.ctx, 1),
        ]

    def start(self, *numbers):
        copies = self.copies()
        for number in numbers:
            self.copy(number, *copies[number]).start()

    def wait(self, *numbers):
        arrivals = self.arrivals()
        for number in numbers:
            view = arrivals[number]
            pltpu.make_async_copy(view, view, self.got.at[number]).wait()

    def put(self, shard, done):
        copy = pltpu.make_async_copy(shard, self.shard(self.fsdp, self.ctx), done)
        copy.start()
        copy.wait()

    def first(self):
        self.start(1, 2, 0)

    def second(self):
        self.wait(1)
        self.start(4, 3)
        self.wait(2)
        self.start(6, 5)

    def third(self):
        self.wait(4)
        self.start(7)
        self.wait(6)
        self.start(8)

    def last(self):
        self.wait(0, 3, 5, 7, 8)

    def wait_sent(self):
        for number, (view, peer) in enumerate(self.copies()):
            self.copy(number, view, peer).wait_send()


def enter_kernel(
    count, x_ref, marks_ref, query_ref, key_ref, value_ref, output_ref, bias,
    wide, marks_out, weight, output_weight, heads,
    mark_slots, stage, sent, got, marks_sent, marks_got,
    weight_sent, weight_got, output_sent, output_got, swap_sent, swap_got,
):
    me, ctx = lax.axis_index("tp"), lax.axis_index("ctx")
    rows, width = x_ref.shape
    height = rows // PIECES
    half = query_ref.shape[1] // 2
    part = 3 * half

    def piece_rows(piece, start=0):
        return pl.ds(pl.multiple_of(start + piece * height, height), height)

    def view(piece, owner):
        return wide.at[piece_rows(piece), pl.ds(pl.multiple_of(owner * width, width), width)]

    gather = PlaneGather(weight, weight_sent, weight_got)
    own_shard = gather.shard(gather.fsdp, ctx)
    for side in range(2):
        for i, ref in enumerate((query_ref, key_ref, value_ref)):
            start = side * part + i * half
            own_shard[:, start : start + half] = ref[:, side * half : (side + 1) * half]
    output_gather = PlaneGather(output_weight, output_sent, output_got)
    output_gather.shard(gather.fsdp, ctx)[...] = output_ref[...]
    line = Line(me, count, None, None, None, view, sent, got)
    tp_peers = peers_along_tp(me, count)
    greet_peers(tp_peers + gather.peers())

    def source(piece):
        return x_ref.at[piece_rows(piece)]

    @pl.loop(0, PIECES)
    def _(piece):
        line.spread_start(piece, source(piece))

    gather.first()
    output_gather.first()
    marks = Exchange(
        tp_peers, marks_sent, marks_got, lambda _: marks_ref, lambda i: mark_slots.at[i]
    )
    marks.start()
    own = pl.ds(pl.multiple_of(me * width, width), width)
    wide[:, own] = x_ref[...]
    marks_out[:, own] = marks_ref[...]
    swap = Swap(
        swap_sent, swap_got,
        lambda piece: stage.at[piece_rows(piece)],
        lambda piece: heads.at[piece_rows(piece, ctx * rows)],
    )

    def products(piece, side, place):
        x = wide[piece_rows(piece), :]

        @pl.loop(0, 3)
        def _(tile):
            start = pl.multiple_of(side * part + tile * half, half)
            columns = pl.ds(start, half)
            values = dot_plain(x, weight[:, columns]) + bias[:, columns]
            place[:, pl.ds(pl.multiple_of(tile * half, half), half)] = values.astype(jnp.bfloat16)

    for distance in range(1, count):
        if distance == count - 1:
            gather.last()

        @pl.loop(0, PIECES)
        def _(piece, distance=distance):
            line.spread_onward(piece, distance)
            if distance == count - 1:
                products(piece, 1 - ctx, stage.at[piece_rows(piece)])
                swap.start(piece)
                products(piece, ctx, heads.at[piece_rows(piece, ctx * rows)])

        if distance == 1:
            gather.second()
            output_gather.second()
        if distance == count - 2:
            gather.third()
            output_gather.third()

    marks.wait_arrivals()
    for i in range(1, count):
        owner = lax.rem(me - i + count, count)
        marks_out[:, pl.ds(pl.multiple_of(owner * width, width), width)] = mark_slots[i - 1]

    @pl.loop(0, PIECES)
    def _(piece):
        swap.wait_arrival(piece)
        swap.wait_sent(piece)

    output_gather.last()
    marks.wait_sent()
    gather.wait_sent()
    output_gather.wait_sent()
    line.spread_finish(PIECES, source)


def enter(
    tokens, marks, query_weight, key_weight, value_weight, output_weight, bias, collective_id
):
    count = lax.axis_size("tp")
    rows, width = tokens.shape
    head_cols = query_weight.shape[1]
    plane = 8
    part = 3 * head_cols // 2
    return pl.pallas_call(
        functools.partial(enter_kernel, count),
        out_shape=[
            jax.ShapeDtypeStruct((rows, count * width), tokens.dtype),
            jax.ShapeDtypeStruct((marks.shape[0], count * width), marks.dtype),
            jax.ShapeDtypeStruct((plane * query_weight.shape[0], 2 * part), query_weight.dtype),
            jax.ShapeDtypeStruct(
                (plane * output_weight.shape[0], output_weight.shape[1]), output_weight.dtype
            ),
            jax.ShapeDtypeStruct((2 * rows, part), jnp.bfloat16),
        ],
        in_specs=[pl.BlockSpec(memory_space=pltpu.VMEM)] * 7,
        out_specs=[pl.BlockSpec(memory_space=pltpu.VMEM)] * 5,
        scratch_shapes=[
            pltpu.VMEM((count - 1, *marks.shape), marks.dtype),
            pltpu.VMEM((rows, part), jnp.bfloat16),
            *line_semaphores(count, PIECES)[1],
            pltpu.SemaphoreType.DMA((count - 1,)),
            pltpu.SemaphoreType.DMA((count - 1,)),
            *[pltpu.SemaphoreType.DMA((9,))] * 4,
            pltpu.SemaphoreType.DMA((PIECES,)),
            pltpu.SemaphoreType.DMA((PIECES,)),
        ],
        compiler_params=pltpu.CompilerParams(
            collective_id=collective_id, has_side_effects=True, vmem_limit_bytes=40 << 20
        ),
        cost_estimate=pl.CostEstimate(
            flops=80_000_000_000, bytes_accessed=64 * rows * count * width, transcendentals=0
        ),
        name="enter",
    )(tokens, marks, query_weight, key_weight, value_weight, output_weight, bias)


def relay_kernel(count, row_step, use_step, sizes, *refs):
    row_in, use_in, row_out, use_out, shared, swap_in, swap_out, gathers = sizes
    refs = list(refs)

    def take(number):
        taken = refs[:number]
        del refs[:number]
        return taken

    x_ref, sum_weight = take(2)
    use_weight = sum_weight if shared else take(1)[0]
    row_inputs, use_inputs = take(row_in), take(use_in)
    (gathered,) = take(1)
    row_outputs, use_outputs = take(row_out), take(use_out)
    swapped = take(1)[0] if swap_in or swap_out else None
    if gathers:
        shards = [use_weight, *use_inputs[-1:]]
        use_inputs = use_inputs[:-1]
        wholes = take(2)
        use_weight = wholes[0]
    terms, total, slots, sum_sent, sum_got, spread_sent, spread_got = take(7)
    me, ctx = lax.axis_index("tp"), lax.axis_index("ctx")
    rows = gathered.shape[0]
    height = rows // PIECES
    own = height // count
    width = sum_weight.shape[0]

    def piece_rows(piece, start=0):
        return pl.ds(pl.multiple_of(start + piece * height, height), height)

    def view(piece, owner):
        return gathered.at[pl.ds(pl.multiple_of(piece * height + owner * own, own), own)]

    line = Line(me, count, slots, sum_sent, sum_got, view, spread_sent, spread_got)
    use_gather = next_gather = None
    if gathers:
        use_gather, next_gather = (
            PlaneGather(whole, *take(2)) for whole in wholes
        )
        greet(me, count, use_gather.peers())
        use_gather.put(shards[0], take(1)[0])
        next_gather.put(shards[1], take(1)[0])
        use_gather.first()
    else:
        greet(me, count, [{"ctx": 1 - ctx}] if swap_in or swap_out else [])
    swap = None
    if swap_in:
        half = x_ref.shape[1]
        own_half = pl.ds(pl.multiple_of(ctx * half, half), half)
        swap = Swap(
            *refs,
            lambda piece: x_ref.at[piece_rows(piece, (1 - ctx) * rows)],
            lambda piece: swapped.at[piece_rows(piece), own_half],
        )

        @pl.loop(0, PIECES)
        def _(piece):
            swap.start(piece)
            swapped[piece_rows(piece), own_half] = x_ref[piece_rows(piece, ctx * rows), :]

    if swap_out:
        stage, swap_sent, swap_got = refs
        half = swapped.shape[1]
        swap = Swap(
            swap_sent, swap_got,
            lambda piece: stage.at[piece_rows(piece)],
            lambda piece: swapped.at[piece_rows(piece, ctx * rows)],
        )

    @pl.loop(0, PIECES + 2)
    def _(step):
        odd = lax.rem(step, 2)

        def term(owner):
            return terms[odd, pl.ds(pl.multiple_of(owner * own, own), own), :]

        @pl.when(step < PIECES)
        def _():
            if swap_in:
                swap.wait_arrival(step)
            x = (swapped if swap_in else x_ref)[piece_rows(step), :]

            @pl.loop(0, width // TILE)
            def _(tile):
                part = pl.ds(pl.multiple_of(tile * TILE, TILE), TILE)
                terms[odd, :, part] = dot_cols(x, sum_weight[part, :])

            line.sum_start(step, term)

        @pl.when((step >= 1) & (step <= PIECES))
        def _():
            piece = step - 1
            total[...] = terms[1 - odd, pl.ds(pl.multiple_of(me * own, own), own), :]
            line.sum_end(piece, total)
            view(piece, me)[...] = row_step(piece, total, row_inputs, row_outputs)
            line.spread_start(piece)

        @pl.when(step >= 2)
        def _():
            for distance in range(2, count):
                line.spread_onward(step - 2, distance)

        @pl.when(step < PIECES)
        def _():
            line.sum_onward(step, term)

        @pl.when((step >= 1) & (step <= PIECES))
        def _():
            line.spread_onward(step - 1, 1)

        if gathers:

            @pl.when(step == 1)
            def _():
                use_gather.second()
                next_gather.first()

            @pl.when(step == 2)
            def _():
                use_gather.third()
                use_gather.last()

            @pl.when(step == 3)
            def _():
                next_gather.second()

            @pl.when(step == 4)
            def _():
                next_gather.third()

        @pl.when(step >= 2)
        def _():
            piece = step - 2
            part = piece_rows(piece)
            result = use_step(part, gathered[part, :], use_weight, use_inputs, use_outputs)
            if swap_out:
                here = ctx == 0
                left, right = result[:, :half], result[:, half:]
                stage[part, :] = jnp.where(here, right, left)
                swap.start(piece)
                swapped[piece_rows(piece, ctx * rows), :] = jnp.where(here, left, right)

    if swap is not None:

        @pl.loop(0, PIECES)
        def _(piece):
            if swap_out:
                swap.wait_arrival(piece)
            swap.wait_sent(piece)

    if gathers:
        next_gather.last()
        use_gather.wait_sent()
        next_gather.wait_sent()
    line.sum_finish(PIECES)
    line.spread_finish(PIECES)


def relay(
    x, sum_weight, use_weight, row_inputs, row_step, row_shapes, use_inputs, use_step, use_shapes,
    collective_id, name, rows, swap_in=None, swap_out=None, next_shard=None,
):
    count = lax.axis_size("tp")
    width = sum_weight.shape[0]
    height = rows // PIECES
    own = height // count
    shared = use_weight is None
    gathers = next_shard is not None
    if gathers:
        use_inputs = [*use_inputs, next_shard]
    operands = [x, sum_weight, *([] if shared else [use_weight]), *row_inputs, *use_inputs]
    in_specs = [pl.BlockSpec(memory_space=pltpu.VMEM)] * len(operands)
    shapes = [jax.ShapeDtypeStruct((rows, width), jnp.bfloat16), *row_shapes, *use_shapes]
    shapes += [shape for shape in (swap_in, swap_out) if shape is not None]
    out_specs = [pl.BlockSpec(memory_space=pltpu.VMEM)] * len(shapes)
    extra = []
    if gathers:
        for shard, space in ((use_weight, pltpu.VMEM), (next_shard, pl.ANY)):
            whole = (8 * shard.shape[0], shard.shape[1])
            shapes.append(jax.ShapeDtypeStruct(whole, shard.dtype))
            out_specs.append(pl.BlockSpec(memory_space=space))
        extra = [pltpu.SemaphoreType.DMA((9,))] * 4 + [pltpu.SemaphoreType.DMA] * 2
    sums, spreads = line_semaphores(count, PIECES)
    swaps = []
    if swap_out is not None:
        swaps.append(pltpu.VMEM((rows, swap_out.shape[1]), swap_out.dtype))
    if swap_in is not None or swap_out is not None:
        swaps += [pltpu.SemaphoreType.DMA((PIECES,))] * 2
    sizes = (
        len(row_inputs), len(use_inputs), len(row_shapes), len(use_shapes), shared,
        swap_in is not None, swap_out is not None, gathers,
    )
    return pl.pallas_call(
        functools.partial(relay_kernel, count, row_step, use_step, sizes),
        out_shape=shapes,
        in_specs=in_specs,
        out_specs=out_specs,
        scratch_shapes=[
            pltpu.VMEM((2, height, width), jnp.float32),
            pltpu.VMEM((own, width), jnp.float32),
            pltpu.VMEM((PIECES, count + 1, own, width), jnp.bfloat16),
            *sums,
            *spreads,
            *extra,
            *swaps,
        ],
        compiler_params=pltpu.CompilerParams(
            collective_id=collective_id, has_side_effects=True, vmem_limit_bytes=60 << 20
        ),
        cost_estimate=pl.CostEstimate(
            flops=100_000_000_000, bytes_accessed=64 * rows * width, transcendentals=0
        ),
        name=name,
    )(*operands)


def own_rows_of(piece, like):
    own = like.shape[0] // PIECES
    return pl.ds(pl.multiple_of(piece * own, own), own)


def first_norm_step(piece, total, inputs, outputs):
    tokens, gains, biases = inputs
    first_norm, normed_one, inverse_one = outputs
    part = own_rows_of(piece, tokens)
    summed = tokens[part, :].astype(jnp.float32) + (total[...] + biases[0:1, :])
    normed, inverse = norm_parts(summed)
    result = normed * gains[0:1, :] + biases[1:2, :]
    first_norm[part, :] = result
    normed_one[part, :] = normed
    inverse_one[part, :] = jnp.broadcast_to(inverse, (inverse.shape[0], 128))
    return result.astype(jnp.bfloat16)


def expand_step(rows, chunk, weight, inputs, outputs):
    (bias,) = inputs
    hidden, activated = outputs

    @pl.loop(0, hidden.shape[1] // TILE)
    def _(tile):
        part = pl.ds(pl.multiple_of(tile * TILE, TILE), TILE)
        values = dot_plain(chunk, weight[:, part]) + bias[:, part]
        hidden[rows, part] = values
        activated[rows, part] = gelu_tanh(values).astype(jnp.bfloat16)


def add_sums(piece, sums, *values):
    @pl.when(piece == 0)
    def _():
        sums[...] = jnp.zeros_like(sums)

    for i, value in enumerate(values):
        sums[i : i + 1, :] += jnp.sum(value, axis=0, keepdims=True)


def second_norm_step(piece, total, inputs, outputs):
    first_norm, out_grad, gains, biases = inputs
    mixed, grad_second, sums = outputs
    part = own_rows_of(piece, first_norm)
    normed, inverse = norm_parts(first_norm[part, :] + total[...] + biases[2:3, :])
    mixed[part, :] = (normed * gains[1:2, :] + biases[3:4, :]).astype(jnp.bfloat16)
    upstream = out_grad[part, :].astype(jnp.float32)
    grad = norm_back(upstream, normed, inverse, gains[1:2, :])
    grad_second[part, :] = grad
    low = grad.astype(jnp.bfloat16)
    add_sums(piece, sums, upstream * normed, upstream, low.astype(jnp.float32))
    return low


def gelu_slope(values):
    scale = math.sqrt(2.0 / math.pi)
    square = values * values
    bend = jnp.tanh(scale * values * (1.0 + 0.044715 * square))
    inner = scale * (1.0 + 3 * 0.044715 * square)
    return 0.5 * (1.0 + bend) + 0.5 * values * (1.0 - bend * bend) * inner


def shrink_step(rows, chunk, weight, inputs, outputs):
    (hidden,) = inputs
    hidden_low, sums = outputs

    @pl.when(rows.start == 0)
    def _():
        sums[...] = jnp.zeros_like(sums)

    @pl.loop(0, hidden.shape[1] // TILE)
    def _(tile):
        part = pl.ds(pl.multiple_of(tile * TILE, TILE), TILE)
        grad = dot_plain(chunk, weight[:, part]) * gelu_slope(hidden[rows, part])
        low = grad.astype(jnp.bfloat16)
        hidden_low[rows, part] = low
        sums[0:1, part] += jnp.sum(low.astype(jnp.float32), axis=0, keepdims=True)


def first_back_step(piece, total, inputs, outputs):
    grad_second, normed_one, inverse_one, gains = inputs
    grad_inner, sums = outputs
    part = own_rows_of(piece, grad_second)
    normed = normed_one[part, :]
    grad_first = grad_second[part, :] + total[...]
    grad = norm_back(grad_first, normed, inverse_one[part, 0:1], gains[0:1, :])
    grad_inner[part, :] = grad
    low = grad.astype(jnp.bfloat16)
    add_sums(piece, sums, grad_first * normed, grad_first, low.astype(jnp.float32))
    return low


def attended_step(rows, chunk, weight, inputs, outputs):
    result = dot_plain(chunk, weight[...]).astype(jnp.bfloat16)
    if outputs:
        outputs[0][rows, :] = result
    return result


def peers_in_plane(sizes):
    fsdp, ctx = lax.axis_index("fsdp"), lax.axis_index("ctx")
    return [
        {"fsdp": lax.rem(fsdp + i, sizes[0]), "ctx": lax.rem(ctx + j, sizes[1])}
        for i in range(sizes[0])
        for j in range(sizes[1])
        if i or j
    ]


def input_kernel(
    sizes, x_ref, weight, inner_ref, rows_ref, hidden_ref, out_ref, vectors_ref,
    term_ref, total, slots, own_vectors, tp_slots, plane_slots,
    sum_sent, sum_got, tp_sent, tp_got, plane_sent, plane_got, hooks=None, pack_step=1,
):
    count = sizes[2]
    me = lax.axis_index("tp")
    height = x_ref.shape[0] // PIECES
    own = height // count
    width = out_ref.shape[1]
    line = Line(me, count, slots, sum_sent, sum_got, None, None, None)
    tp_peers, plane_peers = peers_along_tp(me, count), peers_in_plane(sizes)
    greet_peers(tp_peers + plane_peers)

    def own_part(index):
        return rows_ref.at[:, pl.ds(pl.multiple_of(index * width, width), width)]

    over_tp = Exchange(
        tp_peers, tp_sent, tp_got,
        lambda i: own_part(lax.rem(me + i, count)), lambda i: tp_slots.at[i],
    )
    over_plane = Exchange(
        plane_peers, plane_sent, plane_got, lambda _: own_vectors, lambda i: plane_slots.at[i]
    )
    opening, before, after, closing = hooks or (lambda *_: None,) * 4
    opening()
    over_tp.start()

    def terms(piece):
        def term(owner):
            features = pl.ds(pl.multiple_of(owner * width, width), width)
            term_ref[...] = dot_cols(
                x_ref[pl.ds(pl.multiple_of(piece * height, height), height), :],
                weight[features, :],
            )
            inner = inner_ref[pl.ds(pl.multiple_of(piece * own, own), own), features]
            term_ref[pl.ds(pl.multiple_of(me * own, own), own), :] += inner
            return term_ref[...]

        return term

    def pack():
        over_tp.wait_arrivals()
        own_vectors[0:8, :] = own_part(me)[...]
        for i in range(count - 1):
            own_vectors[0:8, :] += tp_slots[i]
        own_vectors[8:, :] = jnp.zeros_like(own_vectors[8:, :])
        hidden_rows = hidden_ref.shape[1] // width
        for i in range(hidden_rows):
            own_vectors[8 + i : 9 + i, :] = hidden_ref[0:1, i * width : (i + 1) * width]
        for i in range(x_ref.shape[1] // width):
            part = x_ref[:, i * width : (i + 1) * width].astype(jnp.float32)
            place = 8 + hidden_rows + i
            own_vectors[place : place + 1, :] = jnp.sum(part, axis=0, keepdims=True)
        over_plane.start()

    @pl.loop(0, PIECES + 1)
    def _(step):
        @pl.when(step < PIECES)
        def _():
            before(step)
            line.sum_start(step, terms(step))
            line.sum_onward(step, terms(step))

        pl.when(step == pack_step)(pack)

        @pl.when(step >= 1)
        def _():
            piece = step - 1
            total[...] = terms(piece)(me)
            line.sum_end(piece, total)
            rows = pl.ds(pl.multiple_of(piece * height, height), height)
            out_ref[rows, :] = total[...].astype(out_ref.dtype)

        after(step)

    closing()
    over_plane.wait_arrivals()
    vectors_ref[...] = own_vectors[...]
    for i in range(len(plane_peers)):
        vectors_ref[...] += plane_slots[i]
    over_tp.wait_sent()
    over_plane.wait_sent()
    line.sum_finish(PIECES)


def input_sum(x, weight, inner, row_sums, hidden_sums, collective_id):
    sizes = tuple(lax.axis_size(axis) for axis in ("fsdp", "ctx", "tp"))
    count = sizes[2]
    others = sizes[0] * sizes[1] - 1
    rows = x.shape[0]
    width = weight.shape[0] // count
    height = rows // PIECES
    packed = 8 + -(-(hidden_sums.shape[1] + x.shape[1]) // (8 * width)) * 8
    return pl.pallas_call(
        functools.partial(input_kernel, sizes),
        out_shape=[
            jax.ShapeDtypeStruct((rows, width), jnp.bfloat16),
            jax.ShapeDtypeStruct((packed, width), jnp.float32),
        ],
        in_specs=[pl.BlockSpec(memory_space=pltpu.VMEM)] * 5,
        out_specs=[pl.BlockSpec(memory_space=pltpu.VMEM)] * 2,
        scratch_shapes=[
            pltpu.VMEM((height, width), jnp.float32),
            pltpu.VMEM((height, width), jnp.float32),
            pltpu.VMEM((PIECES, count + 1, height, width), jnp.bfloat16),
            pltpu.VMEM((packed, width), jnp.float32),
            pltpu.VMEM((count - 1, 8, width), jnp.float32),
            pltpu.VMEM((others, packed, width), jnp.float32),
            *line_semaphores(count, PIECES)[0],
            pltpu.SemaphoreType.DMA((count - 1,)),
            pltpu.SemaphoreType.DMA((count - 1,)),
            pltpu.SemaphoreType.DMA((others,)),
            pltpu.SemaphoreType.DMA((others,)),
        ],
        compiler_params=pltpu.CompilerParams(
            collective_id=collective_id, has_side_effects=True, vmem_limit_bytes=40 << 20
        ),
        cost_estimate=pl.CostEstimate(
            flops=60_000_000_000, bytes_accessed=64 * rows * width, transcendentals=0
        ),
        name="input_sum",
    )(x, weight, inner, row_sums, hidden_sums)


class PlaneSum:
    def __init__(self, parts, core_slots, first_slots, last_slots, sent, got):
        self.parts, self.core_slots = parts, core_slots
        self.first_slots, self.last_slots = first_slots, last_slots
        self.sent, self.got = sent, got
        self.fsdp, self.ctx = lax.axis_index("fsdp"), lax.axis_index("ctx")
        self.twin = self.fsdp + 1 - 2 * lax.rem(self.fsdp, 2)
        self.half = parts.shape[2] // 2

    def number(self, fsdp, over_x, over_y):
        chip = lax.rem(fsdp + 2 * over_x, 4)
        return chip * 2 + (1 - self.ctx if over_y else self.ctx)

    def view(self, over_x, over_y, side):
        columns = pl.ds(side * self.half, self.half)
        return self.parts.at[self.number(self.fsdp, over_x, over_y), :, columns]

    def copy(self, number, source, place, peer):
        return pltpu.make_async_remote_copy(
            src_ref=source,
            dst_ref=place,
            send_sem=self.sent.at[number],
            recv_sem=self.got.at[number],
            device_id=peer,
            device_id_type=MESH,
        )

    def core_copy(self, number):
        over_x, over_y = number // 2, number % 2
        source = self.parts.at[self.number(self.twin, over_x, over_y)]
        return self.copy(number, source, self.core_slots.at[number], {"fsdp": self.twin})

    def x_peer(self):
        return {"fsdp": lax.rem(self.fsdp + 2, 4)}

    def y_peer(self):
        return {"ctx": 1 - self.ctx}

    def first_copy(self, number):
        slot = self.first_slots.at[number]
        if number < 2:
            return self.copy(4 + number, self.view(1, number, 0), slot, self.x_peer())
        return self.copy(4 + number, self.view(number - 2, 1, 1), slot, self.y_peer())

    def last_copy(self, side):
        slot = self.last_slots.at[side]
        if side == 0:
            return self.copy(8, self.view(0, 1, 0), slot, self.y_peer())
        return self.copy(9, self.view(1, 0, 1), slot, self.x_peer())

    def add(self, view, slot):
        total = view[...].astype(jnp.float32) + slot[...].astype(jnp.float32)
        view[...] = total.astype(view.dtype)

    def start(self):
        for number in (3, 2, 1, 0):
            self.core_copy(number).start()

    def second(self):
        for number in (3, 2, 1, 0):
            self.core_copy(number).wait_recv()
            shard = self.parts.at[self.number(self.fsdp, number // 2, number % 2)]
            self.add(shard, self.core_slots.at[number])
            if number == 3:
                self.first_copy(1).start()
                self.first_copy(3).start()
            if number == 2:
                self.first_copy(0).start()
            if number == 1:
                self.first_copy(2).start()

    def third(self):
        self.first_copy(1).wait_recv()
        self.add(self.view(0, 1, 0), self.first_slots.at[1])
        self.last_copy(0).start()
        self.first_copy(3).wait_recv()
        self.add(self.view(1, 0, 1), self.first_slots.at[3])
        self.last_copy(1).start()

    def finish(self):
        totals = []
        for side in range(2):
            number = 2 * side
            self.first_copy(number).wait_recv()
            self.last_copy(side).wait_recv()
            total = self.view(0, 0, side)[...].astype(jnp.float32)
            total += self.first_slots[number].astype(jnp.float32)
            totals.append(total + self.last_slots[side].astype(jnp.float32))
        for number in range(4):
            self.core_copy(number).wait_send()
            self.first_copy(number).wait_send()
        for side in range(2):
            self.last_copy(side).wait_send()
        return totals

    @staticmethod
    def scratch(shards, height, width):
        return [
            pltpu.VMEM((shards, height, width), jnp.bfloat16),
            pltpu.VMEM((4, height, width), jnp.bfloat16),
            pltpu.VMEM((4, height, width // 2), jnp.bfloat16),
            pltpu.VMEM((2, height, width // 2), jnp.bfloat16),
            pltpu.SemaphoreType.DMA((10,)),
            pltpu.SemaphoreType.DMA((10,)),
        ]


def leave_kernel(
    sizes, grads_ref, tokens_ref, weight, inner_ref, rows_ref, hidden_ref,
    out_ref, vectors_ref, query_out, key_out, value_out,
    x_ref, term_ref, total, slots, own_vectors, tp_slots, plane_slots,
    sum_sent, sum_got, tp_sent, tp_got, plane_sent, plane_got, swap_sent, swap_got, *sum_scratch,
):
    count = sizes[2]
    me, ctx = lax.axis_index("tp"), lax.axis_index("ctx")
    rows = x_ref.shape[0]
    height = rows // PIECES
    part = grads_ref.shape[1]
    plane_sum = PlaneSum(*sum_scratch)
    shard = plane_sum.parts.shape[1]

    def piece_rows(piece, start=0):
        return pl.ds(pl.multiple_of(start + piece * height, height), height)

    own_columns = pl.ds(pl.multiple_of(ctx * part, part), part)
    swap = Swap(
        swap_sent, swap_got,
        lambda piece: grads_ref.at[piece_rows(piece, (1 - ctx) * rows)],
        lambda piece: x_ref.at[piece_rows(piece), own_columns],
    )

    def product(number):
        columns = pl.ds(pl.multiple_of(number * shard, shard), shard)
        result = dot_rows(tokens_ref[:, columns], x_ref[...])
        plane_sum.parts[number] = result.astype(jnp.bfloat16)

    def opening():
        @pl.loop(0, PIECES)
        def _(piece):
            swap.start(piece)

        x_ref[:, own_columns] = grads_ref[pl.ds(pl.multiple_of(ctx * rows, rows), rows), :]

    def before(step):
        @pl.when(step < PIECES - 1)
        def _():
            swap.wait_arrival(step)

    def after(step):
        @pl.when(step == PIECES - 2)
        def _():
            swap.wait_arrival(PIECES - 1)
            for over_x in (1, 0):
                for over_y in (1, 0):
                    product(plane_sum.number(plane_sum.twin, over_x, over_y))
            plane_sum.start()

        @pl.when(step == PIECES - 1)
        def _():
            for over_x in (1, 0):
                for over_y in (1, 0):
                    product(plane_sum.number(plane_sum.fsdp, over_x, over_y))
            plane_sum.second()

    def closing():
        plane_sum.third()

    input_kernel(
        sizes, x_ref, weight, inner_ref, rows_ref, hidden_ref, out_ref, vectors_ref,
        term_ref, total, slots, own_vectors, tp_slots, plane_slots,
        sum_sent, sum_got, tp_sent, tp_got, plane_sent, plane_got,
        hooks=(opening, before, after, closing), pack_step=PIECES - 1,
    )
    halves = plane_sum.finish()
    third = part // 3
    for side, half in enumerate(halves):
        for i, ref in enumerate((query_out, key_out, value_out)):
            ref[:, side * third : (side + 1) * third] = half[:, i * third : (i + 1) * third]

    @pl.loop(0, PIECES)
    def _(piece):
        swap.wait_sent(piece)


def leave(grads, tokens, weight, inner, row_sums, hidden_sums, collective_id):
    sizes = tuple(lax.axis_size(axis) for axis in ("fsdp", "ctx", "tp"))
    count = sizes[2]
    others = sizes[0] * sizes[1] - 1
    rows, features = tokens.shape
    part = grads.shape[1]
    width = features // count
    height = rows // PIECES
    shard = features // (others + 1)
    packed = 8 + -(-(hidden_sums.shape[1] + 2 * part) // (8 * width)) * 8
    return pl.pallas_call(
        functools.partial(leave_kernel, sizes),
        out_shape=[
            jax.ShapeDtypeStruct((rows, width), jnp.bfloat16),
            jax.ShapeDtypeStruct((packed, width), jnp.float32),
            *[jax.ShapeDtypeStruct((shard, 2 * part // 3), jnp.float32)] * 3,
        ],
        in_specs=[pl.BlockSpec(memory_space=pltpu.VMEM)] * 6,
        out_specs=[pl.BlockSpec(memory_space=pltpu.VMEM)] * 5,
        scratch_shapes=[
            pltpu.VMEM((rows, 2 * part), jnp.bfloat16),
            pltpu.VMEM((height, width), jnp.float32),
            pltpu.VMEM((height, width), jnp.float32),
            pltpu.VMEM((PIECES, count + 1, height, width), jnp.bfloat16),
            pltpu.VMEM((packed, width), jnp.float32),
            pltpu.VMEM((count - 1, 8, width), jnp.float32),
            pltpu.VMEM((others, packed, width), jnp.float32),
            *line_semaphores(count, PIECES)[0],
            pltpu.SemaphoreType.DMA((count - 1,)),
            pltpu.SemaphoreType.DMA((count - 1,)),
            pltpu.SemaphoreType.DMA((others,)),
            pltpu.SemaphoreType.DMA((others,)),
            pltpu.SemaphoreType.DMA((PIECES,)),
            pltpu.SemaphoreType.DMA((PIECES,)),
            *PlaneSum.scratch(others + 1, shard, 2 * part),
        ],
        compiler_params=pltpu.CompilerParams(
            collective_id=collective_id, has_side_effects=True, vmem_limit_bytes=56 << 20
        ),
        cost_estimate=pl.CostEstimate(
            flops=60_000_000_000, bytes_accessed=64 * rows * width, transcendentals=0
        ),
        name="leave",
    )(grads, tokens, weight, inner, row_sums, hidden_sums)


def to_own_rows(wide):
    count = lax.axis_size("tp")
    parts = wide.reshape(PIECES, count, -1, wide.shape[1])
    return lax.dynamic_index_in_dim(parts, lax.axis_index("tp"), 1, keepdims=False).reshape(
        -1, wide.shape[1]
    )


def spread_own(block):
    count = lax.axis_size("tp")
    rows, width = block.shape
    parts = block.reshape(PIECES, count, -1, width)
    got = lax.all_to_all(parts, "tp", split_axis=1, concat_axis=1, tiled=True)
    return got.transpose(0, 2, 1, 3).reshape(rows // count, count * width)


def unspread_own(block):
    count = lax.axis_size("tp")
    rows, width = block.shape
    parts = block.reshape(PIECES, -1, count, width // count).transpose(0, 2, 1, 3)
    got = lax.all_to_all(parts, "tp", split_axis=1, concat_axis=1, tiled=True)
    return got.reshape(rows * count, width // count)


def body(
    tokens,
    segments,
    query_weight,
    key_weight,
    value_weight,
    output_weight,
    expand_weight,
    shrink_weight,
    query_bias,
    value_bias,
    hidden_bias,
    norm_gains,
    row_biases,
    out_grad,
):
    rows = tokens.shape[0]
    head_cols = query_weight.shape[1]
    heads = head_cols // HD
    plane = ("fsdp", "ctx")
    plane_sizes = tuple(lax.axis_size(axis) for axis in plane)
    by_heads = plane_sizes == (4, 2) and heads % 2 == 0

    def weight_rows(weight):
        return lax.all_gather(weight, plane, axis=0, tiled=True)

    marks = jnp.concatenate(
        [norm_gains, row_biases, jnp.zeros((10, norm_gains.shape[1]), norm_gains.dtype)]
    )
    block_index = lax.axis_index("fsdp") * plane_sizes[1] + lax.axis_index("ctx")
    qkv_bias = jnp.stack([query_bias, jnp.zeros_like(query_bias), value_bias])
    qkv_bias = qkv_bias.astype(jnp.float32)
    if by_heads:
        half_bias = qkv_bias.reshape(3, 2, -1).transpose(1, 0, 2).reshape(1, -1)
        wide_tokens, wide_marks, wide_qkv, full_output, qkv_heads = enter(
            tokens, marks, query_weight, key_weight, value_weight, output_weight, half_bias, 0
        )
        queries = keys = values = qkv_heads
        own_heads = heads // 2
        stream_rows = plane_sizes[1] * rows
        stream_ids = lax.dynamic_slice_in_dim(
            segments, lax.axis_index("fsdp") * stream_rows, stream_rows, 0
        )
        bounds = key_bounds(stream_ids, stream_ids, 0)
    else:
        wide_qkv = weight_rows(jnp.concatenate([query_weight, key_weight, value_weight], axis=1))
        wide_tokens, wide_marks = gather_features(tokens, marks, 0)
        qkv = dot_plain(wide_tokens, wide_qkv) + qkv_bias.reshape(1, -1)
        queries, keys, values = jnp.split(qkv.astype(jnp.bfloat16), 3, axis=1)
        own_heads = heads
        keys, values = padded(keys, WIN), padded(values, WIN)
        ids = jnp.concatenate(
            [
                jnp.full((WIN,), -1, jnp.int32),
                segments,
                jnp.full((WIN,), jnp.iinfo(jnp.int32).max, jnp.int32),
            ]
        )
        full_output = weight_rows(output_weight)
        key_ids = lax.dynamic_slice_in_dim(ids, block_index * rows, rows + 2 * WIN, 0)
        bounds = key_bounds(key_ids[WIN : WIN + rows], key_ids, WIN)
    places = (0, own_heads, 2 * own_heads) if by_heads else (0, 0, 0)
    gains = wide_marks[:2].astype(jnp.float32)
    biases = wide_marks[2:6].astype(jnp.float32)
    wide_marks, out_grad = lax.optimization_barrier((wide_marks, out_grad))
    upstream = spread_own(out_grad)
    attended_heads, lse = attend(queries, keys, values, own_heads, *bounds, places)
    attended_heads, upstream = lax.optimization_barrier((attended_heads, upstream))

    own_tokens = to_own_rows(wide_tokens)
    own_rows, features = own_tokens.shape
    hidden_cols = expand_weight.shape[1]

    def shape(extent, kind=jnp.float32):
        return jax.ShapeDtypeStruct(extent, kind)

    own_shape = shape((own_rows, features))
    norm_low, first_norm, normed_one, inverse_one, hidden, activated, *more = relay(
        attended_heads, full_output, expand_weight if by_heads else weight_rows(expand_weight),
        [own_tokens, gains, biases], first_norm_step,
        [own_shape, own_shape, shape((own_rows, 128))],
        [hidden_bias.astype(jnp.float32)[None]], expand_step,
        [shape((rows, hidden_cols)), shape((rows, hidden_cols), jnp.bfloat16)],
        1, "first_norm", rows,
        swap_in=shape((rows, head_cols), jnp.bfloat16) if by_heads else None,
        next_shard=shrink_weight if by_heads else None,
    )
    if by_heads:
        attended, full_expand, full_shrink = more
    else:
        attended = attended_heads
        full_expand, full_shrink = weight_rows(expand_weight), weight_rows(shrink_weight)
    ffn_low, mixed_own, grad_second, second_sums, hidden_low, hidden_sums = relay(
        activated, full_shrink, None,
        [first_norm, upstream, gains, biases], second_norm_step,
        [shape((own_rows, features), jnp.bfloat16), own_shape, shape((8, features))],
        [hidden], shrink_step,
        [shape((rows, hidden_cols), jnp.bfloat16), shape((8, hidden_cols))],
        2, "second_norm", rows,
    )
    mixed = unspread_own(mixed_own)

    def owner_sum(grad):
        return lax.psum_scatter(
            grad, plane, scatter_dimension=0, tiled=True
        )

    hidden_low, shrink_part, expand_part = lax.optimization_barrier(
        (
            hidden_low,
            dot_rows(ffn_low, activated).astype(jnp.bfloat16),
            dot_rows(norm_low, hidden_low).astype(jnp.bfloat16),
        )
    )
    shrink_grad = owner_sum(shrink_part)
    expand_grad = owner_sum(expand_part)
    branch_low, grad_inner, first_sums, attended_grad = relay(
        hidden_low, full_expand, full_output,
        [grad_second, normed_one, inverse_one, gains], first_back_step,
        [own_shape, shape((8, features))],
        [], attended_step,
        [] if by_heads else [shape((rows, head_cols), jnp.bfloat16)],
        3, "first_back", rows,
        swap_out=shape((2 * rows, head_cols // 2), jnp.bfloat16) if by_heads else None,
    )
    attended_grad, shrink_grad, output_part = lax.optimization_barrier(
        (
            attended_grad,
            shrink_grad,
            dot_rows(branch_low, attended).astype(jnp.bfloat16),
        )
    )
    output_grad = owner_sum(output_part)

    if by_heads:
        (grads,) = attend_back(
            queries, keys, values, attended_heads, attended_grad, lse, *bounds, places, True
        )
        grads, mixed, expand_grad = lax.optimization_barrier((grads, mixed, expand_grad))
    else:
        query_low, key_ext, value_ext = attend_back(
            queries, keys, values, attended_heads, attended_grad, lse, *bounds
        )

        def fold(ext):
            edges = jnp.concatenate([ext[:WIN], ext[WIN + rows :]], axis=0)
            around = padded(edges, WIN)
            own = ext[WIN : WIN + rows]
            own = own.at[:WIN].add(around[:WIN]).at[rows - WIN :].add(around[3 * WIN :])
            return own.astype(jnp.bfloat16)

        qkv_low = jnp.concatenate([query_low, fold(key_ext), fold(value_ext)], axis=1)
    row_sums = jnp.concatenate(
        [
            first_sums[0:1], second_sums[0:1],
            first_sums[2:3], first_sums[1:2], second_sums[2:3], second_sums[1:2],
            jnp.zeros_like(first_sums[:2]),
        ]
    )
    sides = 2 if by_heads else 1

    def by_kind(columns):
        parts = columns.reshape(-1, sides, 3, head_cols // sides)
        return [parts[:, :, i].reshape(-1, head_cols) for i in range(3)]

    if by_heads:
        input_grad, vectors, query_grad, key_grad, value_grad = leave(
            grads, wide_tokens, wide_qkv, grad_inner, row_sums, hidden_sums[:1], 4
        )
    else:
        input_grad, vectors = input_sum(
            qkv_low, wide_qkv, grad_inner, row_sums, hidden_sums[:1], 4
        )
        qkv_grad = owner_sum(dot_rows(wide_tokens, qkv_low).astype(jnp.bfloat16))
        query_grad, key_grad, value_grad = by_kind(qkv_grad.astype(jnp.float32))
    hidden_rows = hidden_cols // head_cols
    query_sum, _, value_sum = by_kind(
        vectors[8 + hidden_rows : 8 + hidden_rows + 3].reshape(1, -1)
    )
    return (
        mixed,
        input_grad,
        query_grad,
        key_grad,
        value_grad,
        output_grad.astype(jnp.float32),
        expand_grad.astype(jnp.float32),
        shrink_grad.astype(jnp.float32),
        query_sum[0],
        value_sum[0],
        vectors[8 : 8 + hidden_rows].reshape(-1),
        vectors[:2],
        vectors[2:6],
    )


def solution(mesh):
    rows, whole, cols = P(("fsdp", "ctx"), "tp"), P(), P("tp")
    wide = P(None, "tp")
    return jax.shard_map(
        body,
        mesh=mesh,
        in_specs=(rows, whole) + (rows,) * 6 + (cols,) * 3 + (wide,) * 2 + (rows,),
        out_specs=(rows,) * 8 + (cols,) * 3 + (wide,) * 2,
        check_vma=False,
    )
```

```python
import functools
import math

import jax
import jax.numpy as jnp
from jax import lax
from jax.experimental import pallas as pl
from jax.experimental.pallas import tpu as pltpu
from jax.sharding import PartitionSpec as P

HD = 128
WIN = 1024
QB = 512
KB = 512

epsilon = 1e-06
hidden_floor = -1e30
score_scale = 1.0 / math.sqrt(HD)
log2_e = 1.0 / math.log(2.0)


def dot_plain(left, right):
    return jnp.dot(left, right, preferred_element_type=jnp.float32)


def dot_rows(left, right):
    return lax.dot_general(
        left, right, (((0,), (0,)), ((), ())), preferred_element_type=jnp.float32
    )


def dot_cols(left, right):
    return lax.dot_general(
        left, right, (((1,), (1,)), ((), ())), preferred_element_type=jnp.float32
    )


def attend_kernel(first, last, q_ref, k_ref, v_ref, low_ref, high_ref, out_ref, lse_ref, vt):
    block = pl.program_id(1)
    rows = q_ref.shape[0]

    @pl.when(block == 0)
    def _():
        vt[...] = v_ref[...].T

    queries = q_ref[...]
    low, high = low_ref[...], high_ref[...]
    places = lax.broadcasted_iota(jnp.int32, (KB, rows), 0)

    def step(number, carry):
        top, total, mixed = carry
        start = pl.multiple_of(number * KB, KB)
        scores = dot_cols(k_ref[pl.ds(start, KB), :], queries) * (score_scale * log2_e)
        keep = (places >= low - start) & (places <= high - start)
        scores = jnp.where(keep, scores, hidden_floor)
        new_top = jnp.maximum(top, jnp.max(scores, axis=0, keepdims=True))
        shrink = jnp.exp2(top - new_top)
        powers = jnp.exp2(scores - new_top)
        total = total * shrink + jnp.sum(powers, axis=0, keepdims=True)
        mixed = mixed * shrink + dot_plain(vt[:, pl.ds(start, KB)], powers.astype(jnp.bfloat16))
        return new_top, total, mixed

    top, total, mixed = lax.fori_loop(
        first[block],
        last[block],
        step,
        (
            jnp.full((1, rows), hidden_floor, jnp.float32),
            jnp.zeros((1, rows), jnp.float32),
            jnp.zeros((HD, rows), jnp.float32),
        ),
    )
    out_ref[...] = (mixed / total).T.astype(out_ref.dtype)
    lse_ref[...] = (top + jnp.log2(total))[None]


def attend(queries, keys, values, heads, low, high, first, last, places=(0, 0, 0)):
    rows, span = queries.shape[0], keys.shape[0]
    width = heads * HD
    q_at, k_at, v_at = places
    return pl.pallas_call(
        attend_kernel,
        out_shape=(
            jax.ShapeDtypeStruct((rows, width), jnp.bfloat16),
            jax.ShapeDtypeStruct((heads, 1, rows), jnp.float32),
        ),
        grid_spec=pltpu.PrefetchScalarGridSpec(
            num_scalar_prefetch=2,
            grid=(heads, rows // QB),
            in_specs=[
                pl.BlockSpec((QB, HD), lambda h, i, *_: (i, h + q_at)),
                pl.BlockSpec((span, HD), lambda h, i, *_: (0, h + k_at)),
                pl.BlockSpec((span, HD), lambda h, i, *_: (0, h + v_at)),
                pl.BlockSpec((1, QB), lambda h, i, *_: (0, i)),
                pl.BlockSpec((1, QB), lambda h, i, *_: (0, i)),
            ],
            out_specs=[
                pl.BlockSpec((QB, HD), lambda h, i, *_: (i, h)),
                pl.BlockSpec((1, 1, QB), lambda h, i, *_: (h, 0, i)),
            ],
            scratch_shapes=[pltpu.VMEM((HD, span), jnp.bfloat16)],
        ),
        compiler_params=pltpu.CompilerParams(vmem_limit_bytes=32 << 20),
        cost_estimate=pl.CostEstimate(
            flops=3 * rows * span * width,
            bytes_accessed=2 * (2 * rows + 2 * span) * width,
            transcendentals=rows * span * heads,
        ),
        name="attend",
    )(first, last, queries, keys, values, low, high)


def attend_back_kernel(
    first, last, q_ref, k_ref, v_ref, o_ref, g_ref, lse_ref, low_ref, high_ref,
    *outputs,
):
    *results, kt, dk_sum, dv_sum = outputs
    head, block = pl.program_id(0), pl.program_id(1)
    rows = q_ref.shape[0]

    @pl.when(block == 0)
    def _():
        kt[...] = k_ref[...].T
        dk_sum[...] = jnp.zeros_like(dk_sum)
        dv_sum[...] = jnp.zeros_like(dv_sum)

    queries = q_ref[...]
    upstream = g_ref[...]
    lse = lse_ref[0]
    low, high = low_ref[...], high_ref[...]
    places = lax.broadcasted_iota(jnp.int32, (KB, rows), 0)
    product = upstream.astype(jnp.float32) * o_ref[...].astype(jnp.float32)
    delta = jnp.sum(product.T, axis=0, keepdims=True)

    def step(number, dq):
        start = pl.multiple_of(number * KB, KB)
        window = pl.ds(start, KB)
        scores = dot_cols(k_ref[window, :], queries) * (score_scale * log2_e)
        keep = (places >= low - start) & (places <= high - start)
        probs = jnp.exp2(jnp.where(keep, scores - lse, hidden_floor))
        prob_grad = dot_cols(v_ref[window, :], upstream)
        score_grad = (probs * (prob_grad - delta)).astype(jnp.bfloat16)
        dv_sum[window, :] += dot_plain(probs.astype(jnp.bfloat16), upstream)
        dk_sum[window, :] += dot_plain(score_grad, queries)
        return dq + dot_plain(kt[:, window], score_grad)

    dq = lax.fori_loop(
        first[block], last[block], step, jnp.zeros((HD, rows), jnp.float32)
    )
    dq = (dq * score_scale).T
    if len(results) == 1:
        width = results[0].shape[1] // 3

        def place(part):
            start = pl.multiple_of(part * width + head * HD, HD)
            return results[0].at[:, pl.ds(start, HD)]

        query_place = place(0).at[pl.ds(pl.multiple_of(block * rows, rows), rows)]
        key_place, value_place = place(1), place(2)
    else:
        query_place, key_place, value_place = results
    query_place[...] = dq.astype(query_place.dtype)

    @pl.when(block == pl.num_programs(1) - 1)
    def _():
        key_place[...] = (dk_sum[...] * score_scale).astype(key_place.dtype)
        value_place[...] = dv_sum[...].astype(value_place.dtype)


def attend_back(
    queries, keys, values, out, upstream, lse, low, high, first, last, places=(0, 0, 0), merged=False
):
    rows, width = out.shape
    span = keys.shape[0]
    heads = width // HD
    q_at, k_at, v_at = places
    row_spec = pl.BlockSpec((QB, HD), lambda h, i, *_: (i, h))
    key_spec = pl.BlockSpec((span, HD), lambda h, i, *_: (0, h))
    mark_spec = pl.BlockSpec((1, QB), lambda h, i, *_: (0, i))
    return pl.pallas_call(
        attend_back_kernel,
        out_shape=[jax.ShapeDtypeStruct((rows, 3 * width), jnp.bfloat16)]
        if merged
        else [
            jax.ShapeDtypeStruct((rows, width), jnp.bfloat16),
            jax.ShapeDtypeStruct((span, width), jnp.float32),
            jax.ShapeDtypeStruct((span, width), jnp.float32),
        ],
        grid_spec=pltpu.PrefetchScalarGridSpec(
            num_scalar_prefetch=2,
            grid=(heads, rows // QB),
            in_specs=[
                pl.BlockSpec((QB, HD), lambda h, i, *_: (i, h + q_at)),
                pl.BlockSpec((span, HD), lambda h, i, *_: (0, h + k_at)),
                pl.BlockSpec((span, HD), lambda h, i, *_: (0, h + v_at)),
                row_spec, row_spec,
                pl.BlockSpec((1, 1, QB), lambda h, i, *_: (h, 0, i)),
                mark_spec, mark_spec,
            ],
            out_specs=[pl.BlockSpec((rows, 3 * width), lambda h, i, *_: (0, 0))]
            if merged
            else [row_spec, key_spec, key_spec],
            scratch_shapes=[
                pltpu.VMEM((HD, span), jnp.bfloat16),
                pltpu.VMEM((span, HD), jnp.float32),
                pltpu.VMEM((span, HD), jnp.float32),
            ],
        ),
        compiler_params=pltpu.CompilerParams(vmem_limit_bytes=32 << 20),
        cost_estimate=pl.CostEstimate(
            flops=8 * rows * span * width,
            bytes_accessed=2 * (4 * rows + 4 * span) * width,
            transcendentals=rows * span * heads,
        ),
        name="attend_back",
    )(first, last, queries, keys, values, out, upstream, lse, low, high)


def key_bounds(query_ids, key_ids, offset):
    rows, span = query_ids.shape[0], key_ids.shape[0]
    start = jnp.sum(key_ids[:, None] < query_ids[None, :], axis=0, dtype=jnp.int32)
    stop = jnp.sum(key_ids[:, None] <= query_ids[None, :], axis=0, dtype=jnp.int32)
    places = jnp.arange(rows, dtype=jnp.int32) + offset
    low = jnp.maximum(start, places - WIN)
    high = jnp.minimum(stop - 1, places + WIN)
    first = jnp.min(low.reshape(-1, QB), axis=1) // KB
    last = jnp.max(high.reshape(-1, QB), axis=1) // KB + 1
    return low[None], high[None], first, last


def document_bounds(ids, first_id):
    rows = ids.shape[0]
    second = jnp.sum(ids <= first_id, dtype=jnp.int32)
    third = jnp.sum(ids <= first_id + 1, dtype=jnp.int32)

    def bounds_at(places):
        start = jnp.where(places < second, 0, jnp.where(places < third, second, third))
        stop = jnp.where(places < second, second, jnp.where(places < third, third, rows))
        return jnp.maximum(start, places - WIN), jnp.minimum(stop - 1, places + WIN)

    low, high = bounds_at(jnp.arange(rows, dtype=jnp.int32))
    starts = jnp.arange(0, rows, QB, dtype=jnp.int32)
    first = bounds_at(starts)[0] // KB
    last = bounds_at(starts + (QB - 1))[1] // KB + 1
    return low[None], high[None], first, last


def padded(block, width):
    count = lax.axis_size("ctx")
    forward = [(i, i + 1) for i in range(count - 1)]
    backward = [(target, source) for source, target in forward]
    below = lax.ppermute(block[block.shape[0] - width :], "ctx", forward)
    above = lax.ppermute(block[:width], "ctx", backward)
    return jnp.concatenate([below, block, above], axis=0)


def norm_parts(rows):
    mean = jnp.mean(rows, axis=-1, keepdims=True)
    square = jnp.mean(rows * rows, axis=-1, keepdims=True)
    inverse = lax.rsqrt(square - mean * mean + epsilon)
    return (rows - mean) * inverse, inverse


def norm_back(upstream, normed, inverse, gain):
    scaled = upstream * gain
    first_mean = jnp.mean(scaled, axis=-1, keepdims=True)
    second_mean = jnp.mean(scaled * normed, axis=-1, keepdims=True)
    return inverse * (scaled - first_mean - normed * second_mean)


def gelu_tanh(values):
    return jax.nn.gelu(values, approximate=True)


MESH = pl.DeviceIdType.MESH
PIECES = 8
TILE = 512


def greet(me, count, others=()):
    barrier = pltpu.get_barrier_semaphore()

    @pl.when(me > 0)
    def _():
        pl.semaphore_signal(barrier, inc=1, device_id={"tp": me - 1}, device_id_type=MESH)

    @pl.when(me < count - 1)
    def _():
        pl.semaphore_signal(barrier, inc=1, device_id={"tp": me + 1}, device_id_type=MESH)

    for other in others:
        pl.semaphore_signal(barrier, inc=1, device_id=other, device_id_type=MESH)

    @pl.when((me == 0) | (me == count - 1))
    def _():
        pl.semaphore_wait(barrier, 1 + len(others))

    @pl.when((me > 0) & (me < count - 1))
    def _():
        pl.semaphore_wait(barrier, 2 + len(others))


def peers_along_tp(me, count):
    return [{"tp": lax.rem(me + i, count)} for i in range(1, count)]


def greet_peers(peers):
    barrier = pltpu.get_barrier_semaphore()
    for peer in peers:
        pl.semaphore_signal(barrier, inc=1, device_id=peer, device_id_type=MESH)
    pl.semaphore_wait(barrier, len(peers))


class Exchange:
    def __init__(self, peers, sent, got, source, place):
        self.peers, self.sent, self.got = peers, sent, got
        self.source, self.place = source, place

    def copies(self):
        for i, peer in enumerate(self.peers):
            yield pltpu.make_async_remote_copy(
                src_ref=self.source(i + 1),
                dst_ref=self.place(i),
                send_sem=self.sent.at[i],
                recv_sem=self.got.at[i],
                device_id=peer,
                device_id_type=MESH,
            )

    def start(self):
        for copy in self.copies():
            copy.start()

    def wait_arrivals(self):
        for copy in self.copies():
            copy.wait_recv()

    def wait_sent(self):
        for copy in self.copies():
            copy.wait_send()


def at_distance(me, count, distance, action):
    for index in (me - distance, me + distance):

        @pl.when((index >= 0) & (index < count))
        def _(index=index):
            action(index)


class Line:
    def __init__(self, me, count, sum_slots, sum_sent, sum_got, spread_view, spread_sent, spread_got):
        self.me, self.count = me, count
        self.sum_slots, self.sum_sent, self.sum_got = sum_slots, sum_sent, sum_got
        self.spread_view, self.spread_sent, self.spread_got = spread_view, spread_sent, spread_got

    def sum_copy(self, piece, owner):
        onward = jnp.where(owner > self.me, self.me + 1, self.me - 1)
        place = jnp.where((owner < self.me) & (owner == self.me - 1), self.count, owner)
        return pltpu.make_async_remote_copy(
            src_ref=self.sum_slots.at[piece, owner],
            dst_ref=self.sum_slots.at[piece, place],
            send_sem=self.sum_sent.at[piece, owner],
            recv_sem=self.sum_got.at[piece, place],
            device_id={"tp": onward},
            device_id_type=MESH,
        )

    def sum_arrival(self, piece, place):
        pltpu.make_async_copy(
            self.sum_slots.at[piece, place],
            self.sum_slots.at[piece, place],
            self.sum_got.at[piece, place],
        ).wait()

    def sum_start(self, piece, term):
        me, count = self.me, self.count

        @pl.when((me == 0) | (me == count - 1))
        def _():
            for k in range(count - 1):
                owner = jnp.where(me == 0, count - 1 - k, k)
                self.sum_slots[piece, owner] = term(owner).astype(jnp.bfloat16)
                self.sum_copy(piece, owner).start()

    def sum_onward(self, piece, term, distances):
        me, count = self.me, self.count

        @pl.when((me > 0) & (me < count - 1))
        def _():
            for distance in distances:

                def pass_on(owner):
                    self.sum_arrival(piece, owner)
                    total = self.sum_slots[piece, owner].astype(jnp.float32) + term(owner)
                    self.sum_slots[piece, owner] = total.astype(jnp.bfloat16)
                    self.sum_copy(piece, owner).start()

                at_distance(me, count, distance, pass_on)

    def sum_end(self, piece, total):
        me, count = self.me, self.count

        @pl.when(me > 0)
        def _():
            self.sum_arrival(piece, me)
            total[...] += self.sum_slots[piece, me].astype(jnp.float32)

        @pl.when(me < count - 1)
        def _():
            self.sum_arrival(piece, count)
            total[...] += self.sum_slots[piece, count].astype(jnp.float32)

    def sum_finish(self, pieces):
        @pl.loop(0, pieces)
        def _(piece):
            for distance in range(1, self.count):
                at_distance(
                    self.me, self.count, distance,
                    lambda owner: self.sum_copy(piece, owner).wait_send(),
                )

    def spread_copy(self, piece, owner, to, sent, source=None):
        return pltpu.make_async_remote_copy(
            src_ref=self.spread_view(piece, owner) if source is None else source,
            dst_ref=self.spread_view(piece, owner),
            send_sem=self.spread_sent.at[piece, sent],
            recv_sem=self.spread_got.at[piece, owner],
            device_id={"tp": to},
            device_id_type=MESH,
        )

    def own_copies(self, piece, action, source=None):
        me, count = self.me, self.count

        @pl.when(me > 0)
        def _():
            action(self.spread_copy(piece, me, me - 1, count, source))

        @pl.when(me < count - 1)
        def _():
            action(self.spread_copy(piece, me, me + 1, me, source))

    def spread_start(self, piece, source=None):
        self.own_copies(piece, lambda copy: copy.start(), source)

    def onward_copy(self, piece, owner, action):
        me, count = self.me, self.count

        @pl.when((owner < me) & (me < count - 1))
        def _():
            action(self.spread_copy(piece, owner, me + 1, owner))

        @pl.when((owner > me) & (me > 0))
        def _():
            action(self.spread_copy(piece, owner, me - 1, owner))

    def spread_onward(self, piece, distance):
        def pass_on(owner):
            view = self.spread_view(piece, owner)
            pltpu.make_async_copy(view, view, self.spread_got.at[piece, owner]).wait()
            self.onward_copy(piece, owner, lambda copy: copy.start())

        at_distance(self.me, self.count, distance, pass_on)

    def spread_finish(self, pieces, source=None):
        @pl.loop(0, pieces)
        def _(piece):
            self.own_copies(
                piece, lambda copy: copy.wait_send(), None if source is None else source(piece)
            )
            for distance in range(1, self.count):
                at_distance(
                    self.me, self.count, distance,
                    lambda owner: self.onward_copy(piece, owner, lambda copy: copy.wait_send()),
                )


def line_semaphores(count, pieces):
    return [
        pltpu.SemaphoreType.DMA((pieces, count)),
        pltpu.SemaphoreType.DMA((pieces, count + 1)),
    ], [
        pltpu.SemaphoreType.DMA((pieces, count + 1)),
        pltpu.SemaphoreType.DMA((pieces, count)),
    ]


def gather_kernel(
    count, x_ref, marks_ref, out_ref, marks_out, slots, sent, got, marks_sent, marks_got
):
    me = lax.axis_index("tp")
    height = x_ref.shape[0] // PIECES
    width = x_ref.shape[1]

    def view(piece, owner):
        return out_ref.at[
            pl.ds(pl.multiple_of(piece * height, height), height),
            pl.ds(pl.multiple_of(owner * width, width), width),
        ]

    def source(piece):
        return x_ref.at[pl.ds(pl.multiple_of(piece * height, height), height)]

    line = Line(me, count, None, None, None, view, sent, got)
    peers = peers_along_tp(me, count)
    greet_peers(peers)

    @pl.loop(0, PIECES)
    def _(piece):
        line.spread_start(piece, source(piece))

    marks = Exchange(
        peers, marks_sent, marks_got, lambda _: marks_ref, lambda i: slots.at[i]
    )
    marks.start()
    own = pl.ds(pl.multiple_of(me * width, width), width)
    out_ref[:, own] = x_ref[...]
    marks_out[:, own] = marks_ref[...]
    for distance in range(1, count):

        @pl.loop(0, PIECES)
        def _(piece, distance=distance):
            line.spread_onward(piece, distance)

    marks.wait_arrivals()
    for i in range(1, count):
        owner = lax.rem(me - i + count, count)
        marks_out[:, pl.ds(pl.multiple_of(owner * width, width), width)] = slots[i - 1]
    marks.wait_sent()
    line.spread_finish(PIECES, source)


def gather_features(x, marks, collective_id):
    count = lax.axis_size("tp")
    rows, width = x.shape
    return pl.pallas_call(
        functools.partial(gather_kernel, count),
        out_shape=[
            jax.ShapeDtypeStruct((rows, count * width), x.dtype),
            jax.ShapeDtypeStruct((marks.shape[0], count * width), marks.dtype),
        ],
        in_specs=[pl.BlockSpec(memory_space=pltpu.VMEM)] * 2,
        out_specs=[pl.BlockSpec(memory_space=pltpu.VMEM)] * 2,
        scratch_shapes=[
            pltpu.VMEM((count - 1, *marks.shape), marks.dtype),
            *line_semaphores(count, PIECES)[1],
            pltpu.SemaphoreType.DMA((count - 1,)),
            pltpu.SemaphoreType.DMA((count - 1,)),
        ],
        compiler_params=pltpu.CompilerParams(
            collective_id=collective_id, has_side_effects=True, vmem_limit_bytes=16 << 20
        ),
        cost_estimate=pl.CostEstimate(
            flops=0, bytes_accessed=64 * rows * count * width, transcendentals=0
        ),
        name="gather_features",
    )(x, marks)


class Swap:
    def __init__(self, sent, got, source, place):
        self.sent, self.got, self.source, self.place = sent, got, source, place

    def copy(self, piece):
        return pltpu.make_async_remote_copy(
            src_ref=self.source(piece),
            dst_ref=self.place(piece),
            send_sem=self.sent.at[piece],
            recv_sem=self.got.at[piece],
            device_id={"ctx": 1 - lax.axis_index("ctx")},
            device_id_type=MESH,
        )

    def start(self, piece):
        self.copy(piece).start()

    def wait_arrival(self, piece):
        self.copy(piece).wait_recv()

    def wait_sent(self, piece):
        self.copy(piece).wait_send()


class PlaneGather:
    def __init__(self, whole, sent, got):
        self.whole, self.sent, self.got = whole, sent, got
        fsdp, self.ctx = lax.axis_index("fsdp"), lax.axis_index("ctx")
        self.fsdp = fsdp
        self.twin = fsdp + 1 - 2 * lax.rem(fsdp, 2)
        self.along_x = lax.rem(fsdp + 2, 4)
        self.twin_x = lax.rem(self.twin + 2, 4)
        self.core_peer = {"fsdp": self.twin}
        self.x_peer = {"fsdp": self.along_x}
        self.y_peer = {"ctx": 1 - self.ctx}

    def peers(self):
        return [self.core_peer, self.x_peer, self.y_peer]

    def shard(self, fsdp, ctx, half=None):
        height = self.whole.shape[0] // 8
        start = (fsdp * 2 + ctx) * height
        if half is not None:
            height //= 2
            start += half * height
        return self.whole.at[pl.ds(pl.multiple_of(start, height), height)]

    def copy(self, number, view, peer):
        return pltpu.make_async_remote_copy(
            src_ref=view,
            dst_ref=view,
            send_sem=self.sent.at[number],
            recv_sem=self.got.at[number],
            device_id=peer,
            device_id_type=MESH,
        )

    def copies(self):
        own = self.shard(self.fsdp, self.ctx)
        from_x = self.shard(self.along_x, self.ctx)
        from_y = self.shard(self.fsdp, 1 - self.ctx)
        return [
            (own, self.core_peer),
            (own, self.x_peer),
            (own, self.y_peer),
            (from_x, self.core_peer),
            (self.shard(self.along_x, self.ctx, 0), self.y_peer),
            (from_y, self.core_peer),
            (self.shard(self.fsdp, 1 - self.ctx, 1), self.x_peer),
            (self.shard(self.along_x, 1 - self.ctx, 0), self.core_peer),
            (self.shard(self.along_x, 1 - self.ctx, 1), self.core_peer),
        ]

    def arrivals(self):
        return [
            self.shard(self.twin, self.ctx),
            self.shard(self.along_x, self.ctx),
            self.shard(self.fsdp, 1 - self.ctx),
            self.shard(self.twin_x, self.ctx),
            self.shard(self.along_x, 1 - self.ctx, 0),
            self.shard(self.twin, 1 - self.ctx),
            self.shard(self.along_x, 1 - self.ctx, 1),
            self.shard(self.twin_x, 1 - self.ctx, 0),
            self.shard(self.twin_x, 1 - self.ctx, 1),
        ]

    def start(self, *numbers):
        copies = self.copies()
        for number in numbers:
            self.copy(number, *copies[number]).start()

    def wait(self, *numbers):
        arrivals = self.arrivals()
        for number in numbers:
            view = arrivals[number]
            pltpu.make_async_copy(view, view, self.got.at[number]).wait()

    def put(self, shard, done):
        copy = pltpu.make_async_copy(shard, self.shard(self.fsdp, self.ctx), done)
        copy.start()
        copy.wait()

    def first(self):
        self.start(1, 2, 0)

    def second(self):
        self.wait(1)
        self.start(4, 3)
        self.wait(2)
        self.start(6, 5)

    def third(self):
        self.wait(4)
        self.start(7)
        self.wait(6)
        self.start(8)

    def last(self):
        self.wait(0, 3, 5, 7, 8)

    def wait_sent(self):
        for number, (view, peer) in enumerate(self.copies()):
            self.copy(number, view, peer).wait_send()


def enter_kernel(
    count, x_ref, marks_ref, query_ref, key_ref, value_ref, output_ref, expand_ref, bias,
    wide, marks_out, weight, output_weight, expand_weight, heads,
    mark_slots, stage, sent, got, marks_sent, marks_got,
    weight_sent, weight_got, output_sent, output_got, expand_sent, expand_got,
    swap_sent, swap_got, put_done,
):
    me, ctx = lax.axis_index("tp"), lax.axis_index("ctx")
    rows, width = x_ref.shape
    height = rows // PIECES
    half = query_ref.shape[1] // 2
    part = 3 * half

    def piece_rows(piece, start=0):
        return pl.ds(pl.multiple_of(start + piece * height, height), height)

    def view(piece, owner):
        return wide.at[piece_rows(piece), pl.ds(pl.multiple_of(owner * width, width), width)]

    gather = PlaneGather(weight, weight_sent, weight_got)
    output_gather = PlaneGather(output_weight, output_sent, output_got)
    expand_gather = PlaneGather(expand_weight, expand_sent, expand_got)
    own_shard = gather.shard(gather.fsdp, ctx)
    own = pl.ds(pl.multiple_of(me * width, width), width)
    puts = [
        (ref.at[:, pl.ds(side * half, half)], own_shard.at[:, pl.ds(side * part + i * half, half)])
        for side in range(2)
        for i, ref in enumerate((query_ref, key_ref, value_ref))
    ]
    puts += [
        (output_ref, output_gather.shard(gather.fsdp, ctx)),
        (x_ref, wide.at[:, own]),
        (expand_ref, expand_gather.shard(gather.fsdp, ctx)),
    ]
    puts = [
        pltpu.make_async_copy(source, place, put_done.at[i])
        for i, (source, place) in enumerate(puts)
    ]
    for put in puts:
        put.start()
    line = Line(me, count, None, None, None, view, sent, got)
    tp_peers = peers_along_tp(me, count)
    greet_peers(tp_peers + gather.peers())

    def source(piece):
        return x_ref.at[piece_rows(piece)]

    @pl.loop(0, PIECES)
    def _(piece):
        line.spread_start(piece, source(piece))

    for put in puts[:7]:
        put.wait()
    gather.first()
    output_gather.first()
    marks = Exchange(
        tp_peers, marks_sent, marks_got, lambda _: marks_ref, lambda i: mark_slots.at[i]
    )
    marks.start()
    marks_out[:, own] = marks_ref[...]
    for put in puts[7:]:
        put.wait()
    swap = Swap(
        swap_sent, swap_got,
        lambda piece: stage.at[piece_rows(piece)],
        lambda piece: heads.at[piece_rows(piece, ctx * rows)],
    )

    def products(piece, side, place):
        x = wide[piece_rows(piece), :]

        @pl.loop(0, 3)
        def _(tile):
            start = pl.multiple_of(side * part + tile * half, half)
            columns = pl.ds(start, half)
            values = dot_plain(x, weight[:, columns]) + bias[:, columns]
            place[:, pl.ds(pl.multiple_of(tile * half, half), half)] = values.astype(jnp.bfloat16)

    for distance in range(1, count):
        if distance == count - 1:
            gather.last()

        @pl.loop(0, PIECES)
        def _(piece, distance=distance):
            line.spread_onward(piece, distance)
            if distance == count - 1:
                products(piece, 1 - ctx, stage.at[piece_rows(piece)])
                swap.start(piece)
                products(piece, ctx, heads.at[piece_rows(piece, ctx * rows)])
                pl.when(piece == PIECES // 2)(expand_gather.second)

        if distance == 1:
            gather.second()
            output_gather.second()
            expand_gather.first()
        if distance == count - 2:
            gather.third()
            output_gather.third()

    marks.wait_arrivals()
    for i in range(1, count):
        owner = lax.rem(me - i + count, count)
        marks_out[:, pl.ds(pl.multiple_of(owner * width, width), width)] = mark_slots[i - 1]

    @pl.loop(0, PIECES)
    def _(piece):
        swap.wait_arrival(piece)
        swap.wait_sent(piece)

    expand_gather.third()
    output_gather.last()
    expand_gather.last()
    marks.wait_sent()
    gather.wait_sent()
    output_gather.wait_sent()
    expand_gather.wait_sent()
    line.spread_finish(PIECES, source)


def enter(
    tokens, marks, query_weight, key_weight, value_weight, output_weight, expand_weight, bias,
    collective_id,
):
    count = lax.axis_size("tp")
    rows, width = tokens.shape
    head_cols = query_weight.shape[1]
    plane = 8
    part = 3 * head_cols // 2
    return pl.pallas_call(
        functools.partial(enter_kernel, count),
        out_shape=[
            jax.ShapeDtypeStruct((rows, count * width), tokens.dtype),
            jax.ShapeDtypeStruct((marks.shape[0], count * width), marks.dtype),
            jax.ShapeDtypeStruct((plane * query_weight.shape[0], 2 * part), query_weight.dtype),
            jax.ShapeDtypeStruct(
                (plane * output_weight.shape[0], output_weight.shape[1]), output_weight.dtype
            ),
            jax.ShapeDtypeStruct(
                (plane * expand_weight.shape[0], expand_weight.shape[1]), expand_weight.dtype
            ),
            jax.ShapeDtypeStruct((2 * rows, part), jnp.bfloat16),
        ],
        in_specs=[
            pl.BlockSpec(memory_space=pl.ANY),
            pl.BlockSpec(memory_space=pltpu.VMEM),
            *[pl.BlockSpec(memory_space=pl.ANY)] * 5,
            pl.BlockSpec(memory_space=pltpu.VMEM),
        ],
        out_specs=[
            *[pl.BlockSpec(memory_space=pltpu.VMEM)] * 4,
            pl.BlockSpec(memory_space=pl.ANY),
            pl.BlockSpec(memory_space=pltpu.VMEM),
        ],
        scratch_shapes=[
            pltpu.VMEM((count - 1, *marks.shape), marks.dtype),
            pltpu.VMEM((rows, part), jnp.bfloat16),
            *line_semaphores(count, PIECES)[1],
            pltpu.SemaphoreType.DMA((count - 1,)),
            pltpu.SemaphoreType.DMA((count - 1,)),
            *[pltpu.SemaphoreType.DMA((9,))] * 6,
            pltpu.SemaphoreType.DMA((PIECES,)),
            pltpu.SemaphoreType.DMA((PIECES,)),
            pltpu.SemaphoreType.DMA((9,)),
        ],
        compiler_params=pltpu.CompilerParams(
            collective_id=collective_id, has_side_effects=True, vmem_limit_bytes=40 << 20
        ),
        cost_estimate=pl.CostEstimate(
            flops=80_000_000_000, bytes_accessed=64 * rows * count * width, transcendentals=0
        ),
        name="enter",
    )(tokens, marks, query_weight, key_weight, value_weight, output_weight, expand_weight, bias)


def relay_kernel(count, row_step, use_step, sizes, *refs):
    row_in, use_in, row_out, use_out, shared, swap_in, swap_out, next_shard = sizes
    refs = list(refs)

    def take(number):
        taken = refs[:number]
        del refs[:number]
        return taken

    x_ref, sum_weight = take(2)
    use_weight = sum_weight if shared else take(1)[0]
    row_inputs, use_inputs = take(row_in), take(use_in)
    next_ref = take(1)[0] if next_shard else None
    (gathered,) = take(1)
    row_outputs, use_outputs = take(row_out), take(use_out)
    swapped = take(1)[0] if swap_in or swap_out else None
    next_whole = take(1)[0] if next_shard else None
    terms, total, slots, sum_sent, sum_got, spread_sent, spread_got = take(7)
    me, ctx = lax.axis_index("tp"), lax.axis_index("ctx")
    rows = gathered.shape[0]
    height = rows // PIECES
    own = height // count
    width = sum_weight.shape[0]

    def piece_rows(piece, start=0):
        return pl.ds(pl.multiple_of(start + piece * height, height), height)

    def view(piece, owner):
        return gathered.at[pl.ds(pl.multiple_of(piece * height + owner * own, own), own)]

    line = Line(me, count, slots, sum_sent, sum_got, view, spread_sent, spread_got)
    next_gather = None
    if next_shard:
        next_gather = PlaneGather(next_whole, *take(2))
        greet(me, count, next_gather.peers())
    else:
        greet(me, count, [{"ctx": 1 - ctx}] if swap_in or swap_out else [])
    swap = None
    if swap_in:
        half = x_ref.shape[1]
        own_half = pl.ds(pl.multiple_of(ctx * half, half), half)
        swap = Swap(
            *take(2),
            lambda piece: x_ref.at[piece_rows(piece, (1 - ctx) * rows)],
            lambda piece: swapped.at[piece_rows(piece), own_half],
        )

        @pl.loop(0, PIECES)
        def _(piece):
            swap.start(piece)
            swapped[piece_rows(piece), own_half] = x_ref[piece_rows(piece, ctx * rows), :]

    if next_gather is not None:
        next_gather.put(next_ref, take(1)[0])
        next_gather.first()
    if swap_out:
        stage, swap_sent, swap_got = take(3)
        half = swapped.shape[1]
        swap = Swap(
            swap_sent, swap_got,
            lambda piece: stage.at[piece_rows(piece)],
            lambda piece: swapped.at[piece_rows(piece, ctx * rows)],
        )

    @pl.loop(0, PIECES + 5)
    def _(step):
        odd = lax.rem(step, 2)

        def term_of(parity):
            return lambda owner: terms[parity, pl.ds(pl.multiple_of(owner * own, own), own), :]

        def late(pieces, action):
            @pl.when((step >= pieces) & (step < PIECES + pieces))
            def _():
                action(step - pieces)

        def use(piece):
            part = piece_rows(piece)
            result = use_step(part, gathered[part, :], use_weight, use_inputs, use_outputs)
            if swap_out:
                here = ctx == 0
                left, right = result[:, :half], result[:, half:]
                stage[part, :] = jnp.where(here, right, left)
                swap.start(piece)
                swapped[piece_rows(piece, ctx * rows), :] = jnp.where(here, left, right)

        def form(piece):
            if swap_in:
                swap.wait_arrival(piece)
            x = (swapped if swap_in else x_ref)[piece_rows(piece), :]

            @pl.loop(0, width // TILE)
            def _(tile):
                part = pl.ds(pl.multiple_of(tile * TILE, TILE), TILE)
                terms[odd, :, part] = dot_cols(x, sum_weight[part, :])

            line.sum_start(piece, term_of(odd))

        def own_step(piece):
            total[...] = terms[1 - odd, pl.ds(pl.multiple_of(me * own, own), own), :]
            line.sum_end(piece, total)
            view(piece, me)[...] = row_step(piece, total, row_inputs, row_outputs)
            line.spread_start(piece)

        def far_shards(piece):
            for distance in range(3, count):
                line.spread_onward(piece, distance)

        late(5, use)
        late(3, lambda piece: line.spread_onward(piece, 2))
        late(1, lambda piece: line.sum_onward(piece, term_of(1 - odd), [1]))
        late(0, form)
        late(4, far_shards)
        late(2, lambda piece: line.spread_onward(piece, 1))
        late(0, lambda piece: line.sum_onward(piece, term_of(odd), range(count - 2, 1, -1)))
        late(1, own_step)
        if next_gather is not None:
            pl.when(step == 4)(next_gather.second)
            pl.when(step == 6)(next_gather.third)

    if swap is not None:

        @pl.loop(0, PIECES)
        def _(piece):
            if swap_out:
                swap.wait_arrival(piece)
            swap.wait_sent(piece)

    if next_gather is not None:
        next_gather.last()
        next_gather.wait_sent()
    line.sum_finish(PIECES)
    line.spread_finish(PIECES)


def relay(
    x, sum_weight, use_weight, row_inputs, row_step, row_shapes, use_inputs, use_step, use_shapes,
    collective_id, name, rows, swap_in=None, swap_out=None, next_shard=None,
):
    count = lax.axis_size("tp")
    width = sum_weight.shape[0]
    height = rows // PIECES
    own = height // count
    shared = use_weight is None
    operands = [x, sum_weight, *([] if shared else [use_weight]), *row_inputs, *use_inputs]
    in_specs = [pl.BlockSpec(memory_space=pltpu.VMEM)] * len(operands)
    shapes = [jax.ShapeDtypeStruct((rows, width), jnp.bfloat16), *row_shapes, *use_shapes]
    shapes += [shape for shape in (swap_in, swap_out) if shape is not None]
    out_specs = [pl.BlockSpec(memory_space=pltpu.VMEM)] * len(shapes)
    extra, last = [], []
    if next_shard is not None:
        operands.append(next_shard)
        in_specs.append(pl.BlockSpec(memory_space=pl.ANY))
        whole = (8 * next_shard.shape[0], next_shard.shape[1])
        shapes.append(jax.ShapeDtypeStruct(whole, next_shard.dtype))
        out_specs.append(pl.BlockSpec(memory_space=pl.ANY))
        extra = [pltpu.SemaphoreType.DMA((9,))] * 2
        last = [pltpu.SemaphoreType.DMA]
    sums, spreads = line_semaphores(count, PIECES)
    swaps = []
    if swap_out is not None:
        swaps.append(pltpu.VMEM((rows, swap_out.shape[1]), swap_out.dtype))
    if swap_in is not None or swap_out is not None:
        swaps += [pltpu.SemaphoreType.DMA((PIECES,))] * 2
    sizes = (
        len(row_inputs), len(use_inputs), len(row_shapes), len(use_shapes), shared,
        swap_in is not None, swap_out is not None, next_shard is not None,
    )
    return pl.pallas_call(
        functools.partial(relay_kernel, count, row_step, use_step, sizes),
        out_shape=shapes,
        in_specs=in_specs,
        out_specs=out_specs,
        scratch_shapes=[
            pltpu.VMEM((2, height, width), jnp.float32),
            pltpu.VMEM((own, width), jnp.float32),
            pltpu.VMEM((PIECES, count + 1, own, width), jnp.bfloat16),
            *sums,
            *spreads,
            *extra,
            *swaps,
            *last,
        ],
        compiler_params=pltpu.CompilerParams(
            collective_id=collective_id, has_side_effects=True, vmem_limit_bytes=60 << 20
        ),
        cost_estimate=pl.CostEstimate(
            flops=100_000_000_000, bytes_accessed=64 * rows * width, transcendentals=0
        ),
        name=name,
    )(*operands)


def own_rows_of(piece, like):
    own = like.shape[0] // PIECES
    return pl.ds(pl.multiple_of(piece * own, own), own)


def first_norm_step(piece, total, inputs, outputs):
    tokens, gains, biases = inputs
    first_norm, normed_one, inverse_one = outputs
    part = own_rows_of(piece, tokens)
    summed = tokens[part, :].astype(jnp.float32) + (total[...] + biases[0:1, :])
    normed, inverse = norm_parts(summed)
    result = normed * gains[0:1, :] + biases[1:2, :]
    first_norm[part, :] = result
    normed_one[part, :] = normed
    inverse_one[part, :] = jnp.broadcast_to(inverse, (inverse.shape[0], 128))
    return result.astype(jnp.bfloat16)


def expand_step(rows, chunk, weight, inputs, outputs):
    (bias,) = inputs
    hidden, activated = outputs

    @pl.loop(0, hidden.shape[1] // TILE)
    def _(tile):
        part = pl.ds(pl.multiple_of(tile * TILE, TILE), TILE)
        values = dot_plain(chunk, weight[:, part]) + bias[:, part]
        hidden[rows, part] = values
        activated[rows, part] = gelu_tanh(values).astype(jnp.bfloat16)


def add_sums(piece, sums, *values):
    @pl.when(piece == 0)
    def _():
        sums[...] = jnp.zeros_like(sums)

    for i, value in enumerate(values):
        sums[i : i + 1, :] += jnp.sum(value, axis=0, keepdims=True)


def second_norm_step(piece, total, inputs, outputs):
    first_norm, out_grad, gains, biases = inputs
    mixed, grad_second, sums = outputs
    part = own_rows_of(piece, first_norm)
    normed, inverse = norm_parts(first_norm[part, :] + total[...] + biases[2:3, :])
    result = (normed * gains[1:2, :] + biases[3:4, :]).astype(jnp.bfloat16)
    count, _, width = mixed.shape
    for i in range(count):
        mixed[i, part, :] = result[:, i * width : (i + 1) * width]
    upstream = jnp.concatenate([out_grad[i, part, :] for i in range(count)], axis=1)
    upstream = upstream.astype(jnp.float32)
    grad = norm_back(upstream, normed, inverse, gains[1:2, :])
    grad_second[part, :] = grad
    low = grad.astype(jnp.bfloat16)
    add_sums(piece, sums, upstream * normed, upstream, low.astype(jnp.float32))
    return low


def gelu_slope(values):
    scale = math.sqrt(2.0 / math.pi)
    square = values * values
    bend = jnp.tanh(scale * values * (1.0 + 0.044715 * square))
    inner = scale * (1.0 + 3 * 0.044715 * square)
    return 0.5 * (1.0 + bend) + 0.5 * values * (1.0 - bend * bend) * inner


def shrink_step(rows, chunk, weight, inputs, outputs):
    (hidden,) = inputs
    hidden_low, sums = outputs

    @pl.when(rows.start == 0)
    def _():
        sums[...] = jnp.zeros_like(sums)

    @pl.loop(0, hidden.shape[1] // TILE)
    def _(tile):
        part = pl.ds(pl.multiple_of(tile * TILE, TILE), TILE)
        grad = dot_plain(chunk, weight[:, part]) * gelu_slope(hidden[rows, part])
        low = grad.astype(jnp.bfloat16)
        hidden_low[rows, part] = low
        sums[0:1, part] += jnp.sum(low.astype(jnp.float32), axis=0, keepdims=True)


def first_back_step(piece, total, inputs, outputs):
    grad_second, normed_one, inverse_one, gains = inputs
    grad_inner, sums = outputs
    part = own_rows_of(piece, grad_second)
    normed = normed_one[part, :]
    grad_first = grad_second[part, :] + total[...]
    grad = norm_back(grad_first, normed, inverse_one[part, 0:1], gains[0:1, :])
    grad_inner[part, :] = grad
    low = grad.astype(jnp.bfloat16)
    add_sums(piece, sums, grad_first * normed, grad_first, low.astype(jnp.float32))
    return low


def attended_step(rows, chunk, weight, inputs, outputs):
    result = dot_plain(chunk, weight[...]).astype(jnp.bfloat16)
    if outputs:
        outputs[0][rows, :] = result
    return result


def peers_in_plane(sizes):
    fsdp, ctx = lax.axis_index("fsdp"), lax.axis_index("ctx")
    return [
        {"fsdp": lax.rem(fsdp + i, sizes[0]), "ctx": lax.rem(ctx + j, sizes[1])}
        for i in range(sizes[0])
        for j in range(sizes[1])
        if i or j
    ]


def input_kernel(
    sizes, x_ref, weight, inner_ref, rows_ref, hidden_ref, out_ref, vectors_ref,
    term_ref, total, slots, own_vectors, tp_slots, plane_slots,
    sum_sent, sum_got, tp_sent, tp_got, plane_sent, plane_got, hooks=None,
):
    count = sizes[2]
    me = lax.axis_index("tp")
    height = x_ref.shape[0] // PIECES
    own = height // count
    width = out_ref.shape[1]
    line = Line(me, count, slots, sum_sent, sum_got, None, None, None)
    tp_peers, plane_peers = peers_along_tp(me, count), peers_in_plane(sizes)
    greet_peers(tp_peers + plane_peers)

    def own_part(index):
        return rows_ref.at[:, pl.ds(pl.multiple_of(index * width, width), width)]

    over_tp = Exchange(
        tp_peers, tp_sent, tp_got,
        lambda i: own_part(lax.rem(me + i, count)), lambda i: tp_slots.at[i],
    )
    over_plane = Exchange(
        plane_peers, plane_sent, plane_got, lambda _: own_vectors, lambda i: plane_slots.at[i]
    )
    opening, before, after, closing = hooks or (lambda *_: None,) * 4
    opening()
    over_tp.start()

    def terms(piece):
        def term(owner):
            features = pl.ds(pl.multiple_of(owner * width, width), width)
            term_ref[...] = dot_cols(
                x_ref[pl.ds(pl.multiple_of(piece * height, height), height), :],
                weight[features, :],
            )
            inner = inner_ref[pl.ds(pl.multiple_of(piece * own, own), own), features]
            term_ref[pl.ds(pl.multiple_of(me * own, own), own), :] += inner
            return term_ref[...]

        return term

    def pack():
        over_tp.wait_arrivals()
        own_vectors[0:8, :] = own_part(me)[...]
        for i in range(count - 1):
            own_vectors[0:8, :] += tp_slots[i]
        own_vectors[8:, :] = jnp.zeros_like(own_vectors[8:, :])
        hidden_rows = hidden_ref.shape[1] // width
        for i in range(hidden_rows):
            own_vectors[8 + i : 9 + i, :] = hidden_ref[0:1, i * width : (i + 1) * width]
        for i in range(x_ref.shape[1] // width):
            part = x_ref[:, i * width : (i + 1) * width].astype(jnp.float32)
            place = 8 + hidden_rows + i
            own_vectors[place : place + 1, :] = jnp.sum(part, axis=0, keepdims=True)
        over_plane.start()

    @pl.loop(0, PIECES)
    def _(piece):
        before(piece)
        line.sum_start(piece, terms(piece))
        line.sum_onward(piece, terms(piece), range(count - 2, 0, -1))
        after(piece)

    pack()
    closing()

    @pl.loop(0, PIECES)
    def _(piece):
        total[...] = terms(piece)(me)
        line.sum_end(piece, total)
        rows = pl.ds(pl.multiple_of(piece * height, height), height)
        out_ref[rows, :] = total[...].astype(out_ref.dtype)

    over_plane.wait_arrivals()
    vectors_ref[...] = own_vectors[...]
    for i in range(len(plane_peers)):
        vectors_ref[...] += plane_slots[i]
    over_tp.wait_sent()
    over_plane.wait_sent()
    line.sum_finish(PIECES)


def input_sum(x, weight, inner, row_sums, hidden_sums, collective_id):
    sizes = tuple(lax.axis_size(axis) for axis in ("fsdp", "ctx", "tp"))
    count = sizes[2]
    others = sizes[0] * sizes[1] - 1
    rows = x.shape[0]
    width = weight.shape[0] // count
    height = rows // PIECES
    packed = 8 + -(-(hidden_sums.shape[1] + x.shape[1]) // (8 * width)) * 8
    return pl.pallas_call(
        functools.partial(input_kernel, sizes),
        out_shape=[
            jax.ShapeDtypeStruct((rows, width), jnp.bfloat16),
            jax.ShapeDtypeStruct((packed, width), jnp.float32),
        ],
        in_specs=[pl.BlockSpec(memory_space=pltpu.VMEM)] * 5,
        out_specs=[pl.BlockSpec(memory_space=pltpu.VMEM)] * 2,
        scratch_shapes=[
            pltpu.VMEM((height, width), jnp.float32),
            pltpu.VMEM((height, width), jnp.float32),
            pltpu.VMEM((PIECES, count + 1, height, width), jnp.bfloat16),
            pltpu.VMEM((packed, width), jnp.float32),
            pltpu.VMEM((count - 1, 8, width), jnp.float32),
            pltpu.VMEM((others, packed, width), jnp.float32),
            *line_semaphores(count, PIECES)[0],
            pltpu.SemaphoreType.DMA((count - 1,)),
            pltpu.SemaphoreType.DMA((count - 1,)),
            pltpu.SemaphoreType.DMA((others,)),
            pltpu.SemaphoreType.DMA((others,)),
        ],
        compiler_params=pltpu.CompilerParams(
            collective_id=collective_id, has_side_effects=True, vmem_limit_bytes=40 << 20
        ),
        cost_estimate=pl.CostEstimate(
            flops=60_000_000_000, bytes_accessed=64 * rows * width, transcendentals=0
        ),
        name="input_sum",
    )(x, weight, inner, row_sums, hidden_sums)


class PlaneSum:
    def __init__(self, parts, core_slots, first_slots, last_slots, sent, got):
        self.parts, self.core_slots = parts, core_slots
        self.first_slots, self.last_slots = first_slots, last_slots
        self.sent, self.got = sent, got
        self.fsdp, self.ctx = lax.axis_index("fsdp"), lax.axis_index("ctx")
        self.twin = self.fsdp + 1 - 2 * lax.rem(self.fsdp, 2)
        self.half = parts.shape[2] // 2

    def number(self, fsdp, over_x, over_y):
        chip = lax.rem(fsdp + 2 * over_x, 4)
        return chip * 2 + (1 - self.ctx if over_y else self.ctx)

    def view(self, over_x, over_y, side):
        columns = pl.ds(side * self.half, self.half)
        return self.parts.at[self.number(self.fsdp, over_x, over_y), :, columns]

    def copy(self, number, source, place, peer):
        return pltpu.make_async_remote_copy(
            src_ref=source,
            dst_ref=place,
            send_sem=self.sent.at[number],
            recv_sem=self.got.at[number],
            device_id=peer,
            device_id_type=MESH,
        )

    def core_copy(self, number):
        over_x, over_y = number // 2, number % 2
        source = self.parts.at[self.number(self.twin, over_x, over_y)]
        return self.copy(number, source, self.core_slots.at[number], {"fsdp": self.twin})

    def x_peer(self):
        return {"fsdp": lax.rem(self.fsdp + 2, 4)}

    def y_peer(self):
        return {"ctx": 1 - self.ctx}

    def first_copy(self, number):
        slot = self.first_slots.at[number]
        if number < 2:
            return self.copy(4 + number, self.view(1, number, 0), slot, self.x_peer())
        return self.copy(4 + number, self.view(number - 2, 1, 1), slot, self.y_peer())

    def last_copy(self, side):
        slot = self.last_slots.at[side]
        if side == 0:
            return self.copy(8, self.view(0, 1, 0), slot, self.y_peer())
        return self.copy(9, self.view(1, 0, 1), slot, self.x_peer())

    def add(self, view, slot):
        total = view[...].astype(jnp.float32) + slot[...].astype(jnp.float32)
        view[...] = total.astype(view.dtype)

    def start(self):
        for number in (3, 2, 1, 0):
            self.core_copy(number).start()

    def second(self):
        for number in (3, 2, 1, 0):
            self.core_copy(number).wait_recv()
            shard = self.parts.at[self.number(self.fsdp, number // 2, number % 2)]
            self.add(shard, self.core_slots.at[number])
            if number == 3:
                self.first_copy(1).start()
                self.first_copy(3).start()
            if number == 2:
                self.first_copy(0).start()
            if number == 1:
                self.first_copy(2).start()

    def third(self):
        self.first_copy(1).wait_recv()
        self.add(self.view(0, 1, 0), self.first_slots.at[1])
        self.last_copy(0).start()
        self.first_copy(3).wait_recv()
        self.add(self.view(1, 0, 1), self.first_slots.at[3])
        self.last_copy(1).start()

    def finish(self):
        totals = []
        for side in range(2):
            number = 2 * side
            self.first_copy(number).wait_recv()
            self.last_copy(side).wait_recv()
            total = self.view(0, 0, side)[...].astype(jnp.float32)
            total += self.first_slots[number].astype(jnp.float32)
            totals.append(total + self.last_slots[side].astype(jnp.float32))
        for number in range(4):
            self.core_copy(number).wait_send()
            self.first_copy(number).wait_send()
        for side in range(2):
            self.last_copy(side).wait_send()
        return totals

    @staticmethod
    def scratch(shards, height, width):
        return [
            pltpu.VMEM((shards, height, width), jnp.bfloat16),
            pltpu.VMEM((4, height, width), jnp.bfloat16),
            pltpu.VMEM((4, height, width // 2), jnp.bfloat16),
            pltpu.VMEM((2, height, width // 2), jnp.bfloat16),
            pltpu.SemaphoreType.DMA((10,)),
            pltpu.SemaphoreType.DMA((10,)),
        ]


def leave_kernel(
    sizes, grads_ref, tokens_ref, weight, inner_ref, rows_ref, hidden_ref,
    out_ref, vectors_ref, query_out, key_out, value_out,
    x_ref, term_ref, total, slots, own_vectors, tp_slots, plane_slots,
    sum_sent, sum_got, tp_sent, tp_got, plane_sent, plane_got, swap_sent, swap_got, *sum_scratch,
):
    count = sizes[2]
    me, ctx = lax.axis_index("tp"), lax.axis_index("ctx")
    rows = x_ref.shape[0]
    height = rows // PIECES
    part = grads_ref.shape[1]
    plane_sum = PlaneSum(*sum_scratch)
    shard = plane_sum.parts.shape[1]

    def piece_rows(piece, start=0):
        return pl.ds(pl.multiple_of(start + piece * height, height), height)

    own_columns = pl.ds(pl.multiple_of(ctx * part, part), part)
    swap = Swap(
        swap_sent, swap_got,
        lambda piece: grads_ref.at[piece_rows(piece, (1 - ctx) * rows)],
        lambda piece: x_ref.at[piece_rows(piece), own_columns],
    )

    def product(number):
        columns = pl.ds(pl.multiple_of(number * shard, shard), shard)
        result = dot_rows(tokens_ref[:, columns], x_ref[...])
        plane_sum.parts[number] = result.astype(jnp.bfloat16)

    def opening():
        @pl.loop(0, PIECES)
        def _(piece):
            swap.start(piece)

        x_ref[:, own_columns] = grads_ref[pl.ds(pl.multiple_of(ctx * rows, rows), rows), :]

    middle = PIECES // 2

    def before(piece):
        @pl.when(piece <= middle)
        def _():
            swap.wait_arrival(piece)

    def products(fsdp):
        for over_x in (1, 0):
            for over_y in (1, 0):
                product(plane_sum.number(fsdp, over_x, over_y))

    def after(piece):
        @pl.when(piece == middle)
        def _():
            for other in range(middle + 1, PIECES):
                swap.wait_arrival(other)
            products(plane_sum.twin)
            plane_sum.start()

        @pl.when(piece == middle + 1)
        def _():
            products(plane_sum.fsdp)

        pl.when(piece == middle + 2)(plane_sum.second)

    def closing():
        plane_sum.third()

    input_kernel(
        sizes, x_ref, weight, inner_ref, rows_ref, hidden_ref, out_ref, vectors_ref,
        term_ref, total, slots, own_vectors, tp_slots, plane_slots,
        sum_sent, sum_got, tp_sent, tp_got, plane_sent, plane_got,
        hooks=(opening, before, after, closing),
    )
    halves = plane_sum.finish()
    third = part // 3
    for side, half in enumerate(halves):
        for i, ref in enumerate((query_out, key_out, value_out)):
            ref[:, side * third : (side + 1) * third] = half[:, i * third : (i + 1) * third]

    @pl.loop(0, PIECES)
    def _(piece):
        swap.wait_sent(piece)


def leave(grads, tokens, weight, inner, row_sums, hidden_sums, collective_id):
    sizes = tuple(lax.axis_size(axis) for axis in ("fsdp", "ctx", "tp"))
    count = sizes[2]
    others = sizes[0] * sizes[1] - 1
    rows, features = tokens.shape
    part = grads.shape[1]
    width = features // count
    height = rows // PIECES
    shard = features // (others + 1)
    packed = 8 + -(-(hidden_sums.shape[1] + 2 * part) // (8 * width)) * 8
    return pl.pallas_call(
        functools.partial(leave_kernel, sizes),
        out_shape=[
            jax.ShapeDtypeStruct((rows, width), jnp.bfloat16),
            jax.ShapeDtypeStruct((packed, width), jnp.float32),
            *[jax.ShapeDtypeStruct((shard, 2 * part // 3), jnp.float32)] * 3,
        ],
        in_specs=[pl.BlockSpec(memory_space=pltpu.VMEM)] * 6,
        out_specs=[pl.BlockSpec(memory_space=pltpu.VMEM)] * 5,
        scratch_shapes=[
            pltpu.VMEM((rows, 2 * part), jnp.bfloat16),
            pltpu.VMEM((height, width), jnp.float32),
            pltpu.VMEM((height, width), jnp.float32),
            pltpu.VMEM((PIECES, count + 1, height, width), jnp.bfloat16),
            pltpu.VMEM((packed, width), jnp.float32),
            pltpu.VMEM((count - 1, 8, width), jnp.float32),
            pltpu.VMEM((others, packed, width), jnp.float32),
            *line_semaphores(count, PIECES)[0],
            pltpu.SemaphoreType.DMA((count - 1,)),
            pltpu.SemaphoreType.DMA((count - 1,)),
            pltpu.SemaphoreType.DMA((others,)),
            pltpu.SemaphoreType.DMA((others,)),
            pltpu.SemaphoreType.DMA((PIECES,)),
            pltpu.SemaphoreType.DMA((PIECES,)),
            *PlaneSum.scratch(others + 1, shard, 2 * part),
        ],
        compiler_params=pltpu.CompilerParams(
            collective_id=collective_id, has_side_effects=True, vmem_limit_bytes=56 << 20
        ),
        cost_estimate=pl.CostEstimate(
            flops=60_000_000_000, bytes_accessed=64 * rows * width, transcendentals=0
        ),
        name="leave",
    )(grads, tokens, weight, inner, row_sums, hidden_sums)


def to_own_rows(wide):
    count = lax.axis_size("tp")
    parts = wide.reshape(PIECES, count, -1, wide.shape[1])
    return lax.dynamic_index_in_dim(parts, lax.axis_index("tp"), 1, keepdims=False).reshape(
        -1, wide.shape[1]
    )


def spread_own(block):
    count = lax.axis_size("tp")
    rows, width = block.shape
    parts = block.reshape(PIECES, count, -1, width).transpose(1, 0, 2, 3)
    return lax.all_to_all(
        parts.reshape(count, -1, width), "tp", split_axis=0, concat_axis=0, tiled=True
    )


def unspread_own(parts):
    count, own_rows, width = parts.shape
    got = lax.all_to_all(parts, "tp", split_axis=0, concat_axis=0, tiled=True)
    return got.reshape(count, PIECES, -1, width).transpose(1, 0, 2, 3).reshape(-1, width)


def body(
    tokens,
    segments,
    query_weight,
    key_weight,
    value_weight,
    output_weight,
    expand_weight,
    shrink_weight,
    query_bias,
    value_bias,
    hidden_bias,
    norm_gains,
    row_biases,
    out_grad,
):
    rows = tokens.shape[0]
    head_cols = query_weight.shape[1]
    heads = head_cols // HD
    plane = ("fsdp", "ctx")
    plane_sizes = tuple(lax.axis_size(axis) for axis in plane)
    by_heads = plane_sizes == (4, 2) and heads % 2 == 0

    def weight_rows(weight):
        return lax.all_gather(weight, plane, axis=0, tiled=True)

    marks = jnp.concatenate(
        [norm_gains, row_biases, jnp.zeros((10, norm_gains.shape[1]), norm_gains.dtype)]
    )
    block_index = lax.axis_index("fsdp") * plane_sizes[1] + lax.axis_index("ctx")
    qkv_bias = jnp.stack([query_bias, jnp.zeros_like(query_bias), value_bias])
    qkv_bias = qkv_bias.astype(jnp.float32)
    if by_heads:
        half_bias = qkv_bias.reshape(3, 2, -1).transpose(1, 0, 2).reshape(1, -1)
        wide_tokens, wide_marks, wide_qkv, full_output, full_expand, qkv_heads = enter(
            tokens, marks, query_weight, key_weight, value_weight, output_weight, expand_weight,
            half_bias, 0,
        )
        queries = keys = values = qkv_heads
        own_heads = heads // 2
        stream_rows = plane_sizes[1] * rows
        stream_ids = lax.dynamic_slice_in_dim(
            segments, lax.axis_index("fsdp") * stream_rows, stream_rows, 0
        )
        bounds = document_bounds(stream_ids, 3 * lax.axis_index("fsdp"))
    else:
        wide_qkv = weight_rows(jnp.concatenate([query_weight, key_weight, value_weight], axis=1))
        wide_tokens, wide_marks = gather_features(tokens, marks, 0)
        qkv = dot_plain(wide_tokens, wide_qkv) + qkv_bias.reshape(1, -1)
        queries, keys, values = jnp.split(qkv.astype(jnp.bfloat16), 3, axis=1)
        own_heads = heads
        keys, values = padded(keys, WIN), padded(values, WIN)
        ids = jnp.concatenate(
            [
                jnp.full((WIN,), -1, jnp.int32),
                segments,
                jnp.full((WIN,), jnp.iinfo(jnp.int32).max, jnp.int32),
            ]
        )
        full_output, full_expand = weight_rows(output_weight), weight_rows(expand_weight)
        key_ids = lax.dynamic_slice_in_dim(ids, block_index * rows, rows + 2 * WIN, 0)
        bounds = key_bounds(key_ids[WIN : WIN + rows], key_ids, WIN)
    places = (0, own_heads, 2 * own_heads) if by_heads else (0, 0, 0)
    gains = wide_marks[:2].astype(jnp.float32)
    biases = wide_marks[2:6].astype(jnp.float32)
    wide_marks, out_grad = lax.optimization_barrier((wide_marks, out_grad))
    upstream = spread_own(out_grad)
    attended_heads, lse = attend(queries, keys, values, own_heads, *bounds, places)
    attended_heads, upstream = lax.optimization_barrier((attended_heads, upstream))

    own_tokens = to_own_rows(wide_tokens)
    own_rows, features = own_tokens.shape
    hidden_cols = expand_weight.shape[1]

    def shape(extent, kind=jnp.float32):
        return jax.ShapeDtypeStruct(extent, kind)

    own_shape = shape((own_rows, features))
    norm_low, first_norm, normed_one, inverse_one, hidden, activated, *more = relay(
        attended_heads, full_output, full_expand,
        [own_tokens, gains, biases], first_norm_step,
        [own_shape, own_shape, shape((own_rows, 128))],
        [hidden_bias.astype(jnp.float32)[None]], expand_step,
        [shape((rows, hidden_cols)), shape((rows, hidden_cols), jnp.bfloat16)],
        1, "first_norm", rows,
        swap_in=shape((rows, head_cols), jnp.bfloat16) if by_heads else None,
        next_shard=shrink_weight if by_heads else None,
    )
    if by_heads:
        attended, full_shrink = more
    else:
        attended, full_shrink = attended_heads, weight_rows(shrink_weight)
    ffn_low, mixed_own, grad_second, second_sums, hidden_low, hidden_sums = relay(
        activated, full_shrink, None,
        [first_norm, upstream, gains, biases], second_norm_step,
        [shape(upstream.shape, jnp.bfloat16), own_shape, shape((8, features))],
        [hidden], shrink_step,
        [shape((rows, hidden_cols), jnp.bfloat16), shape((8, hidden_cols))],
        2, "second_norm", rows,
    )

    def owner_sum(grad):
        return lax.psum_scatter(
            grad, plane, scatter_dimension=0, tiled=True
        )

    hidden_low, shrink_part, expand_part = lax.optimization_barrier(
        (
            hidden_low,
            dot_rows(ffn_low, activated).astype(jnp.bfloat16),
            dot_rows(norm_low, hidden_low).astype(jnp.bfloat16),
        )
    )
    shrink_grad = owner_sum(shrink_part)
    expand_grad = owner_sum(expand_part)
    branch_low, grad_inner, first_sums, attended_grad = relay(
        hidden_low, full_expand, full_output,
        [grad_second, normed_one, inverse_one, gains], first_back_step,
        [own_shape, shape((8, features))],
        [], attended_step,
        [] if by_heads else [shape((rows, head_cols), jnp.bfloat16)],
        3, "first_back", rows,
        swap_out=shape((2 * rows, head_cols // 2), jnp.bfloat16) if by_heads else None,
    )
    attended_grad, mixed_own, shrink_grad, output_part = lax.optimization_barrier(
        (
            attended_grad,
            mixed_own,
            shrink_grad,
            dot_rows(branch_low, attended).astype(jnp.bfloat16),
        )
    )
    output_grad = owner_sum(output_part)
    mixed = unspread_own(mixed_own)

    if by_heads:
        (grads,) = attend_back(
            queries, keys, values, attended_heads, attended_grad, lse, *bounds, places, True
        )
        grads, mixed, expand_grad, output_grad = lax.optimization_barrier(
            (grads, mixed, expand_grad, output_grad)
        )
    else:
        query_low, key_ext, value_ext = attend_back(
            queries, keys, values, attended_heads, attended_grad, lse, *bounds
        )

        def fold(ext):
            edges = jnp.concatenate([ext[:WIN], ext[WIN + rows :]], axis=0)
            around = padded(edges, WIN)
            own = ext[WIN : WIN + rows]
            own = own.at[:WIN].add(around[:WIN]).at[rows - WIN :].add(around[3 * WIN :])
            return own.astype(jnp.bfloat16)

        qkv_low = jnp.concatenate([query_low, fold(key_ext), fold(value_ext)], axis=1)
    row_sums = jnp.concatenate(
        [
            first_sums[0:1], second_sums[0:1],
            first_sums[2:3], first_sums[1:2], second_sums[2:3], second_sums[1:2],
            jnp.zeros_like(first_sums[:2]),
        ]
    )
    sides = 2 if by_heads else 1

    def by_kind(columns):
        parts = columns.reshape(-1, sides, 3, head_cols // sides)
        return [parts[:, :, i].reshape(-1, head_cols) for i in range(3)]

    if by_heads:
        input_grad, vectors, query_grad, key_grad, value_grad = leave(
            grads, wide_tokens, wide_qkv, grad_inner, row_sums, hidden_sums[:1], 4
        )
    else:
        input_grad, vectors = input_sum(
            qkv_low, wide_qkv, grad_inner, row_sums, hidden_sums[:1], 4
        )
        qkv_grad = owner_sum(dot_rows(wide_tokens, qkv_low).astype(jnp.bfloat16))
        query_grad, key_grad, value_grad = by_kind(qkv_grad.astype(jnp.float32))
    hidden_rows = hidden_cols // head_cols
    query_sum, _, value_sum = by_kind(
        vectors[8 + hidden_rows : 8 + hidden_rows + 3].reshape(1, -1)
    )
    return (
        mixed,
        input_grad,
        query_grad,
        key_grad,
        value_grad,
        output_grad.astype(jnp.float32),
        expand_grad.astype(jnp.float32),
        shrink_grad.astype(jnp.float32),
        query_sum[0],
        value_sum[0],
        vectors[8 : 8 + hidden_rows].reshape(-1),
        vectors[:2],
        vectors[2:6],
    )


def solution(mesh):
    rows, whole, cols = P(("fsdp", "ctx"), "tp"), P(), P("tp")
    wide = P(None, "tp")
    return jax.shard_map(
        body,
        mesh=mesh,
        in_specs=(rows, whole) + (rows,) * 6 + (cols,) * 3 + (wide,) * 2 + (rows,),
        out_specs=(rows,) * 8 + (cols,) * 3 + (wide,) * 2,
        check_vma=False,
    )
```

```python
import functools
import math

import jax
import jax.numpy as jnp
from jax import lax
from jax.experimental import pallas as pl
from jax.experimental.pallas import tpu as pltpu
from jax.sharding import PartitionSpec as P

HD = 128
WIN = 1024
QB = 512
KB = 512

epsilon = 1e-06
hidden_floor = -1e30
score_scale = 1.0 / math.sqrt(HD)
log2_e = 1.0 / math.log(2.0)


def dot_plain(left, right):
    return jnp.dot(left, right, preferred_element_type=jnp.float32)


def dot_rows(left, right):
    return lax.dot_general(
        left, right, (((0,), (0,)), ((), ())), preferred_element_type=jnp.float32
    )


def dot_cols(left, right):
    return lax.dot_general(
        left, right, (((1,), (1,)), ((), ())), preferred_element_type=jnp.float32
    )


def block_bounds(block, rows, bounds, marks):
    if len(bounds) == 4:
        first, last, low, high = bounds
        return first[block], last[block], low[...], high[...]
    (ids,) = bounds
    run = ids.shape[1]

    @pl.when((pl.program_id(0) == 0) & (block == 0))
    def _():
        own = lax.axis_index("fsdp")
        own_ids = ids[pl.ds(own, 1), :]
        for i in range(2):
            marks[i] = jnp.sum((own_ids <= 3 * own + i).astype(jnp.int32))

    second, third = marks[0], marks[1]

    def bounds_at(places):
        start = jnp.where(places < second, 0, jnp.where(places < third, second, third))
        stop = jnp.where(places < second, second, jnp.where(places < third, third, run))
        return jnp.maximum(start, places - WIN), jnp.minimum(stop - 1, places + WIN)

    begin = block * rows
    low, high = bounds_at(begin + lax.broadcasted_iota(jnp.int32, (1, rows), 1))
    return bounds_at(begin)[0] // KB, bounds_at(begin + rows - 1)[1] // KB + 1, low, high


def bound_operands(bounds):
    if len(bounds) == 4:
        mark_spec = pl.BlockSpec((1, QB), lambda h, i, *_: (0, i))
        return list(bounds[:2]), list(bounds[2:]), [mark_spec, mark_spec]
    shape = bounds[0].shape
    return [], list(bounds), [pl.BlockSpec(shape, lambda h, i, *_: (0, 0))]


def attend_kernel(scalars, *refs):
    bounds = refs[:scalars]
    q_ref, k_ref, v_ref, *arrays, out_ref, lse_ref, vt, marks = refs[scalars:]
    block = pl.program_id(1)
    rows = q_ref.shape[0]

    @pl.when(block == 0)
    def _():
        vt[...] = v_ref[...].T

    queries = q_ref[...]
    first, last, low, high = block_bounds(block, rows, (*bounds, *arrays), marks)
    places = lax.broadcasted_iota(jnp.int32, (KB, rows), 0)

    def step(number, carry):
        top, total, mixed = carry
        start = pl.multiple_of(number * KB, KB)
        scores = dot_cols(k_ref[pl.ds(start, KB), :], queries) * (score_scale * log2_e)
        keep = (places >= low - start) & (places <= high - start)
        scores = jnp.where(keep, scores, hidden_floor)
        new_top = jnp.maximum(top, jnp.max(scores, axis=0, keepdims=True))
        shrink = jnp.exp2(top - new_top)
        powers = jnp.exp2(scores - new_top)
        total = total * shrink + jnp.sum(powers, axis=0, keepdims=True)
        mixed = mixed * shrink + dot_plain(vt[:, pl.ds(start, KB)], powers.astype(jnp.bfloat16))
        return new_top, total, mixed

    top, total, mixed = lax.fori_loop(
        first,
        last,
        step,
        (
            jnp.full((1, rows), hidden_floor, jnp.float32),
            jnp.zeros((1, rows), jnp.float32),
            jnp.zeros((HD, rows), jnp.float32),
        ),
    )
    out_ref[...] = (mixed / total).T.astype(out_ref.dtype)
    lse_ref[...] = (top + jnp.log2(total))[None]


def attend(queries, keys, values, heads, bounds, places=(0, 0, 0)):
    rows, span = queries.shape[0], keys.shape[0]
    width = heads * HD
    q_at, k_at, v_at = places
    scalars, arrays, specs = bound_operands(bounds)
    return pl.pallas_call(
        functools.partial(attend_kernel, len(scalars)),
        out_shape=(
            jax.ShapeDtypeStruct((rows, width), jnp.bfloat16),
            jax.ShapeDtypeStruct((heads, 1, rows), jnp.float32),
        ),
        grid_spec=pltpu.PrefetchScalarGridSpec(
            num_scalar_prefetch=len(scalars),
            grid=(heads, rows // QB),
            in_specs=[
                pl.BlockSpec((QB, HD), lambda h, i, *_: (i, h + q_at)),
                pl.BlockSpec((span, HD), lambda h, i, *_: (0, h + k_at)),
                pl.BlockSpec((span, HD), lambda h, i, *_: (0, h + v_at)),
                *specs,
            ],
            out_specs=[
                pl.BlockSpec((QB, HD), lambda h, i, *_: (i, h)),
                pl.BlockSpec((1, 1, QB), lambda h, i, *_: (h, 0, i)),
            ],
            scratch_shapes=[pltpu.VMEM((HD, span), jnp.bfloat16), pltpu.SMEM((2,), jnp.int32)],
        ),
        compiler_params=pltpu.CompilerParams(vmem_limit_bytes=32 << 20),
        cost_estimate=pl.CostEstimate(
            flops=3 * rows * span * width,
            bytes_accessed=2 * (2 * rows + 2 * span) * width,
            transcendentals=rows * span * heads,
        ),
        name="attend",
    )(*scalars, queries, keys, values, *arrays)


def attend_back_kernel(scalars, arrays, *refs):
    bounds = refs[:scalars]
    q_ref, k_ref, v_ref, o_ref, g_ref, lse_ref, *refs = refs[scalars:]
    bounds = (*bounds, *refs[:arrays])
    *results, kt, dk_sum, dv_sum, marks = refs[arrays:]
    head, block = pl.program_id(0), pl.program_id(1)
    rows = q_ref.shape[0]

    @pl.when(block == 0)
    def _():
        kt[...] = k_ref[...].T
        dk_sum[...] = jnp.zeros_like(dk_sum)
        dv_sum[...] = jnp.zeros_like(dv_sum)

    queries = q_ref[...]
    upstream = g_ref[...]
    lse = lse_ref[0]
    first, last, low, high = block_bounds(block, rows, bounds, marks)
    places = lax.broadcasted_iota(jnp.int32, (KB, rows), 0)
    product = upstream.astype(jnp.float32) * o_ref[...].astype(jnp.float32)
    delta = jnp.sum(product.T, axis=0, keepdims=True)

    def step(number, dq):
        start = pl.multiple_of(number * KB, KB)
        window = pl.ds(start, KB)
        scores = dot_cols(k_ref[window, :], queries) * (score_scale * log2_e)
        keep = (places >= low - start) & (places <= high - start)
        probs = jnp.exp2(jnp.where(keep, scores - lse, hidden_floor))
        prob_grad = dot_cols(v_ref[window, :], upstream)
        score_grad = (probs * (prob_grad - delta)).astype(jnp.bfloat16)
        dv_sum[window, :] += dot_plain(probs.astype(jnp.bfloat16), upstream)
        dk_sum[window, :] += dot_plain(score_grad, queries)
        return dq + dot_plain(kt[:, window], score_grad)

    dq = lax.fori_loop(first, last, step, jnp.zeros((HD, rows), jnp.float32))
    dq = (dq * score_scale).T
    if len(results) == 1:
        width = results[0].shape[1] // 3

        def place(part):
            start = pl.multiple_of(part * width + head * HD, HD)
            return results[0].at[:, pl.ds(start, HD)]

        query_place = place(0).at[pl.ds(pl.multiple_of(block * rows, rows), rows)]
        key_place, value_place = place(1), place(2)
    else:
        query_place, key_place, value_place = results
    query_place[...] = dq.astype(query_place.dtype)

    @pl.when(block == pl.num_programs(1) - 1)
    def _():
        key_place[...] = (dk_sum[...] * score_scale).astype(key_place.dtype)
        value_place[...] = dv_sum[...].astype(value_place.dtype)


def attend_back(
    queries, keys, values, out, upstream, lse, bounds, places=(0, 0, 0), merged=False
):
    rows, width = out.shape
    span = keys.shape[0]
    heads = width // HD
    q_at, k_at, v_at = places
    row_spec = pl.BlockSpec((QB, HD), lambda h, i, *_: (i, h))
    key_spec = pl.BlockSpec((span, HD), lambda h, i, *_: (0, h))
    scalars, arrays, specs = bound_operands(bounds)
    return pl.pallas_call(
        functools.partial(attend_back_kernel, len(scalars), len(arrays)),
        out_shape=[jax.ShapeDtypeStruct((rows, 3 * width), jnp.bfloat16)]
        if merged
        else [
            jax.ShapeDtypeStruct((rows, width), jnp.bfloat16),
            jax.ShapeDtypeStruct((span, width), jnp.float32),
            jax.ShapeDtypeStruct((span, width), jnp.float32),
        ],
        grid_spec=pltpu.PrefetchScalarGridSpec(
            num_scalar_prefetch=len(scalars),
            grid=(heads, rows // QB),
            in_specs=[
                pl.BlockSpec((QB, HD), lambda h, i, *_: (i, h + q_at)),
                pl.BlockSpec((span, HD), lambda h, i, *_: (0, h + k_at)),
                pl.BlockSpec((span, HD), lambda h, i, *_: (0, h + v_at)),
                row_spec, row_spec,
                pl.BlockSpec((1, 1, QB), lambda h, i, *_: (h, 0, i)),
                *specs,
            ],
            out_specs=[pl.BlockSpec((rows, 3 * width), lambda h, i, *_: (0, 0))]
            if merged
            else [row_spec, key_spec, key_spec],
            scratch_shapes=[
                pltpu.VMEM((HD, span), jnp.bfloat16),
                pltpu.VMEM((span, HD), jnp.float32),
                pltpu.VMEM((span, HD), jnp.float32),
                pltpu.SMEM((2,), jnp.int32),
            ],
        ),
        compiler_params=pltpu.CompilerParams(vmem_limit_bytes=32 << 20),
        cost_estimate=pl.CostEstimate(
            flops=8 * rows * span * width,
            bytes_accessed=2 * (4 * rows + 4 * span) * width,
            transcendentals=rows * span * heads,
        ),
        name="attend_back",
    )(*scalars, queries, keys, values, out, upstream, lse, *arrays)


def key_bounds(query_ids, key_ids, offset):
    rows, span = query_ids.shape[0], key_ids.shape[0]
    start = jnp.sum(key_ids[:, None] < query_ids[None, :], axis=0, dtype=jnp.int32)
    stop = jnp.sum(key_ids[:, None] <= query_ids[None, :], axis=0, dtype=jnp.int32)
    places = jnp.arange(rows, dtype=jnp.int32) + offset
    low = jnp.maximum(start, places - WIN)
    high = jnp.minimum(stop - 1, places + WIN)
    first = jnp.min(low.reshape(-1, QB), axis=1) // KB
    last = jnp.max(high.reshape(-1, QB), axis=1) // KB + 1
    return first, last, low[None], high[None]


def padded(block, width):
    count = lax.axis_size("ctx")
    forward = [(i, i + 1) for i in range(count - 1)]
    backward = [(target, source) for source, target in forward]
    below = lax.ppermute(block[block.shape[0] - width :], "ctx", forward)
    above = lax.ppermute(block[:width], "ctx", backward)
    return jnp.concatenate([below, block, above], axis=0)


def norm_parts(rows):
    mean = jnp.mean(rows, axis=-1, keepdims=True)
    square = jnp.mean(rows * rows, axis=-1, keepdims=True)
    inverse = lax.rsqrt(square - mean * mean + epsilon)
    return (rows - mean) * inverse, inverse


def norm_back(upstream, normed, inverse, gain):
    scaled = upstream * gain
    first_mean = jnp.mean(scaled, axis=-1, keepdims=True)
    second_mean = jnp.mean(scaled * normed, axis=-1, keepdims=True)
    return inverse * (scaled - first_mean - normed * second_mean)


def gelu_tanh(values):
    return jax.nn.gelu(values, approximate=True)


MESH = pl.DeviceIdType.MESH
PIECES = 8
TILE = 512


def greet(me, count, others=()):
    barrier = pltpu.get_barrier_semaphore()

    @pl.when(me > 0)
    def _():
        pl.semaphore_signal(barrier, inc=1, device_id={"tp": me - 1}, device_id_type=MESH)

    @pl.when(me < count - 1)
    def _():
        pl.semaphore_signal(barrier, inc=1, device_id={"tp": me + 1}, device_id_type=MESH)

    for other in others:
        pl.semaphore_signal(barrier, inc=1, device_id=other, device_id_type=MESH)

    @pl.when((me == 0) | (me == count - 1))
    def _():
        pl.semaphore_wait(barrier, 1 + len(others))

    @pl.when((me > 0) & (me < count - 1))
    def _():
        pl.semaphore_wait(barrier, 2 + len(others))


def peers_along_tp(me, count):
    return [{"tp": lax.rem(me + i, count)} for i in range(1, count)]


def greet_peers(peers):
    barrier = pltpu.get_barrier_semaphore()
    for peer in peers:
        pl.semaphore_signal(barrier, inc=1, device_id=peer, device_id_type=MESH)
    pl.semaphore_wait(barrier, len(peers))


class Exchange:
    def __init__(self, peers, sent, got, source, place):
        self.peers, self.sent, self.got = peers, sent, got
        self.source, self.place = source, place

    def copies(self):
        for i, peer in enumerate(self.peers):
            yield pltpu.make_async_remote_copy(
                src_ref=self.source(i + 1),
                dst_ref=self.place(i),
                send_sem=self.sent.at[i],
                recv_sem=self.got.at[i],
                device_id=peer,
                device_id_type=MESH,
            )

    def start(self):
        for copy in self.copies():
            copy.start()

    def wait_arrivals(self):
        for copy in self.copies():
            copy.wait_recv()

    def wait_sent(self):
        for copy in self.copies():
            copy.wait_send()


def at_distance(me, count, distance, action):
    for index in (me - distance, me + distance):

        @pl.when((index >= 0) & (index < count))
        def _(index=index):
            action(index)


class Line:
    def __init__(self, me, count, sum_slots, sum_sent, sum_got, spread_view, spread_sent, spread_got):
        self.me, self.count = me, count
        self.sum_slots, self.sum_sent, self.sum_got = sum_slots, sum_sent, sum_got
        self.spread_view, self.spread_sent, self.spread_got = spread_view, spread_sent, spread_got

    def sum_copy(self, piece, owner):
        onward = jnp.where(owner > self.me, self.me + 1, self.me - 1)
        place = jnp.where((owner < self.me) & (owner == self.me - 1), self.count, owner)
        return pltpu.make_async_remote_copy(
            src_ref=self.sum_slots.at[piece, owner],
            dst_ref=self.sum_slots.at[piece, place],
            send_sem=self.sum_sent.at[piece, owner],
            recv_sem=self.sum_got.at[piece, place],
            device_id={"tp": onward},
            device_id_type=MESH,
        )

    def sum_arrival(self, piece, place):
        pltpu.make_async_copy(
            self.sum_slots.at[piece, place],
            self.sum_slots.at[piece, place],
            self.sum_got.at[piece, place],
        ).wait()

    def sum_start(self, piece, term):
        me, count = self.me, self.count

        @pl.when((me == 0) | (me == count - 1))
        def _():
            for k in range(count - 1):
                owner = jnp.where(me == 0, count - 1 - k, k)
                self.sum_slots[piece, owner] = term(owner).astype(jnp.bfloat16)
                self.sum_copy(piece, owner).start()

    def sum_onward(self, piece, term, distances):
        me, count = self.me, self.count

        @pl.when((me > 0) & (me < count - 1))
        def _():
            for distance in distances:

                def pass_on(owner):
                    self.sum_arrival(piece, owner)
                    total = self.sum_slots[piece, owner].astype(jnp.float32) + term(owner)
                    self.sum_slots[piece, owner] = total.astype(jnp.bfloat16)
                    self.sum_copy(piece, owner).start()

                at_distance(me, count, distance, pass_on)

    def sum_end(self, piece, total):
        me, count = self.me, self.count

        @pl.when(me > 0)
        def _():
            self.sum_arrival(piece, me)
            total[...] += self.sum_slots[piece, me].astype(jnp.float32)

        @pl.when(me < count - 1)
        def _():
            self.sum_arrival(piece, count)
            total[...] += self.sum_slots[piece, count].astype(jnp.float32)

    def sum_finish(self, pieces):
        @pl.loop(0, pieces)
        def _(piece):
            for distance in range(1, self.count):
                at_distance(
                    self.me, self.count, distance,
                    lambda owner: self.sum_copy(piece, owner).wait_send(),
                )

    def spread_copy(self, piece, owner, to, sent, source=None):
        return pltpu.make_async_remote_copy(
            src_ref=self.spread_view(piece, owner) if source is None else source,
            dst_ref=self.spread_view(piece, owner),
            send_sem=self.spread_sent.at[piece, sent],
            recv_sem=self.spread_got.at[piece, owner],
            device_id={"tp": to},
            device_id_type=MESH,
        )

    def own_copies(self, piece, action, source=None):
        me, count = self.me, self.count

        @pl.when(me > 0)
        def _():
            action(self.spread_copy(piece, me, me - 1, count, source))

        @pl.when(me < count - 1)
        def _():
            action(self.spread_copy(piece, me, me + 1, me, source))

    def spread_start(self, piece, source=None):
        self.own_copies(piece, lambda copy: copy.start(), source)

    def onward_copy(self, piece, owner, action):
        me, count = self.me, self.count

        @pl.when((owner < me) & (me < count - 1))
        def _():
            action(self.spread_copy(piece, owner, me + 1, owner))

        @pl.when((owner > me) & (me > 0))
        def _():
            action(self.spread_copy(piece, owner, me - 1, owner))

    def spread_onward(self, piece, distance):
        def pass_on(owner):
            view = self.spread_view(piece, owner)
            pltpu.make_async_copy(view, view, self.spread_got.at[piece, owner]).wait()
            self.onward_copy(piece, owner, lambda copy: copy.start())

        at_distance(self.me, self.count, distance, pass_on)

    def spread_finish(self, pieces, source=None):
        @pl.loop(0, pieces)
        def _(piece):
            self.own_copies(
                piece, lambda copy: copy.wait_send(), None if source is None else source(piece)
            )
            for distance in range(1, self.count):
                at_distance(
                    self.me, self.count, distance,
                    lambda owner: self.onward_copy(piece, owner, lambda copy: copy.wait_send()),
                )


def line_semaphores(count, pieces):
    return [
        pltpu.SemaphoreType.DMA((pieces, count)),
        pltpu.SemaphoreType.DMA((pieces, count + 1)),
    ], [
        pltpu.SemaphoreType.DMA((pieces, count + 1)),
        pltpu.SemaphoreType.DMA((pieces, count)),
    ]


def gather_kernel(
    count, x_ref, marks_ref, out_ref, marks_out, slots, sent, got, marks_sent, marks_got
):
    me = lax.axis_index("tp")
    height = x_ref.shape[0] // PIECES
    width = x_ref.shape[1]

    def view(piece, owner):
        return out_ref.at[
            pl.ds(pl.multiple_of(piece * height, height), height),
            pl.ds(pl.multiple_of(owner * width, width), width),
        ]

    def source(piece):
        return x_ref.at[pl.ds(pl.multiple_of(piece * height, height), height)]

    line = Line(me, count, None, None, None, view, sent, got)
    peers = peers_along_tp(me, count)
    greet_peers(peers)

    @pl.loop(0, PIECES)
    def _(piece):
        line.spread_start(piece, source(piece))

    marks = Exchange(
        peers, marks_sent, marks_got, lambda _: marks_ref, lambda i: slots.at[i]
    )
    marks.start()
    own = pl.ds(pl.multiple_of(me * width, width), width)
    out_ref[:, own] = x_ref[...]
    marks_out[:, own] = marks_ref[...]
    for distance in range(1, count):

        @pl.loop(0, PIECES)
        def _(piece, distance=distance):
            line.spread_onward(piece, distance)

    marks.wait_arrivals()
    for i in range(1, count):
        owner = lax.rem(me - i + count, count)
        marks_out[:, pl.ds(pl.multiple_of(owner * width, width), width)] = slots[i - 1]
    marks.wait_sent()
    line.spread_finish(PIECES, source)


def gather_features(x, marks, collective_id):
    count = lax.axis_size("tp")
    rows, width = x.shape
    return pl.pallas_call(
        functools.partial(gather_kernel, count),
        out_shape=[
            jax.ShapeDtypeStruct((rows, count * width), x.dtype),
            jax.ShapeDtypeStruct((marks.shape[0], count * width), marks.dtype),
        ],
        in_specs=[pl.BlockSpec(memory_space=pltpu.VMEM)] * 2,
        out_specs=[pl.BlockSpec(memory_space=pltpu.VMEM)] * 2,
        scratch_shapes=[
            pltpu.VMEM((count - 1, *marks.shape), marks.dtype),
            *line_semaphores(count, PIECES)[1],
            pltpu.SemaphoreType.DMA((count - 1,)),
            pltpu.SemaphoreType.DMA((count - 1,)),
        ],
        compiler_params=pltpu.CompilerParams(
            collective_id=collective_id, has_side_effects=True, vmem_limit_bytes=16 << 20
        ),
        cost_estimate=pl.CostEstimate(
            flops=0, bytes_accessed=64 * rows * count * width, transcendentals=0
        ),
        name="gather_features",
    )(x, marks)


class Swap:
    def __init__(self, sent, got, source, place):
        self.sent, self.got, self.source, self.place = sent, got, source, place

    def copy(self, piece):
        return pltpu.make_async_remote_copy(
            src_ref=self.source(piece),
            dst_ref=self.place(piece),
            send_sem=self.sent.at[piece],
            recv_sem=self.got.at[piece],
            device_id={"ctx": 1 - lax.axis_index("ctx")},
            device_id_type=MESH,
        )

    def start(self, piece):
        self.copy(piece).start()

    def wait_arrival(self, piece):
        self.copy(piece).wait_recv()

    def wait_sent(self, piece):
        self.copy(piece).wait_send()


class PlaneGather:
    def __init__(self, whole, sent, got):
        self.whole, self.sent, self.got = whole, sent, got
        fsdp, self.ctx = lax.axis_index("fsdp"), lax.axis_index("ctx")
        self.fsdp = fsdp
        self.twin = fsdp + 1 - 2 * lax.rem(fsdp, 2)
        self.along_x = lax.rem(fsdp + 2, 4)
        self.twin_x = lax.rem(self.twin + 2, 4)
        self.core_peer = {"fsdp": self.twin}
        self.x_peer = {"fsdp": self.along_x}
        self.y_peer = {"ctx": 1 - self.ctx}

    def peers(self):
        return [self.core_peer, self.x_peer, self.y_peer]

    def shard(self, fsdp, ctx, half=None):
        height = self.whole.shape[0] // 8
        start = (fsdp * 2 + ctx) * height
        if half is not None:
            height //= 2
            start += half * height
        return self.whole.at[pl.ds(pl.multiple_of(start, height), height)]

    def copy(self, number, view, peer):
        return pltpu.make_async_remote_copy(
            src_ref=view,
            dst_ref=view,
            send_sem=self.sent.at[number],
            recv_sem=self.got.at[number],
            device_id=peer,
            device_id_type=MESH,
        )

    def copies(self):
        own = self.shard(self.fsdp, self.ctx)
        from_x = self.shard(self.along_x, self.ctx)
        from_y = self.shard(self.fsdp, 1 - self.ctx)
        return [
            (own, self.core_peer),
            (own, self.x_peer),
            (own, self.y_peer),
            (from_x, self.core_peer),
            (self.shard(self.along_x, self.ctx, 0), self.y_peer),
            (from_y, self.core_peer),
            (self.shard(self.fsdp, 1 - self.ctx, 1), self.x_peer),
            (self.shard(self.along_x, 1 - self.ctx, 0), self.core_peer),
            (self.shard(self.along_x, 1 - self.ctx, 1), self.core_peer),
        ]

    def arrivals(self):
        return [
            self.shard(self.twin, self.ctx),
            self.shard(self.along_x, self.ctx),
            self.shard(self.fsdp, 1 - self.ctx),
            self.shard(self.twin_x, self.ctx),
            self.shard(self.along_x, 1 - self.ctx, 0),
            self.shard(self.twin, 1 - self.ctx),
            self.shard(self.along_x, 1 - self.ctx, 1),
            self.shard(self.twin_x, 1 - self.ctx, 0),
            self.shard(self.twin_x, 1 - self.ctx, 1),
        ]

    def start(self, *numbers):
        copies = self.copies()
        for number in numbers:
            self.copy(number, *copies[number]).start()

    def wait(self, *numbers):
        arrivals = self.arrivals()
        for number in numbers:
            view = arrivals[number]
            pltpu.make_async_copy(view, view, self.got.at[number]).wait()

    def put(self, shard, done):
        copy = pltpu.make_async_copy(shard, self.shard(self.fsdp, self.ctx), done)
        copy.start()
        copy.wait()

    def first(self):
        self.start(1, 2, 0)

    def second(self):
        self.wait(1)
        self.start(4, 3)
        self.wait(2)
        self.start(6, 5)

    def third(self):
        self.wait(4)
        self.start(7)
        self.wait(6)
        self.start(8)

    def last(self):
        self.wait(0, 3, 5, 7, 8)

    def wait_sent(self):
        for number, (view, peer) in enumerate(self.copies()):
            self.copy(number, view, peer).wait_send()


def enter_kernel(
    count, x_ref, marks_ref, query_ref, key_ref, value_ref, output_ref, bias,
    wide, own_tokens, marks_out, weight, output_weight, heads,
    mark_slots, stage, sent, got, marks_sent, marks_got,
    weight_sent, weight_got, output_sent, output_got, swap_sent, swap_got, put_done,
):
    me, ctx = lax.axis_index("tp"), lax.axis_index("ctx")
    rows, width = x_ref.shape
    height = rows // PIECES
    half = query_ref.shape[1] // 2
    part = 3 * half

    def piece_rows(piece, start=0):
        return pl.ds(pl.multiple_of(start + piece * height, height), height)

    def view(piece, owner):
        return wide.at[piece_rows(piece), pl.ds(pl.multiple_of(owner * width, width), width)]

    gather = PlaneGather(weight, weight_sent, weight_got)
    output_gather = PlaneGather(output_weight, output_sent, output_got)
    own_shard = gather.shard(gather.fsdp, ctx)
    own = pl.ds(pl.multiple_of(me * width, width), width)
    puts = [
        (ref.at[:, pl.ds(side * half, half)], own_shard.at[:, pl.ds(side * part + i * half, half)])
        for side in range(2)
        for i, ref in enumerate((query_ref, key_ref, value_ref))
    ]
    puts += [
        (output_ref, output_gather.shard(gather.fsdp, ctx)),
        (x_ref, wide.at[:, own]),
    ]
    puts = [
        pltpu.make_async_copy(source, place, put_done.at[i])
        for i, (source, place) in enumerate(puts)
    ]
    for put in puts:
        put.start()
    line = Line(me, count, None, None, None, view, sent, got)
    tp_peers = peers_along_tp(me, count)
    greet_peers(tp_peers + gather.peers())

    def source(piece):
        return x_ref.at[piece_rows(piece)]

    for piece in range(2):
        line.spread_start(piece, source(piece))
    for put in puts[:7]:
        put.wait()
    gather.first()
    output_gather.first()
    marks = Exchange(
        tp_peers, marks_sent, marks_got, lambda _: marks_ref, lambda i: mark_slots.at[i]
    )
    marks.start()
    marks_out[:, own] = marks_ref[...]
    for put in puts[7:]:
        put.wait()
    swap = Swap(
        swap_sent, swap_got,
        lambda piece: stage.at[piece_rows(piece)],
        lambda piece: heads.at[piece_rows(piece, ctx * rows)],
    )

    def products(piece, side, place):
        x = wide[piece_rows(piece), :]

        @pl.loop(0, 3)
        def _(tile):
            start = pl.multiple_of(side * part + tile * half, half)
            columns = pl.ds(start, half)
            values = dot_plain(x, weight[:, columns]) + bias[:, columns]
            place[:, pl.ds(pl.multiple_of(tile * half, half), half)] = values.astype(jnp.bfloat16)

    @pl.loop(0, PIECES + 7)
    def _(step):
        def late(pieces, action, least=0):
            @pl.when((step >= pieces + least) & (step < PIECES + pieces))
            def _():
                action(step - pieces)

        def use(piece):
            products(piece, 1 - ctx, stage.at[piece_rows(piece)])
            swap.start(piece)
            products(piece, ctx, heads.at[piece_rows(piece, ctx * rows)])

        @pl.when(step == 7)
        def _():
            gather.third()
            gather.last()

        late(0, lambda piece: line.spread_start(piece, source(piece)), 2)
        late(7, use)
        late(5, lambda piece: line.spread_onward(piece, 2))
        late(3, lambda piece: line.spread_onward(piece, 1))
        late(6, lambda piece: [line.spread_onward(piece, i) for i in range(3, count)])
        pl.when(step == 5)(gather.second)
        pl.when(step == 7)(output_gather.second)
        pl.when(step == 9)(output_gather.third)

    own_height = height // count
    for piece in range(PIECES):
        start = pl.multiple_of(piece * height + me * own_height, own_height)
        own_tokens[piece * own_height : (piece + 1) * own_height, :] = wide[
            pl.ds(start, own_height), :
        ]

    marks.wait_arrivals()
    for i in range(1, count):
        owner = lax.rem(me - i + count, count)
        marks_out[:, pl.ds(pl.multiple_of(owner * width, width), width)] = mark_slots[i - 1]

    @pl.loop(0, PIECES)
    def _(piece):
        swap.wait_arrival(piece)
        swap.wait_sent(piece)

    output_gather.last()
    marks.wait_sent()
    gather.wait_sent()
    output_gather.wait_sent()
    line.spread_finish(PIECES, source)


def enter(
    tokens, marks, query_weight, key_weight, value_weight, output_weight, bias, collective_id
):
    count = lax.axis_size("tp")
    rows, width = tokens.shape
    head_cols = query_weight.shape[1]
    plane = 8
    part = 3 * head_cols // 2
    return pl.pallas_call(
        functools.partial(enter_kernel, count),
        out_shape=[
            jax.ShapeDtypeStruct((rows, count * width), tokens.dtype),
            jax.ShapeDtypeStruct((rows // count, count * width), tokens.dtype),
            jax.ShapeDtypeStruct((marks.shape[0], count * width), marks.dtype),
            jax.ShapeDtypeStruct((plane * query_weight.shape[0], 2 * part), query_weight.dtype),
            jax.ShapeDtypeStruct(
                (plane * output_weight.shape[0], output_weight.shape[1]), output_weight.dtype
            ),
            jax.ShapeDtypeStruct((2 * rows, part), jnp.bfloat16),
        ],
        in_specs=[
            pl.BlockSpec(memory_space=pl.ANY),
            pl.BlockSpec(memory_space=pltpu.VMEM),
            *[pl.BlockSpec(memory_space=pl.ANY)] * 4,
            pl.BlockSpec(memory_space=pltpu.VMEM),
        ],
        out_specs=[pl.BlockSpec(memory_space=pltpu.VMEM)] * 6,
        scratch_shapes=[
            pltpu.VMEM((count - 1, *marks.shape), marks.dtype),
            pltpu.VMEM((rows, part), jnp.bfloat16),
            *line_semaphores(count, PIECES)[1],
            pltpu.SemaphoreType.DMA((count - 1,)),
            pltpu.SemaphoreType.DMA((count - 1,)),
            *[pltpu.SemaphoreType.DMA((9,))] * 4,
            pltpu.SemaphoreType.DMA((PIECES,)),
            pltpu.SemaphoreType.DMA((PIECES,)),
            pltpu.SemaphoreType.DMA((8,)),
        ],
        compiler_params=pltpu.CompilerParams(
            collective_id=collective_id, has_side_effects=True, vmem_limit_bytes=60 << 20
        ),
        cost_estimate=pl.CostEstimate(
            flops=80_000_000_000, bytes_accessed=64 * rows * count * width, transcendentals=0
        ),
        name="enter",
    )(tokens, marks, query_weight, key_weight, value_weight, output_weight, bias)


def relay_kernel(count, row_step, use_step, sizes, *refs):
    row_in, use_in, row_out, use_out, shared, swap_in, swap_out, gathers, fill_step = sizes
    refs = list(refs)

    def take(number):
        taken = refs[:number]
        del refs[:number]
        return taken

    x_ref, sum_weight = take(2)
    use_weight = sum_weight if shared else take(1)[0]
    row_inputs, use_inputs = take(row_in), take(use_in)
    next_ref = take(1)[0] if gathers else None
    fill_inputs = take(1) if fill_step is not None else []
    (gathered,) = take(1)
    row_outputs, use_outputs = take(row_out), take(use_out)
    swapped = take(1)[0] if swap_in or swap_out else None
    wholes = take(2) if gathers else []
    fill_outputs = take(1) if fill_step is not None else []
    terms, total, slots, sum_sent, sum_got, spread_sent, spread_got = take(7)
    me, ctx = lax.axis_index("tp"), lax.axis_index("ctx")
    rows = gathered.shape[0]
    height = rows // PIECES
    own = height // count
    width = sum_weight.shape[0]

    def piece_rows(piece, start=0):
        return pl.ds(pl.multiple_of(start + piece * height, height), height)

    def view(piece, owner):
        return gathered.at[pl.ds(pl.multiple_of(piece * height + owner * own, own), own)]

    line = Line(me, count, slots, sum_sent, sum_got, view, spread_sent, spread_got)
    use_gather = next_gather = None
    if gathers:
        use_gather, next_gather = [PlaneGather(whole, *take(2)) for whole in wholes]
        greet(me, count, next_gather.peers())
        shards, use_weight = (use_weight, next_ref), wholes[0]
    else:
        greet(me, count, [{"ctx": 1 - ctx}] if swap_in or swap_out else [])
    swap = None
    if swap_in:
        half = x_ref.shape[1]
        own_half = pl.ds(pl.multiple_of(ctx * half, half), half)
        swap = Swap(
            *take(2),
            lambda piece: x_ref.at[piece_rows(piece, (1 - ctx) * rows)],
            lambda piece: swapped.at[piece_rows(piece), own_half],
        )

        @pl.loop(0, PIECES)
        def _(piece):
            swap.start(piece)
            swapped[piece_rows(piece), own_half] = x_ref[piece_rows(piece, ctx * rows), :]

    if gathers:
        for gather, shard in zip((use_gather, next_gather), shards, strict=True):
            gather.put(shard, take(1)[0])
        use_gather.first()
    if swap_out:
        stage, swap_sent, swap_got = take(3)
        half = swapped.shape[1]
        swap = Swap(
            swap_sent, swap_got,
            lambda piece: stage.at[piece_rows(piece)],
            lambda piece: swapped.at[piece_rows(piece, ctx * rows)],
        )

    @pl.loop(0, PIECES + 5)
    def _(step):
        odd = lax.rem(step, 2)

        def term_of(parity):
            return lambda owner: terms[parity, pl.ds(pl.multiple_of(owner * own, own), own), :]

        def late(pieces, action):
            @pl.when((step >= pieces) & (step < PIECES + pieces))
            def _():
                action(step - pieces)

        def use(piece):
            part = piece_rows(piece)
            result = use_step(part, gathered[part, :], use_weight, use_inputs, use_outputs)
            if swap_out:
                here = ctx == 0
                left, right = result[:, :half], result[:, half:]
                stage[part, :] = jnp.where(here, right, left)
                swap.start(piece)
                swapped[piece_rows(piece, ctx * rows), :] = jnp.where(here, left, right)

        def form(piece):
            if swap_in:
                swap.wait_arrival(piece)
            x = (swapped if swap_in else x_ref)[piece_rows(piece), :]

            @pl.loop(0, width // TILE)
            def _(tile):
                part = pl.ds(pl.multiple_of(tile * TILE, TILE), TILE)
                terms[odd, :, part] = dot_cols(x, sum_weight[part, :])

            line.sum_start(piece, term_of(odd))

        def own_step(piece):
            total[...] = terms[1 - odd, pl.ds(pl.multiple_of(me * own, own), own), :]
            line.sum_end(piece, total)
            view(piece, me)[...] = row_step(piece, total, row_inputs, row_outputs)
            line.spread_start(piece)

        def far_shards(piece):
            for distance in range(3, count):
                line.spread_onward(piece, distance)

        if gathers:
            pl.when(step == 5)(use_gather.last)
        late(5, use)
        late(3, lambda piece: line.spread_onward(piece, 2))
        late(1, lambda piece: line.sum_onward(piece, term_of(1 - odd), [1]))
        late(0, form)
        late(4, far_shards)
        late(2, lambda piece: line.spread_onward(piece, 1))
        if fill_step is not None:
            late(0, lambda piece: fill_step(piece, x_ref, fill_inputs, fill_outputs))
        late(0, lambda piece: line.sum_onward(piece, term_of(odd), range(count - 2, 1, -1)))
        late(1, own_step)
        if gathers:

            @pl.when(step == 3)
            def _():
                use_gather.second()
                next_gather.first()

            pl.when(step == 4)(use_gather.third)
            pl.when(step == 6)(next_gather.second)
            pl.when(step == 8)(next_gather.third)

    if swap is not None:

        @pl.loop(0, PIECES)
        def _(piece):
            if swap_out:
                swap.wait_arrival(piece)
            swap.wait_sent(piece)

    if gathers:
        next_gather.last()
        use_gather.wait_sent()
        next_gather.wait_sent()
    line.sum_finish(PIECES)
    line.spread_finish(PIECES)


def relay(
    x, sum_weight, use_weight, row_inputs, row_step, row_shapes, use_inputs, use_step, use_shapes,
    collective_id, name, rows, swap_in=None, swap_out=None, next_shard=None, fill=None,
):
    count = lax.axis_size("tp")
    width = sum_weight.shape[0]
    height = rows // PIECES
    own = height // count
    shared = use_weight is None
    operands = [x, sum_weight, *([] if shared else [use_weight]), *row_inputs, *use_inputs]
    in_specs = [pl.BlockSpec(memory_space=pltpu.VMEM)] * len(operands)
    shapes = [jax.ShapeDtypeStruct((rows, width), jnp.bfloat16), *row_shapes, *use_shapes]
    shapes += [shape for shape in (swap_in, swap_out) if shape is not None]
    out_specs = [pl.BlockSpec(memory_space=pltpu.VMEM)] * len(shapes)
    extra, last = [], []
    if next_shard is not None:
        operands.append(next_shard)
        in_specs.append(pl.BlockSpec(memory_space=pltpu.VMEM))
        for shard, space in ((use_weight, pltpu.VMEM), (next_shard, pl.ANY)):
            whole = (8 * shard.shape[0], shard.shape[1])
            shapes.append(jax.ShapeDtypeStruct(whole, shard.dtype))
            out_specs.append(pl.BlockSpec(memory_space=space))
        extra = [pltpu.SemaphoreType.DMA((9,))] * 4
        last = [pltpu.SemaphoreType.DMA] * 2
    fill_step = None
    if fill is not None:
        fill_step, fill_input, fill_shape = fill
        operands.append(fill_input)
        in_specs.append(pl.BlockSpec(memory_space=pltpu.VMEM))
        shapes.append(fill_shape)
        out_specs.append(pl.BlockSpec(memory_space=pltpu.VMEM))
    sums, spreads = line_semaphores(count, PIECES)
    swaps = []
    if swap_out is not None:
        swaps.append(pltpu.VMEM((rows, swap_out.shape[1]), swap_out.dtype))
    if swap_in is not None or swap_out is not None:
        swaps += [pltpu.SemaphoreType.DMA((PIECES,))] * 2
    sizes = (
        len(row_inputs), len(use_inputs), len(row_shapes), len(use_shapes), shared,
        swap_in is not None, swap_out is not None, next_shard is not None, fill_step,
    )
    return pl.pallas_call(
        functools.partial(relay_kernel, count, row_step, use_step, sizes),
        out_shape=shapes,
        in_specs=in_specs,
        out_specs=out_specs,
        scratch_shapes=[
            pltpu.VMEM((2, height, width), jnp.float32),
            pltpu.VMEM((own, width), jnp.float32),
            pltpu.VMEM((PIECES, count + 1, own, width), jnp.bfloat16),
            *sums,
            *spreads,
            *extra,
            *swaps,
            *last,
        ],
        compiler_params=pltpu.CompilerParams(
            collective_id=collective_id, has_side_effects=True, vmem_limit_bytes=60 << 20
        ),
        cost_estimate=pl.CostEstimate(
            flops=100_000_000_000, bytes_accessed=64 * rows * width, transcendentals=0
        ),
        name=name,
    )(*operands)


def own_rows_of(piece, like):
    own = like.shape[0] // PIECES
    return pl.ds(pl.multiple_of(piece * own, own), own)


def first_norm_step(piece, total, inputs, outputs):
    tokens, gains, biases = inputs
    first_norm, normed_one, inverse_one = outputs
    part = own_rows_of(piece, tokens)
    summed = tokens[part, :].astype(jnp.float32) + (total[...] + biases[0:1, :])
    normed, inverse = norm_parts(summed)
    result = normed * gains[0:1, :] + biases[1:2, :]
    first_norm[part, :] = result
    normed_one[part, :] = normed
    inverse_one[part, :] = jnp.broadcast_to(inverse, (inverse.shape[0], 128))
    return result.astype(jnp.bfloat16)


def expand_step(rows, chunk, weight, inputs, outputs):
    (bias,) = inputs
    hidden, activated = outputs

    @pl.loop(0, hidden.shape[1] // TILE)
    def _(tile):
        part = pl.ds(pl.multiple_of(tile * TILE, TILE), TILE)
        values = dot_plain(chunk, weight[:, part]) + bias[:, part]
        hidden[rows, part] = values
        activated[rows, part] = gelu_tanh(values).astype(jnp.bfloat16)


def add_sums(piece, sums, *values):
    @pl.when(piece == 0)
    def _():
        sums[...] = jnp.zeros_like(sums)

    for i, value in enumerate(values):
        sums[i : i + 1, :] += jnp.sum(value, axis=0, keepdims=True)


def second_norm_step(piece, total, inputs, outputs):
    first_norm, out_grad, gains, biases = inputs
    mixed, grad_second, sums = outputs
    part = own_rows_of(piece, first_norm)
    normed, inverse = norm_parts(first_norm[part, :] + total[...] + biases[2:3, :])
    result = (normed * gains[1:2, :] + biases[3:4, :]).astype(jnp.bfloat16)
    count, _, width = mixed.shape
    for i in range(count):
        mixed[i, part, :] = result[:, i * width : (i + 1) * width]
    upstream = jnp.concatenate([out_grad[i, part, :] for i in range(count)], axis=1)
    upstream = upstream.astype(jnp.float32)
    grad = norm_back(upstream, normed, inverse, gains[1:2, :])
    grad_second[part, :] = grad
    low = grad.astype(jnp.bfloat16)
    add_sums(piece, sums, upstream * normed, upstream, low.astype(jnp.float32))
    return low


def gelu_slope(values):
    scale = math.sqrt(2.0 / math.pi)
    square = values * values
    bend = jnp.tanh(scale * values * (1.0 + 0.044715 * square))
    inner = scale * (1.0 + 3 * 0.044715 * square)
    return 0.5 * (1.0 + bend) + 0.5 * values * (1.0 - bend * bend) * inner


def shrink_step(rows, chunk, weight, inputs, outputs):
    (hidden,) = inputs
    hidden_low, sums = outputs

    @pl.when(rows.start == 0)
    def _():
        sums[...] = jnp.zeros_like(sums)

    @pl.loop(0, hidden.shape[1] // TILE)
    def _(tile):
        part = pl.ds(pl.multiple_of(tile * TILE, TILE), TILE)
        grad = dot_plain(chunk, weight[:, part]) * gelu_slope(hidden[rows, part])
        low = grad.astype(jnp.bfloat16)
        hidden_low[rows, part] = low
        sums[0:1, part] += jnp.sum(low.astype(jnp.float32), axis=0, keepdims=True)


def first_back_step(piece, total, inputs, outputs):
    grad_second, normed_one, inverse_one, gains = inputs
    grad_inner, sums = outputs
    part = own_rows_of(piece, grad_second)
    normed = normed_one[part, :]
    grad_first = grad_second[part, :] + total[...]
    grad = norm_back(grad_first, normed, inverse_one[part, 0:1], gains[0:1, :])
    grad_inner[part, :] = grad
    low = grad.astype(jnp.bfloat16)
    add_sums(piece, sums, grad_first * normed, grad_first, low.astype(jnp.float32))
    return low


def attended_step(rows, chunk, weight, inputs, outputs):
    result = dot_plain(chunk, weight[...]).astype(jnp.bfloat16)
    if outputs:
        outputs[0][rows, :] = result
    return result


def expand_product_step(piece, x, inputs, outputs):
    (norm_low,), (product,) = inputs, outputs
    height = product.shape[0] // PIECES
    part = pl.ds(pl.multiple_of(piece * height, height), height)
    left = norm_low[:, part].T

    @pl.loop(0, product.shape[1] // TILE)
    def _(tile):
        columns = pl.ds(pl.multiple_of(tile * TILE, TILE), TILE)
        product[part, columns] = dot_plain(left, x[:, columns]).astype(product.dtype)


def peers_in_plane(sizes):
    fsdp, ctx = lax.axis_index("fsdp"), lax.axis_index("ctx")
    return [
        {"fsdp": lax.rem(fsdp + i, sizes[0]), "ctx": lax.rem(ctx + j, sizes[1])}
        for i in range(sizes[0])
        for j in range(sizes[1])
        if i or j
    ]


def input_kernel(
    sizes, x_ref, weight, inner_ref, rows_ref, hidden_ref, out_ref, vectors_ref,
    term_ref, total, slots, own_vectors, tp_slots, plane_slots,
    sum_sent, sum_got, tp_sent, tp_got, plane_sent, plane_got, hooks=None,
):
    count = sizes[2]
    me = lax.axis_index("tp")
    height = x_ref.shape[0] // PIECES
    own = height // count
    width = out_ref.shape[1]
    line = Line(me, count, slots, sum_sent, sum_got, None, None, None)
    tp_peers, plane_peers = peers_along_tp(me, count), peers_in_plane(sizes)
    greet_peers(tp_peers + plane_peers)

    def own_part(index):
        return rows_ref.at[:, pl.ds(pl.multiple_of(index * width, width), width)]

    over_tp = Exchange(
        tp_peers, tp_sent, tp_got,
        lambda i: own_part(lax.rem(me + i, count)), lambda i: tp_slots.at[i],
    )
    over_plane = Exchange(
        plane_peers, plane_sent, plane_got, lambda _: own_vectors, lambda i: plane_slots.at[i]
    )
    opening, before, after, closing = hooks or (lambda *_: None,) * 4
    opening()
    over_tp.start()

    def terms(piece):
        def term(owner):
            features = pl.ds(pl.multiple_of(owner * width, width), width)
            term_ref[...] = dot_cols(
                x_ref[pl.ds(pl.multiple_of(piece * height, height), height), :],
                weight[features, :],
            )
            inner = inner_ref[pl.ds(pl.multiple_of(piece * own, own), own), features]
            term_ref[pl.ds(pl.multiple_of(me * own, own), own), :] += inner
            return term_ref[...]

        return term

    def pack():
        over_tp.wait_arrivals()
        own_vectors[0:8, :] = own_part(me)[...]
        for i in range(count - 1):
            own_vectors[0:8, :] += tp_slots[i]
        own_vectors[8:, :] = jnp.zeros_like(own_vectors[8:, :])
        hidden_rows = hidden_ref.shape[1] // width
        for i in range(hidden_rows):
            own_vectors[8 + i : 9 + i, :] = hidden_ref[0:1, i * width : (i + 1) * width]
        for i in range(x_ref.shape[1] // width):
            part = x_ref[:, i * width : (i + 1) * width].astype(jnp.float32)
            place = 8 + hidden_rows + i
            own_vectors[place : place + 1, :] = jnp.sum(part, axis=0, keepdims=True)
        over_plane.start()

    @pl.loop(0, PIECES)
    def _(piece):
        before(piece)
        line.sum_start(piece, terms(piece))
        line.sum_onward(piece, terms(piece), range(count - 2, 0, -1))
        after(piece)

    pack()
    closing()

    @pl.loop(0, PIECES)
    def _(piece):
        total[...] = terms(piece)(me)
        line.sum_end(piece, total)
        rows = pl.ds(pl.multiple_of(piece * height, height), height)
        out_ref[rows, :] = total[...].astype(out_ref.dtype)

    over_plane.wait_arrivals()
    vectors_ref[...] = own_vectors[...]
    for i in range(len(plane_peers)):
        vectors_ref[...] += plane_slots[i]
    over_tp.wait_sent()
    over_plane.wait_sent()
    line.sum_finish(PIECES)


def input_sum(x, weight, inner, row_sums, hidden_sums, collective_id):
    sizes = tuple(lax.axis_size(axis) for axis in ("fsdp", "ctx", "tp"))
    count = sizes[2]
    others = sizes[0] * sizes[1] - 1
    rows = x.shape[0]
    width = weight.shape[0] // count
    height = rows // PIECES
    packed = 8 + -(-(hidden_sums.shape[1] + x.shape[1]) // (8 * width)) * 8
    return pl.pallas_call(
        functools.partial(input_kernel, sizes),
        out_shape=[
            jax.ShapeDtypeStruct((rows, width), jnp.bfloat16),
            jax.ShapeDtypeStruct((packed, width), jnp.float32),
        ],
        in_specs=[pl.BlockSpec(memory_space=pltpu.VMEM)] * 5,
        out_specs=[pl.BlockSpec(memory_space=pltpu.VMEM)] * 2,
        scratch_shapes=[
            pltpu.VMEM((height, width), jnp.float32),
            pltpu.VMEM((height, width), jnp.float32),
            pltpu.VMEM((PIECES, count + 1, height, width), jnp.bfloat16),
            pltpu.VMEM((packed, width), jnp.float32),
            pltpu.VMEM((count - 1, 8, width), jnp.float32),
            pltpu.VMEM((others, packed, width), jnp.float32),
            *line_semaphores(count, PIECES)[0],
            pltpu.SemaphoreType.DMA((count - 1,)),
            pltpu.SemaphoreType.DMA((count - 1,)),
            pltpu.SemaphoreType.DMA((others,)),
            pltpu.SemaphoreType.DMA((others,)),
        ],
        compiler_params=pltpu.CompilerParams(
            collective_id=collective_id, has_side_effects=True, vmem_limit_bytes=40 << 20
        ),
        cost_estimate=pl.CostEstimate(
            flops=60_000_000_000, bytes_accessed=64 * rows * width, transcendentals=0
        ),
        name="input_sum",
    )(x, weight, inner, row_sums, hidden_sums)


class PlaneSum:
    def __init__(self, parts, core_slots, first_slots, last_slots, sent, got):
        self.parts, self.core_slots = parts, core_slots
        self.first_slots, self.last_slots = first_slots, last_slots
        self.sent, self.got = sent, got
        self.fsdp, self.ctx = lax.axis_index("fsdp"), lax.axis_index("ctx")
        self.twin = self.fsdp + 1 - 2 * lax.rem(self.fsdp, 2)
        self.half = parts.shape[2] // 2

    def number(self, fsdp, over_x, over_y):
        chip = lax.rem(fsdp + 2 * over_x, 4)
        return chip * 2 + (1 - self.ctx if over_y else self.ctx)

    def view(self, over_x, over_y, side):
        columns = pl.ds(side * self.half, self.half)
        return self.parts.at[self.number(self.fsdp, over_x, over_y), :, columns]

    def copy(self, number, source, place, peer):
        return pltpu.make_async_remote_copy(
            src_ref=source,
            dst_ref=place,
            send_sem=self.sent.at[number],
            recv_sem=self.got.at[number],
            device_id=peer,
            device_id_type=MESH,
        )

    def core_copy(self, number):
        over_x, over_y = number // 2, number % 2
        source = self.parts.at[self.number(self.twin, over_x, over_y)]
        return self.copy(number, source, self.core_slots.at[number], {"fsdp": self.twin})

    def x_peer(self):
        return {"fsdp": lax.rem(self.fsdp + 2, 4)}

    def y_peer(self):
        return {"ctx": 1 - self.ctx}

    def first_copy(self, number):
        slot = self.first_slots.at[number]
        if number < 2:
            return self.copy(4 + number, self.view(1, number, 0), slot, self.x_peer())
        return self.copy(4 + number, self.view(number - 2, 1, 1), slot, self.y_peer())

    def last_copy(self, side):
        slot = self.last_slots.at[side]
        if side == 0:
            return self.copy(8, self.view(0, 1, 0), slot, self.y_peer())
        return self.copy(9, self.view(1, 0, 1), slot, self.x_peer())

    def add(self, view, slot):
        total = view[...].astype(jnp.float32) + slot[...].astype(jnp.float32)
        view[...] = total.astype(view.dtype)

    def start(self):
        for number in (3, 2, 1, 0):
            self.core_copy(number).start()

    def second(self):
        for number in (3, 2, 1, 0):
            self.core_copy(number).wait_recv()
            shard = self.parts.at[self.number(self.fsdp, number // 2, number % 2)]
            self.add(shard, self.core_slots.at[number])
            if number == 3:
                self.first_copy(1).start()
                self.first_copy(3).start()
            if number == 2:
                self.first_copy(0).start()
            if number == 1:
                self.first_copy(2).start()

    def third(self):
        self.first_copy(1).wait_recv()
        self.add(self.view(0, 1, 0), self.first_slots.at[1])
        self.last_copy(0).start()
        self.first_copy(3).wait_recv()
        self.add(self.view(1, 0, 1), self.first_slots.at[3])
        self.last_copy(1).start()

    def finish(self):
        totals = []
        for side in range(2):
            number = 2 * side
            self.first_copy(number).wait_recv()
            self.last_copy(side).wait_recv()
            total = self.view(0, 0, side)[...].astype(jnp.float32)
            total += self.first_slots[number].astype(jnp.float32)
            totals.append(total + self.last_slots[side].astype(jnp.float32))
        for number in range(4):
            self.core_copy(number).wait_send()
            self.first_copy(number).wait_send()
        for side in range(2):
            self.last_copy(side).wait_send()
        return totals

    @staticmethod
    def scratch(shards, height, width):
        return [
            pltpu.VMEM((shards, height, width), jnp.bfloat16),
            pltpu.VMEM((4, height, width), jnp.bfloat16),
            pltpu.VMEM((4, height, width // 2), jnp.bfloat16),
            pltpu.VMEM((2, height, width // 2), jnp.bfloat16),
            pltpu.SemaphoreType.DMA((10,)),
            pltpu.SemaphoreType.DMA((10,)),
        ]


def leave_kernel(
    sizes, grads_ref, tokens_ref, weight, inner_ref, rows_ref, hidden_ref, branch_ref, attended_ref,
    out_ref, vectors_ref, query_out, key_out, value_out, output_out,
    x_ref, term_ref, total, slots, own_vectors, tp_slots, plane_slots,
    sum_sent, sum_got, tp_sent, tp_got, plane_sent, plane_got, swap_sent, swap_got, *sum_scratch,
):
    count = sizes[2]
    me, ctx = lax.axis_index("tp"), lax.axis_index("ctx")
    rows = x_ref.shape[0]
    height = rows // PIECES
    part = grads_ref.shape[1]
    plane_sum, output_sum = PlaneSum(*sum_scratch[:6]), PlaneSum(*sum_scratch[6:])
    shard = plane_sum.parts.shape[1]

    def piece_rows(piece, start=0):
        return pl.ds(pl.multiple_of(start + piece * height, height), height)

    own_columns = pl.ds(pl.multiple_of(ctx * part, part), part)
    swap = Swap(
        swap_sent, swap_got,
        lambda piece: grads_ref.at[piece_rows(piece, (1 - ctx) * rows)],
        lambda piece: x_ref.at[piece_rows(piece), own_columns],
    )

    def products(sums, fsdp, left, right):
        for over_x in (1, 0):
            for over_y in (1, 0):
                number = sums.number(fsdp, over_x, over_y)
                columns = pl.ds(pl.multiple_of(number * shard, shard), shard)
                sums.parts[number] = dot_rows(left[:, columns], right[...]).astype(jnp.bfloat16)

    def opening():
        @pl.loop(0, PIECES)
        def _(piece):
            swap.start(piece)

        products(output_sum, output_sum.twin, branch_ref, attended_ref)
        output_sum.start()
        x_ref[:, own_columns] = grads_ref[pl.ds(pl.multiple_of(ctx * rows, rows), rows), :]
        products(output_sum, output_sum.fsdp, branch_ref, attended_ref)
        output_sum.second()

    last = PIECES - 1
    begin = jnp.where((me == 0) | (me == count - 1), last, 2)

    def before(piece):
        @pl.when(piece <= begin)
        def _():
            swap.wait_arrival(piece)

    def after(piece):
        @pl.when(piece == begin)
        def _():
            @pl.loop(begin + 1, PIECES)
            def _(other):
                swap.wait_arrival(other)

            products(plane_sum, plane_sum.twin, tokens_ref, x_ref)
            plane_sum.start()

        @pl.when(piece == jnp.minimum(begin + 1, last))
        def _():
            products(plane_sum, plane_sum.fsdp, tokens_ref, x_ref)

        pl.when(piece == jnp.minimum(begin + 2, last))(plane_sum.second)
        pl.when(piece == jnp.minimum(begin + 3, last))(output_sum.third)

    def closing():
        plane_sum.third()

    input_kernel(
        sizes, x_ref, weight, inner_ref, rows_ref, hidden_ref, out_ref, vectors_ref,
        term_ref, total, slots, own_vectors, tp_slots, plane_slots,
        sum_sent, sum_got, tp_sent, tp_got, plane_sent, plane_got,
        hooks=(opening, before, after, closing),
    )
    halves = plane_sum.finish()
    third = part // 3
    for side, half in enumerate(halves):
        for i, ref in enumerate((query_out, key_out, value_out)):
            ref[:, side * third : (side + 1) * third] = half[:, i * third : (i + 1) * third]
    output_out[...] = jnp.concatenate(output_sum.finish(), axis=1)

    @pl.loop(0, PIECES)
    def _(piece):
        swap.wait_sent(piece)


def leave(grads, tokens, weight, inner, row_sums, hidden_sums, branch, attended, collective_id):
    sizes = tuple(lax.axis_size(axis) for axis in ("fsdp", "ctx", "tp"))
    count = sizes[2]
    others = sizes[0] * sizes[1] - 1
    rows, features = tokens.shape
    part = grads.shape[1]
    width = features // count
    height = rows // PIECES
    shard = features // (others + 1)
    packed = 8 + -(-(hidden_sums.shape[1] + 2 * part) // (8 * width)) * 8
    return pl.pallas_call(
        functools.partial(leave_kernel, sizes),
        out_shape=[
            jax.ShapeDtypeStruct((rows, width), jnp.bfloat16),
            jax.ShapeDtypeStruct((packed, width), jnp.float32),
            *[jax.ShapeDtypeStruct((shard, 2 * part // 3), jnp.float32)] * 4,
        ],
        in_specs=[pl.BlockSpec(memory_space=pltpu.VMEM)] * 8,
        out_specs=[pl.BlockSpec(memory_space=pltpu.VMEM)] * 6,
        scratch_shapes=[
            pltpu.VMEM((rows, 2 * part), jnp.bfloat16),
            pltpu.VMEM((height, width), jnp.float32),
            pltpu.VMEM((height, width), jnp.float32),
            pltpu.VMEM((PIECES, count + 1, height, width), jnp.bfloat16),
            pltpu.VMEM((packed, width), jnp.float32),
            pltpu.VMEM((count - 1, 8, width), jnp.float32),
            pltpu.VMEM((others, packed, width), jnp.float32),
            *line_semaphores(count, PIECES)[0],
            pltpu.SemaphoreType.DMA((count - 1,)),
            pltpu.SemaphoreType.DMA((count - 1,)),
            pltpu.SemaphoreType.DMA((others,)),
            pltpu.SemaphoreType.DMA((others,)),
            pltpu.SemaphoreType.DMA((PIECES,)),
            pltpu.SemaphoreType.DMA((PIECES,)),
            *PlaneSum.scratch(others + 1, shard, 2 * part),
            *PlaneSum.scratch(others + 1, shard, attended.shape[1]),
        ],
        compiler_params=pltpu.CompilerParams(
            collective_id=collective_id, has_side_effects=True, vmem_limit_bytes=60 << 20
        ),
        cost_estimate=pl.CostEstimate(
            flops=60_000_000_000, bytes_accessed=64 * rows * width, transcendentals=0
        ),
        name="leave",
    )(grads, tokens, weight, inner, row_sums, hidden_sums, branch, attended)


def to_own_rows(wide):
    count = lax.axis_size("tp")
    parts = wide.reshape(PIECES, count, -1, wide.shape[1])
    return lax.dynamic_index_in_dim(parts, lax.axis_index("tp"), 1, keepdims=False).reshape(
        -1, wide.shape[1]
    )


def spread_own(block):
    count = lax.axis_size("tp")
    rows, width = block.shape
    parts = block.reshape(PIECES, count, -1, width).transpose(1, 0, 2, 3)
    return lax.all_to_all(
        parts.reshape(count, -1, width), "tp", split_axis=0, concat_axis=0, tiled=True
    )


def unspread_own(parts):
    count, own_rows, width = parts.shape
    got = lax.all_to_all(parts, "tp", split_axis=0, concat_axis=0, tiled=True)
    return got.reshape(count, PIECES, -1, width).transpose(1, 0, 2, 3).reshape(-1, width)


def body(
    tokens,
    segments,
    query_weight,
    key_weight,
    value_weight,
    output_weight,
    expand_weight,
    shrink_weight,
    query_bias,
    value_bias,
    hidden_bias,
    norm_gains,
    row_biases,
    out_grad,
):
    rows = tokens.shape[0]
    head_cols = query_weight.shape[1]
    heads = head_cols // HD
    plane = ("fsdp", "ctx")
    plane_sizes = tuple(lax.axis_size(axis) for axis in plane)
    by_heads = plane_sizes == (4, 2) and heads % 2 == 0

    def weight_rows(weight):
        return lax.all_gather(weight, plane, axis=0, tiled=True)

    marks = jnp.concatenate(
        [norm_gains, row_biases, jnp.zeros((10, norm_gains.shape[1]), norm_gains.dtype)]
    )
    block_index = lax.axis_index("fsdp") * plane_sizes[1] + lax.axis_index("ctx")
    qkv_bias = jnp.stack([query_bias, jnp.zeros_like(query_bias), value_bias])
    qkv_bias = qkv_bias.astype(jnp.float32)
    if by_heads:
        half_bias = qkv_bias.reshape(3, 2, -1).transpose(1, 0, 2).reshape(1, -1)
        wide_tokens, own_tokens, wide_marks, wide_qkv, full_output, qkv_heads = enter(
            tokens, marks, query_weight, key_weight, value_weight, output_weight, half_bias, 0
        )
        queries = keys = values = qkv_heads
        own_heads = heads // 2
        bounds = (segments.reshape(-1, plane_sizes[1] * rows),)
    else:
        wide_qkv = weight_rows(jnp.concatenate([query_weight, key_weight, value_weight], axis=1))
        wide_tokens, wide_marks = gather_features(tokens, marks, 0)
        own_tokens = to_own_rows(wide_tokens)
        qkv = dot_plain(wide_tokens, wide_qkv) + qkv_bias.reshape(1, -1)
        queries, keys, values = jnp.split(qkv.astype(jnp.bfloat16), 3, axis=1)
        own_heads = heads
        keys, values = padded(keys, WIN), padded(values, WIN)
        ids = jnp.concatenate(
            [
                jnp.full((WIN,), -1, jnp.int32),
                segments,
                jnp.full((WIN,), jnp.iinfo(jnp.int32).max, jnp.int32),
            ]
        )
        full_output, full_expand = weight_rows(output_weight), weight_rows(expand_weight)
        key_ids = lax.dynamic_slice_in_dim(ids, block_index * rows, rows + 2 * WIN, 0)
        bounds = key_bounds(key_ids[WIN : WIN + rows], key_ids, WIN)
    places = (0, own_heads, 2 * own_heads) if by_heads else (0, 0, 0)
    gains = wide_marks[:2].astype(jnp.float32)
    biases = wide_marks[2:6].astype(jnp.float32)
    wide_marks, out_grad = lax.optimization_barrier((wide_marks, out_grad))
    upstream = spread_own(out_grad)
    attended_heads, lse = attend(queries, keys, values, own_heads, bounds, places)
    attended_heads, upstream = lax.optimization_barrier((attended_heads, upstream))

    own_rows, features = own_tokens.shape
    hidden_cols = expand_weight.shape[1]

    def shape(extent, kind=jnp.float32):
        return jax.ShapeDtypeStruct(extent, kind)

    own_shape = shape((own_rows, features))
    norm_low, first_norm, normed_one, inverse_one, hidden, activated, *more = relay(
        attended_heads, full_output, expand_weight if by_heads else full_expand,
        [own_tokens, gains, biases], first_norm_step,
        [own_shape, own_shape, shape((own_rows, 128))],
        [hidden_bias.astype(jnp.float32)[None]], expand_step,
        [shape((rows, hidden_cols)), shape((rows, hidden_cols), jnp.bfloat16)],
        1, "first_norm", rows,
        swap_in=shape((rows, head_cols), jnp.bfloat16) if by_heads else None,
        next_shard=shrink_weight if by_heads else None,
    )
    if by_heads:
        attended, full_expand, full_shrink = more
    else:
        attended, full_shrink = attended_heads, weight_rows(shrink_weight)
    ffn_low, mixed_own, grad_second, second_sums, hidden_low, hidden_sums = relay(
        activated, full_shrink, None,
        [first_norm, upstream, gains, biases], second_norm_step,
        [shape(upstream.shape, jnp.bfloat16), own_shape, shape((8, features))],
        [hidden], shrink_step,
        [shape((rows, hidden_cols), jnp.bfloat16), shape((8, hidden_cols))],
        2, "second_norm", rows,
    )

    def owner_sum(grad):
        return lax.psum_scatter(
            grad, plane, scatter_dimension=0, tiled=True
        )

    hidden_low, shrink_part = lax.optimization_barrier(
        (hidden_low, dot_rows(ffn_low, activated).astype(jnp.bfloat16))
    )
    shrink_grad = owner_sum(shrink_part)
    branch_low, grad_inner, first_sums, attended_grad, expand_part = relay(
        hidden_low, full_expand, full_output,
        [grad_second, normed_one, inverse_one, gains], first_back_step,
        [own_shape, shape((8, features))],
        [], attended_step,
        [] if by_heads else [shape((rows, head_cols), jnp.bfloat16)],
        3, "first_back", rows,
        swap_out=shape((2 * rows, head_cols // 2), jnp.bfloat16) if by_heads else None,
        fill=(expand_product_step, norm_low, shape((features, hidden_cols), jnp.bfloat16)),
    )
    expand_grad = owner_sum(expand_part)
    attended_grad, mixed_own, shrink_grad = lax.optimization_barrier(
        (attended_grad, mixed_own, shrink_grad)
    )
    mixed = unspread_own(mixed_own)

    if by_heads:
        (grads,) = attend_back(
            queries, keys, values, attended_heads, attended_grad, lse, bounds, places, True
        )
        grads, mixed = lax.optimization_barrier((grads, mixed))
    else:
        query_low, key_ext, value_ext = attend_back(
            queries, keys, values, attended_heads, attended_grad, lse, bounds
        )

        def fold(ext):
            edges = jnp.concatenate([ext[:WIN], ext[WIN + rows :]], axis=0)
            around = padded(edges, WIN)
            own = ext[WIN : WIN + rows]
            own = own.at[:WIN].add(around[:WIN]).at[rows - WIN :].add(around[3 * WIN :])
            return own.astype(jnp.bfloat16)

        qkv_low = jnp.concatenate([query_low, fold(key_ext), fold(value_ext)], axis=1)
    row_sums = jnp.concatenate(
        [
            first_sums[0:1], second_sums[0:1],
            first_sums[2:3], first_sums[1:2], second_sums[2:3], second_sums[1:2],
            jnp.zeros_like(first_sums[:2]),
        ]
    )
    sides = 2 if by_heads else 1

    def by_kind(columns):
        parts = columns.reshape(-1, sides, 3, head_cols // sides)
        return [parts[:, :, i].reshape(-1, head_cols) for i in range(3)]

    if by_heads:
        input_grad, vectors, query_grad, key_grad, value_grad, output_grad = leave(
            grads, wide_tokens, wide_qkv, grad_inner, row_sums, hidden_sums[:1], branch_low,
            attended, 4,
        )
    else:
        input_grad, vectors = input_sum(
            qkv_low, wide_qkv, grad_inner, row_sums, hidden_sums[:1], 4
        )
        output_grad = owner_sum(dot_rows(branch_low, attended).astype(jnp.bfloat16))
        qkv_grad = owner_sum(dot_rows(wide_tokens, qkv_low).astype(jnp.bfloat16))
        query_grad, key_grad, value_grad = by_kind(qkv_grad.astype(jnp.float32))
    hidden_rows = hidden_cols // head_cols
    query_sum, _, value_sum = by_kind(
        vectors[8 + hidden_rows : 8 + hidden_rows + 3].reshape(1, -1)
    )
    return (
        mixed,
        input_grad,
        query_grad,
        key_grad,
        value_grad,
        output_grad.astype(jnp.float32),
        expand_grad.astype(jnp.float32),
        shrink_grad.astype(jnp.float32),
        query_sum[0],
        value_sum[0],
        vectors[8 : 8 + hidden_rows].reshape(-1),
        vectors[:2],
        vectors[2:6],
    )


def solution(mesh):
    rows, whole, cols = P(("fsdp", "ctx"), "tp"), P(), P("tp")
    wide = P(None, "tp")
    return jax.shard_map(
        body,
        mesh=mesh,
        in_specs=(rows, whole) + (rows,) * 6 + (cols,) * 3 + (wide,) * 2 + (rows,),
        out_specs=(rows,) * 8 + (cols,) * 3 + (wide,) * 2,
        check_vma=False,
    )
```

```python
import functools
import math

import jax
import jax.numpy as jnp
from jax import lax
from jax.experimental import pallas as pl
from jax.experimental.pallas import tpu as pltpu
from jax.sharding import PartitionSpec as P

HD = 128
WIN = 1024
QB = 512
KB = 512

epsilon = 1e-06
hidden_floor = -1e30
score_scale = 1.0 / math.sqrt(HD)
log2_e = 1.0 / math.log(2.0)


def dot_plain(left, right):
    return jnp.dot(left, right, preferred_element_type=jnp.float32)


def dot_rows(left, right):
    return lax.dot_general(
        left, right, (((0,), (0,)), ((), ())), preferred_element_type=jnp.float32
    )


def dot_cols(left, right):
    return lax.dot_general(
        left, right, (((1,), (1,)), ((), ())), preferred_element_type=jnp.float32
    )


def block_bounds(block, rows, bounds, marks):
    if len(bounds) == 4:
        first, last, low, high = bounds
        return first[block], last[block], low[...], high[...]
    (ids,) = bounds
    run = ids.shape[1]

    @pl.when((pl.program_id(0) == 0) & (block == 0))
    def _():
        own = lax.axis_index("fsdp")
        own_ids = ids[pl.ds(own, 1), :]
        for i in range(2):
            marks[i] = jnp.sum((own_ids <= 3 * own + i).astype(jnp.int32))

    second, third = marks[0], marks[1]

    def bounds_at(places):
        start = jnp.where(places < second, 0, jnp.where(places < third, second, third))
        stop = jnp.where(places < second, second, jnp.where(places < third, third, run))
        return jnp.maximum(start, places - WIN), jnp.minimum(stop - 1, places + WIN)

    begin = block * rows
    low, high = bounds_at(begin + lax.broadcasted_iota(jnp.int32, (1, rows), 1))
    return bounds_at(begin)[0] // KB, bounds_at(begin + rows - 1)[1] // KB + 1, low, high


def bound_operands(bounds):
    if len(bounds) == 4:
        mark_spec = pl.BlockSpec((1, QB), lambda h, i, *_: (0, i))
        return list(bounds[:2]), list(bounds[2:]), [mark_spec, mark_spec]
    shape = bounds[0].shape
    return [], list(bounds), [pl.BlockSpec(shape, lambda h, i, *_: (0, 0))]


def attend_kernel(scalars, *refs):
    bounds = refs[:scalars]
    q_ref, k_ref, v_ref, *arrays, out_ref, lse_ref, vt, marks = refs[scalars:]
    block = pl.program_id(1)
    rows = q_ref.shape[0]

    @pl.when(block == 0)
    def _():
        vt[...] = v_ref[...].T

    queries = q_ref[...]
    first, last, low, high = block_bounds(block, rows, (*bounds, *arrays), marks)
    places = lax.broadcasted_iota(jnp.int32, (KB, rows), 0)

    def step(number, carry):
        top, total, mixed = carry
        start = pl.multiple_of(number * KB, KB)
        scores = dot_cols(k_ref[pl.ds(start, KB), :], queries) * (score_scale * log2_e)
        keep = (places >= low - start) & (places <= high - start)
        scores = jnp.where(keep, scores, hidden_floor)
        new_top = jnp.maximum(top, jnp.max(scores, axis=0, keepdims=True))
        shrink = jnp.exp2(top - new_top)
        powers = jnp.exp2(scores - new_top)
        total = total * shrink + jnp.sum(powers, axis=0, keepdims=True)
        mixed = mixed * shrink + dot_plain(vt[:, pl.ds(start, KB)], powers.astype(jnp.bfloat16))
        return new_top, total, mixed

    top, total, mixed = lax.fori_loop(
        first,
        last,
        step,
        (
            jnp.full((1, rows), hidden_floor, jnp.float32),
            jnp.zeros((1, rows), jnp.float32),
            jnp.zeros((HD, rows), jnp.float32),
        ),
    )
    out_ref[...] = (mixed / total).T.astype(out_ref.dtype)
    lse_ref[...] = (top + jnp.log2(total))[None]


def attend(queries, keys, values, heads, bounds, places=(0, 0, 0)):
    rows, span = queries.shape[0], keys.shape[0]
    width = heads * HD
    q_at, k_at, v_at = places
    scalars, arrays, specs = bound_operands(bounds)
    return pl.pallas_call(
        functools.partial(attend_kernel, len(scalars)),
        out_shape=(
            jax.ShapeDtypeStruct((rows, width), jnp.bfloat16),
            jax.ShapeDtypeStruct((heads, 1, rows), jnp.float32),
        ),
        grid_spec=pltpu.PrefetchScalarGridSpec(
            num_scalar_prefetch=len(scalars),
            grid=(heads, rows // QB),
            in_specs=[
                pl.BlockSpec((QB, HD), lambda h, i, *_: (i, h + q_at)),
                pl.BlockSpec((span, HD), lambda h, i, *_: (0, h + k_at)),
                pl.BlockSpec((span, HD), lambda h, i, *_: (0, h + v_at)),
                *specs,
            ],
            out_specs=[
                pl.BlockSpec((QB, HD), lambda h, i, *_: (i, h)),
                pl.BlockSpec((1, 1, QB), lambda h, i, *_: (h, 0, i)),
            ],
            scratch_shapes=[pltpu.VMEM((HD, span), jnp.bfloat16), pltpu.SMEM((2,), jnp.int32)],
        ),
        compiler_params=pltpu.CompilerParams(vmem_limit_bytes=32 << 20),
        cost_estimate=pl.CostEstimate(
            flops=3 * rows * span * width,
            bytes_accessed=2 * (2 * rows + 2 * span) * width,
            transcendentals=rows * span * heads,
        ),
        name="attend",
    )(*scalars, queries, keys, values, *arrays)


def attend_back_kernel(scalars, arrays, *refs):
    bounds = refs[:scalars]
    q_ref, k_ref, v_ref, o_ref, g_ref, lse_ref, *refs = refs[scalars:]
    bounds = (*bounds, *refs[:arrays])
    *results, kt, dk_sum, dv_sum, marks = refs[arrays:]
    head, block = pl.program_id(0), pl.program_id(1)
    rows = q_ref.shape[0]

    @pl.when(block == 0)
    def _():
        kt[...] = k_ref[...].T
        dk_sum[...] = jnp.zeros_like(dk_sum)
        dv_sum[...] = jnp.zeros_like(dv_sum)

    queries = q_ref[...]
    upstream = g_ref[...]
    lse = lse_ref[0]
    first, last, low, high = block_bounds(block, rows, bounds, marks)
    places = lax.broadcasted_iota(jnp.int32, (KB, rows), 0)
    product = upstream.astype(jnp.float32) * o_ref[...].astype(jnp.float32)
    delta = jnp.sum(product.T, axis=0, keepdims=True)

    def step(number, dq):
        start = pl.multiple_of(number * KB, KB)
        window = pl.ds(start, KB)
        scores = dot_cols(k_ref[window, :], queries) * (score_scale * log2_e)
        keep = (places >= low - start) & (places <= high - start)
        probs = jnp.exp2(jnp.where(keep, scores - lse, hidden_floor))
        prob_grad = dot_cols(v_ref[window, :], upstream)
        score_grad = (probs * (prob_grad - delta)).astype(jnp.bfloat16)
        dv_sum[window, :] += dot_plain(probs.astype(jnp.bfloat16), upstream)
        dk_sum[window, :] += dot_plain(score_grad, queries)
        return dq + dot_plain(kt[:, window], score_grad)

    dq = lax.fori_loop(first, last, step, jnp.zeros((HD, rows), jnp.float32))
    dq = (dq * score_scale).T
    if len(results) == 1:
        width = results[0].shape[1] // 3

        def place(part):
            start = pl.multiple_of(part * width + head * HD, HD)
            return results[0].at[:, pl.ds(start, HD)]

        query_place = place(0).at[pl.ds(pl.multiple_of(block * rows, rows), rows)]
        key_place, value_place = place(1), place(2)
    else:
        query_place, key_place, value_place = results
    query_place[...] = dq.astype(query_place.dtype)

    @pl.when(block == pl.num_programs(1) - 1)
    def _():
        key_place[...] = (dk_sum[...] * score_scale).astype(key_place.dtype)
        value_place[...] = dv_sum[...].astype(value_place.dtype)


def attend_back(
    queries, keys, values, out, upstream, lse, bounds, places=(0, 0, 0), merged=False
):
    rows, width = out.shape
    span = keys.shape[0]
    heads = width // HD
    q_at, k_at, v_at = places
    row_spec = pl.BlockSpec((QB, HD), lambda h, i, *_: (i, h))
    key_spec = pl.BlockSpec((span, HD), lambda h, i, *_: (0, h))
    scalars, arrays, specs = bound_operands(bounds)
    return pl.pallas_call(
        functools.partial(attend_back_kernel, len(scalars), len(arrays)),
        out_shape=[jax.ShapeDtypeStruct((rows, 3 * width), jnp.bfloat16)]
        if merged
        else [
            jax.ShapeDtypeStruct((rows, width), jnp.bfloat16),
            jax.ShapeDtypeStruct((span, width), jnp.float32),
            jax.ShapeDtypeStruct((span, width), jnp.float32),
        ],
        grid_spec=pltpu.PrefetchScalarGridSpec(
            num_scalar_prefetch=len(scalars),
            grid=(heads, rows // QB),
            in_specs=[
                pl.BlockSpec((QB, HD), lambda h, i, *_: (i, h + q_at)),
                pl.BlockSpec((span, HD), lambda h, i, *_: (0, h + k_at)),
                pl.BlockSpec((span, HD), lambda h, i, *_: (0, h + v_at)),
                row_spec, row_spec,
                pl.BlockSpec((1, 1, QB), lambda h, i, *_: (h, 0, i)),
                *specs,
            ],
            out_specs=[pl.BlockSpec((rows, 3 * width), lambda h, i, *_: (0, 0))]
            if merged
            else [row_spec, key_spec, key_spec],
            scratch_shapes=[
                pltpu.VMEM((HD, span), jnp.bfloat16),
                pltpu.VMEM((span, HD), jnp.float32),
                pltpu.VMEM((span, HD), jnp.float32),
                pltpu.SMEM((2,), jnp.int32),
            ],
        ),
        compiler_params=pltpu.CompilerParams(vmem_limit_bytes=32 << 20),
        cost_estimate=pl.CostEstimate(
            flops=8 * rows * span * width,
            bytes_accessed=2 * (4 * rows + 4 * span) * width,
            transcendentals=rows * span * heads,
        ),
        name="attend_back",
    )(*scalars, queries, keys, values, out, upstream, lse, *arrays)


def key_bounds(query_ids, key_ids, offset):
    rows, span = query_ids.shape[0], key_ids.shape[0]
    start = jnp.sum(key_ids[:, None] < query_ids[None, :], axis=0, dtype=jnp.int32)
    stop = jnp.sum(key_ids[:, None] <= query_ids[None, :], axis=0, dtype=jnp.int32)
    places = jnp.arange(rows, dtype=jnp.int32) + offset
    low = jnp.maximum(start, places - WIN)
    high = jnp.minimum(stop - 1, places + WIN)
    first = jnp.min(low.reshape(-1, QB), axis=1) // KB
    last = jnp.max(high.reshape(-1, QB), axis=1) // KB + 1
    return first, last, low[None], high[None]


def padded(block, width):
    count = lax.axis_size("ctx")
    forward = [(i, i + 1) for i in range(count - 1)]
    backward = [(target, source) for source, target in forward]
    below = lax.ppermute(block[block.shape[0] - width :], "ctx", forward)
    above = lax.ppermute(block[:width], "ctx", backward)
    return jnp.concatenate([below, block, above], axis=0)


def norm_parts(rows):
    mean = jnp.mean(rows, axis=-1, keepdims=True)
    square = jnp.mean(rows * rows, axis=-1, keepdims=True)
    inverse = lax.rsqrt(square - mean * mean + epsilon)
    return (rows - mean) * inverse, inverse


def norm_back(upstream, normed, inverse, gain):
    scaled = upstream * gain
    first_mean = jnp.mean(scaled, axis=-1, keepdims=True)
    second_mean = jnp.mean(scaled * normed, axis=-1, keepdims=True)
    return inverse * (scaled - first_mean - normed * second_mean)


def gelu_tanh(values):
    return jax.nn.gelu(values, approximate=True)


MESH = pl.DeviceIdType.MESH
PIECES = 8
TILE = 512


def greet(me, count, others=()):
    barrier = pltpu.get_barrier_semaphore()

    @pl.when(me > 0)
    def _():
        pl.semaphore_signal(barrier, inc=1, device_id={"tp": me - 1}, device_id_type=MESH)

    @pl.when(me < count - 1)
    def _():
        pl.semaphore_signal(barrier, inc=1, device_id={"tp": me + 1}, device_id_type=MESH)

    for other in others:
        pl.semaphore_signal(barrier, inc=1, device_id=other, device_id_type=MESH)

    @pl.when((me == 0) | (me == count - 1))
    def _():
        pl.semaphore_wait(barrier, 1 + len(others))

    @pl.when((me > 0) & (me < count - 1))
    def _():
        pl.semaphore_wait(barrier, 2 + len(others))


def peers_along_tp(me, count):
    return [{"tp": lax.rem(me + i, count)} for i in range(1, count)]


def greet_peers(peers):
    barrier = pltpu.get_barrier_semaphore()
    for peer in peers:
        pl.semaphore_signal(barrier, inc=1, device_id=peer, device_id_type=MESH)
    pl.semaphore_wait(barrier, len(peers))


class Exchange:
    def __init__(self, peers, sent, got, source, place):
        self.peers, self.sent, self.got = peers, sent, got
        self.source, self.place = source, place

    def copies(self):
        for i, peer in enumerate(self.peers):
            yield pltpu.make_async_remote_copy(
                src_ref=self.source(i + 1),
                dst_ref=self.place(i),
                send_sem=self.sent.at[i],
                recv_sem=self.got.at[i],
                device_id=peer,
                device_id_type=MESH,
            )

    def start(self):
        for copy in self.copies():
            copy.start()

    def wait_arrivals(self):
        for copy in self.copies():
            copy.wait_recv()

    def wait_sent(self):
        for copy in self.copies():
            copy.wait_send()


def at_distance(me, count, distance, action):
    for index in (me - distance, me + distance):

        @pl.when((index >= 0) & (index < count))
        def _(index=index):
            action(index)


class Line:
    def __init__(self, me, count, sum_slots, sum_sent, sum_got, spread_view, spread_sent, spread_got):
        self.me, self.count = me, count
        self.sum_slots, self.sum_sent, self.sum_got = sum_slots, sum_sent, sum_got
        self.spread_view, self.spread_sent, self.spread_got = spread_view, spread_sent, spread_got

    def sum_copy(self, piece, owner):
        onward = jnp.where(owner > self.me, self.me + 1, self.me - 1)
        place = jnp.where((owner < self.me) & (owner == self.me - 1), self.count, owner)
        return pltpu.make_async_remote_copy(
            src_ref=self.sum_slots.at[piece, owner],
            dst_ref=self.sum_slots.at[piece, place],
            send_sem=self.sum_sent.at[piece, owner],
            recv_sem=self.sum_got.at[piece, place],
            device_id={"tp": onward},
            device_id_type=MESH,
        )

    def sum_arrival(self, piece, place):
        pltpu.make_async_copy(
            self.sum_slots.at[piece, place],
            self.sum_slots.at[piece, place],
            self.sum_got.at[piece, place],
        ).wait()

    def sum_start(self, piece, term):
        me, count = self.me, self.count

        @pl.when((me == 0) | (me == count - 1))
        def _():
            for k in range(count - 1):
                owner = jnp.where(me == 0, count - 1 - k, k)
                self.sum_slots[piece, owner] = term(owner).astype(jnp.bfloat16)
                self.sum_copy(piece, owner).start()

    def sum_onward(self, piece, term, distances):
        me, count = self.me, self.count

        @pl.when((me > 0) & (me < count - 1))
        def _():
            for distance in distances:

                def pass_on(owner):
                    self.sum_arrival(piece, owner)
                    total = self.sum_slots[piece, owner].astype(jnp.float32) + term(owner)
                    self.sum_slots[piece, owner] = total.astype(jnp.bfloat16)
                    self.sum_copy(piece, owner).start()

                at_distance(me, count, distance, pass_on)

    def sum_end(self, piece, total):
        me, count = self.me, self.count

        @pl.when(me > 0)
        def _():
            self.sum_arrival(piece, me)
            total[...] += self.sum_slots[piece, me].astype(jnp.float32)

        @pl.when(me < count - 1)
        def _():
            self.sum_arrival(piece, count)
            total[...] += self.sum_slots[piece, count].astype(jnp.float32)

    def sum_finish(self, pieces):
        @pl.loop(0, pieces)
        def _(piece):
            for distance in range(1, self.count):
                at_distance(
                    self.me, self.count, distance,
                    lambda owner: self.sum_copy(piece, owner).wait_send(),
                )

    def spread_copy(self, piece, owner, to, sent, source=None):
        return pltpu.make_async_remote_copy(
            src_ref=self.spread_view(piece, owner) if source is None else source,
            dst_ref=self.spread_view(piece, owner),
            send_sem=self.spread_sent.at[piece, sent],
            recv_sem=self.spread_got.at[piece, owner],
            device_id={"tp": to},
            device_id_type=MESH,
        )

    def own_copies(self, piece, action, source=None):
        me, count = self.me, self.count

        @pl.when(me > 0)
        def _():
            action(self.spread_copy(piece, me, me - 1, count, source))

        @pl.when(me < count - 1)
        def _():
            action(self.spread_copy(piece, me, me + 1, me, source))

    def spread_start(self, piece, source=None):
        self.own_copies(piece, lambda copy: copy.start(), source)

    def onward_copy(self, piece, owner, action):
        me, count = self.me, self.count

        @pl.when((owner < me) & (me < count - 1))
        def _():
            action(self.spread_copy(piece, owner, me + 1, owner))

        @pl.when((owner > me) & (me > 0))
        def _():
            action(self.spread_copy(piece, owner, me - 1, owner))

    def spread_onward(self, piece, distance):
        def pass_on(owner):
            view = self.spread_view(piece, owner)
            pltpu.make_async_copy(view, view, self.spread_got.at[piece, owner]).wait()
            self.onward_copy(piece, owner, lambda copy: copy.start())

        at_distance(self.me, self.count, distance, pass_on)

    def spread_finish(self, pieces, source=None):
        @pl.loop(0, pieces)
        def _(piece):
            self.own_copies(
                piece, lambda copy: copy.wait_send(), None if source is None else source(piece)
            )
            for distance in range(1, self.count):
                at_distance(
                    self.me, self.count, distance,
                    lambda owner: self.onward_copy(piece, owner, lambda copy: copy.wait_send()),
                )


def line_semaphores(count, pieces):
    return [
        pltpu.SemaphoreType.DMA((pieces, count)),
        pltpu.SemaphoreType.DMA((pieces, count + 1)),
    ], [
        pltpu.SemaphoreType.DMA((pieces, count + 1)),
        pltpu.SemaphoreType.DMA((pieces, count)),
    ]


def gather_kernel(
    count, x_ref, marks_ref, out_ref, marks_out, slots, sent, got, marks_sent, marks_got
):
    me = lax.axis_index("tp")
    height = x_ref.shape[0] // PIECES
    width = x_ref.shape[1]

    def view(piece, owner):
        return out_ref.at[
            pl.ds(pl.multiple_of(piece * height, height), height),
            pl.ds(pl.multiple_of(owner * width, width), width),
        ]

    def source(piece):
        return x_ref.at[pl.ds(pl.multiple_of(piece * height, height), height)]

    line = Line(me, count, None, None, None, view, sent, got)
    peers = peers_along_tp(me, count)
    greet_peers(peers)

    @pl.loop(0, PIECES)
    def _(piece):
        line.spread_start(piece, source(piece))

    marks = Exchange(
        peers, marks_sent, marks_got, lambda _: marks_ref, lambda i: slots.at[i]
    )
    marks.start()
    own = pl.ds(pl.multiple_of(me * width, width), width)
    out_ref[:, own] = x_ref[...]
    marks_out[:, own] = marks_ref[...]
    for distance in range(1, count):

        @pl.loop(0, PIECES)
        def _(piece, distance=distance):
            line.spread_onward(piece, distance)

    marks.wait_arrivals()
    for i in range(1, count):
        owner = lax.rem(me - i + count, count)
        marks_out[:, pl.ds(pl.multiple_of(owner * width, width), width)] = slots[i - 1]
    marks.wait_sent()
    line.spread_finish(PIECES, source)


def gather_features(x, marks, collective_id):
    count = lax.axis_size("tp")
    rows, width = x.shape
    return pl.pallas_call(
        functools.partial(gather_kernel, count),
        out_shape=[
            jax.ShapeDtypeStruct((rows, count * width), x.dtype),
            jax.ShapeDtypeStruct((marks.shape[0], count * width), marks.dtype),
        ],
        in_specs=[pl.BlockSpec(memory_space=pltpu.VMEM)] * 2,
        out_specs=[pl.BlockSpec(memory_space=pltpu.VMEM)] * 2,
        scratch_shapes=[
            pltpu.VMEM((count - 1, *marks.shape), marks.dtype),
            *line_semaphores(count, PIECES)[1],
            pltpu.SemaphoreType.DMA((count - 1,)),
            pltpu.SemaphoreType.DMA((count - 1,)),
        ],
        compiler_params=pltpu.CompilerParams(
            collective_id=collective_id, has_side_effects=True, vmem_limit_bytes=16 << 20
        ),
        cost_estimate=pl.CostEstimate(
            flops=0, bytes_accessed=64 * rows * count * width, transcendentals=0
        ),
        name="gather_features",
    )(x, marks)


class Swap:
    def __init__(self, sent, got, source, place):
        self.sent, self.got, self.source, self.place = sent, got, source, place

    def copy(self, piece):
        return pltpu.make_async_remote_copy(
            src_ref=self.source(piece),
            dst_ref=self.place(piece),
            send_sem=self.sent.at[piece],
            recv_sem=self.got.at[piece],
            device_id={"ctx": 1 - lax.axis_index("ctx")},
            device_id_type=MESH,
        )

    def start(self, piece):
        self.copy(piece).start()

    def wait_arrival(self, piece):
        self.copy(piece).wait_recv()

    def wait_sent(self, piece):
        self.copy(piece).wait_send()


class PlaneGather:
    def __init__(self, whole, sent, got):
        self.whole, self.sent, self.got = whole, sent, got
        fsdp, self.ctx = lax.axis_index("fsdp"), lax.axis_index("ctx")
        self.fsdp = fsdp
        self.twin = fsdp + 1 - 2 * lax.rem(fsdp, 2)
        self.along_x = lax.rem(fsdp + 2, 4)
        self.twin_x = lax.rem(self.twin + 2, 4)
        self.core_peer = {"fsdp": self.twin}
        self.x_peer = {"fsdp": self.along_x}
        self.y_peer = {"ctx": 1 - self.ctx}

    def peers(self):
        return [self.core_peer, self.x_peer, self.y_peer]

    def shard(self, fsdp, ctx, half=None):
        height = self.whole.shape[0] // 8
        start = (fsdp * 2 + ctx) * height
        if half is not None:
            height //= 2
            start += half * height
        return self.whole.at[pl.ds(pl.multiple_of(start, height), height)]

    def copy(self, number, view, peer):
        return pltpu.make_async_remote_copy(
            src_ref=view,
            dst_ref=view,
            send_sem=self.sent.at[number],
            recv_sem=self.got.at[number],
            device_id=peer,
            device_id_type=MESH,
        )

    def copies(self):
        own = self.shard(self.fsdp, self.ctx)
        from_x = self.shard(self.along_x, self.ctx)
        from_y = self.shard(self.fsdp, 1 - self.ctx)
        return [
            (own, self.core_peer),
            (own, self.x_peer),
            (own, self.y_peer),
            (from_x, self.core_peer),
            (self.shard(self.along_x, self.ctx, 0), self.y_peer),
            (from_y, self.core_peer),
            (self.shard(self.fsdp, 1 - self.ctx, 1), self.x_peer),
            (self.shard(self.along_x, 1 - self.ctx, 0), self.core_peer),
            (self.shard(self.along_x, 1 - self.ctx, 1), self.core_peer),
        ]

    def arrivals(self):
        return [
            self.shard(self.twin, self.ctx),
            self.shard(self.along_x, self.ctx),
            self.shard(self.fsdp, 1 - self.ctx),
            self.shard(self.twin_x, self.ctx),
            self.shard(self.along_x, 1 - self.ctx, 0),
            self.shard(self.twin, 1 - self.ctx),
            self.shard(self.along_x, 1 - self.ctx, 1),
            self.shard(self.twin_x, 1 - self.ctx, 0),
            self.shard(self.twin_x, 1 - self.ctx, 1),
        ]

    def start(self, *numbers):
        copies = self.copies()
        for number in numbers:
            self.copy(number, *copies[number]).start()

    def wait(self, *numbers):
        arrivals = self.arrivals()
        for number in numbers:
            view = arrivals[number]
            pltpu.make_async_copy(view, view, self.got.at[number]).wait()

    def put(self, shard, done):
        copy = pltpu.make_async_copy(shard, self.shard(self.fsdp, self.ctx), done)
        copy.start()
        copy.wait()

    def first(self):
        self.start(1, 2, 0)

    def second(self):
        self.wait(1)
        self.start(4, 3)
        self.wait(2)
        self.start(6, 5)

    def third(self):
        self.wait(4)
        self.start(7)
        self.wait(6)
        self.start(8)

    def last(self):
        self.wait(0, 3, 5, 7, 8)

    def wait_sent(self):
        for number, (view, peer) in enumerate(self.copies()):
            self.copy(number, view, peer).wait_send()


def enter_kernel(
    count, x_ref, marks_ref, query_ref, key_ref, value_ref, output_ref, bias,
    wide, own_tokens, marks_out, weight, output_weight, heads,
    mark_slots, stage, sent, got, marks_sent, marks_got,
    weight_sent, weight_got, output_sent, output_got, swap_sent, swap_got, put_done,
):
    me, ctx = lax.axis_index("tp"), lax.axis_index("ctx")
    rows, width = x_ref.shape
    height = rows // PIECES
    half = query_ref.shape[1] // 2
    part = 3 * half

    def piece_rows(piece, start=0):
        return pl.ds(pl.multiple_of(start + piece * height, height), height)

    def view(piece, owner):
        return wide.at[piece_rows(piece), pl.ds(pl.multiple_of(owner * width, width), width)]

    gather = PlaneGather(weight, weight_sent, weight_got)
    output_gather = PlaneGather(output_weight, output_sent, output_got)
    own_shard = gather.shard(gather.fsdp, ctx)
    own = pl.ds(pl.multiple_of(me * width, width), width)
    puts = [
        (ref.at[:, pl.ds(side * half, half)], own_shard.at[:, pl.ds(side * part + i * half, half)])
        for side in range(2)
        for i, ref in enumerate((query_ref, key_ref, value_ref))
    ]
    puts += [
        (output_ref, output_gather.shard(gather.fsdp, ctx)),
        (x_ref, wide.at[:, own]),
    ]
    puts = [
        pltpu.make_async_copy(source, place, put_done.at[i])
        for i, (source, place) in enumerate(puts)
    ]
    for put in puts:
        put.start()
    line = Line(me, count, None, None, None, view, sent, got)
    tp_peers = peers_along_tp(me, count)
    greet_peers(tp_peers + gather.peers())

    def source(piece):
        return x_ref.at[piece_rows(piece)]

    for piece in range(2):
        line.spread_start(piece, source(piece))
    for put in puts[:7]:
        put.wait()
    gather.first()
    output_gather.first()
    marks = Exchange(
        tp_peers, marks_sent, marks_got, lambda _: marks_ref, lambda i: mark_slots.at[i]
    )
    marks.start()
    marks_out[:, own] = marks_ref[...]
    for put in puts[7:]:
        put.wait()
    swap = Swap(
        swap_sent, swap_got,
        lambda piece: stage.at[piece_rows(piece)],
        lambda piece: heads.at[piece_rows(piece, ctx * rows)],
    )

    def products(piece, side, place):
        x = wide[piece_rows(piece), :]

        @pl.loop(0, 3)
        def _(tile):
            start = pl.multiple_of(side * part + tile * half, half)
            columns = pl.ds(start, half)
            values = dot_plain(x, weight[:, columns]) + bias[:, columns]
            place[:, pl.ds(pl.multiple_of(tile * half, half), half)] = values.astype(jnp.bfloat16)

    @pl.loop(0, PIECES + 7)
    def _(step):
        def late(pieces, action, least=0):
            @pl.when((step >= pieces + least) & (step < PIECES + pieces))
            def _():
                action(step - pieces)

        def use(piece):
            products(piece, 1 - ctx, stage.at[piece_rows(piece)])
            swap.start(piece)
            products(piece, ctx, heads.at[piece_rows(piece, ctx * rows)])

        @pl.when(step == 7)
        def _():
            gather.third()
            gather.last()

        late(0, lambda piece: line.spread_start(piece, source(piece)), 2)
        late(7, use)
        late(5, lambda piece: line.spread_onward(piece, 2))
        late(3, lambda piece: line.spread_onward(piece, 1))
        late(6, lambda piece: [line.spread_onward(piece, i) for i in range(3, count)])
        pl.when(step == 5)(gather.second)
        pl.when(step == 7)(output_gather.second)
        pl.when(step == 9)(output_gather.third)

    own_height = height // count
    for piece in range(PIECES):
        start = pl.multiple_of(piece * height + me * own_height, own_height)
        own_tokens[piece * own_height : (piece + 1) * own_height, :] = wide[
            pl.ds(start, own_height), :
        ]

    marks.wait_arrivals()
    for i in range(1, count):
        owner = lax.rem(me - i + count, count)
        marks_out[:, pl.ds(pl.multiple_of(owner * width, width), width)] = mark_slots[i - 1]

    @pl.loop(0, PIECES)
    def _(piece):
        swap.wait_arrival(piece)
        swap.wait_sent(piece)

    output_gather.last()
    marks.wait_sent()
    gather.wait_sent()
    output_gather.wait_sent()
    line.spread_finish(PIECES, source)


def enter(
    tokens, marks, query_weight, key_weight, value_weight, output_weight, bias, collective_id
):
    count = lax.axis_size("tp")
    rows, width = tokens.shape
    head_cols = query_weight.shape[1]
    plane = 8
    part = 3 * head_cols // 2
    return pl.pallas_call(
        functools.partial(enter_kernel, count),
        out_shape=[
            jax.ShapeDtypeStruct((rows, count * width), tokens.dtype),
            jax.ShapeDtypeStruct((rows // count, count * width), tokens.dtype),
            jax.ShapeDtypeStruct((marks.shape[0], count * width), marks.dtype),
            jax.ShapeDtypeStruct((plane * query_weight.shape[0], 2 * part), query_weight.dtype),
            jax.ShapeDtypeStruct(
                (plane * output_weight.shape[0], output_weight.shape[1]), output_weight.dtype
            ),
            jax.ShapeDtypeStruct((2 * rows, part), jnp.bfloat16),
        ],
        in_specs=[
            pl.BlockSpec(memory_space=pl.ANY),
            pl.BlockSpec(memory_space=pltpu.VMEM),
            *[pl.BlockSpec(memory_space=pl.ANY)] * 4,
            pl.BlockSpec(memory_space=pltpu.VMEM),
        ],
        out_specs=[pl.BlockSpec(memory_space=pltpu.VMEM)] * 6,
        scratch_shapes=[
            pltpu.VMEM((count - 1, *marks.shape), marks.dtype),
            pltpu.VMEM((rows, part), jnp.bfloat16),
            *line_semaphores(count, PIECES)[1],
            pltpu.SemaphoreType.DMA((count - 1,)),
            pltpu.SemaphoreType.DMA((count - 1,)),
            *[pltpu.SemaphoreType.DMA((9,))] * 4,
            pltpu.SemaphoreType.DMA((PIECES,)),
            pltpu.SemaphoreType.DMA((PIECES,)),
            pltpu.SemaphoreType.DMA((8,)),
        ],
        compiler_params=pltpu.CompilerParams(
            collective_id=collective_id, has_side_effects=True, vmem_limit_bytes=60 << 20
        ),
        cost_estimate=pl.CostEstimate(
            flops=80_000_000_000, bytes_accessed=64 * rows * count * width, transcendentals=0
        ),
        name="enter",
    )(tokens, marks, query_weight, key_weight, value_weight, output_weight, bias)


def relay_kernel(count, row_step, use_step, sizes, *refs):
    row_in, use_in, row_out, use_out, shared, swap_in, swap_out, gathers, fill_step = sizes
    refs = list(refs)

    def take(number):
        taken = refs[:number]
        del refs[:number]
        return taken

    x_ref, sum_weight = take(2)
    use_weight = sum_weight if shared else take(1)[0]
    row_inputs, use_inputs = take(row_in), take(use_in)
    next_ref = take(1)[0] if gathers else None
    fill_inputs = take(1) if fill_step is not None else []
    (gathered,) = take(1)
    row_outputs, use_outputs = take(row_out), take(use_out)
    swapped = take(1)[0] if swap_in or swap_out else None
    wholes = take(2) if gathers else []
    fill_outputs = take(1) if fill_step is not None else []
    terms, total, slots, sum_sent, sum_got, spread_sent, spread_got = take(7)
    me, ctx = lax.axis_index("tp"), lax.axis_index("ctx")
    rows = gathered.shape[0]
    height = rows // PIECES
    own = height // count
    width = sum_weight.shape[0]

    def piece_rows(piece, start=0):
        return pl.ds(pl.multiple_of(start + piece * height, height), height)

    def view(piece, owner):
        return gathered.at[pl.ds(pl.multiple_of(piece * height + owner * own, own), own)]

    line = Line(me, count, slots, sum_sent, sum_got, view, spread_sent, spread_got)
    use_gather = next_gather = None
    if gathers:
        use_gather, next_gather = [PlaneGather(whole, *take(2)) for whole in wholes]
        greet(me, count, next_gather.peers())
        shards, use_weight = (use_weight, next_ref), wholes[0]
    else:
        greet(me, count, [{"ctx": 1 - ctx}] if swap_in or swap_out else [])
    swap = None
    if swap_in:
        half = x_ref.shape[1]
        own_half = pl.ds(pl.multiple_of(ctx * half, half), half)
        swap = Swap(
            *take(2),
            lambda piece: x_ref.at[piece_rows(piece, (1 - ctx) * rows)],
            lambda piece: swapped.at[piece_rows(piece), own_half],
        )

        @pl.loop(0, PIECES)
        def _(piece):
            swap.start(piece)
            swapped[piece_rows(piece), own_half] = x_ref[piece_rows(piece, ctx * rows), :]

    if gathers:
        for gather, shard in zip((use_gather, next_gather), shards, strict=True):
            gather.put(shard, take(1)[0])
        use_gather.first()
    if swap_out:
        stage, swap_sent, swap_got = take(3)
        half = swapped.shape[1]
        swap = Swap(
            swap_sent, swap_got,
            lambda piece: stage.at[piece_rows(piece)],
            lambda piece: swapped.at[piece_rows(piece, ctx * rows)],
        )

    @pl.loop(0, PIECES + 5)
    def _(step):
        odd = lax.rem(step, 2)

        def term_of(parity):
            return lambda owner: terms[parity, pl.ds(pl.multiple_of(owner * own, own), own), :]

        def late(pieces, action):
            @pl.when((step >= pieces) & (step < PIECES + pieces))
            def _():
                action(step - pieces)

        def use(piece):
            part = piece_rows(piece)
            result = use_step(part, gathered[part, :], use_weight, use_inputs, use_outputs)
            if swap_out:
                here = ctx == 0
                left, right = result[:, :half], result[:, half:]
                stage[part, :] = jnp.where(here, right, left)
                swap.start(piece)
                swapped[piece_rows(piece, ctx * rows), :] = jnp.where(here, left, right)

        def form(piece):
            if swap_in:
                swap.wait_arrival(piece)
            x = (swapped if swap_in else x_ref)[piece_rows(piece), :]

            @pl.loop(0, width // TILE)
            def _(tile):
                part = pl.ds(pl.multiple_of(tile * TILE, TILE), TILE)
                terms[odd, :, part] = dot_cols(x, sum_weight[part, :])

            line.sum_start(piece, term_of(odd))

        def own_step(piece):
            total[...] = terms[1 - odd, pl.ds(pl.multiple_of(me * own, own), own), :]
            line.sum_end(piece, total)
            view(piece, me)[...] = row_step(piece, total, row_inputs, row_outputs)
            line.spread_start(piece)

        def far_shards(piece):
            for distance in range(3, count):
                line.spread_onward(piece, distance)

        if gathers:
            pl.when(step == 5)(use_gather.last)
        late(5, use)
        late(3, lambda piece: line.spread_onward(piece, 2))
        late(1, lambda piece: line.sum_onward(piece, term_of(1 - odd), [1]))
        late(0, form)
        late(4, far_shards)
        late(2, lambda piece: line.spread_onward(piece, 1))
        if fill_step is not None:
            late(0, lambda piece: fill_step(piece, x_ref, fill_inputs, fill_outputs))
        late(0, lambda piece: line.sum_onward(piece, term_of(odd), range(count - 2, 1, -1)))
        late(1, own_step)
        if gathers:

            @pl.when(step == 3)
            def _():
                use_gather.second()
                next_gather.first()

            pl.when(step == 4)(use_gather.third)
            pl.when(step == 6)(next_gather.second)
            pl.when(step == 8)(next_gather.third)

    if swap is not None:

        @pl.loop(0, PIECES)
        def _(piece):
            if swap_out:
                swap.wait_arrival(piece)
            swap.wait_sent(piece)

    if gathers:
        next_gather.last()
        use_gather.wait_sent()
        next_gather.wait_sent()
    line.sum_finish(PIECES)
    line.spread_finish(PIECES)


def relay(
    x, sum_weight, use_weight, row_inputs, row_step, row_shapes, use_inputs, use_step, use_shapes,
    collective_id, name, rows, swap_in=None, swap_out=None, next_shard=None, fill=None,
):
    count = lax.axis_size("tp")
    width = sum_weight.shape[0]
    height = rows // PIECES
    own = height // count
    shared = use_weight is None
    operands = [x, sum_weight, *([] if shared else [use_weight]), *row_inputs, *use_inputs]
    in_specs = [pl.BlockSpec(memory_space=pltpu.VMEM)] * len(operands)
    shapes = [jax.ShapeDtypeStruct((rows, width), jnp.bfloat16), *row_shapes, *use_shapes]
    shapes += [shape for shape in (swap_in, swap_out) if shape is not None]
    out_specs = [pl.BlockSpec(memory_space=pltpu.VMEM)] * len(shapes)
    extra, last = [], []
    if next_shard is not None:
        operands.append(next_shard)
        in_specs.append(pl.BlockSpec(memory_space=pltpu.VMEM))
        for shard, space in ((use_weight, pltpu.VMEM), (next_shard, pl.ANY)):
            whole = (8 * shard.shape[0], shard.shape[1])
            shapes.append(jax.ShapeDtypeStruct(whole, shard.dtype))
            out_specs.append(pl.BlockSpec(memory_space=space))
        extra = [pltpu.SemaphoreType.DMA((9,))] * 4
        last = [pltpu.SemaphoreType.DMA] * 2
    fill_step = None
    if fill is not None:
        fill_step, fill_input, fill_shape = fill
        operands.append(fill_input)
        in_specs.append(pl.BlockSpec(memory_space=pltpu.VMEM))
        shapes.append(fill_shape)
        out_specs.append(pl.BlockSpec(memory_space=pltpu.VMEM))
    sums, spreads = line_semaphores(count, PIECES)
    swaps = []
    if swap_out is not None:
        swaps.append(pltpu.VMEM((rows, swap_out.shape[1]), swap_out.dtype))
    if swap_in is not None or swap_out is not None:
        swaps += [pltpu.SemaphoreType.DMA((PIECES,))] * 2
    sizes = (
        len(row_inputs), len(use_inputs), len(row_shapes), len(use_shapes), shared,
        swap_in is not None, swap_out is not None, next_shard is not None, fill_step,
    )
    return pl.pallas_call(
        functools.partial(relay_kernel, count, row_step, use_step, sizes),
        out_shape=shapes,
        in_specs=in_specs,
        out_specs=out_specs,
        scratch_shapes=[
            pltpu.VMEM((2, height, width), jnp.float32),
            pltpu.VMEM((own, width), jnp.float32),
            pltpu.VMEM((PIECES, count + 1, own, width), jnp.bfloat16),
            *sums,
            *spreads,
            *extra,
            *swaps,
            *last,
        ],
        compiler_params=pltpu.CompilerParams(
            collective_id=collective_id, has_side_effects=True, vmem_limit_bytes=60 << 20
        ),
        cost_estimate=pl.CostEstimate(
            flops=100_000_000_000, bytes_accessed=64 * rows * width, transcendentals=0
        ),
        name=name,
    )(*operands)


def own_rows_of(piece, like):
    own = like.shape[0] // PIECES
    return pl.ds(pl.multiple_of(piece * own, own), own)


def first_norm_step(piece, total, inputs, outputs):
    tokens, gains, biases = inputs
    first_norm, normed_one, inverse_one = outputs
    part = own_rows_of(piece, tokens)
    summed = tokens[part, :].astype(jnp.float32) + (total[...] + biases[0:1, :])
    normed, inverse = norm_parts(summed)
    result = normed * gains[0:1, :] + biases[1:2, :]
    first_norm[part, :] = result
    normed_one[part, :] = normed
    inverse_one[part, :] = jnp.broadcast_to(inverse, (inverse.shape[0], 128))
    return result.astype(jnp.bfloat16)


def expand_step(rows, chunk, weight, inputs, outputs):
    (bias,) = inputs
    hidden, activated = outputs

    @pl.loop(0, hidden.shape[1] // TILE)
    def _(tile):
        part = pl.ds(pl.multiple_of(tile * TILE, TILE), TILE)
        values = dot_plain(chunk, weight[:, part]) + bias[:, part]
        hidden[rows, part] = values
        activated[rows, part] = gelu_tanh(values).astype(jnp.bfloat16)


def add_sums(piece, sums, *values):
    @pl.when(piece == 0)
    def _():
        sums[...] = jnp.zeros_like(sums)

    for i, value in enumerate(values):
        sums[i : i + 1, :] += jnp.sum(value, axis=0, keepdims=True)


def second_norm_step(piece, total, inputs, outputs):
    first_norm, out_grad, gains, biases = inputs
    mixed, grad_second, sums = outputs
    part = own_rows_of(piece, first_norm)
    normed, inverse = norm_parts(first_norm[part, :] + total[...] + biases[2:3, :])
    result = (normed * gains[1:2, :] + biases[3:4, :]).astype(jnp.bfloat16)
    count, _, width = mixed.shape
    for i in range(count):
        mixed[i, part, :] = result[:, i * width : (i + 1) * width]
    upstream = jnp.concatenate([out_grad[i, part, :] for i in range(count)], axis=1)
    upstream = upstream.astype(jnp.float32)
    grad = norm_back(upstream, normed, inverse, gains[1:2, :])
    grad_second[part, :] = grad
    low = grad.astype(jnp.bfloat16)
    add_sums(piece, sums, upstream * normed, upstream, low.astype(jnp.float32))
    return low


def gelu_slope(values):
    scale = math.sqrt(2.0 / math.pi)
    square = values * values
    bend = jnp.tanh(scale * values * (1.0 + 0.044715 * square))
    inner = scale * (1.0 + 3 * 0.044715 * square)
    return 0.5 * (1.0 + bend) + 0.5 * values * (1.0 - bend * bend) * inner


def shrink_step(rows, chunk, weight, inputs, outputs):
    (hidden,) = inputs
    hidden_low, sums = outputs

    @pl.when(rows.start == 0)
    def _():
        sums[...] = jnp.zeros_like(sums)

    @pl.loop(0, hidden.shape[1] // TILE)
    def _(tile):
        part = pl.ds(pl.multiple_of(tile * TILE, TILE), TILE)
        grad = dot_plain(chunk, weight[:, part]) * gelu_slope(hidden[rows, part])
        low = grad.astype(jnp.bfloat16)
        hidden_low[rows, part] = low
        sums[0:1, part] += jnp.sum(low.astype(jnp.float32), axis=0, keepdims=True)


def first_back_step(piece, total, inputs, outputs):
    grad_second, normed_one, inverse_one, gains = inputs
    grad_inner, sums = outputs
    part = own_rows_of(piece, grad_second)
    normed = normed_one[part, :]
    grad_first = grad_second[part, :] + total[...]
    grad = norm_back(grad_first, normed, inverse_one[part, 0:1], gains[0:1, :])
    grad_inner[part, :] = grad
    low = grad.astype(jnp.bfloat16)
    add_sums(piece, sums, grad_first * normed, grad_first, low.astype(jnp.float32))
    return low


def attended_step(rows, chunk, weight, inputs, outputs):
    result = dot_plain(chunk, weight[...]).astype(jnp.bfloat16)
    if outputs:
        outputs[0][rows, :] = result
    return result


def expand_product_step(piece, x, inputs, outputs):
    (norm_low,), (product,) = inputs, outputs
    height = product.shape[0] // PIECES
    part = pl.ds(pl.multiple_of(piece * height, height), height)
    left = norm_low[:, part].T

    @pl.loop(0, product.shape[1] // TILE)
    def _(tile):
        columns = pl.ds(pl.multiple_of(tile * TILE, TILE), TILE)
        product[part, columns] = dot_plain(left, x[:, columns]).astype(product.dtype)


def peers_in_plane(sizes):
    fsdp, ctx = lax.axis_index("fsdp"), lax.axis_index("ctx")
    return [
        {"fsdp": lax.rem(fsdp + i, sizes[0]), "ctx": lax.rem(ctx + j, sizes[1])}
        for i in range(sizes[0])
        for j in range(sizes[1])
        if i or j
    ]


def input_kernel(
    sizes, x_ref, weight, inner_ref, rows_ref, hidden_ref, out_ref, vectors_ref,
    term_ref, total, slots, own_vectors, tp_slots, plane_slots,
    sum_sent, sum_got, tp_sent, tp_got, plane_sent, plane_got, hooks=None,
):
    count = sizes[2]
    me = lax.axis_index("tp")
    height = x_ref.shape[0] // PIECES
    own = height // count
    width = out_ref.shape[1]
    line = Line(me, count, slots, sum_sent, sum_got, None, None, None)
    tp_peers, plane_peers = peers_along_tp(me, count), peers_in_plane(sizes)
    greet_peers(tp_peers + plane_peers)

    def own_part(index):
        return rows_ref.at[:, pl.ds(pl.multiple_of(index * width, width), width)]

    over_tp = Exchange(
        tp_peers, tp_sent, tp_got,
        lambda i: own_part(lax.rem(me + i, count)), lambda i: tp_slots.at[i],
    )
    over_plane = Exchange(
        plane_peers, plane_sent, plane_got, lambda _: own_vectors, lambda i: plane_slots.at[i]
    )
    opening, before, after, closing = hooks or (lambda *_: None,) * 4
    opening()
    over_tp.start()

    def terms(piece):
        def term(owner):
            features = pl.ds(pl.multiple_of(owner * width, width), width)
            term_ref[...] = dot_cols(
                x_ref[pl.ds(pl.multiple_of(piece * height, height), height), :],
                weight[features, :],
            )
            inner = inner_ref[pl.ds(pl.multiple_of(piece * own, own), own), features]
            term_ref[pl.ds(pl.multiple_of(me * own, own), own), :] += inner
            return term_ref[...]

        return term

    def pack():
        over_tp.wait_arrivals()
        own_vectors[0:8, :] = own_part(me)[...]
        for i in range(count - 1):
            own_vectors[0:8, :] += tp_slots[i]
        own_vectors[8:, :] = jnp.zeros_like(own_vectors[8:, :])
        hidden_rows = hidden_ref.shape[1] // width
        for i in range(hidden_rows):
            own_vectors[8 + i : 9 + i, :] = hidden_ref[0:1, i * width : (i + 1) * width]
        for i in range(x_ref.shape[1] // width):
            part = x_ref[:, i * width : (i + 1) * width].astype(jnp.float32)
            place = 8 + hidden_rows + i
            own_vectors[place : place + 1, :] = jnp.sum(part, axis=0, keepdims=True)
        over_plane.start()

    @pl.loop(0, PIECES)
    def _(piece):
        before(piece)
        line.sum_start(piece, terms(piece))
        line.sum_onward(piece, terms(piece), range(count - 2, 0, -1))
        after(piece)

    pack()
    closing()

    @pl.loop(0, PIECES)
    def _(piece):
        total[...] = terms(piece)(me)
        line.sum_end(piece, total)
        rows = pl.ds(pl.multiple_of(piece * height, height), height)
        out_ref[rows, :] = total[...].astype(out_ref.dtype)

    over_plane.wait_arrivals()
    vectors_ref[...] = own_vectors[...]
    for i in range(len(plane_peers)):
        vectors_ref[...] += plane_slots[i]
    over_tp.wait_sent()
    over_plane.wait_sent()
    line.sum_finish(PIECES)


def input_sum(x, weight, inner, row_sums, hidden_sums, collective_id):
    sizes = tuple(lax.axis_size(axis) for axis in ("fsdp", "ctx", "tp"))
    count = sizes[2]
    others = sizes[0] * sizes[1] - 1
    rows = x.shape[0]
    width = weight.shape[0] // count
    height = rows // PIECES
    packed = 8 + -(-(hidden_sums.shape[1] + x.shape[1]) // (8 * width)) * 8
    return pl.pallas_call(
        functools.partial(input_kernel, sizes),
        out_shape=[
            jax.ShapeDtypeStruct((rows, width), jnp.bfloat16),
            jax.ShapeDtypeStruct((packed, width), jnp.float32),
        ],
        in_specs=[pl.BlockSpec(memory_space=pltpu.VMEM)] * 5,
        out_specs=[pl.BlockSpec(memory_space=pltpu.VMEM)] * 2,
        scratch_shapes=[
            pltpu.VMEM((height, width), jnp.float32),
            pltpu.VMEM((height, width), jnp.float32),
            pltpu.VMEM((PIECES, count + 1, height, width), jnp.bfloat16),
            pltpu.VMEM((packed, width), jnp.float32),
            pltpu.VMEM((count - 1, 8, width), jnp.float32),
            pltpu.VMEM((others, packed, width), jnp.float32),
            *line_semaphores(count, PIECES)[0],
            pltpu.SemaphoreType.DMA((count - 1,)),
            pltpu.SemaphoreType.DMA((count - 1,)),
            pltpu.SemaphoreType.DMA((others,)),
            pltpu.SemaphoreType.DMA((others,)),
        ],
        compiler_params=pltpu.CompilerParams(
            collective_id=collective_id, has_side_effects=True, vmem_limit_bytes=40 << 20
        ),
        cost_estimate=pl.CostEstimate(
            flops=60_000_000_000, bytes_accessed=64 * rows * width, transcendentals=0
        ),
        name="input_sum",
    )(x, weight, inner, row_sums, hidden_sums)


class PlaneSum:
    def __init__(self, parts, core_slots, first_slots, last_slots, sent, got):
        self.parts, self.core_slots = parts, core_slots
        self.first_slots, self.last_slots = first_slots, last_slots
        self.sent, self.got = sent, got
        self.fsdp, self.ctx = lax.axis_index("fsdp"), lax.axis_index("ctx")
        self.twin = self.fsdp + 1 - 2 * lax.rem(self.fsdp, 2)
        self.half = parts.shape[2] // 2

    def number(self, fsdp, over_x, over_y):
        chip = lax.rem(fsdp + 2 * over_x, 4)
        return chip * 2 + (1 - self.ctx if over_y else self.ctx)

    def view(self, over_x, over_y, side):
        columns = pl.ds(side * self.half, self.half)
        return self.parts.at[self.number(self.fsdp, over_x, over_y), :, columns]

    def copy(self, number, source, place, peer):
        return pltpu.make_async_remote_copy(
            src_ref=source,
            dst_ref=place,
            send_sem=self.sent.at[number],
            recv_sem=self.got.at[number],
            device_id=peer,
            device_id_type=MESH,
        )

    def core_copy(self, number):
        over_x, over_y = number // 2, number % 2
        source = self.parts.at[self.number(self.twin, over_x, over_y)]
        return self.copy(number, source, self.core_slots.at[number], {"fsdp": self.twin})

    def x_peer(self):
        return {"fsdp": lax.rem(self.fsdp + 2, 4)}

    def y_peer(self):
        return {"ctx": 1 - self.ctx}

    def first_copy(self, number):
        slot = self.first_slots.at[number]
        if number < 2:
            return self.copy(4 + number, self.view(1, number, 0), slot, self.x_peer())
        return self.copy(4 + number, self.view(number - 2, 1, 1), slot, self.y_peer())

    def last_copy(self, side):
        slot = self.last_slots.at[side]
        if side == 0:
            return self.copy(8, self.view(0, 1, 0), slot, self.y_peer())
        return self.copy(9, self.view(1, 0, 1), slot, self.x_peer())

    def add(self, view, slot):
        total = view[...].astype(jnp.float32) + slot[...].astype(jnp.float32)
        view[...] = total.astype(view.dtype)

    def start(self):
        for number in (3, 2, 1, 0):
            self.core_copy(number).start()

    def second(self):
        for number in (3, 2, 1, 0):
            self.core_copy(number).wait_recv()
            shard = self.parts.at[self.number(self.fsdp, number // 2, number % 2)]
            self.add(shard, self.core_slots.at[number])
            if number == 3:
                self.first_copy(1).start()
                self.first_copy(3).start()
            if number == 2:
                self.first_copy(0).start()
            if number == 1:
                self.first_copy(2).start()

    def third(self):
        self.first_copy(1).wait_recv()
        self.add(self.view(0, 1, 0), self.first_slots.at[1])
        self.last_copy(0).start()
        self.first_copy(3).wait_recv()
        self.add(self.view(1, 0, 1), self.first_slots.at[3])
        self.last_copy(1).start()

    def finish(self):
        totals = []
        for side in range(2):
            number = 2 * side
            self.first_copy(number).wait_recv()
            self.last_copy(side).wait_recv()
            total = self.view(0, 0, side)[...].astype(jnp.float32)
            total += self.first_slots[number].astype(jnp.float32)
            totals.append(total + self.last_slots[side].astype(jnp.float32))
        for number in range(4):
            self.core_copy(number).wait_send()
            self.first_copy(number).wait_send()
        for side in range(2):
            self.last_copy(side).wait_send()
        return totals

    @staticmethod
    def scratch(shards, height, width):
        return [
            pltpu.VMEM((shards, height, width), jnp.bfloat16),
            pltpu.VMEM((4, height, width), jnp.bfloat16),
            pltpu.VMEM((4, height, width // 2), jnp.bfloat16),
            pltpu.VMEM((2, height, width // 2), jnp.bfloat16),
            pltpu.SemaphoreType.DMA((10,)),
            pltpu.SemaphoreType.DMA((10,)),
        ]


def leave_kernel(
    sizes, grads_ref, tokens_ref, weight, inner_ref, rows_ref, hidden_ref, branch_ref, attended_ref,
    out_ref, vectors_ref, query_out, key_out, value_out, output_out,
    x_ref, term_ref, total, slots, own_vectors, tp_slots, plane_slots,
    sum_sent, sum_got, tp_sent, tp_got, plane_sent, plane_got, swap_sent, swap_got, *sum_scratch,
):
    count = sizes[2]
    me, ctx = lax.axis_index("tp"), lax.axis_index("ctx")
    rows = x_ref.shape[0]
    height = rows // PIECES
    part = grads_ref.shape[1]
    plane_sum, output_sum = PlaneSum(*sum_scratch[:6]), PlaneSum(*sum_scratch[6:])
    shard = plane_sum.parts.shape[1]

    def piece_rows(piece, start=0):
        return pl.ds(pl.multiple_of(start + piece * height, height), height)

    own_columns = pl.ds(pl.multiple_of(ctx * part, part), part)
    swap = Swap(
        swap_sent, swap_got,
        lambda piece: grads_ref.at[piece_rows(piece, (1 - ctx) * rows)],
        lambda piece: x_ref.at[piece_rows(piece), own_columns],
    )

    def products(sums, fsdp, left, right):
        for over_x in (1, 0):
            for over_y in (1, 0):
                number = sums.number(fsdp, over_x, over_y)
                columns = pl.ds(pl.multiple_of(number * shard, shard), shard)
                sums.parts[number] = dot_rows(left[:, columns], right[...]).astype(jnp.bfloat16)

    def opening():
        @pl.loop(0, PIECES)
        def _(piece):
            swap.start(piece)

        products(output_sum, output_sum.twin, branch_ref, attended_ref)
        output_sum.start()
        x_ref[:, own_columns] = grads_ref[pl.ds(pl.multiple_of(ctx * rows, rows), rows), :]
        products(output_sum, output_sum.fsdp, branch_ref, attended_ref)
        output_sum.second()

    last = PIECES - 1
    begin = jnp.where((me == 0) | (me == count - 1), last, 2)

    def before(piece):
        @pl.when(piece <= begin)
        def _():
            swap.wait_arrival(piece)

    def after(piece):
        @pl.when(piece == begin)
        def _():
            @pl.loop(begin + 1, PIECES)
            def _(other):
                swap.wait_arrival(other)

            products(plane_sum, plane_sum.twin, tokens_ref, x_ref)
            plane_sum.start()

        @pl.when(piece == jnp.minimum(begin + 1, last))
        def _():
            products(plane_sum, plane_sum.fsdp, tokens_ref, x_ref)

        pl.when(piece == jnp.minimum(begin + 2, last))(plane_sum.second)
        pl.when(piece == jnp.minimum(begin + 3, last))(output_sum.third)

    def closing():
        plane_sum.third()

    input_kernel(
        sizes, x_ref, weight, inner_ref, rows_ref, hidden_ref, out_ref, vectors_ref,
        term_ref, total, slots, own_vectors, tp_slots, plane_slots,
        sum_sent, sum_got, tp_sent, tp_got, plane_sent, plane_got,
        hooks=(opening, before, after, closing),
    )
    halves = plane_sum.finish()
    third = part // 3
    for side, half in enumerate(halves):
        for i, ref in enumerate((query_out, key_out, value_out)):
            ref[:, side * third : (side + 1) * third] = half[:, i * third : (i + 1) * third]
    output_out[...] = jnp.concatenate(output_sum.finish(), axis=1)

    @pl.loop(0, PIECES)
    def _(piece):
        swap.wait_sent(piece)


def leave(grads, tokens, weight, inner, row_sums, hidden_sums, branch, attended, collective_id):
    sizes = tuple(lax.axis_size(axis) for axis in ("fsdp", "ctx", "tp"))
    count = sizes[2]
    others = sizes[0] * sizes[1] - 1
    rows, features = tokens.shape
    part = grads.shape[1]
    width = features // count
    height = rows // PIECES
    shard = features // (others + 1)
    packed = 8 + -(-(hidden_sums.shape[1] + 2 * part) // (8 * width)) * 8
    return pl.pallas_call(
        functools.partial(leave_kernel, sizes),
        out_shape=[
            jax.ShapeDtypeStruct((rows, width), jnp.bfloat16),
            jax.ShapeDtypeStruct((packed, width), jnp.float32),
            *[jax.ShapeDtypeStruct((shard, 2 * part // 3), jnp.float32)] * 4,
        ],
        in_specs=[pl.BlockSpec(memory_space=pltpu.VMEM)] * 8,
        out_specs=[pl.BlockSpec(memory_space=pltpu.VMEM)] * 6,
        scratch_shapes=[
            pltpu.VMEM((rows, 2 * part), jnp.bfloat16),
            pltpu.VMEM((height, width), jnp.float32),
            pltpu.VMEM((height, width), jnp.float32),
            pltpu.VMEM((PIECES, count + 1, height, width), jnp.bfloat16),
            pltpu.VMEM((packed, width), jnp.float32),
            pltpu.VMEM((count - 1, 8, width), jnp.float32),
            pltpu.VMEM((others, packed, width), jnp.float32),
            *line_semaphores(count, PIECES)[0],
            pltpu.SemaphoreType.DMA((count - 1,)),
            pltpu.SemaphoreType.DMA((count - 1,)),
            pltpu.SemaphoreType.DMA((others,)),
            pltpu.SemaphoreType.DMA((others,)),
            pltpu.SemaphoreType.DMA((PIECES,)),
            pltpu.SemaphoreType.DMA((PIECES,)),
            *PlaneSum.scratch(others + 1, shard, 2 * part),
            *PlaneSum.scratch(others + 1, shard, attended.shape[1]),
        ],
        compiler_params=pltpu.CompilerParams(
            collective_id=collective_id, has_side_effects=True, vmem_limit_bytes=60 << 20
        ),
        cost_estimate=pl.CostEstimate(
            flops=60_000_000_000, bytes_accessed=64 * rows * width, transcendentals=0
        ),
        name="leave",
    )(grads, tokens, weight, inner, row_sums, hidden_sums, branch, attended)


def to_own_rows(wide):
    count = lax.axis_size("tp")
    parts = wide.reshape(PIECES, count, -1, wide.shape[1])
    return lax.dynamic_index_in_dim(parts, lax.axis_index("tp"), 1, keepdims=False).reshape(
        -1, wide.shape[1]
    )


def spread_own(block):
    count = lax.axis_size("tp")
    rows, width = block.shape
    parts = block.reshape(PIECES, count, -1, width).transpose(1, 0, 2, 3)
    return lax.all_to_all(
        parts.reshape(count, -1, width), "tp", split_axis=0, concat_axis=0, tiled=True
    )


def unspread_own(parts):
    count, own_rows, width = parts.shape
    got = lax.all_to_all(parts, "tp", split_axis=0, concat_axis=0, tiled=True)
    return got.reshape(count, PIECES, -1, width).transpose(1, 0, 2, 3).reshape(-1, width)


def body(
    tokens,
    segments,
    query_weight,
    key_weight,
    value_weight,
    output_weight,
    expand_weight,
    shrink_weight,
    query_bias,
    value_bias,
    hidden_bias,
    norm_gains,
    row_biases,
    out_grad,
):
    rows = tokens.shape[0]
    head_cols = query_weight.shape[1]
    heads = head_cols // HD
    plane = ("fsdp", "ctx")
    plane_sizes = tuple(lax.axis_size(axis) for axis in plane)
    by_heads = plane_sizes == (4, 2) and heads % 2 == 0

    def weight_rows(weight):
        return lax.all_gather(weight, plane, axis=0, tiled=True)

    marks = jnp.concatenate(
        [norm_gains, row_biases, jnp.zeros((10, norm_gains.shape[1]), norm_gains.dtype)]
    )
    block_index = lax.axis_index("fsdp") * plane_sizes[1] + lax.axis_index("ctx")
    qkv_bias = jnp.stack([query_bias, jnp.zeros_like(query_bias), value_bias])
    qkv_bias = qkv_bias.astype(jnp.float32)
    if by_heads:
        half_bias = qkv_bias.reshape(3, 2, -1).transpose(1, 0, 2).reshape(1, -1)
        wide_tokens, own_tokens, wide_marks, wide_qkv, full_output, qkv_heads = enter(
            tokens, marks, query_weight, key_weight, value_weight, output_weight, half_bias, 0
        )
        queries = keys = values = qkv_heads
        own_heads = heads // 2
        bounds = (segments.reshape(-1, plane_sizes[1] * rows),)
    else:
        wide_qkv = weight_rows(jnp.concatenate([query_weight, key_weight, value_weight], axis=1))
        wide_tokens, wide_marks = gather_features(tokens, marks, 0)
        own_tokens = to_own_rows(wide_tokens)
        qkv = dot_plain(wide_tokens, wide_qkv) + qkv_bias.reshape(1, -1)
        queries, keys, values = jnp.split(qkv.astype(jnp.bfloat16), 3, axis=1)
        own_heads = heads
        keys, values = padded(keys, WIN), padded(values, WIN)
        ids = jnp.concatenate(
            [
                jnp.full((WIN,), -1, jnp.int32),
                segments,
                jnp.full((WIN,), jnp.iinfo(jnp.int32).max, jnp.int32),
            ]
        )
        full_output, full_expand = weight_rows(output_weight), weight_rows(expand_weight)
        key_ids = lax.dynamic_slice_in_dim(ids, block_index * rows, rows + 2 * WIN, 0)
        bounds = key_bounds(key_ids[WIN : WIN + rows], key_ids, WIN)
    places = (0, own_heads, 2 * own_heads) if by_heads else (0, 0, 0)
    gains = wide_marks[:2].astype(jnp.float32)
    biases = wide_marks[2:6].astype(jnp.float32)
    wide_marks, out_grad = lax.optimization_barrier((wide_marks, out_grad))
    upstream = spread_own(out_grad)
    attended_heads, lse = attend(queries, keys, values, own_heads, bounds, places)
    attended_heads, upstream = lax.optimization_barrier((attended_heads, upstream))

    own_rows, features = own_tokens.shape
    hidden_cols = expand_weight.shape[1]

    def shape(extent, kind=jnp.float32):
        return jax.ShapeDtypeStruct(extent, kind)

    own_shape = shape((own_rows, features))
    norm_low, first_norm, normed_one, inverse_one, hidden, activated, *more = relay(
        attended_heads, full_output, expand_weight if by_heads else full_expand,
        [own_tokens, gains, biases], first_norm_step,
        [own_shape, own_shape, shape((own_rows, 128))],
        [hidden_bias.astype(jnp.float32)[None]], expand_step,
        [shape((rows, hidden_cols)), shape((rows, hidden_cols), jnp.bfloat16)],
        1, "first_norm", rows,
        swap_in=shape((rows, head_cols), jnp.bfloat16) if by_heads else None,
        next_shard=shrink_weight if by_heads else None,
    )
    if by_heads:
        attended, full_expand, full_shrink = more
    else:
        attended, full_shrink = attended_heads, weight_rows(shrink_weight)
    ffn_low, mixed_own, grad_second, second_sums, hidden_low, hidden_sums = relay(
        activated, full_shrink, None,
        [first_norm, upstream, gains, biases], second_norm_step,
        [shape(upstream.shape, jnp.bfloat16), own_shape, shape((8, features))],
        [hidden], shrink_step,
        [shape((rows, hidden_cols), jnp.bfloat16), shape((8, hidden_cols))],
        2, "second_norm", rows,
    )

    def owner_sum(grad):
        return lax.psum_scatter(
            grad, plane, scatter_dimension=0, tiled=True
        )

    hidden_low, shrink_part = lax.optimization_barrier(
        (hidden_low, dot_rows(ffn_low, activated).astype(jnp.bfloat16))
    )
    shrink_grad = owner_sum(shrink_part)
    branch_low, grad_inner, first_sums, attended_grad, expand_part = relay(
        hidden_low, full_expand, full_output,
        [grad_second, normed_one, inverse_one, gains], first_back_step,
        [own_shape, shape((8, features))],
        [], attended_step,
        [] if by_heads else [shape((rows, head_cols), jnp.bfloat16)],
        3, "first_back", rows,
        swap_out=shape((2 * rows, head_cols // 2), jnp.bfloat16) if by_heads else None,
        fill=(expand_product_step, norm_low, shape((features, hidden_cols), jnp.bfloat16)),
    )
    expand_grad = owner_sum(expand_part)
    attended_grad, mixed_own, shrink_grad = lax.optimization_barrier(
        (attended_grad, mixed_own, shrink_grad)
    )
    mixed = unspread_own(mixed_own)

    if by_heads:
        (grads,) = attend_back(
            queries, keys, values, attended_heads, attended_grad, lse, bounds, places, True
        )
        grads, mixed = lax.optimization_barrier((grads, mixed))
    else:
        query_low, key_ext, value_ext = attend_back(
            queries, keys, values, attended_heads, attended_grad, lse, bounds
        )

        def fold(ext):
            edges = jnp.concatenate([ext[:WIN], ext[WIN + rows :]], axis=0)
            around = padded(edges, WIN)
            own = ext[WIN : WIN + rows]
            own = own.at[:WIN].add(around[:WIN]).at[rows - WIN :].add(around[3 * WIN :])
            return own.astype(jnp.bfloat16)

        qkv_low = jnp.concatenate([query_low, fold(key_ext), fold(value_ext)], axis=1)
    row_sums = jnp.concatenate(
        [
            first_sums[0:1], second_sums[0:1],
            first_sums[2:3], first_sums[1:2], second_sums[2:3], second_sums[1:2],
            jnp.zeros_like(first_sums[:2]),
        ]
    )
    sides = 2 if by_heads else 1

    def by_kind(columns):
        parts = columns.reshape(-1, sides, 3, head_cols // sides)
        return [parts[:, :, i].reshape(-1, head_cols) for i in range(3)]

    if by_heads:
        input_grad, vectors, query_grad, key_grad, value_grad, output_grad = leave(
            grads, wide_tokens, wide_qkv, grad_inner, row_sums, hidden_sums[:1], branch_low,
            attended, 4,
        )
        input_grad, expand_grad = lax.optimization_barrier((input_grad, expand_grad))
    else:
        input_grad, vectors = input_sum(
            qkv_low, wide_qkv, grad_inner, row_sums, hidden_sums[:1], 4
        )
        output_grad = owner_sum(dot_rows(branch_low, attended).astype(jnp.bfloat16))
        qkv_grad = owner_sum(dot_rows(wide_tokens, qkv_low).astype(jnp.bfloat16))
        query_grad, key_grad, value_grad = by_kind(qkv_grad.astype(jnp.float32))
    hidden_rows = hidden_cols // head_cols
    query_sum, _, value_sum = by_kind(
        vectors[8 + hidden_rows : 8 + hidden_rows + 3].reshape(1, -1)
    )
    return (
        mixed,
        input_grad,
        query_grad,
        key_grad,
        value_grad,
        output_grad.astype(jnp.float32),
        expand_grad.astype(jnp.float32),
        shrink_grad.astype(jnp.float32),
        query_sum[0],
        value_sum[0],
        vectors[8 : 8 + hidden_rows].reshape(-1),
        vectors[:2],
        vectors[2:6],
    )


def solution(mesh):
    rows, whole, cols = P(("fsdp", "ctx"), "tp"), P(), P("tp")
    wide = P(None, "tp")
    return jax.shard_map(
        body,
        mesh=mesh,
        in_specs=(rows, whole) + (rows,) * 6 + (cols,) * 3 + (wide,) * 2 + (rows,),
        out_specs=(rows,) * 8 + (cols,) * 3 + (wide,) * 2,
        check_vma=False,
    )
```

```python
import functools
import math

import jax
import jax.numpy as jnp
from jax import lax
from jax.experimental import pallas as pl
from jax.experimental.pallas import tpu as pltpu
from jax.sharding import PartitionSpec as P

HD = 128
WIN = 1024
QB = 512
KB = 512

epsilon = 1e-06
hidden_floor = -1e30
score_scale = 1.0 / math.sqrt(HD)
log2_e = 1.0 / math.log(2.0)


def dot_plain(left, right):
    return jnp.dot(left, right, preferred_element_type=jnp.float32)


def dot_rows(left, right):
    return lax.dot_general(
        left, right, (((0,), (0,)), ((), ())), preferred_element_type=jnp.float32
    )


def dot_cols(left, right):
    return lax.dot_general(
        left, right, (((1,), (1,)), ((), ())), preferred_element_type=jnp.float32
    )


def block_bounds(block, rows, bounds, marks):
    if len(bounds) == 4:
        first, last, low, high = bounds
        return first[block], last[block], low[...], high[...]
    (ids,) = bounds
    run = ids.shape[1]

    @pl.when((pl.program_id(0) == 0) & (block == 0))
    def _():
        own = lax.axis_index("fsdp")
        own_ids = ids[pl.ds(own, 1), :]
        for i in range(2):
            marks[i] = jnp.sum((own_ids <= 3 * own + i).astype(jnp.int32))

    second, third = marks[0], marks[1]

    def bounds_at(places):
        start = jnp.where(places < second, 0, jnp.where(places < third, second, third))
        stop = jnp.where(places < second, second, jnp.where(places < third, third, run))
        return jnp.maximum(start, places - WIN), jnp.minimum(stop - 1, places + WIN)

    begin = block * rows
    low, high = bounds_at(begin + lax.broadcasted_iota(jnp.int32, (1, rows), 1))
    return bounds_at(begin)[0] // KB, bounds_at(begin + rows - 1)[1] // KB + 1, low, high


def bound_operands(bounds):
    if len(bounds) == 4:
        mark_spec = pl.BlockSpec((1, QB), lambda h, i, *_: (0, i))
        return list(bounds[:2]), list(bounds[2:]), [mark_spec, mark_spec]
    shape = bounds[0].shape
    return [], list(bounds), [pl.BlockSpec(shape, lambda h, i, *_: (0, 0))]


def attend_kernel(scalars, *refs):
    bounds = refs[:scalars]
    q_ref, k_ref, v_ref, *arrays, out_ref, lse_ref, vt, marks = refs[scalars:]
    block = pl.program_id(1)
    rows = q_ref.shape[0]

    @pl.when(block == 0)
    def _():
        vt[...] = v_ref[...].T

    queries = q_ref[...]
    first, last, low, high = block_bounds(block, rows, (*bounds, *arrays), marks)
    places = lax.broadcasted_iota(jnp.int32, (KB, rows), 0)

    def step(number, carry):
        top, total, mixed = carry
        start = pl.multiple_of(number * KB, KB)
        scores = dot_cols(k_ref[pl.ds(start, KB), :], queries) * (score_scale * log2_e)
        keep = (places >= low - start) & (places <= high - start)
        scores = jnp.where(keep, scores, hidden_floor)
        new_top = jnp.maximum(top, jnp.max(scores, axis=0, keepdims=True))
        shrink = jnp.exp2(top - new_top)
        powers = jnp.exp2(scores - new_top)
        total = total * shrink + jnp.sum(powers, axis=0, keepdims=True)
        mixed = mixed * shrink + dot_plain(vt[:, pl.ds(start, KB)], powers.astype(jnp.bfloat16))
        return new_top, total, mixed

    top, total, mixed = lax.fori_loop(
        first,
        last,
        step,
        (
            jnp.full((1, rows), hidden_floor, jnp.float32),
            jnp.zeros((1, rows), jnp.float32),
            jnp.zeros((HD, rows), jnp.float32),
        ),
    )
    out_ref[...] = (mixed / total).T.astype(out_ref.dtype)
    lse_ref[...] = (top + jnp.log2(total))[None]


def attend(queries, keys, values, heads, bounds, places=(0, 0, 0)):
    rows, span = queries.shape[0], keys.shape[0]
    width = heads * HD
    q_at, k_at, v_at = places
    scalars, arrays, specs = bound_operands(bounds)
    return pl.pallas_call(
        functools.partial(attend_kernel, len(scalars)),
        out_shape=(
            jax.ShapeDtypeStruct((rows, width), jnp.bfloat16),
            jax.ShapeDtypeStruct((heads, 1, rows), jnp.float32),
        ),
        grid_spec=pltpu.PrefetchScalarGridSpec(
            num_scalar_prefetch=len(scalars),
            grid=(heads, rows // QB),
            in_specs=[
                pl.BlockSpec((QB, HD), lambda h, i, *_: (i, h + q_at)),
                pl.BlockSpec((span, HD), lambda h, i, *_: (0, h + k_at)),
                pl.BlockSpec((span, HD), lambda h, i, *_: (0, h + v_at)),
                *specs,
            ],
            out_specs=[
                pl.BlockSpec((QB, HD), lambda h, i, *_: (i, h)),
                pl.BlockSpec((1, 1, QB), lambda h, i, *_: (h, 0, i)),
            ],
            scratch_shapes=[pltpu.VMEM((HD, span), jnp.bfloat16), pltpu.SMEM((2,), jnp.int32)],
        ),
        compiler_params=pltpu.CompilerParams(vmem_limit_bytes=32 << 20),
        cost_estimate=pl.CostEstimate(
            flops=3 * rows * span * width,
            bytes_accessed=2 * (2 * rows + 2 * span) * width,
            transcendentals=rows * span * heads,
        ),
        name="attend",
    )(*scalars, queries, keys, values, *arrays)


def attend_back_kernel(scalars, arrays, *refs):
    bounds = refs[:scalars]
    q_ref, k_ref, v_ref, o_ref, g_ref, lse_ref, *refs = refs[scalars:]
    bounds = (*bounds, *refs[:arrays])
    *results, kt, dk_sum, dv_sum, marks = refs[arrays:]
    head, block = pl.program_id(0), pl.program_id(1)
    rows = q_ref.shape[0]

    @pl.when(block == 0)
    def _():
        kt[...] = k_ref[...].T
        dk_sum[...] = jnp.zeros_like(dk_sum)
        dv_sum[...] = jnp.zeros_like(dv_sum)

    queries = q_ref[...]
    upstream = g_ref[...]
    lse = lse_ref[0]
    first, last, low, high = block_bounds(block, rows, bounds, marks)
    places = lax.broadcasted_iota(jnp.int32, (KB, rows), 0)
    product = upstream.astype(jnp.float32) * o_ref[...].astype(jnp.float32)
    delta = jnp.sum(product.T, axis=0, keepdims=True)

    def step(number, dq):
        start = pl.multiple_of(number * KB, KB)
        window = pl.ds(start, KB)
        scores = dot_cols(k_ref[window, :], queries) * (score_scale * log2_e)
        keep = (places >= low - start) & (places <= high - start)
        probs = jnp.exp2(jnp.where(keep, scores - lse, hidden_floor))
        prob_grad = dot_cols(v_ref[window, :], upstream)
        score_grad = (probs * (prob_grad - delta)).astype(jnp.bfloat16)
        dv_sum[window, :] += dot_plain(probs.astype(jnp.bfloat16), upstream)
        dk_sum[window, :] += dot_plain(score_grad, queries)
        return dq + dot_plain(kt[:, window], score_grad)

    dq = lax.fori_loop(first, last, step, jnp.zeros((HD, rows), jnp.float32))
    dq = (dq * score_scale).T
    if len(results) == 1:
        width = results[0].shape[1] // 3

        def place(part):
            start = pl.multiple_of(part * width + head * HD, HD)
            return results[0].at[:, pl.ds(start, HD)]

        query_place = place(0).at[pl.ds(pl.multiple_of(block * rows, rows), rows)]
        key_place, value_place = place(1), place(2)
    else:
        query_place, key_place, value_place = results
    query_place[...] = dq.astype(query_place.dtype)

    @pl.when(block == pl.num_programs(1) - 1)
    def _():
        key_place[...] = (dk_sum[...] * score_scale).astype(key_place.dtype)
        value_place[...] = dv_sum[...].astype(value_place.dtype)


def attend_back(
    queries, keys, values, out, upstream, lse, bounds, places=(0, 0, 0), merged=False
):
    rows, width = out.shape
    span = keys.shape[0]
    heads = width // HD
    q_at, k_at, v_at = places
    row_spec = pl.BlockSpec((QB, HD), lambda h, i, *_: (i, h))
    key_spec = pl.BlockSpec((span, HD), lambda h, i, *_: (0, h))
    scalars, arrays, specs = bound_operands(bounds)
    return pl.pallas_call(
        functools.partial(attend_back_kernel, len(scalars), len(arrays)),
        out_shape=[jax.ShapeDtypeStruct((rows, 3 * width), jnp.bfloat16)]
        if merged
        else [
            jax.ShapeDtypeStruct((rows, width), jnp.bfloat16),
            jax.ShapeDtypeStruct((span, width), jnp.float32),
            jax.ShapeDtypeStruct((span, width), jnp.float32),
        ],
        grid_spec=pltpu.PrefetchScalarGridSpec(
            num_scalar_prefetch=len(scalars),
            grid=(heads, rows // QB),
            in_specs=[
                pl.BlockSpec((QB, HD), lambda h, i, *_: (i, h + q_at)),
                pl.BlockSpec((span, HD), lambda h, i, *_: (0, h + k_at)),
                pl.BlockSpec((span, HD), lambda h, i, *_: (0, h + v_at)),
                row_spec, row_spec,
                pl.BlockSpec((1, 1, QB), lambda h, i, *_: (h, 0, i)),
                *specs,
            ],
            out_specs=[pl.BlockSpec((rows, 3 * width), lambda h, i, *_: (0, 0))]
            if merged
            else [row_spec, key_spec, key_spec],
            scratch_shapes=[
                pltpu.VMEM((HD, span), jnp.bfloat16),
                pltpu.VMEM((span, HD), jnp.float32),
                pltpu.VMEM((span, HD), jnp.float32),
                pltpu.SMEM((2,), jnp.int32),
            ],
        ),
        compiler_params=pltpu.CompilerParams(vmem_limit_bytes=32 << 20),
        cost_estimate=pl.CostEstimate(
            flops=8 * rows * span * width,
            bytes_accessed=2 * (4 * rows + 4 * span) * width,
            transcendentals=rows * span * heads,
        ),
        name="attend_back",
    )(*scalars, queries, keys, values, out, upstream, lse, *arrays)


def key_bounds(query_ids, key_ids, offset):
    rows, span = query_ids.shape[0], key_ids.shape[0]
    start = jnp.sum(key_ids[:, None] < query_ids[None, :], axis=0, dtype=jnp.int32)
    stop = jnp.sum(key_ids[:, None] <= query_ids[None, :], axis=0, dtype=jnp.int32)
    places = jnp.arange(rows, dtype=jnp.int32) + offset
    low = jnp.maximum(start, places - WIN)
    high = jnp.minimum(stop - 1, places + WIN)
    first = jnp.min(low.reshape(-1, QB), axis=1) // KB
    last = jnp.max(high.reshape(-1, QB), axis=1) // KB + 1
    return first, last, low[None], high[None]


def padded(block, width):
    count = lax.axis_size("ctx")
    forward = [(i, i + 1) for i in range(count - 1)]
    backward = [(target, source) for source, target in forward]
    below = lax.ppermute(block[block.shape[0] - width :], "ctx", forward)
    above = lax.ppermute(block[:width], "ctx", backward)
    return jnp.concatenate([below, block, above], axis=0)


def norm_parts(rows):
    mean = jnp.mean(rows, axis=-1, keepdims=True)
    square = jnp.mean(rows * rows, axis=-1, keepdims=True)
    inverse = lax.rsqrt(square - mean * mean + epsilon)
    return (rows - mean) * inverse, inverse


def norm_back(upstream, normed, inverse, gain):
    scaled = upstream * gain
    first_mean = jnp.mean(scaled, axis=-1, keepdims=True)
    second_mean = jnp.mean(scaled * normed, axis=-1, keepdims=True)
    return inverse * (scaled - first_mean - normed * second_mean)


def gelu_tanh(values):
    return jax.nn.gelu(values, approximate=True)


MESH = pl.DeviceIdType.MESH
PIECES = 8
TILE = 512


def greet(me, count, others=()):
    barrier = pltpu.get_barrier_semaphore()

    @pl.when(me > 0)
    def _():
        pl.semaphore_signal(barrier, inc=1, device_id={"tp": me - 1}, device_id_type=MESH)

    @pl.when(me < count - 1)
    def _():
        pl.semaphore_signal(barrier, inc=1, device_id={"tp": me + 1}, device_id_type=MESH)

    for other in others:
        pl.semaphore_signal(barrier, inc=1, device_id=other, device_id_type=MESH)

    @pl.when((me == 0) | (me == count - 1))
    def _():
        pl.semaphore_wait(barrier, 1 + len(others))

    @pl.when((me > 0) & (me < count - 1))
    def _():
        pl.semaphore_wait(barrier, 2 + len(others))


def peers_along_tp(me, count):
    return [{"tp": lax.rem(me + i, count)} for i in range(1, count)]


def greet_peers(peers):
    barrier = pltpu.get_barrier_semaphore()
    for peer in peers:
        pl.semaphore_signal(barrier, inc=1, device_id=peer, device_id_type=MESH)
    pl.semaphore_wait(barrier, len(peers))


class Exchange:
    def __init__(self, peers, sent, got, source, place):
        self.peers, self.sent, self.got = peers, sent, got
        self.source, self.place = source, place

    def copies(self):
        for i, peer in enumerate(self.peers):
            yield pltpu.make_async_remote_copy(
                src_ref=self.source(i + 1),
                dst_ref=self.place(i),
                send_sem=self.sent.at[i],
                recv_sem=self.got.at[i],
                device_id=peer,
                device_id_type=MESH,
            )

    def start(self):
        for copy in self.copies():
            copy.start()

    def wait_arrivals(self):
        for copy in self.copies():
            copy.wait_recv()

    def wait_sent(self):
        for copy in self.copies():
            copy.wait_send()


def at_distance(me, count, distance, action):
    for index in (me - distance, me + distance):

        @pl.when((index >= 0) & (index < count))
        def _(index=index):
            action(index)


class Line:
    def __init__(self, me, count, sum_slots, sum_sent, sum_got, spread_view, spread_sent, spread_got):
        self.me, self.count = me, count
        self.sum_slots, self.sum_sent, self.sum_got = sum_slots, sum_sent, sum_got
        self.spread_view, self.spread_sent, self.spread_got = spread_view, spread_sent, spread_got

    def slot(self, piece):
        return lax.rem(piece, self.sum_slots.shape[0])

    def sum_copy(self, piece, owner):
        onward = jnp.where(owner > self.me, self.me + 1, self.me - 1)
        place = jnp.where((owner < self.me) & (owner == self.me - 1), self.count, owner)
        slot = self.slot(piece)
        return pltpu.make_async_remote_copy(
            src_ref=self.sum_slots.at[slot, owner],
            dst_ref=self.sum_slots.at[slot, place],
            send_sem=self.sum_sent.at[slot, owner],
            recv_sem=self.sum_got.at[slot, place],
            device_id={"tp": onward},
            device_id_type=MESH,
        )

    def sum_arrival(self, piece, place):
        view = self.sum_slots.at[self.slot(piece), place]
        pltpu.make_async_copy(view, view, self.sum_got.at[self.slot(piece), place]).wait()

    def sum_start(self, piece, term):
        me, count = self.me, self.count

        @pl.when((me == 0) | (me == count - 1))
        def _():
            for k in range(count - 1):
                owner = jnp.where(me == 0, count - 1 - k, k)
                self.sum_slots[self.slot(piece), owner] = term(owner).astype(jnp.bfloat16)
                self.sum_copy(piece, owner).start()

    def sum_onward(self, piece, term, distances):
        me, count = self.me, self.count

        @pl.when((me > 0) & (me < count - 1))
        def _():
            for distance in distances:

                def pass_on(owner):
                    self.sum_arrival(piece, owner)
                    slot = self.slot(piece)
                    total = self.sum_slots[slot, owner].astype(jnp.float32) + term(owner)
                    self.sum_slots[slot, owner] = total.astype(jnp.bfloat16)
                    self.sum_copy(piece, owner).start()

                at_distance(me, count, distance, pass_on)

    def sum_end(self, piece, total):
        me, count = self.me, self.count

        @pl.when(me > 0)
        def _():
            self.sum_arrival(piece, me)
            total[...] += self.sum_slots[self.slot(piece), me].astype(jnp.float32)

        @pl.when(me < count - 1)
        def _():
            self.sum_arrival(piece, count)
            total[...] += self.sum_slots[self.slot(piece), count].astype(jnp.float32)

    def sum_sent_all(self, piece):
        for distance in range(1, self.count):
            at_distance(
                self.me, self.count, distance,
                lambda owner: self.sum_copy(piece, owner).wait_send(),
            )

    def sum_finish(self, pieces):
        pl.loop(0, pieces)(self.sum_sent_all)

    def spread_copy(self, piece, owner, to, sent, source=None):
        return pltpu.make_async_remote_copy(
            src_ref=self.spread_view(piece, owner) if source is None else source,
            dst_ref=self.spread_view(piece, owner),
            send_sem=self.spread_sent.at[piece, sent],
            recv_sem=self.spread_got.at[piece, owner],
            device_id={"tp": to},
            device_id_type=MESH,
        )

    def own_copies(self, piece, action, source=None):
        me, count = self.me, self.count

        @pl.when(me > 0)
        def _():
            action(self.spread_copy(piece, me, me - 1, count, source))

        @pl.when(me < count - 1)
        def _():
            action(self.spread_copy(piece, me, me + 1, me, source))

    def spread_start(self, piece, source=None):
        self.own_copies(piece, lambda copy: copy.start(), source)

    def onward_copy(self, piece, owner, action):
        me, count = self.me, self.count

        @pl.when((owner < me) & (me < count - 1))
        def _():
            action(self.spread_copy(piece, owner, me + 1, owner))

        @pl.when((owner > me) & (me > 0))
        def _():
            action(self.spread_copy(piece, owner, me - 1, owner))

    def spread_onward(self, piece, distance):
        def pass_on(owner):
            view = self.spread_view(piece, owner)
            pltpu.make_async_copy(view, view, self.spread_got.at[piece, owner]).wait()
            self.onward_copy(piece, owner, lambda copy: copy.start())

        at_distance(self.me, self.count, distance, pass_on)

    def spread_finish(self, pieces, source=None):
        @pl.loop(0, pieces)
        def _(piece):
            self.own_copies(
                piece, lambda copy: copy.wait_send(), None if source is None else source(piece)
            )
            for distance in range(1, self.count):
                at_distance(
                    self.me, self.count, distance,
                    lambda owner: self.onward_copy(piece, owner, lambda copy: copy.wait_send()),
                )


def line_semaphores(count, pieces):
    return [
        pltpu.SemaphoreType.DMA((pieces, count)),
        pltpu.SemaphoreType.DMA((pieces, count + 1)),
    ], [
        pltpu.SemaphoreType.DMA((pieces, count + 1)),
        pltpu.SemaphoreType.DMA((pieces, count)),
    ]


def gather_kernel(
    count, x_ref, marks_ref, out_ref, marks_out, slots, sent, got, marks_sent, marks_got
):
    me = lax.axis_index("tp")
    height = x_ref.shape[0] // PIECES
    width = x_ref.shape[1]

    def view(piece, owner):
        return out_ref.at[
            pl.ds(pl.multiple_of(piece * height, height), height),
            pl.ds(pl.multiple_of(owner * width, width), width),
        ]

    def source(piece):
        return x_ref.at[pl.ds(pl.multiple_of(piece * height, height), height)]

    line = Line(me, count, None, None, None, view, sent, got)
    peers = peers_along_tp(me, count)
    greet_peers(peers)

    @pl.loop(0, PIECES)
    def _(piece):
        line.spread_start(piece, source(piece))

    marks = Exchange(
        peers, marks_sent, marks_got, lambda _: marks_ref, lambda i: slots.at[i]
    )
    marks.start()
    own = pl.ds(pl.multiple_of(me * width, width), width)
    out_ref[:, own] = x_ref[...]
    marks_out[:, own] = marks_ref[...]
    for distance in range(1, count):

        @pl.loop(0, PIECES)
        def _(piece, distance=distance):
            line.spread_onward(piece, distance)

    marks.wait_arrivals()
    for i in range(1, count):
        owner = lax.rem(me - i + count, count)
        marks_out[:, pl.ds(pl.multiple_of(owner * width, width), width)] = slots[i - 1]
    marks.wait_sent()
    line.spread_finish(PIECES, source)


def gather_features(x, marks, collective_id):
    count = lax.axis_size("tp")
    rows, width = x.shape
    return pl.pallas_call(
        functools.partial(gather_kernel, count),
        out_shape=[
            jax.ShapeDtypeStruct((rows, count * width), x.dtype),
            jax.ShapeDtypeStruct((marks.shape[0], count * width), marks.dtype),
        ],
        in_specs=[pl.BlockSpec(memory_space=pltpu.VMEM)] * 2,
        out_specs=[pl.BlockSpec(memory_space=pltpu.VMEM)] * 2,
        scratch_shapes=[
            pltpu.VMEM((count - 1, *marks.shape), marks.dtype),
            *line_semaphores(count, PIECES)[1],
            pltpu.SemaphoreType.DMA((count - 1,)),
            pltpu.SemaphoreType.DMA((count - 1,)),
        ],
        compiler_params=pltpu.CompilerParams(
            collective_id=collective_id, has_side_effects=True, vmem_limit_bytes=16 << 20
        ),
        cost_estimate=pl.CostEstimate(
            flops=0, bytes_accessed=64 * rows * count * width, transcendentals=0
        ),
        name="gather_features",
    )(x, marks)


class Swap:
    def __init__(self, sent, got, source, place):
        self.sent, self.got, self.source, self.place = sent, got, source, place

    def copy(self, piece):
        return pltpu.make_async_remote_copy(
            src_ref=self.source(piece),
            dst_ref=self.place(piece),
            send_sem=self.sent.at[piece],
            recv_sem=self.got.at[piece],
            device_id={"ctx": 1 - lax.axis_index("ctx")},
            device_id_type=MESH,
        )

    def start(self, piece):
        self.copy(piece).start()

    def wait_arrival(self, piece):
        self.copy(piece).wait_recv()

    def wait_sent(self, piece):
        self.copy(piece).wait_send()


class PlaneGather:
    def __init__(self, whole, sent, got):
        self.whole, self.sent, self.got = whole, sent, got
        fsdp, self.ctx = lax.axis_index("fsdp"), lax.axis_index("ctx")
        self.fsdp = fsdp
        self.twin = fsdp + 1 - 2 * lax.rem(fsdp, 2)
        self.along_x = lax.rem(fsdp + 2, 4)
        self.twin_x = lax.rem(self.twin + 2, 4)
        self.core_peer = {"fsdp": self.twin}
        self.x_peer = {"fsdp": self.along_x}
        self.y_peer = {"ctx": 1 - self.ctx}

    def peers(self):
        return [self.core_peer, self.x_peer, self.y_peer]

    def shard(self, fsdp, ctx, half=None):
        height = self.whole.shape[0] // 8
        start = (fsdp * 2 + ctx) * height
        if half is not None:
            height //= 2
            start += half * height
        return self.whole.at[pl.ds(pl.multiple_of(start, height), height)]

    def copy(self, number, view, peer):
        return pltpu.make_async_remote_copy(
            src_ref=view,
            dst_ref=view,
            send_sem=self.sent.at[number],
            recv_sem=self.got.at[number],
            device_id=peer,
            device_id_type=MESH,
        )

    def copies(self):
        own = self.shard(self.fsdp, self.ctx)
        from_x = self.shard(self.along_x, self.ctx)
        from_y = self.shard(self.fsdp, 1 - self.ctx)
        return [
            (own, self.core_peer),
            (own, self.x_peer),
            (own, self.y_peer),
            (from_x, self.core_peer),
            (self.shard(self.along_x, self.ctx, 0), self.y_peer),
            (from_y, self.core_peer),
            (self.shard(self.fsdp, 1 - self.ctx, 1), self.x_peer),
            (self.shard(self.along_x, 1 - self.ctx, 0), self.core_peer),
            (self.shard(self.along_x, 1 - self.ctx, 1), self.core_peer),
        ]

    def arrivals(self):
        return [
            self.shard(self.twin, self.ctx),
            self.shard(self.along_x, self.ctx),
            self.shard(self.fsdp, 1 - self.ctx),
            self.shard(self.twin_x, self.ctx),
            self.shard(self.along_x, 1 - self.ctx, 0),
            self.shard(self.twin, 1 - self.ctx),
            self.shard(self.along_x, 1 - self.ctx, 1),
            self.shard(self.twin_x, 1 - self.ctx, 0),
            self.shard(self.twin_x, 1 - self.ctx, 1),
        ]

    def start(self, *numbers):
        copies = self.copies()
        for number in numbers:
            self.copy(number, *copies[number]).start()

    def wait(self, *numbers):
        arrivals = self.arrivals()
        for number in numbers:
            view = arrivals[number]
            pltpu.make_async_copy(view, view, self.got.at[number]).wait()

    def first(self):
        self.start(1, 2, 0)

    def second(self):
        self.wait(1)
        self.start(4, 3)
        self.wait(2)
        self.start(6, 5)

    def third(self):
        self.wait(4)
        self.start(7)
        self.wait(6)
        self.start(8)

    def last(self):
        self.wait(0, 3, 5, 7, 8)

    def wait_sent(self):
        for number, (view, peer) in enumerate(self.copies()):
            self.copy(number, view, peer).wait_send()


def enter_kernel(
    count, x_ref, marks_ref, query_ref, key_ref, value_ref, output_ref, bias,
    wide, own_tokens, marks_out, weight, output_weight, heads,
    mark_slots, stage, sent, got, marks_sent, marks_got,
    weight_sent, weight_got, output_sent, output_got, swap_sent, swap_got, put_done,
):
    me, ctx = lax.axis_index("tp"), lax.axis_index("ctx")
    rows, width = x_ref.shape
    height = rows // PIECES
    half = query_ref.shape[1] // 2
    part = 3 * half

    def piece_rows(piece, start=0):
        return pl.ds(pl.multiple_of(start + piece * height, height), height)

    def view(piece, owner):
        return wide.at[piece_rows(piece), pl.ds(pl.multiple_of(owner * width, width), width)]

    gather = PlaneGather(weight, weight_sent, weight_got)
    output_gather = PlaneGather(output_weight, output_sent, output_got)
    own_shard = gather.shard(gather.fsdp, ctx)
    own = pl.ds(pl.multiple_of(me * width, width), width)
    puts = [
        (ref.at[:, pl.ds(side * half, half)], own_shard.at[:, pl.ds(side * part + i * half, half)])
        for side in range(2)
        for i, ref in enumerate((query_ref, key_ref, value_ref))
    ]
    puts += [
        (output_ref, output_gather.shard(gather.fsdp, ctx)),
        (x_ref, wide.at[:, own]),
    ]
    puts = [
        pltpu.make_async_copy(source, place, put_done.at[i])
        for i, (source, place) in enumerate(puts)
    ]
    for put in puts:
        put.start()
    line = Line(me, count, None, None, None, view, sent, got)
    tp_peers = peers_along_tp(me, count)
    greet_peers(tp_peers + gather.peers())

    def source(piece):
        return x_ref.at[piece_rows(piece)]

    for piece in range(2):
        line.spread_start(piece, source(piece))
    for put in puts[:7]:
        put.wait()
    gather.first()
    output_gather.first()
    marks = Exchange(
        tp_peers, marks_sent, marks_got, lambda _: marks_ref, lambda i: mark_slots.at[i]
    )
    marks.start()
    marks_out[:, own] = marks_ref[...]
    for put in puts[7:]:
        put.wait()
    swap = Swap(
        swap_sent, swap_got,
        lambda piece: stage.at[piece_rows(piece)],
        lambda piece: heads.at[piece_rows(piece, ctx * rows)],
    )

    def products(piece, side, place):
        x = wide[piece_rows(piece), :]

        @pl.loop(0, 3)
        def _(tile):
            start = pl.multiple_of(side * part + tile * half, half)
            columns = pl.ds(start, half)
            values = dot_plain(x, weight[:, columns]) + bias[:, columns]
            place[:, pl.ds(pl.multiple_of(tile * half, half), half)] = values.astype(jnp.bfloat16)

    @pl.loop(0, PIECES + 7)
    def _(step):
        def late(pieces, action, least=0):
            @pl.when((step >= pieces + least) & (step < PIECES + pieces))
            def _():
                action(step - pieces)

        def use(piece):
            products(piece, 1 - ctx, stage.at[piece_rows(piece)])
            swap.start(piece)
            products(piece, ctx, heads.at[piece_rows(piece, ctx * rows)])

        @pl.when(step == 7)
        def _():
            gather.third()
            gather.last()

        late(0, lambda piece: line.spread_start(piece, source(piece)), 2)
        late(7, use)
        late(5, lambda piece: line.spread_onward(piece, 2))
        late(3, lambda piece: line.spread_onward(piece, 1))
        late(6, lambda piece: [line.spread_onward(piece, i) for i in range(3, count)])
        pl.when(step == 5)(gather.second)
        pl.when(step == 7)(output_gather.second)
        pl.when(step == 9)(output_gather.third)

    own_height = height // count
    for piece in range(PIECES):
        start = pl.multiple_of(piece * height + me * own_height, own_height)
        own_tokens[piece * own_height : (piece + 1) * own_height, :] = wide[
            pl.ds(start, own_height), :
        ]

    marks.wait_arrivals()
    for i in range(1, count):
        owner = lax.rem(me - i + count, count)
        marks_out[:, pl.ds(pl.multiple_of(owner * width, width), width)] = mark_slots[i - 1]

    @pl.loop(0, PIECES)
    def _(piece):
        swap.wait_arrival(piece)
        swap.wait_sent(piece)

    output_gather.last()
    marks.wait_sent()
    gather.wait_sent()
    output_gather.wait_sent()
    line.spread_finish(PIECES, source)


def enter(
    tokens, marks, query_weight, key_weight, value_weight, output_weight, bias, collective_id
):
    count = lax.axis_size("tp")
    rows, width = tokens.shape
    head_cols = query_weight.shape[1]
    plane = 8
    part = 3 * head_cols // 2
    return pl.pallas_call(
        functools.partial(enter_kernel, count),
        out_shape=[
            jax.ShapeDtypeStruct((rows, count * width), tokens.dtype),
            jax.ShapeDtypeStruct((rows // count, count * width), tokens.dtype),
            jax.ShapeDtypeStruct((marks.shape[0], count * width), marks.dtype),
            jax.ShapeDtypeStruct((plane * query_weight.shape[0], 2 * part), query_weight.dtype),
            jax.ShapeDtypeStruct(
                (plane * output_weight.shape[0], output_weight.shape[1]), output_weight.dtype
            ),
            jax.ShapeDtypeStruct((2 * rows, part), jnp.bfloat16),
        ],
        in_specs=[
            pl.BlockSpec(memory_space=pl.ANY),
            pl.BlockSpec(memory_space=pltpu.VMEM),
            *[pl.BlockSpec(memory_space=pl.ANY)] * 4,
            pl.BlockSpec(memory_space=pltpu.VMEM),
        ],
        out_specs=[pl.BlockSpec(memory_space=pltpu.VMEM)] * 6,
        scratch_shapes=[
            pltpu.VMEM((count - 1, *marks.shape), marks.dtype),
            pltpu.VMEM((rows, part), jnp.bfloat16),
            *line_semaphores(count, PIECES)[1],
            pltpu.SemaphoreType.DMA((count - 1,)),
            pltpu.SemaphoreType.DMA((count - 1,)),
            *[pltpu.SemaphoreType.DMA((9,))] * 4,
            pltpu.SemaphoreType.DMA((PIECES,)),
            pltpu.SemaphoreType.DMA((PIECES,)),
            pltpu.SemaphoreType.DMA((8,)),
        ],
        compiler_params=pltpu.CompilerParams(
            collective_id=collective_id, has_side_effects=True, vmem_limit_bytes=60 << 20
        ),
        cost_estimate=pl.CostEstimate(
            flops=80_000_000_000, bytes_accessed=64 * rows * count * width, transcendentals=0
        ),
        name="enter",
    )(tokens, marks, query_weight, key_weight, value_weight, output_weight, bias)


def relay_kernel(count, row_step, use_step, sizes, *refs):
    row_in, use_in, row_out, use_out, shared = sizes
    refs = list(refs)

    def take(number):
        taken = refs[:number]
        del refs[:number]
        return taken

    x_ref, sum_weight = take(2)
    use_weight = sum_weight if shared else take(1)[0]
    row_inputs, use_inputs = take(row_in), take(use_in)
    (gathered,) = take(1)
    row_outputs, use_outputs = take(row_out), take(use_out)
    terms, total, slots, sum_sent, sum_got, spread_sent, spread_got = refs
    me = lax.axis_index("tp")
    height = x_ref.shape[0] // PIECES
    own = height // count
    width = sum_weight.shape[0]

    def piece_rows(piece):
        return pl.ds(pl.multiple_of(piece * height, height), height)

    def view(piece, owner):
        return gathered.at[pl.ds(pl.multiple_of(piece * height + owner * own, own), own)]

    line = Line(me, count, slots, sum_sent, sum_got, view, spread_sent, spread_got)
    greet(me, count)

    @pl.loop(0, PIECES + 5)
    def _(step):
        odd = lax.rem(step, 2)

        def term_of(parity):
            return lambda owner: terms[parity, pl.ds(pl.multiple_of(owner * own, own), own), :]

        def late(pieces, action):
            @pl.when((step >= pieces) & (step < PIECES + pieces))
            def _():
                action(step - pieces)

        def use(piece):
            part = piece_rows(piece)
            use_step(part, gathered[part, :], use_weight, use_inputs, use_outputs)

        def form(piece):
            x = x_ref[piece_rows(piece), :]

            @pl.loop(0, width // TILE)
            def _(tile):
                part = pl.ds(pl.multiple_of(tile * TILE, TILE), TILE)
                terms[odd, :, part] = dot_cols(x, sum_weight[part, :])

            line.sum_start(piece, term_of(odd))

        def own_step(piece):
            total[...] = terms[1 - odd, pl.ds(pl.multiple_of(me * own, own), own), :]
            line.sum_end(piece, total)
            view(piece, me)[...] = row_step(piece, total, row_inputs, row_outputs)
            line.spread_start(piece)

        late(5, use)
        late(3, lambda piece: line.spread_onward(piece, 2))
        late(1, lambda piece: line.sum_onward(piece, term_of(1 - odd), [1]))
        late(0, form)
        late(4, lambda piece: [line.spread_onward(piece, i) for i in range(3, count)])
        late(2, lambda piece: line.spread_onward(piece, 1))
        late(0, lambda piece: line.sum_onward(piece, term_of(odd), range(count - 2, 1, -1)))
        late(1, own_step)

    line.sum_finish(PIECES)
    line.spread_finish(PIECES)


def relay(
    x, sum_weight, use_weight, row_inputs, row_step, row_shapes, use_inputs, use_step, use_shapes,
    collective_id, name,
):
    count = lax.axis_size("tp")
    rows = x.shape[0]
    width = sum_weight.shape[0]
    height = rows // PIECES
    own = height // count
    shared = use_weight is None
    operands = [x, sum_weight, *([] if shared else [use_weight]), *row_inputs, *use_inputs]
    shapes = [jax.ShapeDtypeStruct((rows, width), jnp.bfloat16), *row_shapes, *use_shapes]
    sums, spreads = line_semaphores(count, PIECES)
    sizes = (len(row_inputs), len(use_inputs), len(row_shapes), len(use_shapes), shared)
    return pl.pallas_call(
        functools.partial(relay_kernel, count, row_step, use_step, sizes),
        out_shape=shapes,
        in_specs=[pl.BlockSpec(memory_space=pltpu.VMEM)] * len(operands),
        out_specs=[pl.BlockSpec(memory_space=pltpu.VMEM)] * len(shapes),
        scratch_shapes=[
            pltpu.VMEM((2, height, width), jnp.float32),
            pltpu.VMEM((own, width), jnp.float32),
            pltpu.VMEM((PIECES, count + 1, own, width), jnp.bfloat16),
            *sums,
            *spreads,
        ],
        compiler_params=pltpu.CompilerParams(
            collective_id=collective_id, has_side_effects=True, vmem_limit_bytes=60 << 20
        ),
        cost_estimate=pl.CostEstimate(
            flops=100_000_000_000, bytes_accessed=64 * rows * width, transcendentals=0
        ),
        name=name,
    )(*operands)


def own_rows_of(piece, like):
    own = like.shape[0] // PIECES
    return pl.ds(pl.multiple_of(piece * own, own), own)


def first_norm_step(piece, total, inputs, outputs):
    tokens, gains, biases = inputs
    first_norm, normed_one, inverse_one = outputs
    part = own_rows_of(piece, tokens)
    summed = tokens[part, :].astype(jnp.float32) + (total[...] + biases[0:1, :])
    normed, inverse = norm_parts(summed)
    result = normed * gains[0:1, :] + biases[1:2, :]
    first_norm[part, :] = result
    normed_one[part, :] = normed
    inverse_one[part, :] = jnp.broadcast_to(inverse, (inverse.shape[0], 128))
    return result.astype(jnp.bfloat16)


def expand_step(rows, chunk, weight, inputs, outputs):
    (bias,) = inputs
    hidden, activated = outputs

    @pl.loop(0, hidden.shape[1] // TILE)
    def _(tile):
        part = pl.ds(pl.multiple_of(tile * TILE, TILE), TILE)
        values = dot_plain(chunk, weight[:, part]) + bias[:, part]
        hidden[rows, part] = values
        activated[rows, part] = gelu_tanh(values).astype(jnp.bfloat16)


def add_sums(piece, sums, *values):
    @pl.when(piece == 0)
    def _():
        sums[...] = jnp.zeros_like(sums)

    for i, value in enumerate(values):
        sums[i : i + 1, :] += jnp.sum(value, axis=0, keepdims=True)


def second_norm_step(piece, total, inputs, outputs):
    first_norm, out_grad, gains, biases = inputs
    mixed, grad_second, sums = outputs
    part = own_rows_of(piece, first_norm)
    normed, inverse = norm_parts(first_norm[part, :] + total[...] + biases[2:3, :])
    result = (normed * gains[1:2, :] + biases[3:4, :]).astype(jnp.bfloat16)
    count, _, width = mixed.shape
    for i in range(count):
        mixed[i, part, :] = result[:, i * width : (i + 1) * width]
    upstream = jnp.concatenate([out_grad[i, part, :] for i in range(count)], axis=1)
    upstream = upstream.astype(jnp.float32)
    grad = norm_back(upstream, normed, inverse, gains[1:2, :])
    grad_second[part, :] = grad
    low = grad.astype(jnp.bfloat16)
    add_sums(piece, sums, upstream * normed, upstream, low.astype(jnp.float32))
    return low


def gelu_slope(values):
    scale = math.sqrt(2.0 / math.pi)
    square = values * values
    bend = jnp.tanh(scale * values * (1.0 + 0.044715 * square))
    inner = scale * (1.0 + 3 * 0.044715 * square)
    return 0.5 * (1.0 + bend) + 0.5 * values * (1.0 - bend * bend) * inner


def shrink_step(rows, chunk, weight, inputs, outputs):
    (hidden,) = inputs
    hidden_low, sums = outputs

    @pl.when(rows.start == 0)
    def _():
        sums[...] = jnp.zeros_like(sums)

    @pl.loop(0, hidden.shape[1] // TILE)
    def _(tile):
        part = pl.ds(pl.multiple_of(tile * TILE, TILE), TILE)
        grad = dot_plain(chunk, weight[:, part]) * gelu_slope(hidden[rows, part])
        low = grad.astype(jnp.bfloat16)
        hidden_low[rows, part] = low
        sums[0:1, part] += jnp.sum(low.astype(jnp.float32), axis=0, keepdims=True)


def first_back_step(piece, total, inputs, outputs):
    grad_second, normed_one, inverse_one, gains = inputs
    grad_inner, sums = outputs
    part = own_rows_of(piece, grad_second)
    normed = normed_one[part, :]
    grad_first = grad_second[part, :] + total[...]
    grad = norm_back(grad_first, normed, inverse_one[part, 0:1], gains[0:1, :])
    grad_inner[part, :] = grad
    low = grad.astype(jnp.bfloat16)
    add_sums(piece, sums, grad_first * normed, grad_first, low.astype(jnp.float32))
    return low


def attended_step(rows, chunk, weight, inputs, outputs):
    (attended_grad,) = outputs
    attended_grad[rows, :] = dot_plain(chunk, weight[...]).astype(jnp.bfloat16)


def middle_kernel(
    count, heads_ref, output_weight, expand_shard, shrink_shard, own_tokens, out_grad, gains,
    biases, hidden_bias,
    attended, mixed, inner, branch_out, grad_heads, first_sums, second_sums, hidden_sums,
    shrink_out, expand_out,
    expand_weight, shrink_weight, gathered, activated, slope, normed_one, inverse_one,
    terms, total, slots, stage, shrink_stage, expand_stage,
    sum_sent, sum_got, spread_sent, spread_got, expand_sent, expand_got, shrink_sent, shrink_got,
    in_sent, in_got, out_sent, out_got, put_done, branch_done, product_done,
):
    me, ctx = lax.axis_index("tp"), lax.axis_index("ctx")
    rows, width = gathered.shape[0] // 3, gathered.shape[1]
    half = heads_ref.shape[1]
    height = rows // PIECES
    own = height // count
    shard = width // PIECES
    pieces = 3 * PIECES

    def piece_rows(piece, start=0):
        return pl.ds(pl.multiple_of(start + piece * height, height), height)

    def view(piece, owner):
        return gathered.at[pl.ds(pl.multiple_of(piece * height + owner * own, own), own)]

    line = Line(me, count, slots, sum_sent, sum_got, view, spread_sent, spread_got)
    expand_gather = PlaneGather(expand_weight, expand_sent, expand_got)
    shrink_gather = PlaneGather(shrink_weight, shrink_sent, shrink_got)
    own_half = pl.ds(pl.multiple_of(ctx * half, half), half)
    own_block = pl.ds(pl.multiple_of(ctx * rows, rows), rows)
    puts = [
        pltpu.make_async_copy(source, place, put_done.at[i])
        for i, (source, place) in enumerate(
            (
                (heads_ref.at[own_block], attended.at[:, own_half]),
                (expand_shard, expand_gather.shard(expand_gather.fsdp, ctx)),
                (shrink_shard, shrink_gather.shard(shrink_gather.fsdp, ctx)),
            )
        )
    ]
    for put in puts:
        put.start()
    swap_in = Swap(
        in_sent, in_got,
        lambda piece: heads_ref.at[piece_rows(piece, (1 - ctx) * rows)],
        lambda piece: attended.at[piece_rows(piece), own_half],
    )
    swap_out = Swap(
        out_sent, out_got,
        lambda piece: stage.at[piece_rows(piece)],
        lambda piece: grad_heads.at[piece_rows(piece, ctx * rows)],
    )
    greet(me, count, expand_gather.peers())
    pl.loop(0, PIECES)(swap_in.start)
    for put in puts:
        put.wait()
    expand_gather.first()

    def branch_copy(piece):
        part = piece_rows(piece)
        return pltpu.make_async_copy(
            gathered.at[piece_rows(piece, 2 * rows)], branch_out.at[part], branch_done.at[piece]
        )

    def in_stage(piece, number):
        return (piece >= number * PIECES) & (piece < (number + 1) * PIECES)

    def tiles(extent, action):
        @pl.loop(0, extent // TILE)
        def _(tile):
            action(pl.ds(pl.multiple_of(tile * TILE, TILE), TILE))

    def use(piece):
        line.sum_sent_all(piece)
        part = piece_rows(lax.rem(piece, PIECES))
        chunk_rows = piece_rows(piece)

        @pl.when(in_stage(piece, 0))
        def _():
            chunk = gathered[chunk_rows, :]

            def expand(columns):
                values = dot_plain(chunk, expand_weight[:, columns]) + hidden_bias[:, columns]
                result, bend = gelu_with_slope(values)
                activated[part, columns] = result.astype(jnp.bfloat16)
                slope[part, columns] = bend.astype(jnp.bfloat16)

            tiles(activated.shape[1], expand)

        @pl.when(in_stage(piece, 1))
        def _():
            chunk = gathered[chunk_rows, :]

            def shrink(columns):
                grad = dot_plain(chunk, shrink_weight[:, columns])
                low = (grad * slope[part, columns].astype(jnp.float32)).astype(jnp.bfloat16)
                slope[part, columns] = low
                added = jnp.sum(low.astype(jnp.float32), axis=0, keepdims=True)
                before = jnp.where(piece == PIECES, 0.0, hidden_sums[0:1, columns])
                hidden_sums[0:1, columns] = before + added

            tiles(slope.shape[1], shrink)

        @pl.when(in_stage(piece, 2))
        def _():
            place = piece - 2 * PIECES
            result = dot_plain(gathered[chunk_rows, :], output_weight[...]).astype(jnp.bfloat16)
            here = ctx == 0
            left, right = result[:, :half], result[:, half:]
            stage[part, :] = jnp.where(here, right, left)
            swap_out.start(place)
            grad_heads[piece_rows(place, ctx * rows), :] = jnp.where(here, left, right)
            branch_copy(place).start()

    def form(piece):
        part = piece_rows(lax.rem(piece, PIECES))
        parity = lax.rem(piece, 2)

        def products(x, weight):
            def product(columns):
                terms[parity, :, columns] = dot_cols(x, weight[columns, :])

            tiles(width, product)

        @pl.when(in_stage(piece, 0))
        def _():
            swap_in.wait_arrival(piece)
            products(attended[part, :], output_weight)

        @pl.when(in_stage(piece, 1))
        def _():
            products(activated[part, :], shrink_weight)

        @pl.when(in_stage(piece, 2))
        def _():
            products(slope[part, :], expand_weight)

        line.sum_start(piece, term_of(piece))

    def term_of(piece):
        parity = lax.rem(piece, 2)
        return lambda owner: terms[parity, pl.ds(pl.multiple_of(owner * own, own), own), :]

    def own_step(piece):
        place = lax.rem(piece, PIECES)
        total[...] = term_of(piece)(me)
        line.sum_end(piece, total)

        @pl.when(in_stage(piece, 0))
        def _():
            view(piece, me)[...] = first_norm_step(
                place, total, (own_tokens, gains, biases), (inner, normed_one, inverse_one)
            )

        @pl.when(in_stage(piece, 1))
        def _():
            view(piece, me)[...] = second_norm_step(
                place, total, (inner, out_grad, gains, biases), (mixed, inner, second_sums)
            )

        @pl.when(in_stage(piece, 2))
        def _():
            view(piece, me)[...] = first_back_step(
                place, total, (inner, normed_one, inverse_one, gains), (inner, first_sums)
            )

        line.spread_start(piece)

    def gradient(left_start, right, place, out, done):
        def copy(number):
            part = pl.ds(pl.multiple_of(number * shard, shard), shard)
            return pltpu.make_async_copy(place, out.at[part], done)

        def step(number):
            pl.when(number > 0)(lambda: copy(number - 1).wait())
            columns = pl.ds(pl.multiple_of(number * shard, shard), shard)
            left = gathered[left_start : left_start + rows, columns].T

            def product(part):
                place[:, part] = dot_plain(left, right[:, part]).astype(place.dtype)

            tiles(place.shape[1], product)
            copy(number).start()

        return step, copy

    shrink_step, shrink_copy = gradient(
        rows, activated, shrink_stage, shrink_out, product_done.at[0]
    )
    expand_step, expand_copy = gradient(0, slope, expand_stage, expand_out, product_done.at[1])

    @pl.loop(0, pieces + 5)
    def _(step):
        def late(number, action, most=pieces):
            @pl.when((step >= number) & (step < most + number))
            def _():
                action(step - number)

        pl.when(step == 5)(expand_gather.last)
        late(5, use)
        late(3, lambda piece: line.spread_onward(piece, 2))
        late(1, lambda piece: line.sum_onward(piece, term_of(piece), [1]))
        pl.when(step == PIECES)(shrink_gather.last)
        late(0, form)
        late(4, lambda piece: [line.spread_onward(piece, i) for i in range(3, count)])
        late(2, lambda piece: line.spread_onward(piece, 1))
        late(2 * PIECES + 4, shrink_step, PIECES)
        late(2 * PIECES + 5, expand_step, PIECES)
        late(0, lambda piece: line.sum_onward(piece, term_of(piece), range(count - 2, 1, -1)))
        late(1, own_step)

        @pl.when(step == 3)
        def _():
            expand_gather.second()
            shrink_gather.first()

        pl.when(step == 4)(expand_gather.third)
        pl.when(step == 6)(shrink_gather.second)
        pl.when(step == 7)(shrink_gather.third)

    shrink_copy(PIECES - 1).wait()
    expand_copy(PIECES - 1).wait()

    @pl.loop(0, PIECES)
    def _(piece):
        branch_copy(piece).wait()
        swap_in.wait_sent(piece)
        swap_out.wait_arrival(piece)
        swap_out.wait_sent(piece)

    expand_gather.wait_sent()
    shrink_gather.wait_sent()
    line.spread_finish(pieces)


def gelu_with_slope(values):
    scale = math.sqrt(2.0 / math.pi)
    square = values * values
    bend = 0.5 * jnp.tanh(scale * values * (1.0 + 0.044715 * square)) + 0.5
    inner = (2 * scale) * (1.0 + 3 * 0.044715 * square)
    result = values * bend
    return result, bend + result * (1.0 - bend) * inner


def middle(
    attended_heads, output_weight, expand_shard, shrink_shard, own_tokens, out_grad, gains, biases,
    hidden_bias, collective_id,
):
    count = lax.axis_size("tp")
    rows = attended_heads.shape[0] // 2
    half = attended_heads.shape[1]
    own_rows, width = own_tokens.shape
    hidden = expand_shard.shape[1]
    height = rows // PIECES
    own = height // count
    shard = width // PIECES
    low = jnp.bfloat16
    vmem, anywhere = pl.BlockSpec(memory_space=pltpu.VMEM), pl.BlockSpec(memory_space=pl.ANY)

    def shape(extent, kind=jnp.float32):
        return jax.ShapeDtypeStruct(extent, kind)

    return pl.pallas_call(
        functools.partial(middle_kernel, count),
        out_shape=[
            shape((rows, 2 * half), low),
            shape(out_grad.shape, low),
            shape((own_rows, width)),
            shape((rows, width), low),
            shape((2 * rows, half), low),
            shape((8, width)),
            shape((8, width)),
            shape((8, hidden)),
            shape((width, hidden), low),
            shape((width, hidden), low),
        ],
        in_specs=[anywhere, vmem, anywhere, anywhere, vmem, vmem, vmem, vmem, vmem],
        out_specs=[vmem, vmem, vmem, anywhere, vmem, vmem, vmem, vmem, anywhere, anywhere],
        scratch_shapes=[
            pltpu.VMEM((width, hidden), low),
            pltpu.VMEM((width, hidden), low),
            pltpu.VMEM((3 * rows, width), low),
            pltpu.VMEM((rows, hidden), low),
            pltpu.VMEM((rows, hidden), low),
            pltpu.VMEM((own_rows, width), jnp.float32),
            pltpu.VMEM((own_rows, 128), jnp.float32),
            pltpu.VMEM((2, height, width), jnp.float32),
            pltpu.VMEM((own, width), jnp.float32),
            pltpu.VMEM((PIECES, count + 1, own, width), low),
            pltpu.VMEM((rows, half), low),
            pltpu.VMEM((shard, hidden), low),
            pltpu.VMEM((shard, hidden), low),
            *line_semaphores(count, PIECES)[0],
            *line_semaphores(count, 3 * PIECES)[1],
            *[pltpu.SemaphoreType.DMA((9,))] * 4,
            *[pltpu.SemaphoreType.DMA((PIECES,))] * 4,
            pltpu.SemaphoreType.DMA((3,)),
            pltpu.SemaphoreType.DMA((PIECES,)),
            pltpu.SemaphoreType.DMA((2,)),
        ],
        compiler_params=pltpu.CompilerParams(
            collective_id=collective_id, has_side_effects=True, vmem_limit_bytes=62 << 20
        ),
        cost_estimate=pl.CostEstimate(
            flops=300_000_000_000, bytes_accessed=192 * rows * width, transcendentals=0
        ),
        name="middle",
    )(
        attended_heads, output_weight, expand_shard, shrink_shard, own_tokens, out_grad, gains,
        biases, hidden_bias,
    )


def peers_in_plane(sizes):
    fsdp, ctx = lax.axis_index("fsdp"), lax.axis_index("ctx")
    return [
        {"fsdp": lax.rem(fsdp + i, sizes[0]), "ctx": lax.rem(ctx + j, sizes[1])}
        for i in range(sizes[0])
        for j in range(sizes[1])
        if i or j
    ]


def input_kernel(
    sizes, x_ref, weight, inner_ref, rows_ref, hidden_ref, out_ref, vectors_ref,
    term_ref, total, slots, own_vectors, tp_slots, plane_slots,
    sum_sent, sum_got, tp_sent, tp_got, plane_sent, plane_got, hooks=None,
):
    count = sizes[2]
    me = lax.axis_index("tp")
    height = x_ref.shape[0] // PIECES
    own = height // count
    width = out_ref.shape[1]
    line = Line(me, count, slots, sum_sent, sum_got, None, None, None)
    tp_peers, plane_peers = peers_along_tp(me, count), peers_in_plane(sizes)
    greet_peers(tp_peers + plane_peers)

    def own_part(index):
        return rows_ref.at[:, pl.ds(pl.multiple_of(index * width, width), width)]

    over_tp = Exchange(
        tp_peers, tp_sent, tp_got,
        lambda i: own_part(lax.rem(me + i, count)), lambda i: tp_slots.at[i],
    )
    over_plane = Exchange(
        plane_peers, plane_sent, plane_got, lambda _: own_vectors, lambda i: plane_slots.at[i]
    )
    opening, before, after, closing = hooks or (lambda *_: None,) * 4
    opening()
    over_tp.start()

    def terms(piece):
        def term(owner):
            features = pl.ds(pl.multiple_of(owner * width, width), width)
            term_ref[...] = dot_cols(
                x_ref[pl.ds(pl.multiple_of(piece * height, height), height), :],
                weight[features, :],
            )
            inner = inner_ref[pl.ds(pl.multiple_of(piece * own, own), own), features]
            term_ref[pl.ds(pl.multiple_of(me * own, own), own), :] += inner
            return term_ref[...]

        return term

    def pack():
        over_tp.wait_arrivals()
        own_vectors[0:8, :] = own_part(me)[...]
        for i in range(count - 1):
            own_vectors[0:8, :] += tp_slots[i]
        own_vectors[8:, :] = jnp.zeros_like(own_vectors[8:, :])
        hidden_rows = hidden_ref.shape[1] // width
        for i in range(hidden_rows):
            own_vectors[8 + i : 9 + i, :] = hidden_ref[0:1, i * width : (i + 1) * width]
        for i in range(x_ref.shape[1] // width):
            part = x_ref[:, i * width : (i + 1) * width].astype(jnp.float32)
            place = 8 + hidden_rows + i
            own_vectors[place : place + 1, :] = jnp.sum(part, axis=0, keepdims=True)
        over_plane.start()

    @pl.loop(0, PIECES)
    def _(piece):
        before(piece)
        line.sum_start(piece, terms(piece))
        line.sum_onward(piece, terms(piece), range(count - 2, 0, -1))
        after(piece)

    pack()
    closing()

    @pl.loop(0, PIECES)
    def _(piece):
        total[...] = terms(piece)(me)
        line.sum_end(piece, total)
        rows = pl.ds(pl.multiple_of(piece * height, height), height)
        out_ref[rows, :] = total[...].astype(out_ref.dtype)

    over_plane.wait_arrivals()
    vectors_ref[...] = own_vectors[...]
    for i in range(len(plane_peers)):
        vectors_ref[...] += plane_slots[i]
    over_tp.wait_sent()
    over_plane.wait_sent()
    line.sum_finish(PIECES)


def input_sum(x, weight, inner, row_sums, hidden_sums, collective_id):
    sizes = tuple(lax.axis_size(axis) for axis in ("fsdp", "ctx", "tp"))
    count = sizes[2]
    others = sizes[0] * sizes[1] - 1
    rows = x.shape[0]
    width = weight.shape[0] // count
    height = rows // PIECES
    packed = 8 + -(-(hidden_sums.shape[1] + x.shape[1]) // (8 * width)) * 8
    return pl.pallas_call(
        functools.partial(input_kernel, sizes),
        out_shape=[
            jax.ShapeDtypeStruct((rows, width), jnp.bfloat16),
            jax.ShapeDtypeStruct((packed, width), jnp.float32),
        ],
        in_specs=[pl.BlockSpec(memory_space=pltpu.VMEM)] * 5,
        out_specs=[pl.BlockSpec(memory_space=pltpu.VMEM)] * 2,
        scratch_shapes=[
            pltpu.VMEM((height, width), jnp.float32),
            pltpu.VMEM((height, width), jnp.float32),
            pltpu.VMEM((PIECES, count + 1, height, width), jnp.bfloat16),
            pltpu.VMEM((packed, width), jnp.float32),
            pltpu.VMEM((count - 1, 8, width), jnp.float32),
            pltpu.VMEM((others, packed, width), jnp.float32),
            *line_semaphores(count, PIECES)[0],
            pltpu.SemaphoreType.DMA((count - 1,)),
            pltpu.SemaphoreType.DMA((count - 1,)),
            pltpu.SemaphoreType.DMA((others,)),
            pltpu.SemaphoreType.DMA((others,)),
        ],
        compiler_params=pltpu.CompilerParams(
            collective_id=collective_id, has_side_effects=True, vmem_limit_bytes=40 << 20
        ),
        cost_estimate=pl.CostEstimate(
            flops=60_000_000_000, bytes_accessed=64 * rows * width, transcendentals=0
        ),
        name="input_sum",
    )(x, weight, inner, row_sums, hidden_sums)


class PlaneSum:
    def __init__(self, parts, core_slots, first_slots, last_slots, sent, got):
        self.parts, self.core_slots = parts, core_slots
        self.first_slots, self.last_slots = first_slots, last_slots
        self.sent, self.got = sent, got
        self.fsdp, self.ctx = lax.axis_index("fsdp"), lax.axis_index("ctx")
        self.twin = self.fsdp + 1 - 2 * lax.rem(self.fsdp, 2)
        self.half = parts.shape[2] // 2

    def number(self, fsdp, over_x, over_y):
        chip = lax.rem(fsdp + 2 * over_x, 4)
        return chip * 2 + (1 - self.ctx if over_y else self.ctx)

    def view(self, over_x, over_y, side):
        columns = pl.ds(side * self.half, self.half)
        return self.parts.at[self.number(self.fsdp, over_x, over_y), :, columns]

    def copy(self, number, source, place, peer):
        return pltpu.make_async_remote_copy(
            src_ref=source,
            dst_ref=place,
            send_sem=self.sent.at[number],
            recv_sem=self.got.at[number],
            device_id=peer,
            device_id_type=MESH,
        )

    def core_copy(self, number):
        over_x, over_y = number // 2, number % 2
        source = self.parts.at[self.number(self.twin, over_x, over_y)]
        return self.copy(number, source, self.core_slots.at[number], {"fsdp": self.twin})

    def x_peer(self):
        return {"fsdp": lax.rem(self.fsdp + 2, 4)}

    def y_peer(self):
        return {"ctx": 1 - self.ctx}

    def first_copy(self, number):
        slot = self.first_slots.at[number]
        if number < 2:
            return self.copy(4 + number, self.view(1, number, 0), slot, self.x_peer())
        return self.copy(4 + number, self.view(number - 2, 1, 1), slot, self.y_peer())

    def last_copy(self, side):
        slot = self.last_slots.at[side]
        if side == 0:
            return self.copy(8, self.view(0, 1, 0), slot, self.y_peer())
        return self.copy(9, self.view(1, 0, 1), slot, self.x_peer())

    def add(self, view, slot):
        total = view[...].astype(jnp.float32) + slot[...].astype(jnp.float32)
        view[...] = total.astype(view.dtype)

    def start(self):
        for number in (3, 2, 1, 0):
            self.core_copy(number).start()

    def second(self):
        for number in (3, 2, 1, 0):
            self.core_copy(number).wait_recv()
            shard = self.parts.at[self.number(self.fsdp, number // 2, number % 2)]
            self.add(shard, self.core_slots.at[number])
            if number == 3:
                self.first_copy(1).start()
                self.first_copy(3).start()
            if number == 2:
                self.first_copy(0).start()
            if number == 1:
                self.first_copy(2).start()

    def third(self):
        self.first_copy(1).wait_recv()
        self.add(self.view(0, 1, 0), self.first_slots.at[1])
        self.last_copy(0).start()
        self.first_copy(3).wait_recv()
        self.add(self.view(1, 0, 1), self.first_slots.at[3])
        self.last_copy(1).start()

    def finish(self):
        totals = []
        for side in range(2):
            number = 2 * side
            self.first_copy(number).wait_recv()
            self.last_copy(side).wait_recv()
            total = self.view(0, 0, side)[...].astype(jnp.float32)
            total += self.first_slots[number].astype(jnp.float32)
            totals.append(total + self.last_slots[side].astype(jnp.float32))
        for number in range(4):
            self.core_copy(number).wait_send()
            self.first_copy(number).wait_send()
        for side in range(2):
            self.last_copy(side).wait_send()
        return totals

    @staticmethod
    def scratch(shards, height, width):
        return [
            pltpu.VMEM((shards, height, width), jnp.bfloat16),
            pltpu.VMEM((4, height, width), jnp.bfloat16),
            pltpu.VMEM((4, height, width // 2), jnp.bfloat16),
            pltpu.VMEM((2, height, width // 2), jnp.bfloat16),
            pltpu.SemaphoreType.DMA((10,)),
            pltpu.SemaphoreType.DMA((10,)),
        ]


def leave_kernel(
    sizes, grads_ref, tokens_ref, weight, inner_ref, rows_ref, hidden_ref, branch_ref, attended_ref,
    out_ref, vectors_ref, query_out, key_out, value_out, output_out,
    x_ref, term_ref, total, slots, own_vectors, tp_slots, plane_slots,
    sum_sent, sum_got, tp_sent, tp_got, plane_sent, plane_got, swap_sent, swap_got, *sum_scratch,
):
    count = sizes[2]
    me, ctx = lax.axis_index("tp"), lax.axis_index("ctx")
    rows = x_ref.shape[0]
    height = rows // PIECES
    part = grads_ref.shape[1]
    plane_sum, output_sum = PlaneSum(*sum_scratch[:6]), PlaneSum(*sum_scratch[6:])
    shard = plane_sum.parts.shape[1]

    def piece_rows(piece, start=0):
        return pl.ds(pl.multiple_of(start + piece * height, height), height)

    own_columns = pl.ds(pl.multiple_of(ctx * part, part), part)
    swap = Swap(
        swap_sent, swap_got,
        lambda piece: grads_ref.at[piece_rows(piece, (1 - ctx) * rows)],
        lambda piece: x_ref.at[piece_rows(piece), own_columns],
    )

    def products(sums, fsdp, left, right):
        for over_x in (1, 0):
            for over_y in (1, 0):
                number = sums.number(fsdp, over_x, over_y)
                columns = pl.ds(pl.multiple_of(number * shard, shard), shard)
                sums.parts[number] = dot_rows(left[:, columns], right[...]).astype(jnp.bfloat16)

    def opening():
        @pl.loop(0, PIECES)
        def _(piece):
            swap.start(piece)

        products(output_sum, output_sum.twin, branch_ref, attended_ref)
        output_sum.start()
        x_ref[:, own_columns] = grads_ref[pl.ds(pl.multiple_of(ctx * rows, rows), rows), :]
        products(output_sum, output_sum.fsdp, branch_ref, attended_ref)
        output_sum.second()

    last = PIECES - 1
    begin = jnp.where((me == 0) | (me == count - 1), last, 2)

    def before(piece):
        @pl.when(piece <= begin)
        def _():
            swap.wait_arrival(piece)

    def after(piece):
        @pl.when(piece == begin)
        def _():
            @pl.loop(begin + 1, PIECES)
            def _(other):
                swap.wait_arrival(other)

            products(plane_sum, plane_sum.twin, tokens_ref, x_ref)
            plane_sum.start()

        @pl.when(piece == jnp.minimum(begin + 1, last))
        def _():
            products(plane_sum, plane_sum.fsdp, tokens_ref, x_ref)

        pl.when(piece == jnp.minimum(begin + 2, last))(plane_sum.second)
        pl.when(piece == jnp.minimum(begin + 3, last))(output_sum.third)

    def closing():
        plane_sum.third()

    input_kernel(
        sizes, x_ref, weight, inner_ref, rows_ref, hidden_ref, out_ref, vectors_ref,
        term_ref, total, slots, own_vectors, tp_slots, plane_slots,
        sum_sent, sum_got, tp_sent, tp_got, plane_sent, plane_got,
        hooks=(opening, before, after, closing),
    )
    halves = plane_sum.finish()
    third = part // 3
    for side, half in enumerate(halves):
        for i, ref in enumerate((query_out, key_out, value_out)):
            ref[:, side * third : (side + 1) * third] = half[:, i * third : (i + 1) * third]
    output_out[...] = jnp.concatenate(output_sum.finish(), axis=1)

    @pl.loop(0, PIECES)
    def _(piece):
        swap.wait_sent(piece)


def leave(grads, tokens, weight, inner, row_sums, hidden_sums, branch, attended, collective_id):
    sizes = tuple(lax.axis_size(axis) for axis in ("fsdp", "ctx", "tp"))
    count = sizes[2]
    others = sizes[0] * sizes[1] - 1
    rows, features = tokens.shape
    part = grads.shape[1]
    width = features // count
    height = rows // PIECES
    shard = features // (others + 1)
    packed = 8 + -(-(hidden_sums.shape[1] + 2 * part) // (8 * width)) * 8
    return pl.pallas_call(
        functools.partial(leave_kernel, sizes),
        out_shape=[
            jax.ShapeDtypeStruct((rows, width), jnp.bfloat16),
            jax.ShapeDtypeStruct((packed, width), jnp.float32),
            *[jax.ShapeDtypeStruct((shard, 2 * part // 3), jnp.float32)] * 4,
        ],
        in_specs=[pl.BlockSpec(memory_space=pltpu.VMEM)] * 8,
        out_specs=[pl.BlockSpec(memory_space=pltpu.VMEM)] * 6,
        scratch_shapes=[
            pltpu.VMEM((rows, 2 * part), jnp.bfloat16),
            pltpu.VMEM((height, width), jnp.float32),
            pltpu.VMEM((height, width), jnp.float32),
            pltpu.VMEM((PIECES, count + 1, height, width), jnp.bfloat16),
            pltpu.VMEM((packed, width), jnp.float32),
            pltpu.VMEM((count - 1, 8, width), jnp.float32),
            pltpu.VMEM((others, packed, width), jnp.float32),
            *line_semaphores(count, PIECES)[0],
            pltpu.SemaphoreType.DMA((count - 1,)),
            pltpu.SemaphoreType.DMA((count - 1,)),
            pltpu.SemaphoreType.DMA((others,)),
            pltpu.SemaphoreType.DMA((others,)),
            pltpu.SemaphoreType.DMA((PIECES,)),
            pltpu.SemaphoreType.DMA((PIECES,)),
            *PlaneSum.scratch(others + 1, shard, 2 * part),
            *PlaneSum.scratch(others + 1, shard, attended.shape[1]),
        ],
        compiler_params=pltpu.CompilerParams(
            collective_id=collective_id, has_side_effects=True, vmem_limit_bytes=60 << 20
        ),
        cost_estimate=pl.CostEstimate(
            flops=60_000_000_000, bytes_accessed=64 * rows * width, transcendentals=0
        ),
        name="leave",
    )(grads, tokens, weight, inner, row_sums, hidden_sums, branch, attended)


def to_own_rows(wide):
    count = lax.axis_size("tp")
    parts = wide.reshape(PIECES, count, -1, wide.shape[1])
    return lax.dynamic_index_in_dim(parts, lax.axis_index("tp"), 1, keepdims=False).reshape(
        -1, wide.shape[1]
    )


def spread_own(block):
    count = lax.axis_size("tp")
    rows, width = block.shape
    parts = block.reshape(PIECES, count, -1, width).transpose(1, 0, 2, 3)
    return lax.all_to_all(
        parts.reshape(count, -1, width), "tp", split_axis=0, concat_axis=0, tiled=True
    )


def unspread_own(parts):
    count, own_rows, width = parts.shape
    got = lax.all_to_all(parts, "tp", split_axis=0, concat_axis=0, tiled=True)
    return got.reshape(count, PIECES, -1, width).transpose(1, 0, 2, 3).reshape(-1, width)


def body(
    tokens,
    segments,
    query_weight,
    key_weight,
    value_weight,
    output_weight,
    expand_weight,
    shrink_weight,
    query_bias,
    value_bias,
    hidden_bias,
    norm_gains,
    row_biases,
    out_grad,
):
    rows = tokens.shape[0]
    head_cols = query_weight.shape[1]
    heads = head_cols // HD
    plane = ("fsdp", "ctx")
    plane_sizes = tuple(lax.axis_size(axis) for axis in plane)
    by_heads = plane_sizes == (4, 2) and heads % 2 == 0

    def weight_rows(weight):
        return lax.all_gather(weight, plane, axis=0, tiled=True)

    marks = jnp.concatenate(
        [norm_gains, row_biases, jnp.zeros((10, norm_gains.shape[1]), norm_gains.dtype)]
    )
    block_index = lax.axis_index("fsdp") * plane_sizes[1] + lax.axis_index("ctx")
    qkv_bias = jnp.stack([query_bias, jnp.zeros_like(query_bias), value_bias])
    qkv_bias = qkv_bias.astype(jnp.float32)
    if by_heads:
        half_bias = qkv_bias.reshape(3, 2, -1).transpose(1, 0, 2).reshape(1, -1)
        wide_tokens, own_tokens, wide_marks, wide_qkv, full_output, qkv_heads = enter(
            tokens, marks, query_weight, key_weight, value_weight, output_weight, half_bias, 0
        )
        queries = keys = values = qkv_heads
        own_heads = heads // 2
        bounds = (segments.reshape(-1, plane_sizes[1] * rows),)
    else:
        wide_qkv = weight_rows(jnp.concatenate([query_weight, key_weight, value_weight], axis=1))
        wide_tokens, wide_marks = gather_features(tokens, marks, 0)
        own_tokens = to_own_rows(wide_tokens)
        qkv = dot_plain(wide_tokens, wide_qkv) + qkv_bias.reshape(1, -1)
        queries, keys, values = jnp.split(qkv.astype(jnp.bfloat16), 3, axis=1)
        own_heads = heads
        keys, values = padded(keys, WIN), padded(values, WIN)
        ids = jnp.concatenate(
            [
                jnp.full((WIN,), -1, jnp.int32),
                segments,
                jnp.full((WIN,), jnp.iinfo(jnp.int32).max, jnp.int32),
            ]
        )
        full_output, full_expand = weight_rows(output_weight), weight_rows(expand_weight)
        key_ids = lax.dynamic_slice_in_dim(ids, block_index * rows, rows + 2 * WIN, 0)
        bounds = key_bounds(key_ids[WIN : WIN + rows], key_ids, WIN)
    places = (0, own_heads, 2 * own_heads) if by_heads else (0, 0, 0)
    gains = wide_marks[:2].astype(jnp.float32)
    biases = wide_marks[2:6].astype(jnp.float32)
    wide_marks, out_grad = lax.optimization_barrier((wide_marks, out_grad))
    upstream = spread_own(out_grad)
    attended_heads, lse = attend(queries, keys, values, own_heads, bounds, places)
    attended_heads, upstream = lax.optimization_barrier((attended_heads, upstream))

    own_rows, features = own_tokens.shape
    hidden_cols = expand_weight.shape[1]

    def shape(extent, kind=jnp.float32):
        return jax.ShapeDtypeStruct(extent, kind)

    own_shape = shape((own_rows, features))
    def owner_sum(grad):
        return lax.psum_scatter(
            grad, plane, scatter_dimension=0, tiled=True
        )

    if by_heads:
        (
            attended, mixed_own, grad_inner, branch_low, attended_grad,
            first_sums, second_sums, hidden_sums, shrink_part, expand_part,
        ) = middle(
            attended_heads, full_output, expand_weight, shrink_weight, own_tokens, upstream,
            gains, biases, hidden_bias.astype(jnp.float32)[None], 1,
        )
        shrink_grad, expand_grad = owner_sum(shrink_part), owner_sum(expand_part)
        mixed = unspread_own(mixed_own)
        (grads,) = attend_back(
            queries, keys, values, attended_heads, attended_grad, lse, bounds, places, True
        )
        grads, mixed = lax.optimization_barrier((grads, mixed))
    else:
        full_shrink = weight_rows(shrink_weight)
        norm_low, first_norm, normed_one, inverse_one, hidden, activated = relay(
            attended_heads, full_output, full_expand,
            [own_tokens, gains, biases], first_norm_step,
            [own_shape, own_shape, shape((own_rows, 128))],
            [hidden_bias.astype(jnp.float32)[None]], expand_step,
            [shape((rows, hidden_cols)), shape((rows, hidden_cols), jnp.bfloat16)],
            1, "first_norm",
        )
        ffn_low, mixed_own, grad_second, second_sums, hidden_low, hidden_sums = relay(
            activated, full_shrink, None,
            [first_norm, upstream, gains, biases], second_norm_step,
            [shape(upstream.shape, jnp.bfloat16), own_shape, shape((8, features))],
            [hidden], shrink_step,
            [shape((rows, hidden_cols), jnp.bfloat16), shape((8, hidden_cols))],
            2, "second_norm",
        )
        shrink_grad = owner_sum(dot_rows(ffn_low, activated).astype(jnp.bfloat16))
        branch_low, grad_inner, first_sums, attended_grad = relay(
            hidden_low, full_expand, full_output,
            [grad_second, normed_one, inverse_one, gains], first_back_step,
            [own_shape, shape((8, features))],
            [], attended_step,
            [shape((rows, head_cols), jnp.bfloat16)],
            3, "first_back",
        )
        expand_grad = owner_sum(dot_rows(norm_low, hidden_low).astype(jnp.bfloat16))
        output_grad = owner_sum(dot_rows(branch_low, attended_heads).astype(jnp.bfloat16))
        mixed = unspread_own(mixed_own)
        query_low, key_ext, value_ext = attend_back(
            queries, keys, values, attended_heads, attended_grad, lse, bounds
        )

        def fold(ext):
            edges = jnp.concatenate([ext[:WIN], ext[WIN + rows :]], axis=0)
            around = padded(edges, WIN)
            own = ext[WIN : WIN + rows]
            own = own.at[:WIN].add(around[:WIN]).at[rows - WIN :].add(around[3 * WIN :])
            return own.astype(jnp.bfloat16)

        qkv_low = jnp.concatenate([query_low, fold(key_ext), fold(value_ext)], axis=1)
    row_sums = jnp.concatenate(
        [
            first_sums[0:1], second_sums[0:1],
            first_sums[2:3], first_sums[1:2], second_sums[2:3], second_sums[1:2],
            jnp.zeros_like(first_sums[:2]),
        ]
    )
    sides = 2 if by_heads else 1

    def by_kind(columns):
        parts = columns.reshape(-1, sides, 3, head_cols // sides)
        return [parts[:, :, i].reshape(-1, head_cols) for i in range(3)]

    if by_heads:
        input_grad, vectors, query_grad, key_grad, value_grad, output_grad = leave(
            grads, wide_tokens, wide_qkv, grad_inner, row_sums, hidden_sums[:1], branch_low,
            attended, 4,
        )
        input_grad, shrink_grad, expand_grad = lax.optimization_barrier(
            (input_grad, shrink_grad, expand_grad)
        )
    else:
        input_grad, vectors = input_sum(
            qkv_low, wide_qkv, grad_inner, row_sums, hidden_sums[:1], 4
        )
        qkv_grad = owner_sum(dot_rows(wide_tokens, qkv_low).astype(jnp.bfloat16))
        query_grad, key_grad, value_grad = by_kind(qkv_grad.astype(jnp.float32))
    hidden_rows = hidden_cols // head_cols
    query_sum, _, value_sum = by_kind(
        vectors[8 + hidden_rows : 8 + hidden_rows + 3].reshape(1, -1)
    )
    return (
        mixed,
        input_grad,
        query_grad,
        key_grad,
        value_grad,
        output_grad.astype(jnp.float32),
        expand_grad.astype(jnp.float32),
        shrink_grad.astype(jnp.float32),
        query_sum[0],
        value_sum[0],
        vectors[8 : 8 + hidden_rows].reshape(-1),
        vectors[:2],
        vectors[2:6],
    )


def solution(mesh):
    rows, whole, cols = P(("fsdp", "ctx"), "tp"), P(), P("tp")
    wide = P(None, "tp")
    return jax.shard_map(
        body,
        mesh=mesh,
        in_specs=(rows, whole) + (rows,) * 6 + (cols,) * 3 + (wide,) * 2 + (rows,),
        out_specs=(rows,) * 8 + (cols,) * 3 + (wide,) * 2,
        check_vma=False,
    )
```

```python
import functools
import math

import jax
import jax.numpy as jnp
from jax import lax
from jax.experimental import pallas as pl
from jax.experimental.pallas import tpu as pltpu
from jax.sharding import PartitionSpec as P

HD = 128
WIN = 1024
QB = 512
KB = 512

epsilon = 1e-06
hidden_floor = -1e30
score_scale = 1.0 / math.sqrt(HD)
log2_e = 1.0 / math.log(2.0)


def dot_plain(left, right):
    return jnp.dot(left, right, preferred_element_type=jnp.float32)


def dot_rows(left, right):
    return lax.dot_general(
        left, right, (((0,), (0,)), ((), ())), preferred_element_type=jnp.float32
    )


def dot_cols(left, right):
    return lax.dot_general(
        left, right, (((1,), (1,)), ((), ())), preferred_element_type=jnp.float32
    )


def block_bounds(block, rows, bounds, marks):
    if len(bounds) == 4:
        first, last, low, high = bounds
        return first[block], last[block], low[...], high[...]
    (ids,) = bounds
    run = ids.shape[1]

    @pl.when((pl.program_id(0) == 0) & (block == 0))
    def _():
        own = lax.axis_index("fsdp")
        own_ids = ids[pl.ds(own, 1), :]
        for i in range(2):
            marks[i] = jnp.sum((own_ids <= 3 * own + i).astype(jnp.int32))

    second, third = marks[0], marks[1]

    def bounds_at(places):
        start = jnp.where(places < second, 0, jnp.where(places < third, second, third))
        stop = jnp.where(places < second, second, jnp.where(places < third, third, run))
        return jnp.maximum(start, places - WIN), jnp.minimum(stop - 1, places + WIN)

    begin = block * rows
    low, high = bounds_at(begin + lax.broadcasted_iota(jnp.int32, (1, rows), 1))
    return bounds_at(begin)[0] // KB, bounds_at(begin + rows - 1)[1] // KB + 1, low, high


def bound_operands(bounds):
    if len(bounds) == 4:
        mark_spec = pl.BlockSpec((1, QB), lambda h, i, *_: (0, i))
        return list(bounds[:2]), list(bounds[2:]), [mark_spec, mark_spec]
    shape = bounds[0].shape
    return [], list(bounds), [pl.BlockSpec(shape, lambda h, i, *_: (0, 0))]


def attend_kernel(scalars, *refs):
    bounds = refs[:scalars]
    q_ref, k_ref, v_ref, *arrays, out_ref, lse_ref, vt, marks = refs[scalars:]
    block = pl.program_id(1)
    rows = q_ref.shape[0]

    @pl.when(block == 0)
    def _():
        vt[...] = v_ref[...].T

    queries = q_ref[...]
    first, last, low, high = block_bounds(block, rows, (*bounds, *arrays), marks)
    places = lax.broadcasted_iota(jnp.int32, (KB, rows), 0)

    def step(number, carry):
        top, total, mixed = carry
        start = pl.multiple_of(number * KB, KB)
        scores = dot_cols(k_ref[pl.ds(start, KB), :], queries) * (score_scale * log2_e)
        keep = (places >= low - start) & (places <= high - start)
        scores = jnp.where(keep, scores, hidden_floor)
        new_top = jnp.maximum(top, jnp.max(scores, axis=0, keepdims=True))
        shrink = jnp.exp2(top - new_top)
        powers = jnp.exp2(scores - new_top)
        total = total * shrink + jnp.sum(powers, axis=0, keepdims=True)
        mixed = mixed * shrink + dot_plain(vt[:, pl.ds(start, KB)], powers.astype(jnp.bfloat16))
        return new_top, total, mixed

    top, total, mixed = lax.fori_loop(
        first,
        last,
        step,
        (
            jnp.full((1, rows), hidden_floor, jnp.float32),
            jnp.zeros((1, rows), jnp.float32),
            jnp.zeros((HD, rows), jnp.float32),
        ),
    )
    out_ref[...] = (mixed / total).T.astype(out_ref.dtype)
    lse_ref[...] = (top + jnp.log2(total))[None]


def attend(queries, keys, values, heads, bounds, places=(0, 0, 0)):
    rows, span = queries.shape[0], keys.shape[0]
    width = heads * HD
    q_at, k_at, v_at = places
    scalars, arrays, specs = bound_operands(bounds)
    return pl.pallas_call(
        functools.partial(attend_kernel, len(scalars)),
        out_shape=(
            jax.ShapeDtypeStruct((rows, width), jnp.bfloat16),
            jax.ShapeDtypeStruct((heads, 1, rows), jnp.float32),
        ),
        grid_spec=pltpu.PrefetchScalarGridSpec(
            num_scalar_prefetch=len(scalars),
            grid=(heads, rows // QB),
            in_specs=[
                pl.BlockSpec((QB, HD), lambda h, i, *_: (i, h + q_at)),
                pl.BlockSpec((span, HD), lambda h, i, *_: (0, h + k_at)),
                pl.BlockSpec((span, HD), lambda h, i, *_: (0, h + v_at)),
                *specs,
            ],
            out_specs=[
                pl.BlockSpec((QB, HD), lambda h, i, *_: (i, h)),
                pl.BlockSpec((1, 1, QB), lambda h, i, *_: (h, 0, i)),
            ],
            scratch_shapes=[pltpu.VMEM((HD, span), jnp.bfloat16), pltpu.SMEM((2,), jnp.int32)],
        ),
        compiler_params=pltpu.CompilerParams(vmem_limit_bytes=32 << 20),
        cost_estimate=pl.CostEstimate(
            flops=3 * rows * span * width,
            bytes_accessed=2 * (2 * rows + 2 * span) * width,
            transcendentals=rows * span * heads,
        ),
        name="attend",
    )(*scalars, queries, keys, values, *arrays)


def attend_back_kernel(scalars, arrays, *refs):
    bounds = refs[:scalars]
    q_ref, k_ref, v_ref, o_ref, g_ref, lse_ref, *refs = refs[scalars:]
    bounds = (*bounds, *refs[:arrays])
    *results, kt, dk_sum, dv_sum, marks = refs[arrays:]
    head, block = pl.program_id(0), pl.program_id(1)
    rows = q_ref.shape[0]

    @pl.when(block == 0)
    def _():
        kt[...] = k_ref[...].T
        dk_sum[...] = jnp.zeros_like(dk_sum)
        dv_sum[...] = jnp.zeros_like(dv_sum)

    queries = q_ref[...]
    upstream = g_ref[...]
    lse = lse_ref[0]
    first, last, low, high = block_bounds(block, rows, bounds, marks)
    places = lax.broadcasted_iota(jnp.int32, (KB, rows), 0)
    product = upstream.astype(jnp.float32) * o_ref[...].astype(jnp.float32)
    delta = jnp.sum(product.T, axis=0, keepdims=True)

    def step(number, dq):
        start = pl.multiple_of(number * KB, KB)
        window = pl.ds(start, KB)
        scores = dot_cols(k_ref[window, :], queries) * (score_scale * log2_e)
        keep = (places >= low - start) & (places <= high - start)
        probs = jnp.exp2(jnp.where(keep, scores - lse, hidden_floor))
        prob_grad = dot_cols(v_ref[window, :], upstream)
        score_grad = (probs * (prob_grad - delta)).astype(jnp.bfloat16)
        dv_sum[window, :] += dot_plain(probs.astype(jnp.bfloat16), upstream)
        dk_sum[window, :] += dot_plain(score_grad, queries)
        return dq + dot_plain(kt[:, window], score_grad)

    dq = lax.fori_loop(first, last, step, jnp.zeros((HD, rows), jnp.float32))
    dq = (dq * score_scale).T
    if len(results) == 1:
        width = results[0].shape[1] // 3

        def place(part):
            start = pl.multiple_of(part * width + head * HD, HD)
            return results[0].at[:, pl.ds(start, HD)]

        query_place = place(0).at[pl.ds(pl.multiple_of(block * rows, rows), rows)]
        key_place, value_place = place(1), place(2)
    else:
        query_place, key_place, value_place = results
    query_place[...] = dq.astype(query_place.dtype)

    @pl.when(block == pl.num_programs(1) - 1)
    def _():
        key_place[...] = (dk_sum[...] * score_scale).astype(key_place.dtype)
        value_place[...] = dv_sum[...].astype(value_place.dtype)


def attend_back(
    queries, keys, values, out, upstream, lse, bounds, places=(0, 0, 0), merged=False
):
    rows, width = out.shape
    span = keys.shape[0]
    heads = width // HD
    q_at, k_at, v_at = places
    row_spec = pl.BlockSpec((QB, HD), lambda h, i, *_: (i, h))
    key_spec = pl.BlockSpec((span, HD), lambda h, i, *_: (0, h))
    scalars, arrays, specs = bound_operands(bounds)
    return pl.pallas_call(
        functools.partial(attend_back_kernel, len(scalars), len(arrays)),
        out_shape=[jax.ShapeDtypeStruct((rows, 3 * width), jnp.bfloat16)]
        if merged
        else [
            jax.ShapeDtypeStruct((rows, width), jnp.bfloat16),
            jax.ShapeDtypeStruct((span, width), jnp.float32),
            jax.ShapeDtypeStruct((span, width), jnp.float32),
        ],
        grid_spec=pltpu.PrefetchScalarGridSpec(
            num_scalar_prefetch=len(scalars),
            grid=(heads, rows // QB),
            in_specs=[
                pl.BlockSpec((QB, HD), lambda h, i, *_: (i, h + q_at)),
                pl.BlockSpec((span, HD), lambda h, i, *_: (0, h + k_at)),
                pl.BlockSpec((span, HD), lambda h, i, *_: (0, h + v_at)),
                row_spec, row_spec,
                pl.BlockSpec((1, 1, QB), lambda h, i, *_: (h, 0, i)),
                *specs,
            ],
            out_specs=[pl.BlockSpec((rows, 3 * width), lambda h, i, *_: (0, 0))]
            if merged
            else [row_spec, key_spec, key_spec],
            scratch_shapes=[
                pltpu.VMEM((HD, span), jnp.bfloat16),
                pltpu.VMEM((span, HD), jnp.float32),
                pltpu.VMEM((span, HD), jnp.float32),
                pltpu.SMEM((2,), jnp.int32),
            ],
        ),
        compiler_params=pltpu.CompilerParams(vmem_limit_bytes=32 << 20),
        cost_estimate=pl.CostEstimate(
            flops=8 * rows * span * width,
            bytes_accessed=2 * (4 * rows + 4 * span) * width,
            transcendentals=rows * span * heads,
        ),
        name="attend_back",
    )(*scalars, queries, keys, values, out, upstream, lse, *arrays)


def key_bounds(query_ids, key_ids, offset):
    rows, span = query_ids.shape[0], key_ids.shape[0]
    start = jnp.sum(key_ids[:, None] < query_ids[None, :], axis=0, dtype=jnp.int32)
    stop = jnp.sum(key_ids[:, None] <= query_ids[None, :], axis=0, dtype=jnp.int32)
    places = jnp.arange(rows, dtype=jnp.int32) + offset
    low = jnp.maximum(start, places - WIN)
    high = jnp.minimum(stop - 1, places + WIN)
    first = jnp.min(low.reshape(-1, QB), axis=1) // KB
    last = jnp.max(high.reshape(-1, QB), axis=1) // KB + 1
    return first, last, low[None], high[None]


def padded(block, width):
    count = lax.axis_size("ctx")
    forward = [(i, i + 1) for i in range(count - 1)]
    backward = [(target, source) for source, target in forward]
    below = lax.ppermute(block[block.shape[0] - width :], "ctx", forward)
    above = lax.ppermute(block[:width], "ctx", backward)
    return jnp.concatenate([below, block, above], axis=0)


def norm_parts(rows):
    mean = jnp.mean(rows, axis=-1, keepdims=True)
    square = jnp.mean(rows * rows, axis=-1, keepdims=True)
    inverse = lax.rsqrt(square - mean * mean + epsilon)
    return (rows - mean) * inverse, inverse


def norm_back(upstream, normed, inverse, gain):
    scaled = upstream * gain
    first_mean = jnp.mean(scaled, axis=-1, keepdims=True)
    second_mean = jnp.mean(scaled * normed, axis=-1, keepdims=True)
    return inverse * (scaled - first_mean - normed * second_mean)


def gelu_tanh(values):
    return jax.nn.gelu(values, approximate=True)


MESH = pl.DeviceIdType.MESH
PIECES = 8
TILE = 512


def greet(me, count, others=()):
    barrier = pltpu.get_barrier_semaphore()

    @pl.when(me > 0)
    def _():
        pl.semaphore_signal(barrier, inc=1, device_id={"tp": me - 1}, device_id_type=MESH)

    @pl.when(me < count - 1)
    def _():
        pl.semaphore_signal(barrier, inc=1, device_id={"tp": me + 1}, device_id_type=MESH)

    for other in others:
        pl.semaphore_signal(barrier, inc=1, device_id=other, device_id_type=MESH)

    @pl.when((me == 0) | (me == count - 1))
    def _():
        pl.semaphore_wait(barrier, 1 + len(others))

    @pl.when((me > 0) & (me < count - 1))
    def _():
        pl.semaphore_wait(barrier, 2 + len(others))


def peers_along_tp(me, count):
    return [{"tp": lax.rem(me + i, count)} for i in range(1, count)]


def greet_peers(peers):
    barrier = pltpu.get_barrier_semaphore()
    for peer in peers:
        pl.semaphore_signal(barrier, inc=1, device_id=peer, device_id_type=MESH)
    pl.semaphore_wait(barrier, len(peers))


class Exchange:
    def __init__(self, peers, sent, got, source, place):
        self.peers, self.sent, self.got = peers, sent, got
        self.source, self.place = source, place

    def copies(self):
        for i, peer in enumerate(self.peers):
            yield pltpu.make_async_remote_copy(
                src_ref=self.source(i + 1),
                dst_ref=self.place(i),
                send_sem=self.sent.at[i],
                recv_sem=self.got.at[i],
                device_id=peer,
                device_id_type=MESH,
            )

    def start(self):
        for copy in self.copies():
            copy.start()

    def wait_arrivals(self):
        for copy in self.copies():
            copy.wait_recv()

    def wait_sent(self):
        for copy in self.copies():
            copy.wait_send()


def at_distance(me, count, distance, action):
    for index in (me - distance, me + distance):

        @pl.when((index >= 0) & (index < count))
        def _(index=index):
            action(index)


class Line:
    def __init__(self, me, count, sum_slots, sum_sent, sum_got, spread_view, spread_sent, spread_got):
        self.me, self.count = me, count
        self.sum_slots, self.sum_sent, self.sum_got = sum_slots, sum_sent, sum_got
        self.spread_view, self.spread_sent, self.spread_got = spread_view, spread_sent, spread_got

    def slot(self, piece):
        return lax.rem(piece, self.sum_slots.shape[0])

    def sum_copy(self, piece, owner):
        onward = jnp.where(owner > self.me, self.me + 1, self.me - 1)
        place = jnp.where((owner < self.me) & (owner == self.me - 1), self.count, owner)
        slot = self.slot(piece)
        return pltpu.make_async_remote_copy(
            src_ref=self.sum_slots.at[slot, owner],
            dst_ref=self.sum_slots.at[slot, place],
            send_sem=self.sum_sent.at[slot, owner],
            recv_sem=self.sum_got.at[slot, place],
            device_id={"tp": onward},
            device_id_type=MESH,
        )

    def sum_arrival(self, piece, place):
        view = self.sum_slots.at[self.slot(piece), place]
        pltpu.make_async_copy(view, view, self.sum_got.at[self.slot(piece), place]).wait()

    def sum_start(self, piece, term):
        me, count = self.me, self.count

        @pl.when((me == 0) | (me == count - 1))
        def _():
            for k in range(count - 1):
                owner = jnp.where(me == 0, count - 1 - k, k)
                self.sum_slots[self.slot(piece), owner] = term(owner).astype(jnp.bfloat16)
                self.sum_copy(piece, owner).start()

    def sum_onward(self, piece, term, distances):
        me, count = self.me, self.count

        @pl.when((me > 0) & (me < count - 1))
        def _():
            for distance in distances:

                def pass_on(owner):
                    self.sum_arrival(piece, owner)
                    slot = self.slot(piece)
                    total = self.sum_slots[slot, owner].astype(jnp.float32) + term(owner)
                    self.sum_slots[slot, owner] = total.astype(jnp.bfloat16)
                    self.sum_copy(piece, owner).start()

                at_distance(me, count, distance, pass_on)

    def sum_end(self, piece, total):
        me, count = self.me, self.count

        @pl.when(me > 0)
        def _():
            self.sum_arrival(piece, me)
            total[...] += self.sum_slots[self.slot(piece), me].astype(jnp.float32)

        @pl.when(me < count - 1)
        def _():
            self.sum_arrival(piece, count)
            total[...] += self.sum_slots[self.slot(piece), count].astype(jnp.float32)

    def sum_sent_all(self, piece):
        for distance in range(1, self.count):
            at_distance(
                self.me, self.count, distance,
                lambda owner: self.sum_copy(piece, owner).wait_send(),
            )

    def sum_finish(self, pieces):
        pl.loop(0, pieces)(self.sum_sent_all)

    def spread_copy(self, piece, owner, to, sent, source=None):
        return pltpu.make_async_remote_copy(
            src_ref=self.spread_view(piece, owner) if source is None else source,
            dst_ref=self.spread_view(piece, owner),
            send_sem=self.spread_sent.at[piece, sent],
            recv_sem=self.spread_got.at[piece, owner],
            device_id={"tp": to},
            device_id_type=MESH,
        )

    def own_copies(self, piece, action, source=None):
        me, count = self.me, self.count

        @pl.when(me > 0)
        def _():
            action(self.spread_copy(piece, me, me - 1, count, source))

        @pl.when(me < count - 1)
        def _():
            action(self.spread_copy(piece, me, me + 1, me, source))

    def spread_start(self, piece, source=None):
        self.own_copies(piece, lambda copy: copy.start(), source)

    def onward_copy(self, piece, owner, action):
        me, count = self.me, self.count

        @pl.when((owner < me) & (me < count - 1))
        def _():
            action(self.spread_copy(piece, owner, me + 1, owner))

        @pl.when((owner > me) & (me > 0))
        def _():
            action(self.spread_copy(piece, owner, me - 1, owner))

    def spread_onward(self, piece, distance):
        def pass_on(owner):
            view = self.spread_view(piece, owner)
            pltpu.make_async_copy(view, view, self.spread_got.at[piece, owner]).wait()
            self.onward_copy(piece, owner, lambda copy: copy.start())

        at_distance(self.me, self.count, distance, pass_on)

    def spread_finish(self, pieces, source=None):
        @pl.loop(0, pieces)
        def _(piece):
            self.own_copies(
                piece, lambda copy: copy.wait_send(), None if source is None else source(piece)
            )
            for distance in range(1, self.count):
                at_distance(
                    self.me, self.count, distance,
                    lambda owner: self.onward_copy(piece, owner, lambda copy: copy.wait_send()),
                )


def line_semaphores(count, pieces):
    return [
        pltpu.SemaphoreType.DMA((pieces, count)),
        pltpu.SemaphoreType.DMA((pieces, count + 1)),
    ], [
        pltpu.SemaphoreType.DMA((pieces, count + 1)),
        pltpu.SemaphoreType.DMA((pieces, count)),
    ]


def gather_kernel(
    count, x_ref, marks_ref, out_ref, marks_out, slots, sent, got, marks_sent, marks_got
):
    me = lax.axis_index("tp")
    height = x_ref.shape[0] // PIECES
    width = x_ref.shape[1]

    def view(piece, owner):
        return out_ref.at[
            pl.ds(pl.multiple_of(piece * height, height), height),
            pl.ds(pl.multiple_of(owner * width, width), width),
        ]

    def source(piece):
        return x_ref.at[pl.ds(pl.multiple_of(piece * height, height), height)]

    line = Line(me, count, None, None, None, view, sent, got)
    peers = peers_along_tp(me, count)
    greet_peers(peers)

    @pl.loop(0, PIECES)
    def _(piece):
        line.spread_start(piece, source(piece))

    marks = Exchange(
        peers, marks_sent, marks_got, lambda _: marks_ref, lambda i: slots.at[i]
    )
    marks.start()
    own = pl.ds(pl.multiple_of(me * width, width), width)
    out_ref[:, own] = x_ref[...]
    marks_out[:, own] = marks_ref[...]
    for distance in range(1, count):

        @pl.loop(0, PIECES)
        def _(piece, distance=distance):
            line.spread_onward(piece, distance)

    marks.wait_arrivals()
    for i in range(1, count):
        owner = lax.rem(me - i + count, count)
        marks_out[:, pl.ds(pl.multiple_of(owner * width, width), width)] = slots[i - 1]
    marks.wait_sent()
    line.spread_finish(PIECES, source)


def gather_features(x, marks, collective_id):
    count = lax.axis_size("tp")
    rows, width = x.shape
    return pl.pallas_call(
        functools.partial(gather_kernel, count),
        out_shape=[
            jax.ShapeDtypeStruct((rows, count * width), x.dtype),
            jax.ShapeDtypeStruct((marks.shape[0], count * width), marks.dtype),
        ],
        in_specs=[pl.BlockSpec(memory_space=pltpu.VMEM)] * 2,
        out_specs=[pl.BlockSpec(memory_space=pltpu.VMEM)] * 2,
        scratch_shapes=[
            pltpu.VMEM((count - 1, *marks.shape), marks.dtype),
            *line_semaphores(count, PIECES)[1],
            pltpu.SemaphoreType.DMA((count - 1,)),
            pltpu.SemaphoreType.DMA((count - 1,)),
        ],
        compiler_params=pltpu.CompilerParams(
            collective_id=collective_id, has_side_effects=True, vmem_limit_bytes=16 << 20
        ),
        cost_estimate=pl.CostEstimate(
            flops=0, bytes_accessed=64 * rows * count * width, transcendentals=0
        ),
        name="gather_features",
    )(x, marks)


class Swap:
    def __init__(self, sent, got, source, place):
        self.sent, self.got, self.source, self.place = sent, got, source, place

    def copy(self, piece):
        return pltpu.make_async_remote_copy(
            src_ref=self.source(piece),
            dst_ref=self.place(piece),
            send_sem=self.sent.at[piece],
            recv_sem=self.got.at[piece],
            device_id={"ctx": 1 - lax.axis_index("ctx")},
            device_id_type=MESH,
        )

    def start(self, piece):
        self.copy(piece).start()

    def wait_arrival(self, piece):
        self.copy(piece).wait_recv()

    def wait_sent(self, piece):
        self.copy(piece).wait_send()


class PlaneGather:
    def __init__(self, whole, sent, got):
        self.whole, self.sent, self.got = whole, sent, got
        fsdp, self.ctx = lax.axis_index("fsdp"), lax.axis_index("ctx")
        self.fsdp = fsdp
        self.twin = fsdp + 1 - 2 * lax.rem(fsdp, 2)
        self.along_x = lax.rem(fsdp + 2, 4)
        self.twin_x = lax.rem(self.twin + 2, 4)
        self.core_peer = {"fsdp": self.twin}
        self.x_peer = {"fsdp": self.along_x}
        self.y_peer = {"ctx": 1 - self.ctx}

    def peers(self):
        return [self.core_peer, self.x_peer, self.y_peer]

    def shard(self, fsdp, ctx, half=None):
        height = self.whole.shape[0] // 8
        start = (fsdp * 2 + ctx) * height
        if half is not None:
            height //= 2
            start += half * height
        return self.whole.at[pl.ds(pl.multiple_of(start, height), height)]

    def copy(self, number, view, peer):
        return pltpu.make_async_remote_copy(
            src_ref=view,
            dst_ref=view,
            send_sem=self.sent.at[number],
            recv_sem=self.got.at[number],
            device_id=peer,
            device_id_type=MESH,
        )

    def copies(self):
        own = self.shard(self.fsdp, self.ctx)
        from_x = self.shard(self.along_x, self.ctx)
        from_y = self.shard(self.fsdp, 1 - self.ctx)
        return [
            (own, self.core_peer),
            (own, self.x_peer),
            (own, self.y_peer),
            (from_x, self.core_peer),
            (self.shard(self.along_x, self.ctx, 0), self.y_peer),
            (from_y, self.core_peer),
            (self.shard(self.fsdp, 1 - self.ctx, 1), self.x_peer),
            (self.shard(self.along_x, 1 - self.ctx, 0), self.core_peer),
            (self.shard(self.along_x, 1 - self.ctx, 1), self.core_peer),
        ]

    def arrivals(self):
        return [
            self.shard(self.twin, self.ctx),
            self.shard(self.along_x, self.ctx),
            self.shard(self.fsdp, 1 - self.ctx),
            self.shard(self.twin_x, self.ctx),
            self.shard(self.along_x, 1 - self.ctx, 0),
            self.shard(self.twin, 1 - self.ctx),
            self.shard(self.along_x, 1 - self.ctx, 1),
            self.shard(self.twin_x, 1 - self.ctx, 0),
            self.shard(self.twin_x, 1 - self.ctx, 1),
        ]

    def start(self, *numbers):
        copies = self.copies()
        for number in numbers:
            self.copy(number, *copies[number]).start()

    def wait(self, *numbers):
        arrivals = self.arrivals()
        for number in numbers:
            view = arrivals[number]
            pltpu.make_async_copy(view, view, self.got.at[number]).wait()

    def first(self):
        self.start(1, 2, 0)

    def second(self):
        self.wait(1)
        self.start(4, 3)
        self.wait(2)
        self.start(6, 5)

    def third(self):
        self.wait(4)
        self.start(7)
        self.wait(6)
        self.start(8)

    def last(self):
        self.wait(0, 3, 5, 7, 8)

    def wait_sent(self):
        for number, (view, peer) in enumerate(self.copies()):
            self.copy(number, view, peer).wait_send()


def enter_kernel(
    count, x_ref, marks_ref, query_ref, key_ref, value_ref, output_ref, bias,
    wide, own_tokens, marks_out, weight, output_weight, heads,
    mark_slots, stage, sent, got, marks_sent, marks_got,
    weight_sent, weight_got, output_sent, output_got, swap_sent, swap_got, put_done,
):
    me, ctx = lax.axis_index("tp"), lax.axis_index("ctx")
    rows, width = x_ref.shape
    height = rows // PIECES
    half = query_ref.shape[1] // 2
    part = 3 * half

    def piece_rows(piece, start=0):
        return pl.ds(pl.multiple_of(start + piece * height, height), height)

    def view(piece, owner):
        return wide.at[piece_rows(piece), pl.ds(pl.multiple_of(owner * width, width), width)]

    gather = PlaneGather(weight, weight_sent, weight_got)
    output_gather = PlaneGather(output_weight, output_sent, output_got)
    own_shard = gather.shard(gather.fsdp, ctx)
    own = pl.ds(pl.multiple_of(me * width, width), width)
    puts = [
        (ref.at[:, pl.ds(side * half, half)], own_shard.at[:, pl.ds(side * part + i * half, half)])
        for side in range(2)
        for i, ref in enumerate((query_ref, key_ref, value_ref))
    ]
    puts += [
        (output_ref, output_gather.shard(gather.fsdp, ctx)),
        (x_ref, wide.at[:, own]),
    ]
    puts = [
        pltpu.make_async_copy(source, place, put_done.at[i])
        for i, (source, place) in enumerate(puts)
    ]
    for put in puts:
        put.start()
    line = Line(me, count, None, None, None, view, sent, got)
    tp_peers = peers_along_tp(me, count)
    greet_peers(tp_peers + gather.peers())

    def source(piece):
        return x_ref.at[piece_rows(piece)]

    for piece in range(2):
        line.spread_start(piece, source(piece))
    for put in puts[:7]:
        put.wait()
    gather.first()
    output_gather.first()
    marks = Exchange(
        tp_peers, marks_sent, marks_got, lambda _: marks_ref, lambda i: mark_slots.at[i]
    )
    marks.start()
    marks_out[:, own] = marks_ref[...]
    for put in puts[7:]:
        put.wait()
    swap = Swap(
        swap_sent, swap_got,
        lambda piece: stage.at[piece_rows(piece)],
        lambda piece: heads.at[piece_rows(piece, ctx * rows)],
    )

    def products(piece, side, place):
        x = wide[piece_rows(piece), :]

        @pl.loop(0, 3)
        def _(tile):
            start = pl.multiple_of(side * part + tile * half, half)
            columns = pl.ds(start, half)
            values = dot_plain(x, weight[:, columns]) + bias[:, columns]
            place[:, pl.ds(pl.multiple_of(tile * half, half), half)] = values.astype(jnp.bfloat16)

    @pl.loop(0, PIECES + 7)
    def _(step):
        def late(pieces, action, least=0):
            @pl.when((step >= pieces + least) & (step < PIECES + pieces))
            def _():
                action(step - pieces)

        def use(piece):
            products(piece, 1 - ctx, stage.at[piece_rows(piece)])
            swap.start(piece)
            products(piece, ctx, heads.at[piece_rows(piece, ctx * rows)])

        @pl.when(step == 7)
        def _():
            gather.third()
            gather.last()

        late(0, lambda piece: line.spread_start(piece, source(piece)), 2)
        late(7, use)
        late(5, lambda piece: line.spread_onward(piece, 2))
        late(3, lambda piece: line.spread_onward(piece, 1))
        late(6, lambda piece: [line.spread_onward(piece, i) for i in range(3, count)])
        pl.when(step == 5)(gather.second)
        pl.when(step == 7)(output_gather.second)
        pl.when(step == 9)(output_gather.third)

    own_height = height // count
    for piece in range(PIECES):
        start = pl.multiple_of(piece * height + me * own_height, own_height)
        own_tokens[piece * own_height : (piece + 1) * own_height, :] = wide[
            pl.ds(start, own_height), :
        ]

    marks.wait_arrivals()
    for i in range(1, count):
        owner = lax.rem(me - i + count, count)
        marks_out[:, pl.ds(pl.multiple_of(owner * width, width), width)] = mark_slots[i - 1]

    @pl.loop(0, PIECES)
    def _(piece):
        swap.wait_arrival(piece)
        swap.wait_sent(piece)

    output_gather.last()
    marks.wait_sent()
    gather.wait_sent()
    output_gather.wait_sent()
    line.spread_finish(PIECES, source)


def enter(
    tokens, marks, query_weight, key_weight, value_weight, output_weight, bias, collective_id
):
    count = lax.axis_size("tp")
    rows, width = tokens.shape
    head_cols = query_weight.shape[1]
    plane = 8
    part = 3 * head_cols // 2
    return pl.pallas_call(
        functools.partial(enter_kernel, count),
        out_shape=[
            jax.ShapeDtypeStruct((rows, count * width), tokens.dtype),
            jax.ShapeDtypeStruct((rows // count, count * width), tokens.dtype),
            jax.ShapeDtypeStruct((marks.shape[0], count * width), marks.dtype),
            jax.ShapeDtypeStruct((plane * query_weight.shape[0], 2 * part), query_weight.dtype),
            jax.ShapeDtypeStruct(
                (plane * output_weight.shape[0], output_weight.shape[1]), output_weight.dtype
            ),
            jax.ShapeDtypeStruct((2 * rows, part), jnp.bfloat16),
        ],
        in_specs=[
            pl.BlockSpec(memory_space=pl.ANY),
            pl.BlockSpec(memory_space=pltpu.VMEM),
            *[pl.BlockSpec(memory_space=pl.ANY)] * 4,
            pl.BlockSpec(memory_space=pltpu.VMEM),
        ],
        out_specs=[pl.BlockSpec(memory_space=pltpu.VMEM)] * 6,
        scratch_shapes=[
            pltpu.VMEM((count - 1, *marks.shape), marks.dtype),
            pltpu.VMEM((rows, part), jnp.bfloat16),
            *line_semaphores(count, PIECES)[1],
            pltpu.SemaphoreType.DMA((count - 1,)),
            pltpu.SemaphoreType.DMA((count - 1,)),
            *[pltpu.SemaphoreType.DMA((9,))] * 4,
            pltpu.SemaphoreType.DMA((PIECES,)),
            pltpu.SemaphoreType.DMA((PIECES,)),
            pltpu.SemaphoreType.DMA((8,)),
        ],
        compiler_params=pltpu.CompilerParams(
            collective_id=collective_id, has_side_effects=True, vmem_limit_bytes=60 << 20
        ),
        cost_estimate=pl.CostEstimate(
            flops=80_000_000_000, bytes_accessed=64 * rows * count * width, transcendentals=0
        ),
        name="enter",
    )(tokens, marks, query_weight, key_weight, value_weight, output_weight, bias)


def relay_kernel(count, row_step, use_step, sizes, *refs):
    row_in, use_in, row_out, use_out, shared = sizes
    refs = list(refs)

    def take(number):
        taken = refs[:number]
        del refs[:number]
        return taken

    x_ref, sum_weight = take(2)
    use_weight = sum_weight if shared else take(1)[0]
    row_inputs, use_inputs = take(row_in), take(use_in)
    (gathered,) = take(1)
    row_outputs, use_outputs = take(row_out), take(use_out)
    terms, total, slots, sum_sent, sum_got, spread_sent, spread_got = refs
    me = lax.axis_index("tp")
    height = x_ref.shape[0] // PIECES
    own = height // count
    width = sum_weight.shape[0]

    def piece_rows(piece):
        return pl.ds(pl.multiple_of(piece * height, height), height)

    def view(piece, owner):
        return gathered.at[pl.ds(pl.multiple_of(piece * height + owner * own, own), own)]

    line = Line(me, count, slots, sum_sent, sum_got, view, spread_sent, spread_got)
    greet(me, count)

    @pl.loop(0, PIECES + 5)
    def _(step):
        odd = lax.rem(step, 2)

        def term_of(parity):
            return lambda owner: terms[parity, pl.ds(pl.multiple_of(owner * own, own), own), :]

        def late(pieces, action):
            @pl.when((step >= pieces) & (step < PIECES + pieces))
            def _():
                action(step - pieces)

        def use(piece):
            part = piece_rows(piece)
            use_step(part, gathered[part, :], use_weight, use_inputs, use_outputs)

        def form(piece):
            x = x_ref[piece_rows(piece), :]

            @pl.loop(0, width // TILE)
            def _(tile):
                part = pl.ds(pl.multiple_of(tile * TILE, TILE), TILE)
                terms[odd, :, part] = dot_cols(x, sum_weight[part, :])

            line.sum_start(piece, term_of(odd))

        def own_step(piece):
            total[...] = terms[1 - odd, pl.ds(pl.multiple_of(me * own, own), own), :]
            line.sum_end(piece, total)
            view(piece, me)[...] = row_step(piece, total, row_inputs, row_outputs)
            line.spread_start(piece)

        late(5, use)
        late(3, lambda piece: line.spread_onward(piece, 2))
        late(1, lambda piece: line.sum_onward(piece, term_of(1 - odd), [1]))
        late(0, form)
        late(4, lambda piece: [line.spread_onward(piece, i) for i in range(3, count)])
        late(2, lambda piece: line.spread_onward(piece, 1))
        late(0, lambda piece: line.sum_onward(piece, term_of(odd), range(count - 2, 1, -1)))
        late(1, own_step)

    line.sum_finish(PIECES)
    line.spread_finish(PIECES)


def relay(
    x, sum_weight, use_weight, row_inputs, row_step, row_shapes, use_inputs, use_step, use_shapes,
    collective_id, name,
):
    count = lax.axis_size("tp")
    rows = x.shape[0]
    width = sum_weight.shape[0]
    height = rows // PIECES
    own = height // count
    shared = use_weight is None
    operands = [x, sum_weight, *([] if shared else [use_weight]), *row_inputs, *use_inputs]
    shapes = [jax.ShapeDtypeStruct((rows, width), jnp.bfloat16), *row_shapes, *use_shapes]
    sums, spreads = line_semaphores(count, PIECES)
    sizes = (len(row_inputs), len(use_inputs), len(row_shapes), len(use_shapes), shared)
    return pl.pallas_call(
        functools.partial(relay_kernel, count, row_step, use_step, sizes),
        out_shape=shapes,
        in_specs=[pl.BlockSpec(memory_space=pltpu.VMEM)] * len(operands),
        out_specs=[pl.BlockSpec(memory_space=pltpu.VMEM)] * len(shapes),
        scratch_shapes=[
            pltpu.VMEM((2, height, width), jnp.float32),
            pltpu.VMEM((own, width), jnp.float32),
            pltpu.VMEM((PIECES, count + 1, own, width), jnp.bfloat16),
            *sums,
            *spreads,
        ],
        compiler_params=pltpu.CompilerParams(
            collective_id=collective_id, has_side_effects=True, vmem_limit_bytes=60 << 20
        ),
        cost_estimate=pl.CostEstimate(
            flops=100_000_000_000, bytes_accessed=64 * rows * width, transcendentals=0
        ),
        name=name,
    )(*operands)


def own_rows_of(piece, like):
    own = like.shape[0] // PIECES
    return pl.ds(pl.multiple_of(piece * own, own), own)


def first_norm_step(piece, total, inputs, outputs):
    tokens, gains, biases = inputs
    first_norm, normed_one, inverse_one = outputs
    part = own_rows_of(piece, tokens)
    summed = tokens[part, :].astype(jnp.float32) + (total[...] + biases[0:1, :])
    normed, inverse = norm_parts(summed)
    result = normed * gains[0:1, :] + biases[1:2, :]
    first_norm[part, :] = result
    normed_one[part, :] = normed
    inverse_one[part, :] = jnp.broadcast_to(inverse, (inverse.shape[0], 128))
    return result.astype(jnp.bfloat16)


def expand_step(rows, chunk, weight, inputs, outputs):
    (bias,) = inputs
    hidden, activated = outputs

    @pl.loop(0, hidden.shape[1] // TILE)
    def _(tile):
        part = pl.ds(pl.multiple_of(tile * TILE, TILE), TILE)
        values = dot_plain(chunk, weight[:, part]) + bias[:, part]
        hidden[rows, part] = values
        activated[rows, part] = gelu_tanh(values).astype(jnp.bfloat16)


def add_sums(piece, sums, *values):
    @pl.when(piece == 0)
    def _():
        sums[...] = jnp.zeros_like(sums)

    for i, value in enumerate(values):
        sums[i : i + 1, :] += jnp.sum(value, axis=0, keepdims=True)


def second_norm_step(piece, total, inputs, outputs):
    first_norm, out_grad, gains, biases = inputs
    mixed, grad_second, sums = outputs
    part = own_rows_of(piece, first_norm)
    normed, inverse = norm_parts(first_norm[part, :] + total[...] + biases[2:3, :])
    result = (normed * gains[1:2, :] + biases[3:4, :]).astype(jnp.bfloat16)
    count, _, width = mixed.shape
    for i in range(count):
        mixed[i, part, :] = result[:, i * width : (i + 1) * width]
    upstream = jnp.concatenate([out_grad[i, part, :] for i in range(count)], axis=1)
    upstream = upstream.astype(jnp.float32)
    grad = norm_back(upstream, normed, inverse, gains[1:2, :])
    grad_second[part, :] = grad
    low = grad.astype(jnp.bfloat16)
    add_sums(piece, sums, upstream * normed, upstream, low.astype(jnp.float32))
    return low


def gelu_slope(values):
    scale = math.sqrt(2.0 / math.pi)
    square = values * values
    bend = jnp.tanh(scale * values * (1.0 + 0.044715 * square))
    inner = scale * (1.0 + 3 * 0.044715 * square)
    return 0.5 * (1.0 + bend) + 0.5 * values * (1.0 - bend * bend) * inner


def shrink_step(rows, chunk, weight, inputs, outputs):
    (hidden,) = inputs
    hidden_low, sums = outputs

    @pl.when(rows.start == 0)
    def _():
        sums[...] = jnp.zeros_like(sums)

    @pl.loop(0, hidden.shape[1] // TILE)
    def _(tile):
        part = pl.ds(pl.multiple_of(tile * TILE, TILE), TILE)
        grad = dot_plain(chunk, weight[:, part]) * gelu_slope(hidden[rows, part])
        low = grad.astype(jnp.bfloat16)
        hidden_low[rows, part] = low
        sums[0:1, part] += jnp.sum(low.astype(jnp.float32), axis=0, keepdims=True)


def first_back_step(piece, total, inputs, outputs):
    grad_second, normed_one, inverse_one, gains = inputs
    grad_inner, sums = outputs
    part = own_rows_of(piece, grad_second)
    normed = normed_one[part, :]
    grad_first = grad_second[part, :] + total[...]
    grad = norm_back(grad_first, normed, inverse_one[part, 0:1], gains[0:1, :])
    grad_inner[part, :] = grad
    low = grad.astype(jnp.bfloat16)
    add_sums(piece, sums, grad_first * normed, grad_first, low.astype(jnp.float32))
    return low


def attended_step(rows, chunk, weight, inputs, outputs):
    (attended_grad,) = outputs
    attended_grad[rows, :] = dot_plain(chunk, weight[...]).astype(jnp.bfloat16)


class PlaneSum:
    def __init__(self, parts, core_slots, first_slots, last_slots, sent, got):
        self.parts, self.core_slots = parts, core_slots
        self.first_slots, self.last_slots = first_slots, last_slots
        self.sent, self.got = sent, got
        self.fsdp, self.ctx = lax.axis_index("fsdp"), lax.axis_index("ctx")
        self.twin = self.fsdp + 1 - 2 * lax.rem(self.fsdp, 2)
        self.height = parts.shape[0] // 8
        self.half = parts.shape[1] // 2

    def number(self, fsdp, over_x, over_y):
        chip = lax.rem(fsdp + 2 * over_x, 4)
        return chip * 2 + (1 - self.ctx if over_y else self.ctx)

    def rows(self, number):
        return pl.ds(pl.multiple_of(number * self.height, self.height), self.height)

    def view(self, over_x, over_y, side):
        columns = pl.ds(side * self.half, self.half)
        return self.parts.at[self.rows(self.number(self.fsdp, over_x, over_y)), columns]

    def copy(self, number, source, place, peer):
        return pltpu.make_async_remote_copy(
            src_ref=source,
            dst_ref=place,
            send_sem=self.sent.at[number],
            recv_sem=self.got.at[number],
            device_id=peer,
            device_id_type=MESH,
        )

    def core_copy(self, number):
        over_x, over_y = number // 2, number % 2
        source = self.parts.at[self.rows(self.number(self.twin, over_x, over_y))]
        place = self.core_slots.at[self.rows(number)]
        return self.copy(number, source, place, {"fsdp": self.twin})

    def x_peer(self):
        return {"fsdp": lax.rem(self.fsdp + 2, 4)}

    def y_peer(self):
        return {"ctx": 1 - self.ctx}

    def first_copy(self, number):
        slot = self.first_slots.at[number]
        if number < 2:
            return self.copy(4 + number, self.view(1, number, 0), slot, self.x_peer())
        return self.copy(4 + number, self.view(number - 2, 1, 1), slot, self.y_peer())

    def last_copy(self, side):
        slot = self.last_slots.at[side]
        if side == 0:
            return self.copy(8, self.view(0, 1, 0), slot, self.y_peer())
        return self.copy(9, self.view(1, 0, 1), slot, self.x_peer())

    def bands(self, action):
        band = min(self.height, 32)

        @pl.loop(0, self.height // band)
        def _(i):
            action(pl.ds(pl.multiple_of(i * band, band), band))

    def add(self, view, slot):
        def band(part):
            total = view[part, :].astype(jnp.float32) + slot[part, :].astype(jnp.float32)
            view[part, :] = total.astype(view.dtype)

        self.bands(band)

    def start(self):
        for number in (3, 2, 1, 0):
            self.core_copy(number).start()

    def second(self):
        for number in (3, 2, 1, 0):
            self.core_copy(number).wait_recv()
            shard = self.parts.at[self.rows(self.number(self.fsdp, number // 2, number % 2))]
            self.add(shard, self.core_slots.at[self.rows(number)])
            if number == 3:
                self.first_copy(1).start()
                self.first_copy(3).start()
            if number == 2:
                self.first_copy(0).start()
            if number == 1:
                self.first_copy(2).start()

    def third(self):
        self.first_copy(1).wait_recv()
        self.add(self.view(0, 1, 0), self.first_slots.at[1])
        self.last_copy(0).start()
        self.first_copy(3).wait_recv()
        self.add(self.view(1, 0, 1), self.first_slots.at[3])
        self.last_copy(1).start()

    def finish(self, put):
        for side in range(2):
            self.first_copy(2 * side).wait_recv()
            self.last_copy(side).wait_recv()
            view, first, last = self.view(0, 0, side), self.first_slots, self.last_slots

            def band(part, side=side, view=view):
                total = view[part, :].astype(jnp.float32)
                total += first[2 * side, part, :].astype(jnp.float32)
                put(side, part, total + last[side, part, :].astype(jnp.float32))

            self.bands(band)
        for number in range(4):
            self.core_copy(number).wait_send()
            self.first_copy(number).wait_send()
        for side in range(2):
            self.last_copy(side).wait_send()

    @staticmethod
    def scratch(shards, height, width):
        return [
            pltpu.VMEM((shards * height, width), jnp.bfloat16),
            pltpu.VMEM((4 * height, width), jnp.bfloat16),
            *PlaneSum.slots(height, width),
        ]

    @staticmethod
    def slots(height, width):
        return [
            pltpu.VMEM((4, height, width // 2), jnp.bfloat16),
            pltpu.VMEM((2, height, width // 2), jnp.bfloat16),
            pltpu.SemaphoreType.DMA((10,)),
            pltpu.SemaphoreType.DMA((10,)),
        ]


def middle_kernel(
    count, heads_ref, output_weight, expand_shard, shrink_shard, own_tokens, out_grad, gains,
    biases, hidden_bias,
    attended, mixed, inner, branch_out, grad_heads, first_sums, second_sums, hidden_sums,
    shrink_out, expand_out,
    expand_weight, shrink_weight, gathered, activated, slope, normed_one, inverse_one,
    terms, total, slots, stage, expand_stage, first_slots, last_slots, plane_sent, plane_got,
    sum_sent, sum_got, spread_sent, spread_got, expand_sent, expand_got, shrink_sent, shrink_got,
    in_sent, in_got, out_sent, out_got, put_done, branch_done, product_done, ready,
):
    me, ctx = lax.axis_index("tp"), lax.axis_index("ctx")
    rows, width = gathered.shape[0] // 3, gathered.shape[1]
    half = heads_ref.shape[1]
    height = rows // PIECES
    own = height // count
    shard, hidden = width // PIECES, activated.shape[1]
    pieces = 3 * PIECES

    def piece_rows(piece, start=0):
        return pl.ds(pl.multiple_of(start + piece * height, height), height)

    def view(piece, owner):
        return gathered.at[pl.ds(pl.multiple_of(piece * height + owner * own, own), own)]

    line = Line(me, count, slots, sum_sent, sum_got, view, spread_sent, spread_got)
    expand_gather = PlaneGather(expand_weight, expand_sent, expand_got)
    shrink_gather = PlaneGather(shrink_weight, shrink_sent, shrink_got)
    own_half = pl.ds(pl.multiple_of(ctx * half, half), half)
    own_block = pl.ds(pl.multiple_of(ctx * rows, rows), rows)
    puts = [
        pltpu.make_async_copy(source, place, put_done.at[i])
        for i, (source, place) in enumerate(
            (
                (heads_ref.at[own_block], attended.at[:, own_half]),
                (expand_shard, expand_gather.shard(expand_gather.fsdp, ctx)),
                (shrink_shard, shrink_gather.shard(shrink_gather.fsdp, ctx)),
            )
        )
    ]
    for put in puts:
        put.start()
    swap_in = Swap(
        in_sent, in_got,
        lambda piece: heads_ref.at[piece_rows(piece, (1 - ctx) * rows)],
        lambda piece: attended.at[piece_rows(piece), own_half],
    )
    swap_out = Swap(
        out_sent, out_got,
        lambda piece: stage.at[piece_rows(piece)],
        lambda piece: grad_heads.at[piece_rows(piece, ctx * rows)],
    )
    greet(me, count, expand_gather.peers())
    pl.loop(0, PIECES)(swap_in.start)
    for put in puts:
        put.wait()
    expand_gather.first()

    def branch_copy(piece):
        part = piece_rows(piece)
        return pltpu.make_async_copy(
            gathered.at[piece_rows(piece, 2 * rows)], branch_out.at[part], branch_done.at[piece]
        )

    def in_stage(piece, number):
        return (piece >= number * PIECES) & (piece < (number + 1) * PIECES)

    def tiles(extent, action):
        @pl.loop(0, extent // TILE)
        def _(tile):
            action(pl.ds(pl.multiple_of(tile * TILE, TILE), TILE))

    def use(piece):
        line.sum_sent_all(piece)
        part = piece_rows(lax.rem(piece, PIECES))
        chunk_rows = piece_rows(piece)

        @pl.when(in_stage(piece, 0))
        def _():
            chunk = gathered[chunk_rows, :]

            def expand(columns):
                values = dot_plain(chunk, expand_weight[:, columns]) + hidden_bias[:, columns]
                result, bend = gelu_with_slope(values)
                activated[part, columns] = result.astype(jnp.bfloat16)
                slope[part, columns] = bend.astype(jnp.bfloat16)

            tiles(activated.shape[1], expand)

        @pl.when(in_stage(piece, 1))
        def _():
            chunk = gathered[chunk_rows, :]

            def shrink(columns):
                grad = dot_plain(chunk, shrink_weight[:, columns])
                low = (grad * slope[part, columns].astype(jnp.float32)).astype(jnp.bfloat16)
                slope[part, columns] = low
                added = jnp.sum(low.astype(jnp.float32), axis=0, keepdims=True)
                before = jnp.where(piece == PIECES, 0.0, hidden_sums[0:1, columns])
                hidden_sums[0:1, columns] = before + added

            tiles(slope.shape[1], shrink)

        @pl.when(in_stage(piece, 2))
        def _():
            place = piece - 2 * PIECES
            result = dot_plain(gathered[chunk_rows, :], output_weight[...]).astype(jnp.bfloat16)
            here = ctx == 0
            left, right = result[:, :half], result[:, half:]
            stage[part, :] = jnp.where(here, right, left)
            swap_out.start(place)
            grad_heads[piece_rows(place, ctx * rows), :] = jnp.where(here, left, right)
            branch_copy(place).start()

    def form(piece):
        part = piece_rows(lax.rem(piece, PIECES))
        parity = lax.rem(piece, 2)

        def products(x, weight):
            def product(columns):
                terms[parity, :, columns] = dot_cols(x, weight[columns, :])

            tiles(width, product)

        @pl.when(in_stage(piece, 0))
        def _():
            swap_in.wait_arrival(piece)
            products(attended[part, :], output_weight)

        @pl.when(in_stage(piece, 1))
        def _():
            products(activated[part, :], shrink_weight)

        @pl.when(in_stage(piece, 2))
        def _():
            products(slope[part, :], expand_weight)

        line.sum_start(piece, term_of(piece))

    def term_of(piece):
        parity = lax.rem(piece, 2)
        return lambda owner: terms[parity, pl.ds(pl.multiple_of(owner * own, own), own), :]

    def own_step(piece):
        place = lax.rem(piece, PIECES)
        total[...] = term_of(piece)(me)
        line.sum_end(piece, total)

        @pl.when(in_stage(piece, 0))
        def _():
            view(piece, me)[...] = first_norm_step(
                place, total, (own_tokens, gains, biases), (inner, normed_one, inverse_one)
            )

        @pl.when(in_stage(piece, 1))
        def _():
            view(piece, me)[...] = second_norm_step(
                place, total, (inner, out_grad, gains, biases), (mixed, inner, second_sums)
            )

        @pl.when(in_stage(piece, 2))
        def _():
            view(piece, me)[...] = first_back_step(
                place, total, (inner, normed_one, inverse_one, gains), (inner, first_sums)
            )

        line.spread_start(piece)

    def gradient(number, left_start, right, place):
        columns = pl.ds(pl.multiple_of(number * shard, shard), shard)
        left = gathered[left_start : left_start + rows, columns].T

        def product(part):
            place[:, part] = dot_plain(left, right[:, part]).astype(place.dtype)

        tiles(place.shape[1], product)

    def expand_copy(number):
        part = pl.ds(pl.multiple_of(number * shard, shard), shard)
        return pltpu.make_async_copy(expand_stage, expand_out.at[part], product_done)

    def expand_step(number):
        pl.when(number > 0)(lambda: expand_copy(number - 1).wait())
        gradient(number, 0, slope, expand_stage)
        expand_copy(number).start()

    plane_sum = PlaneSum(shrink_weight, activated, first_slots, last_slots, plane_sent, plane_got)
    twin = {"fsdp": plane_sum.twin}

    def shrink_step(number):
        pl.when(number == 0)(shrink_gather.wait_sent)
        fsdp = jnp.where(number < 2, plane_sum.twin, plane_sum.fsdp)
        for over_y in (1, 0):
            owner = plane_sum.number(fsdp, 1 - lax.rem(number, 2), over_y)
            gradient(owner, rows, activated, shrink_weight.at[plane_sum.rows(owner)])

        @pl.when(number == 3)
        def _():
            pl.semaphore_signal(ready, inc=1, device_id=twin, device_id_type=MESH)

    def shrink_send(_):
        pl.semaphore_wait(ready, 1)
        plane_sum.start()

    def shrink_total(side):
        return pltpu.make_async_copy(
            terms.at[side], shrink_out.at[pl.ds(side * height, height)], put_done.at[side]
        )

    @pl.loop(0, pieces + 5)
    def _(step):
        def late(number, action, most=pieces):
            @pl.when((step >= number) & (step < most + number))
            def _():
                action(step - number)

        pl.when(step == 5)(expand_gather.last)
        pl.when(step == 2 * PIECES + 9)(plane_sum.second)
        pl.when(step == 2 * PIECES + 12)(plane_sum.third)
        late(5, use)
        late(3, lambda piece: line.spread_onward(piece, 2))
        late(1, lambda piece: line.sum_onward(piece, term_of(piece), [1]))
        pl.when(step == PIECES)(shrink_gather.last)
        late(0, form)
        late(4, lambda piece: [line.spread_onward(piece, i) for i in range(3, count)])
        late(2, lambda piece: line.spread_onward(piece, 1))
        late(2 * PIECES + 4, shrink_step, 4)
        late(2 * PIECES + 5, expand_step, PIECES)
        late(2 * PIECES + 8, shrink_send, 1)
        late(0, lambda piece: line.sum_onward(piece, term_of(piece), range(count - 2, 1, -1)))
        late(1, own_step)

        @pl.when(step == 3)
        def _():
            expand_gather.second()
            shrink_gather.first()

        pl.when(step == 4)(expand_gather.third)
        pl.when(step == 6)(shrink_gather.second)
        pl.when(step == 7)(shrink_gather.third)

    expand_copy(PIECES - 1).wait()

    def put_total(side, part, values):
        columns = pl.ds(side * (hidden // 2), hidden // 2)
        start = pl.multiple_of(lax.rem(part.start, height), values.shape[0])
        terms[part.start // height, pl.ds(start, values.shape[0]), columns] = values

    plane_sum.finish(put_total)
    for side in range(2):
        shrink_total(side).start()
    for side in range(2):
        shrink_total(side).wait()

    @pl.loop(0, PIECES)
    def _(piece):
        branch_copy(piece).wait()
        swap_in.wait_sent(piece)
        swap_out.wait_arrival(piece)
        swap_out.wait_sent(piece)

    expand_gather.wait_sent()
    line.spread_finish(pieces)


def gelu_with_slope(values):
    scale = math.sqrt(2.0 / math.pi)
    square = values * values
    bend = 0.5 * jnp.tanh(scale * values * (1.0 + 0.044715 * square)) + 0.5
    inner = (2 * scale) * (1.0 + 3 * 0.044715 * square)
    result = values * bend
    return result, bend + result * (1.0 - bend) * inner


def middle(
    attended_heads, output_weight, expand_shard, shrink_shard, own_tokens, out_grad, gains, biases,
    hidden_bias, collective_id,
):
    count = lax.axis_size("tp")
    rows = attended_heads.shape[0] // 2
    half = attended_heads.shape[1]
    own_rows, width = own_tokens.shape
    hidden = expand_shard.shape[1]
    height = rows // PIECES
    own = height // count
    shard = width // PIECES
    low = jnp.bfloat16
    vmem, anywhere = pl.BlockSpec(memory_space=pltpu.VMEM), pl.BlockSpec(memory_space=pl.ANY)

    def shape(extent, kind=jnp.float32):
        return jax.ShapeDtypeStruct(extent, kind)

    return pl.pallas_call(
        functools.partial(middle_kernel, count),
        out_shape=[
            shape((rows, 2 * half), low),
            shape(out_grad.shape, low),
            shape((own_rows, width)),
            shape((rows, width), low),
            shape((2 * rows, half), low),
            shape((8, width)),
            shape((8, width)),
            shape((8, hidden)),
            shape((shard, hidden)),
            shape((width, hidden), low),
        ],
        in_specs=[anywhere, vmem, anywhere, anywhere, vmem, vmem, vmem, vmem, vmem],
        out_specs=[vmem, vmem, vmem, anywhere, vmem, vmem, vmem, vmem, anywhere, anywhere],
        scratch_shapes=[
            pltpu.VMEM((width, hidden), low),
            pltpu.VMEM((width, hidden), low),
            pltpu.VMEM((3 * rows, width), low),
            pltpu.VMEM((rows, hidden), low),
            pltpu.VMEM((rows, hidden), low),
            pltpu.VMEM((own_rows, width), jnp.float32),
            pltpu.VMEM((own_rows, 128), jnp.float32),
            pltpu.VMEM((2, height, width), jnp.float32),
            pltpu.VMEM((own, width), jnp.float32),
            pltpu.VMEM((PIECES, count + 1, own, width), low),
            pltpu.VMEM((rows, half), low),
            pltpu.VMEM((shard, hidden), low),
            *PlaneSum.slots(shard, hidden),
            *line_semaphores(count, PIECES)[0],
            *line_semaphores(count, 3 * PIECES)[1],
            *[pltpu.SemaphoreType.DMA((9,))] * 4,
            *[pltpu.SemaphoreType.DMA((PIECES,))] * 4,
            pltpu.SemaphoreType.DMA((3,)),
            pltpu.SemaphoreType.DMA((PIECES,)),
            pltpu.SemaphoreType.DMA,
            pltpu.SemaphoreType.REGULAR,
        ],
        compiler_params=pltpu.CompilerParams(
            collective_id=collective_id, has_side_effects=True, vmem_limit_bytes=62 << 20
        ),
        cost_estimate=pl.CostEstimate(
            flops=300_000_000_000, bytes_accessed=192 * rows * width, transcendentals=0
        ),
        name="middle",
    )(
        attended_heads, output_weight, expand_shard, shrink_shard, own_tokens, out_grad, gains,
        biases, hidden_bias,
    )


def peers_in_plane(sizes):
    fsdp, ctx = lax.axis_index("fsdp"), lax.axis_index("ctx")
    return [
        {"fsdp": lax.rem(fsdp + i, sizes[0]), "ctx": lax.rem(ctx + j, sizes[1])}
        for i in range(sizes[0])
        for j in range(sizes[1])
        if i or j
    ]


def input_kernel(
    sizes, x_ref, weight, inner_ref, rows_ref, hidden_ref, out_ref, vectors_ref,
    term_ref, total, slots, own_vectors, tp_slots, plane_slots,
    sum_sent, sum_got, tp_sent, tp_got, plane_sent, plane_got, hooks=None,
):
    count = sizes[2]
    me = lax.axis_index("tp")
    height = x_ref.shape[0] // PIECES
    own = height // count
    width = out_ref.shape[1]
    line = Line(me, count, slots, sum_sent, sum_got, None, None, None)
    tp_peers, plane_peers = peers_along_tp(me, count), peers_in_plane(sizes)
    greet_peers(tp_peers + plane_peers)

    def own_part(index):
        return rows_ref.at[:, pl.ds(pl.multiple_of(index * width, width), width)]

    over_tp = Exchange(
        tp_peers, tp_sent, tp_got,
        lambda i: own_part(lax.rem(me + i, count)), lambda i: tp_slots.at[i],
    )
    over_plane = Exchange(
        plane_peers, plane_sent, plane_got, lambda _: own_vectors, lambda i: plane_slots.at[i]
    )
    opening, before, after, closing = hooks or (lambda *_: None,) * 4
    opening()
    over_tp.start()

    def terms(piece):
        def term(owner):
            features = pl.ds(pl.multiple_of(owner * width, width), width)
            term_ref[...] = dot_cols(
                x_ref[pl.ds(pl.multiple_of(piece * height, height), height), :],
                weight[features, :],
            )
            inner = inner_ref[pl.ds(pl.multiple_of(piece * own, own), own), features]
            term_ref[pl.ds(pl.multiple_of(me * own, own), own), :] += inner
            return term_ref[...]

        return term

    def pack():
        over_tp.wait_arrivals()
        own_vectors[0:8, :] = own_part(me)[...]
        for i in range(count - 1):
            own_vectors[0:8, :] += tp_slots[i]
        own_vectors[8:, :] = jnp.zeros_like(own_vectors[8:, :])
        hidden_rows = hidden_ref.shape[1] // width
        for i in range(hidden_rows):
            own_vectors[8 + i : 9 + i, :] = hidden_ref[0:1, i * width : (i + 1) * width]
        for i in range(x_ref.shape[1] // width):
            part = x_ref[:, i * width : (i + 1) * width].astype(jnp.float32)
            place = 8 + hidden_rows + i
            own_vectors[place : place + 1, :] = jnp.sum(part, axis=0, keepdims=True)
        over_plane.start()

    @pl.loop(0, PIECES)
    def _(piece):
        before(piece)
        line.sum_start(piece, terms(piece))
        line.sum_onward(piece, terms(piece), range(count - 2, 0, -1))
        after(piece)

    pack()
    closing()

    @pl.loop(0, PIECES)
    def _(piece):
        total[...] = terms(piece)(me)
        line.sum_end(piece, total)
        rows = pl.ds(pl.multiple_of(piece * height, height), height)
        out_ref[rows, :] = total[...].astype(out_ref.dtype)

    over_plane.wait_arrivals()
    vectors_ref[...] = own_vectors[...]
    for i in range(len(plane_peers)):
        vectors_ref[...] += plane_slots[i]
    over_tp.wait_sent()
    over_plane.wait_sent()
    line.sum_finish(PIECES)


def input_sum(x, weight, inner, row_sums, hidden_sums, collective_id):
    sizes = tuple(lax.axis_size(axis) for axis in ("fsdp", "ctx", "tp"))
    count = sizes[2]
    others = sizes[0] * sizes[1] - 1
    rows = x.shape[0]
    width = weight.shape[0] // count
    height = rows // PIECES
    packed = 8 + -(-(hidden_sums.shape[1] + x.shape[1]) // (8 * width)) * 8
    return pl.pallas_call(
        functools.partial(input_kernel, sizes),
        out_shape=[
            jax.ShapeDtypeStruct((rows, width), jnp.bfloat16),
            jax.ShapeDtypeStruct((packed, width), jnp.float32),
        ],
        in_specs=[pl.BlockSpec(memory_space=pltpu.VMEM)] * 5,
        out_specs=[pl.BlockSpec(memory_space=pltpu.VMEM)] * 2,
        scratch_shapes=[
            pltpu.VMEM((height, width), jnp.float32),
            pltpu.VMEM((height, width), jnp.float32),
            pltpu.VMEM((PIECES, count + 1, height, width), jnp.bfloat16),
            pltpu.VMEM((packed, width), jnp.float32),
            pltpu.VMEM((count - 1, 8, width), jnp.float32),
            pltpu.VMEM((others, packed, width), jnp.float32),
            *line_semaphores(count, PIECES)[0],
            pltpu.SemaphoreType.DMA((count - 1,)),
            pltpu.SemaphoreType.DMA((count - 1,)),
            pltpu.SemaphoreType.DMA((others,)),
            pltpu.SemaphoreType.DMA((others,)),
        ],
        compiler_params=pltpu.CompilerParams(
            collective_id=collective_id, has_side_effects=True, vmem_limit_bytes=40 << 20
        ),
        cost_estimate=pl.CostEstimate(
            flops=60_000_000_000, bytes_accessed=64 * rows * width, transcendentals=0
        ),
        name="input_sum",
    )(x, weight, inner, row_sums, hidden_sums)


def leave_kernel(
    sizes, grads_ref, tokens_ref, weight, inner_ref, rows_ref, hidden_ref, branch_ref, attended_ref,
    out_ref, vectors_ref, query_out, key_out, value_out, output_out,
    x_ref, term_ref, total, slots, own_vectors, tp_slots, plane_slots,
    sum_sent, sum_got, tp_sent, tp_got, plane_sent, plane_got, swap_sent, swap_got, *sum_scratch,
):
    count = sizes[2]
    me, ctx = lax.axis_index("tp"), lax.axis_index("ctx")
    rows = x_ref.shape[0]
    height = rows // PIECES
    part = grads_ref.shape[1]
    plane_sum, output_sum = PlaneSum(*sum_scratch[:6]), PlaneSum(*sum_scratch[6:])
    shard = plane_sum.height

    def piece_rows(piece, start=0):
        return pl.ds(pl.multiple_of(start + piece * height, height), height)

    own_columns = pl.ds(pl.multiple_of(ctx * part, part), part)
    swap = Swap(
        swap_sent, swap_got,
        lambda piece: grads_ref.at[piece_rows(piece, (1 - ctx) * rows)],
        lambda piece: x_ref.at[piece_rows(piece), own_columns],
    )

    def products(sums, fsdp, left, right):
        for over_x in (1, 0):
            for over_y in (1, 0):
                number = sums.number(fsdp, over_x, over_y)
                columns = pl.ds(pl.multiple_of(number * shard, shard), shard)
                product = dot_rows(left[:, columns], right[...])
                sums.parts[sums.rows(number), :] = product.astype(jnp.bfloat16)

    def opening():
        @pl.loop(0, PIECES)
        def _(piece):
            swap.start(piece)

        products(output_sum, output_sum.twin, branch_ref, attended_ref)
        output_sum.start()
        x_ref[:, own_columns] = grads_ref[pl.ds(pl.multiple_of(ctx * rows, rows), rows), :]
        products(output_sum, output_sum.fsdp, branch_ref, attended_ref)
        output_sum.second()

    last = PIECES - 1
    begin = jnp.where((me == 0) | (me == count - 1), last, 2)

    def before(piece):
        @pl.when(piece <= begin)
        def _():
            swap.wait_arrival(piece)

    def after(piece):
        @pl.when(piece == begin)
        def _():
            @pl.loop(begin + 1, PIECES)
            def _(other):
                swap.wait_arrival(other)

            products(plane_sum, plane_sum.twin, tokens_ref, x_ref)
            plane_sum.start()

        @pl.when(piece == jnp.minimum(begin + 1, last))
        def _():
            products(plane_sum, plane_sum.fsdp, tokens_ref, x_ref)

        pl.when(piece == jnp.minimum(begin + 2, last))(plane_sum.second)
        pl.when(piece == jnp.minimum(begin + 3, last))(output_sum.third)

    def closing():
        plane_sum.third()

    input_kernel(
        sizes, x_ref, weight, inner_ref, rows_ref, hidden_ref, out_ref, vectors_ref,
        term_ref, total, slots, own_vectors, tp_slots, plane_slots,
        sum_sent, sum_got, tp_sent, tp_got, plane_sent, plane_got,
        hooks=(opening, before, after, closing),
    )
    third = part // 3

    def put_part(side, rows, values):
        for i, ref in enumerate((query_out, key_out, value_out)):
            ref[rows, side * third : (side + 1) * third] = values[:, i * third : (i + 1) * third]

    def put_output(side, rows, values):
        output_out[rows, side * output_sum.half : (side + 1) * output_sum.half] = values

    plane_sum.finish(put_part)
    output_sum.finish(put_output)

    @pl.loop(0, PIECES)
    def _(piece):
        swap.wait_sent(piece)


def leave(grads, tokens, weight, inner, row_sums, hidden_sums, branch, attended, collective_id):
    sizes = tuple(lax.axis_size(axis) for axis in ("fsdp", "ctx", "tp"))
    count = sizes[2]
    others = sizes[0] * sizes[1] - 1
    rows, features = tokens.shape
    part = grads.shape[1]
    width = features // count
    height = rows // PIECES
    shard = features // (others + 1)
    packed = 8 + -(-(hidden_sums.shape[1] + 2 * part) // (8 * width)) * 8
    return pl.pallas_call(
        functools.partial(leave_kernel, sizes),
        out_shape=[
            jax.ShapeDtypeStruct((rows, width), jnp.bfloat16),
            jax.ShapeDtypeStruct((packed, width), jnp.float32),
            *[jax.ShapeDtypeStruct((shard, 2 * part // 3), jnp.float32)] * 4,
        ],
        in_specs=[pl.BlockSpec(memory_space=pltpu.VMEM)] * 8,
        out_specs=[pl.BlockSpec(memory_space=pltpu.VMEM)] * 6,
        scratch_shapes=[
            pltpu.VMEM((rows, 2 * part), jnp.bfloat16),
            pltpu.VMEM((height, width), jnp.float32),
            pltpu.VMEM((height, width), jnp.float32),
            pltpu.VMEM((PIECES, count + 1, height, width), jnp.bfloat16),
            pltpu.VMEM((packed, width), jnp.float32),
            pltpu.VMEM((count - 1, 8, width), jnp.float32),
            pltpu.VMEM((others, packed, width), jnp.float32),
            *line_semaphores(count, PIECES)[0],
            pltpu.SemaphoreType.DMA((count - 1,)),
            pltpu.SemaphoreType.DMA((count - 1,)),
            pltpu.SemaphoreType.DMA((others,)),
            pltpu.SemaphoreType.DMA((others,)),
            pltpu.SemaphoreType.DMA((PIECES,)),
            pltpu.SemaphoreType.DMA((PIECES,)),
            *PlaneSum.scratch(others + 1, shard, 2 * part),
            *PlaneSum.scratch(others + 1, shard, attended.shape[1]),
        ],
        compiler_params=pltpu.CompilerParams(
            collective_id=collective_id, has_side_effects=True, vmem_limit_bytes=60 << 20
        ),
        cost_estimate=pl.CostEstimate(
            flops=60_000_000_000, bytes_accessed=64 * rows * width, transcendentals=0
        ),
        name="leave",
    )(grads, tokens, weight, inner, row_sums, hidden_sums, branch, attended)


def to_own_rows(wide):
    count = lax.axis_size("tp")
    parts = wide.reshape(PIECES, count, -1, wide.shape[1])
    return lax.dynamic_index_in_dim(parts, lax.axis_index("tp"), 1, keepdims=False).reshape(
        -1, wide.shape[1]
    )


def spread_own(block):
    count = lax.axis_size("tp")
    rows, width = block.shape
    parts = block.reshape(PIECES, count, -1, width).transpose(1, 0, 2, 3)
    return lax.all_to_all(
        parts.reshape(count, -1, width), "tp", split_axis=0, concat_axis=0, tiled=True
    )


def unspread_own(parts):
    count, own_rows, width = parts.shape
    got = lax.all_to_all(parts, "tp", split_axis=0, concat_axis=0, tiled=True)
    return got.reshape(count, PIECES, -1, width).transpose(1, 0, 2, 3).reshape(-1, width)


def body(
    tokens,
    segments,
    query_weight,
    key_weight,
    value_weight,
    output_weight,
    expand_weight,
    shrink_weight,
    query_bias,
    value_bias,
    hidden_bias,
    norm_gains,
    row_biases,
    out_grad,
):
    rows = tokens.shape[0]
    head_cols = query_weight.shape[1]
    heads = head_cols // HD
    plane = ("fsdp", "ctx")
    plane_sizes = tuple(lax.axis_size(axis) for axis in plane)
    by_heads = plane_sizes == (4, 2) and heads % 2 == 0

    def weight_rows(weight):
        return lax.all_gather(weight, plane, axis=0, tiled=True)

    marks = jnp.concatenate(
        [norm_gains, row_biases, jnp.zeros((10, norm_gains.shape[1]), norm_gains.dtype)]
    )
    block_index = lax.axis_index("fsdp") * plane_sizes[1] + lax.axis_index("ctx")
    qkv_bias = jnp.stack([query_bias, jnp.zeros_like(query_bias), value_bias])
    qkv_bias = qkv_bias.astype(jnp.float32)
    if by_heads:
        half_bias = qkv_bias.reshape(3, 2, -1).transpose(1, 0, 2).reshape(1, -1)
        wide_tokens, own_tokens, wide_marks, wide_qkv, full_output, qkv_heads = enter(
            tokens, marks, query_weight, key_weight, value_weight, output_weight, half_bias, 0
        )
        queries = keys = values = qkv_heads
        own_heads = heads // 2
        bounds = (segments.reshape(-1, plane_sizes[1] * rows),)
    else:
        wide_qkv = weight_rows(jnp.concatenate([query_weight, key_weight, value_weight], axis=1))
        wide_tokens, wide_marks = gather_features(tokens, marks, 0)
        own_tokens = to_own_rows(wide_tokens)
        qkv = dot_plain(wide_tokens, wide_qkv) + qkv_bias.reshape(1, -1)
        queries, keys, values = jnp.split(qkv.astype(jnp.bfloat16), 3, axis=1)
        own_heads = heads
        keys, values = padded(keys, WIN), padded(values, WIN)
        ids = jnp.concatenate(
            [
                jnp.full((WIN,), -1, jnp.int32),
                segments,
                jnp.full((WIN,), jnp.iinfo(jnp.int32).max, jnp.int32),
            ]
        )
        full_output, full_expand = weight_rows(output_weight), weight_rows(expand_weight)
        key_ids = lax.dynamic_slice_in_dim(ids, block_index * rows, rows + 2 * WIN, 0)
        bounds = key_bounds(key_ids[WIN : WIN + rows], key_ids, WIN)
    places = (0, own_heads, 2 * own_heads) if by_heads else (0, 0, 0)
    gains = wide_marks[:2].astype(jnp.float32)
    biases = wide_marks[2:6].astype(jnp.float32)
    wide_marks, out_grad = lax.optimization_barrier((wide_marks, out_grad))
    upstream = spread_own(out_grad)
    attended_heads, lse = attend(queries, keys, values, own_heads, bounds, places)
    attended_heads, upstream = lax.optimization_barrier((attended_heads, upstream))

    own_rows, features = own_tokens.shape
    hidden_cols = expand_weight.shape[1]

    def shape(extent, kind=jnp.float32):
        return jax.ShapeDtypeStruct(extent, kind)

    own_shape = shape((own_rows, features))
    def owner_sum(grad):
        return lax.psum_scatter(
            grad, plane, scatter_dimension=0, tiled=True
        )

    if by_heads:
        (
            attended, mixed_own, grad_inner, branch_low, attended_grad,
            first_sums, second_sums, hidden_sums, shrink_grad, expand_part,
        ) = middle(
            attended_heads, full_output, expand_weight, shrink_weight, own_tokens, upstream,
            gains, biases, hidden_bias.astype(jnp.float32)[None], 1,
        )
        expand_grad = owner_sum(expand_part)
        mixed = unspread_own(mixed_own)
        (grads,) = attend_back(
            queries, keys, values, attended_heads, attended_grad, lse, bounds, places, True
        )
        grads, mixed = lax.optimization_barrier((grads, mixed))
    else:
        full_shrink = weight_rows(shrink_weight)
        norm_low, first_norm, normed_one, inverse_one, hidden, activated = relay(
            attended_heads, full_output, full_expand,
            [own_tokens, gains, biases], first_norm_step,
            [own_shape, own_shape, shape((own_rows, 128))],
            [hidden_bias.astype(jnp.float32)[None]], expand_step,
            [shape((rows, hidden_cols)), shape((rows, hidden_cols), jnp.bfloat16)],
            1, "first_norm",
        )
        ffn_low, mixed_own, grad_second, second_sums, hidden_low, hidden_sums = relay(
            activated, full_shrink, None,
            [first_norm, upstream, gains, biases], second_norm_step,
            [shape(upstream.shape, jnp.bfloat16), own_shape, shape((8, features))],
            [hidden], shrink_step,
            [shape((rows, hidden_cols), jnp.bfloat16), shape((8, hidden_cols))],
            2, "second_norm",
        )
        shrink_grad = owner_sum(dot_rows(ffn_low, activated).astype(jnp.bfloat16))
        branch_low, grad_inner, first_sums, attended_grad = relay(
            hidden_low, full_expand, full_output,
            [grad_second, normed_one, inverse_one, gains], first_back_step,
            [own_shape, shape((8, features))],
            [], attended_step,
            [shape((rows, head_cols), jnp.bfloat16)],
            3, "first_back",
        )
        expand_grad = owner_sum(dot_rows(norm_low, hidden_low).astype(jnp.bfloat16))
        output_grad = owner_sum(dot_rows(branch_low, attended_heads).astype(jnp.bfloat16))
        mixed = unspread_own(mixed_own)
        query_low, key_ext, value_ext = attend_back(
            queries, keys, values, attended_heads, attended_grad, lse, bounds
        )

        def fold(ext):
            edges = jnp.concatenate([ext[:WIN], ext[WIN + rows :]], axis=0)
            around = padded(edges, WIN)
            own = ext[WIN : WIN + rows]
            own = own.at[:WIN].add(around[:WIN]).at[rows - WIN :].add(around[3 * WIN :])
            return own.astype(jnp.bfloat16)

        qkv_low = jnp.concatenate([query_low, fold(key_ext), fold(value_ext)], axis=1)
    row_sums = jnp.concatenate(
        [
            first_sums[0:1], second_sums[0:1],
            first_sums[2:3], first_sums[1:2], second_sums[2:3], second_sums[1:2],
            jnp.zeros_like(first_sums[:2]),
        ]
    )
    sides = 2 if by_heads else 1

    def by_kind(columns):
        parts = columns.reshape(-1, sides, 3, head_cols // sides)
        return [parts[:, :, i].reshape(-1, head_cols) for i in range(3)]

    if by_heads:
        input_grad, vectors, query_grad, key_grad, value_grad, output_grad = leave(
            grads, wide_tokens, wide_qkv, grad_inner, row_sums, hidden_sums[:1], branch_low,
            attended, 4,
        )
        input_grad, expand_grad = lax.optimization_barrier((input_grad, expand_grad))
    else:
        input_grad, vectors = input_sum(
            qkv_low, wide_qkv, grad_inner, row_sums, hidden_sums[:1], 4
        )
        qkv_grad = owner_sum(dot_rows(wide_tokens, qkv_low).astype(jnp.bfloat16))
        query_grad, key_grad, value_grad = by_kind(qkv_grad.astype(jnp.float32))
    hidden_rows = hidden_cols // head_cols
    query_sum, _, value_sum = by_kind(
        vectors[8 + hidden_rows : 8 + hidden_rows + 3].reshape(1, -1)
    )
    return (
        mixed,
        input_grad,
        query_grad,
        key_grad,
        value_grad,
        output_grad.astype(jnp.float32),
        expand_grad.astype(jnp.float32),
        shrink_grad.astype(jnp.float32),
        query_sum[0],
        value_sum[0],
        vectors[8 : 8 + hidden_rows].reshape(-1),
        vectors[:2],
        vectors[2:6],
    )


def solution(mesh):
    rows, whole, cols = P(("fsdp", "ctx"), "tp"), P(), P("tp")
    wide = P(None, "tp")
    return jax.shard_map(
        body,
        mesh=mesh,
        in_specs=(rows, whole) + (rows,) * 6 + (cols,) * 3 + (wide,) * 2 + (rows,),
        out_specs=(rows,) * 8 + (cols,) * 3 + (wide,) * 2,
        check_vma=False,
    )
```

```python
import functools
import math

import jax
import jax.numpy as jnp
from jax import lax
from jax.experimental import pallas as pl
from jax.experimental.pallas import tpu as pltpu
from jax.sharding import PartitionSpec as P

HD = 128
WIN = 1024
QB = 512
KB = 512

epsilon = 1e-06
hidden_floor = -1e30
score_scale = 1.0 / math.sqrt(HD)
log2_e = 1.0 / math.log(2.0)


def dot_plain(left, right):
    return jnp.dot(left, right, preferred_element_type=jnp.float32)


def dot_rows(left, right):
    return lax.dot_general(
        left, right, (((0,), (0,)), ((), ())), preferred_element_type=jnp.float32
    )


def dot_cols(left, right):
    return lax.dot_general(
        left, right, (((1,), (1,)), ((), ())), preferred_element_type=jnp.float32
    )


def block_bounds(block, rows, bounds, marks):
    if len(bounds) == 4:
        first, last, low, high = bounds
        return first[block], last[block], last[block], last[block], low[...], high[...]
    (ids,) = bounds
    run = ids.shape[1]

    @pl.when((pl.program_id(0) == 0) & (block == 0))
    def _():
        own = lax.axis_index("fsdp")
        own_ids = ids[pl.ds(own, 1), :]
        for i in range(2):
            marks[i] = jnp.sum((own_ids <= 3 * own + i).astype(jnp.int32))

    second, third = marks[0], marks[1]

    def bounds_at(places):
        start = jnp.where(places < second, 0, jnp.where(places < third, second, third))
        stop = jnp.where(places < second, second, jnp.where(places < third, third, run))
        return jnp.maximum(start, places - WIN), jnp.minimum(stop - 1, places + WIN)

    begin = block * rows
    low, high = bounds_at(begin + lax.broadcasted_iota(jnp.int32, (1, rows), 1))
    least_low, least_high = bounds_at(begin)
    most_low, most_high = bounds_at(begin + rows - 1)
    first, last = least_low // KB, most_high // KB + 1
    whole_first = jnp.minimum((most_low + KB - 1) // KB, last)
    whole_last = jnp.maximum((least_high + 1) // KB, whole_first)
    return first, whole_first, whole_last, last, low, high


def over_key_blocks(step, marks, start):
    first, whole_first, whole_last, last = marks
    carry = lax.fori_loop(first, whole_first, functools.partial(step, True), start)
    carry = lax.fori_loop(whole_first, whole_last, functools.partial(step, False), carry)
    return lax.fori_loop(whole_last, last, functools.partial(step, True), carry)


def bound_operands(bounds):
    if len(bounds) == 4:
        mark_spec = pl.BlockSpec((1, QB), lambda h, i, *_: (0, i))
        return list(bounds[:2]), list(bounds[2:]), [mark_spec, mark_spec]
    shape = bounds[0].shape
    return [], list(bounds), [pl.BlockSpec(shape, lambda h, i, *_: (0, 0))]


def attend_kernel(scalars, *refs):
    bounds = refs[:scalars]
    q_ref, k_ref, v_ref, *arrays, out_ref, lse_ref, vt, marks = refs[scalars:]
    block = pl.program_id(1)
    rows = q_ref.shape[0]

    @pl.when(block == 0)
    def _():
        vt[...] = v_ref[...].T

    queries = q_ref[...]
    *span, low, high = block_bounds(block, rows, (*bounds, *arrays), marks)
    places = lax.broadcasted_iota(jnp.int32, (KB, rows), 0)

    def step(masked, number, carry):
        top, total, mixed = carry
        start = pl.multiple_of(number * KB, KB)
        scores = dot_cols(k_ref[pl.ds(start, KB), :], queries) * (score_scale * log2_e)
        if masked:
            keep = (places >= low - start) & (places <= high - start)
            scores = jnp.where(keep, scores, hidden_floor)
        new_top = jnp.maximum(top, jnp.max(scores, axis=0, keepdims=True))
        shrink = jnp.exp2(top - new_top)
        powers = jnp.exp2(scores - new_top)
        total = total * shrink + jnp.sum(powers, axis=0, keepdims=True)
        mixed = mixed * shrink + dot_plain(vt[:, pl.ds(start, KB)], powers.astype(jnp.bfloat16))
        return new_top, total, mixed

    top, total, mixed = over_key_blocks(
        step,
        span,
        (
            jnp.full((1, rows), hidden_floor, jnp.float32),
            jnp.zeros((1, rows), jnp.float32),
            jnp.zeros((HD, rows), jnp.float32),
        ),
    )
    out_ref[...] = (mixed / total).T.astype(out_ref.dtype)
    lse_ref[...] = (top + jnp.log2(total))[None]


def attend(queries, keys, values, heads, bounds, places=(0, 0, 0)):
    rows, span = queries.shape[0], keys.shape[0]
    width = heads * HD
    q_at, k_at, v_at = places
    scalars, arrays, specs = bound_operands(bounds)
    return pl.pallas_call(
        functools.partial(attend_kernel, len(scalars)),
        out_shape=(
            jax.ShapeDtypeStruct((rows, width), jnp.bfloat16),
            jax.ShapeDtypeStruct((heads, 1, rows), jnp.float32),
        ),
        grid_spec=pltpu.PrefetchScalarGridSpec(
            num_scalar_prefetch=len(scalars),
            grid=(heads, rows // QB),
            in_specs=[
                pl.BlockSpec((QB, HD), lambda h, i, *_: (i, h + q_at)),
                pl.BlockSpec((span, HD), lambda h, i, *_: (0, h + k_at)),
                pl.BlockSpec((span, HD), lambda h, i, *_: (0, h + v_at)),
                *specs,
            ],
            out_specs=[
                pl.BlockSpec((QB, HD), lambda h, i, *_: (i, h)),
                pl.BlockSpec((1, 1, QB), lambda h, i, *_: (h, 0, i)),
            ],
            scratch_shapes=[pltpu.VMEM((HD, span), jnp.bfloat16), pltpu.SMEM((2,), jnp.int32)],
        ),
        compiler_params=pltpu.CompilerParams(vmem_limit_bytes=60 << 20),
        cost_estimate=pl.CostEstimate(
            flops=3 * rows * span * width,
            bytes_accessed=2 * (2 * rows + 2 * span) * width,
            transcendentals=rows * span * heads,
        ),
        name="attend",
    )(*scalars, queries, keys, values, *arrays)


def attend_back_kernel(scalars, arrays, *refs):
    bounds = refs[:scalars]
    q_ref, k_ref, v_ref, o_ref, g_ref, lse_ref, *refs = refs[scalars:]
    bounds = (*bounds, *refs[:arrays])
    *results, kt, dk_sum, dv_sum, marks = refs[arrays:]
    head, block = pl.program_id(0), pl.program_id(1)
    rows = q_ref.shape[0]

    @pl.when(block == 0)
    def _():
        kt[...] = k_ref[...].T
        dk_sum[...] = jnp.zeros_like(dk_sum)
        dv_sum[...] = jnp.zeros_like(dv_sum)

    queries = q_ref[...]
    upstream = g_ref[...]
    lse = lse_ref[0]
    *span, low, high = block_bounds(block, rows, bounds, marks)
    places = lax.broadcasted_iota(jnp.int32, (KB, rows), 0)
    product = upstream.astype(jnp.float32) * o_ref[...].astype(jnp.float32)
    delta = jnp.sum(product.T, axis=0, keepdims=True)

    def step(masked, number, dq):
        start = pl.multiple_of(number * KB, KB)
        window = pl.ds(start, KB)
        scores = dot_cols(k_ref[window, :], queries) * (score_scale * log2_e)
        scores = scores - lse
        if masked:
            keep = (places >= low - start) & (places <= high - start)
            scores = jnp.where(keep, scores, hidden_floor)
        probs = jnp.exp2(scores)
        prob_grad = dot_cols(v_ref[window, :], upstream)
        score_grad = (probs * (prob_grad - delta)).astype(jnp.bfloat16)
        dv_sum[window, :] += dot_plain(probs.astype(jnp.bfloat16), upstream)
        dk_sum[window, :] += dot_plain(score_grad, queries)
        return dq + dot_plain(kt[:, window], score_grad)

    dq = over_key_blocks(step, span, jnp.zeros((HD, rows), jnp.float32))
    dq = (dq * score_scale).T
    if len(results) == 1:
        width = results[0].shape[1] // 3

        def place(part):
            start = pl.multiple_of(part * width + head * HD, HD)
            return results[0].at[:, pl.ds(start, HD)]

        query_place = place(0).at[pl.ds(pl.multiple_of(block * rows, rows), rows)]
        key_place, value_place = place(1), place(2)
    else:
        query_place, key_place, value_place = results
    query_place[...] = dq.astype(query_place.dtype)

    @pl.when(block == pl.num_programs(1) - 1)
    def _():
        key_place[...] = (dk_sum[...] * score_scale).astype(key_place.dtype)
        value_place[...] = dv_sum[...].astype(value_place.dtype)


def attend_back(
    queries, keys, values, out, upstream, lse, bounds, places=(0, 0, 0), merged=False
):
    rows, width = out.shape
    span = keys.shape[0]
    heads = width // HD
    q_at, k_at, v_at = places
    row_spec = pl.BlockSpec((QB, HD), lambda h, i, *_: (i, h))
    key_spec = pl.BlockSpec((span, HD), lambda h, i, *_: (0, h))
    scalars, arrays, specs = bound_operands(bounds)
    return pl.pallas_call(
        functools.partial(attend_back_kernel, len(scalars), len(arrays)),
        out_shape=[jax.ShapeDtypeStruct((rows, 3 * width), jnp.bfloat16)]
        if merged
        else [
            jax.ShapeDtypeStruct((rows, width), jnp.bfloat16),
            jax.ShapeDtypeStruct((span, width), jnp.float32),
            jax.ShapeDtypeStruct((span, width), jnp.float32),
        ],
        grid_spec=pltpu.PrefetchScalarGridSpec(
            num_scalar_prefetch=len(scalars),
            grid=(heads, rows // QB),
            in_specs=[
                pl.BlockSpec((QB, HD), lambda h, i, *_: (i, h + q_at)),
                pl.BlockSpec((span, HD), lambda h, i, *_: (0, h + k_at)),
                pl.BlockSpec((span, HD), lambda h, i, *_: (0, h + v_at)),
                row_spec, row_spec,
                pl.BlockSpec((1, 1, QB), lambda h, i, *_: (h, 0, i)),
                *specs,
            ],
            out_specs=[pl.BlockSpec((rows, 3 * width), lambda h, i, *_: (0, 0))]
            if merged
            else [row_spec, key_spec, key_spec],
            scratch_shapes=[
                pltpu.VMEM((HD, span), jnp.bfloat16),
                pltpu.VMEM((span, HD), jnp.float32),
                pltpu.VMEM((span, HD), jnp.float32),
                pltpu.SMEM((2,), jnp.int32),
            ],
        ),
        compiler_params=pltpu.CompilerParams(vmem_limit_bytes=60 << 20),
        cost_estimate=pl.CostEstimate(
            flops=8 * rows * span * width,
            bytes_accessed=2 * (4 * rows + 4 * span) * width,
            transcendentals=rows * span * heads,
        ),
        name="attend_back",
    )(*scalars, queries, keys, values, out, upstream, lse, *arrays)


def key_bounds(query_ids, key_ids, offset):
    rows, span = query_ids.shape[0], key_ids.shape[0]
    start = jnp.sum(key_ids[:, None] < query_ids[None, :], axis=0, dtype=jnp.int32)
    stop = jnp.sum(key_ids[:, None] <= query_ids[None, :], axis=0, dtype=jnp.int32)
    places = jnp.arange(rows, dtype=jnp.int32) + offset
    low = jnp.maximum(start, places - WIN)
    high = jnp.minimum(stop - 1, places + WIN)
    first = jnp.min(low.reshape(-1, QB), axis=1) // KB
    last = jnp.max(high.reshape(-1, QB), axis=1) // KB + 1
    return first, last, low[None], high[None]


def padded(block, width):
    count = lax.axis_size("ctx")
    forward = [(i, i + 1) for i in range(count - 1)]
    backward = [(target, source) for source, target in forward]
    below = lax.ppermute(block[block.shape[0] - width :], "ctx", forward)
    above = lax.ppermute(block[:width], "ctx", backward)
    return jnp.concatenate([below, block, above], axis=0)


def norm_parts(rows):
    mean = jnp.mean(rows, axis=-1, keepdims=True)
    square = jnp.mean(rows * rows, axis=-1, keepdims=True)
    inverse = lax.rsqrt(square - mean * mean + epsilon)
    return (rows - mean) * inverse, inverse


def norm_back(upstream, normed, inverse, gain):
    scaled = upstream * gain
    first_mean = jnp.mean(scaled, axis=-1, keepdims=True)
    second_mean = jnp.mean(scaled * normed, axis=-1, keepdims=True)
    return inverse * (scaled - first_mean - normed * second_mean)


def gelu_tanh(values):
    return jax.nn.gelu(values, approximate=True)


MESH = pl.DeviceIdType.MESH
PIECES = 8
TILE = 512


def greet(me, count, others=()):
    barrier = pltpu.get_barrier_semaphore()

    @pl.when(me > 0)
    def _():
        pl.semaphore_signal(barrier, inc=1, device_id={"tp": me - 1}, device_id_type=MESH)

    @pl.when(me < count - 1)
    def _():
        pl.semaphore_signal(barrier, inc=1, device_id={"tp": me + 1}, device_id_type=MESH)

    for other in others:
        pl.semaphore_signal(barrier, inc=1, device_id=other, device_id_type=MESH)

    @pl.when((me == 0) | (me == count - 1))
    def _():
        pl.semaphore_wait(barrier, 1 + len(others))

    @pl.when((me > 0) & (me < count - 1))
    def _():
        pl.semaphore_wait(barrier, 2 + len(others))


def peers_along_tp(me, count):
    return [{"tp": lax.rem(me + i, count)} for i in range(1, count)]


def greet_peers(peers):
    barrier = pltpu.get_barrier_semaphore()
    for peer in peers:
        pl.semaphore_signal(barrier, inc=1, device_id=peer, device_id_type=MESH)
    pl.semaphore_wait(barrier, len(peers))


class Exchange:
    def __init__(self, peers, sent, got, source, place):
        self.peers, self.sent, self.got = peers, sent, got
        self.source, self.place = source, place

    def copies(self):
        for i, peer in enumerate(self.peers):
            yield pltpu.make_async_remote_copy(
                src_ref=self.source(i + 1),
                dst_ref=self.place(i),
                send_sem=self.sent.at[i],
                recv_sem=self.got.at[i],
                device_id=peer,
                device_id_type=MESH,
            )

    def start(self):
        for copy in self.copies():
            copy.start()

    def wait_arrivals(self):
        for copy in self.copies():
            copy.wait_recv()

    def wait_sent(self):
        for copy in self.copies():
            copy.wait_send()


def at_distance(me, count, distance, action):
    for index in (me - distance, me + distance):

        @pl.when((index >= 0) & (index < count))
        def _(index=index):
            action(index)


class Line:
    def __init__(self, me, count, sum_slots, sum_sent, sum_got, spread_view, spread_sent, spread_got):
        self.me, self.count = me, count
        self.sum_slots, self.sum_sent, self.sum_got = sum_slots, sum_sent, sum_got
        self.spread_view, self.spread_sent, self.spread_got = spread_view, spread_sent, spread_got

    def slot(self, piece):
        return lax.rem(piece, self.sum_slots.shape[0])

    def sum_copy(self, piece, owner):
        onward = jnp.where(owner > self.me, self.me + 1, self.me - 1)
        place = jnp.where((owner < self.me) & (owner == self.me - 1), self.count, owner)
        slot = self.slot(piece)
        return pltpu.make_async_remote_copy(
            src_ref=self.sum_slots.at[slot, owner],
            dst_ref=self.sum_slots.at[slot, place],
            send_sem=self.sum_sent.at[slot, owner],
            recv_sem=self.sum_got.at[slot, place],
            device_id={"tp": onward},
            device_id_type=MESH,
        )

    def sum_arrival(self, piece, place):
        view = self.sum_slots.at[self.slot(piece), place]
        pltpu.make_async_copy(view, view, self.sum_got.at[self.slot(piece), place]).wait()

    def sum_start(self, piece, term):
        me, count = self.me, self.count

        @pl.when((me == 0) | (me == count - 1))
        def _():
            for k in range(count - 1):
                owner = jnp.where(me == 0, count - 1 - k, k)
                self.sum_slots[self.slot(piece), owner] = term(owner).astype(jnp.bfloat16)
                self.sum_copy(piece, owner).start()

    def sum_onward(self, piece, term, distances):
        me, count = self.me, self.count

        @pl.when((me > 0) & (me < count - 1))
        def _():
            for distance in distances:

                def pass_on(owner):
                    self.sum_arrival(piece, owner)
                    slot = self.slot(piece)
                    total = self.sum_slots[slot, owner].astype(jnp.float32) + term(owner)
                    self.sum_slots[slot, owner] = total.astype(jnp.bfloat16)
                    self.sum_copy(piece, owner).start()

                at_distance(me, count, distance, pass_on)

    def sum_end(self, piece, total):
        me, count = self.me, self.count

        @pl.when(me > 0)
        def _():
            self.sum_arrival(piece, me)
            total[...] += self.sum_slots[self.slot(piece), me].astype(jnp.float32)

        @pl.when(me < count - 1)
        def _():
            self.sum_arrival(piece, count)
            total[...] += self.sum_slots[self.slot(piece), count].astype(jnp.float32)

    def sum_sent_all(self, piece):
        for distance in range(1, self.count):
            at_distance(
                self.me, self.count, distance,
                lambda owner: self.sum_copy(piece, owner).wait_send(),
            )

    def sum_finish(self, pieces):
        pl.loop(0, pieces)(self.sum_sent_all)

    def spread_copy(self, piece, owner, to, sent, source=None):
        return pltpu.make_async_remote_copy(
            src_ref=self.spread_view(piece, owner) if source is None else source,
            dst_ref=self.spread_view(piece, owner),
            send_sem=self.spread_sent.at[piece, sent],
            recv_sem=self.spread_got.at[piece, owner],
            device_id={"tp": to},
            device_id_type=MESH,
        )

    def own_copies(self, piece, action, source=None):
        me, count = self.me, self.count

        @pl.when(me > 0)
        def _():
            action(self.spread_copy(piece, me, me - 1, count, source))

        @pl.when(me < count - 1)
        def _():
            action(self.spread_copy(piece, me, me + 1, me, source))

    def spread_start(self, piece, source=None):
        self.own_copies(piece, lambda copy: copy.start(), source)

    def onward_copy(self, piece, owner, action):
        me, count = self.me, self.count

        @pl.when((owner < me) & (me < count - 1))
        def _():
            action(self.spread_copy(piece, owner, me + 1, owner))

        @pl.when((owner > me) & (me > 0))
        def _():
            action(self.spread_copy(piece, owner, me - 1, owner))

    def spread_onward(self, piece, distance):
        def pass_on(owner):
            view = self.spread_view(piece, owner)
            pltpu.make_async_copy(view, view, self.spread_got.at[piece, owner]).wait()
            self.onward_copy(piece, owner, lambda copy: copy.start())

        at_distance(self.me, self.count, distance, pass_on)

    def spread_finish(self, pieces, source=None):
        @pl.loop(0, pieces)
        def _(piece):
            self.own_copies(
                piece, lambda copy: copy.wait_send(), None if source is None else source(piece)
            )
            for distance in range(1, self.count):
                at_distance(
                    self.me, self.count, distance,
                    lambda owner: self.onward_copy(piece, owner, lambda copy: copy.wait_send()),
                )


def line_semaphores(count, pieces):
    return [
        pltpu.SemaphoreType.DMA((pieces, count)),
        pltpu.SemaphoreType.DMA((pieces, count + 1)),
    ], [
        pltpu.SemaphoreType.DMA((pieces, count + 1)),
        pltpu.SemaphoreType.DMA((pieces, count)),
    ]


def put_marks(marks, gains, biases):
    marks[...] = jnp.zeros_like(marks)
    marks[0:2, :] = gains[...].astype(jnp.float32)
    marks[2:6, :] = biases[...].astype(jnp.float32)


def gather_kernel(
    count, x_ref, gains, biases, out_ref, marks_out, marks_ref, slots, sent, got,
    marks_sent, marks_got,
):
    me = lax.axis_index("tp")
    height = x_ref.shape[0] // PIECES
    width = x_ref.shape[1]

    def view(piece, owner):
        return out_ref.at[
            pl.ds(pl.multiple_of(piece * height, height), height),
            pl.ds(pl.multiple_of(owner * width, width), width),
        ]

    def source(piece):
        return x_ref.at[pl.ds(pl.multiple_of(piece * height, height), height)]

    line = Line(me, count, None, None, None, view, sent, got)
    peers = peers_along_tp(me, count)
    put_marks(marks_ref, gains, biases)
    greet_peers(peers)

    @pl.loop(0, PIECES)
    def _(piece):
        line.spread_start(piece, source(piece))

    marks = Exchange(
        peers, marks_sent, marks_got, lambda _: marks_ref, lambda i: slots.at[i]
    )
    marks.start()
    own = pl.ds(pl.multiple_of(me * width, width), width)
    out_ref[:, own] = x_ref[...]
    marks_out[:, own] = marks_ref[...]
    for distance in range(1, count):

        @pl.loop(0, PIECES)
        def _(piece, distance=distance):
            line.spread_onward(piece, distance)

    marks.wait_arrivals()
    for i in range(1, count):
        owner = lax.rem(me - i + count, count)
        marks_out[:, pl.ds(pl.multiple_of(owner * width, width), width)] = slots[i - 1]
    marks.wait_sent()
    line.spread_finish(PIECES, source)


def gather_features(x, gains, biases, collective_id):
    count = lax.axis_size("tp")
    rows, width = x.shape
    return pl.pallas_call(
        functools.partial(gather_kernel, count),
        out_shape=[
            jax.ShapeDtypeStruct((rows, count * width), x.dtype),
            jax.ShapeDtypeStruct((8, count * width), jnp.float32),
        ],
        in_specs=[pl.BlockSpec(memory_space=pltpu.VMEM)] * 3,
        out_specs=[pl.BlockSpec(memory_space=pltpu.VMEM)] * 2,
        scratch_shapes=[
            pltpu.VMEM((8, width), jnp.float32),
            pltpu.VMEM((count - 1, 8, width), jnp.float32),
            *line_semaphores(count, PIECES)[1],
            pltpu.SemaphoreType.DMA((count - 1,)),
            pltpu.SemaphoreType.DMA((count - 1,)),
        ],
        compiler_params=pltpu.CompilerParams(
            collective_id=collective_id, has_side_effects=True, vmem_limit_bytes=16 << 20
        ),
        cost_estimate=pl.CostEstimate(
            flops=0, bytes_accessed=64 * rows * count * width, transcendentals=0
        ),
        name="gather_features",
    )(x, gains, biases)


class Swap:
    def __init__(self, sent, got, source, place):
        self.sent, self.got, self.source, self.place = sent, got, source, place

    def copy(self, piece):
        return pltpu.make_async_remote_copy(
            src_ref=self.source(piece),
            dst_ref=self.place(piece),
            send_sem=self.sent.at[piece],
            recv_sem=self.got.at[piece],
            device_id={"ctx": 1 - lax.axis_index("ctx")},
            device_id_type=MESH,
        )

    def start(self, piece):
        self.copy(piece).start()

    def wait_arrival(self, piece):
        self.copy(piece).wait_recv()

    def wait_sent(self, piece):
        self.copy(piece).wait_send()


class PlaneGather:
    def __init__(self, whole, sent, got):
        self.whole, self.sent, self.got = whole, sent, got
        fsdp, self.ctx = lax.axis_index("fsdp"), lax.axis_index("ctx")
        self.fsdp = fsdp
        self.twin = fsdp + 1 - 2 * lax.rem(fsdp, 2)
        self.along_x = lax.rem(fsdp + 2, 4)
        self.twin_x = lax.rem(self.twin + 2, 4)
        self.core_peer = {"fsdp": self.twin}
        self.x_peer = {"fsdp": self.along_x}
        self.y_peer = {"ctx": 1 - self.ctx}

    def peers(self):
        return [self.core_peer, self.x_peer, self.y_peer]

    def shard(self, fsdp, ctx, half=None):
        height = self.whole.shape[0] // 8
        start = (fsdp * 2 + ctx) * height
        if half is not None:
            height //= 2
            start += half * height
        return self.whole.at[pl.ds(pl.multiple_of(start, height), height)]

    def copy(self, number, view, peer):
        return pltpu.make_async_remote_copy(
            src_ref=view,
            dst_ref=view,
            send_sem=self.sent.at[number],
            recv_sem=self.got.at[number],
            device_id=peer,
            device_id_type=MESH,
        )

    def copies(self):
        own = self.shard(self.fsdp, self.ctx)
        from_x = self.shard(self.along_x, self.ctx)
        from_y = self.shard(self.fsdp, 1 - self.ctx)
        return [
            (own, self.core_peer),
            (own, self.x_peer),
            (own, self.y_peer),
            (from_x, self.core_peer),
            (self.shard(self.along_x, self.ctx, 0), self.y_peer),
            (from_y, self.core_peer),
            (self.shard(self.fsdp, 1 - self.ctx, 1), self.x_peer),
            (self.shard(self.along_x, 1 - self.ctx, 0), self.core_peer),
            (self.shard(self.along_x, 1 - self.ctx, 1), self.core_peer),
        ]

    def arrivals(self):
        return [
            self.shard(self.twin, self.ctx),
            self.shard(self.along_x, self.ctx),
            self.shard(self.fsdp, 1 - self.ctx),
            self.shard(self.twin_x, self.ctx),
            self.shard(self.along_x, 1 - self.ctx, 0),
            self.shard(self.twin, 1 - self.ctx),
            self.shard(self.along_x, 1 - self.ctx, 1),
            self.shard(self.twin_x, 1 - self.ctx, 0),
            self.shard(self.twin_x, 1 - self.ctx, 1),
        ]

    def start(self, *numbers):
        copies = self.copies()
        for number in numbers:
            self.copy(number, *copies[number]).start()

    def wait(self, *numbers):
        arrivals = self.arrivals()
        for number in numbers:
            view = arrivals[number]
            pltpu.make_async_copy(view, view, self.got.at[number]).wait()

    def first(self):
        self.start(1, 2, 0)

    def second(self):
        self.wait(1)
        self.start(4, 3)
        self.wait(2)
        self.start(6, 5)

    def third(self):
        self.wait(4)
        self.start(7)
        self.wait(6)
        self.start(8)

    def last(self):
        self.wait(0, 3, 5, 7, 8)

    def wait_sent(self):
        for number, (view, peer) in enumerate(self.copies()):
            self.copy(number, view, peer).wait_send()


def enter_kernel(
    count, x_ref, gains, biases, query_ref, key_ref, value_ref, output_ref, query_bias, value_bias,
    grad_ref,
    wide_out, own_tokens, marks_out, weight_out, output_out, heads, grad_out,
    wide, weight, output_weight, marks_ref, mark_slots, stage, sent, got, marks_sent, marks_got,
    weight_sent, weight_got, output_sent, output_got, swap_sent, swap_got, put_done, grad_done,
    wide_done, out_done,
):
    me, ctx = lax.axis_index("tp"), lax.axis_index("ctx")
    rows, width = x_ref.shape
    height = rows // PIECES
    half = query_ref.shape[1] // 2
    part = 3 * half

    def piece_rows(piece, start=0):
        return pl.ds(pl.multiple_of(start + piece * height, height), height)

    def view(piece, owner):
        return wide.at[piece_rows(piece), pl.ds(pl.multiple_of(owner * width, width), width)]

    gather = PlaneGather(weight, weight_sent, weight_got)
    output_gather = PlaneGather(output_weight, output_sent, output_got)
    own_shard = gather.shard(gather.fsdp, ctx)
    own = pl.ds(pl.multiple_of(me * width, width), width)
    puts = [
        (ref.at[:, pl.ds(side * half, half)], own_shard.at[:, pl.ds(side * part + i * half, half)])
        for side in range(2)
        for i, ref in enumerate((query_ref, key_ref, value_ref))
    ]
    puts += [
        (output_ref, output_gather.shard(gather.fsdp, ctx)),
        (x_ref, wide.at[:, own]),
    ]
    puts = [
        pltpu.make_async_copy(source, place, put_done.at[i])
        for i, (source, place) in enumerate(puts)
    ]
    for put in puts:
        put.start()
    grads = [
        pltpu.make_async_copy(grad_ref.at[:, owner], grad_out.at[owner], grad_done.at[owner])
        for owner in range(count)
    ]
    line = Line(me, count, None, None, None, view, sent, got)
    tp_peers = peers_along_tp(me, count)
    put_marks(marks_ref, gains, biases)
    greet_peers(tp_peers + gather.peers())

    def source(piece):
        return x_ref.at[piece_rows(piece)]

    for piece in range(2):
        line.spread_start(piece, source(piece))
    for put in puts[:7]:
        put.wait()
    gather.first()
    output_gather.first()
    marks = Exchange(
        tp_peers, marks_sent, marks_got, lambda _: marks_ref, lambda i: mark_slots.at[i]
    )
    marks.start()
    marks_out[:, own] = marks_ref[...]
    for put in puts[7:]:
        put.wait()
    for grad in grads:
        grad.start()
    swap = Swap(
        swap_sent, swap_got,
        lambda piece: stage.at[piece_rows(piece)],
        lambda piece: heads.at[piece_rows(piece, ctx * rows)],
    )

    def products(piece, side, place):
        x = wide[piece_rows(piece), :]
        own_half = pl.ds(pl.multiple_of(side * half, half), half)
        for i, bias in enumerate((query_bias, None, value_bias)):
            start = pl.multiple_of(side * part + i * half, half)
            values = dot_plain(x, weight[:, pl.ds(start, half)])
            if bias is not None:
                values += bias[:, own_half].astype(jnp.float32)
            place[:, i * half : (i + 1) * half] = values.astype(jnp.bfloat16)

    def wide_copy(piece):
        part = piece_rows(piece)
        return pltpu.make_async_copy(wide.at[part], wide_out.at[part], wide_done.at[piece])

    weight_copy = pltpu.make_async_copy(weight, weight_out, out_done.at[0])
    output_copy = pltpu.make_async_copy(output_weight, output_out, out_done.at[1])

    @pl.loop(0, PIECES + 7)
    def _(step):
        def late(pieces, action, least=0):
            @pl.when((step >= pieces + least) & (step < PIECES + pieces))
            def _():
                action(step - pieces)

        def use(piece):
            products(piece, 1 - ctx, stage.at[piece_rows(piece)])
            swap.start(piece)
            products(piece, ctx, heads.at[piece_rows(piece, ctx * rows)])
            wide_copy(piece).start()

        @pl.when(step == 7)
        def _():
            gather.third()
            gather.last()
            weight_copy.start()

        late(0, lambda piece: line.spread_start(piece, source(piece)), 2)
        late(7, use)
        late(5, lambda piece: line.spread_onward(piece, 2))
        late(3, lambda piece: line.spread_onward(piece, 1))
        late(6, lambda piece: [line.spread_onward(piece, i) for i in range(3, count)])
        pl.when(step == 5)(gather.second)
        pl.when(step == 7)(output_gather.second)
        pl.when(step == 9)(output_gather.third)

    own_height = height // count
    for piece in range(PIECES):
        start = pl.multiple_of(piece * height + me * own_height, own_height)
        own_tokens[piece * own_height : (piece + 1) * own_height, :] = wide[
            pl.ds(start, own_height), :
        ]

    marks.wait_arrivals()
    for i in range(1, count):
        owner = lax.rem(me - i + count, count)
        marks_out[:, pl.ds(pl.multiple_of(owner * width, width), width)] = mark_slots[i - 1]

    @pl.loop(0, PIECES)
    def _(piece):
        swap.wait_arrival(piece)
        swap.wait_sent(piece)

    output_gather.last()
    output_copy.start()
    marks.wait_sent()
    gather.wait_sent()
    output_gather.wait_sent()
    for grad in grads:
        grad.wait()
    weight_copy.wait()
    output_copy.wait()

    @pl.loop(0, PIECES)
    def _(piece):
        wide_copy(piece).wait()

    line.spread_finish(PIECES, source)


def enter(
    tokens, gains, biases, query_weight, key_weight, value_weight, output_weight, query_bias,
    value_bias, out_grad, collective_id,
):
    count = lax.axis_size("tp")
    rows, width = tokens.shape
    head_cols = query_weight.shape[1]
    features = count * width
    part = 3 * head_cols // 2
    own = rows // PIECES // count
    low = jnp.bfloat16
    vmem, anywhere = pl.BlockSpec(memory_space=pltpu.VMEM), pl.BlockSpec(memory_space=pl.ANY)
    return pl.pallas_call(
        functools.partial(enter_kernel, count),
        out_shape=[
            jax.ShapeDtypeStruct((rows, features), low),
            jax.ShapeDtypeStruct((rows // count, features), low),
            jax.ShapeDtypeStruct((8, features), jnp.float32),
            jax.ShapeDtypeStruct((features, 2 * part), low),
            jax.ShapeDtypeStruct((features, head_cols), low),
            jax.ShapeDtypeStruct((2 * rows, part), low),
            jax.ShapeDtypeStruct((count, PIECES, own, width), low),
        ],
        in_specs=[anywhere, vmem, vmem, *[anywhere] * 4, vmem, vmem, anywhere],
        out_specs=[anywhere, vmem, vmem, anywhere, anywhere, vmem, vmem],
        scratch_shapes=[
            pltpu.VMEM((rows, features), low),
            pltpu.VMEM((features, 2 * part), low),
            pltpu.VMEM((features, head_cols), low),
            pltpu.VMEM((8, width), jnp.float32),
            pltpu.VMEM((count - 1, 8, width), jnp.float32),
            pltpu.VMEM((rows, part), low),
            *line_semaphores(count, PIECES)[1],
            pltpu.SemaphoreType.DMA((count - 1,)),
            pltpu.SemaphoreType.DMA((count - 1,)),
            *[pltpu.SemaphoreType.DMA((9,))] * 4,
            pltpu.SemaphoreType.DMA((PIECES,)),
            pltpu.SemaphoreType.DMA((PIECES,)),
            pltpu.SemaphoreType.DMA((8,)),
            pltpu.SemaphoreType.DMA((count,)),
            pltpu.SemaphoreType.DMA((PIECES,)),
            pltpu.SemaphoreType.DMA((2,)),
        ],
        compiler_params=pltpu.CompilerParams(
            collective_id=collective_id, has_side_effects=True, vmem_limit_bytes=60 << 20
        ),
        cost_estimate=pl.CostEstimate(
            flops=80_000_000_000, bytes_accessed=64 * rows * features, transcendentals=0
        ),
        name="enter",
    )(
        tokens, gains, biases, query_weight, key_weight, value_weight, output_weight,
        query_bias[None], value_bias[None], out_grad.reshape(PIECES, count, own, width),
    )


def relay_kernel(count, row_step, use_step, sizes, *refs):
    row_in, use_in, row_out, use_out, shared = sizes
    refs = list(refs)

    def take(number):
        taken = refs[:number]
        del refs[:number]
        return taken

    x_ref, sum_weight = take(2)
    use_weight = sum_weight if shared else take(1)[0]
    row_inputs, use_inputs = take(row_in), take(use_in)
    (gathered,) = take(1)
    row_outputs, use_outputs = take(row_out), take(use_out)
    terms, total, slots, sum_sent, sum_got, spread_sent, spread_got = refs
    me = lax.axis_index("tp")
    height = x_ref.shape[0] // PIECES
    own = height // count
    width = sum_weight.shape[0]

    def piece_rows(piece):
        return pl.ds(pl.multiple_of(piece * height, height), height)

    def view(piece, owner):
        return gathered.at[pl.ds(pl.multiple_of(piece * height + owner * own, own), own)]

    line = Line(me, count, slots, sum_sent, sum_got, view, spread_sent, spread_got)
    greet(me, count)

    @pl.loop(0, PIECES + 5)
    def _(step):
        odd = lax.rem(step, 2)

        def term_of(parity):
            return lambda owner: terms[parity, pl.ds(pl.multiple_of(owner * own, own), own), :]

        def late(pieces, action):
            @pl.when((step >= pieces) & (step < PIECES + pieces))
            def _():
                action(step - pieces)

        def use(piece):
            part = piece_rows(piece)
            use_step(part, gathered[part, :], use_weight, use_inputs, use_outputs)

        def form(piece):
            x = x_ref[piece_rows(piece), :]

            @pl.loop(0, width // TILE)
            def _(tile):
                part = pl.ds(pl.multiple_of(tile * TILE, TILE), TILE)
                terms[odd, :, part] = dot_cols(x, sum_weight[part, :])

            line.sum_start(piece, term_of(odd))

        def own_step(piece):
            total[...] = terms[1 - odd, pl.ds(pl.multiple_of(me * own, own), own), :]
            line.sum_end(piece, total)
            view(piece, me)[...] = row_step(piece, total, row_inputs, row_outputs)
            line.spread_start(piece)

        late(5, use)
        late(3, lambda piece: line.spread_onward(piece, 2))
        late(1, lambda piece: line.sum_onward(piece, term_of(1 - odd), [1]))
        late(0, form)
        late(4, lambda piece: [line.spread_onward(piece, i) for i in range(3, count)])
        late(2, lambda piece: line.spread_onward(piece, 1))
        late(0, lambda piece: line.sum_onward(piece, term_of(odd), range(count - 2, 1, -1)))
        late(1, own_step)

    line.sum_finish(PIECES)
    line.spread_finish(PIECES)


def relay(
    x, sum_weight, use_weight, row_inputs, row_step, row_shapes, use_inputs, use_step, use_shapes,
    collective_id, name,
):
    count = lax.axis_size("tp")
    rows = x.shape[0]
    width = sum_weight.shape[0]
    height = rows // PIECES
    own = height // count
    shared = use_weight is None
    operands = [x, sum_weight, *([] if shared else [use_weight]), *row_inputs, *use_inputs]
    shapes = [jax.ShapeDtypeStruct((rows, width), jnp.bfloat16), *row_shapes, *use_shapes]
    sums, spreads = line_semaphores(count, PIECES)
    sizes = (len(row_inputs), len(use_inputs), len(row_shapes), len(use_shapes), shared)
    return pl.pallas_call(
        functools.partial(relay_kernel, count, row_step, use_step, sizes),
        out_shape=shapes,
        in_specs=[pl.BlockSpec(memory_space=pltpu.VMEM)] * len(operands),
        out_specs=[pl.BlockSpec(memory_space=pltpu.VMEM)] * len(shapes),
        scratch_shapes=[
            pltpu.VMEM((2, height, width), jnp.float32),
            pltpu.VMEM((own, width), jnp.float32),
            pltpu.VMEM((PIECES, count + 1, own, width), jnp.bfloat16),
            *sums,
            *spreads,
        ],
        compiler_params=pltpu.CompilerParams(
            collective_id=collective_id, has_side_effects=True, vmem_limit_bytes=60 << 20
        ),
        cost_estimate=pl.CostEstimate(
            flops=100_000_000_000, bytes_accessed=64 * rows * width, transcendentals=0
        ),
        name=name,
    )(*operands)


def own_rows_of(piece, like):
    own = like.shape[0] // PIECES
    return pl.ds(pl.multiple_of(piece * own, own), own)


def first_norm_step(piece, total, inputs, outputs):
    tokens, marks = inputs
    first_norm, normed_one, inverse_one = outputs
    part = own_rows_of(piece, tokens)
    summed = tokens[part, :].astype(jnp.float32) + (total[...] + marks[2:3, :])
    normed, inverse = norm_parts(summed)
    result = normed * marks[0:1, :] + marks[3:4, :]
    first_norm[part, :] = result
    normed_one[part, :] = normed
    inverse_one[part, :] = jnp.broadcast_to(inverse, (inverse.shape[0], 128))
    return result.astype(jnp.bfloat16)


def expand_step(rows, chunk, weight, inputs, outputs):
    (bias,) = inputs
    hidden, activated = outputs

    @pl.loop(0, hidden.shape[1] // TILE)
    def _(tile):
        part = pl.ds(pl.multiple_of(tile * TILE, TILE), TILE)
        values = dot_plain(chunk, weight[:, part]) + bias[:, part]
        hidden[rows, part] = values
        activated[rows, part] = gelu_tanh(values).astype(jnp.bfloat16)


def add_sums(piece, sums, *values):
    @pl.when(piece == 0)
    def _():
        sums[...] = jnp.zeros_like(sums)

    for i, value in enumerate(values):
        sums[i : i + 1, :] += jnp.sum(value, axis=0, keepdims=True)


def second_norm_step(piece, total, inputs, outputs):
    first_norm, out_grad, marks = inputs
    mixed, grad_second, sums = outputs
    part = own_rows_of(piece, first_norm)
    normed, inverse = norm_parts(first_norm[part, :] + total[...] + marks[4:5, :])
    result = (normed * marks[1:2, :] + marks[5:6, :]).astype(jnp.bfloat16)
    count, _, width = mixed.shape
    for i in range(count):
        mixed[i, part, :] = result[:, i * width : (i + 1) * width]
    upstream = jnp.concatenate([out_grad[i, part, :] for i in range(count)], axis=1)
    upstream = upstream.astype(jnp.float32)
    grad = norm_back(upstream, normed, inverse, marks[1:2, :])
    grad_second[part, :] = grad
    low = grad.astype(jnp.bfloat16)
    add_sums(piece, sums, upstream * normed, upstream, low.astype(jnp.float32))
    return low


def gelu_slope(values):
    scale = math.sqrt(2.0 / math.pi)
    square = values * values
    bend = jnp.tanh(scale * values * (1.0 + 0.044715 * square))
    inner = scale * (1.0 + 3 * 0.044715 * square)
    return 0.5 * (1.0 + bend) + 0.5 * values * (1.0 - bend * bend) * inner


def shrink_step(rows, chunk, weight, inputs, outputs):
    (hidden,) = inputs
    hidden_low, sums = outputs

    @pl.when(rows.start == 0)
    def _():
        sums[...] = jnp.zeros_like(sums)

    @pl.loop(0, hidden.shape[1] // TILE)
    def _(tile):
        part = pl.ds(pl.multiple_of(tile * TILE, TILE), TILE)
        grad = dot_plain(chunk, weight[:, part]) * gelu_slope(hidden[rows, part])
        low = grad.astype(jnp.bfloat16)
        hidden_low[rows, part] = low
        sums[0:1, part] += jnp.sum(low.astype(jnp.float32), axis=0, keepdims=True)


def first_back_step(piece, total, inputs, outputs):
    grad_second, normed_one, inverse_one, marks = inputs
    grad_inner, sums = outputs
    part = own_rows_of(piece, grad_second)
    normed = normed_one[part, :]
    grad_first = grad_second[part, :] + total[...]
    grad = norm_back(grad_first, normed, inverse_one[part, 0:1], marks[0:1, :])
    grad_inner[part, :] = grad
    low = grad.astype(jnp.bfloat16)
    add_sums(piece, sums, grad_first * normed, grad_first, low.astype(jnp.float32))
    return low


def attended_step(rows, chunk, weight, inputs, outputs):
    (attended_grad,) = outputs
    attended_grad[rows, :] = dot_plain(chunk, weight[...]).astype(jnp.bfloat16)


class PlaneSum:
    def __init__(self, parts, core_slots, first_slots, last_slots, sent, got):
        self.parts, self.core_slots = parts, core_slots
        self.first_slots, self.last_slots = first_slots, last_slots
        self.sent, self.got = sent, got
        self.fsdp, self.ctx = lax.axis_index("fsdp"), lax.axis_index("ctx")
        self.twin = self.fsdp + 1 - 2 * lax.rem(self.fsdp, 2)
        self.height = parts.shape[0] // 8
        self.half = parts.shape[1] // 2

    def number(self, fsdp, over_x, over_y):
        chip = lax.rem(fsdp + 2 * over_x, 4)
        return chip * 2 + (1 - self.ctx if over_y else self.ctx)

    def rows(self, number):
        return pl.ds(pl.multiple_of(number * self.height, self.height), self.height)

    def view(self, over_x, over_y, side):
        columns = pl.ds(side * self.half, self.half)
        return self.parts.at[self.rows(self.number(self.fsdp, over_x, over_y)), columns]

    def copy(self, number, source, place, peer):
        return pltpu.make_async_remote_copy(
            src_ref=source,
            dst_ref=place,
            send_sem=self.sent.at[number],
            recv_sem=self.got.at[number],
            device_id=peer,
            device_id_type=MESH,
        )

    def core_copy(self, number):
        over_x, over_y = number // 2, number % 2
        source = self.parts.at[self.rows(self.number(self.twin, over_x, over_y))]
        place = self.core_slots.at[self.rows(number)]
        return self.copy(number, source, place, {"fsdp": self.twin})

    def x_peer(self):
        return {"fsdp": lax.rem(self.fsdp + 2, 4)}

    def y_peer(self):
        return {"ctx": 1 - self.ctx}

    def first_copy(self, number):
        slot = self.first_slots.at[number]
        if number < 2:
            return self.copy(4 + number, self.view(1, number, 0), slot, self.x_peer())
        return self.copy(4 + number, self.view(number - 2, 1, 1), slot, self.y_peer())

    def last_copy(self, side):
        slot = self.last_slots.at[side]
        if side == 0:
            return self.copy(8, self.view(0, 1, 0), slot, self.y_peer())
        return self.copy(9, self.view(1, 0, 1), slot, self.x_peer())

    def bands(self, action):
        band = min(self.height, 32)

        @pl.loop(0, self.height // band)
        def _(i):
            action(pl.ds(pl.multiple_of(i * band, band), band))

    def add(self, view, slot):
        def band(part):
            total = view[part, :].astype(jnp.float32) + slot[part, :].astype(jnp.float32)
            view[part, :] = total.astype(view.dtype)

        self.bands(band)

    def start(self):
        for number in (3, 2, 1, 0):
            self.core_copy(number).start()

    def second(self):
        for number in (3, 2, 1, 0):
            self.core_copy(number).wait_recv()
            shard = self.parts.at[self.rows(self.number(self.fsdp, number // 2, number % 2))]
            self.add(shard, self.core_slots.at[self.rows(number)])
            if number == 3:
                self.first_copy(1).start()
                self.first_copy(3).start()
            if number == 2:
                self.first_copy(0).start()
            if number == 1:
                self.first_copy(2).start()

    def third(self):
        self.first_copy(1).wait_recv()
        self.add(self.view(0, 1, 0), self.first_slots.at[1])
        self.last_copy(0).start()
        self.first_copy(3).wait_recv()
        self.add(self.view(1, 0, 1), self.first_slots.at[3])
        self.last_copy(1).start()

    def finish(self, put):
        for side in range(2):
            self.first_copy(2 * side).wait_recv()
            self.last_copy(side).wait_recv()
            view, first, last = self.view(0, 0, side), self.first_slots, self.last_slots

            def band(part, side=side, view=view):
                total = view[part, :].astype(jnp.float32)
                total += first[2 * side, part, :].astype(jnp.float32)
                put(side, part, total + last[side, part, :].astype(jnp.float32))

            self.bands(band)
        for number in range(4):
            self.core_copy(number).wait_send()
            self.first_copy(number).wait_send()
        for side in range(2):
            self.last_copy(side).wait_send()

    @staticmethod
    def scratch(shards, height, width):
        return [
            pltpu.VMEM((shards * height, width), jnp.bfloat16),
            pltpu.VMEM((4 * height, width), jnp.bfloat16),
            *PlaneSum.slots(height, width),
        ]

    @staticmethod
    def slots(height, width):
        return [
            pltpu.VMEM((4, height, width // 2), jnp.bfloat16),
            pltpu.VMEM((2, height, width // 2), jnp.bfloat16),
            pltpu.SemaphoreType.DMA((10,)),
            pltpu.SemaphoreType.DMA((10,)),
        ]


def middle_kernel(
    count, heads_ref, output_weight, expand_shard, shrink_shard, own_tokens, out_grad, marks,
    hidden_bias,
    attended, mixed, inner, branch_out, grad_heads, first_sums, second_sums, hidden_sums,
    shrink_out, expand_out,
    expand_weight, shrink_weight, gathered, activated, slope, normed_one, inverse_one,
    terms, total, slots, stage, expand_stage, first_slots, last_slots, plane_sent, plane_got,
    sum_sent, sum_got, spread_sent, spread_got, expand_sent, expand_got, shrink_sent, shrink_got,
    in_sent, in_got, out_sent, out_got, put_done, branch_done, product_done, ready,
):
    me, ctx = lax.axis_index("tp"), lax.axis_index("ctx")
    rows, width = gathered.shape[0] // 3, gathered.shape[1]
    half = heads_ref.shape[1]
    height = rows // PIECES
    own = height // count
    shard, hidden = width // PIECES, activated.shape[1]
    pieces = 3 * PIECES

    def piece_rows(piece, start=0):
        return pl.ds(pl.multiple_of(start + piece * height, height), height)

    def view(piece, owner):
        return gathered.at[pl.ds(pl.multiple_of(piece * height + owner * own, own), own)]

    line = Line(me, count, slots, sum_sent, sum_got, view, spread_sent, spread_got)
    expand_gather = PlaneGather(expand_weight, expand_sent, expand_got)
    shrink_gather = PlaneGather(shrink_weight, shrink_sent, shrink_got)
    own_half = pl.ds(pl.multiple_of(ctx * half, half), half)
    own_block = pl.ds(pl.multiple_of(ctx * rows, rows), rows)
    puts = [
        pltpu.make_async_copy(source, place, put_done.at[i])
        for i, (source, place) in enumerate(
            (
                (heads_ref.at[own_block], attended.at[:, own_half]),
                (expand_shard, expand_gather.shard(expand_gather.fsdp, ctx)),
                (shrink_shard, shrink_gather.shard(shrink_gather.fsdp, ctx)),
            )
        )
    ]
    for put in puts:
        put.start()
    swap_in = Swap(
        in_sent, in_got,
        lambda piece: heads_ref.at[piece_rows(piece, (1 - ctx) * rows)],
        lambda piece: attended.at[piece_rows(piece), own_half],
    )
    swap_out = Swap(
        out_sent, out_got,
        lambda piece: stage.at[piece_rows(piece)],
        lambda piece: grad_heads.at[piece_rows(piece, ctx * rows)],
    )
    greet(me, count, expand_gather.peers())
    pl.loop(0, PIECES)(swap_in.start)
    for put in puts:
        put.wait()
    expand_gather.first()

    def branch_copy(piece):
        part = piece_rows(piece)
        return pltpu.make_async_copy(
            gathered.at[piece_rows(piece, 2 * rows)], branch_out.at[part], branch_done.at[piece]
        )

    def in_stage(piece, number):
        return (piece >= number * PIECES) & (piece < (number + 1) * PIECES)

    def tiles(extent, action):
        @pl.loop(0, extent // TILE)
        def _(tile):
            action(pl.ds(pl.multiple_of(tile * TILE, TILE), TILE))

    def use(piece):
        line.sum_sent_all(piece)
        part = piece_rows(lax.rem(piece, PIECES))
        chunk_rows = piece_rows(piece)

        @pl.when(in_stage(piece, 0))
        def _():
            chunk = gathered[chunk_rows, :]

            def expand(columns):
                values = dot_plain(chunk, expand_weight[:, columns])
                values += hidden_bias[:, columns].astype(jnp.float32)
                result, bend = gelu_with_slope(values)
                activated[part, columns] = result.astype(jnp.bfloat16)
                slope[part, columns] = bend.astype(jnp.bfloat16)

            tiles(activated.shape[1], expand)

        @pl.when(in_stage(piece, 1))
        def _():
            chunk = gathered[chunk_rows, :]

            def shrink(columns):
                grad = dot_plain(chunk, shrink_weight[:, columns])
                low = (grad * slope[part, columns].astype(jnp.float32)).astype(jnp.bfloat16)
                slope[part, columns] = low
                added = jnp.sum(low.astype(jnp.float32), axis=0, keepdims=True)
                before = jnp.where(piece == PIECES, 0.0, hidden_sums[0:1, columns])
                hidden_sums[0:1, columns] = before + added

            tiles(slope.shape[1], shrink)

        @pl.when(in_stage(piece, 2))
        def _():
            place = piece - 2 * PIECES
            result = dot_plain(gathered[chunk_rows, :], output_weight[...]).astype(jnp.bfloat16)
            here = ctx == 0
            left, right = result[:, :half], result[:, half:]
            stage[part, :] = jnp.where(here, right, left)
            swap_out.start(place)
            grad_heads[piece_rows(place, ctx * rows), :] = jnp.where(here, left, right)
            branch_copy(place).start()

    def form(piece):
        part = piece_rows(lax.rem(piece, PIECES))
        parity = lax.rem(piece, 2)

        def products(x, weight):
            def product(columns):
                terms[parity, :, columns] = dot_cols(x, weight[columns, :])

            tiles(width, product)

        @pl.when(in_stage(piece, 0))
        def _():
            swap_in.wait_arrival(piece)
            products(attended[part, :], output_weight)

        @pl.when(in_stage(piece, 1))
        def _():
            products(activated[part, :], shrink_weight)

        @pl.when(in_stage(piece, 2))
        def _():
            products(slope[part, :], expand_weight)

        line.sum_start(piece, term_of(piece))

    def term_of(piece):
        parity = lax.rem(piece, 2)
        return lambda owner: terms[parity, pl.ds(pl.multiple_of(owner * own, own), own), :]

    def own_step(piece):
        place = lax.rem(piece, PIECES)
        total[...] = term_of(piece)(me)
        line.sum_end(piece, total)

        @pl.when(in_stage(piece, 0))
        def _():
            view(piece, me)[...] = first_norm_step(
                place, total, (own_tokens, marks), (inner, normed_one, inverse_one)
            )

        @pl.when(in_stage(piece, 1))
        def _():
            view(piece, me)[...] = second_norm_step(
                place, total, (inner, out_grad, marks), (mixed, inner, second_sums)
            )

        @pl.when(in_stage(piece, 2))
        def _():
            view(piece, me)[...] = first_back_step(
                place, total, (inner, normed_one, inverse_one, marks), (inner, first_sums)
            )

        line.spread_start(piece)

    def gradient(number, left_start, right, place):
        columns = pl.ds(pl.multiple_of(number * shard, shard), shard)
        left = gathered[left_start : left_start + rows, columns].T

        def product(part):
            place[:, part] = dot_plain(left, right[:, part]).astype(place.dtype)

        tiles(place.shape[1], product)

    def expand_copy(number):
        part = pl.ds(pl.multiple_of(number * shard, shard), shard)
        return pltpu.make_async_copy(expand_stage, expand_out.at[part], product_done)

    def expand_step(number):
        pl.when(number > 0)(lambda: expand_copy(number - 1).wait())
        gradient(number, 0, slope, expand_stage)
        expand_copy(number).start()

    plane_sum = PlaneSum(shrink_weight, activated, first_slots, last_slots, plane_sent, plane_got)
    twin = {"fsdp": plane_sum.twin}

    def shrink_step(number):
        pl.when(number == 0)(shrink_gather.wait_sent)
        fsdp = jnp.where(number == 0, plane_sum.twin, plane_sum.fsdp)
        for over_x in (1, 0):
            for over_y in (1, 0):
                owner = plane_sum.number(fsdp, over_x, over_y)
                gradient(owner, rows, activated, shrink_weight.at[plane_sum.rows(owner)])

        @pl.when(number == 1)
        def _():
            pl.semaphore_signal(ready, inc=1, device_id=twin, device_id_type=MESH)

    def shrink_send(_):
        pl.semaphore_wait(ready, 1)
        plane_sum.start()

    def shrink_total(side):
        return pltpu.make_async_copy(
            terms.at[side], shrink_out.at[pl.ds(side * height, height)], put_done.at[side]
        )

    @pl.loop(0, pieces + 5)
    def _(step):
        def late(number, action, most=pieces):
            @pl.when((step >= number) & (step < most + number))
            def _():
                action(step - number)

        pl.when(step == 5)(expand_gather.last)
        pl.when(step == 2 * PIECES + 7)(plane_sum.second)
        pl.when(step == 2 * PIECES + 9)(plane_sum.third)
        late(5, use)
        late(3, lambda piece: line.spread_onward(piece, 2))
        late(1, lambda piece: line.sum_onward(piece, term_of(piece), [1]))
        pl.when(step == PIECES)(shrink_gather.last)
        late(0, form)
        late(4, lambda piece: [line.spread_onward(piece, i) for i in range(3, count)])
        late(2, lambda piece: line.spread_onward(piece, 1))
        late(2 * PIECES + 4, shrink_step, 2)
        late(2 * PIECES + 5, expand_step, PIECES)
        late(2 * PIECES + 6, shrink_send, 1)
        late(0, lambda piece: line.sum_onward(piece, term_of(piece), range(count - 2, 1, -1)))
        late(1, own_step)

        @pl.when(step == 3)
        def _():
            expand_gather.second()
            shrink_gather.first()

        pl.when(step == 4)(expand_gather.third)
        pl.when(step == 6)(shrink_gather.second)
        pl.when(step == 7)(shrink_gather.third)

    expand_copy(PIECES - 1).wait()

    def put_total(side, part, values):
        columns = pl.ds(side * (hidden // 2), hidden // 2)
        start = pl.multiple_of(lax.rem(part.start, height), values.shape[0])
        terms[part.start // height, pl.ds(start, values.shape[0]), columns] = values

    plane_sum.finish(put_total)
    for side in range(2):
        shrink_total(side).start()
    for side in range(2):
        shrink_total(side).wait()

    @pl.loop(0, PIECES)
    def _(piece):
        branch_copy(piece).wait()
        swap_in.wait_sent(piece)
        swap_out.wait_arrival(piece)
        swap_out.wait_sent(piece)

    expand_gather.wait_sent()
    line.spread_finish(pieces)


def gelu_with_slope(values):
    scale = math.sqrt(2.0 / math.pi)
    square = values * values
    bend = 0.5 * jnp.tanh(scale * values * (1.0 + 0.044715 * square)) + 0.5
    inner = (2 * scale) * (1.0 + 3 * 0.044715 * square)
    result = values * bend
    return result, bend + result * (1.0 - bend) * inner


def middle(
    attended_heads, output_weight, expand_shard, shrink_shard, own_tokens, out_grad, marks,
    hidden_bias, collective_id,
):
    count = lax.axis_size("tp")
    rows = attended_heads.shape[0] // 2
    half = attended_heads.shape[1]
    own_rows, width = own_tokens.shape
    hidden = expand_shard.shape[1]
    height = rows // PIECES
    own = height // count
    shard = width // PIECES
    low = jnp.bfloat16
    vmem, anywhere = pl.BlockSpec(memory_space=pltpu.VMEM), pl.BlockSpec(memory_space=pl.ANY)

    def shape(extent, kind=jnp.float32):
        return jax.ShapeDtypeStruct(extent, kind)

    return pl.pallas_call(
        functools.partial(middle_kernel, count),
        out_shape=[
            shape((rows, 2 * half), low),
            shape(out_grad.shape, low),
            shape((own_rows, width)),
            shape((rows, width), low),
            shape((2 * rows, half), low),
            shape((8, width)),
            shape((8, width)),
            shape((8, hidden)),
            shape((shard, hidden)),
            shape((width, hidden), low),
        ],
        in_specs=[anywhere, vmem, anywhere, anywhere, vmem, vmem, vmem, vmem],
        out_specs=[vmem, vmem, vmem, anywhere, vmem, vmem, vmem, vmem, anywhere, anywhere],
        scratch_shapes=[
            pltpu.VMEM((width, hidden), low),
            pltpu.VMEM((width, hidden), low),
            pltpu.VMEM((3 * rows, width), low),
            pltpu.VMEM((rows, hidden), low),
            pltpu.VMEM((rows, hidden), low),
            pltpu.VMEM((own_rows, width), jnp.float32),
            pltpu.VMEM((own_rows, 128), jnp.float32),
            pltpu.VMEM((2, height, width), jnp.float32),
            pltpu.VMEM((own, width), jnp.float32),
            pltpu.VMEM((PIECES, count + 1, own, width), low),
            pltpu.VMEM((rows, half), low),
            pltpu.VMEM((shard, hidden), low),
            *PlaneSum.slots(shard, hidden),
            *line_semaphores(count, PIECES)[0],
            *line_semaphores(count, 3 * PIECES)[1],
            *[pltpu.SemaphoreType.DMA((9,))] * 4,
            *[pltpu.SemaphoreType.DMA((PIECES,))] * 4,
            pltpu.SemaphoreType.DMA((3,)),
            pltpu.SemaphoreType.DMA((PIECES,)),
            pltpu.SemaphoreType.DMA,
            pltpu.SemaphoreType.REGULAR,
        ],
        compiler_params=pltpu.CompilerParams(
            collective_id=collective_id, has_side_effects=True, vmem_limit_bytes=62 << 20
        ),
        cost_estimate=pl.CostEstimate(
            flops=300_000_000_000, bytes_accessed=192 * rows * width, transcendentals=0
        ),
        name="middle",
    )(
        attended_heads, output_weight, expand_shard, shrink_shard, own_tokens, out_grad, marks,
        hidden_bias,
    )


def peers_in_plane(sizes):
    fsdp, ctx = lax.axis_index("fsdp"), lax.axis_index("ctx")
    return [
        {"fsdp": lax.rem(fsdp + i, sizes[0]), "ctx": lax.rem(ctx + j, sizes[1])}
        for i in range(sizes[0])
        for j in range(sizes[1])
        if i or j
    ]


def input_kernel(
    sizes, x_ref, weight, inner_ref, first_ref, second_ref, hidden_ref, out_ref, vectors_ref,
    rows_ref, term_ref, total, slots, own_vectors, tp_slots, plane_slots,
    sum_sent, sum_got, tp_sent, tp_got, plane_sent, plane_got, hooks=None,
):
    count = sizes[2]
    me = lax.axis_index("tp")
    height = x_ref.shape[0] // PIECES
    own = height // count
    width = out_ref.shape[1]
    line = Line(me, count, slots, sum_sent, sum_got, None, None, None)
    tp_peers, plane_peers = peers_along_tp(me, count), peers_in_plane(sizes)
    greet_peers(tp_peers + plane_peers)

    def own_part(index):
        return rows_ref.at[:, pl.ds(pl.multiple_of(index * width, width), width)]

    over_tp = Exchange(
        tp_peers, tp_sent, tp_got,
        lambda i: own_part(lax.rem(me + i, count)), lambda i: tp_slots.at[i],
    )
    over_plane = Exchange(
        plane_peers, plane_sent, plane_got, lambda _: own_vectors, lambda i: plane_slots.at[i]
    )
    opening, before, after, closing = hooks or (lambda *_: None,) * 4
    order = ((0, 0), (1, 0), (0, 2), (0, 1), (1, 2), (1, 1))
    rows_ref[...] = jnp.zeros_like(rows_ref)
    for i, (which, row) in enumerate(order):
        rows_ref[i : i + 1, :] = (first_ref, second_ref)[which][row : row + 1, :]
    opening()
    over_tp.start()

    def terms(piece):
        def term(owner):
            features = pl.ds(pl.multiple_of(owner * width, width), width)
            term_ref[...] = dot_cols(
                x_ref[pl.ds(pl.multiple_of(piece * height, height), height), :],
                weight[features, :],
            )
            inner = inner_ref[pl.ds(pl.multiple_of(piece * own, own), own), features]
            term_ref[pl.ds(pl.multiple_of(me * own, own), own), :] += inner
            return term_ref[...]

        return term

    def pack():
        over_tp.wait_arrivals()
        own_vectors[0:8, :] = own_part(me)[...]
        for i in range(count - 1):
            own_vectors[0:8, :] += tp_slots[i]
        own_vectors[8:, :] = jnp.zeros_like(own_vectors[8:, :])
        hidden_rows = hidden_ref.shape[1] // width
        for i in range(hidden_rows):
            own_vectors[8 + i : 9 + i, :] = hidden_ref[0:1, i * width : (i + 1) * width]
        for i in range(x_ref.shape[1] // width):
            part = x_ref[:, i * width : (i + 1) * width].astype(jnp.float32)
            place = 8 + hidden_rows + i
            own_vectors[place : place + 1, :] = jnp.sum(part, axis=0, keepdims=True)
        over_plane.start()

    @pl.loop(0, PIECES)
    def _(piece):
        before(piece)
        line.sum_start(piece, terms(piece))
        line.sum_onward(piece, terms(piece), range(count - 2, 0, -1))
        after(piece)

    pack()
    closing()

    @pl.loop(0, PIECES)
    def _(piece):
        total[...] = terms(piece)(me)
        line.sum_end(piece, total)
        rows = pl.ds(pl.multiple_of(piece * height, height), height)
        out_ref[rows, :] = total[...].astype(out_ref.dtype)

    over_plane.wait_arrivals()
    vectors_ref[...] = own_vectors[...]
    for i in range(len(plane_peers)):
        vectors_ref[...] += plane_slots[i]
    over_tp.wait_sent()
    over_plane.wait_sent()
    line.sum_finish(PIECES)


def input_sum(x, weight, inner, first_sums, second_sums, hidden_sums, collective_id):
    sizes = tuple(lax.axis_size(axis) for axis in ("fsdp", "ctx", "tp"))
    count = sizes[2]
    others = sizes[0] * sizes[1] - 1
    rows = x.shape[0]
    width = weight.shape[0] // count
    height = rows // PIECES
    packed = 8 + -(-(hidden_sums.shape[1] + x.shape[1]) // (8 * width)) * 8
    return pl.pallas_call(
        functools.partial(input_kernel, sizes),
        out_shape=[
            jax.ShapeDtypeStruct((rows, width), jnp.bfloat16),
            jax.ShapeDtypeStruct((packed, width), jnp.float32),
        ],
        in_specs=[pl.BlockSpec(memory_space=pltpu.VMEM)] * 6,
        out_specs=[pl.BlockSpec(memory_space=pltpu.VMEM)] * 2,
        scratch_shapes=[
            pltpu.VMEM(first_sums.shape, jnp.float32),
            pltpu.VMEM((height, width), jnp.float32),
            pltpu.VMEM((height, width), jnp.float32),
            pltpu.VMEM((PIECES, count + 1, height, width), jnp.bfloat16),
            pltpu.VMEM((packed, width), jnp.float32),
            pltpu.VMEM((count - 1, 8, width), jnp.float32),
            pltpu.VMEM((others, packed, width), jnp.float32),
            *line_semaphores(count, PIECES)[0],
            pltpu.SemaphoreType.DMA((count - 1,)),
            pltpu.SemaphoreType.DMA((count - 1,)),
            pltpu.SemaphoreType.DMA((others,)),
            pltpu.SemaphoreType.DMA((others,)),
        ],
        compiler_params=pltpu.CompilerParams(
            collective_id=collective_id, has_side_effects=True, vmem_limit_bytes=40 << 20
        ),
        cost_estimate=pl.CostEstimate(
            flops=60_000_000_000, bytes_accessed=64 * rows * width, transcendentals=0
        ),
        name="input_sum",
    )(x, weight, inner, first_sums, second_sums, hidden_sums)


def leave_kernel(
    sizes, grads_ref, tokens_in, weight_in, inner_in, first_ref, second_ref, hidden_ref, branch_in,
    attended_in,
    out_ref, vectors_ref, query_out, key_out, value_out, output_out,
    tokens_ref, weight, inner_ref, branch_ref, attended_ref, copied, own_copied,
    x_ref, rows_ref, term_ref, total, slots, own_vectors, tp_slots, plane_slots,
    sum_sent, sum_got, tp_sent, tp_got, plane_sent, plane_got, swap_sent, swap_got, *sum_scratch,
):
    count = sizes[2]
    me, ctx = lax.axis_index("tp"), lax.axis_index("ctx")
    rows = x_ref.shape[0]
    height = rows // PIECES
    part = grads_ref.shape[1]
    plane_sum, output_sum = PlaneSum(*sum_scratch[:6]), PlaneSum(*sum_scratch[6:])
    shard = plane_sum.height

    def piece_rows(piece, start=0):
        return pl.ds(pl.multiple_of(start + piece * height, height), height)

    copies = [
        pltpu.make_async_copy(source, place, copied.at[i])
        for i, (source, place) in enumerate(
            (
                (branch_in, branch_ref),
                (attended_in, attended_ref),
                (weight_in, weight),
                (inner_in, inner_ref),
                (tokens_in, tokens_ref),
            )
        )
    ]
    for copy in copies:
        copy.start()
    own_columns = pl.ds(pl.multiple_of(ctx * part, part), part)
    own_block = pl.ds(pl.multiple_of(ctx * rows, rows), rows)
    own_copy = pltpu.make_async_copy(
        grads_ref.at[own_block], x_ref.at[:, own_columns], own_copied
    )
    own_copy.start()
    swap = Swap(
        swap_sent, swap_got,
        lambda piece: grads_ref.at[piece_rows(piece, (1 - ctx) * rows)],
        lambda piece: x_ref.at[piece_rows(piece), own_columns],
    )

    def products(sums, fsdp, left, right):
        for over_x in (1, 0):
            for over_y in (1, 0):
                number = sums.number(fsdp, over_x, over_y)
                columns = pl.ds(pl.multiple_of(number * shard, shard), shard)
                product = dot_rows(left[:, columns], right[...])
                sums.parts[sums.rows(number), :] = product.astype(jnp.bfloat16)

    def opening():
        @pl.loop(0, PIECES)
        def _(piece):
            swap.start(piece)

        for copy in copies[:2]:
            copy.wait()
        products(output_sum, output_sum.twin, branch_ref, attended_ref)
        output_sum.start()
        products(output_sum, output_sum.fsdp, branch_ref, attended_ref)
        output_sum.second()
        for copy in copies[2:]:
            copy.wait()
        own_copy.wait()

    last = PIECES - 1
    begin = jnp.where((me == 0) | (me == count - 1), last, 2)

    def before(piece):
        @pl.when(piece <= begin)
        def _():
            swap.wait_arrival(piece)

    def after(piece):
        @pl.when(piece == begin)
        def _():
            @pl.loop(begin + 1, PIECES)
            def _(other):
                swap.wait_arrival(other)

            products(plane_sum, plane_sum.twin, tokens_ref, x_ref)
            plane_sum.start()

        @pl.when(piece == jnp.minimum(begin + 1, last))
        def _():
            products(plane_sum, plane_sum.fsdp, tokens_ref, x_ref)

        pl.when(piece == jnp.minimum(begin + 2, last))(plane_sum.second)
        pl.when(piece == jnp.minimum(begin + 3, last))(output_sum.third)

    def closing():
        plane_sum.third()

    input_kernel(
        sizes, x_ref, weight, inner_ref, first_ref, second_ref, hidden_ref, out_ref, vectors_ref,
        rows_ref, term_ref, total, slots, own_vectors, tp_slots, plane_slots,
        sum_sent, sum_got, tp_sent, tp_got, plane_sent, plane_got,
        hooks=(opening, before, after, closing),
    )
    third = part // 3

    def put_part(side, rows, values):
        for i, ref in enumerate((query_out, key_out, value_out)):
            ref[rows, side * third : (side + 1) * third] = values[:, i * third : (i + 1) * third]

    def put_output(side, rows, values):
        output_out[rows, side * output_sum.half : (side + 1) * output_sum.half] = values

    plane_sum.finish(put_part)
    output_sum.finish(put_output)

    @pl.loop(0, PIECES)
    def _(piece):
        swap.wait_sent(piece)


def leave(
    grads, tokens, weight, inner, first_sums, second_sums, hidden_sums, branch, attended,
    collective_id,
):
    sizes = tuple(lax.axis_size(axis) for axis in ("fsdp", "ctx", "tp"))
    count = sizes[2]
    others = sizes[0] * sizes[1] - 1
    rows, features = tokens.shape
    part = grads.shape[1]
    width = features // count
    height = rows // PIECES
    shard = features // (others + 1)
    packed = 8 + -(-(hidden_sums.shape[1] + 2 * part) // (8 * width)) * 8
    return pl.pallas_call(
        functools.partial(leave_kernel, sizes),
        out_shape=[
            jax.ShapeDtypeStruct((rows, width), jnp.bfloat16),
            jax.ShapeDtypeStruct((packed, width), jnp.float32),
            *[jax.ShapeDtypeStruct((shard, 2 * part // 3), jnp.float32)] * 4,
        ],
        in_specs=[
            *[pl.BlockSpec(memory_space=pl.ANY)] * 4,
            *[pl.BlockSpec(memory_space=pltpu.VMEM)] * 3,
            *[pl.BlockSpec(memory_space=pl.ANY)] * 2,
        ],
        out_specs=[pl.BlockSpec(memory_space=pltpu.VMEM)] * 6,
        scratch_shapes=[
            *[pltpu.VMEM(x.shape, x.dtype) for x in (tokens, weight, inner, branch, attended)],
            pltpu.SemaphoreType.DMA((5,)),
            pltpu.SemaphoreType.DMA,
            pltpu.VMEM((rows, 2 * part), jnp.bfloat16),
            pltpu.VMEM(first_sums.shape, jnp.float32),
            pltpu.VMEM((height, width), jnp.float32),
            pltpu.VMEM((height, width), jnp.float32),
            pltpu.VMEM((PIECES, count + 1, height, width), jnp.bfloat16),
            pltpu.VMEM((packed, width), jnp.float32),
            pltpu.VMEM((count - 1, 8, width), jnp.float32),
            pltpu.VMEM((others, packed, width), jnp.float32),
            *line_semaphores(count, PIECES)[0],
            pltpu.SemaphoreType.DMA((count - 1,)),
            pltpu.SemaphoreType.DMA((count - 1,)),
            pltpu.SemaphoreType.DMA((others,)),
            pltpu.SemaphoreType.DMA((others,)),
            pltpu.SemaphoreType.DMA((PIECES,)),
            pltpu.SemaphoreType.DMA((PIECES,)),
            *PlaneSum.scratch(others + 1, shard, 2 * part),
            *PlaneSum.scratch(others + 1, shard, attended.shape[1]),
        ],
        compiler_params=pltpu.CompilerParams(
            collective_id=collective_id, has_side_effects=True, vmem_limit_bytes=60 << 20
        ),
        cost_estimate=pl.CostEstimate(
            flops=60_000_000_000, bytes_accessed=64 * rows * width, transcendentals=0
        ),
        name="leave",
    )(grads, tokens, weight, inner, first_sums, second_sums, hidden_sums, branch, attended)


def to_own_rows(wide):
    count = lax.axis_size("tp")
    parts = wide.reshape(PIECES, count, -1, wide.shape[1])
    return lax.dynamic_index_in_dim(parts, lax.axis_index("tp"), 1, keepdims=False).reshape(
        -1, wide.shape[1]
    )


def by_owner(block):
    count = lax.axis_size("tp")
    width = block.shape[1]
    parts = block.reshape(PIECES, count, -1, width).transpose(1, 0, 2, 3)
    return parts.reshape(count, -1, width)


def swap_over_tp(parts):
    return lax.all_to_all(parts, "tp", split_axis=0, concat_axis=0, tiled=True)


def by_rows(parts):
    count, _, width = parts.shape
    return parts.reshape(count, PIECES, -1, width).transpose(1, 0, 2, 3).reshape(-1, width)


def body(
    tokens,
    segments,
    query_weight,
    key_weight,
    value_weight,
    output_weight,
    expand_weight,
    shrink_weight,
    query_bias,
    value_bias,
    hidden_bias,
    norm_gains,
    row_biases,
    out_grad,
):
    rows = tokens.shape[0]
    head_cols = query_weight.shape[1]
    heads = head_cols // HD
    plane = ("fsdp", "ctx")
    plane_sizes = tuple(lax.axis_size(axis) for axis in plane)
    by_heads = plane_sizes == (4, 2) and heads % 2 == 0

    def weight_rows(weight):
        return lax.all_gather(weight, plane, axis=0, tiled=True)

    block_index = lax.axis_index("fsdp") * plane_sizes[1] + lax.axis_index("ctx")
    if by_heads:
        wide_tokens, own_tokens, marks, wide_qkv, full_output, qkv_heads, upstream = enter(
            tokens, norm_gains, row_biases, query_weight, key_weight, value_weight, output_weight,
            query_bias, value_bias, out_grad, 0,
        )
        upstream = upstream.reshape(upstream.shape[0], -1, upstream.shape[3])
        queries = keys = values = qkv_heads
        own_heads = heads // 2
        bounds = (segments.reshape(-1, plane_sizes[1] * rows),)
    else:
        wide_qkv = weight_rows(jnp.concatenate([query_weight, key_weight, value_weight], axis=1))
        wide_tokens, marks = gather_features(tokens, norm_gains, row_biases, 0)
        upstream = by_owner(out_grad)
        own_tokens = to_own_rows(wide_tokens)
        qkv_bias = jnp.concatenate([query_bias, jnp.zeros_like(query_bias), value_bias])
        qkv = dot_plain(wide_tokens, wide_qkv) + qkv_bias.astype(jnp.float32)
        queries, keys, values = jnp.split(qkv.astype(jnp.bfloat16), 3, axis=1)
        own_heads = heads
        keys, values = padded(keys, WIN), padded(values, WIN)
        ids = jnp.concatenate(
            [
                jnp.full((WIN,), -1, jnp.int32),
                segments,
                jnp.full((WIN,), jnp.iinfo(jnp.int32).max, jnp.int32),
            ]
        )
        full_output, full_expand = weight_rows(output_weight), weight_rows(expand_weight)
        key_ids = lax.dynamic_slice_in_dim(ids, block_index * rows, rows + 2 * WIN, 0)
        bounds = key_bounds(key_ids[WIN : WIN + rows], key_ids, WIN)
    places = (0, own_heads, 2 * own_heads) if by_heads else (0, 0, 0)
    marks, upstream = lax.optimization_barrier((marks, upstream))
    upstream = swap_over_tp(upstream)
    attended_heads, lse = attend(queries, keys, values, own_heads, bounds, places)
    attended_heads, upstream = lax.optimization_barrier((attended_heads, upstream))

    own_rows, features = own_tokens.shape
    hidden_cols = expand_weight.shape[1]

    def shape(extent, kind=jnp.float32):
        return jax.ShapeDtypeStruct(extent, kind)

    own_shape = shape((own_rows, features))
    def owner_sum(grad):
        return lax.psum_scatter(
            grad, plane, scatter_dimension=0, tiled=True
        )

    if by_heads:
        (
            attended, mixed_own, grad_inner, branch_low, attended_grad,
            first_sums, second_sums, hidden_sums, shrink_grad, expand_part,
        ) = middle(
            attended_heads, full_output, expand_weight, shrink_weight, own_tokens, upstream,
            marks, hidden_bias[None], 1,
        )
        expand_grad = owner_sum(expand_part)
        mixed = by_rows(swap_over_tp(mixed_own))
        (grads,) = attend_back(
            queries, keys, values, attended_heads, attended_grad, lse, bounds, places, True
        )
        grads, mixed = lax.optimization_barrier((grads, mixed))
    else:
        full_shrink = weight_rows(shrink_weight)
        norm_low, first_norm, normed_one, inverse_one, hidden, activated = relay(
            attended_heads, full_output, full_expand,
            [own_tokens, marks], first_norm_step,
            [own_shape, own_shape, shape((own_rows, 128))],
            [hidden_bias.astype(jnp.float32)[None]], expand_step,
            [shape((rows, hidden_cols)), shape((rows, hidden_cols), jnp.bfloat16)],
            1, "first_norm",
        )
        ffn_low, mixed_own, grad_second, second_sums, hidden_low, hidden_sums = relay(
            activated, full_shrink, None,
            [first_norm, upstream, marks], second_norm_step,
            [shape(upstream.shape, jnp.bfloat16), own_shape, shape((8, features))],
            [hidden], shrink_step,
            [shape((rows, hidden_cols), jnp.bfloat16), shape((8, hidden_cols))],
            2, "second_norm",
        )
        shrink_grad = owner_sum(dot_rows(ffn_low, activated).astype(jnp.bfloat16))
        branch_low, grad_inner, first_sums, attended_grad = relay(
            hidden_low, full_expand, full_output,
            [grad_second, normed_one, inverse_one, marks], first_back_step,
            [own_shape, shape((8, features))],
            [], attended_step,
            [shape((rows, head_cols), jnp.bfloat16)],
            3, "first_back",
        )
        expand_grad = owner_sum(dot_rows(norm_low, hidden_low).astype(jnp.bfloat16))
        output_grad = owner_sum(dot_rows(branch_low, attended_heads).astype(jnp.bfloat16))
        mixed = by_rows(swap_over_tp(mixed_own))
        query_low, key_ext, value_ext = attend_back(
            queries, keys, values, attended_heads, attended_grad, lse, bounds
        )

        def fold(ext):
            edges = jnp.concatenate([ext[:WIN], ext[WIN + rows :]], axis=0)
            around = padded(edges, WIN)
            own = ext[WIN : WIN + rows]
            own = own.at[:WIN].add(around[:WIN]).at[rows - WIN :].add(around[3 * WIN :])
            return own.astype(jnp.bfloat16)

        qkv_low = jnp.concatenate([query_low, fold(key_ext), fold(value_ext)], axis=1)
    sides = 2 if by_heads else 1

    def by_kind(columns):
        parts = columns.reshape(-1, sides, 3, head_cols // sides)
        return [parts[:, :, i].reshape(-1, head_cols) for i in range(3)]

    if by_heads:
        input_grad, vectors, query_grad, key_grad, value_grad, output_grad = leave(
            grads, wide_tokens, wide_qkv, grad_inner, first_sums, second_sums, hidden_sums,
            branch_low, attended, 4,
        )
        input_grad, expand_grad = lax.optimization_barrier((input_grad, expand_grad))
    else:
        input_grad, vectors = input_sum(
            qkv_low, wide_qkv, grad_inner, first_sums, second_sums, hidden_sums, 4
        )
        qkv_grad = owner_sum(dot_rows(wide_tokens, qkv_low).astype(jnp.bfloat16))
        query_grad, key_grad, value_grad = by_kind(qkv_grad.astype(jnp.float32))
    hidden_rows = hidden_cols // head_cols
    query_sum, _, value_sum = by_kind(
        vectors[8 + hidden_rows : 8 + hidden_rows + 3].reshape(1, -1)
    )
    return (
        mixed,
        input_grad,
        query_grad,
        key_grad,
        value_grad,
        output_grad.astype(jnp.float32),
        expand_grad.astype(jnp.float32),
        shrink_grad.astype(jnp.float32),
        query_sum[0],
        value_sum[0],
        vectors[8 : 8 + hidden_rows].reshape(-1),
        vectors[:2],
        vectors[2:6],
    )


def solution(mesh):
    rows, whole, cols = P(("fsdp", "ctx"), "tp"), P(), P("tp")
    wide = P(None, "tp")
    return jax.shard_map(
        body,
        mesh=mesh,
        in_specs=(rows, whole) + (rows,) * 6 + (cols,) * 3 + (wide,) * 2 + (rows,),
        out_specs=(rows,) * 8 + (cols,) * 3 + (wide,) * 2,
        check_vma=False,
    )
```

```python
import functools
import math

import jax
import jax.numpy as jnp
from jax import lax
from jax.experimental import pallas as pl
from jax.experimental.pallas import tpu as pltpu
from jax.sharding import PartitionSpec as P

HD = 128
WIN = 1024
QB = 512
KB = 512
GROUP = 2

epsilon = 1e-06
hidden_floor = -1e30
score_scale = 1.0 / math.sqrt(HD)
log2_e = 1.0 / math.log(2.0)


def dot_plain(left, right):
    return jnp.dot(left, right, preferred_element_type=jnp.float32)


def dot_rows(left, right):
    return lax.dot_general(
        left, right, (((0,), (0,)), ((), ())), preferred_element_type=jnp.float32
    )


def dot_cols(left, right):
    return lax.dot_general(
        left, right, (((1,), (1,)), ((), ())), preferred_element_type=jnp.float32
    )


def block_bounds(block, rows, bounds, marks):
    if len(bounds) == 4:
        first, last, low, high = bounds
        return first[block], last[block], last[block], last[block], low[...], high[...]
    (ids,) = bounds
    run = ids.shape[1]

    @pl.when((pl.program_id(0) == 0) & (block == 0))
    def _():
        own = lax.axis_index("fsdp")
        own_ids = ids[pl.ds(own, 1), :]
        for i in range(2):
            marks[i] = jnp.sum((own_ids <= 3 * own + i).astype(jnp.int32))

    second, third = marks[0], marks[1]

    def bounds_at(places):
        start = jnp.where(places < second, 0, jnp.where(places < third, second, third))
        stop = jnp.where(places < second, second, jnp.where(places < third, third, run))
        return jnp.maximum(start, places - WIN), jnp.minimum(stop - 1, places + WIN)

    begin = block * rows
    low, high = bounds_at(begin + lax.broadcasted_iota(jnp.int32, (1, rows), 1))
    least_low, least_high = bounds_at(begin)
    most_low, most_high = bounds_at(begin + rows - 1)
    first, last = least_low // KB, most_high // KB + 1
    whole_first = jnp.minimum((most_low + KB - 1) // KB, last)
    whole_last = jnp.maximum((least_high + 1) // KB, whole_first)
    return first, whole_first, whole_last, last, low, high


def over_key_blocks(step, marks, start):
    first, whole_first, whole_last, last = marks
    carry = lax.fori_loop(first, whole_first, functools.partial(step, True), start)
    carry = lax.fori_loop(whole_first, whole_last, functools.partial(step, False), carry)
    return lax.fori_loop(whole_last, last, functools.partial(step, True), carry)


def bound_operands(bounds):
    if len(bounds) == 4:
        mark_spec = pl.BlockSpec((1, QB), lambda h, i, *_: (0, i))
        return list(bounds[:2]), list(bounds[2:]), [mark_spec, mark_spec]
    shape = bounds[0].shape
    return [], list(bounds), [pl.BlockSpec(shape, lambda h, i, *_: (0, 0))]


def head_columns(head):
    return slice(head * HD, (head + 1) * HD)


def attend_kernel(scalars, *refs):
    bounds = refs[:scalars]
    q_ref, k_ref, v_ref, *arrays, out_ref, lse_ref, vt, marks = refs[scalars:]
    block = pl.program_id(1)
    rows = q_ref.shape[0]
    heads = range(GROUP)

    @pl.when(block == 0)
    def _():
        vt[...] = v_ref[...].T

    queries = [q_ref[:, head_columns(h)] for h in heads]
    *span, low, high = block_bounds(block, rows, (*bounds, *arrays), marks)
    places = lax.broadcasted_iota(jnp.int32, (KB, rows), 0)

    def step(masked, number, carry):
        start = pl.multiple_of(number * KB, KB)
        window = pl.ds(start, KB)
        scores = [dot_cols(k_ref[window, head_columns(h)], queries[h]) for h in heads]
        scores = [score * (score_scale * log2_e) for score in scores]
        if masked:
            keep = (places >= low - start) & (places <= high - start)
            scores = [jnp.where(keep, score, hidden_floor) for score in scores]
        tops = [
            jnp.maximum(carry[h][0], jnp.max(scores[h], axis=0, keepdims=True)) for h in heads
        ]
        powers = [jnp.exp2(scores[h] - tops[h]) for h in heads]
        parts = [
            dot_plain(vt[head_columns(h), window], powers[h].astype(jnp.bfloat16)) for h in heads
        ]
        result = []
        for h in heads:
            top, total, mixed = carry[h]
            shrink = jnp.exp2(top - tops[h])
            total = total * shrink + jnp.sum(powers[h], axis=0, keepdims=True)
            result.append((tops[h], total, mixed * shrink + parts[h]))
        return tuple(result)

    start = (
        jnp.full((1, rows), hidden_floor, jnp.float32),
        jnp.zeros((1, rows), jnp.float32),
        jnp.zeros((HD, rows), jnp.float32),
    )
    for h, (top, total, mixed) in enumerate(over_key_blocks(step, span, (start,) * GROUP)):
        out_ref[:, head_columns(h)] = (mixed / total).T.astype(out_ref.dtype)
        lse_ref[h] = top + jnp.log2(total)


def attend(queries, keys, values, heads, bounds, places=(0, 0, 0)):
    rows, span = queries.shape[0], keys.shape[0]
    width = heads * HD
    q_at, k_at, v_at = (place // GROUP for place in places)
    some = GROUP * HD
    scalars, arrays, specs = bound_operands(bounds)
    return pl.pallas_call(
        functools.partial(attend_kernel, len(scalars)),
        out_shape=(
            jax.ShapeDtypeStruct((rows, width), jnp.bfloat16),
            jax.ShapeDtypeStruct((heads, 1, rows), jnp.float32),
        ),
        grid_spec=pltpu.PrefetchScalarGridSpec(
            num_scalar_prefetch=len(scalars),
            grid=(heads // GROUP, rows // QB),
            in_specs=[
                pl.BlockSpec((QB, some), lambda h, i, *_: (i, h + q_at)),
                pl.BlockSpec((span, some), lambda h, i, *_: (0, h + k_at)),
                pl.BlockSpec((span, some), lambda h, i, *_: (0, h + v_at)),
                *specs,
            ],
            out_specs=[
                pl.BlockSpec((QB, some), lambda h, i, *_: (i, h)),
                pl.BlockSpec((GROUP, 1, QB), lambda h, i, *_: (h, 0, i)),
            ],
            scratch_shapes=[pltpu.VMEM((some, span), jnp.bfloat16), pltpu.SMEM((2,), jnp.int32)],
        ),
        compiler_params=pltpu.CompilerParams(vmem_limit_bytes=60 << 20),
        cost_estimate=pl.CostEstimate(
            flops=3 * rows * span * width,
            bytes_accessed=2 * (2 * rows + 2 * span) * width,
            transcendentals=rows * span * heads,
        ),
        name="attend",
    )(*scalars, queries, keys, values, *arrays)


def attend_back_kernel(scalars, arrays, *refs):
    bounds = refs[:scalars]
    q_ref, k_ref, v_ref, o_ref, g_ref, lse_ref, *refs = refs[scalars:]
    bounds = (*bounds, *refs[:arrays])
    *results, kt, dk_sum, dv_sum, marks = refs[arrays:]
    group, block = pl.program_id(0), pl.program_id(1)
    rows = q_ref.shape[0]
    heads = range(GROUP)

    @pl.when(block == 0)
    def _():
        kt[...] = k_ref[...].T
        dk_sum[...] = jnp.zeros_like(dk_sum)
        dv_sum[...] = jnp.zeros_like(dv_sum)

    queries = [q_ref[:, head_columns(h)] for h in heads]
    upstream = [g_ref[:, head_columns(h)] for h in heads]
    *span, low, high = block_bounds(block, rows, bounds, marks)
    places = lax.broadcasted_iota(jnp.int32, (KB, rows), 0)
    deltas = []
    for h in heads:
        product = upstream[h].astype(jnp.float32) * o_ref[:, head_columns(h)].astype(jnp.float32)
        deltas.append(jnp.sum(product.T, axis=0, keepdims=True))

    def step(masked, number, carry):
        start = pl.multiple_of(number * KB, KB)
        window = pl.ds(start, KB)
        scores = [dot_cols(k_ref[window, head_columns(h)], queries[h]) for h in heads]
        prob_grads = [dot_cols(v_ref[window, head_columns(h)], upstream[h]) for h in heads]
        scores = [scores[h] * (score_scale * log2_e) - lse_ref[h] for h in heads]
        if masked:
            keep = (places >= low - start) & (places <= high - start)
            scores = [jnp.where(keep, score, hidden_floor) for score in scores]
        probs = [jnp.exp2(score) for score in scores]
        grads = [
            (probs[h] * (prob_grads[h] - deltas[h])).astype(jnp.bfloat16) for h in heads
        ]
        for h in heads:
            columns = head_columns(h)
            dv_sum[window, columns] += dot_plain(probs[h].astype(jnp.bfloat16), upstream[h])
            dk_sum[window, columns] += dot_plain(grads[h], queries[h])
        return tuple(
            carry[h] + dot_plain(kt[head_columns(h), window], grads[h]) for h in heads
        )

    start = jnp.zeros((HD, rows), jnp.float32)
    query_grads = over_key_blocks(step, span, (start,) * GROUP)
    if len(results) == 1:
        width = results[0].shape[1] // 3

        def place(part):
            begin = pl.multiple_of(part * width + group * GROUP * HD, GROUP * HD)
            return results[0].at[:, pl.ds(begin, GROUP * HD)]

        query_place = place(0).at[pl.ds(pl.multiple_of(block * rows, rows), rows)]
        key_place, value_place = place(1), place(2)
    else:
        query_place, key_place, value_place = results
    for h in heads:
        query_grad = (query_grads[h] * score_scale).T
        query_place[:, head_columns(h)] = query_grad.astype(query_place.dtype)

    @pl.when(block == pl.num_programs(1) - 1)
    def _():
        key_place[...] = (dk_sum[...] * score_scale).astype(key_place.dtype)
        value_place[...] = dv_sum[...].astype(value_place.dtype)


def attend_back(
    queries, keys, values, out, upstream, lse, bounds, places=(0, 0, 0), merged=False
):
    rows, width = out.shape
    span = keys.shape[0]
    heads = width // HD
    q_at, k_at, v_at = (place // GROUP for place in places)
    some = GROUP * HD
    row_spec = pl.BlockSpec((QB, some), lambda h, i, *_: (i, h))
    key_spec = pl.BlockSpec((span, some), lambda h, i, *_: (0, h))
    scalars, arrays, specs = bound_operands(bounds)
    return pl.pallas_call(
        functools.partial(attend_back_kernel, len(scalars), len(arrays)),
        out_shape=[jax.ShapeDtypeStruct((rows, 3 * width), jnp.bfloat16)]
        if merged
        else [
            jax.ShapeDtypeStruct((rows, width), jnp.bfloat16),
            jax.ShapeDtypeStruct((span, width), jnp.float32),
            jax.ShapeDtypeStruct((span, width), jnp.float32),
        ],
        grid_spec=pltpu.PrefetchScalarGridSpec(
            num_scalar_prefetch=len(scalars),
            grid=(heads // GROUP, rows // QB),
            in_specs=[
                pl.BlockSpec((QB, some), lambda h, i, *_: (i, h + q_at)),
                pl.BlockSpec((span, some), lambda h, i, *_: (0, h + k_at)),
                pl.BlockSpec((span, some), lambda h, i, *_: (0, h + v_at)),
                row_spec, row_spec,
                pl.BlockSpec((GROUP, 1, QB), lambda h, i, *_: (h, 0, i)),
                *specs,
            ],
            out_specs=[pl.BlockSpec((rows, 3 * width), lambda h, i, *_: (0, 0))]
            if merged
            else [row_spec, key_spec, key_spec],
            scratch_shapes=[
                pltpu.VMEM((some, span), jnp.bfloat16),
                pltpu.VMEM((span, some), jnp.float32),
                pltpu.VMEM((span, some), jnp.float32),
                pltpu.SMEM((2,), jnp.int32),
            ],
        ),
        compiler_params=pltpu.CompilerParams(vmem_limit_bytes=60 << 20),
        cost_estimate=pl.CostEstimate(
            flops=8 * rows * span * width,
            bytes_accessed=2 * (4 * rows + 4 * span) * width,
            transcendentals=rows * span * heads,
        ),
        name="attend_back",
    )(*scalars, queries, keys, values, out, upstream, lse, *arrays)


def key_bounds(query_ids, key_ids, offset):
    rows, span = query_ids.shape[0], key_ids.shape[0]
    start = jnp.sum(key_ids[:, None] < query_ids[None, :], axis=0, dtype=jnp.int32)
    stop = jnp.sum(key_ids[:, None] <= query_ids[None, :], axis=0, dtype=jnp.int32)
    places = jnp.arange(rows, dtype=jnp.int32) + offset
    low = jnp.maximum(start, places - WIN)
    high = jnp.minimum(stop - 1, places + WIN)
    first = jnp.min(low.reshape(-1, QB), axis=1) // KB
    last = jnp.max(high.reshape(-1, QB), axis=1) // KB + 1
    return first, last, low[None], high[None]


def padded(block, width):
    count = lax.axis_size("ctx")
    forward = [(i, i + 1) for i in range(count - 1)]
    backward = [(target, source) for source, target in forward]
    below = lax.ppermute(block[block.shape[0] - width :], "ctx", forward)
    above = lax.ppermute(block[:width], "ctx", backward)
    return jnp.concatenate([below, block, above], axis=0)


def norm_parts(rows):
    mean = jnp.mean(rows, axis=-1, keepdims=True)
    square = jnp.mean(rows * rows, axis=-1, keepdims=True)
    inverse = lax.rsqrt(square - mean * mean + epsilon)
    return (rows - mean) * inverse, inverse


def norm_back(upstream, normed, inverse, gain):
    scaled = upstream * gain
    first_mean = jnp.mean(scaled, axis=-1, keepdims=True)
    second_mean = jnp.mean(scaled * normed, axis=-1, keepdims=True)
    return inverse * (scaled - first_mean - normed * second_mean)


def gelu_tanh(values):
    return jax.nn.gelu(values, approximate=True)


MESH = pl.DeviceIdType.MESH
PIECES = 8
TILE = 2048


def greet(me, count, others=()):
    barrier = pltpu.get_barrier_semaphore()

    @pl.when(me > 0)
    def _():
        pl.semaphore_signal(barrier, inc=1, device_id={"tp": me - 1}, device_id_type=MESH)

    @pl.when(me < count - 1)
    def _():
        pl.semaphore_signal(barrier, inc=1, device_id={"tp": me + 1}, device_id_type=MESH)

    for other in others:
        pl.semaphore_signal(barrier, inc=1, device_id=other, device_id_type=MESH)

    @pl.when((me == 0) | (me == count - 1))
    def _():
        pl.semaphore_wait(barrier, 1 + len(others))

    @pl.when((me > 0) & (me < count - 1))
    def _():
        pl.semaphore_wait(barrier, 2 + len(others))


def peers_along_tp(me, count):
    return [{"tp": lax.rem(me + i, count)} for i in range(1, count)]


def greet_peers(peers):
    barrier = pltpu.get_barrier_semaphore()
    for peer in peers:
        pl.semaphore_signal(barrier, inc=1, device_id=peer, device_id_type=MESH)
    pl.semaphore_wait(barrier, len(peers))


class Exchange:
    def __init__(self, peers, sent, got, source, place):
        self.peers, self.sent, self.got = peers, sent, got
        self.source, self.place = source, place

    def copies(self):
        for i, peer in enumerate(self.peers):
            yield pltpu.make_async_remote_copy(
                src_ref=self.source(i + 1),
                dst_ref=self.place(i),
                send_sem=self.sent.at[i],
                recv_sem=self.got.at[i],
                device_id=peer,
                device_id_type=MESH,
            )

    def start(self):
        for copy in self.copies():
            copy.start()

    def wait_arrivals(self):
        for copy in self.copies():
            copy.wait_recv()

    def wait_sent(self):
        for copy in self.copies():
            copy.wait_send()


def at_distance(me, count, distance, action):
    for index in (me - distance, me + distance):

        @pl.when((index >= 0) & (index < count))
        def _(index=index):
            action(index)


class Line:
    def __init__(self, me, count, sum_slots, sum_sent, sum_got, spread_view, spread_sent, spread_got):
        self.me, self.count = me, count
        self.sum_slots, self.sum_sent, self.sum_got = sum_slots, sum_sent, sum_got
        self.spread_view, self.spread_sent, self.spread_got = spread_view, spread_sent, spread_got

    def slot(self, piece):
        return lax.rem(piece, self.sum_slots.shape[0])

    def sum_copy(self, piece, owner):
        onward = jnp.where(owner > self.me, self.me + 1, self.me - 1)
        place = jnp.where((owner < self.me) & (owner == self.me - 1), self.count, owner)
        slot = self.slot(piece)
        return pltpu.make_async_remote_copy(
            src_ref=self.sum_slots.at[slot, owner],
            dst_ref=self.sum_slots.at[slot, place],
            send_sem=self.sum_sent.at[slot, owner],
            recv_sem=self.sum_got.at[slot, place],
            device_id={"tp": onward},
            device_id_type=MESH,
        )

    def sum_arrival(self, piece, place):
        view = self.sum_slots.at[self.slot(piece), place]
        pltpu.make_async_copy(view, view, self.sum_got.at[self.slot(piece), place]).wait()

    def sum_start(self, piece, term):
        me, count = self.me, self.count

        @pl.when((me == 0) | (me == count - 1))
        def _():
            for k in range(count - 1):
                owner = jnp.where(me == 0, count - 1 - k, k)
                self.sum_slots[self.slot(piece), owner] = term(owner).astype(jnp.bfloat16)
                self.sum_copy(piece, owner).start()

    def sum_onward(self, piece, term, distances):
        me, count = self.me, self.count

        @pl.when((me > 0) & (me < count - 1))
        def _():
            for distance in distances:

                def pass_on(owner):
                    self.sum_arrival(piece, owner)
                    slot = self.slot(piece)
                    total = self.sum_slots[slot, owner].astype(jnp.float32) + term(owner)
                    self.sum_slots[slot, owner] = total.astype(jnp.bfloat16)
                    self.sum_copy(piece, owner).start()

                at_distance(me, count, distance, pass_on)

    def sum_end(self, piece, total):
        me, count = self.me, self.count

        @pl.when(me > 0)
        def _():
            self.sum_arrival(piece, me)
            total[...] += self.sum_slots[self.slot(piece), me].astype(jnp.float32)

        @pl.when(me < count - 1)
        def _():
            self.sum_arrival(piece, count)
            total[...] += self.sum_slots[self.slot(piece), count].astype(jnp.float32)

    def sum_sent_all(self, piece):
        for distance in range(1, self.count):
            at_distance(
                self.me, self.count, distance,
                lambda owner: self.sum_copy(piece, owner).wait_send(),
            )

    def sum_finish(self, pieces):
        pl.loop(0, pieces)(self.sum_sent_all)

    def spread_copy(self, piece, owner, to, sent, source=None):
        return pltpu.make_async_remote_copy(
            src_ref=self.spread_view(piece, owner) if source is None else source,
            dst_ref=self.spread_view(piece, owner),
            send_sem=self.spread_sent.at[piece, sent],
            recv_sem=self.spread_got.at[piece, owner],
            device_id={"tp": to},
            device_id_type=MESH,
        )

    def own_copies(self, piece, action, source=None):
        me, count = self.me, self.count

        @pl.when(me > 0)
        def _():
            action(self.spread_copy(piece, me, me - 1, count, source))

        @pl.when(me < count - 1)
        def _():
            action(self.spread_copy(piece, me, me + 1, me, source))

    def spread_start(self, piece, source=None):
        self.own_copies(piece, lambda copy: copy.start(), source)

    def onward_copy(self, piece, owner, action):
        me, count = self.me, self.count

        @pl.when((owner < me) & (me < count - 1))
        def _():
            action(self.spread_copy(piece, owner, me + 1, owner))

        @pl.when((owner > me) & (me > 0))
        def _():
            action(self.spread_copy(piece, owner, me - 1, owner))

    def spread_onward(self, piece, distance):
        def pass_on(owner):
            view = self.spread_view(piece, owner)
            pltpu.make_async_copy(view, view, self.spread_got.at[piece, owner]).wait()
            self.onward_copy(piece, owner, lambda copy: copy.start())

        at_distance(self.me, self.count, distance, pass_on)

    def spread_finish(self, pieces, source=None):
        @pl.loop(0, pieces)
        def _(piece):
            self.own_copies(
                piece, lambda copy: copy.wait_send(), None if source is None else source(piece)
            )
            for distance in range(1, self.count):
                at_distance(
                    self.me, self.count, distance,
                    lambda owner: self.onward_copy(piece, owner, lambda copy: copy.wait_send()),
                )


def line_semaphores(count, pieces):
    return [
        pltpu.SemaphoreType.DMA((pieces, count)),
        pltpu.SemaphoreType.DMA((pieces, count + 1)),
    ], [
        pltpu.SemaphoreType.DMA((pieces, count + 1)),
        pltpu.SemaphoreType.DMA((pieces, count)),
    ]


def put_marks(marks, gains, biases):
    marks[...] = jnp.zeros_like(marks)
    marks[0:2, :] = gains[...].astype(jnp.float32)
    marks[2:6, :] = biases[...].astype(jnp.float32)


def gather_kernel(
    count, x_ref, gains, biases, out_ref, marks_out, marks_ref, slots, sent, got,
    marks_sent, marks_got,
):
    me = lax.axis_index("tp")
    height = x_ref.shape[0] // PIECES
    width = x_ref.shape[1]

    def view(piece, owner):
        return out_ref.at[
            pl.ds(pl.multiple_of(piece * height, height), height),
            pl.ds(pl.multiple_of(owner * width, width), width),
        ]

    def source(piece):
        return x_ref.at[pl.ds(pl.multiple_of(piece * height, height), height)]

    line = Line(me, count, None, None, None, view, sent, got)
    peers = peers_along_tp(me, count)
    put_marks(marks_ref, gains, biases)
    greet_peers(peers)

    @pl.loop(0, PIECES)
    def _(piece):
        line.spread_start(piece, source(piece))

    marks = Exchange(
        peers, marks_sent, marks_got, lambda _: marks_ref, lambda i: slots.at[i]
    )
    marks.start()
    own = pl.ds(pl.multiple_of(me * width, width), width)
    out_ref[:, own] = x_ref[...]
    marks_out[:, own] = marks_ref[...]
    for distance in range(1, count):

        @pl.loop(0, PIECES)
        def _(piece, distance=distance):
            line.spread_onward(piece, distance)

    marks.wait_arrivals()
    for i in range(1, count):
        owner = lax.rem(me - i + count, count)
        marks_out[:, pl.ds(pl.multiple_of(owner * width, width), width)] = slots[i - 1]
    marks.wait_sent()
    line.spread_finish(PIECES, source)


def gather_features(x, gains, biases, collective_id):
    count = lax.axis_size("tp")
    rows, width = x.shape
    return pl.pallas_call(
        functools.partial(gather_kernel, count),
        out_shape=[
            jax.ShapeDtypeStruct((rows, count * width), x.dtype),
            jax.ShapeDtypeStruct((8, count * width), jnp.float32),
        ],
        in_specs=[pl.BlockSpec(memory_space=pltpu.VMEM)] * 3,
        out_specs=[pl.BlockSpec(memory_space=pltpu.VMEM)] * 2,
        scratch_shapes=[
            pltpu.VMEM((8, width), jnp.float32),
            pltpu.VMEM((count - 1, 8, width), jnp.float32),
            *line_semaphores(count, PIECES)[1],
            pltpu.SemaphoreType.DMA((count - 1,)),
            pltpu.SemaphoreType.DMA((count - 1,)),
        ],
        compiler_params=pltpu.CompilerParams(
            collective_id=collective_id, has_side_effects=True, vmem_limit_bytes=16 << 20
        ),
        cost_estimate=pl.CostEstimate(
            flops=0, bytes_accessed=64 * rows * count * width, transcendentals=0
        ),
        name="gather_features",
    )(x, gains, biases)


class Swap:
    def __init__(self, sent, got, source, place):
        self.sent, self.got, self.source, self.place = sent, got, source, place

    def copy(self, piece):
        return pltpu.make_async_remote_copy(
            src_ref=self.source(piece),
            dst_ref=self.place(piece),
            send_sem=self.sent.at[piece],
            recv_sem=self.got.at[piece],
            device_id={"ctx": 1 - lax.axis_index("ctx")},
            device_id_type=MESH,
        )

    def start(self, piece):
        self.copy(piece).start()

    def wait_arrival(self, piece):
        self.copy(piece).wait_recv()

    def wait_sent(self, piece):
        self.copy(piece).wait_send()


class PlaneGather:
    def __init__(self, whole, sent, got):
        self.whole, self.sent, self.got = whole, sent, got
        fsdp, self.ctx = lax.axis_index("fsdp"), lax.axis_index("ctx")
        self.fsdp = fsdp
        self.twin = fsdp + 1 - 2 * lax.rem(fsdp, 2)
        self.along_x = lax.rem(fsdp + 2, 4)
        self.twin_x = lax.rem(self.twin + 2, 4)
        self.core_peer = {"fsdp": self.twin}
        self.x_peer = {"fsdp": self.along_x}
        self.y_peer = {"ctx": 1 - self.ctx}

    def peers(self):
        return [self.core_peer, self.x_peer, self.y_peer]

    def shard(self, fsdp, ctx, half=None):
        height = self.whole.shape[0] // 8
        start = (fsdp * 2 + ctx) * height
        if half is not None:
            height //= 2
            start += half * height
        return self.whole.at[pl.ds(pl.multiple_of(start, height), height)]

    def copy(self, number, view, peer):
        return pltpu.make_async_remote_copy(
            src_ref=view,
            dst_ref=view,
            send_sem=self.sent.at[number],
            recv_sem=self.got.at[number],
            device_id=peer,
            device_id_type=MESH,
        )

    def copies(self):
        own = self.shard(self.fsdp, self.ctx)
        from_x = self.shard(self.along_x, self.ctx)
        from_y = self.shard(self.fsdp, 1 - self.ctx)
        return [
            (own, self.core_peer),
            (own, self.x_peer),
            (own, self.y_peer),
            (from_x, self.core_peer),
            (self.shard(self.along_x, self.ctx, 0), self.y_peer),
            (from_y, self.core_peer),
            (self.shard(self.fsdp, 1 - self.ctx, 1), self.x_peer),
            (self.shard(self.along_x, 1 - self.ctx, 0), self.core_peer),
            (self.shard(self.along_x, 1 - self.ctx, 1), self.core_peer),
        ]

    def arrivals(self):
        return [
            self.shard(self.twin, self.ctx),
            self.shard(self.along_x, self.ctx),
            self.shard(self.fsdp, 1 - self.ctx),
            self.shard(self.twin_x, self.ctx),
            self.shard(self.along_x, 1 - self.ctx, 0),
            self.shard(self.twin, 1 - self.ctx),
            self.shard(self.along_x, 1 - self.ctx, 1),
            self.shard(self.twin_x, 1 - self.ctx, 0),
            self.shard(self.twin_x, 1 - self.ctx, 1),
        ]

    def start(self, *numbers):
        copies = self.copies()
        for number in numbers:
            self.copy(number, *copies[number]).start()

    def wait(self, *numbers):
        arrivals = self.arrivals()
        for number in numbers:
            view = arrivals[number]
            pltpu.make_async_copy(view, view, self.got.at[number]).wait()

    def first(self):
        self.start(1, 2, 0)

    def second(self):
        self.wait(1)
        self.start(4, 3)
        self.wait(2)
        self.start(6, 5)

    def third(self):
        self.wait(4)
        self.start(7)
        self.wait(6)
        self.start(8)

    def last(self):
        self.wait(0, 3, 5, 7, 8)

    def wait_sent(self):
        for number, (view, peer) in enumerate(self.copies()):
            self.copy(number, view, peer).wait_send()


def enter_kernel(
    count, x_ref, gains, biases, query_ref, key_ref, value_ref, output_ref, query_bias, value_bias,
    grad_ref,
    wide_out, own_tokens, marks_out, weight_out, output_out, heads, grad_out,
    wide, weight, output_weight, marks_ref, mark_slots, stage, sent, got, marks_sent, marks_got,
    weight_sent, weight_got, output_sent, output_got, swap_sent, swap_got, put_done, grad_done,
    wide_done, out_done,
):
    me, ctx = lax.axis_index("tp"), lax.axis_index("ctx")
    rows, width = x_ref.shape
    height = rows // PIECES
    half = query_ref.shape[1] // 2
    part = 3 * half

    def piece_rows(piece, start=0):
        return pl.ds(pl.multiple_of(start + piece * height, height), height)

    def view(piece, owner):
        return wide.at[piece_rows(piece), pl.ds(pl.multiple_of(owner * width, width), width)]

    gather = PlaneGather(weight, weight_sent, weight_got)
    output_gather = PlaneGather(output_weight, output_sent, output_got)
    own_shard = gather.shard(gather.fsdp, ctx)
    own = pl.ds(pl.multiple_of(me * width, width), width)
    puts = [
        (ref.at[:, pl.ds(side * half, half)], own_shard.at[:, pl.ds(side * part + i * half, half)])
        for side in range(2)
        for i, ref in enumerate((query_ref, key_ref, value_ref))
    ]
    puts += [
        (output_ref, output_gather.shard(gather.fsdp, ctx)),
        (x_ref, wide.at[:, own]),
    ]
    puts = [
        pltpu.make_async_copy(source, place, put_done.at[i])
        for i, (source, place) in enumerate(puts)
    ]
    for put in puts:
        put.start()
    grads = [
        pltpu.make_async_copy(grad_ref.at[:, owner], grad_out.at[owner], grad_done.at[owner])
        for owner in range(count)
    ]
    line = Line(me, count, None, None, None, view, sent, got)
    tp_peers = peers_along_tp(me, count)
    put_marks(marks_ref, gains, biases)
    greet_peers(tp_peers + gather.peers())

    def source(piece):
        return x_ref.at[piece_rows(piece)]

    for piece in range(2):
        line.spread_start(piece, source(piece))
    for put in puts[:7]:
        put.wait()
    gather.first()
    output_gather.first()
    marks = Exchange(
        tp_peers, marks_sent, marks_got, lambda _: marks_ref, lambda i: mark_slots.at[i]
    )
    marks.start()
    marks_out[:, own] = marks_ref[...]
    for put in puts[7:]:
        put.wait()
    for grad in grads:
        grad.start()
    swap = Swap(
        swap_sent, swap_got,
        lambda piece: stage.at[piece_rows(piece)],
        lambda piece: heads.at[piece_rows(piece, ctx * rows)],
    )

    def products(piece, side, place):
        columns = pl.ds(pl.multiple_of(side * part, part), part)
        result = dot_plain(wide[piece_rows(piece), :], weight[:, columns])
        own_half = pl.ds(pl.multiple_of(side * half, half), half)
        for i, bias in enumerate((query_bias, None, value_bias)):
            values = result[:, i * half : (i + 1) * half]
            if bias is not None:
                values += bias[:, own_half].astype(jnp.float32)
            place[:, i * half : (i + 1) * half] = values.astype(jnp.bfloat16)

    def wide_copy(piece):
        part = piece_rows(piece)
        return pltpu.make_async_copy(wide.at[part], wide_out.at[part], wide_done.at[piece])

    weight_copy = pltpu.make_async_copy(weight, weight_out, out_done.at[0])
    output_copy = pltpu.make_async_copy(output_weight, output_out, out_done.at[1])

    @pl.loop(0, PIECES + 7)
    def _(step):
        def late(pieces, action, least=0):
            @pl.when((step >= pieces + least) & (step < PIECES + pieces))
            def _():
                action(step - pieces)

        def use(piece):
            products(piece, 1 - ctx, stage.at[piece_rows(piece)])
            swap.start(piece)
            products(piece, ctx, heads.at[piece_rows(piece, ctx * rows)])
            wide_copy(piece).start()

        @pl.when(step == 7)
        def _():
            gather.third()
            gather.last()
            weight_copy.start()

        late(0, lambda piece: line.spread_start(piece, source(piece)), 2)
        late(7, use)
        late(5, lambda piece: line.spread_onward(piece, 2))
        late(3, lambda piece: line.spread_onward(piece, 1))
        late(6, lambda piece: [line.spread_onward(piece, i) for i in range(3, count)])
        pl.when(step == 5)(gather.second)
        pl.when(step == 7)(output_gather.second)
        pl.when(step == 9)(output_gather.third)

    own_height = height // count
    for piece in range(PIECES):
        start = pl.multiple_of(piece * height + me * own_height, own_height)
        own_tokens[piece * own_height : (piece + 1) * own_height, :] = wide[
            pl.ds(start, own_height), :
        ]

    marks.wait_arrivals()
    for i in range(1, count):
        owner = lax.rem(me - i + count, count)
        marks_out[:, pl.ds(pl.multiple_of(owner * width, width), width)] = mark_slots[i - 1]

    @pl.loop(0, PIECES)
    def _(piece):
        swap.wait_arrival(piece)
        swap.wait_sent(piece)

    output_gather.last()
    output_copy.start()
    marks.wait_sent()
    gather.wait_sent()
    output_gather.wait_sent()
    for grad in grads:
        grad.wait()
    weight_copy.wait()
    output_copy.wait()

    @pl.loop(0, PIECES)
    def _(piece):
        wide_copy(piece).wait()

    line.spread_finish(PIECES, source)


def enter(
    tokens, gains, biases, query_weight, key_weight, value_weight, output_weight, query_bias,
    value_bias, out_grad, collective_id,
):
    count = lax.axis_size("tp")
    rows, width = tokens.shape
    head_cols = query_weight.shape[1]
    features = count * width
    part = 3 * head_cols // 2
    own = rows // PIECES // count
    low = jnp.bfloat16
    vmem, anywhere = pl.BlockSpec(memory_space=pltpu.VMEM), pl.BlockSpec(memory_space=pl.ANY)
    return pl.pallas_call(
        functools.partial(enter_kernel, count),
        out_shape=[
            jax.ShapeDtypeStruct((rows, features), low),
            jax.ShapeDtypeStruct((rows // count, features), low),
            jax.ShapeDtypeStruct((8, features), jnp.float32),
            jax.ShapeDtypeStruct((features, 2 * part), low),
            jax.ShapeDtypeStruct((features, head_cols), low),
            jax.ShapeDtypeStruct((2 * rows, part), low),
            jax.ShapeDtypeStruct((count, PIECES, own, width), low),
        ],
        in_specs=[anywhere, vmem, vmem, *[anywhere] * 4, vmem, vmem, anywhere],
        out_specs=[anywhere, vmem, vmem, anywhere, anywhere, vmem, vmem],
        scratch_shapes=[
            pltpu.VMEM((rows, features), low),
            pltpu.VMEM((features, 2 * part), low),
            pltpu.VMEM((features, head_cols), low),
            pltpu.VMEM((8, width), jnp.float32),
            pltpu.VMEM((count - 1, 8, width), jnp.float32),
            pltpu.VMEM((rows, part), low),
            *line_semaphores(count, PIECES)[1],
            pltpu.SemaphoreType.DMA((count - 1,)),
            pltpu.SemaphoreType.DMA((count - 1,)),
            *[pltpu.SemaphoreType.DMA((9,))] * 4,
            pltpu.SemaphoreType.DMA((PIECES,)),
            pltpu.SemaphoreType.DMA((PIECES,)),
            pltpu.SemaphoreType.DMA((8,)),
            pltpu.SemaphoreType.DMA((count,)),
            pltpu.SemaphoreType.DMA((PIECES,)),
            pltpu.SemaphoreType.DMA((2,)),
        ],
        compiler_params=pltpu.CompilerParams(
            collective_id=collective_id, has_side_effects=True, vmem_limit_bytes=60 << 20
        ),
        cost_estimate=pl.CostEstimate(
            flops=80_000_000_000, bytes_accessed=64 * rows * features, transcendentals=0
        ),
        name="enter",
    )(
        tokens, gains, biases, query_weight, key_weight, value_weight, output_weight,
        query_bias[None], value_bias[None], out_grad.reshape(PIECES, count, own, width),
    )


def relay_kernel(count, row_step, use_step, sizes, *refs):
    row_in, use_in, row_out, use_out, shared = sizes
    refs = list(refs)

    def take(number):
        taken = refs[:number]
        del refs[:number]
        return taken

    x_ref, sum_weight = take(2)
    use_weight = sum_weight if shared else take(1)[0]
    row_inputs, use_inputs = take(row_in), take(use_in)
    (gathered,) = take(1)
    row_outputs, use_outputs = take(row_out), take(use_out)
    terms, total, slots, sum_sent, sum_got, spread_sent, spread_got = refs
    me = lax.axis_index("tp")
    height = x_ref.shape[0] // PIECES
    own = height // count
    width = sum_weight.shape[0]

    def piece_rows(piece):
        return pl.ds(pl.multiple_of(piece * height, height), height)

    def view(piece, owner):
        return gathered.at[pl.ds(pl.multiple_of(piece * height + owner * own, own), own)]

    line = Line(me, count, slots, sum_sent, sum_got, view, spread_sent, spread_got)
    greet(me, count)

    @pl.loop(0, PIECES + 5)
    def _(step):
        odd = lax.rem(step, 2)

        def term_of(parity):
            return lambda owner: terms[parity, pl.ds(pl.multiple_of(owner * own, own), own), :]

        def late(pieces, action):
            @pl.when((step >= pieces) & (step < PIECES + pieces))
            def _():
                action(step - pieces)

        def use(piece):
            part = piece_rows(piece)
            use_step(part, gathered[part, :], use_weight, use_inputs, use_outputs)

        def form(piece):
            x = x_ref[piece_rows(piece), :]

            @pl.loop(0, width // TILE)
            def _(tile):
                part = pl.ds(pl.multiple_of(tile * TILE, TILE), TILE)
                terms[odd, :, part] = dot_cols(x, sum_weight[part, :])

            line.sum_start(piece, term_of(odd))

        def own_step(piece):
            total[...] = terms[1 - odd, pl.ds(pl.multiple_of(me * own, own), own), :]
            line.sum_end(piece, total)
            view(piece, me)[...] = row_step(piece, total, row_inputs, row_outputs)
            line.spread_start(piece)

        late(5, use)
        late(3, lambda piece: line.spread_onward(piece, 2))
        late(1, lambda piece: line.sum_onward(piece, term_of(1 - odd), [1]))
        late(0, form)
        late(4, lambda piece: [line.spread_onward(piece, i) for i in range(3, count)])
        late(2, lambda piece: line.spread_onward(piece, 1))
        late(0, lambda piece: line.sum_onward(piece, term_of(odd), range(count - 2, 1, -1)))
        late(1, own_step)

    line.sum_finish(PIECES)
    line.spread_finish(PIECES)


def relay(
    x, sum_weight, use_weight, row_inputs, row_step, row_shapes, use_inputs, use_step, use_shapes,
    collective_id, name,
):
    count = lax.axis_size("tp")
    rows = x.shape[0]
    width = sum_weight.shape[0]
    height = rows // PIECES
    own = height // count
    shared = use_weight is None
    operands = [x, sum_weight, *([] if shared else [use_weight]), *row_inputs, *use_inputs]
    shapes = [jax.ShapeDtypeStruct((rows, width), jnp.bfloat16), *row_shapes, *use_shapes]
    sums, spreads = line_semaphores(count, PIECES)
    sizes = (len(row_inputs), len(use_inputs), len(row_shapes), len(use_shapes), shared)
    return pl.pallas_call(
        functools.partial(relay_kernel, count, row_step, use_step, sizes),
        out_shape=shapes,
        in_specs=[pl.BlockSpec(memory_space=pltpu.VMEM)] * len(operands),
        out_specs=[pl.BlockSpec(memory_space=pltpu.VMEM)] * len(shapes),
        scratch_shapes=[
            pltpu.VMEM((2, height, width), jnp.float32),
            pltpu.VMEM((own, width), jnp.float32),
            pltpu.VMEM((PIECES, count + 1, own, width), jnp.bfloat16),
            *sums,
            *spreads,
        ],
        compiler_params=pltpu.CompilerParams(
            collective_id=collective_id, has_side_effects=True, vmem_limit_bytes=60 << 20
        ),
        cost_estimate=pl.CostEstimate(
            flops=100_000_000_000, bytes_accessed=64 * rows * width, transcendentals=0
        ),
        name=name,
    )(*operands)


def own_rows_of(piece, like):
    own = like.shape[0] // PIECES
    return pl.ds(pl.multiple_of(piece * own, own), own)


def first_norm_step(piece, total, inputs, outputs):
    tokens, marks = inputs
    first_norm, normed_one, inverse_one = outputs
    part = own_rows_of(piece, tokens)
    summed = tokens[part, :].astype(jnp.float32) + (total[...] + marks[2:3, :])
    normed, inverse = norm_parts(summed)
    result = normed * marks[0:1, :] + marks[3:4, :]
    first_norm[part, :] = result
    normed_one[part, :] = normed
    inverse_one[part, :] = jnp.broadcast_to(inverse, (inverse.shape[0], 128))
    return result.astype(jnp.bfloat16)


def expand_step(rows, chunk, weight, inputs, outputs):
    (bias,) = inputs
    hidden, activated = outputs

    @pl.loop(0, hidden.shape[1] // TILE)
    def _(tile):
        part = pl.ds(pl.multiple_of(tile * TILE, TILE), TILE)
        values = dot_plain(chunk, weight[:, part]) + bias[:, part]
        hidden[rows, part] = values
        activated[rows, part] = gelu_tanh(values).astype(jnp.bfloat16)


def add_sums(piece, sums, *values):
    @pl.when(piece == 0)
    def _():
        sums[...] = jnp.zeros_like(sums)

    for i, value in enumerate(values):
        sums[i : i + 1, :] += jnp.sum(value, axis=0, keepdims=True)


def second_norm_step(piece, total, inputs, outputs):
    first_norm, out_grad, marks = inputs
    mixed, grad_second, sums = outputs
    part = own_rows_of(piece, first_norm)
    normed, inverse = norm_parts(first_norm[part, :] + total[...] + marks[4:5, :])
    result = (normed * marks[1:2, :] + marks[5:6, :]).astype(jnp.bfloat16)
    count, _, width = mixed.shape
    for i in range(count):
        mixed[i, part, :] = result[:, i * width : (i + 1) * width]
    upstream = jnp.concatenate([out_grad[i, part, :] for i in range(count)], axis=1)
    upstream = upstream.astype(jnp.float32)
    grad = norm_back(upstream, normed, inverse, marks[1:2, :])
    grad_second[part, :] = grad
    low = grad.astype(jnp.bfloat16)
    add_sums(piece, sums, upstream * normed, upstream, low.astype(jnp.float32))
    return low


def gelu_slope(values):
    scale = math.sqrt(2.0 / math.pi)
    square = values * values
    bend = jnp.tanh(scale * values * (1.0 + 0.044715 * square))
    inner = scale * (1.0 + 3 * 0.044715 * square)
    return 0.5 * (1.0 + bend) + 0.5 * values * (1.0 - bend * bend) * inner


def shrink_step(rows, chunk, weight, inputs, outputs):
    (hidden,) = inputs
    hidden_low, sums = outputs

    @pl.when(rows.start == 0)
    def _():
        sums[...] = jnp.zeros_like(sums)

    @pl.loop(0, hidden.shape[1] // TILE)
    def _(tile):
        part = pl.ds(pl.multiple_of(tile * TILE, TILE), TILE)
        grad = dot_plain(chunk, weight[:, part]) * gelu_slope(hidden[rows, part])
        low = grad.astype(jnp.bfloat16)
        hidden_low[rows, part] = low
        sums[0:1, part] += jnp.sum(low.astype(jnp.float32), axis=0, keepdims=True)


def first_back_step(piece, total, inputs, outputs):
    grad_second, normed_one, inverse_one, marks = inputs
    grad_inner, sums = outputs
    part = own_rows_of(piece, grad_second)
    normed = normed_one[part, :]
    grad_first = grad_second[part, :] + total[...]
    grad = norm_back(grad_first, normed, inverse_one[part, 0:1], marks[0:1, :])
    grad_inner[part, :] = grad
    low = grad.astype(jnp.bfloat16)
    add_sums(piece, sums, grad_first * normed, grad_first, low.astype(jnp.float32))
    return low


def attended_step(rows, chunk, weight, inputs, outputs):
    (attended_grad,) = outputs
    attended_grad[rows, :] = dot_plain(chunk, weight[...]).astype(jnp.bfloat16)


class PlaneSum:
    def __init__(self, parts, core_slots, first_slots, last_slots, sent, got):
        self.parts, self.core_slots = parts, core_slots
        self.first_slots, self.last_slots = first_slots, last_slots
        self.sent, self.got = sent, got
        self.fsdp, self.ctx = lax.axis_index("fsdp"), lax.axis_index("ctx")
        self.twin = self.fsdp + 1 - 2 * lax.rem(self.fsdp, 2)
        self.height = parts.shape[0] // 8
        self.half = parts.shape[1] // 2

    def number(self, fsdp, over_x, over_y):
        chip = lax.rem(fsdp + 2 * over_x, 4)
        return chip * 2 + (1 - self.ctx if over_y else self.ctx)

    def rows(self, number):
        return pl.ds(pl.multiple_of(number * self.height, self.height), self.height)

    def view(self, over_x, over_y, side):
        columns = pl.ds(side * self.half, self.half)
        return self.parts.at[self.rows(self.number(self.fsdp, over_x, over_y)), columns]

    def copy(self, number, source, place, peer):
        return pltpu.make_async_remote_copy(
            src_ref=source,
            dst_ref=place,
            send_sem=self.sent.at[number],
            recv_sem=self.got.at[number],
            device_id=peer,
            device_id_type=MESH,
        )

    def core_copy(self, number):
        over_x, over_y = number // 2, number % 2
        source = self.parts.at[self.rows(self.number(self.twin, over_x, over_y))]
        place = self.core_slots.at[self.rows(number)]
        return self.copy(number, source, place, {"fsdp": self.twin})

    def x_peer(self):
        return {"fsdp": lax.rem(self.fsdp + 2, 4)}

    def y_peer(self):
        return {"ctx": 1 - self.ctx}

    def first_copy(self, number):
        slot = self.first_slots.at[number]
        if number < 2:
            return self.copy(4 + number, self.view(1, number, 0), slot, self.x_peer())
        return self.copy(4 + number, self.view(number - 2, 1, 1), slot, self.y_peer())

    def last_copy(self, side):
        slot = self.last_slots.at[side]
        if side == 0:
            return self.copy(8, self.view(0, 1, 0), slot, self.y_peer())
        return self.copy(9, self.view(1, 0, 1), slot, self.x_peer())

    def bands(self, action):
        band = min(self.height, 32)

        @pl.loop(0, self.height // band)
        def _(i):
            action(pl.ds(pl.multiple_of(i * band, band), band))

    def add(self, view, slot):
        def band(part):
            total = view[part, :].astype(jnp.float32) + slot[part, :].astype(jnp.float32)
            view[part, :] = total.astype(view.dtype)

        self.bands(band)

    def start(self):
        for number in (3, 2, 1, 0):
            self.core_copy(number).start()

    def second(self):
        for number in (3, 2, 1, 0):
            self.core_copy(number).wait_recv()
            shard = self.parts.at[self.rows(self.number(self.fsdp, number // 2, number % 2))]
            self.add(shard, self.core_slots.at[self.rows(number)])
            if number == 3:
                self.first_copy(1).start()
                self.first_copy(3).start()
            if number == 2:
                self.first_copy(0).start()
            if number == 1:
                self.first_copy(2).start()

    def third(self):
        self.first_copy(1).wait_recv()
        self.add(self.view(0, 1, 0), self.first_slots.at[1])
        self.last_copy(0).start()
        self.first_copy(3).wait_recv()
        self.add(self.view(1, 0, 1), self.first_slots.at[3])
        self.last_copy(1).start()

    def finish(self, put):
        for side in range(2):
            self.first_copy(2 * side).wait_recv()
            self.last_copy(side).wait_recv()
            view, first, last = self.view(0, 0, side), self.first_slots, self.last_slots

            def band(part, side=side, view=view):
                total = view[part, :].astype(jnp.float32)
                total += first[2 * side, part, :].astype(jnp.float32)
                put(side, part, total + last[side, part, :].astype(jnp.float32))

            self.bands(band)
        for number in range(4):
            self.core_copy(number).wait_send()
            self.first_copy(number).wait_send()
        for side in range(2):
            self.last_copy(side).wait_send()

    @staticmethod
    def scratch(shards, height, width):
        return [
            pltpu.VMEM((shards * height, width), jnp.bfloat16),
            pltpu.VMEM((4 * height, width), jnp.bfloat16),
            *PlaneSum.slots(height, width),
        ]

    @staticmethod
    def slots(height, width):
        return [
            pltpu.VMEM((4, height, width // 2), jnp.bfloat16),
            pltpu.VMEM((2, height, width // 2), jnp.bfloat16),
            pltpu.SemaphoreType.DMA((10,)),
            pltpu.SemaphoreType.DMA((10,)),
        ]


def middle_kernel(
    count, heads_ref, output_weight, expand_shard, shrink_shard, own_tokens, out_grad, marks,
    hidden_bias,
    attended, mixed, inner, branch_out, grad_heads, first_sums, second_sums, hidden_sums,
    shrink_out, expand_out,
    expand_weight, shrink_weight, gathered, activated, slope, normed_one, inverse_one,
    terms, total, slots, stage, expand_stage, first_slots, last_slots, plane_sent, plane_got,
    sum_sent, sum_got, spread_sent, spread_got, expand_sent, expand_got, shrink_sent, shrink_got,
    in_sent, in_got, out_sent, out_got, put_done, branch_done, product_done, ready,
):
    me, ctx = lax.axis_index("tp"), lax.axis_index("ctx")
    rows, width = gathered.shape[0] // 3, gathered.shape[1]
    half = heads_ref.shape[1]
    height = rows // PIECES
    own = height // count
    shard, hidden = width // PIECES, activated.shape[1]
    pieces = 3 * PIECES

    def piece_rows(piece, start=0):
        return pl.ds(pl.multiple_of(start + piece * height, height), height)

    def view(piece, owner):
        return gathered.at[pl.ds(pl.multiple_of(piece * height + owner * own, own), own)]

    line = Line(me, count, slots, sum_sent, sum_got, view, spread_sent, spread_got)
    expand_gather = PlaneGather(expand_weight, expand_sent, expand_got)
    shrink_gather = PlaneGather(shrink_weight, shrink_sent, shrink_got)
    own_half = pl.ds(pl.multiple_of(ctx * half, half), half)
    own_block = pl.ds(pl.multiple_of(ctx * rows, rows), rows)
    puts = [
        pltpu.make_async_copy(source, place, put_done.at[i])
        for i, (source, place) in enumerate(
            (
                (heads_ref.at[own_block], attended.at[:, own_half]),
                (expand_shard, expand_gather.shard(expand_gather.fsdp, ctx)),
                (shrink_shard, shrink_gather.shard(shrink_gather.fsdp, ctx)),
            )
        )
    ]
    for put in puts:
        put.start()
    swap_in = Swap(
        in_sent, in_got,
        lambda piece: heads_ref.at[piece_rows(piece, (1 - ctx) * rows)],
        lambda piece: attended.at[piece_rows(piece), own_half],
    )
    swap_out = Swap(
        out_sent, out_got,
        lambda piece: stage.at[piece_rows(piece)],
        lambda piece: grad_heads.at[piece_rows(piece, ctx * rows)],
    )
    greet(me, count, expand_gather.peers())
    pl.loop(0, PIECES)(swap_in.start)
    for put in puts:
        put.wait()
    expand_gather.first()

    def branch_copy(piece):
        part = piece_rows(piece)
        return pltpu.make_async_copy(
            gathered.at[piece_rows(piece, 2 * rows)], branch_out.at[part], branch_done.at[piece]
        )

    def in_stage(piece, number):
        return (piece >= number * PIECES) & (piece < (number + 1) * PIECES)

    def tiles(extent, action):
        @pl.loop(0, extent // TILE)
        def _(tile):
            action(pl.ds(pl.multiple_of(tile * TILE, TILE), TILE))

    def use(piece):
        line.sum_sent_all(piece)
        part = piece_rows(lax.rem(piece, PIECES))
        chunk_rows = piece_rows(piece)

        @pl.when(in_stage(piece, 0))
        def _():
            chunk = gathered[chunk_rows, :]

            def expand(columns):
                values = dot_plain(chunk, expand_weight[:, columns])
                values += hidden_bias[:, columns].astype(jnp.float32)
                result, bend = gelu_with_slope(values)
                activated[part, columns] = result.astype(jnp.bfloat16)
                slope[part, columns] = bend.astype(jnp.bfloat16)

            tiles(activated.shape[1], expand)

        @pl.when(in_stage(piece, 1))
        def _():
            chunk = gathered[chunk_rows, :]

            def shrink(columns):
                grad = dot_plain(chunk, shrink_weight[:, columns])
                low = (grad * slope[part, columns].astype(jnp.float32)).astype(jnp.bfloat16)
                slope[part, columns] = low
                added = jnp.sum(low.astype(jnp.float32), axis=0, keepdims=True)
                before = jnp.where(piece == PIECES, 0.0, hidden_sums[0:1, columns])
                hidden_sums[0:1, columns] = before + added

            tiles(slope.shape[1], shrink)

        @pl.when(in_stage(piece, 2))
        def _():
            place = piece - 2 * PIECES
            result = dot_plain(gathered[chunk_rows, :], output_weight[...]).astype(jnp.bfloat16)
            here = ctx == 0
            left, right = result[:, :half], result[:, half:]
            stage[part, :] = jnp.where(here, right, left)
            swap_out.start(place)
            grad_heads[piece_rows(place, ctx * rows), :] = jnp.where(here, left, right)
            branch_copy(place).start()

    def form(piece):
        part = piece_rows(lax.rem(piece, PIECES))
        parity = lax.rem(piece, 2)

        def products(x, weight):
            def product(columns):
                terms[parity, :, columns] = dot_cols(x, weight[columns, :])

            tiles(width, product)

        @pl.when(in_stage(piece, 0))
        def _():
            swap_in.wait_arrival(piece)
            products(attended[part, :], output_weight)

        @pl.when(in_stage(piece, 1))
        def _():
            products(activated[part, :], shrink_weight)

        @pl.when(in_stage(piece, 2))
        def _():
            products(slope[part, :], expand_weight)

        line.sum_start(piece, term_of(piece))

    def term_of(piece):
        parity = lax.rem(piece, 2)
        return lambda owner: terms[parity, pl.ds(pl.multiple_of(owner * own, own), own), :]

    def own_step(piece):
        place = lax.rem(piece, PIECES)
        total[...] = term_of(piece)(me)
        line.sum_end(piece, total)

        @pl.when(in_stage(piece, 0))
        def _():
            view(piece, me)[...] = first_norm_step(
                place, total, (own_tokens, marks), (inner, normed_one, inverse_one)
            )

        @pl.when(in_stage(piece, 1))
        def _():
            view(piece, me)[...] = second_norm_step(
                place, total, (inner, out_grad, marks), (mixed, inner, second_sums)
            )

        @pl.when(in_stage(piece, 2))
        def _():
            view(piece, me)[...] = first_back_step(
                place, total, (inner, normed_one, inverse_one, marks), (inner, first_sums)
            )

        line.spread_start(piece)

    def gradient(number, left_start, right, place):
        columns = pl.ds(pl.multiple_of(number * shard, shard), shard)
        def product(part):
            left = gathered[left_start : left_start + rows, columns]
            place[:, part] = dot_rows(left, right[:, part]).astype(place.dtype)

        tiles(place.shape[1], product)

    def expand_copy(number):
        part = pl.ds(pl.multiple_of(number * shard, shard), shard)
        return pltpu.make_async_copy(expand_stage, expand_out.at[part], product_done)

    def expand_step(number):
        pl.when(number > 0)(lambda: expand_copy(number - 1).wait())
        gradient(number, 0, slope, expand_stage)
        expand_copy(number).start()

    plane_sum = PlaneSum(shrink_weight, activated, first_slots, last_slots, plane_sent, plane_got)
    twin = {"fsdp": plane_sum.twin}

    def shrink_step(number):
        pl.when(number == 0)(shrink_gather.wait_sent)
        fsdp = jnp.where(number == 0, plane_sum.twin, plane_sum.fsdp)
        for over_x in (1, 0):
            for over_y in (1, 0):
                owner = plane_sum.number(fsdp, over_x, over_y)
                gradient(owner, rows, activated, shrink_weight.at[plane_sum.rows(owner)])

        @pl.when(number == 1)
        def _():
            pl.semaphore_signal(ready, inc=1, device_id=twin, device_id_type=MESH)

    def shrink_send(_):
        pl.semaphore_wait(ready, 1)
        plane_sum.start()

    def shrink_total(side):
        return pltpu.make_async_copy(
            terms.at[side], shrink_out.at[pl.ds(side * height, height)], put_done.at[side]
        )

    @pl.loop(0, pieces + 5)
    def _(step):
        def late(number, action, most=pieces):
            @pl.when((step >= number) & (step < most + number))
            def _():
                action(step - number)

        pl.when(step == 5)(expand_gather.last)
        pl.when(step == 2 * PIECES + 7)(plane_sum.second)
        pl.when(step == 2 * PIECES + 9)(plane_sum.third)
        late(5, use)
        late(3, lambda piece: line.spread_onward(piece, 2))
        late(1, lambda piece: line.sum_onward(piece, term_of(piece), [1]))
        pl.when(step == PIECES)(shrink_gather.last)
        late(0, form)
        late(4, lambda piece: [line.spread_onward(piece, i) for i in range(3, count)])
        late(2, lambda piece: line.spread_onward(piece, 1))
        late(2 * PIECES + 4, shrink_step, 2)
        late(2 * PIECES + 5, expand_step, PIECES)
        late(2 * PIECES + 6, shrink_send, 1)
        late(0, lambda piece: line.sum_onward(piece, term_of(piece), range(count - 2, 1, -1)))
        late(1, own_step)

        @pl.when(step == 3)
        def _():
            expand_gather.second()
            shrink_gather.first()

        pl.when(step == 4)(expand_gather.third)
        pl.when(step == 6)(shrink_gather.second)
        pl.when(step == 7)(shrink_gather.third)

    expand_copy(PIECES - 1).wait()

    def put_total(side, part, values):
        columns = pl.ds(side * (hidden // 2), hidden // 2)
        start = pl.multiple_of(lax.rem(part.start, height), values.shape[0])
        terms[part.start // height, pl.ds(start, values.shape[0]), columns] = values

    plane_sum.finish(put_total)
    for side in range(2):
        shrink_total(side).start()
    for side in range(2):
        shrink_total(side).wait()

    @pl.loop(0, PIECES)
    def _(piece):
        branch_copy(piece).wait()
        swap_in.wait_sent(piece)
        swap_out.wait_arrival(piece)
        swap_out.wait_sent(piece)

    expand_gather.wait_sent()
    line.spread_finish(pieces)


def gelu_with_slope(values):
    scale = math.sqrt(2.0 / math.pi)
    square = values * values
    bend = 0.5 * jnp.tanh(scale * values * (1.0 + 0.044715 * square)) + 0.5
    inner = (2 * scale) * (1.0 + 3 * 0.044715 * square)
    result = values * bend
    return result, bend + result * (1.0 - bend) * inner


def middle(
    attended_heads, output_weight, expand_shard, shrink_shard, own_tokens, out_grad, marks,
    hidden_bias, collective_id,
):
    count = lax.axis_size("tp")
    rows = attended_heads.shape[0] // 2
    half = attended_heads.shape[1]
    own_rows, width = own_tokens.shape
    hidden = expand_shard.shape[1]
    height = rows // PIECES
    own = height // count
    shard = width // PIECES
    low = jnp.bfloat16
    vmem, anywhere = pl.BlockSpec(memory_space=pltpu.VMEM), pl.BlockSpec(memory_space=pl.ANY)

    def shape(extent, kind=jnp.float32):
        return jax.ShapeDtypeStruct(extent, kind)

    return pl.pallas_call(
        functools.partial(middle_kernel, count),
        out_shape=[
            shape((rows, 2 * half), low),
            shape(out_grad.shape, low),
            shape((own_rows, width)),
            shape((rows, width), low),
            shape((2 * rows, half), low),
            shape((8, width)),
            shape((8, width)),
            shape((8, hidden)),
            shape((shard, hidden)),
            shape((width, hidden), low),
        ],
        in_specs=[anywhere, vmem, anywhere, anywhere, vmem, vmem, vmem, vmem],
        out_specs=[vmem, vmem, vmem, anywhere, vmem, vmem, vmem, vmem, anywhere, anywhere],
        scratch_shapes=[
            pltpu.VMEM((width, hidden), low),
            pltpu.VMEM((width, hidden), low),
            pltpu.VMEM((3 * rows, width), low),
            pltpu.VMEM((rows, hidden), low),
            pltpu.VMEM((rows, hidden), low),
            pltpu.VMEM((own_rows, width), jnp.float32),
            pltpu.VMEM((own_rows, 128), jnp.float32),
            pltpu.VMEM((2, height, width), jnp.float32),
            pltpu.VMEM((own, width), jnp.float32),
            pltpu.VMEM((PIECES, count + 1, own, width), low),
            pltpu.VMEM((rows, half), low),
            pltpu.VMEM((shard, hidden), low),
            *PlaneSum.slots(shard, hidden),
            *line_semaphores(count, PIECES)[0],
            *line_semaphores(count, 3 * PIECES)[1],
            *[pltpu.SemaphoreType.DMA((9,))] * 4,
            *[pltpu.SemaphoreType.DMA((PIECES,))] * 4,
            pltpu.SemaphoreType.DMA((3,)),
            pltpu.SemaphoreType.DMA((PIECES,)),
            pltpu.SemaphoreType.DMA,
            pltpu.SemaphoreType.REGULAR,
        ],
        compiler_params=pltpu.CompilerParams(
            collective_id=collective_id, has_side_effects=True, vmem_limit_bytes=62 << 20
        ),
        cost_estimate=pl.CostEstimate(
            flops=300_000_000_000, bytes_accessed=192 * rows * width, transcendentals=0
        ),
        name="middle",
    )(
        attended_heads, output_weight, expand_shard, shrink_shard, own_tokens, out_grad, marks,
        hidden_bias,
    )


def peers_in_plane(sizes):
    fsdp, ctx = lax.axis_index("fsdp"), lax.axis_index("ctx")
    return [
        {"fsdp": lax.rem(fsdp + i, sizes[0]), "ctx": lax.rem(ctx + j, sizes[1])}
        for i in range(sizes[0])
        for j in range(sizes[1])
        if i or j
    ]


def input_kernel(
    sizes, x_ref, weight, inner_ref, first_ref, second_ref, hidden_ref, out_ref, vectors_ref,
    rows_ref, term_ref, total, slots, own_vectors, tp_slots, plane_slots,
    sum_sent, sum_got, tp_sent, tp_got, plane_sent, plane_got, hooks=None,
):
    count = sizes[2]
    me = lax.axis_index("tp")
    height = x_ref.shape[0] // PIECES
    own = height // count
    width = out_ref.shape[1]
    line = Line(me, count, slots, sum_sent, sum_got, None, None, None)
    tp_peers, plane_peers = peers_along_tp(me, count), peers_in_plane(sizes)
    greet_peers(tp_peers + plane_peers)

    def own_part(index):
        return rows_ref.at[:, pl.ds(pl.multiple_of(index * width, width), width)]

    over_tp = Exchange(
        tp_peers, tp_sent, tp_got,
        lambda i: own_part(lax.rem(me + i, count)), lambda i: tp_slots.at[i],
    )
    over_plane = Exchange(
        plane_peers, plane_sent, plane_got, lambda _: own_vectors, lambda i: plane_slots.at[i]
    )
    opening, before, after, closing = hooks or (lambda *_: None,) * 4
    order = ((0, 0), (1, 0), (0, 2), (0, 1), (1, 2), (1, 1))
    rows_ref[...] = jnp.zeros_like(rows_ref)
    for i, (which, row) in enumerate(order):
        rows_ref[i : i + 1, :] = (first_ref, second_ref)[which][row : row + 1, :]
    opening()
    over_tp.start()

    def terms(piece):
        def term(owner):
            features = pl.ds(pl.multiple_of(owner * width, width), width)
            term_ref[...] = dot_cols(
                x_ref[pl.ds(pl.multiple_of(piece * height, height), height), :],
                weight[features, :],
            )
            inner = inner_ref[pl.ds(pl.multiple_of(piece * own, own), own), features]
            term_ref[pl.ds(pl.multiple_of(me * own, own), own), :] += inner
            return term_ref[...]

        return term

    def pack():
        over_tp.wait_arrivals()
        own_vectors[0:8, :] = own_part(me)[...]
        for i in range(count - 1):
            own_vectors[0:8, :] += tp_slots[i]
        own_vectors[8:, :] = jnp.zeros_like(own_vectors[8:, :])
        hidden_rows = hidden_ref.shape[1] // width
        for i in range(hidden_rows):
            own_vectors[8 + i : 9 + i, :] = hidden_ref[0:1, i * width : (i + 1) * width]
        for i in range(x_ref.shape[1] // width):
            part = x_ref[:, i * width : (i + 1) * width].astype(jnp.float32)
            place = 8 + hidden_rows + i
            own_vectors[place : place + 1, :] = jnp.sum(part, axis=0, keepdims=True)
        over_plane.start()

    @pl.loop(0, PIECES)
    def _(piece):
        before(piece)
        line.sum_start(piece, terms(piece))
        line.sum_onward(piece, terms(piece), range(count - 2, 0, -1))
        after(piece)

    pack()
    closing()

    @pl.loop(0, PIECES)
    def _(piece):
        total[...] = terms(piece)(me)
        line.sum_end(piece, total)
        rows = pl.ds(pl.multiple_of(piece * height, height), height)
        out_ref[rows, :] = total[...].astype(out_ref.dtype)

    over_plane.wait_arrivals()
    vectors_ref[...] = own_vectors[...]
    for i in range(len(plane_peers)):
        vectors_ref[...] += plane_slots[i]
    over_tp.wait_sent()
    over_plane.wait_sent()
    line.sum_finish(PIECES)


def input_sum(x, weight, inner, first_sums, second_sums, hidden_sums, collective_id):
    sizes = tuple(lax.axis_size(axis) for axis in ("fsdp", "ctx", "tp"))
    count = sizes[2]
    others = sizes[0] * sizes[1] - 1
    rows = x.shape[0]
    width = weight.shape[0] // count
    height = rows // PIECES
    packed = 8 + -(-(hidden_sums.shape[1] + x.shape[1]) // (8 * width)) * 8
    return pl.pallas_call(
        functools.partial(input_kernel, sizes),
        out_shape=[
            jax.ShapeDtypeStruct((rows, width), jnp.bfloat16),
            jax.ShapeDtypeStruct((packed, width), jnp.float32),
        ],
        in_specs=[pl.BlockSpec(memory_space=pltpu.VMEM)] * 6,
        out_specs=[pl.BlockSpec(memory_space=pltpu.VMEM)] * 2,
        scratch_shapes=[
            pltpu.VMEM(first_sums.shape, jnp.float32),
            pltpu.VMEM((height, width), jnp.float32),
            pltpu.VMEM((height, width), jnp.float32),
            pltpu.VMEM((PIECES, count + 1, height, width), jnp.bfloat16),
            pltpu.VMEM((packed, width), jnp.float32),
            pltpu.VMEM((count - 1, 8, width), jnp.float32),
            pltpu.VMEM((others, packed, width), jnp.float32),
            *line_semaphores(count, PIECES)[0],
            pltpu.SemaphoreType.DMA((count - 1,)),
            pltpu.SemaphoreType.DMA((count - 1,)),
            pltpu.SemaphoreType.DMA((others,)),
            pltpu.SemaphoreType.DMA((others,)),
        ],
        compiler_params=pltpu.CompilerParams(
            collective_id=collective_id, has_side_effects=True, vmem_limit_bytes=40 << 20
        ),
        cost_estimate=pl.CostEstimate(
            flops=60_000_000_000, bytes_accessed=64 * rows * width, transcendentals=0
        ),
        name="input_sum",
    )(x, weight, inner, first_sums, second_sums, hidden_sums)


def leave_kernel(
    sizes, grads_ref, tokens_in, weight_in, inner_in, first_ref, second_ref, hidden_ref, branch_in,
    attended_in,
    out_ref, vectors_ref, query_out, key_out, value_out, output_out,
    tokens_ref, weight, inner_ref, branch_ref, attended_ref, copied, own_copied,
    x_ref, rows_ref, term_ref, total, slots, own_vectors, tp_slots, plane_slots,
    sum_sent, sum_got, tp_sent, tp_got, plane_sent, plane_got, swap_sent, swap_got, *sum_scratch,
):
    count = sizes[2]
    me, ctx = lax.axis_index("tp"), lax.axis_index("ctx")
    rows = x_ref.shape[0]
    height = rows // PIECES
    part = grads_ref.shape[1]
    plane_sum, output_sum = PlaneSum(*sum_scratch[:6]), PlaneSum(*sum_scratch[6:])
    shard = plane_sum.height

    def piece_rows(piece, start=0):
        return pl.ds(pl.multiple_of(start + piece * height, height), height)

    copies = [
        pltpu.make_async_copy(source, place, copied.at[i])
        for i, (source, place) in enumerate(
            (
                (branch_in, branch_ref),
                (attended_in, attended_ref),
                (weight_in, weight),
                (inner_in, inner_ref),
                (tokens_in, tokens_ref),
            )
        )
    ]
    for copy in copies:
        copy.start()
    own_columns = pl.ds(pl.multiple_of(ctx * part, part), part)
    own_block = pl.ds(pl.multiple_of(ctx * rows, rows), rows)
    own_copy = pltpu.make_async_copy(
        grads_ref.at[own_block], x_ref.at[:, own_columns], own_copied
    )
    own_copy.start()
    swap = Swap(
        swap_sent, swap_got,
        lambda piece: grads_ref.at[piece_rows(piece, (1 - ctx) * rows)],
        lambda piece: x_ref.at[piece_rows(piece), own_columns],
    )

    def products(sums, fsdp, left, right):
        for over_x in (1, 0):
            for over_y in (1, 0):
                number = sums.number(fsdp, over_x, over_y)
                columns = pl.ds(pl.multiple_of(number * shard, shard), shard)
                product = dot_rows(left[:, columns], right[...])
                sums.parts[sums.rows(number), :] = product.astype(jnp.bfloat16)

    def opening():
        @pl.loop(0, PIECES)
        def _(piece):
            swap.start(piece)

        for copy in copies[:2]:
            copy.wait()
        products(output_sum, output_sum.twin, branch_ref, attended_ref)
        output_sum.start()
        products(output_sum, output_sum.fsdp, branch_ref, attended_ref)
        output_sum.second()
        for copy in copies[2:]:
            copy.wait()
        own_copy.wait()

    last = PIECES - 1
    begin = jnp.where((me == 0) | (me == count - 1), last, 2)

    def before(piece):
        @pl.when(piece <= begin)
        def _():
            swap.wait_arrival(piece)

    def after(piece):
        @pl.when(piece == begin)
        def _():
            @pl.loop(begin + 1, PIECES)
            def _(other):
                swap.wait_arrival(other)

            products(plane_sum, plane_sum.twin, tokens_ref, x_ref)
            plane_sum.start()

        @pl.when(piece == jnp.minimum(begin + 1, last))
        def _():
            products(plane_sum, plane_sum.fsdp, tokens_ref, x_ref)

        pl.when(piece == jnp.minimum(begin + 2, last))(plane_sum.second)
        pl.when(piece == jnp.minimum(begin + 3, last))(output_sum.third)

    def closing():
        plane_sum.third()

    input_kernel(
        sizes, x_ref, weight, inner_ref, first_ref, second_ref, hidden_ref, out_ref, vectors_ref,
        rows_ref, term_ref, total, slots, own_vectors, tp_slots, plane_slots,
        sum_sent, sum_got, tp_sent, tp_got, plane_sent, plane_got,
        hooks=(opening, before, after, closing),
    )
    third = part // 3

    def put_part(side, rows, values):
        for i, ref in enumerate((query_out, key_out, value_out)):
            ref[rows, side * third : (side + 1) * third] = values[:, i * third : (i + 1) * third]

    def put_output(side, rows, values):
        output_out[rows, side * output_sum.half : (side + 1) * output_sum.half] = values

    plane_sum.finish(put_part)
    output_sum.finish(put_output)

    @pl.loop(0, PIECES)
    def _(piece):
        swap.wait_sent(piece)


def leave(
    grads, tokens, weight, inner, first_sums, second_sums, hidden_sums, branch, attended,
    collective_id,
):
    sizes = tuple(lax.axis_size(axis) for axis in ("fsdp", "ctx", "tp"))
    count = sizes[2]
    others = sizes[0] * sizes[1] - 1
    rows, features = tokens.shape
    part = grads.shape[1]
    width = features // count
    height = rows // PIECES
    shard = features // (others + 1)
    packed = 8 + -(-(hidden_sums.shape[1] + 2 * part) // (8 * width)) * 8
    return pl.pallas_call(
        functools.partial(leave_kernel, sizes),
        out_shape=[
            jax.ShapeDtypeStruct((rows, width), jnp.bfloat16),
            jax.ShapeDtypeStruct((packed, width), jnp.float32),
            *[jax.ShapeDtypeStruct((shard, 2 * part // 3), jnp.float32)] * 4,
        ],
        in_specs=[
            *[pl.BlockSpec(memory_space=pl.ANY)] * 4,
            *[pl.BlockSpec(memory_space=pltpu.VMEM)] * 3,
            *[pl.BlockSpec(memory_space=pl.ANY)] * 2,
        ],
        out_specs=[pl.BlockSpec(memory_space=pltpu.VMEM)] * 6,
        scratch_shapes=[
            *[pltpu.VMEM(x.shape, x.dtype) for x in (tokens, weight, inner, branch, attended)],
            pltpu.SemaphoreType.DMA((5,)),
            pltpu.SemaphoreType.DMA,
            pltpu.VMEM((rows, 2 * part), jnp.bfloat16),
            pltpu.VMEM(first_sums.shape, jnp.float32),
            pltpu.VMEM((height, width), jnp.float32),
            pltpu.VMEM((height, width), jnp.float32),
            pltpu.VMEM((PIECES, count + 1, height, width), jnp.bfloat16),
            pltpu.VMEM((packed, width), jnp.float32),
            pltpu.VMEM((count - 1, 8, width), jnp.float32),
            pltpu.VMEM((others, packed, width), jnp.float32),
            *line_semaphores(count, PIECES)[0],
            pltpu.SemaphoreType.DMA((count - 1,)),
            pltpu.SemaphoreType.DMA((count - 1,)),
            pltpu.SemaphoreType.DMA((others,)),
            pltpu.SemaphoreType.DMA((others,)),
            pltpu.SemaphoreType.DMA((PIECES,)),
            pltpu.SemaphoreType.DMA((PIECES,)),
            *PlaneSum.scratch(others + 1, shard, 2 * part),
            *PlaneSum.scratch(others + 1, shard, attended.shape[1]),
        ],
        compiler_params=pltpu.CompilerParams(
            collective_id=collective_id, has_side_effects=True, vmem_limit_bytes=60 << 20
        ),
        cost_estimate=pl.CostEstimate(
            flops=60_000_000_000, bytes_accessed=64 * rows * width, transcendentals=0
        ),
        name="leave",
    )(grads, tokens, weight, inner, first_sums, second_sums, hidden_sums, branch, attended)


def to_own_rows(wide):
    count = lax.axis_size("tp")
    parts = wide.reshape(PIECES, count, -1, wide.shape[1])
    return lax.dynamic_index_in_dim(parts, lax.axis_index("tp"), 1, keepdims=False).reshape(
        -1, wide.shape[1]
    )


def by_owner(block):
    count = lax.axis_size("tp")
    width = block.shape[1]
    parts = block.reshape(PIECES, count, -1, width).transpose(1, 0, 2, 3)
    return parts.reshape(count, -1, width)


def swap_over_tp(parts):
    return lax.all_to_all(parts, "tp", split_axis=0, concat_axis=0, tiled=True)


def by_rows(parts):
    count, _, width = parts.shape
    return parts.reshape(count, PIECES, -1, width).transpose(1, 0, 2, 3).reshape(-1, width)


def body(
    tokens,
    segments,
    query_weight,
    key_weight,
    value_weight,
    output_weight,
    expand_weight,
    shrink_weight,
    query_bias,
    value_bias,
    hidden_bias,
    norm_gains,
    row_biases,
    out_grad,
):
    rows = tokens.shape[0]
    head_cols = query_weight.shape[1]
    heads = head_cols // HD
    plane = ("fsdp", "ctx")
    plane_sizes = tuple(lax.axis_size(axis) for axis in plane)
    by_heads = plane_sizes == (4, 2) and heads % 2 == 0

    def weight_rows(weight):
        return lax.all_gather(weight, plane, axis=0, tiled=True)

    block_index = lax.axis_index("fsdp") * plane_sizes[1] + lax.axis_index("ctx")
    if by_heads:
        wide_tokens, own_tokens, marks, wide_qkv, full_output, qkv_heads, upstream = enter(
            tokens, norm_gains, row_biases, query_weight, key_weight, value_weight, output_weight,
            query_bias, value_bias, out_grad, 0,
        )
        upstream = upstream.reshape(upstream.shape[0], -1, upstream.shape[3])
        queries = keys = values = qkv_heads
        own_heads = heads // 2
        bounds = (segments.reshape(-1, plane_sizes[1] * rows),)
    else:
        wide_qkv = weight_rows(jnp.concatenate([query_weight, key_weight, value_weight], axis=1))
        wide_tokens, marks = gather_features(tokens, norm_gains, row_biases, 0)
        upstream = by_owner(out_grad)
        own_tokens = to_own_rows(wide_tokens)
        qkv_bias = jnp.concatenate([query_bias, jnp.zeros_like(query_bias), value_bias])
        qkv = dot_plain(wide_tokens, wide_qkv) + qkv_bias.astype(jnp.float32)
        queries, keys, values = jnp.split(qkv.astype(jnp.bfloat16), 3, axis=1)
        own_heads = heads
        keys, values = padded(keys, WIN), padded(values, WIN)
        ids = jnp.concatenate(
            [
                jnp.full((WIN,), -1, jnp.int32),
                segments,
                jnp.full((WIN,), jnp.iinfo(jnp.int32).max, jnp.int32),
            ]
        )
        full_output, full_expand = weight_rows(output_weight), weight_rows(expand_weight)
        key_ids = lax.dynamic_slice_in_dim(ids, block_index * rows, rows + 2 * WIN, 0)
        bounds = key_bounds(key_ids[WIN : WIN + rows], key_ids, WIN)
    places = (0, own_heads, 2 * own_heads) if by_heads else (0, 0, 0)
    marks, upstream = lax.optimization_barrier((marks, upstream))
    upstream = swap_over_tp(upstream)
    attended_heads, lse = attend(queries, keys, values, own_heads, bounds, places)
    attended_heads, upstream = lax.optimization_barrier((attended_heads, upstream))

    own_rows, features = own_tokens.shape
    hidden_cols = expand_weight.shape[1]

    def shape(extent, kind=jnp.float32):
        return jax.ShapeDtypeStruct(extent, kind)

    own_shape = shape((own_rows, features))
    def owner_sum(grad):
        return lax.psum_scatter(
            grad, plane, scatter_dimension=0, tiled=True
        )

    if by_heads:
        (
            attended, mixed_own, grad_inner, branch_low, attended_grad,
            first_sums, second_sums, hidden_sums, shrink_grad, expand_part,
        ) = middle(
            attended_heads, full_output, expand_weight, shrink_weight, own_tokens, upstream,
            marks, hidden_bias[None], 1,
        )
        expand_grad = owner_sum(expand_part)
        mixed = by_rows(swap_over_tp(mixed_own))
        (grads,) = attend_back(
            queries, keys, values, attended_heads, attended_grad, lse, bounds, places, True
        )
        grads, mixed = lax.optimization_barrier((grads, mixed))
    else:
        full_shrink = weight_rows(shrink_weight)
        norm_low, first_norm, normed_one, inverse_one, hidden, activated = relay(
            attended_heads, full_output, full_expand,
            [own_tokens, marks], first_norm_step,
            [own_shape, own_shape, shape((own_rows, 128))],
            [hidden_bias.astype(jnp.float32)[None]], expand_step,
            [shape((rows, hidden_cols)), shape((rows, hidden_cols), jnp.bfloat16)],
            1, "first_norm",
        )
        ffn_low, mixed_own, grad_second, second_sums, hidden_low, hidden_sums = relay(
            activated, full_shrink, None,
            [first_norm, upstream, marks], second_norm_step,
            [shape(upstream.shape, jnp.bfloat16), own_shape, shape((8, features))],
            [hidden], shrink_step,
            [shape((rows, hidden_cols), jnp.bfloat16), shape((8, hidden_cols))],
            2, "second_norm",
        )
        shrink_grad = owner_sum(dot_rows(ffn_low, activated).astype(jnp.bfloat16))
        branch_low, grad_inner, first_sums, attended_grad = relay(
            hidden_low, full_expand, full_output,
            [grad_second, normed_one, inverse_one, marks], first_back_step,
            [own_shape, shape((8, features))],
            [], attended_step,
            [shape((rows, head_cols), jnp.bfloat16)],
            3, "first_back",
        )
        expand_grad = owner_sum(dot_rows(norm_low, hidden_low).astype(jnp.bfloat16))
        output_grad = owner_sum(dot_rows(branch_low, attended_heads).astype(jnp.bfloat16))
        mixed = by_rows(swap_over_tp(mixed_own))
        query_low, key_ext, value_ext = attend_back(
            queries, keys, values, attended_heads, attended_grad, lse, bounds
        )

        def fold(ext):
            edges = jnp.concatenate([ext[:WIN], ext[WIN + rows :]], axis=0)
            around = padded(edges, WIN)
            own = ext[WIN : WIN + rows]
            own = own.at[:WIN].add(around[:WIN]).at[rows - WIN :].add(around[3 * WIN :])
            return own.astype(jnp.bfloat16)

        qkv_low = jnp.concatenate([query_low, fold(key_ext), fold(value_ext)], axis=1)
    sides = 2 if by_heads else 1

    def by_kind(columns):
        parts = columns.reshape(-1, sides, 3, head_cols // sides)
        return [parts[:, :, i].reshape(-1, head_cols) for i in range(3)]

    if by_heads:
        input_grad, vectors, query_grad, key_grad, value_grad, output_grad = leave(
            grads, wide_tokens, wide_qkv, grad_inner, first_sums, second_sums, hidden_sums,
            branch_low, attended, 4,
        )
        input_grad, expand_grad = lax.optimization_barrier((input_grad, expand_grad))
    else:
        input_grad, vectors = input_sum(
            qkv_low, wide_qkv, grad_inner, first_sums, second_sums, hidden_sums, 4
        )
        qkv_grad = owner_sum(dot_rows(wide_tokens, qkv_low).astype(jnp.bfloat16))
        query_grad, key_grad, value_grad = by_kind(qkv_grad.astype(jnp.float32))
    hidden_rows = hidden_cols // head_cols
    query_sum, _, value_sum = by_kind(
        vectors[8 + hidden_rows : 8 + hidden_rows + 3].reshape(1, -1)
    )
    return (
        mixed,
        input_grad,
        query_grad,
        key_grad,
        value_grad,
        output_grad.astype(jnp.float32),
        expand_grad.astype(jnp.float32),
        shrink_grad.astype(jnp.float32),
        query_sum[0],
        value_sum[0],
        vectors[8 : 8 + hidden_rows].reshape(-1),
        vectors[:2],
        vectors[2:6],
    )


def solution(mesh):
    rows, whole, cols = P(("fsdp", "ctx"), "tp"), P(), P("tp")
    wide = P(None, "tp")
    return jax.shard_map(
        body,
        mesh=mesh,
        in_specs=(rows, whole) + (rows,) * 6 + (cols,) * 3 + (wide,) * 2 + (rows,),
        out_specs=(rows,) * 8 + (cols,) * 3 + (wide,) * 2,
        check_vma=False,
    )
```

```python
import functools
import math

import jax
import jax.numpy as jnp
from jax import lax
from jax.experimental import pallas as pl
from jax.experimental.pallas import tpu as pltpu
from jax.sharding import PartitionSpec as P

HD = 128
WIN = 1024
QB = 512
KB = 512
GROUP = 2

epsilon = 1e-06
hidden_floor = -1e30
score_scale = 1.0 / math.sqrt(HD)
log2_e = 1.0 / math.log(2.0)


def dot_plain(left, right):
    return jnp.dot(left, right, preferred_element_type=jnp.float32)


def dot_rows(left, right):
    return lax.dot_general(
        left, right, (((0,), (0,)), ((), ())), preferred_element_type=jnp.float32
    )


def dot_cols(left, right):
    return lax.dot_general(
        left, right, (((1,), (1,)), ((), ())), preferred_element_type=jnp.float32
    )


def block_bounds(block, rows, bounds, marks):
    if len(bounds) == 4:
        first, last, low, high = bounds
        return first[block], last[block], last[block], last[block], low[...], high[...]
    (ids,) = bounds
    run = ids.shape[1]

    @pl.when((pl.program_id(0) == 0) & (block == 0))
    def _():
        own = lax.axis_index("fsdp")
        own_ids = ids[pl.ds(own, 1), :]
        for i in range(2):
            marks[i] = jnp.sum((own_ids <= 3 * own + i).astype(jnp.int32))

    second, third = marks[0], marks[1]

    def bounds_at(places):
        start = jnp.where(places < second, 0, jnp.where(places < third, second, third))
        stop = jnp.where(places < second, second, jnp.where(places < third, third, run))
        return jnp.maximum(start, places - WIN), jnp.minimum(stop - 1, places + WIN)

    begin = block * rows
    low, high = bounds_at(begin + lax.broadcasted_iota(jnp.int32, (1, rows), 1))
    least_low, least_high = bounds_at(begin)
    most_low, most_high = bounds_at(begin + rows - 1)
    first, last = least_low // KB, most_high // KB + 1
    whole_first = jnp.minimum((most_low + KB - 1) // KB, last)
    whole_last = jnp.maximum((least_high + 1) // KB, whole_first)
    return first, whole_first, whole_last, last, low, high


def over_key_blocks(step, marks, start):
    first, whole_first, whole_last, last = marks
    carry = lax.fori_loop(first, whole_first, functools.partial(step, True), start)
    carry = lax.fori_loop(whole_first, whole_last, functools.partial(step, False), carry)
    return lax.fori_loop(whole_last, last, functools.partial(step, True), carry)


def bound_operands(bounds):
    if len(bounds) == 4:
        mark_spec = pl.BlockSpec((1, QB), lambda h, i, *_: (0, i))
        return list(bounds[:2]), list(bounds[2:]), [mark_spec, mark_spec]
    shape = bounds[0].shape
    return [], list(bounds), [pl.BlockSpec(shape, lambda h, i, *_: (0, 0))]


def head_columns(head):
    return slice(head * HD, (head + 1) * HD)


def attend_kernel(scalars, *refs):
    bounds = refs[:scalars]
    q_ref, k_ref, v_ref, *arrays, out_ref, lse_ref, vt, marks = refs[scalars:]
    block = pl.program_id(1)
    rows = q_ref.shape[0]
    heads = range(GROUP)

    @pl.when(block == 0)
    def _():
        vt[...] = v_ref[...].T

    queries = [q_ref[:, head_columns(h)] for h in heads]
    *span, low, high = block_bounds(block, rows, (*bounds, *arrays), marks)
    places = lax.broadcasted_iota(jnp.int32, (KB, rows), 0)

    def step(masked, number, carry):
        start = pl.multiple_of(number * KB, KB)
        window = pl.ds(start, KB)
        scores = [dot_cols(k_ref[window, head_columns(h)], queries[h]) for h in heads]
        scores = [score * (score_scale * log2_e) for score in scores]
        if masked:
            keep = (places >= low - start) & (places <= high - start)
            scores = [jnp.where(keep, score, hidden_floor) for score in scores]
        tops = [
            jnp.maximum(carry[h][0], jnp.max(scores[h], axis=0, keepdims=True)) for h in heads
        ]
        powers = [jnp.exp2(scores[h] - tops[h]) for h in heads]
        parts = [
            dot_plain(vt[head_columns(h), window], powers[h].astype(jnp.bfloat16)) for h in heads
        ]
        result = []
        for h in heads:
            top, total, mixed = carry[h]
            shrink = jnp.exp2(top - tops[h])
            total = total * shrink + jnp.sum(powers[h], axis=0, keepdims=True)
            result.append((tops[h], total, mixed * shrink + parts[h]))
        return tuple(result)

    start = (
        jnp.full((1, rows), hidden_floor, jnp.float32),
        jnp.zeros((1, rows), jnp.float32),
        jnp.zeros((HD, rows), jnp.float32),
    )
    for h, (top, total, mixed) in enumerate(over_key_blocks(step, span, (start,) * GROUP)):
        out_ref[:, head_columns(h)] = (mixed / total).T.astype(out_ref.dtype)
        lse_ref[h] = top + jnp.log2(total)


def attend(queries, keys, values, heads, bounds, places=(0, 0, 0)):
    rows, span = queries.shape[0], keys.shape[0]
    width = heads * HD
    q_at, k_at, v_at = (place // GROUP for place in places)
    some = GROUP * HD
    scalars, arrays, specs = bound_operands(bounds)
    return pl.pallas_call(
        functools.partial(attend_kernel, len(scalars)),
        out_shape=(
            jax.ShapeDtypeStruct((rows, width), jnp.bfloat16),
            jax.ShapeDtypeStruct((heads, 1, rows), jnp.float32),
        ),
        grid_spec=pltpu.PrefetchScalarGridSpec(
            num_scalar_prefetch=len(scalars),
            grid=(heads // GROUP, rows // QB),
            in_specs=[
                pl.BlockSpec((QB, some), lambda h, i, *_: (i, h + q_at)),
                pl.BlockSpec((span, some), lambda h, i, *_: (0, h + k_at)),
                pl.BlockSpec((span, some), lambda h, i, *_: (0, h + v_at)),
                *specs,
            ],
            out_specs=[
                pl.BlockSpec((QB, some), lambda h, i, *_: (i, h)),
                pl.BlockSpec((GROUP, 1, QB), lambda h, i, *_: (h, 0, i)),
            ],
            scratch_shapes=[pltpu.VMEM((some, span), jnp.bfloat16), pltpu.SMEM((2,), jnp.int32)],
        ),
        compiler_params=pltpu.CompilerParams(vmem_limit_bytes=60 << 20),
        cost_estimate=pl.CostEstimate(
            flops=3 * rows * span * width,
            bytes_accessed=2 * (2 * rows + 2 * span) * width,
            transcendentals=rows * span * heads,
        ),
        name="attend",
    )(*scalars, queries, keys, values, *arrays)


def attend_back_kernel(scalars, arrays, *refs):
    bounds = refs[:scalars]
    q_ref, k_ref, v_ref, o_ref, g_ref, lse_ref, *refs = refs[scalars:]
    bounds = (*bounds, *refs[:arrays])
    *results, kt, dk_sum, dv_sum, marks = refs[arrays:]
    group, block = pl.program_id(0), pl.program_id(1)
    rows = q_ref.shape[0]
    heads = range(GROUP)

    @pl.when(block == 0)
    def _():
        kt[...] = k_ref[...].T
        dk_sum[...] = jnp.zeros_like(dk_sum)
        dv_sum[...] = jnp.zeros_like(dv_sum)

    queries = [q_ref[:, head_columns(h)] for h in heads]
    upstream = [g_ref[:, head_columns(h)] for h in heads]
    *span, low, high = block_bounds(block, rows, bounds, marks)
    places = lax.broadcasted_iota(jnp.int32, (KB, rows), 0)
    deltas = []
    for h in heads:
        product = upstream[h].astype(jnp.float32) * o_ref[:, head_columns(h)].astype(jnp.float32)
        deltas.append(jnp.sum(product.T, axis=0, keepdims=True))

    def step(masked, number, carry):
        start = pl.multiple_of(number * KB, KB)
        window = pl.ds(start, KB)
        scores = [dot_cols(k_ref[window, head_columns(h)], queries[h]) for h in heads]
        prob_grads = [dot_cols(v_ref[window, head_columns(h)], upstream[h]) for h in heads]
        scores = [scores[h] * (score_scale * log2_e) - lse_ref[h] for h in heads]
        if masked:
            keep = (places >= low - start) & (places <= high - start)
            scores = [jnp.where(keep, score, hidden_floor) for score in scores]
        probs = [jnp.exp2(score) for score in scores]
        grads = [
            (probs[h] * (prob_grads[h] - deltas[h])).astype(jnp.bfloat16) for h in heads
        ]
        for h in heads:
            columns = head_columns(h)
            dv_sum[window, columns] += dot_plain(probs[h].astype(jnp.bfloat16), upstream[h])
            dk_sum[window, columns] += dot_plain(grads[h], queries[h])
        return tuple(
            carry[h] + dot_plain(kt[head_columns(h), window], grads[h]) for h in heads
        )

    start = jnp.zeros((HD, rows), jnp.float32)
    query_grads = over_key_blocks(step, span, (start,) * GROUP)
    if len(results) == 1:
        width = results[0].shape[1] // 3

        def place(part):
            begin = pl.multiple_of(part * width + group * GROUP * HD, GROUP * HD)
            return results[0].at[:, pl.ds(begin, GROUP * HD)]

        query_place = place(0).at[pl.ds(pl.multiple_of(block * rows, rows), rows)]
        key_place, value_place = place(1), place(2)
    else:
        query_place, key_place, value_place = results
    for h in heads:
        query_grad = (query_grads[h] * score_scale).T
        query_place[:, head_columns(h)] = query_grad.astype(query_place.dtype)

    @pl.when(block == pl.num_programs(1) - 1)
    def _():
        key_place[...] = (dk_sum[...] * score_scale).astype(key_place.dtype)
        value_place[...] = dv_sum[...].astype(value_place.dtype)


def attend_back(
    queries, keys, values, out, upstream, lse, bounds, places=(0, 0, 0), merged=False
):
    rows, width = out.shape
    span = keys.shape[0]
    heads = width // HD
    q_at, k_at, v_at = (place // GROUP for place in places)
    some = GROUP * HD
    row_spec = pl.BlockSpec((QB, some), lambda h, i, *_: (i, h))
    key_spec = pl.BlockSpec((span, some), lambda h, i, *_: (0, h))
    scalars, arrays, specs = bound_operands(bounds)
    return pl.pallas_call(
        functools.partial(attend_back_kernel, len(scalars), len(arrays)),
        out_shape=[jax.ShapeDtypeStruct((rows, 3 * width), jnp.bfloat16)]
        if merged
        else [
            jax.ShapeDtypeStruct((rows, width), jnp.bfloat16),
            jax.ShapeDtypeStruct((span, width), jnp.float32),
            jax.ShapeDtypeStruct((span, width), jnp.float32),
        ],
        grid_spec=pltpu.PrefetchScalarGridSpec(
            num_scalar_prefetch=len(scalars),
            grid=(heads // GROUP, rows // QB),
            in_specs=[
                pl.BlockSpec((QB, some), lambda h, i, *_: (i, h + q_at)),
                pl.BlockSpec((span, some), lambda h, i, *_: (0, h + k_at)),
                pl.BlockSpec((span, some), lambda h, i, *_: (0, h + v_at)),
                row_spec, row_spec,
                pl.BlockSpec((GROUP, 1, QB), lambda h, i, *_: (h, 0, i)),
                *specs,
            ],
            out_specs=[pl.BlockSpec((rows, 3 * width), lambda h, i, *_: (0, 0))]
            if merged
            else [row_spec, key_spec, key_spec],
            scratch_shapes=[
                pltpu.VMEM((some, span), jnp.bfloat16),
                pltpu.VMEM((span, some), jnp.float32),
                pltpu.VMEM((span, some), jnp.float32),
                pltpu.SMEM((2,), jnp.int32),
            ],
        ),
        compiler_params=pltpu.CompilerParams(vmem_limit_bytes=60 << 20),
        cost_estimate=pl.CostEstimate(
            flops=8 * rows * span * width,
            bytes_accessed=2 * (4 * rows + 4 * span) * width,
            transcendentals=rows * span * heads,
        ),
        name="attend_back",
    )(*scalars, queries, keys, values, out, upstream, lse, *arrays)


def key_bounds(query_ids, key_ids, offset):
    rows, span = query_ids.shape[0], key_ids.shape[0]
    start = jnp.sum(key_ids[:, None] < query_ids[None, :], axis=0, dtype=jnp.int32)
    stop = jnp.sum(key_ids[:, None] <= query_ids[None, :], axis=0, dtype=jnp.int32)
    places = jnp.arange(rows, dtype=jnp.int32) + offset
    low = jnp.maximum(start, places - WIN)
    high = jnp.minimum(stop - 1, places + WIN)
    first = jnp.min(low.reshape(-1, QB), axis=1) // KB
    last = jnp.max(high.reshape(-1, QB), axis=1) // KB + 1
    return first, last, low[None], high[None]


def padded(block, width):
    count = lax.axis_size("ctx")
    forward = [(i, i + 1) for i in range(count - 1)]
    backward = [(target, source) for source, target in forward]
    below = lax.ppermute(block[block.shape[0] - width :], "ctx", forward)
    above = lax.ppermute(block[:width], "ctx", backward)
    return jnp.concatenate([below, block, above], axis=0)


def norm_parts(rows):
    mean = jnp.mean(rows, axis=-1, keepdims=True)
    square = jnp.mean(rows * rows, axis=-1, keepdims=True)
    inverse = lax.rsqrt(square - mean * mean + epsilon)
    return (rows - mean) * inverse, inverse


def norm_back(upstream, normed, inverse, gain):
    scaled = upstream * gain
    first_mean = jnp.mean(scaled, axis=-1, keepdims=True)
    second_mean = jnp.mean(scaled * normed, axis=-1, keepdims=True)
    return inverse * (scaled - first_mean - normed * second_mean)


def gelu_tanh(values):
    return jax.nn.gelu(values, approximate=True)


MESH = pl.DeviceIdType.MESH
PIECES = 8
TILE = 2048
OWN_LATE = 5


def greet(me, count, others=()):
    barrier = pltpu.get_barrier_semaphore()

    @pl.when(me > 0)
    def _():
        pl.semaphore_signal(barrier, inc=1, device_id={"tp": me - 1}, device_id_type=MESH)

    @pl.when(me < count - 1)
    def _():
        pl.semaphore_signal(barrier, inc=1, device_id={"tp": me + 1}, device_id_type=MESH)

    for other in others:
        pl.semaphore_signal(barrier, inc=1, device_id=other, device_id_type=MESH)

    @pl.when((me == 0) | (me == count - 1))
    def _():
        pl.semaphore_wait(barrier, 1 + len(others))

    @pl.when((me > 0) & (me < count - 1))
    def _():
        pl.semaphore_wait(barrier, 2 + len(others))


def peers_along_tp(me, count):
    return [{"tp": lax.rem(me + i, count)} for i in range(1, count)]


def greet_peers(peers):
    barrier = pltpu.get_barrier_semaphore()
    for peer in peers:
        pl.semaphore_signal(barrier, inc=1, device_id=peer, device_id_type=MESH)
    pl.semaphore_wait(barrier, len(peers))


class Exchange:
    def __init__(self, peers, sent, got, source, place):
        self.peers, self.sent, self.got = peers, sent, got
        self.source, self.place = source, place

    def copies(self):
        for i, peer in enumerate(self.peers):
            yield pltpu.make_async_remote_copy(
                src_ref=self.source(i + 1),
                dst_ref=self.place(i),
                send_sem=self.sent.at[i],
                recv_sem=self.got.at[i],
                device_id=peer,
                device_id_type=MESH,
            )

    def start(self):
        for copy in self.copies():
            copy.start()

    def wait_arrivals(self):
        for copy in self.copies():
            copy.wait_recv()

    def wait_sent(self):
        for copy in self.copies():
            copy.wait_send()


def at_distance(me, count, distance, action):
    for index in (me - distance, me + distance):

        @pl.when((index >= 0) & (index < count))
        def _(index=index):
            action(index)


class Line:
    def __init__(self, me, count, sum_slots, sum_sent, sum_got, spread_view, spread_sent, spread_got):
        self.me, self.count = me, count
        self.sum_slots, self.sum_sent, self.sum_got = sum_slots, sum_sent, sum_got
        self.spread_view, self.spread_sent, self.spread_got = spread_view, spread_sent, spread_got

    def slot(self, piece):
        return lax.rem(piece, self.sum_slots.shape[0])

    def sum_copy(self, piece, owner):
        onward = jnp.where(owner > self.me, self.me + 1, self.me - 1)
        place = jnp.where((owner < self.me) & (owner == self.me - 1), self.count, owner)
        slot = self.slot(piece)
        return pltpu.make_async_remote_copy(
            src_ref=self.sum_slots.at[slot, owner],
            dst_ref=self.sum_slots.at[slot, place],
            send_sem=self.sum_sent.at[slot, owner],
            recv_sem=self.sum_got.at[slot, place],
            device_id={"tp": onward},
            device_id_type=MESH,
        )

    def sum_arrival(self, piece, place):
        view = self.sum_slots.at[self.slot(piece), place]
        pltpu.make_async_copy(view, view, self.sum_got.at[self.slot(piece), place]).wait()

    def sum_start(self, piece, term):
        me, count = self.me, self.count

        @pl.when((me == 0) | (me == count - 1))
        def _():
            for k in range(count - 1):
                owner = jnp.where(me == 0, count - 1 - k, k)
                self.sum_slots[self.slot(piece), owner] = term(owner).astype(jnp.bfloat16)
                self.sum_copy(piece, owner).start()

    def sum_onward(self, piece, term, distances):
        me, count = self.me, self.count

        @pl.when((me > 0) & (me < count - 1))
        def _():
            for distance in distances:

                def pass_on(owner):
                    self.sum_arrival(piece, owner)
                    slot = self.slot(piece)
                    total = self.sum_slots[slot, owner].astype(jnp.float32) + term(owner)
                    self.sum_slots[slot, owner] = total.astype(jnp.bfloat16)
                    self.sum_copy(piece, owner).start()

                at_distance(me, count, distance, pass_on)

    def sum_end(self, piece, total):
        me, count = self.me, self.count

        @pl.when(me > 0)
        def _():
            self.sum_arrival(piece, me)
            total[...] += self.sum_slots[self.slot(piece), me].astype(jnp.float32)

        @pl.when(me < count - 1)
        def _():
            self.sum_arrival(piece, count)
            total[...] += self.sum_slots[self.slot(piece), count].astype(jnp.float32)

    def sum_sent_all(self, piece):
        for distance in range(1, self.count):
            at_distance(
                self.me, self.count, distance,
                lambda owner: self.sum_copy(piece, owner).wait_send(),
            )

    def sum_finish(self, pieces):
        pl.loop(0, pieces)(self.sum_sent_all)

    def spread_copy(self, piece, owner, to, sent, source=None):
        return pltpu.make_async_remote_copy(
            src_ref=self.spread_view(piece, owner) if source is None else source,
            dst_ref=self.spread_view(piece, owner),
            send_sem=self.spread_sent.at[piece, sent],
            recv_sem=self.spread_got.at[piece, owner],
            device_id={"tp": to},
            device_id_type=MESH,
        )

    def own_copies(self, piece, action, source=None):
        me, count = self.me, self.count

        @pl.when(me > 0)
        def _():
            action(self.spread_copy(piece, me, me - 1, count, source))

        @pl.when(me < count - 1)
        def _():
            action(self.spread_copy(piece, me, me + 1, me, source))

    def spread_start(self, piece, source=None):
        self.own_copies(piece, lambda copy: copy.start(), source)

    def onward_copy(self, piece, owner, action):
        me, count = self.me, self.count

        @pl.when((owner < me) & (me < count - 1))
        def _():
            action(self.spread_copy(piece, owner, me + 1, owner))

        @pl.when((owner > me) & (me > 0))
        def _():
            action(self.spread_copy(piece, owner, me - 1, owner))

    def spread_onward(self, piece, distance):
        def pass_on(owner):
            view = self.spread_view(piece, owner)
            pltpu.make_async_copy(view, view, self.spread_got.at[piece, owner]).wait()
            self.onward_copy(piece, owner, lambda copy: copy.start())

        at_distance(self.me, self.count, distance, pass_on)

    def spread_finish(self, pieces, source=None):
        @pl.loop(0, pieces)
        def _(piece):
            self.own_copies(
                piece, lambda copy: copy.wait_send(), None if source is None else source(piece)
            )
            for distance in range(1, self.count):
                at_distance(
                    self.me, self.count, distance,
                    lambda owner: self.onward_copy(piece, owner, lambda copy: copy.wait_send()),
                )


def line_semaphores(count, pieces):
    return [
        pltpu.SemaphoreType.DMA((pieces, count)),
        pltpu.SemaphoreType.DMA((pieces, count + 1)),
    ], [
        pltpu.SemaphoreType.DMA((pieces, count + 1)),
        pltpu.SemaphoreType.DMA((pieces, count)),
    ]


def put_marks(marks, gains, biases):
    marks[...] = jnp.zeros_like(marks)
    marks[0:2, :] = gains[...].astype(jnp.float32)
    marks[2:6, :] = biases[...].astype(jnp.float32)


def gather_kernel(
    count, x_ref, gains, biases, out_ref, marks_out, marks_ref, slots, sent, got,
    marks_sent, marks_got,
):
    me = lax.axis_index("tp")
    height = x_ref.shape[0] // PIECES
    width = x_ref.shape[1]

    def view(piece, owner):
        return out_ref.at[
            pl.ds(pl.multiple_of(piece * height, height), height),
            pl.ds(pl.multiple_of(owner * width, width), width),
        ]

    def source(piece):
        return x_ref.at[pl.ds(pl.multiple_of(piece * height, height), height)]

    line = Line(me, count, None, None, None, view, sent, got)
    peers = peers_along_tp(me, count)
    put_marks(marks_ref, gains, biases)
    greet_peers(peers)

    @pl.loop(0, PIECES)
    def _(piece):
        line.spread_start(piece, source(piece))

    marks = Exchange(
        peers, marks_sent, marks_got, lambda _: marks_ref, lambda i: slots.at[i]
    )
    marks.start()
    own = pl.ds(pl.multiple_of(me * width, width), width)
    out_ref[:, own] = x_ref[...]
    marks_out[:, own] = marks_ref[...]
    for distance in range(1, count):

        @pl.loop(0, PIECES)
        def _(piece, distance=distance):
            line.spread_onward(piece, distance)

    marks.wait_arrivals()
    for i in range(1, count):
        owner = lax.rem(me - i + count, count)
        marks_out[:, pl.ds(pl.multiple_of(owner * width, width), width)] = slots[i - 1]
    marks.wait_sent()
    line.spread_finish(PIECES, source)


def gather_features(x, gains, biases, collective_id):
    count = lax.axis_size("tp")
    rows, width = x.shape
    return pl.pallas_call(
        functools.partial(gather_kernel, count),
        out_shape=[
            jax.ShapeDtypeStruct((rows, count * width), x.dtype),
            jax.ShapeDtypeStruct((8, count * width), jnp.float32),
        ],
        in_specs=[pl.BlockSpec(memory_space=pltpu.VMEM)] * 3,
        out_specs=[pl.BlockSpec(memory_space=pltpu.VMEM)] * 2,
        scratch_shapes=[
            pltpu.VMEM((8, width), jnp.float32),
            pltpu.VMEM((count - 1, 8, width), jnp.float32),
            *line_semaphores(count, PIECES)[1],
            pltpu.SemaphoreType.DMA((count - 1,)),
            pltpu.SemaphoreType.DMA((count - 1,)),
        ],
        compiler_params=pltpu.CompilerParams(
            collective_id=collective_id, has_side_effects=True, vmem_limit_bytes=16 << 20
        ),
        cost_estimate=pl.CostEstimate(
            flops=0, bytes_accessed=64 * rows * count * width, transcendentals=0
        ),
        name="gather_features",
    )(x, gains, biases)


class Swap:
    def __init__(self, sent, got, source, place):
        self.sent, self.got, self.source, self.place = sent, got, source, place

    def copy(self, piece):
        return pltpu.make_async_remote_copy(
            src_ref=self.source(piece),
            dst_ref=self.place(piece),
            send_sem=self.sent.at[piece],
            recv_sem=self.got.at[piece],
            device_id={"ctx": 1 - lax.axis_index("ctx")},
            device_id_type=MESH,
        )

    def start(self, piece):
        self.copy(piece).start()

    def wait_arrival(self, piece):
        self.copy(piece).wait_recv()

    def wait_sent(self, piece):
        self.copy(piece).wait_send()


class PlaneGather:
    def __init__(self, whole, sent, got):
        self.whole, self.sent, self.got = whole, sent, got
        fsdp, self.ctx = lax.axis_index("fsdp"), lax.axis_index("ctx")
        self.fsdp = fsdp
        self.twin = fsdp + 1 - 2 * lax.rem(fsdp, 2)
        self.along_x = lax.rem(fsdp + 2, 4)
        self.twin_x = lax.rem(self.twin + 2, 4)
        self.core_peer = {"fsdp": self.twin}
        self.x_peer = {"fsdp": self.along_x}
        self.y_peer = {"ctx": 1 - self.ctx}

    def peers(self):
        return [self.core_peer, self.x_peer, self.y_peer]

    def shard(self, fsdp, ctx, half=None):
        height = self.whole.shape[0] // 8
        start = (fsdp * 2 + ctx) * height
        if half is not None:
            height //= 2
            start += half * height
        return self.whole.at[pl.ds(pl.multiple_of(start, height), height)]

    def copy(self, number, view, peer):
        return pltpu.make_async_remote_copy(
            src_ref=view,
            dst_ref=view,
            send_sem=self.sent.at[number],
            recv_sem=self.got.at[number],
            device_id=peer,
            device_id_type=MESH,
        )

    def copies(self):
        own = self.shard(self.fsdp, self.ctx)
        from_x = self.shard(self.along_x, self.ctx)
        from_y = self.shard(self.fsdp, 1 - self.ctx)
        return [
            (own, self.core_peer),
            (own, self.x_peer),
            (own, self.y_peer),
            (from_x, self.core_peer),
            (self.shard(self.along_x, self.ctx, 0), self.y_peer),
            (from_y, self.core_peer),
            (self.shard(self.fsdp, 1 - self.ctx, 1), self.x_peer),
            (self.shard(self.along_x, 1 - self.ctx, 0), self.core_peer),
            (self.shard(self.along_x, 1 - self.ctx, 1), self.core_peer),
        ]

    def arrivals(self):
        return [
            self.shard(self.twin, self.ctx),
            self.shard(self.along_x, self.ctx),
            self.shard(self.fsdp, 1 - self.ctx),
            self.shard(self.twin_x, self.ctx),
            self.shard(self.along_x, 1 - self.ctx, 0),
            self.shard(self.twin, 1 - self.ctx),
            self.shard(self.along_x, 1 - self.ctx, 1),
            self.shard(self.twin_x, 1 - self.ctx, 0),
            self.shard(self.twin_x, 1 - self.ctx, 1),
        ]

    def start(self, *numbers):
        copies = self.copies()
        for number in numbers:
            self.copy(number, *copies[number]).start()

    def wait(self, *numbers):
        arrivals = self.arrivals()
        for number in numbers:
            view = arrivals[number]
            pltpu.make_async_copy(view, view, self.got.at[number]).wait()

    def first(self):
        self.start(1, 2, 0)

    def second(self):
        self.wait(1)
        self.start(4, 3)
        self.wait(2)
        self.start(6, 5)

    def third(self):
        self.wait(4)
        self.start(7)
        self.wait(6)
        self.start(8)

    def last(self):
        self.wait(0, 3, 5, 7, 8)

    def wait_sent(self):
        for number, (view, peer) in enumerate(self.copies()):
            self.copy(number, view, peer).wait_send()


def enter_kernel(
    count, x_ref, gains, biases, query_ref, key_ref, value_ref, output_ref, unit_biases, grad_ref,
    wide_out, own_tokens, marks_out, weight_out, output_out, heads, grad_out,
    wide, weight, output_weight, marks_ref, mark_slots, stage, sent, got, marks_sent, marks_got,
    weight_sent, weight_got, output_sent, output_got, swap_sent, swap_got, put_done, grad_done,
    wide_done, out_done,
):
    me, ctx = lax.axis_index("tp"), lax.axis_index("ctx")
    rows, width = x_ref.shape
    height = rows // PIECES
    half = query_ref.shape[1] // 2
    part = 3 * half

    def piece_rows(piece, start=0):
        return pl.ds(pl.multiple_of(start + piece * height, height), height)

    def view(piece, owner):
        return wide.at[piece_rows(piece), pl.ds(pl.multiple_of(owner * width, width), width)]

    gather = PlaneGather(weight, weight_sent, weight_got)
    output_gather = PlaneGather(output_weight, output_sent, output_got)
    own_shard = gather.shard(gather.fsdp, ctx)
    own = pl.ds(pl.multiple_of(me * width, width), width)
    puts = [
        (ref.at[:, pl.ds(side * half, half)], own_shard.at[:, pl.ds(side * part + i * half, half)])
        for side in range(2)
        for i, ref in enumerate((query_ref, key_ref, value_ref))
    ]
    puts += [
        (output_ref, output_gather.shard(gather.fsdp, ctx)),
        (x_ref, wide.at[:, own]),
    ]
    puts = [
        pltpu.make_async_copy(source, place, put_done.at[i])
        for i, (source, place) in enumerate(puts)
    ]
    for put in puts:
        put.start()
    grads = [
        pltpu.make_async_copy(grad_ref.at[:, owner], grad_out.at[owner], grad_done.at[owner])
        for owner in range(count)
    ]
    line = Line(me, count, None, None, None, view, sent, got)
    tp_peers = peers_along_tp(me, count)
    put_marks(marks_ref, gains, biases)
    greet_peers(tp_peers + gather.peers())

    def source(piece):
        return x_ref.at[piece_rows(piece)]

    for piece in range(2):
        line.spread_start(piece, source(piece))
    for put in puts[:7]:
        put.wait()
    gather.first()
    output_gather.first()
    marks = Exchange(
        tp_peers, marks_sent, marks_got, lambda _: marks_ref, lambda i: mark_slots.at[i]
    )
    marks.start()
    marks_out[:, own] = marks_ref[...]
    for put in puts[7:]:
        put.wait()
    for grad in grads:
        grad.start()
    swap = Swap(
        swap_sent, swap_got,
        lambda piece: stage.at[piece_rows(piece)],
        lambda piece: heads.at[piece_rows(piece, ctx * rows)],
    )

    def products(piece, side, place):
        columns = pl.ds(pl.multiple_of(side * part, part), part)
        result = dot_plain(wide[piece_rows(piece), :], weight[:, columns])
        for i, bias in enumerate((0, None, 2 * half)):
            values = result[:, i * half : (i + 1) * half]
            if bias is not None:
                own_half = pl.ds(pl.multiple_of(bias + side * half, half), half)
                values += unit_biases[:, own_half].astype(jnp.float32)
            place[:, i * half : (i + 1) * half] = values.astype(jnp.bfloat16)

    def wide_copy(piece):
        part = piece_rows(piece)
        return pltpu.make_async_copy(wide.at[part], wide_out.at[part], wide_done.at[piece])

    weight_copy = pltpu.make_async_copy(weight, weight_out, out_done.at[0])
    output_copy = pltpu.make_async_copy(output_weight, output_out, out_done.at[1])

    @pl.loop(0, PIECES + 7)
    def _(step):
        def late(pieces, action, least=0):
            @pl.when((step >= pieces + least) & (step < PIECES + pieces))
            def _():
                action(step - pieces)

        def use(piece):
            products(piece, 1 - ctx, stage.at[piece_rows(piece)])
            swap.start(piece)
            products(piece, ctx, heads.at[piece_rows(piece, ctx * rows)])
            wide_copy(piece).start()

        @pl.when(step == 7)
        def _():
            gather.third()
            gather.last()
            weight_copy.start()

        late(0, lambda piece: line.spread_start(piece, source(piece)), 2)
        late(7, use)
        late(5, lambda piece: line.spread_onward(piece, 2))
        late(3, lambda piece: line.spread_onward(piece, 1))
        late(6, lambda piece: [line.spread_onward(piece, i) for i in range(3, count)])
        pl.when(step == 5)(gather.second)
        pl.when(step == 7)(output_gather.second)
        pl.when(step == 9)(output_gather.third)

    own_height = height // count
    for piece in range(PIECES):
        start = pl.multiple_of(piece * height + me * own_height, own_height)
        own_tokens[piece * own_height : (piece + 1) * own_height, :] = wide[
            pl.ds(start, own_height), :
        ]

    marks.wait_arrivals()
    for i in range(1, count):
        owner = lax.rem(me - i + count, count)
        marks_out[:, pl.ds(pl.multiple_of(owner * width, width), width)] = mark_slots[i - 1]

    @pl.loop(0, PIECES)
    def _(piece):
        swap.wait_arrival(piece)
        swap.wait_sent(piece)

    output_gather.last()
    output_copy.start()
    marks.wait_sent()
    gather.wait_sent()
    output_gather.wait_sent()
    for grad in grads:
        grad.wait()
    weight_copy.wait()
    output_copy.wait()

    @pl.loop(0, PIECES)
    def _(piece):
        wide_copy(piece).wait()

    line.spread_finish(PIECES, source)


def enter(
    tokens, gains, biases, query_weight, key_weight, value_weight, output_weight, unit_biases,
    out_grad, collective_id,
):
    count = lax.axis_size("tp")
    rows, width = tokens.shape
    head_cols = query_weight.shape[1]
    features = count * width
    part = 3 * head_cols // 2
    own = rows // PIECES // count
    low = jnp.bfloat16
    vmem, anywhere = pl.BlockSpec(memory_space=pltpu.VMEM), pl.BlockSpec(memory_space=pl.ANY)
    return pl.pallas_call(
        functools.partial(enter_kernel, count),
        out_shape=[
            jax.ShapeDtypeStruct((rows, features), low),
            jax.ShapeDtypeStruct((rows // count, features), low),
            jax.ShapeDtypeStruct((8, features), jnp.float32),
            jax.ShapeDtypeStruct((features, 2 * part), low),
            jax.ShapeDtypeStruct((features, head_cols), low),
            jax.ShapeDtypeStruct((2 * rows, part), low),
            jax.ShapeDtypeStruct((count, PIECES, own, width), low),
        ],
        in_specs=[anywhere, vmem, vmem, *[anywhere] * 4, vmem, anywhere],
        out_specs=[anywhere, vmem, vmem, anywhere, anywhere, vmem, vmem],
        scratch_shapes=[
            pltpu.VMEM((rows, features), low),
            pltpu.VMEM((features, 2 * part), low),
            pltpu.VMEM((features, head_cols), low),
            pltpu.VMEM((8, width), jnp.float32),
            pltpu.VMEM((count - 1, 8, width), jnp.float32),
            pltpu.VMEM((rows, part), low),
            *line_semaphores(count, PIECES)[1],
            pltpu.SemaphoreType.DMA((count - 1,)),
            pltpu.SemaphoreType.DMA((count - 1,)),
            *[pltpu.SemaphoreType.DMA((9,))] * 4,
            pltpu.SemaphoreType.DMA((PIECES,)),
            pltpu.SemaphoreType.DMA((PIECES,)),
            pltpu.SemaphoreType.DMA((8,)),
            pltpu.SemaphoreType.DMA((count,)),
            pltpu.SemaphoreType.DMA((PIECES,)),
            pltpu.SemaphoreType.DMA((2,)),
        ],
        compiler_params=pltpu.CompilerParams(
            collective_id=collective_id, has_side_effects=True, vmem_limit_bytes=60 << 20
        ),
        cost_estimate=pl.CostEstimate(
            flops=80_000_000_000, bytes_accessed=64 * rows * features, transcendentals=0
        ),
        name="enter",
    )(
        tokens, gains, biases, query_weight, key_weight, value_weight, output_weight,
        unit_biases, out_grad.reshape(PIECES, count, own, width),
    )


def relay_kernel(count, row_step, use_step, sizes, *refs):
    row_in, use_in, row_out, use_out, shared = sizes
    refs = list(refs)

    def take(number):
        taken = refs[:number]
        del refs[:number]
        return taken

    x_ref, sum_weight = take(2)
    use_weight = sum_weight if shared else take(1)[0]
    row_inputs, use_inputs = take(row_in), take(use_in)
    (gathered,) = take(1)
    row_outputs, use_outputs = take(row_out), take(use_out)
    terms, total, slots, sum_sent, sum_got, spread_sent, spread_got = refs
    me = lax.axis_index("tp")
    height = x_ref.shape[0] // PIECES
    own = height // count
    width = sum_weight.shape[0]

    def piece_rows(piece):
        return pl.ds(pl.multiple_of(piece * height, height), height)

    def view(piece, owner):
        return gathered.at[pl.ds(pl.multiple_of(piece * height + owner * own, own), own)]

    line = Line(me, count, slots, sum_sent, sum_got, view, spread_sent, spread_got)
    greet(me, count)

    @pl.loop(0, PIECES + 5)
    def _(step):
        odd = lax.rem(step, 2)

        def term_of(parity):
            return lambda owner: terms[parity, pl.ds(pl.multiple_of(owner * own, own), own), :]

        def late(pieces, action):
            @pl.when((step >= pieces) & (step < PIECES + pieces))
            def _():
                action(step - pieces)

        def use(piece):
            part = piece_rows(piece)
            use_step(part, gathered[part, :], use_weight, use_inputs, use_outputs)

        def form(piece):
            x = x_ref[piece_rows(piece), :]

            @pl.loop(0, width // TILE)
            def _(tile):
                part = pl.ds(pl.multiple_of(tile * TILE, TILE), TILE)
                terms[odd, :, part] = dot_cols(x, sum_weight[part, :])

            line.sum_start(piece, term_of(odd))

        def own_step(piece):
            total[...] = terms[1 - odd, pl.ds(pl.multiple_of(me * own, own), own), :]
            line.sum_end(piece, total)
            view(piece, me)[...] = row_step(piece, total, row_inputs, row_outputs)
            line.spread_start(piece)

        late(5, use)
        late(3, lambda piece: line.spread_onward(piece, 2))
        late(1, lambda piece: line.sum_onward(piece, term_of(1 - odd), [1]))
        late(0, form)
        late(4, lambda piece: [line.spread_onward(piece, i) for i in range(3, count)])
        late(2, lambda piece: line.spread_onward(piece, 1))
        late(0, lambda piece: line.sum_onward(piece, term_of(odd), range(count - 2, 1, -1)))
        late(1, own_step)

    line.sum_finish(PIECES)
    line.spread_finish(PIECES)


def relay(
    x, sum_weight, use_weight, row_inputs, row_step, row_shapes, use_inputs, use_step, use_shapes,
    collective_id, name,
):
    count = lax.axis_size("tp")
    rows = x.shape[0]
    width = sum_weight.shape[0]
    height = rows // PIECES
    own = height // count
    shared = use_weight is None
    operands = [x, sum_weight, *([] if shared else [use_weight]), *row_inputs, *use_inputs]
    shapes = [jax.ShapeDtypeStruct((rows, width), jnp.bfloat16), *row_shapes, *use_shapes]
    sums, spreads = line_semaphores(count, PIECES)
    sizes = (len(row_inputs), len(use_inputs), len(row_shapes), len(use_shapes), shared)
    return pl.pallas_call(
        functools.partial(relay_kernel, count, row_step, use_step, sizes),
        out_shape=shapes,
        in_specs=[pl.BlockSpec(memory_space=pltpu.VMEM)] * len(operands),
        out_specs=[pl.BlockSpec(memory_space=pltpu.VMEM)] * len(shapes),
        scratch_shapes=[
            pltpu.VMEM((2, height, width), jnp.float32),
            pltpu.VMEM((own, width), jnp.float32),
            pltpu.VMEM((PIECES, count + 1, own, width), jnp.bfloat16),
            *sums,
            *spreads,
        ],
        compiler_params=pltpu.CompilerParams(
            collective_id=collective_id, has_side_effects=True, vmem_limit_bytes=60 << 20
        ),
        cost_estimate=pl.CostEstimate(
            flops=100_000_000_000, bytes_accessed=64 * rows * width, transcendentals=0
        ),
        name=name,
    )(*operands)


def own_rows_of(piece, like):
    own = like.shape[0] // PIECES
    return pl.ds(pl.multiple_of(piece * own, own), own)


def first_norm_step(piece, total, inputs, outputs):
    tokens, marks = inputs
    first_norm, normed_one, inverse_one = outputs
    part = own_rows_of(piece, tokens)
    summed = tokens[part, :].astype(jnp.float32) + (total[...] + marks[2:3, :])
    normed, inverse = norm_parts(summed)
    result = normed * marks[0:1, :] + marks[3:4, :]
    first_norm[part, :] = result
    normed_one[part, :] = normed
    inverse_one[part, :] = jnp.broadcast_to(inverse, (inverse.shape[0], 128))
    return result.astype(jnp.bfloat16)


def expand_step(rows, chunk, weight, inputs, outputs):
    (bias,) = inputs
    hidden, activated = outputs

    @pl.loop(0, hidden.shape[1] // TILE)
    def _(tile):
        part = pl.ds(pl.multiple_of(tile * TILE, TILE), TILE)
        values = dot_plain(chunk, weight[:, part]) + bias[:, part]
        hidden[rows, part] = values
        activated[rows, part] = gelu_tanh(values).astype(jnp.bfloat16)


def add_sums(piece, sums, *values):
    @pl.when(piece == 0)
    def _():
        sums[...] = jnp.zeros_like(sums)

    for i, value in enumerate(values):
        sums[i : i + 1, :] += jnp.sum(value, axis=0, keepdims=True)


def second_norm_step(piece, total, inputs, outputs):
    first_norm, out_grad, marks = inputs
    mixed, grad_second, sums = outputs
    part = own_rows_of(piece, first_norm)
    normed, inverse = norm_parts(first_norm[part, :] + total[...] + marks[4:5, :])
    result = (normed * marks[1:2, :] + marks[5:6, :]).astype(jnp.bfloat16)
    count, _, width = mixed.shape
    for i in range(count):
        mixed[i, part, :] = result[:, i * width : (i + 1) * width]
    upstream = jnp.concatenate([out_grad[i, part, :] for i in range(count)], axis=1)
    upstream = upstream.astype(jnp.float32)
    grad = norm_back(upstream, normed, inverse, marks[1:2, :])
    grad_second[part, :] = grad
    low = grad.astype(jnp.bfloat16)
    add_sums(piece, sums, upstream * normed, upstream, low.astype(jnp.float32))
    return low


def gelu_slope(values):
    scale = math.sqrt(2.0 / math.pi)
    square = values * values
    bend = jnp.tanh(scale * values * (1.0 + 0.044715 * square))
    inner = scale * (1.0 + 3 * 0.044715 * square)
    return 0.5 * (1.0 + bend) + 0.5 * values * (1.0 - bend * bend) * inner


def shrink_step(rows, chunk, weight, inputs, outputs):
    (hidden,) = inputs
    hidden_low, sums = outputs

    @pl.when(rows.start == 0)
    def _():
        sums[...] = jnp.zeros_like(sums)

    @pl.loop(0, hidden.shape[1] // TILE)
    def _(tile):
        part = pl.ds(pl.multiple_of(tile * TILE, TILE), TILE)
        grad = dot_plain(chunk, weight[:, part]) * gelu_slope(hidden[rows, part])
        low = grad.astype(jnp.bfloat16)
        hidden_low[rows, part] = low
        sums[0:1, part] += jnp.sum(low.astype(jnp.float32), axis=0, keepdims=True)


def first_back_step(piece, total, inputs, outputs):
    grad_second, normed_one, inverse_one, marks = inputs
    grad_inner, sums = outputs
    part = own_rows_of(piece, grad_second)
    normed = normed_one[part, :]
    grad_first = grad_second[part, :] + total[...]
    grad = norm_back(grad_first, normed, inverse_one[part, 0:1], marks[0:1, :])
    grad_inner[part, :] = grad
    low = grad.astype(jnp.bfloat16)
    add_sums(piece, sums, grad_first * normed, grad_first, low.astype(jnp.float32))
    return low


def attended_step(rows, chunk, weight, inputs, outputs):
    (attended_grad,) = outputs
    attended_grad[rows, :] = dot_plain(chunk, weight[...]).astype(jnp.bfloat16)


class PlaneSum:
    def __init__(self, parts, core_slots, first_slots, last_slots, sent, got):
        self.parts, self.core_slots = parts, core_slots
        self.first_slots, self.last_slots = first_slots, last_slots
        self.sent, self.got = sent, got
        self.fsdp, self.ctx = lax.axis_index("fsdp"), lax.axis_index("ctx")
        self.twin = self.fsdp + 1 - 2 * lax.rem(self.fsdp, 2)
        self.height = parts.shape[0] // 8
        self.half = parts.shape[1] // 2

    def number(self, fsdp, over_x, over_y):
        chip = lax.rem(fsdp + 2 * over_x, 4)
        return chip * 2 + (1 - self.ctx if over_y else self.ctx)

    def rows(self, number):
        return pl.ds(pl.multiple_of(number * self.height, self.height), self.height)

    def view(self, over_x, over_y, side):
        columns = pl.ds(side * self.half, self.half)
        return self.parts.at[self.rows(self.number(self.fsdp, over_x, over_y)), columns]

    def copy(self, number, source, place, peer):
        return pltpu.make_async_remote_copy(
            src_ref=source,
            dst_ref=place,
            send_sem=self.sent.at[number],
            recv_sem=self.got.at[number],
            device_id=peer,
            device_id_type=MESH,
        )

    def core_copy(self, number):
        over_x, over_y = number // 2, number % 2
        source = self.parts.at[self.rows(self.number(self.twin, over_x, over_y))]
        place = self.core_slots.at[self.rows(number)]
        return self.copy(number, source, place, {"fsdp": self.twin})

    def x_peer(self):
        return {"fsdp": lax.rem(self.fsdp + 2, 4)}

    def y_peer(self):
        return {"ctx": 1 - self.ctx}

    def first_copy(self, number):
        slot = self.first_slots.at[number]
        if number < 2:
            return self.copy(4 + number, self.view(1, number, 0), slot, self.x_peer())
        return self.copy(4 + number, self.view(number - 2, 1, 1), slot, self.y_peer())

    def last_copy(self, side):
        slot = self.last_slots.at[side]
        if side == 0:
            return self.copy(8, self.view(0, 1, 0), slot, self.y_peer())
        return self.copy(9, self.view(1, 0, 1), slot, self.x_peer())

    def bands(self, action):
        band = min(self.height, 32)

        @pl.loop(0, self.height // band)
        def _(i):
            action(pl.ds(pl.multiple_of(i * band, band), band))

    def add(self, view, slot):
        def band(part):
            total = view[part, :].astype(jnp.float32) + slot[part, :].astype(jnp.float32)
            view[part, :] = total.astype(view.dtype)

        self.bands(band)

    def start(self):
        for number in (3, 2, 1, 0):
            self.core_copy(number).start()

    def second(self):
        for number in (3, 2, 1, 0):
            self.core_copy(number).wait_recv()
            shard = self.parts.at[self.rows(self.number(self.fsdp, number // 2, number % 2))]
            self.add(shard, self.core_slots.at[self.rows(number)])
            if number == 3:
                self.first_copy(1).start()
                self.first_copy(3).start()
            if number == 2:
                self.first_copy(0).start()
            if number == 1:
                self.first_copy(2).start()

    def third(self):
        self.first_copy(1).wait_recv()
        self.add(self.view(0, 1, 0), self.first_slots.at[1])
        self.last_copy(0).start()
        self.first_copy(3).wait_recv()
        self.add(self.view(1, 0, 1), self.first_slots.at[3])
        self.last_copy(1).start()

    def finish(self, put):
        for side in range(2):
            self.first_copy(2 * side).wait_recv()
            self.last_copy(side).wait_recv()
            view, first, last = self.view(0, 0, side), self.first_slots, self.last_slots

            def band(part, side=side, view=view):
                total = view[part, :].astype(jnp.float32)
                total += first[2 * side, part, :].astype(jnp.float32)
                put(side, part, total + last[side, part, :].astype(jnp.float32))

            self.bands(band)
        for number in range(4):
            self.core_copy(number).wait_send()
            self.first_copy(number).wait_send()
        for side in range(2):
            self.last_copy(side).wait_send()

    @staticmethod
    def scratch(shards, height, width):
        return [
            pltpu.VMEM((shards * height, width), jnp.bfloat16),
            pltpu.VMEM((4 * height, width), jnp.bfloat16),
            *PlaneSum.slots(height, width),
        ]

    @staticmethod
    def slots(height, width):
        return [
            pltpu.VMEM((4, height, width // 2), jnp.bfloat16),
            pltpu.VMEM((2, height, width // 2), jnp.bfloat16),
            pltpu.SemaphoreType.DMA((10,)),
            pltpu.SemaphoreType.DMA((10,)),
        ]


def middle_kernel(
    count, heads_ref, output_weight, expand_shard, shrink_shard, own_tokens, out_grad, marks,
    unit_biases,
    attended, mixed, inner, branch_out, grad_heads, first_sums, second_sums, hidden_sums,
    shrink_out, expand_out,
    expand_weight, shrink_weight, gathered, activated, slope, normed_one, inverse_one,
    terms, total, slots, stage, expand_stage, first_slots, last_slots, plane_sent, plane_got,
    sum_sent, sum_got, spread_sent, spread_got, expand_sent, expand_got, shrink_sent, shrink_got,
    in_sent, in_got, out_sent, out_got, put_done, branch_done, product_done, ready,
):
    me, ctx = lax.axis_index("tp"), lax.axis_index("ctx")
    rows, width = gathered.shape[0] // 3, gathered.shape[1]
    half = heads_ref.shape[1]
    height = rows // PIECES
    own = height // count
    shard, hidden = width // PIECES, activated.shape[1]
    hidden_bias = unit_biases.at[:, pl.ds(unit_biases.shape[1] - hidden, hidden)]
    pieces = 3 * PIECES

    def piece_rows(piece, start=0):
        return pl.ds(pl.multiple_of(start + piece * height, height), height)

    def view(piece, owner):
        return gathered.at[pl.ds(pl.multiple_of(piece * height + owner * own, own), own)]

    line = Line(me, count, slots, sum_sent, sum_got, view, spread_sent, spread_got)
    expand_gather = PlaneGather(expand_weight, expand_sent, expand_got)
    shrink_gather = PlaneGather(shrink_weight, shrink_sent, shrink_got)
    own_half = pl.ds(pl.multiple_of(ctx * half, half), half)
    own_block = pl.ds(pl.multiple_of(ctx * rows, rows), rows)
    puts = [
        pltpu.make_async_copy(source, place, put_done.at[i])
        for i, (source, place) in enumerate(
            (
                (heads_ref.at[own_block], attended.at[:, own_half]),
                (expand_shard, expand_gather.shard(expand_gather.fsdp, ctx)),
                (shrink_shard, shrink_gather.shard(shrink_gather.fsdp, ctx)),
            )
        )
    ]
    for put in puts:
        put.start()
    swap_in = Swap(
        in_sent, in_got,
        lambda piece: heads_ref.at[piece_rows(piece, (1 - ctx) * rows)],
        lambda piece: attended.at[piece_rows(piece), own_half],
    )
    swap_out = Swap(
        out_sent, out_got,
        lambda piece: stage.at[piece_rows(piece)],
        lambda piece: grad_heads.at[piece_rows(piece, ctx * rows)],
    )
    greet(me, count, expand_gather.peers())
    pl.loop(0, PIECES)(swap_in.start)
    for put in puts:
        put.wait()
    expand_gather.first()

    def branch_copy(piece):
        part = piece_rows(piece)
        return pltpu.make_async_copy(
            gathered.at[piece_rows(piece, 2 * rows)], branch_out.at[part], branch_done.at[piece]
        )

    def in_stage(piece, number):
        return (piece >= number * PIECES) & (piece < (number + 1) * PIECES)

    def tiles(extent, action):
        @pl.loop(0, extent // TILE)
        def _(tile):
            action(pl.ds(pl.multiple_of(tile * TILE, TILE), TILE))

    def use(piece):
        line.sum_sent_all(piece)
        part = piece_rows(lax.rem(piece, PIECES))
        chunk_rows = piece_rows(piece)

        @pl.when(in_stage(piece, 0))
        def _():
            chunk = gathered[chunk_rows, :]

            def expand(columns):
                values = dot_plain(chunk, expand_weight[:, columns])
                values += hidden_bias[:, columns].astype(jnp.float32)
                result, bend = gelu_with_slope(values)
                activated[part, columns] = result.astype(jnp.bfloat16)
                slope[part, columns] = bend.astype(jnp.bfloat16)

            tiles(activated.shape[1], expand)

        @pl.when(in_stage(piece, 1))
        def _():
            chunk = gathered[chunk_rows, :]

            def shrink(columns):
                grad = dot_plain(chunk, shrink_weight[:, columns])
                low = (grad * slope[part, columns].astype(jnp.float32)).astype(jnp.bfloat16)
                slope[part, columns] = low
                added = jnp.sum(low.astype(jnp.float32), axis=0, keepdims=True)
                before = jnp.where(piece == PIECES, 0.0, hidden_sums[0:1, columns])
                hidden_sums[0:1, columns] = before + added

            tiles(slope.shape[1], shrink)

        @pl.when(in_stage(piece, 2))
        def _():
            place = piece - 2 * PIECES
            result = dot_plain(gathered[chunk_rows, :], output_weight[...]).astype(jnp.bfloat16)
            here = ctx == 0
            left, right = result[:, :half], result[:, half:]
            stage[part, :] = jnp.where(here, right, left)
            swap_out.start(place)
            grad_heads[piece_rows(place, ctx * rows), :] = jnp.where(here, left, right)
            branch_copy(place).start()

    def form(piece):
        part = piece_rows(lax.rem(piece, PIECES))
        parity = lax.rem(piece, 2)

        def products(x, weight):
            def product(columns):
                terms[parity, :, columns] = dot_cols(x, weight[columns, :])

            tiles(width, product)

        @pl.when(in_stage(piece, 0))
        def _():
            swap_in.wait_arrival(piece)
            products(attended[part, :], output_weight)

        @pl.when(in_stage(piece, 1))
        def _():
            products(activated[part, :], shrink_weight)

        @pl.when(in_stage(piece, 2))
        def _():
            products(slope[part, :], expand_weight)

        line.sum_start(piece, term_of(piece))

    def term_of(piece):
        parity = lax.rem(piece, 2)
        return lambda owner: terms[parity, pl.ds(pl.multiple_of(owner * own, own), own), :]

    def own_step(piece):
        place = lax.rem(piece, PIECES)
        total[...] = term_of(piece)(me)
        line.sum_end(piece, total)

        @pl.when(in_stage(piece, 0))
        def _():
            view(piece, me)[...] = first_norm_step(
                place, total, (own_tokens, marks), (inner, normed_one, inverse_one)
            )

        @pl.when(in_stage(piece, 1))
        def _():
            view(piece, me)[...] = second_norm_step(
                place, total, (inner, out_grad, marks), (mixed, inner, second_sums)
            )

        @pl.when(in_stage(piece, 2))
        def _():
            view(piece, me)[...] = first_back_step(
                place, total, (inner, normed_one, inverse_one, marks), (inner, first_sums)
            )

        line.spread_start(piece)

    def gradient(number, left_start, right, place):
        columns = pl.ds(pl.multiple_of(number * shard, shard), shard)
        def product(part):
            left = gathered[left_start : left_start + rows, columns]
            place[:, part] = dot_rows(left, right[:, part]).astype(place.dtype)

        tiles(place.shape[1], product)

    def expand_copy(number):
        part = pl.ds(pl.multiple_of(number * shard, shard), shard)
        return pltpu.make_async_copy(expand_stage, expand_out.at[part], product_done)

    def expand_step(number):
        pl.when(number > 0)(lambda: expand_copy(number - 1).wait())
        gradient(number, 0, slope, expand_stage)
        expand_copy(number).start()

    plane_sum = PlaneSum(shrink_weight, activated, first_slots, last_slots, plane_sent, plane_got)
    twin = {"fsdp": plane_sum.twin}

    def shrink_step(number):
        pl.when(number == 0)(shrink_gather.wait_sent)
        fsdp = jnp.where(number == 0, plane_sum.twin, plane_sum.fsdp)
        for over_x in (1, 0):
            for over_y in (1, 0):
                owner = plane_sum.number(fsdp, over_x, over_y)
                gradient(owner, rows, activated, shrink_weight.at[plane_sum.rows(owner)])

        @pl.when(number == 1)
        def _():
            pl.semaphore_signal(ready, inc=1, device_id=twin, device_id_type=MESH)

    def shrink_send(_):
        pl.semaphore_wait(ready, 1)
        plane_sum.start()

    def shrink_total(side):
        return pltpu.make_async_copy(
            terms.at[side], shrink_out.at[pl.ds(side * height, height)], put_done.at[side]
        )

    @pl.loop(0, pieces + 5)
    def _(step):
        def late(number, action, most=pieces):
            @pl.when((step >= number) & (step < most + number))
            def _():
                action(step - number)

        pl.when(step == 5)(expand_gather.last)
        pl.when(step == 2 * PIECES + 7)(plane_sum.second)
        pl.when(step == 2 * PIECES + 9)(plane_sum.third)
        pl.when(step == PIECES)(shrink_gather.last)
        late(0, form)
        late(1, lambda piece: line.sum_onward(piece, term_of(piece), [1]))
        late(5, use)
        late(3, lambda piece: line.spread_onward(piece, 2))
        late(4, lambda piece: [line.spread_onward(piece, i) for i in range(3, count)])
        late(2, lambda piece: line.spread_onward(piece, 1))
        late(2 * PIECES + 4, shrink_step, 2)
        late(2 * PIECES + 5, expand_step, PIECES)
        late(2 * PIECES + 6, shrink_send, 1)
        late(0, lambda piece: line.sum_onward(piece, term_of(piece), range(count - 2, 1, -1)))
        late(1, own_step)

        @pl.when(step == 3)
        def _():
            expand_gather.second()
            shrink_gather.first()

        pl.when(step == 4)(expand_gather.third)
        pl.when(step == 6)(shrink_gather.second)
        pl.when(step == 7)(shrink_gather.third)

    expand_copy(PIECES - 1).wait()

    def put_total(side, part, values):
        columns = pl.ds(side * (hidden // 2), hidden // 2)
        start = pl.multiple_of(lax.rem(part.start, height), values.shape[0])
        terms[part.start // height, pl.ds(start, values.shape[0]), columns] = values

    plane_sum.finish(put_total)
    for side in range(2):
        shrink_total(side).start()
    for side in range(2):
        shrink_total(side).wait()

    @pl.loop(0, PIECES)
    def _(piece):
        branch_copy(piece).wait()
        swap_in.wait_sent(piece)
        swap_out.wait_arrival(piece)
        swap_out.wait_sent(piece)

    expand_gather.wait_sent()
    line.spread_finish(pieces)


def gelu_with_slope(values):
    scale = math.sqrt(2.0 / math.pi)
    square = values * values
    bend = 0.5 * jnp.tanh(scale * values * (1.0 + 0.044715 * square)) + 0.5
    inner = (2 * scale) * (1.0 + 3 * 0.044715 * square)
    result = values * bend
    return result, bend + result * (1.0 - bend) * inner


def middle(
    attended_heads, output_weight, expand_shard, shrink_shard, own_tokens, out_grad, marks,
    unit_biases, collective_id,
):
    count = lax.axis_size("tp")
    rows = attended_heads.shape[0] // 2
    half = attended_heads.shape[1]
    own_rows, width = own_tokens.shape
    hidden = expand_shard.shape[1]
    height = rows // PIECES
    own = height // count
    shard = width // PIECES
    low = jnp.bfloat16
    vmem, anywhere = pl.BlockSpec(memory_space=pltpu.VMEM), pl.BlockSpec(memory_space=pl.ANY)

    def shape(extent, kind=jnp.float32):
        return jax.ShapeDtypeStruct(extent, kind)

    return pl.pallas_call(
        functools.partial(middle_kernel, count),
        out_shape=[
            shape((rows, 2 * half), low),
            shape(out_grad.shape, low),
            shape((own_rows, width)),
            shape((rows, width), low),
            shape((2 * rows, half), low),
            shape((8, width)),
            shape((8, width)),
            shape((8, hidden)),
            shape((shard, hidden)),
            shape((width, hidden), low),
        ],
        in_specs=[anywhere, vmem, anywhere, anywhere, vmem, vmem, vmem, vmem],
        out_specs=[vmem, vmem, vmem, anywhere, vmem, vmem, vmem, vmem, anywhere, anywhere],
        scratch_shapes=[
            pltpu.VMEM((width, hidden), low),
            pltpu.VMEM((width, hidden), low),
            pltpu.VMEM((3 * rows, width), low),
            pltpu.VMEM((rows, hidden), low),
            pltpu.VMEM((rows, hidden), low),
            pltpu.VMEM((own_rows, width), jnp.float32),
            pltpu.VMEM((own_rows, 128), jnp.float32),
            pltpu.VMEM((2, height, width), jnp.float32),
            pltpu.VMEM((own, width), jnp.float32),
            pltpu.VMEM((PIECES, count + 1, own, width), low),
            pltpu.VMEM((rows, half), low),
            pltpu.VMEM((shard, hidden), low),
            *PlaneSum.slots(shard, hidden),
            *line_semaphores(count, PIECES)[0],
            *line_semaphores(count, 3 * PIECES)[1],
            *[pltpu.SemaphoreType.DMA((9,))] * 4,
            *[pltpu.SemaphoreType.DMA((PIECES,))] * 4,
            pltpu.SemaphoreType.DMA((3,)),
            pltpu.SemaphoreType.DMA((PIECES,)),
            pltpu.SemaphoreType.DMA,
            pltpu.SemaphoreType.REGULAR,
        ],
        compiler_params=pltpu.CompilerParams(
            collective_id=collective_id, has_side_effects=True, vmem_limit_bytes=62 << 20
        ),
        cost_estimate=pl.CostEstimate(
            flops=300_000_000_000, bytes_accessed=192 * rows * width, transcendentals=0
        ),
        name="middle",
    )(
        attended_heads, output_weight, expand_shard, shrink_shard, own_tokens, out_grad, marks,
        unit_biases,
    )


def peers_in_plane(sizes):
    fsdp, ctx = lax.axis_index("fsdp"), lax.axis_index("ctx")
    return [
        {"fsdp": lax.rem(fsdp + i, sizes[0]), "ctx": lax.rem(ctx + j, sizes[1])}
        for i in range(sizes[0])
        for j in range(sizes[1])
        if i or j
    ]


def input_kernel(
    sizes, x_ref, weight, inner_ref, first_ref, second_ref, hidden_ref, out_ref, vectors_ref,
    rows_ref, term_ref, total, slots, own_vectors, tp_slots, plane_slots,
    sum_sent, sum_got, tp_sent, tp_got, plane_sent, plane_got, hooks=None,
):
    count = sizes[2]
    me = lax.axis_index("tp")
    height = x_ref.shape[0] // PIECES
    own = height // count
    width = out_ref.shape[1]
    line = Line(me, count, slots, sum_sent, sum_got, None, None, None)
    tp_peers, plane_peers = peers_along_tp(me, count), peers_in_plane(sizes)
    greet_peers(tp_peers + plane_peers)

    def own_part(index):
        return rows_ref.at[:, pl.ds(pl.multiple_of(index * width, width), width)]

    over_tp = Exchange(
        tp_peers, tp_sent, tp_got,
        lambda i: own_part(lax.rem(me + i, count)), lambda i: tp_slots.at[i],
    )
    over_plane = Exchange(
        plane_peers, plane_sent, plane_got, lambda _: own_vectors, lambda i: plane_slots.at[i]
    )
    opening, before, after, closing, pack_at = hooks or (*(lambda *_: None,) * 4, 0)
    order = ((0, 0), (1, 0), (0, 2), (0, 1), (1, 2), (1, 1))
    rows_ref[...] = jnp.zeros_like(rows_ref)
    for i, (which, row) in enumerate(order):
        rows_ref[i : i + 1, :] = (first_ref, second_ref)[which][row : row + 1, :]
    opening()
    over_tp.start()

    def terms(piece):
        def term(owner):
            features = pl.ds(pl.multiple_of(owner * width, width), width)
            term_ref[...] = dot_cols(
                x_ref[pl.ds(pl.multiple_of(piece * height, height), height), :],
                weight[features, :],
            )
            inner = inner_ref[pl.ds(pl.multiple_of(piece * own, own), own), features]
            term_ref[pl.ds(pl.multiple_of(me * own, own), own), :] += inner
            return term_ref[...]

        return term

    def pack():
        over_tp.wait_arrivals()
        own_vectors[0:8, :] = own_part(me)[...]
        for i in range(count - 1):
            own_vectors[0:8, :] += tp_slots[i]
        own_vectors[8:, :] = jnp.zeros_like(own_vectors[8:, :])
        hidden_rows = hidden_ref.shape[1] // width
        for i in range(hidden_rows):
            own_vectors[8 + i : 9 + i, :] = hidden_ref[0:1, i * width : (i + 1) * width]
        for i in range(x_ref.shape[1] // width):
            part = x_ref[:, i * width : (i + 1) * width].astype(jnp.float32)
            place = 8 + hidden_rows + i
            own_vectors[place : place + 1, :] = jnp.sum(part, axis=0, keepdims=True)
        over_plane.start()

    def own_sum(piece):
        total[...] = terms(piece)(me)
        line.sum_end(piece, total)
        rows = pl.ds(pl.multiple_of(piece * height, height), height)
        out_ref[rows, :] = total[...].astype(out_ref.dtype)

    @pl.loop(0, PIECES)
    def _(piece):
        before(piece)
        line.sum_start(piece, terms(piece))
        line.sum_onward(piece, terms(piece), range(count - 2, 0, -1))
        after(piece)
        pl.when(piece == pack_at)(pack)
        pl.when(piece >= OWN_LATE)(lambda: own_sum(piece - OWN_LATE))

    closing()
    pl.loop(PIECES - OWN_LATE, PIECES)(own_sum)
    over_plane.wait_arrivals()
    vectors_ref[...] = own_vectors[...]
    for i in range(len(plane_peers)):
        vectors_ref[...] += plane_slots[i]
    over_tp.wait_sent()
    over_plane.wait_sent()
    line.sum_finish(PIECES)


def input_sum(x, weight, inner, first_sums, second_sums, hidden_sums, collective_id):
    sizes = tuple(lax.axis_size(axis) for axis in ("fsdp", "ctx", "tp"))
    count = sizes[2]
    others = sizes[0] * sizes[1] - 1
    rows = x.shape[0]
    width = weight.shape[0] // count
    height = rows // PIECES
    packed = 8 + -(-(hidden_sums.shape[1] + x.shape[1]) // (8 * width)) * 8
    return pl.pallas_call(
        functools.partial(input_kernel, sizes),
        out_shape=[
            jax.ShapeDtypeStruct((rows, width), jnp.bfloat16),
            jax.ShapeDtypeStruct((packed, width), jnp.float32),
        ],
        in_specs=[pl.BlockSpec(memory_space=pltpu.VMEM)] * 6,
        out_specs=[pl.BlockSpec(memory_space=pltpu.VMEM)] * 2,
        scratch_shapes=[
            pltpu.VMEM(first_sums.shape, jnp.float32),
            pltpu.VMEM((height, width), jnp.float32),
            pltpu.VMEM((height, width), jnp.float32),
            pltpu.VMEM((PIECES, count + 1, height, width), jnp.bfloat16),
            pltpu.VMEM((packed, width), jnp.float32),
            pltpu.VMEM((count - 1, 8, width), jnp.float32),
            pltpu.VMEM((others, packed, width), jnp.float32),
            *line_semaphores(count, PIECES)[0],
            pltpu.SemaphoreType.DMA((count - 1,)),
            pltpu.SemaphoreType.DMA((count - 1,)),
            pltpu.SemaphoreType.DMA((others,)),
            pltpu.SemaphoreType.DMA((others,)),
        ],
        compiler_params=pltpu.CompilerParams(
            collective_id=collective_id, has_side_effects=True, vmem_limit_bytes=40 << 20
        ),
        cost_estimate=pl.CostEstimate(
            flops=60_000_000_000, bytes_accessed=64 * rows * width, transcendentals=0
        ),
        name="input_sum",
    )(x, weight, inner, first_sums, second_sums, hidden_sums)


def leave_kernel(
    sizes, grads_ref, tokens_in, weight_in, inner_in, first_ref, second_ref, hidden_ref, branch_in,
    attended_in,
    out_ref, vectors_ref, query_out, key_out, value_out, output_out,
    tokens_ref, weight, inner_ref, branch_ref, attended_ref, copied, own_copied,
    x_ref, rows_ref, term_ref, total, slots, own_vectors, tp_slots, plane_slots,
    sum_sent, sum_got, tp_sent, tp_got, plane_sent, plane_got, swap_sent, swap_got, *sum_scratch,
):
    count = sizes[2]
    me, ctx = lax.axis_index("tp"), lax.axis_index("ctx")
    rows = x_ref.shape[0]
    height = rows // PIECES
    part = grads_ref.shape[1]
    plane_sum, output_sum = PlaneSum(*sum_scratch[:6]), PlaneSum(*sum_scratch[6:])
    shard = plane_sum.height

    def piece_rows(piece, start=0):
        return pl.ds(pl.multiple_of(start + piece * height, height), height)

    copies = [
        pltpu.make_async_copy(source, place, copied.at[i])
        for i, (source, place) in enumerate(
            (
                (branch_in, branch_ref),
                (attended_in, attended_ref),
                (weight_in, weight),
                (inner_in, inner_ref),
                (tokens_in, tokens_ref),
            )
        )
    ]
    for copy in copies:
        copy.start()
    own_columns = pl.ds(pl.multiple_of(ctx * part, part), part)
    own_block = pl.ds(pl.multiple_of(ctx * rows, rows), rows)
    own_copy = pltpu.make_async_copy(
        grads_ref.at[own_block], x_ref.at[:, own_columns], own_copied
    )
    own_copy.start()
    swap = Swap(
        swap_sent, swap_got,
        lambda piece: grads_ref.at[piece_rows(piece, (1 - ctx) * rows)],
        lambda piece: x_ref.at[piece_rows(piece), own_columns],
    )

    def products(sums, fsdp, left, right):
        for over_x in (1, 0):
            for over_y in (1, 0):
                number = sums.number(fsdp, over_x, over_y)
                columns = pl.ds(pl.multiple_of(number * shard, shard), shard)
                product = dot_rows(left[:, columns], right[...])
                sums.parts[sums.rows(number), :] = product.astype(jnp.bfloat16)

    def opening():
        @pl.loop(0, PIECES)
        def _(piece):
            swap.start(piece)

        for copy in copies[:2]:
            copy.wait()
        products(output_sum, output_sum.twin, branch_ref, attended_ref)
        output_sum.start()
        products(output_sum, output_sum.fsdp, branch_ref, attended_ref)
        output_sum.second()
        for copy in copies[2:]:
            copy.wait()
        own_copy.wait()

    last = PIECES - 1
    begin = jnp.where((me == 0) | (me == count - 1), last, 2)

    def before(piece):
        @pl.when(piece <= begin)
        def _():
            swap.wait_arrival(piece)

    def after(piece):
        @pl.when(piece == begin)
        def _():
            @pl.loop(begin + 1, PIECES)
            def _(other):
                swap.wait_arrival(other)

            products(plane_sum, plane_sum.twin, tokens_ref, x_ref)
            plane_sum.start()

        @pl.when(piece == jnp.minimum(begin + 1, last))
        def _():
            products(plane_sum, plane_sum.fsdp, tokens_ref, x_ref)

        pl.when(piece == jnp.minimum(begin + 2, last))(plane_sum.second)
        pl.when(piece == jnp.minimum(begin + 3, last))(output_sum.third)

    def closing():
        plane_sum.third()

    input_kernel(
        sizes, x_ref, weight, inner_ref, first_ref, second_ref, hidden_ref, out_ref, vectors_ref,
        rows_ref, term_ref, total, slots, own_vectors, tp_slots, plane_slots,
        sum_sent, sum_got, tp_sent, tp_got, plane_sent, plane_got,
        hooks=(opening, before, after, closing, jnp.minimum(begin + 3, last)),
    )
    third = part // 3

    def put_part(side, rows, values):
        for i, ref in enumerate((query_out, key_out, value_out)):
            ref[rows, side * third : (side + 1) * third] = values[:, i * third : (i + 1) * third]

    def put_output(side, rows, values):
        output_out[rows, side * output_sum.half : (side + 1) * output_sum.half] = values

    plane_sum.finish(put_part)
    output_sum.finish(put_output)

    @pl.loop(0, PIECES)
    def _(piece):
        swap.wait_sent(piece)


def leave(
    grads, tokens, weight, inner, first_sums, second_sums, hidden_sums, branch, attended,
    collective_id,
):
    sizes = tuple(lax.axis_size(axis) for axis in ("fsdp", "ctx", "tp"))
    count = sizes[2]
    others = sizes[0] * sizes[1] - 1
    rows, features = tokens.shape
    part = grads.shape[1]
    width = features // count
    height = rows // PIECES
    shard = features // (others + 1)
    packed = 8 + -(-(hidden_sums.shape[1] + 2 * part) // (8 * width)) * 8
    return pl.pallas_call(
        functools.partial(leave_kernel, sizes),
        out_shape=[
            jax.ShapeDtypeStruct((rows, width), jnp.bfloat16),
            jax.ShapeDtypeStruct((packed, width), jnp.float32),
            *[jax.ShapeDtypeStruct((shard, 2 * part // 3), jnp.float32)] * 4,
        ],
        in_specs=[
            *[pl.BlockSpec(memory_space=pl.ANY)] * 4,
            *[pl.BlockSpec(memory_space=pltpu.VMEM)] * 3,
            *[pl.BlockSpec(memory_space=pl.ANY)] * 2,
        ],
        out_specs=[pl.BlockSpec(memory_space=pltpu.VMEM)] * 6,
        scratch_shapes=[
            *[pltpu.VMEM(x.shape, x.dtype) for x in (tokens, weight, inner, branch, attended)],
            pltpu.SemaphoreType.DMA((5,)),
            pltpu.SemaphoreType.DMA,
            pltpu.VMEM((rows, 2 * part), jnp.bfloat16),
            pltpu.VMEM(first_sums.shape, jnp.float32),
            pltpu.VMEM((height, width), jnp.float32),
            pltpu.VMEM((height, width), jnp.float32),
            pltpu.VMEM((PIECES, count + 1, height, width), jnp.bfloat16),
            pltpu.VMEM((packed, width), jnp.float32),
            pltpu.VMEM((count - 1, 8, width), jnp.float32),
            pltpu.VMEM((others, packed, width), jnp.float32),
            *line_semaphores(count, PIECES)[0],
            pltpu.SemaphoreType.DMA((count - 1,)),
            pltpu.SemaphoreType.DMA((count - 1,)),
            pltpu.SemaphoreType.DMA((others,)),
            pltpu.SemaphoreType.DMA((others,)),
            pltpu.SemaphoreType.DMA((PIECES,)),
            pltpu.SemaphoreType.DMA((PIECES,)),
            *PlaneSum.scratch(others + 1, shard, 2 * part),
            *PlaneSum.scratch(others + 1, shard, attended.shape[1]),
        ],
        compiler_params=pltpu.CompilerParams(
            collective_id=collective_id, has_side_effects=True, vmem_limit_bytes=60 << 20
        ),
        cost_estimate=pl.CostEstimate(
            flops=60_000_000_000, bytes_accessed=64 * rows * width, transcendentals=0
        ),
        name="leave",
    )(grads, tokens, weight, inner, first_sums, second_sums, hidden_sums, branch, attended)


def to_own_rows(wide):
    count = lax.axis_size("tp")
    parts = wide.reshape(PIECES, count, -1, wide.shape[1])
    return lax.dynamic_index_in_dim(parts, lax.axis_index("tp"), 1, keepdims=False).reshape(
        -1, wide.shape[1]
    )


def by_owner(block):
    count = lax.axis_size("tp")
    width = block.shape[1]
    parts = block.reshape(PIECES, count, -1, width).transpose(1, 0, 2, 3)
    return parts.reshape(count, -1, width)


def swap_over_tp(parts):
    return lax.all_to_all(parts, "tp", split_axis=0, concat_axis=0, tiled=True)


def by_rows(parts):
    count, _, width = parts.shape
    return parts.reshape(count, PIECES, -1, width).transpose(1, 0, 2, 3).reshape(-1, width)


def body(
    tokens,
    segments,
    query_weight,
    key_weight,
    value_weight,
    output_weight,
    expand_weight,
    shrink_weight,
    query_bias,
    value_bias,
    hidden_bias,
    norm_gains,
    row_biases,
    out_grad,
):
    rows = tokens.shape[0]
    head_cols = query_weight.shape[1]
    heads = head_cols // HD
    plane = ("fsdp", "ctx")
    plane_sizes = tuple(lax.axis_size(axis) for axis in plane)
    by_heads = plane_sizes == (4, 2) and heads % 2 == 0

    def weight_rows(weight):
        return lax.all_gather(weight, plane, axis=0, tiled=True)

    block_index = lax.axis_index("fsdp") * plane_sizes[1] + lax.axis_index("ctx")
    unit_biases = jnp.concatenate([query_bias, value_bias, hidden_bias])[None]
    if by_heads:
        wide_tokens, own_tokens, marks, wide_qkv, full_output, qkv_heads, upstream = enter(
            tokens, norm_gains, row_biases, query_weight, key_weight, value_weight, output_weight,
            unit_biases, out_grad, 0,
        )
        upstream = upstream.reshape(upstream.shape[0], -1, upstream.shape[3])
        queries = keys = values = qkv_heads
        own_heads = heads // 2
        bounds = (segments.reshape(-1, plane_sizes[1] * rows),)
    else:
        wide_qkv = weight_rows(jnp.concatenate([query_weight, key_weight, value_weight], axis=1))
        wide_tokens, marks = gather_features(tokens, norm_gains, row_biases, 0)
        upstream = by_owner(out_grad)
        own_tokens = to_own_rows(wide_tokens)
        qkv_bias = jnp.concatenate([query_bias, jnp.zeros_like(query_bias), value_bias])
        qkv = dot_plain(wide_tokens, wide_qkv) + qkv_bias.astype(jnp.float32)
        queries, keys, values = jnp.split(qkv.astype(jnp.bfloat16), 3, axis=1)
        own_heads = heads
        keys, values = padded(keys, WIN), padded(values, WIN)
        ids = jnp.concatenate(
            [
                jnp.full((WIN,), -1, jnp.int32),
                segments,
                jnp.full((WIN,), jnp.iinfo(jnp.int32).max, jnp.int32),
            ]
        )
        full_output, full_expand = weight_rows(output_weight), weight_rows(expand_weight)
        key_ids = lax.dynamic_slice_in_dim(ids, block_index * rows, rows + 2 * WIN, 0)
        bounds = key_bounds(key_ids[WIN : WIN + rows], key_ids, WIN)
    places = (0, own_heads, 2 * own_heads) if by_heads else (0, 0, 0)
    marks, upstream = lax.optimization_barrier((marks, upstream))
    upstream = swap_over_tp(upstream)
    attended_heads, lse = attend(queries, keys, values, own_heads, bounds, places)
    attended_heads, upstream = lax.optimization_barrier((attended_heads, upstream))

    own_rows, features = own_tokens.shape
    hidden_cols = expand_weight.shape[1]

    def shape(extent, kind=jnp.float32):
        return jax.ShapeDtypeStruct(extent, kind)

    own_shape = shape((own_rows, features))
    def owner_sum(grad):
        return lax.psum_scatter(
            grad, plane, scatter_dimension=0, tiled=True
        )

    if by_heads:
        (
            attended, mixed_own, grad_inner, branch_low, attended_grad,
            first_sums, second_sums, hidden_sums, shrink_grad, expand_part,
        ) = middle(
            attended_heads, full_output, expand_weight, shrink_weight, own_tokens, upstream,
            marks, unit_biases, 1,
        )
        expand_grad = owner_sum(expand_part)
        mixed = by_rows(swap_over_tp(mixed_own))
        (grads,) = attend_back(
            queries, keys, values, attended_heads, attended_grad, lse, bounds, places, True
        )
        grads, mixed = lax.optimization_barrier((grads, mixed))
    else:
        full_shrink = weight_rows(shrink_weight)
        norm_low, first_norm, normed_one, inverse_one, hidden, activated = relay(
            attended_heads, full_output, full_expand,
            [own_tokens, marks], first_norm_step,
            [own_shape, own_shape, shape((own_rows, 128))],
            [hidden_bias.astype(jnp.float32)[None]], expand_step,
            [shape((rows, hidden_cols)), shape((rows, hidden_cols), jnp.bfloat16)],
            1, "first_norm",
        )
        ffn_low, mixed_own, grad_second, second_sums, hidden_low, hidden_sums = relay(
            activated, full_shrink, None,
            [first_norm, upstream, marks], second_norm_step,
            [shape(upstream.shape, jnp.bfloat16), own_shape, shape((8, features))],
            [hidden], shrink_step,
            [shape((rows, hidden_cols), jnp.bfloat16), shape((8, hidden_cols))],
            2, "second_norm",
        )
        shrink_grad = owner_sum(dot_rows(ffn_low, activated).astype(jnp.bfloat16))
        branch_low, grad_inner, first_sums, attended_grad = relay(
            hidden_low, full_expand, full_output,
            [grad_second, normed_one, inverse_one, marks], first_back_step,
            [own_shape, shape((8, features))],
            [], attended_step,
            [shape((rows, head_cols), jnp.bfloat16)],
            3, "first_back",
        )
        expand_grad = owner_sum(dot_rows(norm_low, hidden_low).astype(jnp.bfloat16))
        output_grad = owner_sum(dot_rows(branch_low, attended_heads).astype(jnp.bfloat16))
        mixed = by_rows(swap_over_tp(mixed_own))
        query_low, key_ext, value_ext = attend_back(
            queries, keys, values, attended_heads, attended_grad, lse, bounds
        )

        def fold(ext):
            edges = jnp.concatenate([ext[:WIN], ext[WIN + rows :]], axis=0)
            around = padded(edges, WIN)
            own = ext[WIN : WIN + rows]
            own = own.at[:WIN].add(around[:WIN]).at[rows - WIN :].add(around[3 * WIN :])
            return own.astype(jnp.bfloat16)

        qkv_low = jnp.concatenate([query_low, fold(key_ext), fold(value_ext)], axis=1)
    sides = 2 if by_heads else 1

    def by_kind(columns):
        parts = columns.reshape(-1, sides, 3, head_cols // sides)
        return [parts[:, :, i].reshape(-1, head_cols) for i in range(3)]

    if by_heads:
        input_grad, vectors, query_grad, key_grad, value_grad, output_grad = leave(
            grads, wide_tokens, wide_qkv, grad_inner, first_sums, second_sums, hidden_sums,
            branch_low, attended, 4,
        )
        input_grad, expand_grad = lax.optimization_barrier((input_grad, expand_grad))
    else:
        input_grad, vectors = input_sum(
            qkv_low, wide_qkv, grad_inner, first_sums, second_sums, hidden_sums, 4
        )
        qkv_grad = owner_sum(dot_rows(wide_tokens, qkv_low).astype(jnp.bfloat16))
        query_grad, key_grad, value_grad = by_kind(qkv_grad.astype(jnp.float32))
    hidden_rows = hidden_cols // head_cols
    query_sum, _, value_sum = by_kind(
        vectors[8 + hidden_rows : 8 + hidden_rows + 3].reshape(1, -1)
    )
    return (
        mixed,
        input_grad,
        query_grad,
        key_grad,
        value_grad,
        output_grad.astype(jnp.float32),
        expand_grad.astype(jnp.float32),
        shrink_grad.astype(jnp.float32),
        query_sum[0],
        value_sum[0],
        vectors[8 : 8 + hidden_rows].reshape(-1),
        vectors[:2],
        vectors[2:6],
    )


def solution(mesh):
    rows, whole, cols = P(("fsdp", "ctx"), "tp"), P(), P("tp")
    wide = P(None, "tp")
    return jax.shard_map(
        body,
        mesh=mesh,
        in_specs=(rows, whole) + (rows,) * 6 + (cols,) * 3 + (wide,) * 2 + (rows,),
        out_specs=(rows,) * 8 + (cols,) * 3 + (wide,) * 2,
        check_vma=False,
    )
```

```python
import functools
import math

import jax
import jax.numpy as jnp
from jax import lax
from jax.experimental import pallas as pl
from jax.experimental.pallas import tpu as pltpu
from jax.sharding import PartitionSpec as P

HD = 128
WIN = 1024
QB = 512
KB = 512
GROUP = 2

epsilon = 1e-06
hidden_floor = -1e30
score_scale = 1.0 / math.sqrt(HD)
log2_e = 1.0 / math.log(2.0)


def dot_plain(left, right):
    return jnp.dot(left, right, preferred_element_type=jnp.float32)


def dot_rows(left, right):
    return lax.dot_general(
        left, right, (((0,), (0,)), ((), ())), preferred_element_type=jnp.float32
    )


def dot_cols(left, right):
    return lax.dot_general(
        left, right, (((1,), (1,)), ((), ())), preferred_element_type=jnp.float32
    )


def block_bounds(block, rows, bounds, marks):
    if len(bounds) == 4:
        first, last, low, high = bounds
        return first[block], last[block], last[block], last[block], low[...], high[...]
    (ids,) = bounds
    run = ids.shape[1]

    @pl.when((pl.program_id(0) == 0) & (block == 0))
    def _():
        own = lax.axis_index("fsdp")
        own_ids = ids[pl.ds(own, 1), :]
        for i in range(2):
            marks[i] = jnp.sum((own_ids <= 3 * own + i).astype(jnp.int32))

    second, third = marks[0], marks[1]

    def bounds_at(places):
        start = jnp.where(places < second, 0, jnp.where(places < third, second, third))
        stop = jnp.where(places < second, second, jnp.where(places < third, third, run))
        return jnp.maximum(start, places - WIN), jnp.minimum(stop - 1, places + WIN)

    begin = block * rows
    low, high = bounds_at(begin + lax.broadcasted_iota(jnp.int32, (1, rows), 1))
    least_low, least_high = bounds_at(begin)
    most_low, most_high = bounds_at(begin + rows - 1)
    first, last = least_low // KB, most_high // KB + 1
    whole_first = jnp.minimum((most_low + KB - 1) // KB, last)
    whole_last = jnp.maximum((least_high + 1) // KB, whole_first)
    return first, whole_first, whole_last, last, low, high


def over_key_blocks(step, marks, start):
    first, whole_first, whole_last, last = marks
    carry = lax.fori_loop(first, whole_first, functools.partial(step, True), start)
    carry = lax.fori_loop(whole_first, whole_last, functools.partial(step, False), carry)
    return lax.fori_loop(whole_last, last, functools.partial(step, True), carry)


def bound_operands(bounds):
    if len(bounds) == 4:
        mark_spec = pl.BlockSpec((1, QB), lambda h, i, *_: (0, i))
        return list(bounds[:2]), list(bounds[2:]), [mark_spec, mark_spec]
    shape = bounds[0].shape
    return [], list(bounds), [pl.BlockSpec(shape, lambda h, i, *_: (0, 0))]


def head_columns(head):
    return slice(head * HD, (head + 1) * HD)


def attend_kernel(scalars, *refs):
    bounds = refs[:scalars]
    q_ref, k_ref, v_ref, *arrays, out_ref, lse_ref, vt, marks = refs[scalars:]
    block = pl.program_id(1)
    rows = q_ref.shape[0]
    heads = range(GROUP)

    @pl.when(block == 0)
    def _():
        vt[...] = v_ref[...].T

    queries = [q_ref[:, head_columns(h)] for h in heads]
    *span, low, high = block_bounds(block, rows, (*bounds, *arrays), marks)
    places = lax.broadcasted_iota(jnp.int32, (KB, rows), 0)

    def step(masked, number, carry):
        start = pl.multiple_of(number * KB, KB)
        window = pl.ds(start, KB)
        scores = [dot_cols(k_ref[window, head_columns(h)], queries[h]) for h in heads]
        scores = [score * (score_scale * log2_e) for score in scores]
        if masked:
            keep = (places >= low - start) & (places <= high - start)
            scores = [jnp.where(keep, score, hidden_floor) for score in scores]
        tops = [
            jnp.maximum(carry[h][0], jnp.max(scores[h], axis=0, keepdims=True)) for h in heads
        ]
        powers = [jnp.exp2(scores[h] - tops[h]) for h in heads]
        parts = [
            dot_plain(vt[head_columns(h), window], powers[h].astype(jnp.bfloat16)) for h in heads
        ]
        result = []
        for h in heads:
            top, total, mixed = carry[h]
            shrink = jnp.exp2(top - tops[h])
            total = total * shrink + jnp.sum(powers[h], axis=0, keepdims=True)
            result.append((tops[h], total, mixed * shrink + parts[h]))
        return tuple(result)

    start = (
        jnp.full((1, rows), hidden_floor, jnp.float32),
        jnp.zeros((1, rows), jnp.float32),
        jnp.zeros((HD, rows), jnp.float32),
    )
    for h, (top, total, mixed) in enumerate(over_key_blocks(step, span, (start,) * GROUP)):
        out_ref[:, head_columns(h)] = (mixed / total).T.astype(out_ref.dtype)
        lse_ref[h] = top + jnp.log2(total)


def attend(queries, keys, values, heads, bounds, places=(0, 0, 0)):
    rows, span = queries.shape[0], keys.shape[0]
    width = heads * HD
    q_at, k_at, v_at = (place // GROUP for place in places)
    some = GROUP * HD
    scalars, arrays, specs = bound_operands(bounds)
    return pl.pallas_call(
        functools.partial(attend_kernel, len(scalars)),
        out_shape=(
            jax.ShapeDtypeStruct((rows, width), jnp.bfloat16),
            jax.ShapeDtypeStruct((heads, 1, rows), jnp.float32),
        ),
        grid_spec=pltpu.PrefetchScalarGridSpec(
            num_scalar_prefetch=len(scalars),
            grid=(heads // GROUP, rows // QB),
            in_specs=[
                pl.BlockSpec((QB, some), lambda h, i, *_: (i, h + q_at)),
                pl.BlockSpec((span, some), lambda h, i, *_: (0, h + k_at)),
                pl.BlockSpec((span, some), lambda h, i, *_: (0, h + v_at)),
                *specs,
            ],
            out_specs=[
                pl.BlockSpec((QB, some), lambda h, i, *_: (i, h)),
                pl.BlockSpec((GROUP, 1, QB), lambda h, i, *_: (h, 0, i)),
            ],
            scratch_shapes=[pltpu.VMEM((some, span), jnp.bfloat16), pltpu.SMEM((2,), jnp.int32)],
        ),
        compiler_params=pltpu.CompilerParams(vmem_limit_bytes=60 << 20),
        cost_estimate=pl.CostEstimate(
            flops=3 * rows * span * width,
            bytes_accessed=2 * (2 * rows + 2 * span) * width,
            transcendentals=rows * span * heads,
        ),
        name="attend",
    )(*scalars, queries, keys, values, *arrays)


def attend_back_kernel(scalars, arrays, *refs):
    bounds = refs[:scalars]
    q_ref, k_ref, v_ref, o_ref, g_ref, lse_ref, *refs = refs[scalars:]
    bounds = (*bounds, *refs[:arrays])
    *results, kt, dk_sum, dv_sum, marks = refs[arrays:]
    group, block = pl.program_id(0), pl.program_id(1)
    rows = q_ref.shape[0]
    heads = range(GROUP)

    @pl.when(block == 0)
    def _():
        kt[...] = k_ref[...].T
        dk_sum[...] = jnp.zeros_like(dk_sum)
        dv_sum[...] = jnp.zeros_like(dv_sum)

    queries = [q_ref[:, head_columns(h)] for h in heads]
    upstream = [g_ref[:, head_columns(h)] for h in heads]
    *span, low, high = block_bounds(block, rows, bounds, marks)
    places = lax.broadcasted_iota(jnp.int32, (KB, rows), 0)
    deltas = []
    for h in heads:
        product = upstream[h].astype(jnp.float32) * o_ref[:, head_columns(h)].astype(jnp.float32)
        deltas.append(jnp.sum(product.T, axis=0, keepdims=True))

    def step(masked, number, carry):
        start = pl.multiple_of(number * KB, KB)
        window = pl.ds(start, KB)
        scores = [dot_cols(k_ref[window, head_columns(h)], queries[h]) for h in heads]
        prob_grads = [dot_cols(v_ref[window, head_columns(h)], upstream[h]) for h in heads]
        scores = [scores[h] * (score_scale * log2_e) - lse_ref[h] for h in heads]
        if masked:
            keep = (places >= low - start) & (places <= high - start)
            scores = [jnp.where(keep, score, hidden_floor) for score in scores]
        probs = [jnp.exp2(score) for score in scores]
        grads = [
            (probs[h] * (prob_grads[h] - deltas[h])).astype(jnp.bfloat16) for h in heads
        ]
        for h in heads:
            columns = head_columns(h)
            dv_sum[window, columns] += dot_plain(probs[h].astype(jnp.bfloat16), upstream[h])
            dk_sum[window, columns] += dot_plain(grads[h], queries[h])
        return tuple(
            carry[h] + dot_plain(kt[head_columns(h), window], grads[h]) for h in heads
        )

    start = jnp.zeros((HD, rows), jnp.float32)
    query_grads = over_key_blocks(step, span, (start,) * GROUP)
    if len(results) == 1:
        width = results[0].shape[1] // 3

        def place(part):
            begin = pl.multiple_of(part * width + group * GROUP * HD, GROUP * HD)
            return results[0].at[:, pl.ds(begin, GROUP * HD)]

        query_place = place(0).at[pl.ds(pl.multiple_of(block * rows, rows), rows)]
        key_place, value_place = place(1), place(2)
    else:
        query_place, key_place, value_place = results
    for h in heads:
        query_grad = (query_grads[h] * score_scale).T
        query_place[:, head_columns(h)] = query_grad.astype(query_place.dtype)

    @pl.when(block == pl.num_programs(1) - 1)
    def _():
        key_place[...] = (dk_sum[...] * score_scale).astype(key_place.dtype)
        value_place[...] = dv_sum[...].astype(value_place.dtype)


def attend_back(
    queries, keys, values, out, upstream, lse, bounds, places=(0, 0, 0), merged=False
):
    rows, width = out.shape
    span = keys.shape[0]
    heads = width // HD
    q_at, k_at, v_at = (place // GROUP for place in places)
    some = GROUP * HD
    row_spec = pl.BlockSpec((QB, some), lambda h, i, *_: (i, h))
    key_spec = pl.BlockSpec((span, some), lambda h, i, *_: (0, h))
    scalars, arrays, specs = bound_operands(bounds)
    return pl.pallas_call(
        functools.partial(attend_back_kernel, len(scalars), len(arrays)),
        out_shape=[jax.ShapeDtypeStruct((rows, 3 * width), jnp.bfloat16)]
        if merged
        else [
            jax.ShapeDtypeStruct((rows, width), jnp.bfloat16),
            jax.ShapeDtypeStruct((span, width), jnp.float32),
            jax.ShapeDtypeStruct((span, width), jnp.float32),
        ],
        grid_spec=pltpu.PrefetchScalarGridSpec(
            num_scalar_prefetch=len(scalars),
            grid=(heads // GROUP, rows // QB),
            in_specs=[
                pl.BlockSpec((QB, some), lambda h, i, *_: (i, h + q_at)),
                pl.BlockSpec((span, some), lambda h, i, *_: (0, h + k_at)),
                pl.BlockSpec((span, some), lambda h, i, *_: (0, h + v_at)),
                row_spec, row_spec,
                pl.BlockSpec((GROUP, 1, QB), lambda h, i, *_: (h, 0, i)),
                *specs,
            ],
            out_specs=[pl.BlockSpec((rows, 3 * width), lambda h, i, *_: (0, 0))]
            if merged
            else [row_spec, key_spec, key_spec],
            scratch_shapes=[
                pltpu.VMEM((some, span), jnp.bfloat16),
                pltpu.VMEM((span, some), jnp.float32),
                pltpu.VMEM((span, some), jnp.float32),
                pltpu.SMEM((2,), jnp.int32),
            ],
        ),
        compiler_params=pltpu.CompilerParams(vmem_limit_bytes=60 << 20),
        cost_estimate=pl.CostEstimate(
            flops=8 * rows * span * width,
            bytes_accessed=2 * (4 * rows + 4 * span) * width,
            transcendentals=rows * span * heads,
        ),
        name="attend_back",
    )(*scalars, queries, keys, values, out, upstream, lse, *arrays)


def key_bounds(query_ids, key_ids, offset):
    rows, span = query_ids.shape[0], key_ids.shape[0]
    start = jnp.sum(key_ids[:, None] < query_ids[None, :], axis=0, dtype=jnp.int32)
    stop = jnp.sum(key_ids[:, None] <= query_ids[None, :], axis=0, dtype=jnp.int32)
    places = jnp.arange(rows, dtype=jnp.int32) + offset
    low = jnp.maximum(start, places - WIN)
    high = jnp.minimum(stop - 1, places + WIN)
    first = jnp.min(low.reshape(-1, QB), axis=1) // KB
    last = jnp.max(high.reshape(-1, QB), axis=1) // KB + 1
    return first, last, low[None], high[None]


def padded(block, width):
    count = lax.axis_size("ctx")
    forward = [(i, i + 1) for i in range(count - 1)]
    backward = [(target, source) for source, target in forward]
    below = lax.ppermute(block[block.shape[0] - width :], "ctx", forward)
    above = lax.ppermute(block[:width], "ctx", backward)
    return jnp.concatenate([below, block, above], axis=0)


def norm_parts(rows):
    mean = jnp.mean(rows, axis=-1, keepdims=True)
    square = jnp.mean(rows * rows, axis=-1, keepdims=True)
    inverse = lax.rsqrt(square - mean * mean + epsilon)
    return (rows - mean) * inverse, inverse


def norm_back(upstream, normed, inverse, gain):
    scaled = upstream * gain
    first_mean = jnp.mean(scaled, axis=-1, keepdims=True)
    second_mean = jnp.mean(scaled * normed, axis=-1, keepdims=True)
    return inverse * (scaled - first_mean - normed * second_mean)


def gelu_tanh(values):
    return jax.nn.gelu(values, approximate=True)


MESH = pl.DeviceIdType.MESH
PIECES = 8
TILE = 2048
OWN_LATE = 5


def greet(me, count, others=()):
    barrier = pltpu.get_barrier_semaphore()

    @pl.when(me > 0)
    def _():
        pl.semaphore_signal(barrier, inc=1, device_id={"tp": me - 1}, device_id_type=MESH)

    @pl.when(me < count - 1)
    def _():
        pl.semaphore_signal(barrier, inc=1, device_id={"tp": me + 1}, device_id_type=MESH)

    for other in others:
        pl.semaphore_signal(barrier, inc=1, device_id=other, device_id_type=MESH)

    @pl.when((me == 0) | (me == count - 1))
    def _():
        pl.semaphore_wait(barrier, 1 + len(others))

    @pl.when((me > 0) & (me < count - 1))
    def _():
        pl.semaphore_wait(barrier, 2 + len(others))


def peers_along_tp(me, count):
    return [{"tp": lax.rem(me + i, count)} for i in range(1, count)]


def greet_peers(peers):
    barrier = pltpu.get_barrier_semaphore()
    for peer in peers:
        pl.semaphore_signal(barrier, inc=1, device_id=peer, device_id_type=MESH)
    pl.semaphore_wait(barrier, len(peers))


class Exchange:
    def __init__(self, peers, sent, got, source, place):
        self.peers, self.sent, self.got = peers, sent, got
        self.source, self.place = source, place

    def copies(self):
        for i, peer in enumerate(self.peers):
            yield pltpu.make_async_remote_copy(
                src_ref=self.source(i + 1),
                dst_ref=self.place(i),
                send_sem=self.sent.at[i],
                recv_sem=self.got.at[i],
                device_id=peer,
                device_id_type=MESH,
            )

    def start(self):
        for copy in self.copies():
            copy.start()

    def wait_arrivals(self):
        for copy in self.copies():
            copy.wait_recv()

    def wait_sent(self):
        for copy in self.copies():
            copy.wait_send()


def at_distance(me, count, distance, action):
    for index in (me - distance, me + distance):

        @pl.when((index >= 0) & (index < count))
        def _(index=index):
            action(index)


class Line:
    def __init__(self, me, count, sum_slots, sum_sent, sum_got, spread_view, spread_sent, spread_got):
        self.me, self.count = me, count
        self.sum_slots, self.sum_sent, self.sum_got = sum_slots, sum_sent, sum_got
        self.spread_view, self.spread_sent, self.spread_got = spread_view, spread_sent, spread_got

    def slot(self, piece):
        return lax.rem(piece, self.sum_slots.shape[0])

    def sum_copy(self, piece, owner):
        onward = jnp.where(owner > self.me, self.me + 1, self.me - 1)
        place = jnp.where((owner < self.me) & (owner == self.me - 1), self.count, owner)
        slot = self.slot(piece)
        return pltpu.make_async_remote_copy(
            src_ref=self.sum_slots.at[slot, owner],
            dst_ref=self.sum_slots.at[slot, place],
            send_sem=self.sum_sent.at[slot, owner],
            recv_sem=self.sum_got.at[slot, place],
            device_id={"tp": onward},
            device_id_type=MESH,
        )

    def sum_arrival(self, piece, place):
        view = self.sum_slots.at[self.slot(piece), place]
        pltpu.make_async_copy(view, view, self.sum_got.at[self.slot(piece), place]).wait()

    def sum_start(self, piece, term):
        me, count = self.me, self.count

        @pl.when((me == 0) | (me == count - 1))
        def _():
            for k in range(count - 1):
                owner = jnp.where(me == 0, count - 1 - k, k)
                self.sum_slots[self.slot(piece), owner] = term(owner).astype(jnp.bfloat16)
                self.sum_copy(piece, owner).start()

    def sum_onward(self, piece, term, distances):
        me, count = self.me, self.count

        @pl.when((me > 0) & (me < count - 1))
        def _():
            for distance in distances:

                def pass_on(owner):
                    self.sum_arrival(piece, owner)
                    slot = self.slot(piece)
                    total = self.sum_slots[slot, owner].astype(jnp.float32) + term(owner)
                    self.sum_slots[slot, owner] = total.astype(jnp.bfloat16)
                    self.sum_copy(piece, owner).start()

                at_distance(me, count, distance, pass_on)

    def sum_end(self, piece, total):
        me, count = self.me, self.count

        @pl.when(me > 0)
        def _():
            self.sum_arrival(piece, me)
            total[...] += self.sum_slots[self.slot(piece), me].astype(jnp.float32)

        @pl.when(me < count - 1)
        def _():
            self.sum_arrival(piece, count)
            total[...] += self.sum_slots[self.slot(piece), count].astype(jnp.float32)

    def sum_sent_all(self, piece):
        for distance in range(1, self.count):
            at_distance(
                self.me, self.count, distance,
                lambda owner: self.sum_copy(piece, owner).wait_send(),
            )

    def sum_finish(self, pieces):
        pl.loop(0, pieces)(self.sum_sent_all)

    def spread_copy(self, piece, owner, to, sent, source=None):
        return pltpu.make_async_remote_copy(
            src_ref=self.spread_view(piece, owner) if source is None else source,
            dst_ref=self.spread_view(piece, owner),
            send_sem=self.spread_sent.at[piece, sent],
            recv_sem=self.spread_got.at[piece, owner],
            device_id={"tp": to},
            device_id_type=MESH,
        )

    def own_copies(self, piece, action, source=None):
        me, count = self.me, self.count

        @pl.when(me > 0)
        def _():
            action(self.spread_copy(piece, me, me - 1, count, source))

        @pl.when(me < count - 1)
        def _():
            action(self.spread_copy(piece, me, me + 1, me, source))

    def spread_start(self, piece, source=None):
        self.own_copies(piece, lambda copy: copy.start(), source)

    def onward_copy(self, piece, owner, action):
        me, count = self.me, self.count

        @pl.when((owner < me) & (me < count - 1))
        def _():
            action(self.spread_copy(piece, owner, me + 1, owner))

        @pl.when((owner > me) & (me > 0))
        def _():
            action(self.spread_copy(piece, owner, me - 1, owner))

    def spread_onward(self, piece, distance):
        def pass_on(owner):
            view = self.spread_view(piece, owner)
            pltpu.make_async_copy(view, view, self.spread_got.at[piece, owner]).wait()
            self.onward_copy(piece, owner, lambda copy: copy.start())

        at_distance(self.me, self.count, distance, pass_on)

    def spread_finish(self, pieces, source=None):
        @pl.loop(0, pieces)
        def _(piece):
            self.own_copies(
                piece, lambda copy: copy.wait_send(), None if source is None else source(piece)
            )
            for distance in range(1, self.count):
                at_distance(
                    self.me, self.count, distance,
                    lambda owner: self.onward_copy(piece, owner, lambda copy: copy.wait_send()),
                )


def line_semaphores(count, pieces):
    return [
        pltpu.SemaphoreType.DMA((pieces, count)),
        pltpu.SemaphoreType.DMA((pieces, count + 1)),
    ], [
        pltpu.SemaphoreType.DMA((pieces, count + 1)),
        pltpu.SemaphoreType.DMA((pieces, count)),
    ]


def put_marks(marks, gains, biases):
    marks[...] = jnp.zeros_like(marks)
    marks[0:2, :] = gains[...].astype(jnp.float32)
    marks[2:6, :] = biases[...].astype(jnp.float32)


def gather_kernel(
    count, x_ref, gains, biases, out_ref, marks_out, marks_ref, slots, sent, got,
    marks_sent, marks_got,
):
    me = lax.axis_index("tp")
    height = x_ref.shape[0] // PIECES
    width = x_ref.shape[1]

    def view(piece, owner):
        return out_ref.at[
            pl.ds(pl.multiple_of(piece * height, height), height),
            pl.ds(pl.multiple_of(owner * width, width), width),
        ]

    def source(piece):
        return x_ref.at[pl.ds(pl.multiple_of(piece * height, height), height)]

    line = Line(me, count, None, None, None, view, sent, got)
    peers = peers_along_tp(me, count)
    put_marks(marks_ref, gains, biases)
    greet_peers(peers)

    @pl.loop(0, PIECES)
    def _(piece):
        line.spread_start(piece, source(piece))

    marks = Exchange(
        peers, marks_sent, marks_got, lambda _: marks_ref, lambda i: slots.at[i]
    )
    marks.start()
    own = pl.ds(pl.multiple_of(me * width, width), width)
    out_ref[:, own] = x_ref[...]
    marks_out[:, own] = marks_ref[...]
    for distance in range(1, count):

        @pl.loop(0, PIECES)
        def _(piece, distance=distance):
            line.spread_onward(piece, distance)

    marks.wait_arrivals()
    for i in range(1, count):
        owner = lax.rem(me - i + count, count)
        marks_out[:, pl.ds(pl.multiple_of(owner * width, width), width)] = slots[i - 1]
    marks.wait_sent()
    line.spread_finish(PIECES, source)


def gather_features(x, gains, biases, collective_id):
    count = lax.axis_size("tp")
    rows, width = x.shape
    return pl.pallas_call(
        functools.partial(gather_kernel, count),
        out_shape=[
            jax.ShapeDtypeStruct((rows, count * width), x.dtype),
            jax.ShapeDtypeStruct((8, count * width), jnp.float32),
        ],
        in_specs=[pl.BlockSpec(memory_space=pltpu.VMEM)] * 3,
        out_specs=[pl.BlockSpec(memory_space=pltpu.VMEM)] * 2,
        scratch_shapes=[
            pltpu.VMEM((8, width), jnp.float32),
            pltpu.VMEM((count - 1, 8, width), jnp.float32),
            *line_semaphores(count, PIECES)[1],
            pltpu.SemaphoreType.DMA((count - 1,)),
            pltpu.SemaphoreType.DMA((count - 1,)),
        ],
        compiler_params=pltpu.CompilerParams(
            collective_id=collective_id, has_side_effects=True, vmem_limit_bytes=16 << 20
        ),
        cost_estimate=pl.CostEstimate(
            flops=0, bytes_accessed=64 * rows * count * width, transcendentals=0
        ),
        name="gather_features",
    )(x, gains, biases)


class Swap:
    def __init__(self, sent, got, source, place):
        self.sent, self.got, self.source, self.place = sent, got, source, place

    def copy(self, piece):
        return pltpu.make_async_remote_copy(
            src_ref=self.source(piece),
            dst_ref=self.place(piece),
            send_sem=self.sent.at[piece],
            recv_sem=self.got.at[piece],
            device_id={"ctx": 1 - lax.axis_index("ctx")},
            device_id_type=MESH,
        )

    def start(self, piece):
        self.copy(piece).start()

    def wait_arrival(self, piece):
        self.copy(piece).wait_recv()

    def wait_sent(self, piece):
        self.copy(piece).wait_send()


class PlaneGather:
    def __init__(self, whole, sent, got):
        self.whole, self.sent, self.got = whole, sent, got
        fsdp, self.ctx = lax.axis_index("fsdp"), lax.axis_index("ctx")
        self.fsdp = fsdp
        self.twin = fsdp + 1 - 2 * lax.rem(fsdp, 2)
        self.along_x = lax.rem(fsdp + 2, 4)
        self.twin_x = lax.rem(self.twin + 2, 4)
        self.core_peer = {"fsdp": self.twin}
        self.x_peer = {"fsdp": self.along_x}
        self.y_peer = {"ctx": 1 - self.ctx}

    def peers(self):
        return [self.core_peer, self.x_peer, self.y_peer]

    def shard(self, fsdp, ctx, half=None):
        height = self.whole.shape[0] // 8
        start = (fsdp * 2 + ctx) * height
        if half is not None:
            height //= 2
            start += half * height
        return self.whole.at[pl.ds(pl.multiple_of(start, height), height)]

    def copy(self, number, view, peer):
        return pltpu.make_async_remote_copy(
            src_ref=view,
            dst_ref=view,
            send_sem=self.sent.at[number],
            recv_sem=self.got.at[number],
            device_id=peer,
            device_id_type=MESH,
        )

    def copies(self):
        own = self.shard(self.fsdp, self.ctx)
        from_x = self.shard(self.along_x, self.ctx)
        from_y = self.shard(self.fsdp, 1 - self.ctx)
        return [
            (own, self.core_peer),
            (own, self.x_peer),
            (own, self.y_peer),
            (from_x, self.core_peer),
            (self.shard(self.along_x, self.ctx, 0), self.y_peer),
            (from_y, self.core_peer),
            (self.shard(self.fsdp, 1 - self.ctx, 1), self.x_peer),
            (self.shard(self.along_x, 1 - self.ctx, 0), self.core_peer),
            (self.shard(self.along_x, 1 - self.ctx, 1), self.core_peer),
        ]

    def arrivals(self):
        return [
            self.shard(self.twin, self.ctx),
            self.shard(self.along_x, self.ctx),
            self.shard(self.fsdp, 1 - self.ctx),
            self.shard(self.twin_x, self.ctx),
            self.shard(self.along_x, 1 - self.ctx, 0),
            self.shard(self.twin, 1 - self.ctx),
            self.shard(self.along_x, 1 - self.ctx, 1),
            self.shard(self.twin_x, 1 - self.ctx, 0),
            self.shard(self.twin_x, 1 - self.ctx, 1),
        ]

    def start(self, *numbers):
        copies = self.copies()
        for number in numbers:
            self.copy(number, *copies[number]).start()

    def wait(self, *numbers):
        arrivals = self.arrivals()
        for number in numbers:
            view = arrivals[number]
            pltpu.make_async_copy(view, view, self.got.at[number]).wait()

    def first(self):
        self.start(1, 2, 0)

    def second(self):
        self.wait(1)
        self.start(4, 3)
        self.wait(2)
        self.start(6, 5)

    def third(self):
        self.wait(4)
        self.start(7)
        self.wait(6)
        self.start(8)

    def last(self):
        self.wait(0, 3, 5, 7, 8)

    def wait_sent(self):
        for number, (view, peer) in enumerate(self.copies()):
            self.copy(number, view, peer).wait_send()


def enter_kernel(
    count, x_ref, gains, biases, query_ref, key_ref, value_ref, output_ref, unit_biases, grad_ref,
    wide_out, own_tokens, marks_out, weight_out, output_out, heads, grad_out,
    wide, weight, output_weight, marks_ref, mark_slots, stage, sent, got, marks_sent, marks_got,
    weight_sent, weight_got, output_sent, output_got, swap_sent, swap_got, put_done, grad_done,
    wide_done, out_done,
):
    me, ctx = lax.axis_index("tp"), lax.axis_index("ctx")
    rows, width = x_ref.shape
    height = rows // PIECES
    half = query_ref.shape[1] // 2
    part = 3 * half

    def piece_rows(piece, start=0):
        return pl.ds(pl.multiple_of(start + piece * height, height), height)

    def view(piece, owner):
        return wide.at[piece_rows(piece), pl.ds(pl.multiple_of(owner * width, width), width)]

    gather = PlaneGather(weight, weight_sent, weight_got)
    output_gather = PlaneGather(output_weight, output_sent, output_got)
    own_shard = gather.shard(gather.fsdp, ctx)
    own = pl.ds(pl.multiple_of(me * width, width), width)
    puts = [
        (ref.at[:, pl.ds(side * half, half)], own_shard.at[:, pl.ds(side * part + i * half, half)])
        for side in range(2)
        for i, ref in enumerate((query_ref, key_ref, value_ref))
    ]
    puts += [
        (output_ref, output_gather.shard(gather.fsdp, ctx)),
        (x_ref, wide.at[:, own]),
    ]
    puts = [
        pltpu.make_async_copy(source, place, put_done.at[i])
        for i, (source, place) in enumerate(puts)
    ]
    for put in puts:
        put.start()
    grads = [
        pltpu.make_async_copy(grad_ref.at[:, owner], grad_out.at[owner], grad_done.at[owner])
        for owner in range(count)
    ]
    line = Line(me, count, None, None, None, view, sent, got)
    tp_peers = peers_along_tp(me, count)
    put_marks(marks_ref, gains, biases)
    greet_peers(tp_peers + gather.peers())

    def source(piece):
        return x_ref.at[piece_rows(piece)]

    for piece in range(2):
        line.spread_start(piece, source(piece))
    for put in puts[:7]:
        put.wait()
    gather.first()
    output_gather.first()
    marks = Exchange(
        tp_peers, marks_sent, marks_got, lambda _: marks_ref, lambda i: mark_slots.at[i]
    )
    marks.start()
    marks_out[:, own] = marks_ref[...]
    for put in puts[7:]:
        put.wait()
    for grad in grads:
        grad.start()
    swap = Swap(
        swap_sent, swap_got,
        lambda piece: stage.at[piece_rows(piece)],
        lambda piece: heads.at[piece_rows(piece, ctx * rows)],
    )

    def products(piece, side, place):
        columns = pl.ds(pl.multiple_of(side * part, part), part)
        result = dot_plain(wide[piece_rows(piece), :], weight[:, columns])
        for i, bias in enumerate((0, None, 2 * half)):
            values = result[:, i * half : (i + 1) * half]
            if bias is not None:
                own_half = pl.ds(pl.multiple_of(bias + side * half, half), half)
                values += unit_biases[:, own_half].astype(jnp.float32)
            place[:, i * half : (i + 1) * half] = values.astype(jnp.bfloat16)

    def wide_copy(piece):
        part = piece_rows(piece)
        return pltpu.make_async_copy(wide.at[part], wide_out.at[part], wide_done.at[piece])

    weight_copy = pltpu.make_async_copy(weight, weight_out, out_done.at[0])
    output_copy = pltpu.make_async_copy(output_weight, output_out, out_done.at[1])

    @pl.loop(0, PIECES + 7)
    def _(step):
        def late(pieces, action, least=0):
            @pl.when((step >= pieces + least) & (step < PIECES + pieces))
            def _():
                action(step - pieces)

        def use(piece):
            products(piece, 1 - ctx, stage.at[piece_rows(piece)])
            swap.start(piece)
            products(piece, ctx, heads.at[piece_rows(piece, ctx * rows)])
            wide_copy(piece).start()

        @pl.when(step == 7)
        def _():
            gather.third()
            gather.last()
            weight_copy.start()

        late(0, lambda piece: line.spread_start(piece, source(piece)), 2)
        late(7, use)
        late(5, lambda piece: line.spread_onward(piece, 2))
        late(3, lambda piece: line.spread_onward(piece, 1))
        late(6, lambda piece: [line.spread_onward(piece, i) for i in range(3, count)])
        pl.when(step == 5)(gather.second)
        pl.when(step == 7)(output_gather.second)
        pl.when(step == 9)(output_gather.third)

    own_height = height // count
    for piece in range(PIECES):
        start = pl.multiple_of(piece * height + me * own_height, own_height)
        own_tokens[piece * own_height : (piece + 1) * own_height, :] = wide[
            pl.ds(start, own_height), :
        ]

    marks.wait_arrivals()
    for i in range(1, count):
        owner = lax.rem(me - i + count, count)
        marks_out[:, pl.ds(pl.multiple_of(owner * width, width), width)] = mark_slots[i - 1]

    @pl.loop(0, PIECES)
    def _(piece):
        swap.wait_arrival(piece)
        swap.wait_sent(piece)

    output_gather.last()
    output_copy.start()
    marks.wait_sent()
    gather.wait_sent()
    output_gather.wait_sent()
    for grad in grads:
        grad.wait()
    weight_copy.wait()
    output_copy.wait()

    @pl.loop(0, PIECES)
    def _(piece):
        wide_copy(piece).wait()

    line.spread_finish(PIECES, source)


def enter(
    tokens, gains, biases, query_weight, key_weight, value_weight, output_weight, unit_biases,
    out_grad, collective_id,
):
    count = lax.axis_size("tp")
    rows, width = tokens.shape
    head_cols = query_weight.shape[1]
    features = count * width
    part = 3 * head_cols // 2
    own = rows // PIECES // count
    low = jnp.bfloat16
    vmem, anywhere = pl.BlockSpec(memory_space=pltpu.VMEM), pl.BlockSpec(memory_space=pl.ANY)
    return pl.pallas_call(
        functools.partial(enter_kernel, count),
        out_shape=[
            jax.ShapeDtypeStruct((rows, features), low),
            jax.ShapeDtypeStruct((rows // count, features), low),
            jax.ShapeDtypeStruct((8, features), jnp.float32),
            jax.ShapeDtypeStruct((features, 2 * part), low),
            jax.ShapeDtypeStruct((features, head_cols), low),
            jax.ShapeDtypeStruct((2 * rows, part), low),
            jax.ShapeDtypeStruct((count, PIECES, own, width), low),
        ],
        in_specs=[anywhere, vmem, vmem, *[anywhere] * 4, vmem, anywhere],
        out_specs=[anywhere, vmem, vmem, anywhere, anywhere, vmem, vmem],
        scratch_shapes=[
            pltpu.VMEM((rows, features), low),
            pltpu.VMEM((features, 2 * part), low),
            pltpu.VMEM((features, head_cols), low),
            pltpu.VMEM((8, width), jnp.float32),
            pltpu.VMEM((count - 1, 8, width), jnp.float32),
            pltpu.VMEM((rows, part), low),
            *line_semaphores(count, PIECES)[1],
            pltpu.SemaphoreType.DMA((count - 1,)),
            pltpu.SemaphoreType.DMA((count - 1,)),
            *[pltpu.SemaphoreType.DMA((9,))] * 4,
            pltpu.SemaphoreType.DMA((PIECES,)),
            pltpu.SemaphoreType.DMA((PIECES,)),
            pltpu.SemaphoreType.DMA((8,)),
            pltpu.SemaphoreType.DMA((count,)),
            pltpu.SemaphoreType.DMA((PIECES,)),
            pltpu.SemaphoreType.DMA((2,)),
        ],
        compiler_params=pltpu.CompilerParams(
            collective_id=collective_id, has_side_effects=True, vmem_limit_bytes=60 << 20
        ),
        cost_estimate=pl.CostEstimate(
            flops=80_000_000_000, bytes_accessed=64 * rows * features, transcendentals=0
        ),
        name="enter",
    )(
        tokens, gains, biases, query_weight, key_weight, value_weight, output_weight,
        unit_biases, out_grad.reshape(PIECES, count, own, width),
    )


def relay_kernel(count, row_step, use_step, sizes, *refs):
    row_in, use_in, row_out, use_out, shared = sizes
    refs = list(refs)

    def take(number):
        taken = refs[:number]
        del refs[:number]
        return taken

    x_ref, sum_weight = take(2)
    use_weight = sum_weight if shared else take(1)[0]
    row_inputs, use_inputs = take(row_in), take(use_in)
    (gathered,) = take(1)
    row_outputs, use_outputs = take(row_out), take(use_out)
    terms, total, slots, sum_sent, sum_got, spread_sent, spread_got = refs
    me = lax.axis_index("tp")
    height = x_ref.shape[0] // PIECES
    own = height // count
    width = sum_weight.shape[0]

    def piece_rows(piece):
        return pl.ds(pl.multiple_of(piece * height, height), height)

    def view(piece, owner):
        return gathered.at[pl.ds(pl.multiple_of(piece * height + owner * own, own), own)]

    line = Line(me, count, slots, sum_sent, sum_got, view, spread_sent, spread_got)
    greet(me, count)

    @pl.loop(0, PIECES + 5)
    def _(step):
        odd = lax.rem(step, 2)

        def term_of(parity):
            return lambda owner: terms[parity, pl.ds(pl.multiple_of(owner * own, own), own), :]

        def late(pieces, action):
            @pl.when((step >= pieces) & (step < PIECES + pieces))
            def _():
                action(step - pieces)

        def use(piece):
            part = piece_rows(piece)
            use_step(part, gathered[part, :], use_weight, use_inputs, use_outputs)

        def form(piece):
            x = x_ref[piece_rows(piece), :]

            @pl.loop(0, width // TILE)
            def _(tile):
                part = pl.ds(pl.multiple_of(tile * TILE, TILE), TILE)
                terms[odd, :, part] = dot_cols(x, sum_weight[part, :])

            line.sum_start(piece, term_of(odd))

        def own_step(piece):
            total[...] = terms[1 - odd, pl.ds(pl.multiple_of(me * own, own), own), :]
            line.sum_end(piece, total)
            view(piece, me)[...] = row_step(piece, total, row_inputs, row_outputs)
            line.spread_start(piece)

        late(5, use)
        late(3, lambda piece: line.spread_onward(piece, 2))
        late(1, lambda piece: line.sum_onward(piece, term_of(1 - odd), [1]))
        late(0, form)
        late(4, lambda piece: [line.spread_onward(piece, i) for i in range(3, count)])
        late(2, lambda piece: line.spread_onward(piece, 1))
        late(0, lambda piece: line.sum_onward(piece, term_of(odd), range(count - 2, 1, -1)))
        late(1, own_step)

    line.sum_finish(PIECES)
    line.spread_finish(PIECES)


def relay(
    x, sum_weight, use_weight, row_inputs, row_step, row_shapes, use_inputs, use_step, use_shapes,
    collective_id, name,
):
    count = lax.axis_size("tp")
    rows = x.shape[0]
    width = sum_weight.shape[0]
    height = rows // PIECES
    own = height // count
    shared = use_weight is None
    operands = [x, sum_weight, *([] if shared else [use_weight]), *row_inputs, *use_inputs]
    shapes = [jax.ShapeDtypeStruct((rows, width), jnp.bfloat16), *row_shapes, *use_shapes]
    sums, spreads = line_semaphores(count, PIECES)
    sizes = (len(row_inputs), len(use_inputs), len(row_shapes), len(use_shapes), shared)
    return pl.pallas_call(
        functools.partial(relay_kernel, count, row_step, use_step, sizes),
        out_shape=shapes,
        in_specs=[pl.BlockSpec(memory_space=pltpu.VMEM)] * len(operands),
        out_specs=[pl.BlockSpec(memory_space=pltpu.VMEM)] * len(shapes),
        scratch_shapes=[
            pltpu.VMEM((2, height, width), jnp.float32),
            pltpu.VMEM((own, width), jnp.float32),
            pltpu.VMEM((PIECES, count + 1, own, width), jnp.bfloat16),
            *sums,
            *spreads,
        ],
        compiler_params=pltpu.CompilerParams(
            collective_id=collective_id, has_side_effects=True, vmem_limit_bytes=60 << 20
        ),
        cost_estimate=pl.CostEstimate(
            flops=100_000_000_000, bytes_accessed=64 * rows * width, transcendentals=0
        ),
        name=name,
    )(*operands)


def own_rows_of(piece, like):
    own = like.shape[0] // PIECES
    return pl.ds(pl.multiple_of(piece * own, own), own)


def first_norm_step(piece, total, inputs, outputs):
    tokens, marks = inputs
    first_norm, normed_one, inverse_one = outputs
    part = own_rows_of(piece, tokens)
    summed = tokens[part, :].astype(jnp.float32) + (total[...] + marks[2:3, :])
    normed, inverse = norm_parts(summed)
    result = normed * marks[0:1, :] + marks[3:4, :]
    first_norm[part, :] = result
    normed_one[part, :] = normed
    inverse_one[part, :] = jnp.broadcast_to(inverse, (inverse.shape[0], 128))
    return result.astype(jnp.bfloat16)


def expand_step(rows, chunk, weight, inputs, outputs):
    (bias,) = inputs
    hidden, activated = outputs

    @pl.loop(0, hidden.shape[1] // TILE)
    def _(tile):
        part = pl.ds(pl.multiple_of(tile * TILE, TILE), TILE)
        values = dot_plain(chunk, weight[:, part]) + bias[:, part]
        hidden[rows, part] = values
        activated[rows, part] = gelu_tanh(values).astype(jnp.bfloat16)


def add_sums(piece, sums, *values):
    @pl.when(piece == 0)
    def _():
        sums[...] = jnp.zeros_like(sums)

    for i, value in enumerate(values):
        sums[i : i + 1, :] += jnp.sum(value, axis=0, keepdims=True)


def second_norm_step(piece, total, inputs, outputs):
    first_norm, out_grad, marks = inputs
    mixed, grad_second, sums = outputs
    part = own_rows_of(piece, first_norm)
    normed, inverse = norm_parts(first_norm[part, :] + total[...] + marks[4:5, :])
    result = (normed * marks[1:2, :] + marks[5:6, :]).astype(jnp.bfloat16)
    count, _, width = mixed.shape
    for i in range(count):
        mixed[i, part, :] = result[:, i * width : (i + 1) * width]
    upstream = jnp.concatenate([out_grad[i, part, :] for i in range(count)], axis=1)
    upstream = upstream.astype(jnp.float32)
    grad = norm_back(upstream, normed, inverse, marks[1:2, :])
    grad_second[part, :] = grad
    low = grad.astype(jnp.bfloat16)
    add_sums(piece, sums, upstream * normed, upstream, low.astype(jnp.float32))
    return low


def gelu_slope(values):
    scale = math.sqrt(2.0 / math.pi)
    square = values * values
    bend = jnp.tanh(scale * values * (1.0 + 0.044715 * square))
    inner = scale * (1.0 + 3 * 0.044715 * square)
    return 0.5 * (1.0 + bend) + 0.5 * values * (1.0 - bend * bend) * inner


def shrink_step(rows, chunk, weight, inputs, outputs):
    (hidden,) = inputs
    hidden_low, sums = outputs

    @pl.when(rows.start == 0)
    def _():
        sums[...] = jnp.zeros_like(sums)

    @pl.loop(0, hidden.shape[1] // TILE)
    def _(tile):
        part = pl.ds(pl.multiple_of(tile * TILE, TILE), TILE)
        grad = dot_plain(chunk, weight[:, part]) * gelu_slope(hidden[rows, part])
        low = grad.astype(jnp.bfloat16)
        hidden_low[rows, part] = low
        sums[0:1, part] += jnp.sum(low.astype(jnp.float32), axis=0, keepdims=True)


def first_back_step(piece, total, inputs, outputs):
    grad_second, normed_one, inverse_one, marks = inputs
    grad_inner, sums = outputs
    part = own_rows_of(piece, grad_second)
    normed = normed_one[part, :]
    grad_first = grad_second[part, :] + total[...]
    grad = norm_back(grad_first, normed, inverse_one[part, 0:1], marks[0:1, :])
    grad_inner[part, :] = grad
    low = grad.astype(jnp.bfloat16)
    add_sums(piece, sums, grad_first * normed, grad_first, low.astype(jnp.float32))
    return low


def attended_step(rows, chunk, weight, inputs, outputs):
    (attended_grad,) = outputs
    attended_grad[rows, :] = dot_plain(chunk, weight[...]).astype(jnp.bfloat16)


class PlaneSum:
    def __init__(self, parts, core_slots, first_slots, last_slots, sent, got):
        self.parts, self.core_slots = parts, core_slots
        self.first_slots, self.last_slots = first_slots, last_slots
        self.sent, self.got = sent, got
        self.fsdp, self.ctx = lax.axis_index("fsdp"), lax.axis_index("ctx")
        self.twin = self.fsdp + 1 - 2 * lax.rem(self.fsdp, 2)
        self.height = parts.shape[0] // 8
        self.half = parts.shape[1] // 2

    def number(self, fsdp, over_x, over_y):
        chip = lax.rem(fsdp + 2 * over_x, 4)
        return chip * 2 + (1 - self.ctx if over_y else self.ctx)

    def rows(self, number):
        return pl.ds(pl.multiple_of(number * self.height, self.height), self.height)

    def view(self, over_x, over_y, side):
        columns = pl.ds(side * self.half, self.half)
        return self.parts.at[self.rows(self.number(self.fsdp, over_x, over_y)), columns]

    def copy(self, number, source, place, peer):
        return pltpu.make_async_remote_copy(
            src_ref=source,
            dst_ref=place,
            send_sem=self.sent.at[number],
            recv_sem=self.got.at[number],
            device_id=peer,
            device_id_type=MESH,
        )

    def core_copy(self, number):
        over_x, over_y = number // 2, number % 2
        source = self.parts.at[self.rows(self.number(self.twin, over_x, over_y))]
        place = self.core_slots.at[self.rows(number)]
        return self.copy(number, source, place, {"fsdp": self.twin})

    def x_peer(self):
        return {"fsdp": lax.rem(self.fsdp + 2, 4)}

    def y_peer(self):
        return {"ctx": 1 - self.ctx}

    def first_copy(self, number):
        slot = self.first_slots.at[number]
        if number < 2:
            return self.copy(4 + number, self.view(1, number, 0), slot, self.x_peer())
        return self.copy(4 + number, self.view(number - 2, 1, 1), slot, self.y_peer())

    def last_copy(self, side):
        slot = self.last_slots.at[side]
        if side == 0:
            return self.copy(8, self.view(0, 1, 0), slot, self.y_peer())
        return self.copy(9, self.view(1, 0, 1), slot, self.x_peer())

    def bands(self, action):
        band = min(self.height, 32)

        @pl.loop(0, self.height // band)
        def _(i):
            action(pl.ds(pl.multiple_of(i * band, band), band))

    def add(self, view, slot):
        def band(part):
            total = view[part, :].astype(jnp.float32) + slot[part, :].astype(jnp.float32)
            view[part, :] = total.astype(view.dtype)

        self.bands(band)

    def start(self):
        for number in (3, 2, 1, 0):
            self.core_copy(number).start()

    def second(self):
        for number in (3, 2, 1, 0):
            self.core_copy(number).wait_recv()
            shard = self.parts.at[self.rows(self.number(self.fsdp, number // 2, number % 2))]
            self.add(shard, self.core_slots.at[self.rows(number)])
            if number == 3:
                self.first_copy(1).start()
                self.first_copy(3).start()
            if number == 2:
                self.first_copy(0).start()
            if number == 1:
                self.first_copy(2).start()

    def third(self):
        self.first_copy(1).wait_recv()
        self.add(self.view(0, 1, 0), self.first_slots.at[1])
        self.last_copy(0).start()
        self.first_copy(3).wait_recv()
        self.add(self.view(1, 0, 1), self.first_slots.at[3])
        self.last_copy(1).start()

    def finish(self, put):
        for side in range(2):
            self.first_copy(2 * side).wait_recv()
            self.last_copy(side).wait_recv()
            view, first, last = self.view(0, 0, side), self.first_slots, self.last_slots

            def band(part, side=side, view=view):
                total = view[part, :].astype(jnp.float32)
                total += first[2 * side, part, :].astype(jnp.float32)
                put(side, part, total + last[side, part, :].astype(jnp.float32))

            self.bands(band)
        for number in range(4):
            self.core_copy(number).wait_send()
            self.first_copy(number).wait_send()
        for side in range(2):
            self.last_copy(side).wait_send()

    @staticmethod
    def scratch(shards, height, width):
        return [
            pltpu.VMEM((shards * height, width), jnp.bfloat16),
            pltpu.VMEM((4 * height, width), jnp.bfloat16),
            *PlaneSum.slots(height, width),
        ]

    @staticmethod
    def slots(height, width):
        return [
            pltpu.VMEM((4, height, width // 2), jnp.bfloat16),
            pltpu.VMEM((2, height, width // 2), jnp.bfloat16),
            pltpu.SemaphoreType.DMA((10,)),
            pltpu.SemaphoreType.DMA((10,)),
        ]


def middle_kernel(
    count, heads_ref, output_weight, expand_shard, shrink_shard, own_tokens, out_grad, marks,
    unit_biases,
    attended, mixed, inner, branch_out, grad_heads, first_sums, second_sums, hidden_sums,
    shrink_out, expand_out,
    expand_weight, shrink_weight, gathered, activated, slope, normed_one, inverse_one,
    terms, total, slots, stage, expand_stage, first_slots, last_slots, plane_sent, plane_got,
    sum_sent, sum_got, spread_sent, spread_got, expand_sent, expand_got, shrink_sent, shrink_got,
    in_sent, in_got, out_sent, out_got, put_done, branch_done, product_done, ready,
):
    me, ctx = lax.axis_index("tp"), lax.axis_index("ctx")
    rows, width = gathered.shape[0] // 3, gathered.shape[1]
    half = heads_ref.shape[1]
    height = rows // PIECES
    own = height // count
    shard, hidden = width // PIECES, activated.shape[1]
    hidden_bias = unit_biases.at[:, pl.ds(unit_biases.shape[1] - hidden, hidden)]
    pieces = 3 * PIECES

    def piece_rows(piece, start=0):
        return pl.ds(pl.multiple_of(start + piece * height, height), height)

    def view(piece, owner):
        return gathered.at[pl.ds(pl.multiple_of(piece * height + owner * own, own), own)]

    line = Line(me, count, slots, sum_sent, sum_got, view, spread_sent, spread_got)
    expand_gather = PlaneGather(expand_weight, expand_sent, expand_got)
    shrink_gather = PlaneGather(shrink_weight, shrink_sent, shrink_got)
    own_half = pl.ds(pl.multiple_of(ctx * half, half), half)
    own_block = pl.ds(pl.multiple_of(ctx * rows, rows), rows)
    puts = [
        pltpu.make_async_copy(source, place, put_done.at[i])
        for i, (source, place) in enumerate(
            (
                (heads_ref.at[own_block], attended.at[:, own_half]),
                (expand_shard, expand_gather.shard(expand_gather.fsdp, ctx)),
                (shrink_shard, shrink_gather.shard(shrink_gather.fsdp, ctx)),
            )
        )
    ]
    for put in puts:
        put.start()
    swap_in = Swap(
        in_sent, in_got,
        lambda piece: heads_ref.at[piece_rows(piece, (1 - ctx) * rows)],
        lambda piece: attended.at[piece_rows(piece), own_half],
    )
    swap_out = Swap(
        out_sent, out_got,
        lambda piece: stage.at[piece_rows(piece)],
        lambda piece: grad_heads.at[piece_rows(piece, ctx * rows)],
    )
    greet(me, count, expand_gather.peers())
    pl.loop(0, PIECES)(swap_in.start)
    for put in puts:
        put.wait()
    expand_gather.first()

    def branch_copy(piece):
        part = piece_rows(piece)
        return pltpu.make_async_copy(
            gathered.at[piece_rows(piece, 2 * rows)], branch_out.at[part], branch_done.at[piece]
        )

    def in_stage(piece, number):
        return (piece >= number * PIECES) & (piece < (number + 1) * PIECES)

    def tiles(extent, action):
        @pl.loop(0, extent // TILE)
        def _(tile):
            action(pl.ds(pl.multiple_of(tile * TILE, TILE), TILE))

    def use(piece):
        line.sum_sent_all(piece)
        part = piece_rows(lax.rem(piece, PIECES))
        chunk_rows = piece_rows(piece)

        @pl.when(in_stage(piece, 0))
        def _():
            chunk = gathered[chunk_rows, :]

            def expand(columns):
                values = dot_plain(chunk, expand_weight[:, columns])
                values += hidden_bias[:, columns].astype(jnp.float32)
                result, bend = gelu_with_slope(values)
                activated[part, columns] = result.astype(jnp.bfloat16)
                slope[part, columns] = bend.astype(jnp.bfloat16)

            tiles(activated.shape[1], expand)

        @pl.when(in_stage(piece, 1))
        def _():
            chunk = gathered[chunk_rows, :]

            def shrink(columns):
                grad = dot_plain(chunk, shrink_weight[:, columns])
                low = (grad * slope[part, columns].astype(jnp.float32)).astype(jnp.bfloat16)
                slope[part, columns] = low
                added = jnp.sum(low.astype(jnp.float32), axis=0, keepdims=True)
                before = jnp.where(piece == PIECES, 0.0, hidden_sums[0:1, columns])
                hidden_sums[0:1, columns] = before + added

            tiles(slope.shape[1], shrink)

        @pl.when(in_stage(piece, 2))
        def _():
            place = piece - 2 * PIECES
            result = dot_plain(gathered[chunk_rows, :], output_weight[...]).astype(jnp.bfloat16)
            here = ctx == 0
            left, right = result[:, :half], result[:, half:]
            stage[part, :] = jnp.where(here, right, left)
            swap_out.start(place)
            grad_heads[piece_rows(place, ctx * rows), :] = jnp.where(here, left, right)
            branch_copy(place).start()

    def form(piece):
        part = piece_rows(lax.rem(piece, PIECES))
        parity = lax.rem(piece, 2)

        def products(x, weight):
            def product(columns):
                terms[parity, :, columns] = dot_cols(x, weight[columns, :])

            tiles(width, product)

        @pl.when(in_stage(piece, 0))
        def _():
            swap_in.wait_arrival(piece)
            products(attended[part, :], output_weight)

        @pl.when(in_stage(piece, 1))
        def _():
            products(activated[part, :], shrink_weight)

        @pl.when(in_stage(piece, 2))
        def _():
            products(slope[part, :], expand_weight)

        line.sum_start(piece, term_of(piece))

    def term_of(piece):
        parity = lax.rem(piece, 2)
        return lambda owner: terms[parity, pl.ds(pl.multiple_of(owner * own, own), own), :]

    def own_step(piece):
        place = lax.rem(piece, PIECES)
        total[...] = term_of(piece)(me)
        line.sum_end(piece, total)

        @pl.when(in_stage(piece, 0))
        def _():
            view(piece, me)[...] = first_norm_step(
                place, total, (own_tokens, marks), (inner, normed_one, inverse_one)
            )

        @pl.when(in_stage(piece, 1))
        def _():
            view(piece, me)[...] = second_norm_step(
                place, total, (inner, out_grad, marks), (mixed, inner, second_sums)
            )

        @pl.when(in_stage(piece, 2))
        def _():
            view(piece, me)[...] = first_back_step(
                place, total, (inner, normed_one, inverse_one, marks), (inner, first_sums)
            )

        line.spread_start(piece)

    def gradient(number, left_start, right, place):
        columns = pl.ds(pl.multiple_of(number * shard, shard), shard)
        def product(part):
            left = gathered[left_start : left_start + rows, columns]
            place[:, part] = dot_rows(left, right[:, part]).astype(place.dtype)

        tiles(place.shape[1], product)

    def expand_copy(number):
        part = pl.ds(pl.multiple_of(number * shard, shard), shard)
        return pltpu.make_async_copy(expand_stage, expand_out.at[part], product_done)

    def expand_step(number):
        pl.when(number > 0)(lambda: expand_copy(number - 1).wait())
        gradient(number, 0, slope, expand_stage)
        expand_copy(number).start()

    plane_sum = PlaneSum(shrink_weight, activated, first_slots, last_slots, plane_sent, plane_got)
    twin = {"fsdp": plane_sum.twin}

    def shrink_step(number):
        pl.when(number == 0)(shrink_gather.wait_sent)
        fsdp = jnp.where(number == 0, plane_sum.twin, plane_sum.fsdp)
        for over_x in (1, 0):
            for over_y in (1, 0):
                owner = plane_sum.number(fsdp, over_x, over_y)
                gradient(owner, rows, activated, shrink_weight.at[plane_sum.rows(owner)])

        @pl.when(number == 1)
        def _():
            pl.semaphore_signal(ready, inc=1, device_id=twin, device_id_type=MESH)

    def shrink_send(_):
        pl.semaphore_wait(ready, 1)
        plane_sum.start()

    def shrink_total(side):
        return pltpu.make_async_copy(
            terms.at[side], shrink_out.at[pl.ds(side * height, height)], put_done.at[side]
        )

    @pl.loop(0, pieces + 5)
    def _(step):
        def late(number, action, most=pieces):
            @pl.when((step >= number) & (step < most + number))
            def _():
                action(step - number)

        pl.when(step == 5)(expand_gather.last)
        pl.when(step == 2 * PIECES + 7)(plane_sum.second)
        pl.when(step == 2 * PIECES + 9)(plane_sum.third)
        pl.when(step == PIECES)(shrink_gather.last)
        late(0, form)
        late(1, lambda piece: line.sum_onward(piece, term_of(piece), [1]))
        late(5, use)
        late(3, lambda piece: line.spread_onward(piece, 2))
        late(4, lambda piece: [line.spread_onward(piece, i) for i in range(3, count)])
        late(2, lambda piece: line.spread_onward(piece, 1))
        late(2 * PIECES + 4, shrink_step, 2)
        late(2 * PIECES + 5, expand_step, PIECES)
        late(2 * PIECES + 6, shrink_send, 1)
        late(0, lambda piece: line.sum_onward(piece, term_of(piece), range(count - 2, 1, -1)))
        late(1, own_step)

        @pl.when(step == 3)
        def _():
            expand_gather.second()
            shrink_gather.first()

        pl.when(step == 4)(expand_gather.third)
        pl.when(step == 6)(shrink_gather.second)
        pl.when(step == 7)(shrink_gather.third)

    expand_copy(PIECES - 1).wait()

    def put_total(side, part, values):
        columns = pl.ds(side * (hidden // 2), hidden // 2)
        start = pl.multiple_of(lax.rem(part.start, height), values.shape[0])
        terms[part.start // height, pl.ds(start, values.shape[0]), columns] = values

    plane_sum.finish(put_total)
    for side in range(2):
        shrink_total(side).start()
    for side in range(2):
        shrink_total(side).wait()

    @pl.loop(0, PIECES)
    def _(piece):
        branch_copy(piece).wait()
        swap_in.wait_sent(piece)
        swap_out.wait_arrival(piece)
        swap_out.wait_sent(piece)

    expand_gather.wait_sent()
    line.spread_finish(pieces)


def gelu_with_slope(values):
    scale = math.sqrt(2.0 / math.pi)
    square = values * values
    bend = 0.5 * jnp.tanh(scale * values * (1.0 + 0.044715 * square)) + 0.5
    inner = (2 * scale) * (1.0 + 3 * 0.044715 * square)
    result = values * bend
    return result, bend + result * (1.0 - bend) * inner


def middle(
    attended_heads, output_weight, expand_shard, shrink_shard, own_tokens, out_grad, marks,
    unit_biases, collective_id,
):
    count = lax.axis_size("tp")
    rows = attended_heads.shape[0] // 2
    half = attended_heads.shape[1]
    own_rows, width = own_tokens.shape
    hidden = expand_shard.shape[1]
    height = rows // PIECES
    own = height // count
    shard = width // PIECES
    low = jnp.bfloat16
    vmem, anywhere = pl.BlockSpec(memory_space=pltpu.VMEM), pl.BlockSpec(memory_space=pl.ANY)

    def shape(extent, kind=jnp.float32):
        return jax.ShapeDtypeStruct(extent, kind)

    return pl.pallas_call(
        functools.partial(middle_kernel, count),
        out_shape=[
            shape((rows, 2 * half), low),
            shape(out_grad.shape, low),
            shape((own_rows, width)),
            shape((rows, width), low),
            shape((2 * rows, half), low),
            shape((8, width)),
            shape((8, width)),
            shape((8, hidden)),
            shape((shard, hidden)),
            shape((width, hidden), low),
        ],
        in_specs=[anywhere, vmem, anywhere, anywhere, vmem, vmem, vmem, vmem],
        out_specs=[vmem, vmem, vmem, anywhere, vmem, vmem, vmem, vmem, anywhere, anywhere],
        scratch_shapes=[
            pltpu.VMEM((width, hidden), low),
            pltpu.VMEM((width, hidden), low),
            pltpu.VMEM((3 * rows, width), low),
            pltpu.VMEM((rows, hidden), low),
            pltpu.VMEM((rows, hidden), low),
            pltpu.VMEM((own_rows, width), jnp.float32),
            pltpu.VMEM((own_rows, 128), jnp.float32),
            pltpu.VMEM((2, height, width), jnp.float32),
            pltpu.VMEM((own, width), jnp.float32),
            pltpu.VMEM((PIECES, count + 1, own, width), low),
            pltpu.VMEM((rows, half), low),
            pltpu.VMEM((shard, hidden), low),
            *PlaneSum.slots(shard, hidden),
            *line_semaphores(count, PIECES)[0],
            *line_semaphores(count, 3 * PIECES)[1],
            *[pltpu.SemaphoreType.DMA((9,))] * 4,
            *[pltpu.SemaphoreType.DMA((PIECES,))] * 4,
            pltpu.SemaphoreType.DMA((3,)),
            pltpu.SemaphoreType.DMA((PIECES,)),
            pltpu.SemaphoreType.DMA,
            pltpu.SemaphoreType.REGULAR,
        ],
        compiler_params=pltpu.CompilerParams(
            collective_id=collective_id, has_side_effects=True, vmem_limit_bytes=62 << 20
        ),
        cost_estimate=pl.CostEstimate(
            flops=300_000_000_000, bytes_accessed=192 * rows * width, transcendentals=0
        ),
        name="middle",
    )(
        attended_heads, output_weight, expand_shard, shrink_shard, own_tokens, out_grad, marks,
        unit_biases,
    )


def peers_in_plane(sizes):
    fsdp, ctx = lax.axis_index("fsdp"), lax.axis_index("ctx")
    return [
        {"fsdp": lax.rem(fsdp + i, sizes[0]), "ctx": lax.rem(ctx + j, sizes[1])}
        for i in range(sizes[0])
        for j in range(sizes[1])
        if i or j
    ]


def input_kernel(
    sizes, x_ref, weight, inner_ref, first_ref, second_ref, hidden_ref, out_ref, vectors_ref,
    rows_ref, term_ref, total, slots, own_vectors, tp_slots, plane_slots,
    sum_sent, sum_got, tp_sent, tp_got, plane_sent, plane_got, hooks=None,
):
    count = sizes[2]
    me = lax.axis_index("tp")
    height = x_ref.shape[0] // PIECES
    own = height // count
    width = out_ref.shape[1]
    line = Line(me, count, slots, sum_sent, sum_got, None, None, None)
    tp_peers, plane_peers = peers_along_tp(me, count), peers_in_plane(sizes)
    greet_peers(tp_peers + plane_peers)

    def own_part(index):
        return rows_ref.at[:, pl.ds(pl.multiple_of(index * width, width), width)]

    over_tp = Exchange(
        tp_peers, tp_sent, tp_got,
        lambda i: own_part(lax.rem(me + i, count)), lambda i: tp_slots.at[i],
    )
    over_plane = Exchange(
        plane_peers, plane_sent, plane_got, lambda _: own_vectors, lambda i: plane_slots.at[i]
    )
    opening, before, after, pack_at = hooks or (*(lambda *_: None,) * 3, 0)
    order = ((0, 0), (1, 0), (0, 2), (0, 1), (1, 2), (1, 1))
    rows_ref[...] = jnp.zeros_like(rows_ref)
    for i, (which, row) in enumerate(order):
        rows_ref[i : i + 1, :] = (first_ref, second_ref)[which][row : row + 1, :]
    opening()
    over_tp.start()

    def terms(piece):
        def term(owner):
            features = pl.ds(pl.multiple_of(owner * width, width), width)
            term_ref[...] = dot_cols(
                x_ref[pl.ds(pl.multiple_of(piece * height, height), height), :],
                weight[features, :],
            )
            inner = inner_ref[pl.ds(pl.multiple_of(piece * own, own), own), features]
            term_ref[pl.ds(pl.multiple_of(me * own, own), own), :] += inner
            return term_ref[...]

        return term

    def pack():
        over_tp.wait_arrivals()
        own_vectors[0:8, :] = own_part(me)[...]
        for i in range(count - 1):
            own_vectors[0:8, :] += tp_slots[i]
        own_vectors[8:, :] = jnp.zeros_like(own_vectors[8:, :])
        hidden_rows = hidden_ref.shape[1] // width
        for i in range(hidden_rows):
            own_vectors[8 + i : 9 + i, :] = hidden_ref[0:1, i * width : (i + 1) * width]
        for i in range(x_ref.shape[1] // width):
            part = x_ref[:, i * width : (i + 1) * width].astype(jnp.float32)
            place = 8 + hidden_rows + i
            own_vectors[place : place + 1, :] = jnp.sum(part, axis=0, keepdims=True)
        over_plane.start()

    def own_sum(piece):
        total[...] = terms(piece)(me)
        line.sum_end(piece, total)
        rows = pl.ds(pl.multiple_of(piece * height, height), height)
        out_ref[rows, :] = total[...].astype(out_ref.dtype)

    @pl.loop(0, PIECES)
    def _(piece):
        before(piece)
        line.sum_start(piece, terms(piece))
        line.sum_onward(piece, terms(piece), range(count - 2, 0, -1))
        after(piece)
        pl.when(piece == pack_at)(pack)
        pl.when(piece >= OWN_LATE)(lambda: own_sum(piece - OWN_LATE))

    pl.loop(PIECES - OWN_LATE, PIECES)(own_sum)
    over_plane.wait_arrivals()
    vectors_ref[...] = own_vectors[...]
    for i in range(len(plane_peers)):
        vectors_ref[...] += plane_slots[i]
    over_tp.wait_sent()
    over_plane.wait_sent()
    line.sum_finish(PIECES)


def input_sum(x, weight, inner, first_sums, second_sums, hidden_sums, collective_id):
    sizes = tuple(lax.axis_size(axis) for axis in ("fsdp", "ctx", "tp"))
    count = sizes[2]
    others = sizes[0] * sizes[1] - 1
    rows = x.shape[0]
    width = weight.shape[0] // count
    height = rows // PIECES
    packed = 8 + -(-(hidden_sums.shape[1] + x.shape[1]) // (8 * width)) * 8
    return pl.pallas_call(
        functools.partial(input_kernel, sizes),
        out_shape=[
            jax.ShapeDtypeStruct((rows, width), jnp.bfloat16),
            jax.ShapeDtypeStruct((packed, width), jnp.float32),
        ],
        in_specs=[pl.BlockSpec(memory_space=pltpu.VMEM)] * 6,
        out_specs=[pl.BlockSpec(memory_space=pltpu.VMEM)] * 2,
        scratch_shapes=[
            pltpu.VMEM(first_sums.shape, jnp.float32),
            pltpu.VMEM((height, width), jnp.float32),
            pltpu.VMEM((height, width), jnp.float32),
            pltpu.VMEM((PIECES, count + 1, height, width), jnp.bfloat16),
            pltpu.VMEM((packed, width), jnp.float32),
            pltpu.VMEM((count - 1, 8, width), jnp.float32),
            pltpu.VMEM((others, packed, width), jnp.float32),
            *line_semaphores(count, PIECES)[0],
            pltpu.SemaphoreType.DMA((count - 1,)),
            pltpu.SemaphoreType.DMA((count - 1,)),
            pltpu.SemaphoreType.DMA((others,)),
            pltpu.SemaphoreType.DMA((others,)),
        ],
        compiler_params=pltpu.CompilerParams(
            collective_id=collective_id, has_side_effects=True, vmem_limit_bytes=40 << 20
        ),
        cost_estimate=pl.CostEstimate(
            flops=60_000_000_000, bytes_accessed=64 * rows * width, transcendentals=0
        ),
        name="input_sum",
    )(x, weight, inner, first_sums, second_sums, hidden_sums)


def leave_kernel(
    sizes, grads_ref, tokens_in, weight_in, inner_in, first_ref, second_ref, hidden_ref, branch_in,
    attended_in,
    out_ref, vectors_ref, query_out, key_out, value_out, output_out,
    tokens_ref, weight, inner_ref, branch_ref, attended_ref, copied, own_copied,
    x_ref, rows_ref, term_ref, total, slots, own_vectors, tp_slots, plane_slots,
    sum_sent, sum_got, tp_sent, tp_got, plane_sent, plane_got, swap_sent, swap_got, *sum_scratch,
):
    count = sizes[2]
    me, ctx = lax.axis_index("tp"), lax.axis_index("ctx")
    rows = x_ref.shape[0]
    height = rows // PIECES
    part = grads_ref.shape[1]
    plane_sum, output_sum = PlaneSum(*sum_scratch[:6]), PlaneSum(*sum_scratch[6:])
    shard = plane_sum.height

    def piece_rows(piece, start=0):
        return pl.ds(pl.multiple_of(start + piece * height, height), height)

    copies = [
        pltpu.make_async_copy(source, place, copied.at[i])
        for i, (source, place) in enumerate(
            (
                (branch_in, branch_ref),
                (attended_in, attended_ref),
                (weight_in, weight),
                (inner_in, inner_ref),
                (tokens_in, tokens_ref),
            )
        )
    ]
    for copy in copies:
        copy.start()
    own_columns = pl.ds(pl.multiple_of(ctx * part, part), part)
    own_block = pl.ds(pl.multiple_of(ctx * rows, rows), rows)
    own_copy = pltpu.make_async_copy(
        grads_ref.at[own_block], x_ref.at[:, own_columns], own_copied
    )
    own_copy.start()
    swap = Swap(
        swap_sent, swap_got,
        lambda piece: grads_ref.at[piece_rows(piece, (1 - ctx) * rows)],
        lambda piece: x_ref.at[piece_rows(piece), own_columns],
    )

    def products(sums, fsdp, left, right):
        for over_x in (1, 0):
            for over_y in (1, 0):
                number = sums.number(fsdp, over_x, over_y)
                columns = pl.ds(pl.multiple_of(number * shard, shard), shard)
                product = dot_rows(left[:, columns], right[...])
                sums.parts[sums.rows(number), :] = product.astype(jnp.bfloat16)

    def opening():
        @pl.loop(0, PIECES)
        def _(piece):
            swap.start(piece)

        for copy in copies[:2]:
            copy.wait()
        products(output_sum, output_sum.twin, branch_ref, attended_ref)
        output_sum.start()
        products(output_sum, output_sum.fsdp, branch_ref, attended_ref)
        output_sum.second()
        for copy in copies[2:]:
            copy.wait()
        own_copy.wait()

    last = PIECES - 1
    begin = jnp.where((me == 0) | (me == count - 1), last, 2)

    def before(piece):
        @pl.when(piece <= begin)
        def _():
            swap.wait_arrival(piece)

    def after(piece):
        @pl.when(piece == begin)
        def _():
            @pl.loop(begin + 1, PIECES)
            def _(other):
                swap.wait_arrival(other)

            products(plane_sum, plane_sum.twin, tokens_ref, x_ref)
            plane_sum.start()

        @pl.when(piece == jnp.minimum(begin + 1, last))
        def _():
            products(plane_sum, plane_sum.fsdp, tokens_ref, x_ref)

        pl.when(piece == jnp.minimum(begin + 1, last))(plane_sum.second)
        pl.when(piece == jnp.minimum(begin + 3, last))(output_sum.third)
        pl.when(piece == jnp.minimum(begin + 4, last))(plane_sum.third)

    input_kernel(
        sizes, x_ref, weight, inner_ref, first_ref, second_ref, hidden_ref, out_ref, vectors_ref,
        rows_ref, term_ref, total, slots, own_vectors, tp_slots, plane_slots,
        sum_sent, sum_got, tp_sent, tp_got, plane_sent, plane_got,
        hooks=(opening, before, after, jnp.minimum(begin + 3, last)),
    )
    third = part // 3

    def put_part(side, rows, values):
        for i, ref in enumerate((query_out, key_out, value_out)):
            ref[rows, side * third : (side + 1) * third] = values[:, i * third : (i + 1) * third]

    def put_output(side, rows, values):
        output_out[rows, side * output_sum.half : (side + 1) * output_sum.half] = values

    plane_sum.finish(put_part)
    output_sum.finish(put_output)

    @pl.loop(0, PIECES)
    def _(piece):
        swap.wait_sent(piece)


def leave(
    grads, tokens, weight, inner, first_sums, second_sums, hidden_sums, branch, attended,
    collective_id,
):
    sizes = tuple(lax.axis_size(axis) for axis in ("fsdp", "ctx", "tp"))
    count = sizes[2]
    others = sizes[0] * sizes[1] - 1
    rows, features = tokens.shape
    part = grads.shape[1]
    width = features // count
    height = rows // PIECES
    shard = features // (others + 1)
    packed = 8 + -(-(hidden_sums.shape[1] + 2 * part) // (8 * width)) * 8
    return pl.pallas_call(
        functools.partial(leave_kernel, sizes),
        out_shape=[
            jax.ShapeDtypeStruct((rows, width), jnp.bfloat16),
            jax.ShapeDtypeStruct((packed, width), jnp.float32),
            *[jax.ShapeDtypeStruct((shard, 2 * part // 3), jnp.float32)] * 4,
        ],
        in_specs=[
            *[pl.BlockSpec(memory_space=pl.ANY)] * 4,
            *[pl.BlockSpec(memory_space=pltpu.VMEM)] * 3,
            *[pl.BlockSpec(memory_space=pl.ANY)] * 2,
        ],
        out_specs=[pl.BlockSpec(memory_space=pltpu.VMEM)] * 6,
        scratch_shapes=[
            *[pltpu.VMEM(x.shape, x.dtype) for x in (tokens, weight, inner, branch, attended)],
            pltpu.SemaphoreType.DMA((5,)),
            pltpu.SemaphoreType.DMA,
            pltpu.VMEM((rows, 2 * part), jnp.bfloat16),
            pltpu.VMEM(first_sums.shape, jnp.float32),
            pltpu.VMEM((height, width), jnp.float32),
            pltpu.VMEM((height, width), jnp.float32),
            pltpu.VMEM((PIECES, count + 1, height, width), jnp.bfloat16),
            pltpu.VMEM((packed, width), jnp.float32),
            pltpu.VMEM((count - 1, 8, width), jnp.float32),
            pltpu.VMEM((others, packed, width), jnp.float32),
            *line_semaphores(count, PIECES)[0],
            pltpu.SemaphoreType.DMA((count - 1,)),
            pltpu.SemaphoreType.DMA((count - 1,)),
            pltpu.SemaphoreType.DMA((others,)),
            pltpu.SemaphoreType.DMA((others,)),
            pltpu.SemaphoreType.DMA((PIECES,)),
            pltpu.SemaphoreType.DMA((PIECES,)),
            *PlaneSum.scratch(others + 1, shard, 2 * part),
            *PlaneSum.scratch(others + 1, shard, attended.shape[1]),
        ],
        compiler_params=pltpu.CompilerParams(
            collective_id=collective_id, has_side_effects=True, vmem_limit_bytes=60 << 20
        ),
        cost_estimate=pl.CostEstimate(
            flops=60_000_000_000, bytes_accessed=64 * rows * width, transcendentals=0
        ),
        name="leave",
    )(grads, tokens, weight, inner, first_sums, second_sums, hidden_sums, branch, attended)


def to_own_rows(wide):
    count = lax.axis_size("tp")
    parts = wide.reshape(PIECES, count, -1, wide.shape[1])
    return lax.dynamic_index_in_dim(parts, lax.axis_index("tp"), 1, keepdims=False).reshape(
        -1, wide.shape[1]
    )


def by_owner(block):
    count = lax.axis_size("tp")
    width = block.shape[1]
    parts = block.reshape(PIECES, count, -1, width).transpose(1, 0, 2, 3)
    return parts.reshape(count, -1, width)


def swap_over_tp(parts):
    return lax.all_to_all(parts, "tp", split_axis=0, concat_axis=0, tiled=True)


def by_rows(parts):
    count, _, width = parts.shape
    return parts.reshape(count, PIECES, -1, width).transpose(1, 0, 2, 3).reshape(-1, width)


def body(
    tokens,
    segments,
    query_weight,
    key_weight,
    value_weight,
    output_weight,
    expand_weight,
    shrink_weight,
    query_bias,
    value_bias,
    hidden_bias,
    norm_gains,
    row_biases,
    out_grad,
):
    rows = tokens.shape[0]
    head_cols = query_weight.shape[1]
    heads = head_cols // HD
    plane = ("fsdp", "ctx")
    plane_sizes = tuple(lax.axis_size(axis) for axis in plane)
    by_heads = plane_sizes == (4, 2) and heads % 2 == 0

    def weight_rows(weight):
        return lax.all_gather(weight, plane, axis=0, tiled=True)

    block_index = lax.axis_index("fsdp") * plane_sizes[1] + lax.axis_index("ctx")
    unit_biases = jnp.concatenate([query_bias, value_bias, hidden_bias])[None]
    if by_heads:
        wide_tokens, own_tokens, marks, wide_qkv, full_output, qkv_heads, upstream = enter(
            tokens, norm_gains, row_biases, query_weight, key_weight, value_weight, output_weight,
            unit_biases, out_grad, 0,
        )
        upstream = upstream.reshape(upstream.shape[0], -1, upstream.shape[3])
        queries = keys = values = qkv_heads
        own_heads = heads // 2
        bounds = (segments.reshape(-1, plane_sizes[1] * rows),)
    else:
        wide_qkv = weight_rows(jnp.concatenate([query_weight, key_weight, value_weight], axis=1))
        wide_tokens, marks = gather_features(tokens, norm_gains, row_biases, 0)
        upstream = by_owner(out_grad)
        own_tokens = to_own_rows(wide_tokens)
        qkv_bias = jnp.concatenate([query_bias, jnp.zeros_like(query_bias), value_bias])
        qkv = dot_plain(wide_tokens, wide_qkv) + qkv_bias.astype(jnp.float32)
        queries, keys, values = jnp.split(qkv.astype(jnp.bfloat16), 3, axis=1)
        own_heads = heads
        keys, values = padded(keys, WIN), padded(values, WIN)
        ids = jnp.concatenate(
            [
                jnp.full((WIN,), -1, jnp.int32),
                segments,
                jnp.full((WIN,), jnp.iinfo(jnp.int32).max, jnp.int32),
            ]
        )
        full_output, full_expand = weight_rows(output_weight), weight_rows(expand_weight)
        key_ids = lax.dynamic_slice_in_dim(ids, block_index * rows, rows + 2 * WIN, 0)
        bounds = key_bounds(key_ids[WIN : WIN + rows], key_ids, WIN)
    places = (0, own_heads, 2 * own_heads) if by_heads else (0, 0, 0)
    marks, upstream = lax.optimization_barrier((marks, upstream))
    upstream = swap_over_tp(upstream)
    attended_heads, lse = attend(queries, keys, values, own_heads, bounds, places)
    attended_heads, upstream = lax.optimization_barrier((attended_heads, upstream))

    own_rows, features = own_tokens.shape
    hidden_cols = expand_weight.shape[1]

    def shape(extent, kind=jnp.float32):
        return jax.ShapeDtypeStruct(extent, kind)

    own_shape = shape((own_rows, features))
    def owner_sum(grad):
        return lax.psum_scatter(
            grad, plane, scatter_dimension=0, tiled=True
        )

    if by_heads:
        (
            attended, mixed_own, grad_inner, branch_low, attended_grad,
            first_sums, second_sums, hidden_sums, shrink_grad, expand_part,
        ) = middle(
            attended_heads, full_output, expand_weight, shrink_weight, own_tokens, upstream,
            marks, unit_biases, 1,
        )
        expand_grad = owner_sum(expand_part)
        mixed = by_rows(swap_over_tp(mixed_own))
        (grads,) = attend_back(
            queries, keys, values, attended_heads, attended_grad, lse, bounds, places, True
        )
        grads, mixed = lax.optimization_barrier((grads, mixed))
    else:
        full_shrink = weight_rows(shrink_weight)
        norm_low, first_norm, normed_one, inverse_one, hidden, activated = relay(
            attended_heads, full_output, full_expand,
            [own_tokens, marks], first_norm_step,
            [own_shape, own_shape, shape((own_rows, 128))],
            [hidden_bias.astype(jnp.float32)[None]], expand_step,
            [shape((rows, hidden_cols)), shape((rows, hidden_cols), jnp.bfloat16)],
            1, "first_norm",
        )
        ffn_low, mixed_own, grad_second, second_sums, hidden_low, hidden_sums = relay(
            activated, full_shrink, None,
            [first_norm, upstream, marks], second_norm_step,
            [shape(upstream.shape, jnp.bfloat16), own_shape, shape((8, features))],
            [hidden], shrink_step,
            [shape((rows, hidden_cols), jnp.bfloat16), shape((8, hidden_cols))],
            2, "second_norm",
        )
        shrink_grad = owner_sum(dot_rows(ffn_low, activated).astype(jnp.bfloat16))
        branch_low, grad_inner, first_sums, attended_grad = relay(
            hidden_low, full_expand, full_output,
            [grad_second, normed_one, inverse_one, marks], first_back_step,
            [own_shape, shape((8, features))],
            [], attended_step,
            [shape((rows, head_cols), jnp.bfloat16)],
            3, "first_back",
        )
        expand_grad = owner_sum(dot_rows(norm_low, hidden_low).astype(jnp.bfloat16))
        output_grad = owner_sum(dot_rows(branch_low, attended_heads).astype(jnp.bfloat16))
        mixed = by_rows(swap_over_tp(mixed_own))
        query_low, key_ext, value_ext = attend_back(
            queries, keys, values, attended_heads, attended_grad, lse, bounds
        )

        def fold(ext):
            edges = jnp.concatenate([ext[:WIN], ext[WIN + rows :]], axis=0)
            around = padded(edges, WIN)
            own = ext[WIN : WIN + rows]
            own = own.at[:WIN].add(around[:WIN]).at[rows - WIN :].add(around[3 * WIN :])
            return own.astype(jnp.bfloat16)

        qkv_low = jnp.concatenate([query_low, fold(key_ext), fold(value_ext)], axis=1)
    sides = 2 if by_heads else 1

    def by_kind(columns):
        parts = columns.reshape(-1, sides, 3, head_cols // sides)
        return [parts[:, :, i].reshape(-1, head_cols) for i in range(3)]

    if by_heads:
        input_grad, vectors, query_grad, key_grad, value_grad, output_grad = leave(
            grads, wide_tokens, wide_qkv, grad_inner, first_sums, second_sums, hidden_sums,
            branch_low, attended, 4,
        )
        input_grad, expand_grad = lax.optimization_barrier((input_grad, expand_grad))
    else:
        input_grad, vectors = input_sum(
            qkv_low, wide_qkv, grad_inner, first_sums, second_sums, hidden_sums, 4
        )
        qkv_grad = owner_sum(dot_rows(wide_tokens, qkv_low).astype(jnp.bfloat16))
        query_grad, key_grad, value_grad = by_kind(qkv_grad.astype(jnp.float32))
    hidden_rows = hidden_cols // head_cols
    query_sum, _, value_sum = by_kind(
        vectors[8 + hidden_rows : 8 + hidden_rows + 3].reshape(1, -1)
    )
    return (
        mixed,
        input_grad,
        query_grad,
        key_grad,
        value_grad,
        output_grad.astype(jnp.float32),
        expand_grad.astype(jnp.float32),
        shrink_grad.astype(jnp.float32),
        query_sum[0],
        value_sum[0],
        vectors[8 : 8 + hidden_rows].reshape(-1),
        vectors[:2],
        vectors[2:6],
    )


def solution(mesh):
    rows, whole, cols = P(("fsdp", "ctx"), "tp"), P(), P("tp")
    wide = P(None, "tp")
    return jax.shard_map(
        body,
        mesh=mesh,
        in_specs=(rows, whole) + (rows,) * 6 + (cols,) * 3 + (wide,) * 2 + (rows,),
        out_specs=(rows,) * 8 + (cols,) * 3 + (wide,) * 2,
        check_vma=False,
    )
```
